32 devices in a mesh: pipe: 4 (over x, core), dp: 8 (over z, y).
Axes of the slice: x: 2, y: 2, z: 4, core: 2. Of those that a mesh axis runs over, the one named last changes fastest.
Arguments:
- token_ids: int32 [96, 126], P('dp'), may hold values from 0 to 1023
- segment_ids: int32 [96, 126], P('dp'), may hold values from 0 to 3, never falling along the last dimension, each value on 1 to 63 neighbouring positions
- target_ids: int32 [96, 126], P('dp'), may hold values from 0 to 1023
- embed_table: bfloat16 [1024, 512], replicated, may hold values from -6 to 6
- qkv_weight: bfloat16 [4, 512, 1536], P('pipe'), may hold values from -0.25 to 0.25
- qv_bias: float32 [4, 2, 512], P('pipe'), may hold values from -1.75 to 1.75
- out_weight: bfloat16 [4, 512, 512], P('pipe'), may hold values from -1 to 1
- out_biases: float32 [4, 2, 512], P('pipe'), may hold values from -1.75 to 1.75
- ff_in: bfloat16 [4, 512, 2048], P('pipe'), may hold values from -0.25 to 0.25
- ff_in_bias: float32 [4, 2048], P('pipe'), may hold values from -1.75 to 1.75
- ff_out: bfloat16 [4, 2048, 512], P('pipe'), may hold values from -0.125 to 0.125
- norm_gains: float32 [4, 2, 512], P('pipe'), may hold values from 0.5 to 1.5
- norm_biases: float32 [4, 2, 512], P('pipe'), may hold values from -1.75 to 1.75
- final_gain: float32 [512], replicated, may hold values from 0.5 to 1.5
- final_bias: float32 [512], replicated, may hold values from -1.75 to 1.75
- head_weight: bfloat16 [1024, 512], replicated, may hold values from -0.5 to 0.5
Outputs:
- embed_grad: float32 [1024, 512], P(('pipe', 'dp'))
- qkv_grad: float32 [4, 512, 1536], P('pipe', 'dp')
- qv_bias_grad: float32 [4, 2, 512], P('pipe', None, 'dp')
- out_weight_grad: float32 [4, 512, 512], P('pipe', 'dp')
- out_biases_grad: float32 [4, 2, 512], P('pipe', None, 'dp')
- ff_in_grad: float32 [4, 512, 2048], P('pipe', 'dp')
- ff_in_bias_grad: float32 [4, 2048], P('pipe', 'dp')
- ff_out_grad: float32 [4, 2048, 512], P('pipe', 'dp')
- norm_gains_grad: float32 [4, 2, 512], P('pipe', None, 'dp')
- norm_biases_grad: float32 [4, 2, 512], P('pipe', None, 'dp')
- final_gain_grad: float32 [512], replicated
- final_bias_grad: float32 [512], replicated
- head_grad: float32 [1024, 512], P(('pipe', 'dp'))
The draws below stay inside these ranges and needn't reach their ends.
Inputs may be any that keep to these rules, and one draw needn't show every extreme that they name: `segment_ids`: along a row segment numbers never fall; a fragment has at most 63 tokens.
All inputs are finite; a program needn't handle non-finite values.
Results may differ from the reference program's by a relative error of at most 0.0055.
Values may be sent and summed in bfloat16 or wider, within the bound.
A program may use at most 256 MiB of HBM per device.

```python
import math
import jax
import jax.numpy as jnp
import numpy as np
from jax import lax

D = 512
HEADS = 8
FF = 2048
VOCAB = 1024
SEQ = 126
FRAME = 6
LAYERS = 4
ROWS_DEV = 12
ROWS = 96


def plant(array, rng, smallest, high):
    index_at = [jax.random.randint(jax.random.fold_in(rng, axis), (), 0, length) for axis, length in enumerate(array.shape)]
    main_axis = array.shape.index(max(array.shape))
    beside = index_at[:main_axis] + [(index_at[main_axis] + 1) % array.shape[main_axis]] + index_at[main_axis + 1:]
    return array.at[tuple(index_at)].set(smallest).at[tuple(beside)].set(high)


def levels(key, shape, shards, smallest, high):
    gain = 1.0
    for dim, blocks in shards:
        heights = jax.random.uniform(jax.random.fold_in(jax.random.fold_in(key, 6), dim), (blocks,), jnp.float32, smallest / len(shards), high / len(shards))
        gain = gain * jnp.repeat(jnp.exp(heights), shape[dim] // blocks).reshape((-1,) + (1,) * (len(shape) - 1 - dim))
    return gain


def cumulative_ranks(amount, lean):
    portions = [(1 << 20) // math.isqrt(rank ** lean) + 1 for rank in range(1, amount + 1)]
    width = 1 + sum(portions) // (1 << 30)
    return np.cumsum(np.array([max(1, weight // width) for weight in portions]))


def ranked(rng, extent, count, lean):
    grid = cumulative_ranks(count, lean)
    pick = jax.random.randint(jax.random.fold_in(rng, 1), extent, 0, int(grid[count - 1]))
    rank = jnp.searchsorted(jnp.asarray(grid, jnp.int32), pick, side="right")
    return jax.random.permutation(jax.random.fold_in(rng, 2), count)[rank].astype(jnp.int32)


def profile(number_of, total, limit, skew):
    weights = [(1 << 20) // math.isqrt(grade ** skew) + 1 for grade in range(2, number_of + 1)]
    spare, holding = total - limit - (number_of - 1), [1] * (number_of - 1)
    while spare > 0:
        movable = [i for i in range(number_of - 1) if holding[i] < limit]
        pool, remaining = sum([weights[i] for i in movable]), spare
        for i in movable:
            addition = min(limit - holding[i], max(1, remaining * weights[i] // pool), spare)
            holding[i] = holding[i] + addition
            spare = spare - addition
    return np.array([limit] + holding)


def uneven(rng, count, total, limit, skew):
    if count == 2:
        one = jax.random.randint(rng, (), max(1, total - limit), min(limit, total - 1) + 1)
        return jnp.stack([one, total - one])
    sizes = jnp.asarray(profile(count, total, limit, skew), jnp.int32)
    pairs = (count - 1) // 2
    source_of, taker = sizes[1:1 + 2 * pairs:2], sizes[2:2 + 2 * pairs:2]
    slack = jnp.minimum(source_of - 1, limit - taker)
    passed = jax.random.randint(jax.random.fold_in(rng, 1), (pairs,), 0, 1 << 20) % (slack + 1)
    sizes = sizes.at[1:1 + 2 * pairs:2].set(source_of - passed).at[2:2 + 2 * pairs:2].set(taker + passed)
    return sizes[jax.random.permutation(jax.random.fold_in(rng, 2), count)]


def gaussian(key, extent, width, most, cuts=(), kind=jnp.bfloat16):
    array = width * jax.random.normal(key, extent, jnp.float32)
    if cuts:
        array = array * levels(key, extent, cuts, -0.22, 0.18)
    return jnp.clip(array, -most, most).astype(kind)


def setup_inputs(seed: int = 0) -> dict:
    splits = jax.random.split(jax.random.key(seed), 17)
    token_ids = plant(ranked(splits[0], (ROWS, SEQ), VOCAB, 2), jax.random.fold_in(splits[0], 3), 0, VOCAB - 1).astype(jnp.int32)
    segment_ids = jax.vmap(lambda own: jnp.searchsorted(jnp.cumsum(uneven(own, 4, SEQ, SEQ // 2, 1)), jnp.arange(SEQ), side="right"))(jax.random.split(splits[1], ROWS)).reshape((ROWS, SEQ)).astype(jnp.int32)
    target_ids = plant(ranked(splits[2], (ROWS, SEQ), VOCAB, 1), jax.random.fold_in(splits[2], 3), 0, VOCAB - 1).astype(jnp.int32)
    embed_table = gaussian(splits[3], (VOCAB, D), 1.0, 6.0)
    qkv_weight = gaussian(splits[4], (LAYERS, D, 3 * D), D ** -0.5, 0.25, ((0, 4),))
    qv_bias = gaussian(splits[5], (LAYERS, 2, D), 0.3, 1.75, ((0, 4),), jnp.float32)
    out_weight = gaussian(splits[6], (LAYERS, D, D), (D // 16) ** -0.5, 1.0, ((0, 4),))
    out_biases = gaussian(splits[7], (LAYERS, 2, D), 0.3, 1.75, ((0, 4),), jnp.float32)
    ff_in = gaussian(splits[8], (LAYERS, D, FF), D ** -0.5, 0.25, ((0, 4),))
    ff_in_bias = gaussian(splits[9], (LAYERS, FF), 0.3, 1.75, ((0, 4),), jnp.float32)
    ff_out = gaussian(splits[10], (LAYERS, FF, D), FF ** -0.5, 0.125, ((0, 4),))
    norm_gains = jnp.clip(1.0 + 0.1 * jax.random.normal(splits[11], (LAYERS, 2, D), jnp.float32), 0.5, 1.5)
    norm_biases = gaussian(splits[12], (LAYERS, 2, D), 0.3, 1.75, ((0, 4),), jnp.float32)
    final_gain = jnp.clip(1.0 + 0.1 * jax.random.normal(splits[13], (D,), jnp.float32), 0.5, 1.5)
    final_bias = gaussian(splits[14], (D,), 0.3, 1.75, (), jnp.float32)
    head_weight = gaussian(splits[15], (VOCAB, D), (D // 4) ** -0.5, 0.5)
    return {"token_ids": token_ids, "segment_ids": segment_ids, "target_ids": target_ids, "embed_table": embed_table, "qkv_weight": qkv_weight, "qv_bias": qv_bias, "out_weight": out_weight, "out_biases": out_biases, "ff_in": ff_in, "ff_in_bias": ff_in_bias, "ff_out": ff_out, "norm_gains": norm_gains, "norm_biases": norm_biases, "final_gain": final_gain, "final_bias": final_bias, "head_weight": head_weight}


@jax.custom_vjp
def low(v):
    return lax.optimization_barrier(v.astype(jnp.bfloat16)).astype(jnp.float32)

@jax.custom_vjp
def low_back(v):
    return v

def low_keep(v):
    return (low(v), None)

def low_pass(kept, grad):
    return (grad,)

def back_keep(v):
    return (v, None)

def back_low(kept, grad):
    return (low(grad),)
low.defvjp(low_keep, low_pass)
low_back.defvjp(back_keep, back_low)
highest = lax.Precision.HIGHEST
masked_score = -1e+30

def layer_norm(values, norm_gain, norm_shift):
    centre = lax.optimization_barrier(jnp.mean(values, axis=-1, keepdims=True))
    centered = values - centre
    spread = lax.optimization_barrier(jnp.mean(centered * centered, axis=-1, keepdims=True))
    return centered * lax.rsqrt(spread + 1e-05) * norm_gain + norm_shift

def visible_keys(segments):
    frames = jnp.arange(segments.shape[-1], dtype=jnp.int32) // FRAME
    same_piece = segments[:, :, None] == segments[:, None, :]
    earlier = frames[None, :] <= frames[:, None]
    return same_piece & earlier[None, :, :]

def layer_apply(stream, layer_params, visible):
    qkv_w, qv_b, out_w, out_b, in_w, in_b, down_w, gains_l, shifts_l = layer_params
    rows_n, seq_len, model_width = stream.shape
    head_dim = model_width // HEADS
    normed = low(layer_norm(stream, gains_l[0], shifts_l[0]))
    bias_full = jnp.concatenate([qv_b[0], jnp.zeros_like(qv_b[0]), qv_b[1]])
    projected = jnp.einsum('rsd,de->rse', normed, qkv_w, precision=highest) + bias_full
    projected = low(low_back(projected))
    split_heads = projected.reshape(rows_n, seq_len, 3, HEADS, head_dim)
    scores = jnp.einsum('rqhd,rkhd->rhqk', split_heads[:, :, 0], split_heads[:, :, 1], precision=highest) * head_dim ** (-0.5)
    scores = low_back(jnp.where(visible[:, None], scores, masked_score))
    attn_probs = jax.nn.softmax(scores, axis=-1)
    mixed = jnp.einsum('rhqk,rkhd->rqhd', low(attn_probs), split_heads[:, :, 2], precision=highest)
    mixed = low(low_back(mixed.reshape(rows_n, seq_len, model_width)))
    branch = low_back(jnp.einsum('rsd,de->rse', mixed, out_w, precision=highest) + out_b[0])
    middle = stream + branch
    normed_two = low(layer_norm(middle, gains_l[1], shifts_l[1]))
    hidden = low_back(jnp.einsum('rsd,df->rsf', normed_two, in_w, precision=highest) + in_b)
    active = low(jax.nn.gelu(hidden, approximate=True))
    result = low_back(jnp.einsum('rsf,fd->rsd', active, down_w, precision=highest) + out_b[1])
    return middle + result

def forward_loss(params, batch_ids, batch_segments, batch_targets):
    embed_rows, qkv_w, qv_b, out_w, out_b, in_w, in_b, down_w, gains, shifts, final_gain, final_bias, head_rows = params
    visible = visible_keys(batch_segments)
    stream = low_back(jnp.take(embed_rows, batch_ids, axis=0))
    for layer_index in range(LAYERS):
        layer_params = (qkv_w[layer_index], qv_b[layer_index], out_w[layer_index], out_b[layer_index], in_w[layer_index], in_b[layer_index], down_w[layer_index], gains[layer_index], shifts[layer_index])
        stream = layer_apply(stream, layer_params, visible)
        if layer_index + 1 < LAYERS:
            stream = low(low_back(stream))
    final = low(layer_norm(stream, final_gain, final_bias))
    logits = low_back(jnp.einsum('rsd,vd->rsv', final, head_rows, precision=highest))
    chosen = jnp.take_along_axis(logits, batch_targets[..., None], axis=-1)[..., 0]
    return jnp.sum(jax.nn.logsumexp(logits, axis=-1) - chosen)

def reference(token_ids, segment_ids, target_ids, embed_table, qkv_weight, qv_bias, out_weight, out_biases, ff_in, ff_in_bias, ff_out, norm_gains, norm_biases, final_gain, final_bias, head_weight):
    params = tuple((source.astype(jnp.float32) for source in (embed_table, qkv_weight, qv_bias, out_weight, out_biases, ff_in, ff_in_bias, ff_out, norm_gains, norm_biases, final_gain, final_bias, head_weight)))
    block_rows = ROWS_DEV
    blocks = token_ids.shape[0] // block_rows
    seq_len = token_ids.shape[1]
    id_blocks = token_ids.reshape(blocks, block_rows, seq_len)
    segment_blocks = segment_ids.reshape(blocks, block_rows, seq_len)
    target_blocks = target_ids.reshape(blocks, block_rows, seq_len)

    def accumulate(totals, batch):
        batch_ids, batch_segments, batch_targets = batch
        loss_value, pullback = jax.vjp(lambda inner: forward_loss(inner, batch_ids, batch_segments, batch_targets), params)
        grads = pullback(jnp.ones((), jnp.float32))[0]
        return (jax.tree.map(jnp.add, totals, grads), None)
    starting = jax.tree.map(jnp.zeros_like, params)
    totals, _ = lax.scan(accumulate, starting, (id_blocks, segment_blocks, target_blocks))
    return tuple(totals)
```

```python
import functools

import jax
import jax.numpy as jnp
from jax import lax
from jax.experimental import pallas as pl
from jax.experimental.pallas import tpu as pltpu
from jax.sharding import PartitionSpec as P

HEADS = 8
FRAME = 6
ROW = 128
GROUP = 2
MASKED = -1e30
GELU_A = 0.7978845608
GELU_B = 0.044715
MESH = pl.DeviceIdType.MESH
F32 = jnp.float32
BF16 = jnp.bfloat16

VEC_ROWS = 16
V_QUERY, V_VALUE, V_BRANCH, V_RESULT, V_GAIN1, V_GAIN2, V_SHIFT1, V_SHIFT2 = range(8)
V_HIDDEN = 8
V_FINAL_GAIN, V_FINAL_BIAS = 12, 13


def dot(a, b):
    return lax.dot_general(a, b, (((1,), (0,)), ((), ())), preferred_element_type=F32)


def dot_nt(a, b):
    return lax.dot_general(a, b, (((1,), (1,)), ((), ())), preferred_element_type=F32)


def dot_tn(a, b):
    return lax.dot_general(a, b, (((0,), (0,)), ((), ())), preferred_element_type=F32)


def normalise(values):
    centre = jnp.mean(values, axis=-1, keepdims=True)
    centered = values - centre
    spread = jnp.mean(centered * centered, axis=-1, keepdims=True)
    scale = lax.rsqrt(spread + 1e-05)
    return centered * scale, scale


def norm_backward(grad, normal, scale, gain):
    grad_n = grad * gain
    mean_grad = jnp.mean(grad_n, axis=-1, keepdims=True)
    mean_proj = jnp.mean(grad_n * normal, axis=-1, keepdims=True)
    return scale * (grad_n - mean_grad - normal * mean_proj)


def column_sum(values):
    return jnp.sum(values, axis=0, keepdims=True)


def stack_pair(pair, low_lanes):
    zero = jnp.zeros_like(pair)
    return jnp.concatenate(
        [jnp.where(low_lanes, pair, zero), jnp.where(low_lanes, zero, pair)], axis=0
    )


def join_pair(stacked, low_lanes):
    half = stacked.shape[0] // 2
    return jnp.where(low_lanes, stacked[:half], stacked[half:])


def pipeline_kernel(
    stages,
    micros,
    ids,
    seg_rows,
    embed,
    qkv_w,
    qv_b,
    out_w,
    out_b,
    in_w,
    in_b,
    down_w,
    gains,
    shifts,
    fin_gain,
    fin_bias,
    head_w,
    normed_o,
    mixed_o,
    normed2_o,
    active_o,
    gres_o,
    ghid_o,
    gbr_o,
    gproj_o,
    xl_o,
    xr_o,
    vec,
    instream,
    outb,
    gin,
    gs,
    normed,
    proj,
    probs,
    mixed,
    middle,
    normed2,
    hidden,
    lo,
    go,
    gmid,
    s_active,
    s_gres,
    s_ghid,
    s_gbr,
    s_gproj,
    s_xl,
    fsend,
    frecv,
    bsend,
    brecv,
    osem,
):
    stage = lax.axis_index("pipe")
    tokens, width = instream.shape[1], instream.shape[2]
    hidden_n = in_b.shape[1]
    vocab = head_w.shape[0]
    pairs = width // ROW
    chunk = 512
    is_first = stage == 0
    is_last = stage == stages - 1
    up = jnp.minimum(stage + 1, stages - 1)
    down = jnp.maximum(stage - 1, 0)

    barrier = pltpu.get_barrier_semaphore()

    @pl.when(jnp.logical_not(is_first))
    def _():
        pl.semaphore_signal(barrier, inc=1, device_id={"pipe": down}, device_id_type=MESH)

    @pl.when(jnp.logical_not(is_last))
    def _():
        pl.semaphore_signal(barrier, inc=1, device_id={"pipe": up}, device_id_type=MESH)

    pl.semaphore_wait(barrier, jnp.where(is_first | is_last, 1, 2))
    vec[...] = jnp.zeros_like(vec)

    def forward_copy(m):
        return pltpu.make_async_remote_copy(
            src_ref=outb.at[m],
            dst_ref=instream.at[m],
            send_sem=fsend.at[m],
            recv_sem=frecv.at[m],
            device_id={"pipe": up},
            device_id_type=MESH,
        )

    def backward_copy(m):
        return pltpu.make_async_remote_copy(
            src_ref=gs.at[m],
            dst_ref=gin.at[m],
            send_sem=bsend.at[m],
            recv_sem=brecv.at[m],
            device_id={"pipe": down},
            device_id_type=MESH,
        )

    def save(index, src, dst, m):
        return pltpu.make_async_copy(src, dst.at[m], osem.at[index, m])

    def saves_forward(m):
        return [
            save(0, normed.at[m], normed_o, m),
            save(1, mixed.at[m], mixed_o, m),
            save(2, normed2.at[m], normed2_o, m),
        ]

    def saves_backward(m):
        slot = lax.rem(m, 2)
        return [
            save(3, s_active.at[slot], active_o, m),
            save(4, s_gres.at[slot], gres_o, m),
            save(5, s_ghid.at[slot], ghid_o, m),
            save(6, s_gbr.at[slot], gbr_o, m),
            save(7, s_gproj.at[slot], gproj_o, m),
        ]

    def save_xl(m):
        return save(8, s_xl.at[lax.rem(m, 2)], xl_o, m)

    def put_xl(m, value):
        @pl.when(m >= 2)
        def _():
            save_xl(m - 2).wait()

        s_xl[lax.rem(m, 2)] = value
        save_xl(m).start()

    lane_low = lax.broadcasted_iota(jnp.int32, (ROW, ROW), 1) < ROW // 2

    def forward(m):
        base = pl.multiple_of(m * tokens, tokens)

        @pl.when(is_first)
        def _():
            tok = ids[pl.ds(base, tokens), 0:1]
            hot = (tok == lax.broadcasted_iota(jnp.int32, (tokens, vocab), 1)).astype(F32).astype(BF16)
            put_xl(m, hot)
            instream[m] = dot(hot, embed[...]).astype(BF16)

        @pl.when(jnp.logical_not(is_first))
        def _():
            forward_copy(m).wait_recv()

        normal, _ = normalise(instream[m].astype(F32))
        normed[m] = (normal * gains[0:1, :] + shifts[0:1, :]).astype(BF16)
        low = normed[m]
        queries = dot(low, qkv_w[:, 0:width]) + qv_b[0:1, :]
        proj[m, :, 0:width] = (queries * (ROW // 2) ** -0.5).astype(BF16)
        proj[m, :, width : 2 * width] = dot(low, qkv_w[:, width : 2 * width]).astype(BF16)
        proj[m, :, 2 * width : 3 * width] = (
            dot(low, qkv_w[:, 2 * width : 3 * width]) + qv_b[1:2, :]
        ).astype(BF16)
        for r in range(GROUP):
            rows = slice(r * ROW, (r + 1) * ROW)
            start = pl.multiple_of(base + r * ROW, ROW)
            seg_q = ids[pl.ds(start, ROW), 1:2]
            limit = ids[pl.ds(start, ROW), 3:4]
            seg_k = seg_rows[pl.ds(m * GROUP + r, 1), :]
            seen = (seg_q == seg_k) & (lax.broadcasted_iota(jnp.int32, (ROW, ROW), 1) < limit)
            for p in range(pairs):
                lanes = slice(p * ROW, (p + 1) * ROW)
                q = stack_pair(proj[m, rows, lanes], lane_low)
                k = proj[m, rows, width + p * ROW : width + (p + 1) * ROW]
                v = proj[m, rows, 2 * width + p * ROW : 2 * width + (p + 1) * ROW]
                scores = dot_nt(q, k).reshape(2, ROW, ROW)
                scores = jnp.where(seen[None], scores, MASKED)
                top = jnp.max(scores, axis=-1, keepdims=True)
                expo = jnp.exp(scores - top)
                total = jnp.sum(expo, axis=-1, keepdims=True)
                weights = (expo * (1.0 / total)).astype(BF16).reshape(2 * ROW, ROW)
                probs[m, r * pairs + p] = weights
                mixed[m, rows, lanes] = join_pair(dot(weights, v), lane_low).astype(BF16)
        mid = instream[m].astype(F32) + (dot(mixed[m], out_w[...]) + out_b[0:1, :])
        middle[m] = mid
        normal2, _ = normalise(mid)
        normed2[m] = (normal2 * gains[1:2, :] + shifts[1:2, :]).astype(BF16)
        low2 = normed2[m]
        for copy in saves_forward(m):
            copy.start()
        total = None
        for c in range(hidden_n // chunk):
            cols = slice(c * chunk, (c + 1) * chunk)
            hid = dot(low2, in_w[:, cols]) + in_b[0:1, cols]
            hidden[m, :, cols] = hid
            act = 0.5 * hid * (1.0 + jnp.tanh(GELU_A * (hid + GELU_B * (hid * hid * hid))))
            term = dot(act.astype(BF16), down_w[cols, :])
            total = term if total is None else total + term
        lo[...] = middle[m] + (total + out_b[1:2, :])

        @pl.when(jnp.logical_not(is_last))
        def _():
            outb[m] = lo[...].astype(BF16)
            forward_copy(m).start()

    def head(m):
        base = pl.multiple_of(m * tokens, tokens)
        normal, scale = normalise(lo[...])
        outb[m] = (normal * fin_gain[...] + fin_bias[...]).astype(BF16)
        save(9, outb.at[m], xr_o, m).start()
        logits = dot_nt(outb[m], head_w[...])
        top = jnp.max(logits, axis=-1, keepdims=True)
        expo = jnp.exp(logits - top)
        total = jnp.sum(expo, axis=-1, keepdims=True)
        target = ids[pl.ds(base, tokens), 2:3]
        hot = (target == lax.broadcasted_iota(jnp.int32, (tokens, vocab), 1)).astype(F32)
        real = target >= 0
        grad_logits = jnp.where(real, expo * (1.0 / total) - hot, 0.0).astype(BF16)
        put_xl(m, grad_logits)
        grad_final = dot(grad_logits, head_w[...])
        vec[V_FINAL_GAIN : V_FINAL_GAIN + 1, :] += column_sum(grad_final * normal)
        vec[V_FINAL_BIAS : V_FINAL_BIAS + 1, :] += column_sum(grad_final)
        go[...] = norm_backward(grad_final, normal, scale, fin_gain[...])

    def backward(m):
        slot = lax.rem(m, 2)

        @pl.when(m >= 2)
        def _():
            for copy in saves_backward(m - 2):
                copy.wait()

        @pl.when(jnp.logical_not(is_last))
        def _():
            backward_copy(m).wait_recv()
            go[...] = gin[m].astype(F32)

        s_gres[slot] = go[...].astype(BF16)
        gres = s_gres[slot]
        vec[V_RESULT : V_RESULT + 1, :] += column_sum(gres.astype(F32))
        total = None
        for c in range(hidden_n // chunk):
            cols = slice(c * chunk, (c + 1) * chunk)
            gact = dot_nt(gres, down_w[cols, :])
            hid = hidden[m, :, cols]
            square = hid * hid
            tan = jnp.tanh(GELU_A * (hid + GELU_B * (hid * square)))
            half = 0.5 * (1.0 + tan)
            s_active[slot, :, cols] = (hid * half).astype(BF16)
            slope = half + (0.5 * GELU_A) * hid * (1.0 - tan * tan) * (1.0 + (3.0 * GELU_B) * square)
            ghid = (gact * slope).astype(BF16)
            s_ghid[slot, :, cols] = ghid
            vec[V_HIDDEN + c : V_HIDDEN + c + 1, :] += column_sum(ghid.astype(F32))
            term = dot_nt(ghid, in_w[:, cols])
            total = term if total is None else total + term
        normal2, scale2 = normalise(middle[m])
        vec[V_GAIN2 : V_GAIN2 + 1, :] += column_sum(total * normal2)
        vec[V_SHIFT2 : V_SHIFT2 + 1, :] += column_sum(total)
        gmid[...] = go[...] + norm_backward(total, normal2, scale2, gains[1:2, :])
        s_gbr[slot] = gmid[...].astype(BF16)
        gbr = s_gbr[slot]
        vec[V_BRANCH : V_BRANCH + 1, :] += column_sum(gbr.astype(F32))
        gmix = dot_nt(gbr, out_w[...]).astype(BF16)
        for r in range(GROUP):
            rows = slice(r * ROW, (r + 1) * ROW)
            for p in range(pairs):
                lanes = slice(p * ROW, (p + 1) * ROW)
                klanes = slice(width + p * ROW, width + (p + 1) * ROW)
                vlanes = slice(2 * width + p * ROW, 2 * width + (p + 1) * ROW)
                gm = stack_pair(gmix[rows, lanes], lane_low)
                q = stack_pair(proj[m, rows, lanes], lane_low)
                k = proj[m, rows, klanes]
                v = proj[m, rows, vlanes]
                weights = probs[m, r * pairs + p]
                gp = dot_nt(gm, v)
                wf = weights.astype(F32)
                inner = jnp.sum(wf * gp, axis=-1, keepdims=True)
                gsc = (wf * (gp - inner)).astype(BF16)
                gq = join_pair(dot(gsc, k), lane_low) * (ROW // 2) ** -0.5
                s_gproj[slot, rows, lanes] = gq.astype(BF16)
                s_gproj[slot, rows, klanes] = dot_tn(gsc, q).astype(BF16)
                s_gproj[slot, rows, vlanes] = dot_tn(weights, gm).astype(BF16)
        for copy in saves_backward(m):
            copy.start()
        gproj = s_gproj[slot]
        vec[V_QUERY : V_QUERY + 1, :] += column_sum(gproj[:, 0:width].astype(F32))
        vec[V_VALUE : V_VALUE + 1, :] += column_sum(gproj[:, 2 * width : 3 * width].astype(F32))
        gnormed = dot_nt(gproj, qkv_w[...])
        normal, scale = normalise(instream[m].astype(F32))
        vec[V_GAIN1 : V_GAIN1 + 1, :] += column_sum(gnormed * normal)
        vec[V_SHIFT1 : V_SHIFT1 + 1, :] += column_sum(gnormed)
        gs[m] = (gmid[...] + norm_backward(gnormed, normal, scale, gains[0:1, :])).astype(BF16)

        @pl.when(is_first)
        def _():
            save(9, gs.at[m], xr_o, m).start()

        @pl.when(jnp.logical_not(is_first))
        def _():
            backward_copy(m).start()

    def tick(t, carry):
        m_forward = t - stage
        m_backward = t - (2 * (stages - 1) - stage)

        @pl.when((m_forward >= 0) & (m_forward < micros))
        def _():
            forward(m_forward)

        @pl.when((m_backward >= 0) & (m_backward < micros))
        def _():
            @pl.when(is_last)
            def _():
                head(m_backward)

            backward(m_backward)

        return carry

    lax.fori_loop(0, micros + 2 * (stages - 1), tick, 0)

    for m in range(micros):
        for copy in saves_forward(m):
            copy.wait()

        @pl.when(jnp.logical_not(is_last))
        def _():
            forward_copy(m).wait_send()

        @pl.when(jnp.logical_not(is_first))
        def _():
            backward_copy(m).wait_send()

        @pl.when(is_first)
        def _():
            save(9, gs.at[m], xr_o, m).wait()

        @pl.when(is_last)
        def _():
            save(9, outb.at[m], xr_o, m).wait()

    for m in range(max(0, micros - 2), micros):
        for copy in saves_backward(m):
            copy.wait()

        @pl.when(is_first | is_last)
        def _():
            save_xl(m).wait()


def run_pipeline(stages, ids, seg_rows, params):
    embed, qkv_w, qv_b, out_w, out_b, in_w, in_b, down_w, gains, shifts, fg, fb, head_w = params
    width = embed.shape[1]
    vocab = head_w.shape[0]
    hid = in_w.shape[1]
    tokens = GROUP * ROW
    micros = ids.shape[0] // tokens
    pairs = width // ROW
    vmem = pl.BlockSpec(memory_space=pltpu.VMEM)
    hbm = pl.BlockSpec(memory_space=pl.ANY)

    def kept(columns):
        return jax.ShapeDtypeStruct((micros, tokens, columns), BF16)

    def scratch(lead, columns, kind=BF16):
        return pltpu.VMEM((lead, tokens, columns), kind)

    out_shape = [
        kept(width),
        kept(width),
        kept(width),
        kept(hid),
        kept(width),
        kept(hid),
        kept(width),
        kept(3 * width),
        kept(vocab),
        kept(width),
        jax.ShapeDtypeStruct((VEC_ROWS, width), F32),
    ]
    return pl.pallas_call(
        functools.partial(pipeline_kernel, stages, micros),
        out_shape=out_shape,
        in_specs=[vmem] * 15,
        out_specs=[hbm] * 10 + [vmem],
        scratch_shapes=[
            scratch(micros, width),
            scratch(micros, width),
            scratch(micros, width),
            scratch(micros, width),
            scratch(micros, width),
            scratch(micros, 3 * width),
            pltpu.VMEM((micros, GROUP * pairs, 2 * ROW, ROW), BF16),
            scratch(micros, width),
            scratch(micros, width, F32),
            scratch(micros, width),
            scratch(micros, hid, F32),
            pltpu.VMEM((tokens, width), F32),
            pltpu.VMEM((tokens, width), F32),
            pltpu.VMEM((tokens, width), F32),
            scratch(2, hid),
            scratch(2, width),
            scratch(2, hid),
            scratch(2, width),
            scratch(2, 3 * width),
            scratch(2, vocab),
            pltpu.SemaphoreType.DMA((micros,)),
            pltpu.SemaphoreType.DMA((micros,)),
            pltpu.SemaphoreType.DMA((micros,)),
            pltpu.SemaphoreType.DMA((micros,)),
            pltpu.SemaphoreType.DMA((10, micros)),
        ],
        compiler_params=pltpu.CompilerParams(
            collective_id=0, has_side_effects=True, vmem_limit_bytes=62 * 1024 * 1024
        ),
        name="pipeline",
    )(ids, seg_rows, embed, qkv_w, qv_b, out_w, out_b, in_w, in_b, down_w, gains, shifts, fg, fb, head_w)


def line_dims(devices):
    dims, stride = [], 1
    if devices == 8:
        return [(2, 1), (4, 2)]
    while devices > 1:
        size = 4 if devices % 4 == 0 else 2
        dims.append((size, stride))
        stride *= size
        devices //= size
    return dims


def chunk_plan(width, hid, vocab, stages, devices):
    slim, deep = width // devices, hid // devices
    plan = []
    for c in range(2):
        plan.append(("down", c, (deep, width // 2)))
    plan.append(("extra", 0, (stages, vocab // (stages * devices), width)))
    for c in range(hid // width):
        plan.append(("in", c, (slim, width)))
    plan.append(("out", 0, (slim, width)))
    for c in range(3):
        plan.append(("qkv", c, (slim, width)))
    return plan


def gradient_kernel(stages, devices, plan, *refs):
    dims = line_dims(devices)
    refs = list(refs)

    def take(amount):
        head, refs[:] = refs[:amount], refs[amount:]
        return head

    inputs = take(10)
    vec_in = take(1)[0]
    qkv_out, out_out, in_out, down_out, embed_out, head_out, vec_out = take(7)
    local = take(10)
    in_sem = take(1)[0]
    mats = dict(
        zip(
            ("normed", "mixed", "normed2", "active", "gres", "ghid", "gbr", "gproj", "xl", "xr"),
            local,
        )
    )
    names = list(mats)
    stage = lax.axis_index("pipe")
    place = lax.axis_index("dp")
    is_extra = (stage == 0) | (stage == stages - 1)
    width = mats["normed"].shape[1]
    where = [lax.rem(place // stride, size) for size, stride in dims]

    barrier = pltpu.get_barrier_semaphore()

    def greet(offset, carry):
        peer = lax.rem(place + offset, devices)
        pl.semaphore_signal(barrier, inc=1, device_id={"dp": peer}, device_id_type=MESH)
        return carry

    def greet_stage(offset, carry):
        peer = lax.rem(stage + offset, stages)
        pl.semaphore_signal(barrier, inc=1, device_id={"pipe": peer}, device_id_type=MESH)
        return carry

    lax.fori_loop(1, devices, greet, 0)
    lax.fori_loop(1, stages, greet_stage, 0)

    def load(name):
        i = names.index(name)
        return pltpu.make_async_copy(inputs[i], mats[name], in_sem.at[i])

    order = ["gres", "active", "normed2", "ghid", "mixed", "gbr", "normed", "gproj"]
    for name in order[:2]:
        load(name).start()

    @pl.when(is_extra)
    def _():
        load("xl").start()
        load("xr").start()

    for name in order[2:]:
        load(name).start()

    pl.semaphore_wait(barrier, devices - 1 + stages - 1)
    loaded = set()

    def need(*wanted):
        for name in wanted:
            if name not in loaded:
                loaded.add(name)
                load(name).wait()

    bits = devices.bit_length() - 1
    vec_send, vec_recv = take(2)
    vec_sems = take(2)

    def vec_copy(k):
        peer = jnp.bitwise_xor(place, 1 << k)
        return pltpu.make_async_remote_copy(
            src_ref=vec_send.at[k],
            dst_ref=vec_recv.at[k],
            send_sem=vec_sems[0].at[k],
            recv_sem=vec_sems[1].at[k],
            device_id={"dp": peer},
            device_id_type=MESH,
        )

    def vec_step(k):
        def run():
            if k == 0:
                vec_send[0] = vec_in[...]
            else:
                vec_copy(k - 1).wait_recv()
                vec_send[k] = vec_send[k - 1] + vec_recv[k - 1]
            if k < bits:
                vec_copy(k).start()

        return run

    final_send, final_recv = take(2)
    final_sems = take(2)

    def final_copy(offset):
        peer = lax.rem(stages - 1 + offset, stages)
        return pltpu.make_async_remote_copy(
            src_ref=final_send,
            dst_ref=final_recv,
            send_sem=final_sems[0].at[offset],
            recv_sem=final_sems[1].at[0],
            device_id={"pipe": peer},
            device_id_type=MESH,
        )

    def vec_last():
        vec_step(bits)()
        vec_out[...] = vec_send[bits]

        @pl.when(stage == stages - 1)
        def _():
            final_send[...] = vec_send[bits, 8:16, :]
            for offset in range(1, stages):
                final_copy(offset).start()

    def vec_finish():
        @pl.when(stage != stages - 1)
        def _():
            final_copy(1).wait_recv()
            vec_out[V_FINAL_GAIN : V_FINAL_BIAS + 1, :] = final_recv[
                V_FINAL_GAIN - 8 : V_FINAL_BIAS - 7, :
            ]

    def vec_drain():
        for k in range(bits):
            vec_copy(k).wait_send()

        @pl.when(stage == stages - 1)
        def _():
            for offset in range(1, stages):
                final_copy(offset).wait_send()

    extra_sum, extra_send_sem, extra_recv_sem = take(3)

    def extra_copy(source, offset, target):
        peer = lax.rem(source + offset, stages)
        return pltpu.make_async_remote_copy(
            src_ref=extra_sum.at[peer],
            dst_ref=target,
            send_sem=extra_send_sem.at[offset],
            recv_sem=extra_recv_sem.at[0 if source == 0 else 1],
            device_id={"pipe": peer},
            device_id_type=MESH,
        )

    def chunk_steps(kind, c, block):
        full = take(1)[0]

        def compute():
            if kind == "down":
                need("gres", "active")
                half = width // 2

                def body(i, carry):
                    depth = block[0]
                    lanes = pl.ds(pl.multiple_of(i * 256, 256), 256)
                    part = dot_tn(mats["active"][:, lanes], mats["gres"][:, c * half : (c + 1) * half])
                    per = 256 // depth
                    put_blocks(full, i, per, part.astype(BF16).reshape((per,) + block))
                    return carry

                lax.fori_loop(0, mats["active"].shape[1] // 256, body, 0)
            elif kind == "extra":
                load("xl").wait()
                load("xr").wait()
                rows = mats["xl"].shape[1] // stages
                for p in range(stages):
                    part = dot_tn(mats["xl"][:, p * rows : (p + 1) * rows], mats["xr"][...])
                    part = part.astype(BF16).reshape((devices,) + block[1:])
                    for d in range(devices):
                        full[split(d) + (p,)] = part[d]
            else:
                left, right = {
                    "in": ("normed2", "ghid"),
                    "out": ("mixed", "gbr"),
                    "qkv": ("normed", "gproj"),
                }[kind]
                need(left, right)
                cols = slice(c * width, (c + 1) * width)

                def body(i, carry):
                    lanes = pl.ds(pl.multiple_of(i * 128, 128), 128)
                    part = dot_tn(mats[left][:, lanes], mats[right][:, cols])
                    per = 128 // block[0]
                    put_blocks(full, i, per, part.astype(BF16).reshape((per,) + block))
                    return carry

                lax.fori_loop(0, width // 128, body, 0)

        def split(d):
            return tuple((d // stride) % size for size, stride in reversed(dims))

        def put_blocks(ref, i, per, values):
            for q in range(per):
                d = i * per + q
                index = tuple(lax.rem(d // stride, size) for size, stride in reversed(dims))
                ref[index] = values[q]

        steps = [[compute]]
        for phase, (size, _) in enumerate(dims):
            buffers = take(3)
            steps[-1].append(functools.partial(line_step, phase, size, 1, full, buffers))
            for t in range(2, size):
                steps.append([functools.partial(line_step, phase, size, t, full, buffers)])
            drains.append((kind, functools.partial(line_drain, phase, size, full, buffers)))
            steps.append([functools.partial(line_final, kind, c, phase, size, full, buffers)])
        if kind == "extra":
            steps = [[gated(step)] for step in steps]
        return steps

    def gated(step):
        def run():
            @pl.when(is_extra)
            def _():
                for part in step:
                    part()

        return run

    def block_of(full, phase, j):
        later = [slice(None)] * (len(dims) - 1 - phase)
        return full.at[tuple(later + [j] + where[:phase][::-1])]

    def line_copy(phase, size, t, side, full, buffers):
        recv, ssem, rsem = buffers
        i = where[phase]
        stride = dims[phase][1]
        if side == 0:
            j, peer = size - t + i, place + jnp.where(i < size - 1, stride, 0)
        else:
            j, peer = t - size + i, place - jnp.where(i > 0, stride, 0)
        return pltpu.make_async_remote_copy(
            src_ref=block_of(full, phase, jnp.clip(j, 0, size - 1)),
            dst_ref=recv.at[0 if size == 2 else side, t - 1],
            send_sem=ssem.at[side, t - 1],
            recv_sem=rsem.at[side, t - 1],
            device_id={"dp": peer},
            device_id_type=MESH,
        )

    def sends(i, size, t, side):
        return (i <= t - 1) if side == 0 else (i >= size - t)

    def line_step(phase, size, t, full, buffers):
        i = where[phase]
        for side in range(2):
            at_end = (i == 0) if side == 0 else (i == size - 1)
            j = size - t + i if side == 0 else t - size + i
            j = jnp.clip(j, 0, size - 1)

            @pl.when(sends(i, size, t, side))
            def _():
                if t > 1:
                    @pl.when(jnp.logical_not(at_end))
                    def _():
                        line_copy(phase, size, t - 1, side, full, buffers).wait_recv()
                        own = block_of(full, phase, j)
                        got = buffers[0][0 if size == 2 else side, t - 2]
                        own[...] = (own[...].astype(F32) + got.astype(F32)).astype(BF16)

                line_copy(phase, size, t, side, full, buffers).start()

    def line_final(kind, c, phase, size, full, buffers):
        i = where[phase]
        own = block_of(full, phase, i)
        total = own
        if phase == len(dims) - 1:
            slots = {
                "qkv": lambda: qkv_out.at[:, c * width : (c + 1) * width],
                "in": lambda: in_out.at[:, c * width : (c + 1) * width],
                "out": lambda: out_out,
                "down": lambda: down_out.at[:, c * (width // 2) : (c + 1) * (width // 2)],
                "extra": lambda: extra_sum,
            }
            total = slots[kind]()
        lower, upper = i > 0, i < size - 1

        def arrived(side):
            line_copy(phase, size, size - 1, side, full, buffers).wait_recv()
            return buffers[0][0 if size == 2 else side, size - 2].astype(F32)

        @pl.when(lower & upper)
        def _():
            total[...] = (own[...].astype(F32) + arrived(0) + arrived(1)).astype(total.dtype)

        @pl.when(lower & jnp.logical_not(upper))
        def _():
            total[...] = (own[...].astype(F32) + arrived(0)).astype(total.dtype)

        @pl.when(jnp.logical_not(lower))
        def _():
            total[...] = (own[...].astype(F32) + arrived(1)).astype(total.dtype)

        if phase == len(dims) - 1 and kind == "extra":
            for source_stage, out in ((0, embed_out), (stages - 1, head_out)):
                @pl.when(stage == source_stage)
                def _():
                    for offset in range(1, stages):
                        extra_copy(source_stage, offset, extra_recv[0 if source_stage == 0 else 1]).start()
                    out[...] = extra_sum[source_stage]

    def line_drain(phase, size, full, buffers):
        i = where[phase]
        for side in range(2):
            for t in range(1, size):
                @pl.when(sends(i, size, t, side))
                def _():
                    line_copy(phase, size, t, side, full, buffers).wait_send()

    extra_recv = take(2)
    drains = []
    chains = [chunk_steps(*item) for item in plan]
    depth = len(chains[0])
    vec_chain = [vec_step(k) for k in range(bits)] + [vec_last]
    for r in range(len(chains) + depth - 1):
        for d in range(depth):
            if 0 <= r - d < len(chains):
                for part in chains[r - d][d]:
                    part()
        if r < len(vec_chain):
            vec_chain[r]()
    vec_finish()
    for source_stage, out in ((0, embed_out), (stages - 1, head_out)):
        @pl.when(stage != source_stage)
        def _():
            got = extra_recv[0 if source_stage == 0 else 1]
            extra_copy(source_stage, 1, got).wait_recv()
            out[...] = got[...]

        @pl.when(stage == source_stage)
        def _():
            for offset in range(1, stages):
                extra_copy(source_stage, offset, extra_recv[0]).wait_send()

    vec_drain()
    for kind, drain in drains:
        if kind == "extra":
            gated([drain])()
        else:
            drain()


def run_gradients(stages, devices, saved, vec):
    dims = line_dims(devices)
    micros, tokens, width = saved[0].shape
    hid, vocab = saved[3].shape[2], saved[8].shape[2]
    plan = chunk_plan(width, hid, vocab, stages, devices)
    saved = [member.reshape(micros * tokens, member.shape[2]) for member in saved]
    vmem = pl.BlockSpec(memory_space=pltpu.VMEM)
    hbm = pl.BlockSpec(memory_space=pl.ANY)
    bits = devices.bit_length() - 1
    share = vocab // (stages * devices)
    scratch = [pltpu.VMEM(member.shape, BF16) for member in saved]
    scratch += [pltpu.SemaphoreType.DMA((len(saved),))]
    scratch += [
        pltpu.VMEM((bits + 1,) + vec.shape, F32),
        pltpu.VMEM((bits,) + vec.shape, F32),
        pltpu.SemaphoreType.DMA((bits,)),
        pltpu.SemaphoreType.DMA((bits,)),
        pltpu.VMEM((8, width), F32),
        pltpu.VMEM((8, width), F32),
        pltpu.SemaphoreType.DMA((stages,)),
        pltpu.SemaphoreType.DMA((1,)),
        pltpu.VMEM((stages, share, width), F32),
        pltpu.SemaphoreType.DMA((stages,)),
        pltpu.SemaphoreType.DMA((2,)),
        pltpu.VMEM((share, width), F32),
        pltpu.VMEM((share, width), F32),
    ]
    sizes = [size for size, _ in reversed(dims)]
    for _, _, block in plan:
        scratch.append(pltpu.VMEM(tuple(sizes) + block, BF16))
        for phase, (size, _) in enumerate(dims):
            piece = tuple(sizes[: len(dims) - 1 - phase]) + block
            scratch.append(pltpu.VMEM((1 if size == 2 else 2, size - 1) + piece, BF16))
            scratch += [pltpu.SemaphoreType.DMA((2, size - 1))] * 2
    return pl.pallas_call(
        functools.partial(gradient_kernel, stages, devices, plan),
        out_shape=[
            jax.ShapeDtypeStruct((width // devices, 3 * width), F32),
            jax.ShapeDtypeStruct((width // devices, width), F32),
            jax.ShapeDtypeStruct((width // devices, hid), F32),
            jax.ShapeDtypeStruct((hid // devices, width), F32),
            jax.ShapeDtypeStruct((share, width), F32),
            jax.ShapeDtypeStruct((share, width), F32),
            jax.ShapeDtypeStruct(vec.shape, F32),
        ],
        in_specs=[hbm] * len(saved) + [vmem],
        out_specs=[vmem] * 7,
        scratch_shapes=scratch,
        compiler_params=pltpu.CompilerParams(
            collective_id=1, has_side_effects=True, vmem_limit_bytes=62 * 1024 * 1024
        ),
        name="gradients",
    )(*saved, vec)


def on_device(
    token_ids,
    segment_ids,
    target_ids,
    embed_table,
    qkv_weight,
    qv_bias,
    out_weight,
    out_biases,
    ff_in,
    ff_in_bias,
    ff_out,
    norm_gains,
    norm_biases,
    final_gain,
    final_bias,
    head_weight,
):
    stages = lax.axis_size("pipe")
    devices = lax.axis_size("dp")
    place = lax.axis_index("dp")
    rows, seq = token_ids.shape
    width = embed_table.shape[1]

    def padded(values):
        return jnp.pad(values, ((0, 0), (0, ROW - seq)), constant_values=-1)

    limit = (jnp.arange(ROW, dtype=jnp.int32) // FRAME + 1) * FRAME
    limit = jnp.broadcast_to(limit, (rows, ROW))
    seg_rows = padded(segment_ids)
    ids = jnp.stack([padded(token_ids), seg_rows, padded(target_ids), limit], axis=-1)
    ids = ids.reshape(rows * ROW, 4)
    params = (
        embed_table,
        qkv_weight[0],
        qv_bias[0],
        out_weight[0],
        out_biases[0],
        ff_in[0],
        ff_in_bias,
        ff_out[0],
        norm_gains[0],
        norm_biases[0],
        final_gain[None],
        final_bias[None],
        head_weight,
    )
    *saved, vec = run_pipeline(stages, ids, seg_rows, params)
    qkv_g, out_g, in_g, down_g, embed_g, head_g, sums = run_gradients(stages, devices, saved, vec)
    lanes = width // devices

    def shard(first):
        return lax.dynamic_slice(sums, (first, place * lanes), (2, lanes))[None]

    hidden_sum = sums[V_HIDDEN : V_HIDDEN + ff_in_bias.shape[1] // width].reshape(-1)
    share = hidden_sum.shape[0] // devices
    return (
        embed_g,
        qkv_g[None],
        shard(V_QUERY),
        out_g[None],
        shard(V_BRANCH),
        in_g[None],
        lax.dynamic_slice(hidden_sum, (place * share,), (share,))[None],
        down_g[None],
        shard(V_GAIN1),
        shard(V_SHIFT1),
        sums[V_FINAL_GAIN],
        sums[V_FINAL_BIAS],
        head_g,
    )


def solution(mesh):
    layer3 = P("pipe", None, None)
    return jax.shard_map(
        on_device,
        mesh=mesh,
        in_specs=(
            P("dp", None),
            P("dp", None),
            P("dp", None),
            P(),
            layer3,
            layer3,
            layer3,
            layer3,
            layer3,
            P("pipe", None),
            layer3,
            layer3,
            layer3,
            P(),
            P(),
            P(),
        ),
        out_specs=(
            P(("pipe", "dp"), None),
            P("pipe", "dp", None),
            P("pipe", None, "dp"),
            P("pipe", "dp", None),
            P("pipe", None, "dp"),
            P("pipe", "dp", None),
            P("pipe", "dp"),
            P("pipe", "dp", None),
            P("pipe", None, "dp"),
            P("pipe", None, "dp"),
            P(),
            P(),
            P(("pipe", "dp"), None),
        ),
        check_vma=False,
    )
```

```python
import functools

import jax
import jax.numpy as jnp
from jax import lax
from jax.experimental import pallas as pl
from jax.experimental.pallas import tpu as pltpu
from jax.sharding import PartitionSpec as P

HEADS = 8
FRAME = 6
ROW = 128
GROUP = 1
MASKED = -1e30
GELU_A = 0.7978845608
GELU_B = 0.044715
MESH = pl.DeviceIdType.MESH
F32 = jnp.float32
BF16 = jnp.bfloat16

VEC_ROWS = 16
V_QUERY, V_VALUE, V_BRANCH, V_RESULT, V_GAIN1, V_GAIN2, V_SHIFT1, V_SHIFT2 = range(8)
V_HIDDEN = 8
V_FINAL_GAIN, V_FINAL_BIAS = 12, 13


def dot(a, b):
    return lax.dot_general(a, b, (((1,), (0,)), ((), ())), preferred_element_type=F32)


def dot_nt(a, b):
    return lax.dot_general(a, b, (((1,), (1,)), ((), ())), preferred_element_type=F32)


def dot_tn(a, b):
    return lax.dot_general(a, b, (((0,), (0,)), ((), ())), preferred_element_type=F32)


def normalise(values):
    centre = jnp.mean(values, axis=-1, keepdims=True)
    centered = values - centre
    spread = jnp.mean(centered * centered, axis=-1, keepdims=True)
    scale = lax.rsqrt(spread + 1e-05)
    return centered * scale, scale


def norm_backward(grad, normal, scale, gain):
    grad_n = grad * gain
    mean_grad = jnp.mean(grad_n, axis=-1, keepdims=True)
    mean_proj = jnp.mean(grad_n * normal, axis=-1, keepdims=True)
    return scale * (grad_n - mean_grad - normal * mean_proj)


def column_sum(values):
    return jnp.sum(values, axis=0, keepdims=True)


def stack_pair(pair, low_lanes):
    zero = jnp.zeros_like(pair)
    return jnp.concatenate(
        [jnp.where(low_lanes, pair, zero), jnp.where(low_lanes, zero, pair)], axis=0
    )


def join_pair(stacked, low_lanes):
    half = stacked.shape[0] // 2
    return jnp.where(low_lanes, stacked[:half], stacked[half:])


def pipeline_kernel(
    stages,
    micros,
    ids,
    seg_rows,
    embed,
    qkv_w,
    qv_b,
    out_w,
    out_b,
    in_w,
    in_b,
    down_w,
    gains,
    shifts,
    fin_gain,
    fin_bias,
    head_w,
    normed_o,
    mixed_o,
    normed2_o,
    active_o,
    gres_o,
    ghid_o,
    gbr_o,
    gproj_o,
    xl_o,
    xr_o,
    vec,
    instream,
    outb,
    gin,
    gs,
    normed,
    proj,
    probs,
    mixed,
    middle,
    normed2,
    hidden,
    lo,
    go,
    gmid,
    s_active,
    s_gres,
    s_ghid,
    s_gbr,
    s_gproj,
    s_xl,
    fsend,
    frecv,
    bsend,
    brecv,
    osem,
):
    stage = lax.axis_index("pipe")
    tokens, width = instream.shape[1], instream.shape[2]
    hidden_n = in_b.shape[1]
    vocab = head_w.shape[0]
    pairs = width // ROW
    chunk = 512
    is_first = stage == 0
    is_last = stage == stages - 1
    up = jnp.minimum(stage + 1, stages - 1)
    down = jnp.maximum(stage - 1, 0)

    barrier = pltpu.get_barrier_semaphore()

    @pl.when(jnp.logical_not(is_first))
    def _():
        pl.semaphore_signal(barrier, inc=1, device_id={"pipe": down}, device_id_type=MESH)

    @pl.when(jnp.logical_not(is_last))
    def _():
        pl.semaphore_signal(barrier, inc=1, device_id={"pipe": up}, device_id_type=MESH)

    pl.semaphore_wait(barrier, jnp.where(is_first | is_last, 1, 2))
    vec[...] = jnp.zeros_like(vec)

    def forward_copy(m):
        return pltpu.make_async_remote_copy(
            src_ref=outb.at[m],
            dst_ref=instream.at[m],
            send_sem=fsend.at[m],
            recv_sem=frecv.at[m],
            device_id={"pipe": up},
            device_id_type=MESH,
        )

    def backward_copy(m):
        return pltpu.make_async_remote_copy(
            src_ref=gs.at[m],
            dst_ref=gin.at[m],
            send_sem=bsend.at[m],
            recv_sem=brecv.at[m],
            device_id={"pipe": down},
            device_id_type=MESH,
        )

    def save(index, src, dst, m):
        return pltpu.make_async_copy(src, dst.at[m], osem.at[index, m])

    def saves_forward(m):
        return [
            save(0, normed.at[m], normed_o, m),
            save(1, mixed.at[m], mixed_o, m),
            save(2, normed2.at[m], normed2_o, m),
        ]

    def saves_backward(m):
        slot = lax.rem(m, 2)
        return [
            save(3, s_active.at[slot], active_o, m),
            save(4, s_gres.at[slot], gres_o, m),
            save(5, s_ghid.at[slot], ghid_o, m),
            save(6, s_gbr.at[slot], gbr_o, m),
            save(7, s_gproj.at[slot], gproj_o, m),
        ]

    def save_xl(m):
        return save(8, s_xl.at[lax.rem(m, 2)], xl_o, m)

    def put_xl(m, value):
        @pl.when(m >= 2)
        def _():
            save_xl(m - 2).wait()

        s_xl[lax.rem(m, 2)] = value
        save_xl(m).start()

    lane_low = lax.broadcasted_iota(jnp.int32, (ROW, ROW), 1) < ROW // 2

    def forward(m):
        base = pl.multiple_of(m * tokens, tokens)

        @pl.when(is_first)
        def _():
            tok = ids[pl.ds(base, tokens), 0:1]
            hot = (tok == lax.broadcasted_iota(jnp.int32, (tokens, vocab), 1)).astype(F32).astype(BF16)
            put_xl(m, hot)
            instream[m] = dot(hot, embed[...]).astype(BF16)

        @pl.when(jnp.logical_not(is_first))
        def _():
            forward_copy(m).wait_recv()

        normal, _ = normalise(instream[m].astype(F32))
        normed[m] = (normal * gains[0:1, :] + shifts[0:1, :]).astype(BF16)
        low = normed[m]
        queries = dot(low, qkv_w[:, 0:width]) + qv_b[0:1, :]
        proj[m, :, 0:width] = (queries * (ROW // 2) ** -0.5).astype(BF16)
        proj[m, :, width : 2 * width] = dot(low, qkv_w[:, width : 2 * width]).astype(BF16)
        proj[m, :, 2 * width : 3 * width] = (
            dot(low, qkv_w[:, 2 * width : 3 * width]) + qv_b[1:2, :]
        ).astype(BF16)
        for r in range(GROUP):
            rows = slice(r * ROW, (r + 1) * ROW)
            start = pl.multiple_of(base + r * ROW, ROW)
            seg_q = ids[pl.ds(start, ROW), 1:2]
            limit = ids[pl.ds(start, ROW), 3:4]
            seg_k = seg_rows[pl.ds(m * GROUP + r, 1), :]
            seen = (seg_q == seg_k) & (lax.broadcasted_iota(jnp.int32, (ROW, ROW), 1) < limit)
            for p in range(pairs):
                lanes = slice(p * ROW, (p + 1) * ROW)
                q = stack_pair(proj[m, rows, lanes], lane_low)
                k = proj[m, rows, width + p * ROW : width + (p + 1) * ROW]
                v = proj[m, rows, 2 * width + p * ROW : 2 * width + (p + 1) * ROW]
                scores = dot_nt(q, k).reshape(2, ROW, ROW)
                scores = jnp.where(seen[None], scores, MASKED)
                top = jnp.max(scores, axis=-1, keepdims=True)
                expo = jnp.exp(scores - top)
                total = jnp.sum(expo, axis=-1, keepdims=True)
                weights = (expo * (1.0 / total)).astype(BF16).reshape(2 * ROW, ROW)
                probs[m, r * pairs + p] = weights
                mixed[m, rows, lanes] = join_pair(dot(weights, v), lane_low).astype(BF16)
        mid = instream[m].astype(F32) + (dot(mixed[m], out_w[...]) + out_b[0:1, :])
        middle[m] = mid
        normal2, _ = normalise(mid)
        normed2[m] = (normal2 * gains[1:2, :] + shifts[1:2, :]).astype(BF16)
        low2 = normed2[m]
        for copy in saves_forward(m):
            copy.start()
        total = None
        for c in range(hidden_n // chunk):
            cols = slice(c * chunk, (c + 1) * chunk)
            hid = dot(low2, in_w[:, cols]) + in_b[0:1, cols]
            hidden[m, :, cols] = hid
            act = 0.5 * hid * (1.0 + jnp.tanh(GELU_A * (hid + GELU_B * (hid * hid * hid))))
            term = dot(act.astype(BF16), down_w[cols, :])
            total = term if total is None else total + term
        lo[...] = middle[m] + (total + out_b[1:2, :])

        @pl.when(jnp.logical_not(is_last))
        def _():
            outb[m] = lo[...].astype(BF16)
            forward_copy(m).start()

    def head(m):
        base = pl.multiple_of(m * tokens, tokens)
        normal, scale = normalise(lo[...])
        outb[m] = (normal * fin_gain[...] + fin_bias[...]).astype(BF16)
        save(9, outb.at[m], xr_o, m).start()
        logits = dot_nt(outb[m], head_w[...])
        top = jnp.max(logits, axis=-1, keepdims=True)
        expo = jnp.exp(logits - top)
        total = jnp.sum(expo, axis=-1, keepdims=True)
        target = ids[pl.ds(base, tokens), 2:3]
        hot = (target == lax.broadcasted_iota(jnp.int32, (tokens, vocab), 1)).astype(F32)
        real = target >= 0
        grad_logits = jnp.where(real, expo * (1.0 / total) - hot, 0.0).astype(BF16)
        put_xl(m, grad_logits)
        grad_final = dot(grad_logits, head_w[...])
        vec[V_FINAL_GAIN : V_FINAL_GAIN + 1, :] += column_sum(grad_final * normal)
        vec[V_FINAL_BIAS : V_FINAL_BIAS + 1, :] += column_sum(grad_final)
        go[...] = norm_backward(grad_final, normal, scale, fin_gain[...])

    def backward(m):
        slot = lax.rem(m, 2)

        @pl.when(m >= 2)
        def _():
            for copy in saves_backward(m - 2):
                copy.wait()

        @pl.when(jnp.logical_not(is_last))
        def _():
            backward_copy(m).wait_recv()
            go[...] = gin[m].astype(F32)

        s_gres[slot] = go[...].astype(BF16)
        gres = s_gres[slot]
        vec[V_RESULT : V_RESULT + 1, :] += column_sum(gres.astype(F32))
        total = None
        for c in range(hidden_n // chunk):
            cols = slice(c * chunk, (c + 1) * chunk)
            gact = dot_nt(gres, down_w[cols, :])
            hid = hidden[m, :, cols]
            square = hid * hid
            tan = jnp.tanh(GELU_A * (hid + GELU_B * (hid * square)))
            half = 0.5 * (1.0 + tan)
            s_active[slot, :, cols] = (hid * half).astype(BF16)
            slope = half + (0.5 * GELU_A) * hid * (1.0 - tan * tan) * (1.0 + (3.0 * GELU_B) * square)
            ghid = (gact * slope).astype(BF16)
            s_ghid[slot, :, cols] = ghid
            vec[V_HIDDEN + c : V_HIDDEN + c + 1, :] += column_sum(ghid.astype(F32))
            term = dot_nt(ghid, in_w[:, cols])
            total = term if total is None else total + term
        normal2, scale2 = normalise(middle[m])
        vec[V_GAIN2 : V_GAIN2 + 1, :] += column_sum(total * normal2)
        vec[V_SHIFT2 : V_SHIFT2 + 1, :] += column_sum(total)
        gmid[...] = go[...] + norm_backward(total, normal2, scale2, gains[1:2, :])
        s_gbr[slot] = gmid[...].astype(BF16)
        gbr = s_gbr[slot]
        vec[V_BRANCH : V_BRANCH + 1, :] += column_sum(gbr.astype(F32))
        gmix = dot_nt(gbr, out_w[...]).astype(BF16)
        for r in range(GROUP):
            rows = slice(r * ROW, (r + 1) * ROW)
            for p in range(pairs):
                lanes = slice(p * ROW, (p + 1) * ROW)
                klanes = slice(width + p * ROW, width + (p + 1) * ROW)
                vlanes = slice(2 * width + p * ROW, 2 * width + (p + 1) * ROW)
                gm = stack_pair(gmix[rows, lanes], lane_low)
                q = stack_pair(proj[m, rows, lanes], lane_low)
                k = proj[m, rows, klanes]
                v = proj[m, rows, vlanes]
                weights = probs[m, r * pairs + p]
                gp = dot_nt(gm, v)
                wf = weights.astype(F32)
                inner = jnp.sum(wf * gp, axis=-1, keepdims=True)
                gsc = (wf * (gp - inner)).astype(BF16)
                gq = join_pair(dot(gsc, k), lane_low) * (ROW // 2) ** -0.5
                s_gproj[slot, rows, lanes] = gq.astype(BF16)
                s_gproj[slot, rows, klanes] = dot_tn(gsc, q).astype(BF16)
                s_gproj[slot, rows, vlanes] = dot_tn(weights, gm).astype(BF16)
        for copy in saves_backward(m):
            copy.start()
        gproj = s_gproj[slot]
        vec[V_QUERY : V_QUERY + 1, :] += column_sum(gproj[:, 0:width].astype(F32))
        vec[V_VALUE : V_VALUE + 1, :] += column_sum(gproj[:, 2 * width : 3 * width].astype(F32))
        gnormed = dot_nt(gproj, qkv_w[...])
        normal, scale = normalise(instream[m].astype(F32))
        vec[V_GAIN1 : V_GAIN1 + 1, :] += column_sum(gnormed * normal)
        vec[V_SHIFT1 : V_SHIFT1 + 1, :] += column_sum(gnormed)
        gs[m] = (gmid[...] + norm_backward(gnormed, normal, scale, gains[0:1, :])).astype(BF16)

        @pl.when(is_first)
        def _():
            save(9, gs.at[m], xr_o, m).start()

        @pl.when(jnp.logical_not(is_first))
        def _():
            backward_copy(m).start()

    def tick(t, carry):
        m_forward = t - stage
        m_backward = t - (2 * (stages - 1) - stage)

        @pl.when((m_forward >= 0) & (m_forward < micros))
        def _():
            forward(m_forward)

        @pl.when((m_backward >= 0) & (m_backward < micros))
        def _():
            @pl.when(is_last)
            def _():
                head(m_backward)

            backward(m_backward)

        return carry

    lax.fori_loop(0, micros + 2 * (stages - 1), tick, 0)

    for m in range(micros):
        for copy in saves_forward(m):
            copy.wait()

        @pl.when(jnp.logical_not(is_last))
        def _():
            forward_copy(m).wait_send()

        @pl.when(jnp.logical_not(is_first))
        def _():
            backward_copy(m).wait_send()

        @pl.when(is_first)
        def _():
            save(9, gs.at[m], xr_o, m).wait()

        @pl.when(is_last)
        def _():
            save(9, outb.at[m], xr_o, m).wait()

    for m in range(max(0, micros - 2), micros):
        for copy in saves_backward(m):
            copy.wait()

        @pl.when(is_first | is_last)
        def _():
            save_xl(m).wait()


def run_pipeline(stages, ids, seg_rows, params):
    embed, qkv_w, qv_b, out_w, out_b, in_w, in_b, down_w, gains, shifts, fg, fb, head_w = params
    width = embed.shape[1]
    vocab = head_w.shape[0]
    hid = in_w.shape[1]
    tokens = GROUP * ROW
    micros = ids.shape[0] // tokens
    pairs = width // ROW
    vmem = pl.BlockSpec(memory_space=pltpu.VMEM)
    hbm = pl.BlockSpec(memory_space=pl.ANY)

    def kept(columns):
        return jax.ShapeDtypeStruct((micros, tokens, columns), BF16)

    def scratch(lead, columns, kind=BF16):
        return pltpu.VMEM((lead, tokens, columns), kind)

    out_shape = [
        kept(width),
        kept(width),
        kept(width),
        kept(hid),
        kept(width),
        kept(hid),
        kept(width),
        kept(3 * width),
        kept(vocab),
        kept(width),
        jax.ShapeDtypeStruct((VEC_ROWS, width), F32),
    ]
    return pl.pallas_call(
        functools.partial(pipeline_kernel, stages, micros),
        out_shape=out_shape,
        in_specs=[vmem] * 15,
        out_specs=[hbm] * 10 + [vmem],
        scratch_shapes=[
            scratch(micros, width),
            scratch(micros, width),
            scratch(micros, width),
            scratch(micros, width),
            scratch(micros, width),
            scratch(micros, 3 * width),
            pltpu.VMEM((micros, GROUP * pairs, 2 * ROW, ROW), BF16),
            scratch(micros, width),
            scratch(micros, width, F32),
            scratch(micros, width),
            scratch(micros, hid, F32),
            pltpu.VMEM((tokens, width), F32),
            pltpu.VMEM((tokens, width), F32),
            pltpu.VMEM((tokens, width), F32),
            scratch(2, hid),
            scratch(2, width),
            scratch(2, hid),
            scratch(2, width),
            scratch(2, 3 * width),
            scratch(2, vocab),
            pltpu.SemaphoreType.DMA((micros,)),
            pltpu.SemaphoreType.DMA((micros,)),
            pltpu.SemaphoreType.DMA((micros,)),
            pltpu.SemaphoreType.DMA((micros,)),
            pltpu.SemaphoreType.DMA((10, micros)),
        ],
        compiler_params=pltpu.CompilerParams(
            collective_id=0, has_side_effects=True, vmem_limit_bytes=62 * 1024 * 1024
        ),
        name="pipeline",
    )(ids, seg_rows, embed, qkv_w, qv_b, out_w, out_b, in_w, in_b, down_w, gains, shifts, fg, fb, head_w)


def line_dims(devices):
    dims, stride = [], 1
    if devices == 8:
        return [(2, 1), (4, 2)]
    while devices > 1:
        size = 4 if devices % 4 == 0 else 2
        dims.append((size, stride))
        stride *= size
        devices //= size
    return dims


def chunk_plan(width, hid, vocab, stages, devices):
    slim, deep = width // devices, hid // devices
    plan = []
    for c in range(2):
        plan.append(("down", c, (deep, width // 2)))
    plan.append(("extra", 0, (stages, vocab // (stages * devices), width)))
    for c in range(hid // width):
        plan.append(("in", c, (slim, width)))
    plan.append(("out", 0, (slim, width)))
    for c in range(3):
        plan.append(("qkv", c, (slim, width)))
    return plan


def gradient_kernel(stages, devices, plan, *refs):
    dims = line_dims(devices)
    refs = list(refs)

    def take(amount):
        head, refs[:] = refs[:amount], refs[amount:]
        return head

    inputs = take(10)
    vec_in = take(1)[0]
    qkv_out, out_out, in_out, down_out, embed_out, head_out, vec_out = take(7)
    local = take(10)
    in_sem = take(1)[0]
    mats = dict(
        zip(
            ("normed", "mixed", "normed2", "active", "gres", "ghid", "gbr", "gproj", "xl", "xr"),
            local,
        )
    )
    names = list(mats)
    stage = lax.axis_index("pipe")
    place = lax.axis_index("dp")
    is_extra = (stage == 0) | (stage == stages - 1)
    width = mats["normed"].shape[1]
    where = [lax.rem(place // stride, size) for size, stride in dims]

    barrier = pltpu.get_barrier_semaphore()

    def greet(offset, carry):
        peer = lax.rem(place + offset, devices)
        pl.semaphore_signal(barrier, inc=1, device_id={"dp": peer}, device_id_type=MESH)
        return carry

    def greet_stage(offset, carry):
        peer = lax.rem(stage + offset, stages)
        pl.semaphore_signal(barrier, inc=1, device_id={"pipe": peer}, device_id_type=MESH)
        return carry

    lax.fori_loop(1, devices, greet, 0)
    lax.fori_loop(1, stages, greet_stage, 0)

    def load(name):
        i = names.index(name)
        return pltpu.make_async_copy(inputs[i], mats[name], in_sem.at[i])

    order = ["gres", "active", "normed2", "ghid", "mixed", "gbr", "normed", "gproj"]
    for name in order[:2]:
        load(name).start()

    @pl.when(is_extra)
    def _():
        load("xl").start()
        load("xr").start()

    for name in order[2:]:
        load(name).start()

    pl.semaphore_wait(barrier, devices - 1 + stages - 1)
    loaded = set()

    def need(*wanted):
        for name in wanted:
            if name not in loaded:
                loaded.add(name)
                load(name).wait()

    bits = devices.bit_length() - 1
    vec_send, vec_recv = take(2)
    vec_sems = take(2)

    def vec_copy(k):
        peer = jnp.bitwise_xor(place, 1 << k)
        return pltpu.make_async_remote_copy(
            src_ref=vec_send.at[k],
            dst_ref=vec_recv.at[k],
            send_sem=vec_sems[0].at[k],
            recv_sem=vec_sems[1].at[k],
            device_id={"dp": peer},
            device_id_type=MESH,
        )

    def vec_step(k):
        def run():
            if k == 0:
                vec_send[0] = vec_in[...]
            else:
                vec_copy(k - 1).wait_recv()
                vec_send[k] = vec_send[k - 1] + vec_recv[k - 1]
            if k < bits:
                vec_copy(k).start()

        return run

    final_send, final_recv = take(2)
    final_sems = take(2)

    def final_copy(offset):
        peer = lax.rem(stages - 1 + offset, stages)
        return pltpu.make_async_remote_copy(
            src_ref=final_send,
            dst_ref=final_recv,
            send_sem=final_sems[0].at[offset],
            recv_sem=final_sems[1].at[0],
            device_id={"pipe": peer},
            device_id_type=MESH,
        )

    def vec_last():
        vec_step(bits)()
        vec_out[...] = vec_send[bits]

        @pl.when(stage == stages - 1)
        def _():
            final_send[...] = vec_send[bits, 8:16, :]
            for offset in range(1, stages):
                final_copy(offset).start()

    def vec_finish():
        @pl.when(stage != stages - 1)
        def _():
            final_copy(1).wait_recv()
            vec_out[V_FINAL_GAIN : V_FINAL_BIAS + 1, :] = final_recv[
                V_FINAL_GAIN - 8 : V_FINAL_BIAS - 7, :
            ]

    def vec_drain():
        for k in range(bits):
            vec_copy(k).wait_send()

        @pl.when(stage == stages - 1)
        def _():
            for offset in range(1, stages):
                final_copy(offset).wait_send()

    extra_sum, extra_send_sem, extra_recv_sem = take(3)

    def extra_copy(source, offset, target):
        peer = lax.rem(source + offset, stages)
        return pltpu.make_async_remote_copy(
            src_ref=extra_sum.at[peer],
            dst_ref=target,
            send_sem=extra_send_sem.at[offset],
            recv_sem=extra_recv_sem.at[0 if source == 0 else 1],
            device_id={"pipe": peer},
            device_id_type=MESH,
        )

    def chunk_steps(kind, c, block):
        full = take(1)[0]

        def compute():
            if kind == "down":
                need("gres", "active")
                half = width // 2

                def body(i, carry):
                    depth = block[0]
                    lanes = pl.ds(pl.multiple_of(i * 256, 256), 256)
                    part = dot_tn(mats["active"][:, lanes], mats["gres"][:, c * half : (c + 1) * half])
                    per = 256 // depth
                    put_blocks(full, i, per, part.astype(BF16).reshape((per,) + block))
                    return carry

                lax.fori_loop(0, mats["active"].shape[1] // 256, body, 0)
            elif kind == "extra":
                load("xl").wait()
                load("xr").wait()
                rows = mats["xl"].shape[1] // stages
                for p in range(stages):
                    part = dot_tn(mats["xl"][:, p * rows : (p + 1) * rows], mats["xr"][...])
                    part = part.astype(BF16).reshape((devices,) + block[1:])
                    for d in range(devices):
                        full[split(d) + (p,)] = part[d]
            else:
                left, right = {
                    "in": ("normed2", "ghid"),
                    "out": ("mixed", "gbr"),
                    "qkv": ("normed", "gproj"),
                }[kind]
                need(left, right)
                cols = slice(c * width, (c + 1) * width)

                def body(i, carry):
                    lanes = pl.ds(pl.multiple_of(i * 128, 128), 128)
                    part = dot_tn(mats[left][:, lanes], mats[right][:, cols])
                    per = 128 // block[0]
                    put_blocks(full, i, per, part.astype(BF16).reshape((per,) + block))
                    return carry

                lax.fori_loop(0, width // 128, body, 0)

        def split(d):
            return tuple((d // stride) % size for size, stride in reversed(dims))

        def put_blocks(ref, i, per, values):
            for q in range(per):
                d = i * per + q
                index = tuple(lax.rem(d // stride, size) for size, stride in reversed(dims))
                ref[index] = values[q]

        steps = [[compute]]
        for phase, (size, _) in enumerate(dims):
            buffers = take(3)
            steps[-1].append(functools.partial(line_step, phase, size, 1, full, buffers))
            for t in range(2, size):
                steps.append([functools.partial(line_step, phase, size, t, full, buffers)])
            drains.append((kind, functools.partial(line_drain, phase, size, full, buffers)))
            steps.append([functools.partial(line_final, kind, c, phase, size, full, buffers)])
        if kind == "extra":
            steps = [[gated(step)] for step in steps]
        return steps

    def gated(step):
        def run():
            @pl.when(is_extra)
            def _():
                for part in step:
                    part()

        return run

    def block_of(full, phase, j):
        later = [slice(None)] * (len(dims) - 1 - phase)
        return full.at[tuple(later + [j] + where[:phase][::-1])]

    def line_copy(phase, size, t, side, full, buffers):
        recv, ssem, rsem = buffers
        i = where[phase]
        stride = dims[phase][1]
        if side == 0:
            j, peer = size - t + i, place + jnp.where(i < size - 1, stride, 0)
        else:
            j, peer = t - size + i, place - jnp.where(i > 0, stride, 0)
        return pltpu.make_async_remote_copy(
            src_ref=block_of(full, phase, jnp.clip(j, 0, size - 1)),
            dst_ref=recv.at[0 if size == 2 else side, t - 1],
            send_sem=ssem.at[side, t - 1],
            recv_sem=rsem.at[side, t - 1],
            device_id={"dp": peer},
            device_id_type=MESH,
        )

    def sends(i, size, t, side):
        return (i <= t - 1) if side == 0 else (i >= size - t)

    def line_step(phase, size, t, full, buffers):
        i = where[phase]
        for side in range(2):
            at_end = (i == 0) if side == 0 else (i == size - 1)
            j = size - t + i if side == 0 else t - size + i
            j = jnp.clip(j, 0, size - 1)

            @pl.when(sends(i, size, t, side))
            def _():
                if t > 1:
                    @pl.when(jnp.logical_not(at_end))
                    def _():
                        line_copy(phase, size, t - 1, side, full, buffers).wait_recv()
                        own = block_of(full, phase, j)
                        got = buffers[0][0 if size == 2 else side, t - 2]
                        own[...] = (own[...].astype(F32) + got.astype(F32)).astype(BF16)

                line_copy(phase, size, t, side, full, buffers).start()

    def line_final(kind, c, phase, size, full, buffers):
        i = where[phase]
        own = block_of(full, phase, i)
        total = own
        if phase == len(dims) - 1:
            slots = {
                "qkv": lambda: qkv_out.at[:, c * width : (c + 1) * width],
                "in": lambda: in_out.at[:, c * width : (c + 1) * width],
                "out": lambda: out_out,
                "down": lambda: down_out.at[:, c * (width // 2) : (c + 1) * (width // 2)],
                "extra": lambda: extra_sum,
            }
            total = slots[kind]()
        lower, upper = i > 0, i < size - 1

        def arrived(side):
            line_copy(phase, size, size - 1, side, full, buffers).wait_recv()
            return buffers[0][0 if size == 2 else side, size - 2].astype(F32)

        @pl.when(lower & upper)
        def _():
            total[...] = (own[...].astype(F32) + arrived(0) + arrived(1)).astype(total.dtype)

        @pl.when(lower & jnp.logical_not(upper))
        def _():
            total[...] = (own[...].astype(F32) + arrived(0)).astype(total.dtype)

        @pl.when(jnp.logical_not(lower))
        def _():
            total[...] = (own[...].astype(F32) + arrived(1)).astype(total.dtype)

        if phase == len(dims) - 1 and kind == "extra":
            for source_stage, out in ((0, embed_out), (stages - 1, head_out)):
                @pl.when(stage == source_stage)
                def _():
                    for offset in range(1, stages):
                        extra_copy(source_stage, offset, extra_recv[0 if source_stage == 0 else 1]).start()
                    out[...] = extra_sum[source_stage]

    def line_drain(phase, size, full, buffers):
        i = where[phase]
        for side in range(2):
            for t in range(1, size):
                @pl.when(sends(i, size, t, side))
                def _():
                    line_copy(phase, size, t, side, full, buffers).wait_send()

    extra_recv = take(2)
    drains = []
    chains = [chunk_steps(*item) for item in plan]
    depth = len(chains[0])
    vec_chain = [vec_step(k) for k in range(bits)] + [vec_last]
    for r in range(len(chains) + depth - 1):
        for d in range(depth):
            if 0 <= r - d < len(chains):
                for part in chains[r - d][d]:
                    part()
        if r < len(vec_chain):
            vec_chain[r]()
    vec_finish()
    for source_stage, out in ((0, embed_out), (stages - 1, head_out)):
        @pl.when(stage != source_stage)
        def _():
            got = extra_recv[0 if source_stage == 0 else 1]
            extra_copy(source_stage, 1, got).wait_recv()
            out[...] = got[...]

        @pl.when(stage == source_stage)
        def _():
            for offset in range(1, stages):
                extra_copy(source_stage, offset, extra_recv[0]).wait_send()

    vec_drain()
    for kind, drain in drains:
        if kind == "extra":
            gated([drain])()
        else:
            drain()


def run_gradients(stages, devices, saved, vec):
    dims = line_dims(devices)
    micros, tokens, width = saved[0].shape
    hid, vocab = saved[3].shape[2], saved[8].shape[2]
    plan = chunk_plan(width, hid, vocab, stages, devices)
    saved = [member.reshape(micros * tokens, member.shape[2]) for member in saved]
    vmem = pl.BlockSpec(memory_space=pltpu.VMEM)
    hbm = pl.BlockSpec(memory_space=pl.ANY)
    bits = devices.bit_length() - 1
    share = vocab // (stages * devices)
    scratch = [pltpu.VMEM(member.shape, BF16) for member in saved]
    scratch += [pltpu.SemaphoreType.DMA((len(saved),))]
    scratch += [
        pltpu.VMEM((bits + 1,) + vec.shape, F32),
        pltpu.VMEM((bits,) + vec.shape, F32),
        pltpu.SemaphoreType.DMA((bits,)),
        pltpu.SemaphoreType.DMA((bits,)),
        pltpu.VMEM((8, width), F32),
        pltpu.VMEM((8, width), F32),
        pltpu.SemaphoreType.DMA((stages,)),
        pltpu.SemaphoreType.DMA((1,)),
        pltpu.VMEM((stages, share, width), F32),
        pltpu.SemaphoreType.DMA((stages,)),
        pltpu.SemaphoreType.DMA((2,)),
        pltpu.VMEM((share, width), F32),
        pltpu.VMEM((share, width), F32),
    ]
    sizes = [size for size, _ in reversed(dims)]
    for _, _, block in plan:
        scratch.append(pltpu.VMEM(tuple(sizes) + block, BF16))
        for phase, (size, _) in enumerate(dims):
            piece = tuple(sizes[: len(dims) - 1 - phase]) + block
            scratch.append(pltpu.VMEM((1 if size == 2 else 2, size - 1) + piece, BF16))
            scratch += [pltpu.SemaphoreType.DMA((2, size - 1))] * 2
    return pl.pallas_call(
        functools.partial(gradient_kernel, stages, devices, plan),
        out_shape=[
            jax.ShapeDtypeStruct((width // devices, 3 * width), F32),
            jax.ShapeDtypeStruct((width // devices, width), F32),
            jax.ShapeDtypeStruct((width // devices, hid), F32),
            jax.ShapeDtypeStruct((hid // devices, width), F32),
            jax.ShapeDtypeStruct((share, width), F32),
            jax.ShapeDtypeStruct((share, width), F32),
            jax.ShapeDtypeStruct(vec.shape, F32),
        ],
        in_specs=[hbm] * len(saved) + [vmem],
        out_specs=[vmem] * 7,
        scratch_shapes=scratch,
        compiler_params=pltpu.CompilerParams(
            collective_id=1, has_side_effects=True, vmem_limit_bytes=62 * 1024 * 1024
        ),
        name="gradients",
    )(*saved, vec)


def on_device(
    token_ids,
    segment_ids,
    target_ids,
    embed_table,
    qkv_weight,
    qv_bias,
    out_weight,
    out_biases,
    ff_in,
    ff_in_bias,
    ff_out,
    norm_gains,
    norm_biases,
    final_gain,
    final_bias,
    head_weight,
):
    stages = lax.axis_size("pipe")
    devices = lax.axis_size("dp")
    place = lax.axis_index("dp")
    rows, seq = token_ids.shape
    width = embed_table.shape[1]

    def padded(values):
        return jnp.pad(values, ((0, 0), (0, ROW - seq)), constant_values=-1)

    limit = (jnp.arange(ROW, dtype=jnp.int32) // FRAME + 1) * FRAME
    limit = jnp.broadcast_to(limit, (rows, ROW))
    seg_rows = padded(segment_ids)
    ids = jnp.stack([padded(token_ids), seg_rows, padded(target_ids), limit], axis=-1)
    ids = ids.reshape(rows * ROW, 4)
    params = (
        embed_table,
        qkv_weight[0],
        qv_bias[0],
        out_weight[0],
        out_biases[0],
        ff_in[0],
        ff_in_bias,
        ff_out[0],
        norm_gains[0],
        norm_biases[0],
        final_gain[None],
        final_bias[None],
        head_weight,
    )
    *saved, vec = run_pipeline(stages, ids, seg_rows, params)
    qkv_g, out_g, in_g, down_g, embed_g, head_g, sums = run_gradients(stages, devices, saved, vec)
    lanes = width // devices

    def shard(first):
        return lax.dynamic_slice(sums, (first, place * lanes), (2, lanes))[None]

    hidden_sum = sums[V_HIDDEN : V_HIDDEN + ff_in_bias.shape[1] // width].reshape(-1)
    share = hidden_sum.shape[0] // devices
    return (
        embed_g,
        qkv_g[None],
        shard(V_QUERY),
        out_g[None],
        shard(V_BRANCH),
        in_g[None],
        lax.dynamic_slice(hidden_sum, (place * share,), (share,))[None],
        down_g[None],
        shard(V_GAIN1),
        shard(V_SHIFT1),
        sums[V_FINAL_GAIN],
        sums[V_FINAL_BIAS],
        head_g,
    )


def solution(mesh):
    layer3 = P("pipe", None, None)
    return jax.shard_map(
        on_device,
        mesh=mesh,
        in_specs=(
            P("dp", None),
            P("dp", None),
            P("dp", None),
            P(),
            layer3,
            layer3,
            layer3,
            layer3,
            layer3,
            P("pipe", None),
            layer3,
            layer3,
            layer3,
            P(),
            P(),
            P(),
        ),
        out_specs=(
            P(("pipe", "dp"), None),
            P("pipe", "dp", None),
            P("pipe", None, "dp"),
            P("pipe", "dp", None),
            P("pipe", None, "dp"),
            P("pipe", "dp", None),
            P("pipe", "dp"),
            P("pipe", "dp", None),
            P("pipe", None, "dp"),
            P("pipe", None, "dp"),
            P(),
            P(),
            P(("pipe", "dp"), None),
        ),
        check_vma=False,
    )
```

```python
import functools

import jax
import jax.numpy as jnp
from jax import lax
from jax.experimental import pallas as pl
from jax.experimental.pallas import tpu as pltpu
from jax.sharding import PartitionSpec as P

HEADS = 8
FRAME = 6
ROW = 128
GROUP = 2
MASKED = -1e30
GELU_A = 0.7978845608
GELU_B = 0.044715
MESH = pl.DeviceIdType.MESH
F32 = jnp.float32
BF16 = jnp.bfloat16

VEC_ROWS = 16
V_QUERY, V_VALUE, V_BRANCH, V_RESULT, V_GAIN1, V_GAIN2, V_SHIFT1, V_SHIFT2 = range(8)
V_HIDDEN = 8
V_FINAL_GAIN, V_FINAL_BIAS = 12, 13


def dot(a, b):
    return lax.dot_general(a, b, (((1,), (0,)), ((), ())), preferred_element_type=F32)


def dot_nt(a, b):
    return lax.dot_general(a, b, (((1,), (1,)), ((), ())), preferred_element_type=F32)


def dot_tn(a, b):
    return lax.dot_general(a, b, (((0,), (0,)), ((), ())), preferred_element_type=F32)


def normalise(values):
    centre = jnp.mean(values, axis=-1, keepdims=True)
    centered = values - centre
    spread = jnp.mean(centered * centered, axis=-1, keepdims=True)
    scale = lax.rsqrt(spread + 1e-05)
    return centered * scale, scale


def norm_backward(grad, normal, scale, gain):
    grad_n = grad * gain
    mean_grad = jnp.mean(grad_n, axis=-1, keepdims=True)
    mean_proj = jnp.mean(grad_n * normal, axis=-1, keepdims=True)
    return scale * (grad_n - mean_grad - normal * mean_proj)


def column_sum(values):
    return jnp.sum(values, axis=0, keepdims=True)


def stack_pair(pair, low_lanes):
    zero = jnp.zeros_like(pair)
    return jnp.concatenate(
        [jnp.where(low_lanes, pair, zero), jnp.where(low_lanes, zero, pair)], axis=0
    )


def join_pair(stacked, low_lanes):
    half = stacked.shape[0] // 2
    return jnp.where(low_lanes, stacked[:half], stacked[half:])


def pipeline_kernel(
    stages,
    micros,
    token_ids,
    segment_ids,
    target_ids,
    embed,
    qkv_w,
    qv_b,
    out_w,
    out_b,
    in_w,
    in_b,
    down_w,
    gains,
    shifts,
    fin_gain,
    fin_bias,
    head_w,
    normed_o,
    mixed_o,
    normed2_o,
    active_o,
    gres_o,
    ghid_o,
    gbr_o,
    gproj_o,
    xl_o,
    xr_o,
    vec,
    instream,
    outb,
    gin,
    gs,
    normed,
    proj,
    probs,
    mixed,
    middle,
    normed2,
    active,
    slope,
    lo,
    go,
    gmid,
    s_gres,
    s_ghid,
    s_gbr,
    s_gproj,
    s_xl,
    ids,
    frames,
    fsend,
    frecv,
    bsend,
    brecv,
    osem,
):
    stage = lax.axis_index("pipe")
    tokens, width = instream.shape[1], instream.shape[2]
    hidden_n = in_b.shape[1]
    vocab = head_w.shape[0]
    pairs = width // ROW
    chunk = 512
    is_first = stage == 0
    is_last = stage == stages - 1
    up = jnp.minimum(stage + 1, stages - 1)
    down = jnp.maximum(stage - 1, 0)

    barrier = pltpu.get_barrier_semaphore()

    @pl.when(jnp.logical_not(is_first))
    def _():
        pl.semaphore_signal(barrier, inc=1, device_id={"pipe": down}, device_id_type=MESH)

    @pl.when(jnp.logical_not(is_last))
    def _():
        pl.semaphore_signal(barrier, inc=1, device_id={"pipe": up}, device_id_type=MESH)

    pl.semaphore_wait(barrier, jnp.where(is_first | is_last, 1, 2))
    vec[...] = jnp.zeros_like(vec)
    rows_n, seq = token_ids.shape
    for index, member in enumerate((token_ids, segment_ids, target_ids)):
        ids[index] = jnp.full(ids.shape[1:], 4.0 if index == 1 else -1.0, F32)
        ids[index, 0:rows_n, 0:seq] = member[...].astype(F32)
    at_query = lax.broadcasted_iota(jnp.int32, (ROW, ROW), 0)
    at_key = lax.broadcasted_iota(jnp.int32, (ROW, ROW), 1)
    frames[...] = jnp.where(at_key < ((at_query * 43) // 256) * FRAME + FRAME, 1.0, 0.0)

    def column(index, row):
        values = jnp.broadcast_to(ids[index, pl.ds(row, 1), :], (8, ROW))
        return values.T[:, 0:1]

    def hot_rows(index, m):
        parts = [column(index, m * GROUP + r) for r in range(GROUP)]
        values = jnp.concatenate(parts, axis=0)
        places = lax.broadcasted_iota(jnp.int32, (tokens, vocab), 1).astype(F32)
        return values, jnp.where(values == places, 1.0, 0.0)

    def forward_copy(m):
        return pltpu.make_async_remote_copy(
            src_ref=outb.at[m],
            dst_ref=instream.at[m],
            send_sem=fsend.at[m],
            recv_sem=frecv.at[m],
            device_id={"pipe": up},
            device_id_type=MESH,
        )

    def backward_copy(m):
        return pltpu.make_async_remote_copy(
            src_ref=gs.at[m],
            dst_ref=gin.at[m],
            send_sem=bsend.at[m],
            recv_sem=brecv.at[m],
            device_id={"pipe": down},
            device_id_type=MESH,
        )

    def save(index, src, dst, m):
        return pltpu.make_async_copy(src, dst.at[m], osem.at[index, m])

    def saves_forward(m):
        return [
            save(0, normed.at[m], normed_o, m),
            save(1, mixed.at[m], mixed_o, m),
            save(2, normed2.at[m], normed2_o, m),
            save(3, active.at[m], active_o, m),
        ]

    def saves_backward(m):
        slot = lax.rem(m, 2)
        return [
            save(4, s_gres.at[slot], gres_o, m),
            save(5, s_ghid.at[slot], ghid_o, m),
            save(6, s_gbr.at[slot], gbr_o, m),
            save(7, s_gproj.at[slot], gproj_o, m),
        ]

    def save_xl(m):
        return save(8, s_xl.at[lax.rem(m, 2)], xl_o, m)

    def put_xl(m, value):
        @pl.when(m >= 2)
        def _():
            save_xl(m - 2).wait()

        s_xl[lax.rem(m, 2)] = value
        save_xl(m).start()

    lane_low = lax.broadcasted_iota(jnp.int32, (ROW, ROW), 1) < ROW // 2

    def forward(m):
        @pl.when(is_first)
        def _():
            hot = hot_rows(0, m)[1].astype(BF16)
            put_xl(m, hot)
            instream[m] = dot(hot, embed[...]).astype(BF16)

        @pl.when(jnp.logical_not(is_first))
        def _():
            forward_copy(m).wait_recv()

        normal, _ = normalise(instream[m].astype(F32))
        normed[m] = (normal * gains[0:1, :] + shifts[0:1, :]).astype(BF16)
        low = normed[m]
        queries = dot(low, qkv_w[:, 0:width]) + qv_b[0:1, :]
        proj[m, :, 0:width] = (queries * (ROW // 2) ** -0.5).astype(BF16)
        proj[m, :, width : 2 * width] = dot(low, qkv_w[:, width : 2 * width]).astype(BF16)
        proj[m, :, 2 * width : 3 * width] = (
            dot(low, qkv_w[:, 2 * width : 3 * width]) + qv_b[1:2, :]
        ).astype(BF16)
        for r in range(GROUP):
            rows = slice(r * ROW, (r + 1) * ROW)
            kinds = lax.broadcasted_iota(jnp.int32, (16, ROW), 0).astype(F32)
            member = jnp.where(ids[1, pl.ds(m * GROUP + r, 1), :] == kinds, 1.0, 0.0).astype(BF16)
            mask = jnp.where(dot_tn(member, member) * frames[...] > 0.5, 0.0, MASKED)
            for p in range(pairs):
                lanes = slice(p * ROW, (p + 1) * ROW)
                q = stack_pair(proj[m, rows, lanes], lane_low)
                k = proj[m, rows, width + p * ROW : width + (p + 1) * ROW]
                v = proj[m, rows, 2 * width + p * ROW : 2 * width + (p + 1) * ROW]
                scores = dot_nt(q, k).reshape(2, ROW, ROW)
                scores = scores + mask[None]
                top = jnp.max(scores, axis=-1, keepdims=True)
                expo = jnp.exp(scores - top)
                total = jnp.sum(expo, axis=-1, keepdims=True)
                weights = (expo * (1.0 / total)).astype(BF16).reshape(2 * ROW, ROW)
                probs[m, r * pairs + p] = weights
                mixed[m, rows, lanes] = join_pair(dot(weights, v), lane_low).astype(BF16)
        mid = instream[m].astype(F32) + (dot(mixed[m], out_w[...]) + out_b[0:1, :])
        middle[m] = mid
        normal2, _ = normalise(mid)
        normed2[m] = (normal2 * gains[1:2, :] + shifts[1:2, :]).astype(BF16)
        low2 = normed2[m]
        total = None
        for c in range(hidden_n // chunk):
            cols = slice(c * chunk, (c + 1) * chunk)
            hid = dot(low2, in_w[:, cols]) + in_b[0:1, cols]
            square = hid * hid
            tan = jnp.tanh(hid * (GELU_A + (GELU_A * GELU_B) * square))
            half = 0.5 + 0.5 * tan
            act = (hid * half).astype(BF16)
            active[m, :, cols] = act
            rise = (1.0 - tan * tan) * (0.5 * GELU_A + (1.5 * GELU_A * GELU_B) * square)
            slope[m, :, cols] = (half + hid * rise).astype(BF16)
            term = dot(act, down_w[cols, :])
            total = term if total is None else total + term
        for copy in saves_forward(m):
            copy.start()
        lo[...] = middle[m] + (total + out_b[1:2, :])

        @pl.when(jnp.logical_not(is_last))
        def _():
            outb[m] = lo[...].astype(BF16)
            forward_copy(m).start()

    def head(m):
        normal, scale = normalise(lo[...])
        outb[m] = (normal * fin_gain[...] + fin_bias[...]).astype(BF16)
        save(9, outb.at[m], xr_o, m).start()
        logits = dot_nt(outb[m], head_w[...])
        top = jnp.max(logits, axis=-1, keepdims=True)
        expo = jnp.exp(logits - top)
        total = jnp.sum(expo, axis=-1, keepdims=True)
        target, hot = hot_rows(2, m)
        grad_logits = jnp.where(target >= 0.0, expo * (1.0 / total) - hot, 0.0).astype(BF16)
        put_xl(m, grad_logits)
        grad_final = dot(grad_logits, head_w[...])
        vec[V_FINAL_GAIN : V_FINAL_GAIN + 1, :] += column_sum(grad_final * normal)
        vec[V_FINAL_BIAS : V_FINAL_BIAS + 1, :] += column_sum(grad_final)
        go[...] = norm_backward(grad_final, normal, scale, fin_gain[...])

    def backward(m):
        slot = lax.rem(m, 2)

        @pl.when(m >= 2)
        def _():
            for copy in saves_backward(m - 2):
                copy.wait()

        @pl.when(jnp.logical_not(is_last))
        def _():
            backward_copy(m).wait_recv()
            go[...] = gin[m].astype(F32)

        s_gres[slot] = go[...].astype(BF16)
        gres = s_gres[slot]
        total = None
        for c in range(hidden_n // chunk):
            cols = slice(c * chunk, (c + 1) * chunk)
            gact = dot_nt(gres, down_w[cols, :])
            ghid = (gact * slope[m, :, cols].astype(F32)).astype(BF16)
            s_ghid[slot, :, cols] = ghid
            term = dot_nt(ghid, in_w[:, cols])
            total = term if total is None else total + term
        normal2, scale2 = normalise(middle[m])
        vec[V_GAIN2 : V_GAIN2 + 1, :] += column_sum(total * normal2)
        vec[V_SHIFT2 : V_SHIFT2 + 1, :] += column_sum(total)
        gmid[...] = go[...] + norm_backward(total, normal2, scale2, gains[1:2, :])
        s_gbr[slot] = gmid[...].astype(BF16)
        gbr = s_gbr[slot]
        gmix = dot_nt(gbr, out_w[...]).astype(BF16)
        for r in range(GROUP):
            rows = slice(r * ROW, (r + 1) * ROW)
            for p in range(pairs):
                lanes = slice(p * ROW, (p + 1) * ROW)
                klanes = slice(width + p * ROW, width + (p + 1) * ROW)
                vlanes = slice(2 * width + p * ROW, 2 * width + (p + 1) * ROW)
                gm = stack_pair(gmix[rows, lanes], lane_low)
                q = stack_pair(proj[m, rows, lanes], lane_low)
                k = proj[m, rows, klanes]
                v = proj[m, rows, vlanes]
                weights = probs[m, r * pairs + p]
                gp = dot_nt(gm, v)
                wf = weights.astype(F32)
                inner = jnp.sum(wf * gp, axis=-1, keepdims=True)
                gsc = (wf * (gp - inner)).astype(BF16)
                gq = join_pair(dot(gsc, k), lane_low) * (ROW // 2) ** -0.5
                s_gproj[slot, rows, lanes] = gq.astype(BF16)
                s_gproj[slot, rows, klanes] = dot_tn(gsc, q).astype(BF16)
                s_gproj[slot, rows, vlanes] = dot_tn(weights, gm).astype(BF16)
        for copy in saves_backward(m):
            copy.start()
        gproj = s_gproj[slot]
        gnormed = dot_nt(gproj, qkv_w[...])
        normal, scale = normalise(instream[m].astype(F32))
        vec[V_GAIN1 : V_GAIN1 + 1, :] += column_sum(gnormed * normal)
        vec[V_SHIFT1 : V_SHIFT1 + 1, :] += column_sum(gnormed)
        gs[m] = (gmid[...] + norm_backward(gnormed, normal, scale, gains[0:1, :])).astype(BF16)

        @pl.when(is_first)
        def _():
            save(9, gs.at[m], xr_o, m).start()

        @pl.when(jnp.logical_not(is_first))
        def _():
            backward_copy(m).start()

    def tick(t, carry):
        m_forward = t - stage
        m_backward = t - (2 * (stages - 1) - stage)

        @pl.when((m_forward >= 0) & (m_forward < micros))
        def _():
            forward(m_forward)

        @pl.when((m_backward >= 0) & (m_backward < micros))
        def _():
            @pl.when(is_last)
            def _():
                head(m_backward)

            backward(m_backward)

        return carry

    lax.fori_loop(0, micros + 2 * (stages - 1), tick, 0)

    for m in range(micros):
        for copy in saves_forward(m):
            copy.wait()

        @pl.when(jnp.logical_not(is_last))
        def _():
            forward_copy(m).wait_send()

        @pl.when(jnp.logical_not(is_first))
        def _():
            backward_copy(m).wait_send()

        @pl.when(is_first)
        def _():
            save(9, gs.at[m], xr_o, m).wait()

        @pl.when(is_last)
        def _():
            save(9, outb.at[m], xr_o, m).wait()

    for m in range(max(0, micros - 2), micros):
        for copy in saves_backward(m):
            copy.wait()

        @pl.when(is_first | is_last)
        def _():
            save_xl(m).wait()


def run_pipeline(stages, token_ids, segment_ids, target_ids, params):
    embed, in_w, head_w = params[0], params[5], params[12]
    width = embed.shape[1]
    vocab = head_w.shape[0]
    hid = in_w.shape[1]
    tokens = GROUP * ROW
    micros = token_ids.shape[0] // GROUP
    pairs = width // ROW
    vmem = pl.BlockSpec(memory_space=pltpu.VMEM)
    hbm = pl.BlockSpec(memory_space=pl.ANY)

    def kept(columns):
        return jax.ShapeDtypeStruct((micros, tokens, columns), BF16)

    def scratch(lead, columns, kind=BF16):
        return pltpu.VMEM((lead, tokens, columns), kind)

    out_shape = [
        kept(width),
        kept(width),
        kept(width),
        kept(hid),
        kept(width),
        kept(hid),
        kept(width),
        kept(3 * width),
        kept(vocab),
        kept(width),
        jax.ShapeDtypeStruct((VEC_ROWS, width), F32),
    ]
    return pl.pallas_call(
        functools.partial(pipeline_kernel, stages, micros),
        out_shape=out_shape,
        in_specs=[vmem] * 16,
        out_specs=[hbm] * 10 + [vmem],
        scratch_shapes=[
            scratch(micros, width),
            scratch(micros, width),
            scratch(micros, width),
            scratch(micros, width),
            scratch(micros, width),
            scratch(micros, 3 * width),
            pltpu.VMEM((micros, GROUP * pairs, 2 * ROW, ROW), BF16),
            scratch(micros, width),
            scratch(micros, width, F32),
            scratch(micros, width),
            scratch(micros, hid),
            scratch(micros, hid),
            pltpu.VMEM((tokens, width), F32),
            pltpu.VMEM((tokens, width), F32),
            pltpu.VMEM((tokens, width), F32),
            scratch(2, width),
            scratch(2, hid),
            scratch(2, width),
            scratch(2, 3 * width),
            scratch(2, vocab),
            pltpu.VMEM((3, 16, ROW), F32),
            pltpu.VMEM((ROW, ROW), F32),
            pltpu.SemaphoreType.DMA((micros,)),
            pltpu.SemaphoreType.DMA((micros,)),
            pltpu.SemaphoreType.DMA((micros,)),
            pltpu.SemaphoreType.DMA((micros,)),
            pltpu.SemaphoreType.DMA((10, micros)),
        ],
        compiler_params=pltpu.CompilerParams(
            collective_id=0, has_side_effects=True, vmem_limit_bytes=62 * 1024 * 1024
        ),
        name="pipeline",
    )(token_ids, segment_ids, target_ids, *params)


def line_dims(devices):
    dims, stride = [], 1
    if devices == 8:
        return [(2, 1), (4, 2)]
    while devices > 1:
        size = 4 if devices % 4 == 0 else 2
        dims.append((size, stride))
        stride *= size
        devices //= size
    return dims


def chunk_plan(width, hid, vocab, stages, devices):
    slim, deep = width // devices, hid // devices
    plan = []
    for c in range(2):
        plan.append(("down", c, (deep, width // 2)))
    plan.append(("extra", 0, (stages, vocab // (stages * devices), width)))
    for c in range(hid // width):
        plan.append(("in", c, (slim, width)))
    plan.append(("out", 0, (slim, width)))
    for c in range(3):
        plan.append(("qkv", c, (slim, width)))
    return plan


def gradient_kernel(stages, devices, plan, *refs):
    dims = line_dims(devices)
    refs = list(refs)

    def take(amount):
        head, refs[:] = refs[:amount], refs[amount:]
        return head

    inputs = take(10)
    vec_in = take(1)[0]
    qkv_out, out_out, in_out, down_out, embed_out, head_out, vec_out = take(7)
    local = take(10)
    in_sem = take(1)[0]
    mats = dict(
        zip(
            ("normed", "mixed", "normed2", "active", "gres", "ghid", "gbr", "gproj", "xl", "xr"),
            local,
        )
    )
    names = list(mats)
    stage = lax.axis_index("pipe")
    place = lax.axis_index("dp")
    is_extra = (stage == 0) | (stage == stages - 1)
    width = mats["normed"].shape[1]
    where = [lax.rem(place // stride, size) for size, stride in dims]

    barrier = pltpu.get_barrier_semaphore()

    def greet(offset, carry):
        peer = lax.rem(place + offset, devices)
        pl.semaphore_signal(barrier, inc=1, device_id={"dp": peer}, device_id_type=MESH)
        return carry

    def greet_stage(offset, carry):
        peer = lax.rem(stage + offset, stages)
        pl.semaphore_signal(barrier, inc=1, device_id={"pipe": peer}, device_id_type=MESH)
        return carry

    lax.fori_loop(1, devices, greet, 0)
    lax.fori_loop(1, stages, greet_stage, 0)

    def load(name):
        i = names.index(name)
        return pltpu.make_async_copy(inputs[i], mats[name], in_sem.at[i])

    order = ["gres", "active", "normed2", "ghid", "mixed", "gbr", "normed", "gproj"]
    for name in order[:2]:
        load(name).start()

    @pl.when(is_extra)
    def _():
        load("xl").start()
        load("xr").start()

    for name in order[2:]:
        load(name).start()

    pl.semaphore_wait(barrier, devices - 1 + stages - 1)
    loaded = set()

    def need(*wanted):
        for name in wanted:
            if name not in loaded:
                loaded.add(name)
                load(name).wait()

    bits = devices.bit_length() - 1
    vec_send, vec_recv = take(2)
    vec_sems = take(2)

    def vec_copy(k):
        peer = jnp.bitwise_xor(place, 1 << k)
        return pltpu.make_async_remote_copy(
            src_ref=vec_send.at[k],
            dst_ref=vec_recv.at[k],
            send_sem=vec_sems[0].at[k],
            recv_sem=vec_sems[1].at[k],
            device_id={"dp": peer},
            device_id_type=MESH,
        )

    def vec_step(k):
        def run():
            if k == 0:
                need("gres", "ghid", "gbr", "gproj")
                vec_send[0] = vec_in[...]
                ones = jnp.ones((16, mats["gres"].shape[0]), BF16)
                for name, start, row in (
                    ("gproj", 0, V_QUERY),
                    ("gproj", 2 * width, V_VALUE),
                    ("gbr", 0, V_BRANCH),
                    ("gres", 0, V_RESULT),
                ):
                    part = dot(ones, mats[name][:, start : start + width])
                    vec_send[0, row : row + 1, :] = part[0:1, :]
                for q in range(mats["ghid"].shape[1] // width):
                    part = dot(ones, mats["ghid"][:, q * width : (q + 1) * width])
                    vec_send[0, V_HIDDEN + q : V_HIDDEN + q + 1, :] = part[0:1, :]
            else:
                vec_copy(k - 1).wait_recv()
                vec_send[k] = vec_send[k - 1] + vec_recv[k - 1]
            if k < bits:
                vec_copy(k).start()

        return run

    final_send, final_recv = take(2)
    final_sems = take(2)

    def final_copy(offset):
        peer = lax.rem(stages - 1 + offset, stages)
        return pltpu.make_async_remote_copy(
            src_ref=final_send,
            dst_ref=final_recv,
            send_sem=final_sems[0].at[offset],
            recv_sem=final_sems[1].at[0],
            device_id={"pipe": peer},
            device_id_type=MESH,
        )

    def vec_last():
        vec_step(bits)()
        vec_out[...] = vec_send[bits]

        @pl.when(stage == stages - 1)
        def _():
            final_send[...] = vec_send[bits, 8:16, :]
            for offset in range(1, stages):
                final_copy(offset).start()

    def vec_finish():
        @pl.when(stage != stages - 1)
        def _():
            final_copy(1).wait_recv()
            vec_out[V_FINAL_GAIN : V_FINAL_BIAS + 1, :] = final_recv[
                V_FINAL_GAIN - 8 : V_FINAL_BIAS - 7, :
            ]

    def vec_drain():
        for k in range(bits):
            vec_copy(k).wait_send()

        @pl.when(stage == stages - 1)
        def _():
            for offset in range(1, stages):
                final_copy(offset).wait_send()

    extra_sum, extra_send_sem, extra_recv_sem = take(3)

    def extra_copy(source, offset, target):
        peer = lax.rem(source + offset, stages)
        return pltpu.make_async_remote_copy(
            src_ref=extra_sum.at[peer],
            dst_ref=target,
            send_sem=extra_send_sem.at[offset],
            recv_sem=extra_recv_sem.at[0 if source == 0 else 1],
            device_id={"pipe": peer},
            device_id_type=MESH,
        )

    def chunk_steps(kind, c, block):
        full = take(1)[0]

        def compute():
            if kind == "down":
                need("gres", "active")
                half = width // 2

                def body(i, carry):
                    depth = block[0]
                    lanes = pl.ds(pl.multiple_of(i * 256, 256), 256)
                    part = dot_tn(mats["active"][:, lanes], mats["gres"][:, c * half : (c + 1) * half])
                    per = 256 // depth
                    put_blocks(full, i, per, part.astype(BF16).reshape((per,) + block))
                    return carry

                lax.fori_loop(0, mats["active"].shape[1] // 256, body, 0)
            elif kind == "extra":
                load("xl").wait()
                load("xr").wait()
                rows = mats["xl"].shape[1] // stages
                for p in range(stages):
                    part = dot_tn(mats["xl"][:, p * rows : (p + 1) * rows], mats["xr"][...])
                    part = part.astype(BF16).reshape((devices,) + block[1:])
                    for d in range(devices):
                        full[split(d) + (p,)] = part[d]
            else:
                left, right = {
                    "in": ("normed2", "ghid"),
                    "out": ("mixed", "gbr"),
                    "qkv": ("normed", "gproj"),
                }[kind]
                need(left, right)
                cols = slice(c * width, (c + 1) * width)

                def body(i, carry):
                    lanes = pl.ds(pl.multiple_of(i * 128, 128), 128)
                    part = dot_tn(mats[left][:, lanes], mats[right][:, cols])
                    per = 128 // block[0]
                    put_blocks(full, i, per, part.astype(BF16).reshape((per,) + block))
                    return carry

                lax.fori_loop(0, width // 128, body, 0)

        def split(d):
            return tuple((d // stride) % size for size, stride in reversed(dims))

        def put_blocks(ref, i, per, values):
            for q in range(per):
                d = i * per + q
                index = tuple(lax.rem(d // stride, size) for size, stride in reversed(dims))
                ref[index] = values[q]

        steps = [[compute]]
        for phase, (size, _) in enumerate(dims):
            buffers = take(3)
            steps[-1].append(functools.partial(line_step, phase, size, 1, full, buffers))
            for t in range(2, size):
                steps.append([functools.partial(line_step, phase, size, t, full, buffers)])
            drains.append((kind, functools.partial(line_drain, phase, size, full, buffers)))
            steps.append([functools.partial(line_final, kind, c, phase, size, full, buffers)])
        if kind == "extra":
            steps = [[gated(step)] for step in steps]
        return steps

    def gated(step):
        def run():
            @pl.when(is_extra)
            def _():
                for part in step:
                    part()

        return run

    def block_of(full, phase, j):
        later = [slice(None)] * (len(dims) - 1 - phase)
        return full.at[tuple(later + [j] + where[:phase][::-1])]

    def line_copy(phase, size, t, side, full, buffers):
        recv, ssem, rsem = buffers
        i = where[phase]
        stride = dims[phase][1]
        if side == 0:
            j, peer = size - t + i, place + jnp.where(i < size - 1, stride, 0)
        else:
            j, peer = t - size + i, place - jnp.where(i > 0, stride, 0)
        return pltpu.make_async_remote_copy(
            src_ref=block_of(full, phase, jnp.clip(j, 0, size - 1)),
            dst_ref=recv.at[0 if size == 2 else side, t - 1],
            send_sem=ssem.at[side, t - 1],
            recv_sem=rsem.at[side, t - 1],
            device_id={"dp": peer},
            device_id_type=MESH,
        )

    def sends(i, size, t, side):
        return (i <= t - 1) if side == 0 else (i >= size - t)

    def line_step(phase, size, t, full, buffers):
        i = where[phase]
        for side in range(2):
            at_end = (i == 0) if side == 0 else (i == size - 1)
            j = size - t + i if side == 0 else t - size + i
            j = jnp.clip(j, 0, size - 1)

            @pl.when(sends(i, size, t, side))
            def _():
                if t > 1:
                    @pl.when(jnp.logical_not(at_end))
                    def _():
                        line_copy(phase, size, t - 1, side, full, buffers).wait_recv()
                        own = block_of(full, phase, j)
                        got = buffers[0][0 if size == 2 else side, t - 2]
                        own[...] = (own[...].astype(F32) + got.astype(F32)).astype(BF16)

                line_copy(phase, size, t, side, full, buffers).start()

    def line_final(kind, c, phase, size, full, buffers):
        i = where[phase]
        own = block_of(full, phase, i)
        total = own
        if phase == len(dims) - 1:
            slots = {
                "qkv": lambda: qkv_out.at[:, c * width : (c + 1) * width],
                "in": lambda: in_out.at[:, c * width : (c + 1) * width],
                "out": lambda: out_out,
                "down": lambda: down_out.at[:, c * (width // 2) : (c + 1) * (width // 2)],
                "extra": lambda: extra_sum,
            }
            total = slots[kind]()
        lower, upper = i > 0, i < size - 1

        def arrived(side):
            line_copy(phase, size, size - 1, side, full, buffers).wait_recv()
            return buffers[0][0 if size == 2 else side, size - 2].astype(F32)

        @pl.when(lower & upper)
        def _():
            total[...] = (own[...].astype(F32) + arrived(0) + arrived(1)).astype(total.dtype)

        @pl.when(lower & jnp.logical_not(upper))
        def _():
            total[...] = (own[...].astype(F32) + arrived(0)).astype(total.dtype)

        @pl.when(jnp.logical_not(lower))
        def _():
            total[...] = (own[...].astype(F32) + arrived(1)).astype(total.dtype)

        if phase == len(dims) - 1 and kind == "extra":
            for source_stage, out in ((0, embed_out), (stages - 1, head_out)):
                @pl.when(stage == source_stage)
                def _():
                    for offset in range(1, stages):
                        extra_copy(source_stage, offset, extra_recv[0 if source_stage == 0 else 1]).start()
                    out[...] = extra_sum[source_stage]

    def line_drain(phase, size, full, buffers):
        i = where[phase]
        for side in range(2):
            for t in range(1, size):
                @pl.when(sends(i, size, t, side))
                def _():
                    line_copy(phase, size, t, side, full, buffers).wait_send()

    extra_recv = take(2)
    drains = []
    chains = [chunk_steps(*item) for item in plan]
    depth = len(chains[0])
    vec_chain = [vec_step(k) for k in range(bits)] + [vec_last]
    for r in range(len(chains) + depth - 1):
        for d in range(depth):
            if 0 <= r - d < len(chains):
                for part in chains[r - d][d]:
                    part()
        if 3 <= r < 3 + len(vec_chain):
            vec_chain[r - 3]()
    vec_finish()
    for source_stage, out in ((0, embed_out), (stages - 1, head_out)):
        @pl.when(stage != source_stage)
        def _():
            got = extra_recv[0 if source_stage == 0 else 1]
            extra_copy(source_stage, 1, got).wait_recv()
            out[...] = got[...]

        @pl.when(stage == source_stage)
        def _():
            for offset in range(1, stages):
                extra_copy(source_stage, offset, extra_recv[0]).wait_send()

    vec_drain()
    for kind, drain in drains:
        if kind == "extra":
            gated([drain])()
        else:
            drain()


def run_gradients(stages, devices, saved, vec):
    dims = line_dims(devices)
    micros, tokens, width = saved[0].shape
    hid, vocab = saved[3].shape[2], saved[8].shape[2]
    plan = chunk_plan(width, hid, vocab, stages, devices)
    saved = [member.reshape(micros * tokens, member.shape[2]) for member in saved]
    vmem = pl.BlockSpec(memory_space=pltpu.VMEM)
    hbm = pl.BlockSpec(memory_space=pl.ANY)
    bits = devices.bit_length() - 1
    share = vocab // (stages * devices)
    scratch = [pltpu.VMEM(member.shape, BF16) for member in saved]
    scratch += [pltpu.SemaphoreType.DMA((len(saved),))]
    scratch += [
        pltpu.VMEM((bits + 1,) + vec.shape, F32),
        pltpu.VMEM((bits,) + vec.shape, F32),
        pltpu.SemaphoreType.DMA((bits,)),
        pltpu.SemaphoreType.DMA((bits,)),
        pltpu.VMEM((8, width), F32),
        pltpu.VMEM((8, width), F32),
        pltpu.SemaphoreType.DMA((stages,)),
        pltpu.SemaphoreType.DMA((1,)),
        pltpu.VMEM((stages, share, width), F32),
        pltpu.SemaphoreType.DMA((stages,)),
        pltpu.SemaphoreType.DMA((2,)),
        pltpu.VMEM((share, width), F32),
        pltpu.VMEM((share, width), F32),
    ]
    sizes = [size for size, _ in reversed(dims)]
    for _, _, block in plan:
        scratch.append(pltpu.VMEM(tuple(sizes) + block, BF16))
        for phase, (size, _) in enumerate(dims):
            piece = tuple(sizes[: len(dims) - 1 - phase]) + block
            scratch.append(pltpu.VMEM((1 if size == 2 else 2, size - 1) + piece, BF16))
            scratch += [pltpu.SemaphoreType.DMA((2, size - 1))] * 2
    return pl.pallas_call(
        functools.partial(gradient_kernel, stages, devices, plan),
        out_shape=[
            jax.ShapeDtypeStruct((width // devices, 3 * width), F32),
            jax.ShapeDtypeStruct((width // devices, width), F32),
            jax.ShapeDtypeStruct((width // devices, hid), F32),
            jax.ShapeDtypeStruct((hid // devices, width), F32),
            jax.ShapeDtypeStruct((share, width), F32),
            jax.ShapeDtypeStruct((share, width), F32),
            jax.ShapeDtypeStruct(vec.shape, F32),
        ],
        in_specs=[hbm] * len(saved) + [vmem],
        out_specs=[vmem] * 7,
        scratch_shapes=scratch,
        compiler_params=pltpu.CompilerParams(
            collective_id=1, has_side_effects=True, vmem_limit_bytes=62 * 1024 * 1024
        ),
        name="gradients",
    )(*saved, vec)


def finish_kernel(devices, embed_g, qkv_g, out_g, in_g, down_g, head_g, vec, *outs):
    place = lax.axis_index("dp")
    width = vec.shape[1]
    sem = outs[-1]
    (embed_o, qkv_o, qv_o, out_o, outb_o, in_o, inb_o, down_o, gain_o, shift_o, fg_o, fb_o, head_o) = outs[:-1]
    moved = (
        (embed_g, embed_o),
        (qkv_g, qkv_o.at[0]),
        (out_g, out_o.at[0]),
        (in_g, in_o.at[0]),
        (down_g, down_o.at[0]),
        (head_g, head_o),
    )
    copies = [pltpu.make_async_copy(src, dst, sem.at[i]) for i, (src, dst) in enumerate(moved)]
    for copy in copies:
        copy.start()
    lanes = width // devices
    turned = pltpu.roll(vec[0:8, :], lax.rem(width - place * lanes, width), 1)
    for row, out in ((V_QUERY, qv_o), (V_BRANCH, outb_o), (V_GAIN1, gain_o), (V_SHIFT1, shift_o)):
        out[0] = turned[row : row + 2, 0:lanes]
    share = inb_o.shape[1]
    first = place * share
    row = vec[pl.ds(V_HIDDEN + first // width, 1), :]
    wide = jnp.broadcast_to(row, (8, width))
    inb_o[...] = pltpu.roll(wide, lax.rem(width - lax.rem(first, width), width), 1)[0:1, 0:share]
    fg_o[...] = vec[V_FINAL_GAIN : V_FINAL_GAIN + 1, :]
    fb_o[...] = vec[V_FINAL_BIAS : V_FINAL_BIAS + 1, :]
    for copy in copies:
        copy.wait()


def run_finish(devices, embed_g, qkv_g, out_g, in_g, down_g, head_g, vec):
    vmem = pl.BlockSpec(memory_space=pltpu.VMEM)
    hbm = pl.BlockSpec(memory_space=pl.ANY)
    width = vec.shape[1]
    lanes = width // devices

    def shape(*sizes):
        return jax.ShapeDtypeStruct(sizes, F32)

    pair = shape(1, 2, lanes)
    return pl.pallas_call(
        functools.partial(finish_kernel, devices),
        out_shape=[
            shape(*embed_g.shape),
            shape(1, *qkv_g.shape),
            pair,
            shape(1, *out_g.shape),
            pair,
            shape(1, *in_g.shape),
            shape(1, in_g.shape[1] // devices),
            shape(1, *down_g.shape),
            pair,
            pair,
            shape(1, width),
            shape(1, width),
            shape(*head_g.shape),
        ],
        in_specs=[hbm] * 6 + [vmem],
        out_specs=[hbm, hbm, vmem, hbm, vmem, hbm, vmem, hbm, vmem, vmem, vmem, vmem, hbm],
        scratch_shapes=[pltpu.SemaphoreType.DMA((6,))],
        name="finish",
    )(embed_g, qkv_g, out_g, in_g, down_g, head_g, vec)


def on_device(
    token_ids,
    segment_ids,
    target_ids,
    embed_table,
    qkv_weight,
    qv_bias,
    out_weight,
    out_biases,
    ff_in,
    ff_in_bias,
    ff_out,
    norm_gains,
    norm_biases,
    final_gain,
    final_bias,
    head_weight,
):
    stages = lax.axis_size("pipe")
    devices = lax.axis_size("dp")
    params = (
        embed_table,
        qkv_weight[0],
        qv_bias[0],
        out_weight[0],
        out_biases[0],
        ff_in[0],
        ff_in_bias,
        ff_out[0],
        norm_gains[0],
        norm_biases[0],
        final_gain[None],
        final_bias[None],
        head_weight,
    )
    *saved, vec = run_pipeline(stages, token_ids, segment_ids, target_ids, params)
    qkv_g, out_g, in_g, down_g, embed_g, head_g, sums = run_gradients(stages, devices, saved, vec)
    done = list(run_finish(devices, embed_g, qkv_g, out_g, in_g, down_g, head_g, sums))
    done[10], done[11] = done[10][0], done[11][0]
    return tuple(done)


def solution(mesh):
    layer3 = P("pipe", None, None)
    return jax.shard_map(
        on_device,
        mesh=mesh,
        in_specs=(
            P("dp", None),
            P("dp", None),
            P("dp", None),
            P(),
            layer3,
            layer3,
            layer3,
            layer3,
            layer3,
            P("pipe", None),
            layer3,
            layer3,
            layer3,
            P(),
            P(),
            P(),
        ),
        out_specs=(
            P(("pipe", "dp"), None),
            P("pipe", "dp", None),
            P("pipe", None, "dp"),
            P("pipe", "dp", None),
            P("pipe", None, "dp"),
            P("pipe", "dp", None),
            P("pipe", "dp"),
            P("pipe", "dp", None),
            P("pipe", None, "dp"),
            P("pipe", None, "dp"),
            P(),
            P(),
            P(("pipe", "dp"), None),
        ),
        check_vma=False,
    )
```

```python
import functools

import jax
import jax.numpy as jnp
from jax import lax
from jax.experimental import pallas as pl
from jax.experimental.pallas import tpu as pltpu
from jax.sharding import PartitionSpec as P

HEADS = 8
FRAME = 6
ROW = 128
GROUP = 2
MASKED = -1e30
GELU_A = 0.7978845608
GELU_B = 0.044715
MESH = pl.DeviceIdType.MESH
F32 = jnp.float32
BF16 = jnp.bfloat16

VEC_ROWS = 16
V_QUERY, V_VALUE, V_BRANCH, V_RESULT, V_GAIN1, V_GAIN2, V_SHIFT1, V_SHIFT2 = range(8)
V_HIDDEN = 8
V_FINAL_GAIN, V_FINAL_BIAS = 12, 13


def dot(a, b):
    return lax.dot_general(a, b, (((1,), (0,)), ((), ())), preferred_element_type=F32)


def dot_nt(a, b):
    return lax.dot_general(a, b, (((1,), (1,)), ((), ())), preferred_element_type=F32)


def dot_tn(a, b):
    return lax.dot_general(a, b, (((0,), (0,)), ((), ())), preferred_element_type=F32)


def normalise(values):
    centre = jnp.mean(values, axis=-1, keepdims=True)
    centered = values - centre
    spread = jnp.mean(centered * centered, axis=-1, keepdims=True)
    scale = lax.rsqrt(spread + 1e-05)
    return centered * scale, scale


def norm_backward(grad, normal, scale, gain):
    grad_n = grad * gain
    mean_grad = jnp.mean(grad_n, axis=-1, keepdims=True)
    mean_proj = jnp.mean(grad_n * normal, axis=-1, keepdims=True)
    return scale * (grad_n - mean_grad - normal * mean_proj)


def column_sum(values):
    return jnp.sum(values, axis=0, keepdims=True)


def stack_pair(pair, low_lanes):
    zero = jnp.zeros_like(pair)
    return jnp.concatenate(
        [jnp.where(low_lanes, pair, zero), jnp.where(low_lanes, zero, pair)], axis=0
    )


def join_pair(stacked, low_lanes):
    half = stacked.shape[0] // 2
    return jnp.where(low_lanes, stacked[:half], stacked[half:])


def pipeline_kernel(
    stages,
    micros,
    token_ids,
    segment_ids,
    target_ids,
    embed,
    qkv_w,
    qv_b,
    out_w,
    out_b,
    in_w,
    in_b,
    down_w,
    gains,
    shifts,
    fin_gain,
    fin_bias,
    head_w,
    normed_o,
    mixed_o,
    normed2_o,
    active_o,
    gres_o,
    ghid_o,
    gbr_o,
    gproj_o,
    xl_o,
    xr_o,
    vec,
    instream,
    outb,
    gin,
    gs,
    normed,
    proj,
    probs,
    mixed,
    middle,
    normed2,
    active,
    slope,
    lo,
    go,
    gmid,
    s_gres,
    s_ghid,
    s_gbr,
    s_gproj,
    s_xl,
    ids,
    frames,
    fsend,
    frecv,
    bsend,
    brecv,
    osem,
):
    stage = lax.axis_index("pipe")
    tokens, width = instream.shape[1], instream.shape[2]
    hidden_n = in_b.shape[1]
    vocab = head_w.shape[0]
    pairs = width // ROW
    chunk = 512
    is_first = stage == 0
    is_last = stage == stages - 1
    up = jnp.minimum(stage + 1, stages - 1)
    down = jnp.maximum(stage - 1, 0)

    barrier = pltpu.get_barrier_semaphore()

    @pl.when(jnp.logical_not(is_first))
    def _():
        pl.semaphore_signal(barrier, inc=1, device_id={"pipe": down}, device_id_type=MESH)

    @pl.when(jnp.logical_not(is_last))
    def _():
        pl.semaphore_signal(barrier, inc=1, device_id={"pipe": up}, device_id_type=MESH)

    pl.semaphore_wait(barrier, jnp.where(is_first | is_last, 1, 2))
    vec[...] = jnp.zeros_like(vec)
    rows_n, seq = token_ids.shape
    for index, member in enumerate((token_ids, segment_ids, target_ids)):
        ids[index] = jnp.full(ids.shape[1:], 4.0 if index == 1 else -1.0, F32)
        ids[index, 0:rows_n, 0:seq] = member[...].astype(F32)
    at_query = lax.broadcasted_iota(jnp.int32, (ROW, ROW), 1)
    at_key = lax.broadcasted_iota(jnp.int32, (ROW, ROW), 0)
    frames[...] = jnp.where(at_key < ((at_query * 43) // 256) * FRAME + FRAME, 1.0, 0.0)

    def column(index, row):
        values = jnp.broadcast_to(ids[index, pl.ds(row, 1), :], (8, ROW))
        return values.T[:, 0:1]

    def hot_rows(index, m):
        parts = [column(index, m * GROUP + r) for r in range(GROUP)]
        values = jnp.concatenate(parts, axis=0)
        places = lax.broadcasted_iota(jnp.int32, (tokens, vocab), 1).astype(F32)
        return values, jnp.where(values == places, 1.0, 0.0)

    def forward_copy(m):
        return pltpu.make_async_remote_copy(
            src_ref=outb.at[m],
            dst_ref=instream.at[m],
            send_sem=fsend.at[m],
            recv_sem=frecv.at[m],
            device_id={"pipe": up},
            device_id_type=MESH,
        )

    def backward_copy(m):
        return pltpu.make_async_remote_copy(
            src_ref=gs.at[m],
            dst_ref=gin.at[m],
            send_sem=bsend.at[m],
            recv_sem=brecv.at[m],
            device_id={"pipe": down},
            device_id_type=MESH,
        )

    def save(index, src, dst, m):
        return pltpu.make_async_copy(src, dst.at[m], osem.at[index, m])

    def saves_forward(m):
        return [
            save(0, normed.at[m], normed_o, m),
            save(1, mixed.at[m], mixed_o, m),
            save(2, normed2.at[m], normed2_o, m),
            save(3, active.at[m], active_o, m),
        ]

    def saves_backward(m):
        slot = lax.rem(m, 2)
        return [
            save(4, s_gres.at[slot], gres_o, m),
            save(5, s_ghid.at[slot], ghid_o, m),
            save(6, s_gbr.at[slot], gbr_o, m),
            save(7, s_gproj.at[slot], gproj_o, m),
        ]

    def save_xl(m):
        return save(8, s_xl.at[lax.rem(m, 2)], xl_o, m)

    def put_xl(m, value):
        @pl.when(m >= 2)
        def _():
            save_xl(m - 2).wait()

        s_xl[lax.rem(m, 2)] = value
        save_xl(m).start()

    lane_low = lax.broadcasted_iota(jnp.int32, (ROW, ROW), 1) < ROW // 2

    def forward(m):
        @pl.when(is_first)
        def _():
            hot = hot_rows(0, m)[1].astype(BF16)
            put_xl(m, hot)
            instream[m] = dot(hot, embed[...]).astype(BF16)

        @pl.when(jnp.logical_not(is_first))
        def _():
            forward_copy(m).wait_recv()

        normal, _ = normalise(instream[m].astype(F32))
        normed[m] = (normal * gains[0:1, :] + shifts[0:1, :]).astype(BF16)
        low = normed[m]
        queries = dot(low, qkv_w[:, 0:width]) + qv_b[0:1, :]
        proj[m, :, 0:width] = (queries * (ROW // 2) ** -0.5).astype(BF16)
        proj[m, :, width : 2 * width] = dot(low, qkv_w[:, width : 2 * width]).astype(BF16)
        proj[m, :, 2 * width : 3 * width] = (
            dot(low, qkv_w[:, 2 * width : 3 * width]) + qv_b[1:2, :]
        ).astype(BF16)
        masks, scores = [], []
        for r in range(GROUP):
            rows = slice(r * ROW, (r + 1) * ROW)
            kinds = lax.broadcasted_iota(jnp.int32, (16, ROW), 0).astype(F32)
            member = jnp.where(ids[1, pl.ds(m * GROUP + r, 1), :] == kinds, 1.0, 0.0).astype(BF16)
            mask = jnp.where(dot_tn(member, member) * frames[...] > 0.5, 0.0, MASKED)
            masks.append(jnp.concatenate([mask, mask], axis=1))
            for p in range(pairs):
                q = stack_pair(proj[m, rows, p * ROW : (p + 1) * ROW], lane_low)
                k = proj[m, rows, width + p * ROW : width + (p + 1) * ROW]
                scores.append(dot_nt(k, q))

        def mix(unit):
            r, p = unit // pairs, unit % pairs
            rows = slice(r * ROW, (r + 1) * ROW)
            v = proj[m, rows, 2 * width + p * ROW : 2 * width + (p + 1) * ROW]
            both = dot_tn(probs[m, unit], v)
            mixed[m, rows, p * ROW : (p + 1) * ROW] = join_pair(both, lane_low).astype(BF16)

        for unit in range(GROUP * pairs):
            masked = scores[unit] + masks[unit // pairs]
            expo = jnp.exp(masked - jnp.max(masked, axis=0, keepdims=True))
            total = jnp.sum(expo, axis=0, keepdims=True)
            probs[m, unit] = (expo * (1.0 / total)).astype(BF16)
            if unit:
                mix(unit - 1)
        mix(GROUP * pairs - 1)
        mid = instream[m].astype(F32) + (dot(mixed[m], out_w[...]) + out_b[0:1, :])
        middle[m] = mid
        normal2, _ = normalise(mid)
        normed2[m] = (normal2 * gains[1:2, :] + shifts[1:2, :]).astype(BF16)
        low2 = normed2[m]
        parts = hidden_n // chunk

        def spread(c):
            return dot(low2, in_w[:, c * chunk : (c + 1) * chunk])

        total, ahead = None, spread(0)
        for c in range(parts):
            cols = slice(c * chunk, (c + 1) * chunk)
            hid = ahead + in_b[0:1, cols]
            if c + 1 < parts:
                ahead = spread(c + 1)
            square = hid * hid
            tan = jnp.tanh(hid * (GELU_A + (GELU_A * GELU_B) * square))
            half = 0.5 + 0.5 * tan
            act = (hid * half).astype(BF16)
            active[m, :, cols] = act
            rise = (1.0 - tan * tan) * (0.5 * GELU_A + (1.5 * GELU_A * GELU_B) * square)
            slope[m, :, cols] = (half + hid * rise).astype(BF16)
            term = dot(act, down_w[cols, :])
            total = term if total is None else total + term
        for copy in saves_forward(m):
            copy.start()
        lo[...] = middle[m] + (total + out_b[1:2, :])

        @pl.when(jnp.logical_not(is_last))
        def _():
            outb[m] = lo[...].astype(BF16)
            forward_copy(m).start()

    def head(m):
        normal, scale = normalise(lo[...])
        outb[m] = (normal * fin_gain[...] + fin_bias[...]).astype(BF16)
        save(9, outb.at[m], xr_o, m).start()
        logits = dot_nt(outb[m], head_w[...])
        top = jnp.max(logits, axis=-1, keepdims=True)
        expo = jnp.exp(logits - top)
        total = jnp.sum(expo, axis=-1, keepdims=True)
        target, hot = hot_rows(2, m)
        grad_logits = jnp.where(target >= 0.0, expo * (1.0 / total) - hot, 0.0).astype(BF16)
        put_xl(m, grad_logits)
        grad_final = dot(grad_logits, head_w[...])
        vec[V_FINAL_GAIN : V_FINAL_GAIN + 1, :] += column_sum(grad_final * normal)
        vec[V_FINAL_BIAS : V_FINAL_BIAS + 1, :] += column_sum(grad_final)
        go[...] = norm_backward(grad_final, normal, scale, fin_gain[...])

    def backward(m):
        slot = lax.rem(m, 2)

        @pl.when(m >= 2)
        def _():
            for copy in saves_backward(m - 2):
                copy.wait()

        @pl.when(jnp.logical_not(is_last))
        def _():
            backward_copy(m).wait_recv()
            go[...] = gin[m].astype(F32)

        s_gres[slot] = go[...].astype(BF16)
        gres = s_gres[slot]
        parts = hidden_n // chunk

        def spread(c):
            return dot_nt(gres, down_w[c * chunk : (c + 1) * chunk, :])

        total, ahead = None, spread(0)
        for c in range(parts):
            cols = slice(c * chunk, (c + 1) * chunk)
            gact = ahead
            if c + 1 < parts:
                ahead = spread(c + 1)
            ghid = (gact * slope[m, :, cols].astype(F32)).astype(BF16)
            s_ghid[slot, :, cols] = ghid
            term = dot_nt(ghid, in_w[:, cols])
            total = term if total is None else total + term
        normal2, scale2 = normalise(middle[m])
        vec[V_GAIN2 : V_GAIN2 + 1, :] += column_sum(total * normal2)
        vec[V_SHIFT2 : V_SHIFT2 + 1, :] += column_sum(total)
        gmid[...] = go[...] + norm_backward(total, normal2, scale2, gains[1:2, :])
        s_gbr[slot] = gmid[...].astype(BF16)
        gbr = s_gbr[slot]
        gmix = dot_nt(gbr, out_w[...]).astype(BF16)
        grads = []
        for r in range(GROUP):
            rows = slice(r * ROW, (r + 1) * ROW)
            for p in range(pairs):
                gm = stack_pair(gmix[rows, p * ROW : (p + 1) * ROW], lane_low)
                vlanes = slice(2 * width + p * ROW, 2 * width + (p + 1) * ROW)
                grads.append(dot_nt(proj[m, rows, vlanes], gm))
                s_gproj[slot, rows, vlanes] = dot(probs[m, r * pairs + p], gm).astype(BF16)

        def pull(unit, gsc):
            r, p = unit // pairs, unit % pairs
            rows = slice(r * ROW, (r + 1) * ROW)
            lanes = slice(p * ROW, (p + 1) * ROW)
            klanes = slice(width + p * ROW, width + (p + 1) * ROW)
            q = stack_pair(proj[m, rows, lanes], lane_low)
            s_gproj[slot, rows, klanes] = dot(gsc, q).astype(BF16)
            gq = join_pair(dot_tn(gsc, proj[m, rows, klanes]), lane_low) * (ROW // 2) ** -0.5
            s_gproj[slot, rows, lanes] = gq.astype(BF16)

        waiting = None
        for unit in range(GROUP * pairs):
            weights = probs[m, unit].astype(F32)
            inner = jnp.sum(weights * grads[unit], axis=0, keepdims=True)
            gsc = (weights * (grads[unit] - inner)).astype(BF16)
            if waiting is not None:
                pull(unit - 1, waiting)
            waiting = gsc
        pull(GROUP * pairs - 1, waiting)
        for copy in saves_backward(m):
            copy.start()
        gproj = s_gproj[slot]
        gnormed = dot_nt(gproj, qkv_w[...])
        normal, scale = normalise(instream[m].astype(F32))
        vec[V_GAIN1 : V_GAIN1 + 1, :] += column_sum(gnormed * normal)
        vec[V_SHIFT1 : V_SHIFT1 + 1, :] += column_sum(gnormed)
        gs[m] = (gmid[...] + norm_backward(gnormed, normal, scale, gains[0:1, :])).astype(BF16)

        @pl.when(is_first)
        def _():
            save(9, gs.at[m], xr_o, m).start()

        @pl.when(jnp.logical_not(is_first))
        def _():
            backward_copy(m).start()

    def tick(t, carry):
        m_forward = t - stage
        m_backward = t - (2 * (stages - 1) - stage)

        @pl.when((m_forward >= 0) & (m_forward < micros))
        def _():
            forward(m_forward)

        @pl.when((m_backward >= 0) & (m_backward < micros))
        def _():
            @pl.when(is_last)
            def _():
                head(m_backward)

            backward(m_backward)

        return carry

    lax.fori_loop(0, micros + 2 * (stages - 1), tick, 0)

    for m in range(micros):
        for copy in saves_forward(m):
            copy.wait()

        @pl.when(jnp.logical_not(is_last))
        def _():
            forward_copy(m).wait_send()

        @pl.when(jnp.logical_not(is_first))
        def _():
            backward_copy(m).wait_send()

        @pl.when(is_first)
        def _():
            save(9, gs.at[m], xr_o, m).wait()

        @pl.when(is_last)
        def _():
            save(9, outb.at[m], xr_o, m).wait()

    for m in range(max(0, micros - 2), micros):
        for copy in saves_backward(m):
            copy.wait()

        @pl.when(is_first | is_last)
        def _():
            save_xl(m).wait()


def run_pipeline(stages, token_ids, segment_ids, target_ids, params):
    embed, in_w, head_w = params[0], params[5], params[12]
    width = embed.shape[1]
    vocab = head_w.shape[0]
    hid = in_w.shape[1]
    tokens = GROUP * ROW
    micros = token_ids.shape[0] // GROUP
    pairs = width // ROW
    vmem = pl.BlockSpec(memory_space=pltpu.VMEM)
    hbm = pl.BlockSpec(memory_space=pl.ANY)

    def kept(columns):
        return jax.ShapeDtypeStruct((micros, tokens, columns), BF16)

    def scratch(lead, columns, kind=BF16):
        return pltpu.VMEM((lead, tokens, columns), kind)

    out_shape = [
        kept(width),
        kept(width),
        kept(width),
        kept(hid),
        kept(width),
        kept(hid),
        kept(width),
        kept(3 * width),
        kept(vocab),
        kept(width),
        jax.ShapeDtypeStruct((VEC_ROWS, width), F32),
    ]
    return pl.pallas_call(
        functools.partial(pipeline_kernel, stages, micros),
        out_shape=out_shape,
        in_specs=[vmem] * 16,
        out_specs=[hbm] * 10 + [vmem],
        scratch_shapes=[
            scratch(micros, width),
            scratch(micros, width),
            scratch(micros, width),
            scratch(micros, width),
            scratch(micros, width),
            scratch(micros, 3 * width),
            pltpu.VMEM((micros, GROUP * pairs, ROW, 2 * ROW), BF16),
            scratch(micros, width),
            scratch(micros, width, F32),
            scratch(micros, width),
            scratch(micros, hid),
            scratch(micros, hid),
            pltpu.VMEM((tokens, width), F32),
            pltpu.VMEM((tokens, width), F32),
            pltpu.VMEM((tokens, width), F32),
            scratch(2, width),
            scratch(2, hid),
            scratch(2, width),
            scratch(2, 3 * width),
            scratch(2, vocab),
            pltpu.VMEM((3, 16, ROW), F32),
            pltpu.VMEM((ROW, ROW), F32),
            pltpu.SemaphoreType.DMA((micros,)),
            pltpu.SemaphoreType.DMA((micros,)),
            pltpu.SemaphoreType.DMA((micros,)),
            pltpu.SemaphoreType.DMA((micros,)),
            pltpu.SemaphoreType.DMA((10, micros)),
        ],
        compiler_params=pltpu.CompilerParams(
            collective_id=0, has_side_effects=True, vmem_limit_bytes=62 * 1024 * 1024
        ),
        name="pipeline",
    )(token_ids, segment_ids, target_ids, *params)


def line_dims(devices):
    dims, stride = [], 1
    if devices == 8:
        return [(2, 1), (4, 2)]
    while devices > 1:
        size = 4 if devices % 4 == 0 else 2
        dims.append((size, stride))
        stride *= size
        devices //= size
    return dims


def chunk_plan(width, hid, vocab, stages, devices):
    slim, deep = width // devices, hid // devices
    plan = [("out", 0, (slim, width), False)]
    for c in range(2):
        plan.append(("down", c, (deep, width // 2), False))
    plan.append(("extra", 0, (stages, vocab // (stages * devices), width), False))
    for c in range(hid // width):
        plan.append(("in", c, (slim, width), c == 1))
    for c in range(3):
        plan.append(("qkv", c, (slim, width), c == 0))
    return plan


def gradient_kernel(stages, devices, plan, *refs):
    dims = line_dims(devices)
    refs = list(refs)

    def take(amount):
        head, refs[:] = refs[:amount], refs[amount:]
        return head

    inputs = take(10)
    vec_in = take(1)[0]
    qkv_out, out_out, in_out, down_out, embed_out, head_out, vec_out = take(7)
    local = take(10)
    in_sem = take(1)[0]
    mats = dict(
        zip(
            ("normed", "mixed", "normed2", "active", "gres", "ghid", "gbr", "gproj", "xl", "xr"),
            local,
        )
    )
    names = list(mats)
    stage = lax.axis_index("pipe")
    place = lax.axis_index("dp")
    is_extra = (stage == 0) | (stage == stages - 1)
    width = mats["normed"].shape[1]
    where = [lax.rem(place // stride, size) for size, stride in dims]

    barrier = pltpu.get_barrier_semaphore()

    def greet(offset, carry):
        peer = lax.rem(place + offset, devices)
        pl.semaphore_signal(barrier, inc=1, device_id={"dp": peer}, device_id_type=MESH)
        return carry

    def greet_stage(offset, carry):
        peer = lax.rem(stage + offset, stages)
        pl.semaphore_signal(barrier, inc=1, device_id={"pipe": peer}, device_id_type=MESH)
        return carry

    lax.fori_loop(1, devices, greet, 0)
    lax.fori_loop(1, stages, greet_stage, 0)

    def load(name):
        i = names.index(name)
        return pltpu.make_async_copy(inputs[i], mats[name], in_sem.at[i])

    order = ["gres", "active", "normed2", "ghid", "mixed", "gbr", "normed", "gproj"]
    for name in order[:2]:
        load(name).start()

    @pl.when(is_extra)
    def _():
        load("xl").start()
        load("xr").start()

    for name in order[2:]:
        load(name).start()

    pl.semaphore_wait(barrier, devices - 1 + stages - 1)
    loaded = set()

    def need(*wanted):
        for name in wanted:
            if name not in loaded:
                loaded.add(name)
                load(name).wait()

    bits = devices.bit_length() - 1
    vec_send, vec_recv = take(2)
    vec_sems = take(2)

    def vec_copy(k):
        peer = jnp.bitwise_xor(place, 1 << k)
        return pltpu.make_async_remote_copy(
            src_ref=vec_send.at[k],
            dst_ref=vec_recv.at[k],
            send_sem=vec_sems[0].at[k],
            recv_sem=vec_sems[1].at[k],
            device_id={"dp": peer},
            device_id_type=MESH,
        )

    def vec_step(k):
        def run():
            if k == 0:
                need("gres", "ghid", "gbr", "gproj")
                vec_send[0] = vec_in[...]
                ones = jnp.ones((16, mats["gres"].shape[0]), BF16)
                for name, start, row in (
                    ("gproj", 0, V_QUERY),
                    ("gproj", 2 * width, V_VALUE),
                    ("gbr", 0, V_BRANCH),
                    ("gres", 0, V_RESULT),
                ):
                    part = dot(ones, mats[name][:, start : start + width])
                    vec_send[0, row : row + 1, :] = part[0:1, :]
                for q in range(mats["ghid"].shape[1] // width):
                    part = dot(ones, mats["ghid"][:, q * width : (q + 1) * width])
                    vec_send[0, V_HIDDEN + q : V_HIDDEN + q + 1, :] = part[0:1, :]
            else:
                vec_copy(k - 1).wait_recv()
                vec_send[k] = vec_send[k - 1] + vec_recv[k - 1]
            if k < bits:
                vec_copy(k).start()

        return run

    final_send, final_recv = take(2)
    final_sems = take(2)

    def final_copy(offset):
        peer = lax.rem(stages - 1 + offset, stages)
        return pltpu.make_async_remote_copy(
            src_ref=final_send,
            dst_ref=final_recv,
            send_sem=final_sems[0].at[offset],
            recv_sem=final_sems[1].at[0],
            device_id={"pipe": peer},
            device_id_type=MESH,
        )

    def vec_last():
        vec_step(bits)()
        vec_out[...] = vec_send[bits]

        @pl.when(stage == stages - 1)
        def _():
            final_send[...] = vec_send[bits, 8:16, :]
            for offset in range(1, stages):
                final_copy(offset).start()

    def vec_finish():
        @pl.when(stage != stages - 1)
        def _():
            final_copy(1).wait_recv()
            vec_out[V_FINAL_GAIN : V_FINAL_BIAS + 1, :] = final_recv[
                V_FINAL_GAIN - 8 : V_FINAL_BIAS - 7, :
            ]

    def vec_drain():
        for k in range(bits):
            vec_copy(k).wait_send()

        @pl.when(stage == stages - 1)
        def _():
            for offset in range(1, stages):
                final_copy(offset).wait_send()

    extra_sum, extra_send_sem, extra_recv_sem = take(3)

    def extra_copy(source, offset, target):
        peer = lax.rem(source + offset, stages)
        return pltpu.make_async_remote_copy(
            src_ref=extra_sum.at[peer],
            dst_ref=target,
            send_sem=extra_send_sem.at[offset],
            recv_sem=extra_recv_sem.at[0 if source == 0 else 1],
            device_id={"pipe": peer},
            device_id_type=MESH,
        )

    def chunk_steps(kind, c, block, turned):
        order = list(range(len(dims)))
        if turned:
            order.reverse()
        full = take(1)[0]

        def compute():
            if kind == "down":
                need("gres", "active")
                half = width // 2

                def body(i, carry):
                    depth = block[0]
                    lanes = pl.ds(pl.multiple_of(i * 256, 256), 256)
                    part = dot_tn(mats["active"][:, lanes], mats["gres"][:, c * half : (c + 1) * half])
                    per = 256 // depth
                    put_blocks(full, i, per, part.astype(BF16).reshape((per,) + block))
                    return carry

                lax.fori_loop(0, mats["active"].shape[1] // 256, body, 0)
            elif kind == "extra":
                load("xl").wait()
                load("xr").wait()
                rows = mats["xl"].shape[1] // stages
                for p in range(stages):
                    part = dot_tn(mats["xl"][:, p * rows : (p + 1) * rows], mats["xr"][...])
                    part = part.astype(BF16).reshape((devices,) + block[1:])
                    for d in range(devices):
                        full[split(d) + (p,)] = part[d]
            else:
                left, right = {
                    "in": ("normed2", "ghid"),
                    "out": ("mixed", "gbr"),
                    "qkv": ("normed", "gproj"),
                }[kind]
                need(left, right)
                cols = slice(c * width, (c + 1) * width)

                def body(i, carry):
                    lanes = pl.ds(pl.multiple_of(i * 128, 128), 128)
                    part = dot_tn(mats[left][:, lanes], mats[right][:, cols])
                    per = 128 // block[0]
                    put_blocks(full, i, per, part.astype(BF16).reshape((per,) + block))
                    return carry

                lax.fori_loop(0, width // 128, body, 0)

        def split(d):
            return tuple((d // stride) % size for size, stride in reversed(dims))

        def put_blocks(ref, i, per, values):
            for q in range(per):
                d = i * per + q
                index = tuple(lax.rem(d // stride, size) for size, stride in reversed(dims))
                ref[index] = values[q]

        steps = [[compute]]
        for at, phase in enumerate(order):
            size = dims[phase][0]
            buffers = take(3)
            done = order[:at]
            last = at == len(order) - 1
            steps[-1].append(functools.partial(line_step, phase, size, 1, full, buffers, done))
            for t in range(2, size):
                steps.append([functools.partial(line_step, phase, size, t, full, buffers, done)])
            drains.append((kind, functools.partial(line_drain, phase, size, full, buffers, done)))
            steps.append([functools.partial(line_final, kind, c, phase, size, full, buffers, done, last)])
        if kind == "extra":
            steps = [[gated(step)] for step in steps]
        return steps

    def gated(step):
        def run():
            @pl.when(is_extra)
            def _():
                for part in step:
                    part()

        return run

    def block_of(full, phase, j, done):
        spot = [slice(None)] * len(dims)
        for other in done:
            spot[len(dims) - 1 - other] = where[other]
        spot[len(dims) - 1 - phase] = j
        return full.at[tuple(spot)]

    def line_copy(phase, size, t, side, full, buffers, done):
        recv, ssem, rsem = buffers
        i = where[phase]
        stride = dims[phase][1]
        if side == 0:
            j, peer = size - t + i, place + jnp.where(i < size - 1, stride, 0)
        else:
            j, peer = t - size + i, place - jnp.where(i > 0, stride, 0)
        return pltpu.make_async_remote_copy(
            src_ref=block_of(full, phase, jnp.clip(j, 0, size - 1), done),
            dst_ref=recv.at[0 if size == 2 else side, t - 1],
            send_sem=ssem.at[side, t - 1],
            recv_sem=rsem.at[side, t - 1],
            device_id={"dp": peer},
            device_id_type=MESH,
        )

    def sends(i, size, t, side):
        return (i <= t - 1) if side == 0 else (i >= size - t)

    def line_step(phase, size, t, full, buffers, done):
        i = where[phase]
        for side in range(2):
            at_end = (i == 0) if side == 0 else (i == size - 1)
            j = size - t + i if side == 0 else t - size + i
            j = jnp.clip(j, 0, size - 1)

            @pl.when(sends(i, size, t, side))
            def _():
                if t > 1:
                    @pl.when(jnp.logical_not(at_end))
                    def _():
                        line_copy(phase, size, t - 1, side, full, buffers, done).wait_recv()
                        own = block_of(full, phase, j, done)
                        got = buffers[0][0 if size == 2 else side, t - 2]
                        own[...] = (own[...].astype(F32) + got.astype(F32)).astype(BF16)

                line_copy(phase, size, t, side, full, buffers, done).start()

    def line_final(kind, c, phase, size, full, buffers, done, last):
        i = where[phase]
        own = block_of(full, phase, i, done)
        total = own
        if last:
            slots = {
                "qkv": lambda: qkv_out.at[:, c * width : (c + 1) * width],
                "in": lambda: in_out.at[:, c * width : (c + 1) * width],
                "out": lambda: out_out,
                "down": lambda: down_out.at[:, c * (width // 2) : (c + 1) * (width // 2)],
                "extra": lambda: extra_sum,
            }
            total = slots[kind]()
        lower, upper = i > 0, i < size - 1

        def arrived(side):
            line_copy(phase, size, size - 1, side, full, buffers, done).wait_recv()
            return buffers[0][0 if size == 2 else side, size - 2].astype(F32)

        @pl.when(lower & upper)
        def _():
            total[...] = (own[...].astype(F32) + arrived(0) + arrived(1)).astype(total.dtype)

        @pl.when(lower & jnp.logical_not(upper))
        def _():
            total[...] = (own[...].astype(F32) + arrived(0)).astype(total.dtype)

        @pl.when(jnp.logical_not(lower))
        def _():
            total[...] = (own[...].astype(F32) + arrived(1)).astype(total.dtype)

        if last and kind == "extra":
            for source_stage, out in ((0, embed_out), (stages - 1, head_out)):
                @pl.when(stage == source_stage)
                def _():
                    for offset in range(1, stages):
                        extra_copy(source_stage, offset, extra_recv[0 if source_stage == 0 else 1]).start()
                    out[...] = extra_sum[source_stage]

    def line_drain(phase, size, full, buffers, done):
        i = where[phase]
        for side in range(2):
            for t in range(1, size):
                @pl.when(sends(i, size, t, side))
                def _():
                    line_copy(phase, size, t, side, full, buffers, done).wait_send()

    extra_recv = take(2)
    drains = []
    chains = [chunk_steps(*item) for item in plan]
    depth = len(chains[0])
    vec_chain = [vec_step(k) for k in range(bits)] + [vec_last]
    for r in range(len(chains) + depth - 1):
        for d in [0] + list(range(depth - 1, 0, -1)):
            if 0 <= r - d < len(chains):
                for part in chains[r - d][d]:
                    part()
        if 3 <= r < 3 + len(vec_chain):
            vec_chain[r - 3]()
    vec_finish()
    for source_stage, out in ((0, embed_out), (stages - 1, head_out)):
        @pl.when(stage != source_stage)
        def _():
            got = extra_recv[0 if source_stage == 0 else 1]
            extra_copy(source_stage, 1, got).wait_recv()
            out[...] = got[...]

        @pl.when(stage == source_stage)
        def _():
            for offset in range(1, stages):
                extra_copy(source_stage, offset, extra_recv[0]).wait_send()

    vec_drain()
    for kind, drain in drains:
        if kind == "extra":
            gated([drain])()
        else:
            drain()


def run_gradients(stages, devices, saved, vec):
    dims = line_dims(devices)
    micros, tokens, width = saved[0].shape
    hid, vocab = saved[3].shape[2], saved[8].shape[2]
    plan = chunk_plan(width, hid, vocab, stages, devices)
    saved = [member.reshape(micros * tokens, member.shape[2]) for member in saved]
    vmem = pl.BlockSpec(memory_space=pltpu.VMEM)
    hbm = pl.BlockSpec(memory_space=pl.ANY)
    bits = devices.bit_length() - 1
    share = vocab // (stages * devices)
    scratch = [pltpu.VMEM(member.shape, BF16) for member in saved]
    scratch += [pltpu.SemaphoreType.DMA((len(saved),))]
    scratch += [
        pltpu.VMEM((bits + 1,) + vec.shape, F32),
        pltpu.VMEM((bits,) + vec.shape, F32),
        pltpu.SemaphoreType.DMA((bits,)),
        pltpu.SemaphoreType.DMA((bits,)),
        pltpu.VMEM((8, width), F32),
        pltpu.VMEM((8, width), F32),
        pltpu.SemaphoreType.DMA((stages,)),
        pltpu.SemaphoreType.DMA((1,)),
        pltpu.VMEM((stages, share, width), F32),
        pltpu.SemaphoreType.DMA((stages,)),
        pltpu.SemaphoreType.DMA((2,)),
        pltpu.VMEM((share, width), F32),
        pltpu.VMEM((share, width), F32),
    ]
    sizes = [size for size, _ in reversed(dims)]
    for _, _, block, turned in plan:
        scratch.append(pltpu.VMEM(tuple(sizes) + block, BF16))
        remain = list(reversed(dims))
        for size, stride in dims[::-1] if turned else dims:
            remain.remove((size, stride))
            piece = tuple(other for other, _ in remain) + block
            scratch.append(pltpu.VMEM((1 if size == 2 else 2, size - 1) + piece, BF16))
            scratch += [pltpu.SemaphoreType.DMA((2, size - 1))] * 2
    return pl.pallas_call(
        functools.partial(gradient_kernel, stages, devices, plan),
        out_shape=[
            jax.ShapeDtypeStruct((width // devices, 3 * width), F32),
            jax.ShapeDtypeStruct((width // devices, width), F32),
            jax.ShapeDtypeStruct((width // devices, hid), F32),
            jax.ShapeDtypeStruct((hid // devices, width), F32),
            jax.ShapeDtypeStruct((share, width), F32),
            jax.ShapeDtypeStruct((share, width), F32),
            jax.ShapeDtypeStruct(vec.shape, F32),
        ],
        in_specs=[hbm] * len(saved) + [vmem],
        out_specs=[vmem] * 7,
        scratch_shapes=scratch,
        compiler_params=pltpu.CompilerParams(
            collective_id=1, has_side_effects=True, vmem_limit_bytes=62 * 1024 * 1024
        ),
        name="gradients",
    )(*saved, vec)


def finish_kernel(devices, embed_g, qkv_g, out_g, in_g, down_g, head_g, vec, *outs):
    place = lax.axis_index("dp")
    width = vec.shape[1]
    (embed_o, qkv_o, qv_o, out_o, outb_o, in_o, inb_o, down_o, gain_o, shift_o, fg_o, fb_o, head_o) = outs
    embed_o[...] = embed_g[...]
    head_o[...] = head_g[...]
    for source, target in ((qkv_g, qkv_o), (out_g, out_o), (in_g, in_o), (down_g, down_o)):
        target[0] = source[...]
    lanes = width // devices
    turned = pltpu.roll(vec[0:8, :], lax.rem(width - place * lanes, width), 1)
    for row, out in ((V_QUERY, qv_o), (V_BRANCH, outb_o), (V_GAIN1, gain_o), (V_SHIFT1, shift_o)):
        out[0] = turned[row : row + 2, 0:lanes]
    share = inb_o.shape[1]
    first = place * share
    row = vec[pl.ds(V_HIDDEN + first // width, 1), :]
    wide = jnp.broadcast_to(row, (8, width))
    inb_o[...] = pltpu.roll(wide, lax.rem(width - lax.rem(first, width), width), 1)[0:1, 0:share]
    fg_o[...] = vec[V_FINAL_GAIN : V_FINAL_GAIN + 1, :]
    fb_o[...] = vec[V_FINAL_BIAS : V_FINAL_BIAS + 1, :]


def run_finish(devices, embed_g, qkv_g, out_g, in_g, down_g, head_g, vec):
    vmem = pl.BlockSpec(memory_space=pltpu.VMEM)
    width = vec.shape[1]
    lanes = width // devices

    def shape(*sizes):
        return jax.ShapeDtypeStruct(sizes, F32)

    pair = shape(1, 2, lanes)
    return pl.pallas_call(
        functools.partial(finish_kernel, devices),
        out_shape=[
            shape(*embed_g.shape),
            shape(1, *qkv_g.shape),
            pair,
            shape(1, *out_g.shape),
            pair,
            shape(1, *in_g.shape),
            shape(1, in_g.shape[1] // devices),
            shape(1, *down_g.shape),
            pair,
            pair,
            shape(1, width),
            shape(1, width),
            shape(*head_g.shape),
        ],
        in_specs=[vmem] * 7,
        out_specs=[vmem] * 13,
        name="finish",
    )(embed_g, qkv_g, out_g, in_g, down_g, head_g, vec)


def on_device(
    token_ids,
    segment_ids,
    target_ids,
    embed_table,
    qkv_weight,
    qv_bias,
    out_weight,
    out_biases,
    ff_in,
    ff_in_bias,
    ff_out,
    norm_gains,
    norm_biases,
    final_gain,
    final_bias,
    head_weight,
):
    stages = lax.axis_size("pipe")
    devices = lax.axis_size("dp")
    params = (
        embed_table,
        qkv_weight[0],
        qv_bias[0],
        out_weight[0],
        out_biases[0],
        ff_in[0],
        ff_in_bias,
        ff_out[0],
        norm_gains[0],
        norm_biases[0],
        final_gain[None],
        final_bias[None],
        head_weight,
    )
    *saved, vec = run_pipeline(stages, token_ids, segment_ids, target_ids, params)
    qkv_g, out_g, in_g, down_g, embed_g, head_g, sums = run_gradients(stages, devices, saved, vec)
    done = list(run_finish(devices, embed_g, qkv_g, out_g, in_g, down_g, head_g, sums))
    done[10], done[11] = done[10][0], done[11][0]
    return tuple(done)


def solution(mesh):
    layer3 = P("pipe", None, None)
    return jax.shard_map(
        on_device,
        mesh=mesh,
        in_specs=(
            P("dp", None),
            P("dp", None),
            P("dp", None),
            P(),
            layer3,
            layer3,
            layer3,
            layer3,
            layer3,
            P("pipe", None),
            layer3,
            layer3,
            layer3,
            P(),
            P(),
            P(),
        ),
        out_specs=(
            P(("pipe", "dp"), None),
            P("pipe", "dp", None),
            P("pipe", None, "dp"),
            P("pipe", "dp", None),
            P("pipe", None, "dp"),
            P("pipe", "dp", None),
            P("pipe", "dp"),
            P("pipe", "dp", None),
            P("pipe", None, "dp"),
            P("pipe", None, "dp"),
            P(),
            P(),
            P(("pipe", "dp"), None),
        ),
        check_vma=False,
    )
```

```python
import functools

import jax
import jax.numpy as jnp
from jax import lax
from jax.experimental import pallas as pl
from jax.experimental.pallas import tpu as pltpu
from jax.sharding import PartitionSpec as P

HEADS = 8
FRAME = 6
ROW = 128
GROUP = 2
MASKED = -1e30
GELU_A = 0.7978845608
GELU_B = 0.044715
MESH = pl.DeviceIdType.MESH
F32 = jnp.float32
BF16 = jnp.bfloat16

VEC_ROWS = 16
V_QUERY, V_VALUE, V_BRANCH, V_RESULT, V_GAIN1, V_GAIN2, V_SHIFT1, V_SHIFT2 = range(8)
V_HIDDEN = 8
V_FINAL_GAIN, V_FINAL_BIAS = 12, 13


def dot(a, b):
    return lax.dot_general(a, b, (((1,), (0,)), ((), ())), preferred_element_type=F32)


def dot_nt(a, b):
    return lax.dot_general(a, b, (((1,), (1,)), ((), ())), preferred_element_type=F32)


def dot_tn(a, b):
    return lax.dot_general(a, b, (((0,), (0,)), ((), ())), preferred_element_type=F32)


def normalise(values):
    centre = jnp.mean(values, axis=-1, keepdims=True)
    centered = values - centre
    spread = jnp.mean(centered * centered, axis=-1, keepdims=True)
    scale = lax.rsqrt(spread + 1e-05)
    return centered * scale, scale


def norm_backward(grad, normal, scale, gain):
    grad_n = grad * gain
    mean_grad = jnp.mean(grad_n, axis=-1, keepdims=True)
    mean_proj = jnp.mean(grad_n * normal, axis=-1, keepdims=True)
    return scale * (grad_n - mean_grad - normal * mean_proj)


def column_sum(values):
    return jnp.sum(values, axis=0, keepdims=True)


def stack_pair(pair, low_lanes):
    zero = jnp.zeros_like(pair)
    return jnp.concatenate(
        [jnp.where(low_lanes, pair, zero), jnp.where(low_lanes, zero, pair)], axis=0
    )


def join_pair(stacked, low_lanes):
    half = stacked.shape[0] // 2
    return jnp.where(low_lanes, stacked[:half], stacked[half:])


def pipeline_kernel(
    stages,
    micros,
    token_ids,
    segment_ids,
    target_ids,
    embed,
    qkv_w,
    qv_b,
    out_w,
    out_b,
    in_w,
    in_b,
    down_w,
    gains,
    shifts,
    fin_gain,
    fin_bias,
    head_w,
    normed_o,
    mixed_o,
    normed2_o,
    active_o,
    gres_o,
    ghid_o,
    gbr_o,
    gproj_o,
    xl_o,
    xr_o,
    vec,
    instream,
    outb,
    gin,
    gs,
    normed,
    proj,
    probs,
    mixed,
    middle,
    normed2,
    active,
    slope,
    lo,
    go,
    gmid,
    s_gres,
    s_ghid,
    s_gbr,
    s_gproj,
    s_xl,
    ids,
    frames,
    fsend,
    frecv,
    bsend,
    brecv,
    osem,
):
    stage = lax.axis_index("pipe")
    tokens, width = instream.shape[1], instream.shape[2]
    hidden_n = in_b.shape[1]
    vocab = head_w.shape[0]
    pairs = width // ROW
    chunk = 512
    is_first = stage == 0
    is_last = stage == stages - 1
    up = jnp.minimum(stage + 1, stages - 1)
    down = jnp.maximum(stage - 1, 0)

    barrier = pltpu.get_barrier_semaphore()

    @pl.when(jnp.logical_not(is_first))
    def _():
        pl.semaphore_signal(barrier, inc=1, device_id={"pipe": down}, device_id_type=MESH)

    @pl.when(jnp.logical_not(is_last))
    def _():
        pl.semaphore_signal(barrier, inc=1, device_id={"pipe": up}, device_id_type=MESH)

    pl.semaphore_wait(barrier, jnp.where(is_first | is_last, 1, 2))
    vec[...] = jnp.zeros_like(vec)
    rows_n, seq = token_ids.shape
    for index, member in enumerate((token_ids, segment_ids, target_ids)):
        ids[index] = jnp.full(ids.shape[1:], 4.0 if index == 1 else -1.0, F32)
        ids[index, 0:rows_n, 0:seq] = member[...].astype(F32)
    at_query = lax.broadcasted_iota(jnp.int32, (ROW, ROW), 1)
    at_key = lax.broadcasted_iota(jnp.int32, (ROW, ROW), 0)
    frames[...] = jnp.where(at_key < ((at_query * 43) // 256) * FRAME + FRAME, 1.0, 0.0)

    def column(index, row):
        values = jnp.broadcast_to(ids[index, pl.ds(row, 1), :], (8, ROW))
        return values.T[:, 0:1]

    def hot_rows(index, m):
        parts = [column(index, m * GROUP + r) for r in range(GROUP)]
        values = jnp.concatenate(parts, axis=0)
        places = lax.broadcasted_iota(jnp.int32, (tokens, vocab), 1).astype(F32)
        return values, jnp.where(values == places, 1.0, 0.0)

    def forward_copy(m):
        return pltpu.make_async_remote_copy(
            src_ref=outb.at[m],
            dst_ref=instream.at[m],
            send_sem=fsend.at[m],
            recv_sem=frecv.at[m],
            device_id={"pipe": up},
            device_id_type=MESH,
        )

    def backward_copy(m):
        return pltpu.make_async_remote_copy(
            src_ref=gs.at[m],
            dst_ref=gin.at[m],
            send_sem=bsend.at[m],
            recv_sem=brecv.at[m],
            device_id={"pipe": down},
            device_id_type=MESH,
        )

    def save(index, src, dst, m):
        return pltpu.make_async_copy(src, dst.at[m], osem.at[index, m])

    def saves_forward(m):
        return [
            save(0, normed.at[m], normed_o, m),
            save(1, mixed.at[m], mixed_o, m),
            save(2, normed2.at[m], normed2_o, m),
            save(3, active.at[m], active_o, m),
        ]

    def saves_backward(m):
        slot = lax.rem(m, 2)
        return [
            save(4, s_gres.at[slot], gres_o, m),
            save(5, s_ghid.at[slot], ghid_o, m),
            save(6, s_gbr.at[slot], gbr_o, m),
            save(7, s_gproj.at[slot], gproj_o, m),
        ]

    def save_xl(m):
        return save(8, s_xl.at[lax.rem(m, 2)], xl_o, m)

    def put_xl(m, value):
        @pl.when(m >= 2)
        def _():
            save_xl(m - 2).wait()

        s_xl[lax.rem(m, 2)] = value
        save_xl(m).start()

    lane_low = lax.broadcasted_iota(jnp.int32, (ROW, ROW), 1) < ROW // 2

    def forward(m):
        @pl.when(is_first)
        def _():
            hot = hot_rows(0, m)[1].astype(BF16)
            instream[m] = dot(hot, embed[...]).astype(BF16)

        @pl.when(jnp.logical_not(is_first))
        def _():
            forward_copy(m).wait_recv()

        normal, _ = normalise(instream[m].astype(F32))
        normed[m] = (normal * gains[0:1, :] + shifts[0:1, :]).astype(BF16)
        low = normed[m]
        queries = dot(low, qkv_w[:, 0:width]) + qv_b[0:1, :]
        proj[m, :, 0:width] = (queries * (ROW // 2) ** -0.5).astype(BF16)
        proj[m, :, width : 2 * width] = dot(low, qkv_w[:, width : 2 * width]).astype(BF16)
        proj[m, :, 2 * width : 3 * width] = (
            dot(low, qkv_w[:, 2 * width : 3 * width]) + qv_b[1:2, :]
        ).astype(BF16)
        masks, scores = [], []
        for r in range(GROUP):
            rows = slice(r * ROW, (r + 1) * ROW)
            kinds = lax.broadcasted_iota(jnp.int32, (16, ROW), 0).astype(F32)
            member = jnp.where(ids[1, pl.ds(m * GROUP + r, 1), :] == kinds, 1.0, 0.0).astype(BF16)
            mask = jnp.where(dot_tn(member, member) * frames[...] > 0.5, 0.0, MASKED)
            masks.append(jnp.concatenate([mask, mask], axis=1))
            for p in range(pairs):
                q = stack_pair(proj[m, rows, p * ROW : (p + 1) * ROW], lane_low)
                k = proj[m, rows, width + p * ROW : width + (p + 1) * ROW]
                scores.append(dot_nt(k, q))

        def mix(unit):
            r, p = unit // pairs, unit % pairs
            rows = slice(r * ROW, (r + 1) * ROW)
            v = proj[m, rows, 2 * width + p * ROW : 2 * width + (p + 1) * ROW]
            both = dot_tn(probs[m, unit], v)
            mixed[m, rows, p * ROW : (p + 1) * ROW] = join_pair(both, lane_low).astype(BF16)

        for unit in range(GROUP * pairs):
            masked = scores[unit] + masks[unit // pairs]
            expo = jnp.exp(masked - jnp.max(masked, axis=0, keepdims=True))
            total = jnp.sum(expo, axis=0, keepdims=True)
            probs[m, unit] = (expo * (1.0 / total)).astype(BF16)
            if unit:
                mix(unit - 1)
        mix(GROUP * pairs - 1)
        mid = instream[m].astype(F32) + (dot(mixed[m], out_w[...]) + out_b[0:1, :])
        middle[m] = mid
        normal2, _ = normalise(mid)
        normed2[m] = (normal2 * gains[1:2, :] + shifts[1:2, :]).astype(BF16)
        low2 = normed2[m]
        parts = hidden_n // chunk

        def spread(c):
            return dot(low2, in_w[:, c * chunk : (c + 1) * chunk])

        total, ahead = None, spread(0)
        for c in range(parts):
            cols = slice(c * chunk, (c + 1) * chunk)
            hid = ahead + in_b[0:1, cols]
            if c + 1 < parts:
                ahead = spread(c + 1)
            square = hid * hid
            tan = jnp.tanh(hid * (GELU_A + (GELU_A * GELU_B) * square))
            half = 0.5 + 0.5 * tan
            act = (hid * half).astype(BF16)
            active[m, :, cols] = act
            rise = (1.0 - tan * tan) * (0.5 * GELU_A + (1.5 * GELU_A * GELU_B) * square)
            slope[m, :, cols] = (half + hid * rise).astype(BF16)
            term = dot(act, down_w[cols, :])
            total = term if total is None else total + term
        for copy in saves_forward(m):
            copy.start()
        lo[...] = middle[m] + (total + out_b[1:2, :])

        @pl.when(jnp.logical_not(is_last))
        def _():
            outb[m] = lo[...].astype(BF16)
            forward_copy(m).start()

    def head(m):
        normal, scale = normalise(lo[...])
        outb[m] = (normal * fin_gain[...] + fin_bias[...]).astype(BF16)
        save(9, outb.at[m], xr_o, m).start()
        logits = dot_nt(outb[m], head_w[...])
        top = jnp.max(logits, axis=-1, keepdims=True)
        expo = jnp.exp(logits - top)
        total = jnp.sum(expo, axis=-1, keepdims=True)
        target, hot = hot_rows(2, m)
        grad_logits = jnp.where(target >= 0.0, expo * (1.0 / total) - hot, 0.0).astype(BF16)
        put_xl(m, grad_logits)
        grad_final = dot(grad_logits, head_w[...])
        vec[V_FINAL_GAIN : V_FINAL_GAIN + 1, :] += column_sum(grad_final * normal)
        vec[V_FINAL_BIAS : V_FINAL_BIAS + 1, :] += column_sum(grad_final)
        go[...] = norm_backward(grad_final, normal, scale, fin_gain[...])

    def backward(m):
        slot = lax.rem(m, 2)

        @pl.when(m >= 2)
        def _():
            for copy in saves_backward(m - 2):
                copy.wait()

        @pl.when(jnp.logical_not(is_last))
        def _():
            backward_copy(m).wait_recv()
            go[...] = gin[m].astype(F32)

        s_gres[slot] = go[...].astype(BF16)
        gres = s_gres[slot]
        parts = hidden_n // chunk

        def spread(c):
            return dot_nt(gres, down_w[c * chunk : (c + 1) * chunk, :])

        total, ahead = None, spread(0)
        for c in range(parts):
            cols = slice(c * chunk, (c + 1) * chunk)
            gact = ahead
            if c + 1 < parts:
                ahead = spread(c + 1)
            ghid = (gact * slope[m, :, cols].astype(F32)).astype(BF16)
            s_ghid[slot, :, cols] = ghid
            term = dot_nt(ghid, in_w[:, cols])
            total = term if total is None else total + term
        normal2, scale2 = normalise(middle[m])
        vec[V_GAIN2 : V_GAIN2 + 1, :] += column_sum(total * normal2)
        vec[V_SHIFT2 : V_SHIFT2 + 1, :] += column_sum(total)
        gmid[...] = go[...] + norm_backward(total, normal2, scale2, gains[1:2, :])
        s_gbr[slot] = gmid[...].astype(BF16)
        gbr = s_gbr[slot]
        gmix = dot_nt(gbr, out_w[...]).astype(BF16)
        grads = []
        for r in range(GROUP):
            rows = slice(r * ROW, (r + 1) * ROW)
            for p in range(pairs):
                gm = stack_pair(gmix[rows, p * ROW : (p + 1) * ROW], lane_low)
                vlanes = slice(2 * width + p * ROW, 2 * width + (p + 1) * ROW)
                grads.append(dot_nt(proj[m, rows, vlanes], gm))
                s_gproj[slot, rows, vlanes] = dot(probs[m, r * pairs + p], gm).astype(BF16)

        def pull(unit, gsc):
            r, p = unit // pairs, unit % pairs
            rows = slice(r * ROW, (r + 1) * ROW)
            lanes = slice(p * ROW, (p + 1) * ROW)
            klanes = slice(width + p * ROW, width + (p + 1) * ROW)
            q = stack_pair(proj[m, rows, lanes], lane_low)
            s_gproj[slot, rows, klanes] = dot(gsc, q).astype(BF16)
            gq = join_pair(dot_tn(gsc, proj[m, rows, klanes]), lane_low) * (ROW // 2) ** -0.5
            s_gproj[slot, rows, lanes] = gq.astype(BF16)

        waiting = None
        for unit in range(GROUP * pairs):
            weights = probs[m, unit].astype(F32)
            inner = jnp.sum(weights * grads[unit], axis=0, keepdims=True)
            gsc = (weights * (grads[unit] - inner)).astype(BF16)
            if waiting is not None:
                pull(unit - 1, waiting)
            waiting = gsc
        pull(GROUP * pairs - 1, waiting)
        for copy in saves_backward(m):
            copy.start()
        gproj = s_gproj[slot]
        gnormed = dot_nt(gproj, qkv_w[...])
        normal, scale = normalise(instream[m].astype(F32))
        vec[V_GAIN1 : V_GAIN1 + 1, :] += column_sum(gnormed * normal)
        vec[V_SHIFT1 : V_SHIFT1 + 1, :] += column_sum(gnormed)
        gs[m] = (gmid[...] + norm_backward(gnormed, normal, scale, gains[0:1, :])).astype(BF16)

        @pl.when(is_first)
        def _():
            save(9, gs.at[m], xr_o, m).start()

        @pl.when(jnp.logical_not(is_first))
        def _():
            backward_copy(m).start()

    def tick(t, carry):
        m_forward = t - stage
        m_backward = t - (2 * (stages - 1) - stage)

        @pl.when((m_forward >= 0) & (m_forward < micros))
        def _():
            forward(m_forward)

        @pl.when((m_backward >= 0) & (m_backward < micros))
        def _():
            @pl.when(is_last)
            def _():
                head(m_backward)

            backward(m_backward)

        return carry

    lax.fori_loop(0, micros + 2 * (stages - 1), tick, 0)

    for m in range(micros):
        for copy in saves_forward(m):
            copy.wait()

        @pl.when(jnp.logical_not(is_last))
        def _():
            forward_copy(m).wait_send()

        @pl.when(jnp.logical_not(is_first))
        def _():
            backward_copy(m).wait_send()

        @pl.when(is_first)
        def _():
            save(9, gs.at[m], xr_o, m).wait()

        @pl.when(is_last)
        def _():
            save(9, outb.at[m], xr_o, m).wait()

    for m in range(max(0, micros - 2), micros):
        for copy in saves_backward(m):
            copy.wait()

        @pl.when(is_last)
        def _():
            save_xl(m).wait()


def run_pipeline(stages, token_ids, segment_ids, target_ids, params):
    embed, in_w, head_w = params[0], params[5], params[12]
    width = embed.shape[1]
    vocab = head_w.shape[0]
    hid = in_w.shape[1]
    tokens = GROUP * ROW
    micros = token_ids.shape[0] // GROUP
    pairs = width // ROW
    vmem = pl.BlockSpec(memory_space=pltpu.VMEM)
    hbm = pl.BlockSpec(memory_space=pl.ANY)

    def kept(columns):
        return jax.ShapeDtypeStruct((micros, tokens, columns), BF16)

    def scratch(lead, columns, kind=BF16):
        return pltpu.VMEM((lead, tokens, columns), kind)

    out_shape = [
        kept(width),
        kept(width),
        kept(width),
        kept(hid),
        kept(width),
        kept(hid),
        kept(width),
        kept(3 * width),
        kept(vocab),
        kept(width),
        jax.ShapeDtypeStruct((VEC_ROWS, width), F32),
    ]
    return pl.pallas_call(
        functools.partial(pipeline_kernel, stages, micros),
        out_shape=out_shape,
        in_specs=[vmem] * 16,
        out_specs=[hbm] * 10 + [vmem],
        scratch_shapes=[
            scratch(micros, width),
            scratch(micros, width),
            scratch(micros, width),
            scratch(micros, width),
            scratch(micros, width),
            scratch(micros, 3 * width),
            pltpu.VMEM((micros, GROUP * pairs, ROW, 2 * ROW), BF16),
            scratch(micros, width),
            scratch(micros, width, F32),
            scratch(micros, width),
            scratch(micros, hid),
            scratch(micros, hid),
            pltpu.VMEM((tokens, width), F32),
            pltpu.VMEM((tokens, width), F32),
            pltpu.VMEM((tokens, width), F32),
            scratch(2, width),
            scratch(2, hid),
            scratch(2, width),
            scratch(2, 3 * width),
            scratch(2, vocab),
            pltpu.VMEM((3, 16, ROW), F32),
            pltpu.VMEM((ROW, ROW), F32),
            pltpu.SemaphoreType.DMA((micros,)),
            pltpu.SemaphoreType.DMA((micros,)),
            pltpu.SemaphoreType.DMA((micros,)),
            pltpu.SemaphoreType.DMA((micros,)),
            pltpu.SemaphoreType.DMA((10, micros)),
        ],
        compiler_params=pltpu.CompilerParams(
            collective_id=0, has_side_effects=True, vmem_limit_bytes=62 * 1024 * 1024
        ),
        name="pipeline",
    )(token_ids, segment_ids, target_ids, *params)


def line_dims(devices):
    dims, stride = [], 1
    if devices == 8:
        return [(2, 1), (4, 2)]
    while devices > 1:
        size = 4 if devices % 4 == 0 else 2
        dims.append((size, stride))
        stride *= size
        devices //= size
    return dims


def chunk_plan(width, hid, vocab, stages, devices):
    slim, deep = width // devices, hid // devices
    plan = [("out", 0, (slim, width), False)]
    for c in range(2):
        plan.append(("down", c, (deep, width // 2), False))
    plan.append(("extra", 0, (stages, vocab // (stages * devices), width), False))
    for c in range(hid // width):
        plan.append(("in", c, (slim, width), c == 1))
    for c in range(3):
        plan.append(("qkv", c, (slim, width), c == 0))
    return plan


def gradient_kernel(stages, devices, plan, *refs):
    dims = line_dims(devices)
    refs = list(refs)

    def take(amount):
        head, refs[:] = refs[:amount], refs[amount:]
        return head

    inputs = take(10)
    vec_in, token_ids = take(2)
    qkv_out, out_out, in_out, down_out, embed_out, head_out, vec_out = take(7)
    local = take(10)
    in_sem = take(1)[0]
    turned_left, turned_xl = take(2)
    mats = dict(
        zip(
            ("normed", "mixed", "normed2", "active", "gres", "ghid", "gbr", "gproj", "xl", "xr"),
            local,
        )
    )
    names = list(mats)
    stage = lax.axis_index("pipe")
    place = lax.axis_index("dp")
    is_extra = (stage == 0) | (stage == stages - 1)
    width = mats["normed"].shape[1]
    where = [lax.rem(place // stride, size) for size, stride in dims]

    barrier = pltpu.get_barrier_semaphore()

    def greet(offset, carry):
        peer = lax.rem(place + offset, devices)
        pl.semaphore_signal(barrier, inc=1, device_id={"dp": peer}, device_id_type=MESH)
        return carry

    def greet_stage(offset, carry):
        peer = lax.rem(stage + offset, stages)
        pl.semaphore_signal(barrier, inc=1, device_id={"pipe": peer}, device_id_type=MESH)
        return carry

    lax.fori_loop(1, devices, greet, 0)
    lax.fori_loop(1, stages, greet_stage, 0)

    def load(name):
        i = names.index(name)
        return pltpu.make_async_copy(inputs[i], mats[name], in_sem.at[i])

    order = ["mixed", "gbr", "gres", "active", "normed2", "ghid", "normed", "gproj"]
    for name in order[:2]:
        load(name).start()

    for name in order[2:]:
        load(name).start()

    @pl.when(is_extra)
    def _():
        load("xr").start()

    @pl.when(stage == stages - 1)
    def _():
        load("xl").start()

    pl.semaphore_wait(barrier, devices - 1 + stages - 1)
    loaded = set()

    def need(*wanted):
        for name in wanted:
            if name not in loaded:
                loaded.add(name)
                load(name).wait()

    def identity(size):
        here = lax.broadcasted_iota(jnp.int32, (size, size), 0)
        there = lax.broadcasted_iota(jnp.int32, (size, size), 1)
        return jnp.where(here == there, 1.0, 0.0).astype(BF16)

    def turn(name):
        unit = identity(256)
        for q in range(width // 256):
            part = dot_nt(unit, mats[name][:, q * 256 : (q + 1) * 256])
            turned_left[q * 256 : (q + 1) * 256, :] = part.astype(BF16)

    bits = devices.bit_length() - 1
    vec_send, vec_recv = take(2)
    vec_sems = take(2)

    def vec_copy(k):
        peer = jnp.bitwise_xor(place, 1 << k)
        return pltpu.make_async_remote_copy(
            src_ref=vec_send.at[k],
            dst_ref=vec_recv.at[k],
            send_sem=vec_sems[0].at[k],
            recv_sem=vec_sems[1].at[k],
            device_id={"dp": peer},
            device_id_type=MESH,
        )

    def vec_step(k):
        def run():
            if k == 0:
                need("gres", "ghid", "gbr", "gproj")
                vec_send[0] = vec_in[...]
                ones = jnp.ones((16, mats["gres"].shape[0]), BF16)
                for name, start, row in (
                    ("gproj", 0, V_QUERY),
                    ("gproj", 2 * width, V_VALUE),
                    ("gbr", 0, V_BRANCH),
                    ("gres", 0, V_RESULT),
                ):
                    part = dot(ones, mats[name][:, start : start + width])
                    vec_send[0, row : row + 1, :] = part[0:1, :]
                for q in range(mats["ghid"].shape[1] // width):
                    part = dot(ones, mats["ghid"][:, q * width : (q + 1) * width])
                    vec_send[0, V_HIDDEN + q : V_HIDDEN + q + 1, :] = part[0:1, :]
            else:
                vec_copy(k - 1).wait_recv()
                vec_send[k] = vec_send[k - 1] + vec_recv[k - 1]
            if k < bits:
                vec_copy(k).start()

        return run

    final_send, final_recv = take(2)
    final_sems = take(2)

    def final_copy(offset):
        peer = lax.rem(stages - 1 + offset, stages)
        return pltpu.make_async_remote_copy(
            src_ref=final_send,
            dst_ref=final_recv,
            send_sem=final_sems[0].at[offset],
            recv_sem=final_sems[1].at[0],
            device_id={"pipe": peer},
            device_id_type=MESH,
        )

    def vec_last():
        vec_step(bits)()
        vec_out[...] = vec_send[bits]

        @pl.when(stage == stages - 1)
        def _():
            final_send[...] = vec_send[bits, 8:16, :]
            for offset in range(1, stages):
                final_copy(offset).start()

    def vec_finish():
        @pl.when(stage != stages - 1)
        def _():
            final_copy(1).wait_recv()
            vec_out[V_FINAL_GAIN : V_FINAL_BIAS + 1, :] = final_recv[
                V_FINAL_GAIN - 8 : V_FINAL_BIAS - 7, :
            ]

    def vec_drain():
        for k in range(bits):
            vec_copy(k).wait_send()

        @pl.when(stage == stages - 1)
        def _():
            for offset in range(1, stages):
                final_copy(offset).wait_send()

    extra_sum, extra_send_sem, extra_recv_sem = take(3)

    def extra_copy(source, offset, target):
        peer = lax.rem(source + offset, stages)
        return pltpu.make_async_remote_copy(
            src_ref=extra_sum.at[peer],
            dst_ref=target,
            send_sem=extra_send_sem.at[offset],
            recv_sem=extra_recv_sem.at[0 if source == 0 else 1],
            device_id={"pipe": peer},
            device_id_type=MESH,
        )

    def chunk_steps(kind, c, block, turned):
        order = list(range(len(dims)))
        if turned:
            order.reverse()
        full = take(1)[0]

        def compute():
            if kind == "down":
                need("gres", "active")
                if c == 0:
                    turn("gres")
                half, deep = width // 2, 256
                per = deep // block[0]
                unit = identity(deep)

                def body(i, carry):
                    lanes = pl.ds(pl.multiple_of(i * deep, deep), deep)
                    part = dot(turned_left[c * half : (c + 1) * half, :], mats["active"][:, lanes])
                    part = dot_nt(unit, part.astype(BF16)).astype(BF16)
                    put_blocks(full, i, per, part.reshape((per,) + block))
                    return carry

                lax.fori_loop(0, mats["active"].shape[1] // deep, body, 0)
            elif kind == "extra":
                load("xr").wait()
                vocab = turned_xl.shape[0]

                @pl.when(stage == 0)
                def _():
                    rows_n, seq = token_ids.shape
                    places = lax.broadcasted_iota(jnp.int32, (vocab, ROW), 0)
                    gap = jnp.full((1, ROW - seq), -1, jnp.int32)
                    for r in range(rows_n):
                        row = jnp.concatenate([token_ids[r : r + 1, :], gap], axis=1)
                        hot = jnp.where(places == row, 1.0, 0.0)
                        turned_xl[:, r * ROW : (r + 1) * ROW] = hot.astype(BF16)

                @pl.when(stage == stages - 1)
                def _():
                    load("xl").wait()
                    unit = identity(256)
                    for q in range(vocab // 256):
                        part = dot_nt(unit, mats["xl"][:, q * 256 : (q + 1) * 256])
                        turned_xl[q * 256 : (q + 1) * 256, :] = part.astype(BF16)

                rows = vocab // stages
                for p in range(stages):
                    part = dot(turned_xl[p * rows : (p + 1) * rows, :], mats["xr"][...])
                    part = part.astype(BF16).reshape((devices,) + block[1:])
                    for d in range(devices):
                        full[split(d) + (p,)] = part[d]
            else:
                left, right = {
                    "in": ("normed2", "ghid"),
                    "out": ("mixed", "gbr"),
                    "qkv": ("normed", "gproj"),
                }[kind]
                need(left, right)
                if c == 0:
                    turn(left)
                cols = slice(c * width, (c + 1) * width)
                per = 256 // block[0]

                def body(i, carry):
                    lines = pl.ds(pl.multiple_of(i * 256, 256), 256)
                    part = dot(turned_left[lines, :], mats[right][:, cols]).astype(BF16)
                    put_blocks(full, i, per, part.reshape((per,) + block))
                    return carry

                lax.fori_loop(0, width // 256, body, 0)

        def split(d):
            return tuple((d // stride) % size for size, stride in reversed(dims))

        def put_blocks(ref, i, per, values):
            for q in range(per):
                d = i * per + q
                index = tuple(lax.rem(d // stride, size) for size, stride in reversed(dims))
                ref[index] = values[q]

        steps = [[compute]]
        for at, phase in enumerate(order):
            size = dims[phase][0]
            buffers = take(3)
            done = order[:at]
            last = at == len(order) - 1
            steps[-1].append(functools.partial(line_step, phase, size, 1, full, buffers, done))
            for t in range(2, size):
                steps.append([functools.partial(line_step, phase, size, t, full, buffers, done)])
            drains.append((kind, functools.partial(line_drain, phase, size, full, buffers, done)))
            steps.append([functools.partial(line_final, kind, c, phase, size, full, buffers, done, last)])
        if kind == "extra":
            steps = [[gated(step)] for step in steps]
        return steps

    def gated(step):
        def run():
            @pl.when(is_extra)
            def _():
                for part in step:
                    part()

        return run

    def block_of(full, phase, j, done):
        spot = [slice(None)] * len(dims)
        for other in done:
            spot[len(dims) - 1 - other] = where[other]
        spot[len(dims) - 1 - phase] = j
        return full.at[tuple(spot)]

    def line_copy(phase, size, t, side, full, buffers, done):
        recv, ssem, rsem = buffers
        i = where[phase]
        stride = dims[phase][1]
        if side == 0:
            j, peer = size - t + i, place + jnp.where(i < size - 1, stride, 0)
        else:
            j, peer = t - size + i, place - jnp.where(i > 0, stride, 0)
        return pltpu.make_async_remote_copy(
            src_ref=block_of(full, phase, jnp.clip(j, 0, size - 1), done),
            dst_ref=recv.at[0 if size == 2 else side, t - 1],
            send_sem=ssem.at[side, t - 1],
            recv_sem=rsem.at[side, t - 1],
            device_id={"dp": peer},
            device_id_type=MESH,
        )

    def sends(i, size, t, side):
        return (i <= t - 1) if side == 0 else (i >= size - t)

    def line_step(phase, size, t, full, buffers, done):
        i = where[phase]
        for side in range(2):
            at_end = (i == 0) if side == 0 else (i == size - 1)
            j = size - t + i if side == 0 else t - size + i
            j = jnp.clip(j, 0, size - 1)

            @pl.when(sends(i, size, t, side))
            def _():
                if t > 1:
                    @pl.when(jnp.logical_not(at_end))
                    def _():
                        line_copy(phase, size, t - 1, side, full, buffers, done).wait_recv()
                        own = block_of(full, phase, j, done)
                        got = buffers[0][0 if size == 2 else side, t - 2]
                        own[...] = (own[...].astype(F32) + got.astype(F32)).astype(BF16)

                line_copy(phase, size, t, side, full, buffers, done).start()

    def line_final(kind, c, phase, size, full, buffers, done, last):
        i = where[phase]
        own = block_of(full, phase, i, done)
        total = own
        if last:
            slots = {
                "qkv": lambda: qkv_out.at[:, c * width : (c + 1) * width],
                "in": lambda: in_out.at[:, c * width : (c + 1) * width],
                "out": lambda: out_out,
                "down": lambda: down_out.at[:, c * (width // 2) : (c + 1) * (width // 2)],
                "extra": lambda: extra_sum,
            }
            total = slots[kind]()
        lower, upper = i > 0, i < size - 1

        def arrived(side):
            line_copy(phase, size, size - 1, side, full, buffers, done).wait_recv()
            return buffers[0][0 if size == 2 else side, size - 2].astype(F32)

        @pl.when(lower & upper)
        def _():
            total[...] = (own[...].astype(F32) + arrived(0) + arrived(1)).astype(total.dtype)

        @pl.when(lower & jnp.logical_not(upper))
        def _():
            total[...] = (own[...].astype(F32) + arrived(0)).astype(total.dtype)

        @pl.when(jnp.logical_not(lower))
        def _():
            total[...] = (own[...].astype(F32) + arrived(1)).astype(total.dtype)

        if last and kind == "extra":
            for source_stage, out in ((0, embed_out), (stages - 1, head_out)):
                @pl.when(stage == source_stage)
                def _():
                    for offset in range(1, stages):
                        extra_copy(source_stage, offset, extra_recv[0 if source_stage == 0 else 1]).start()
                    out[...] = extra_sum[source_stage]

    def line_drain(phase, size, full, buffers, done):
        i = where[phase]
        for side in range(2):
            for t in range(1, size):
                @pl.when(sends(i, size, t, side))
                def _():
                    line_copy(phase, size, t, side, full, buffers, done).wait_send()

    extra_recv = take(2)
    drains = []
    chains = [chunk_steps(*item) for item in plan]
    depth = len(chains[0])
    vec_chain = [vec_step(k) for k in range(bits)] + [vec_last]
    for r in range(len(chains) + depth - 1):
        for d in [0] + list(range(depth - 1, 0, -1)):
            if 0 <= r - d < len(chains):
                for part in chains[r - d][d]:
                    part()
        if 3 <= r < 3 + len(vec_chain):
            vec_chain[r - 3]()
    vec_finish()
    for source_stage, out in ((0, embed_out), (stages - 1, head_out)):
        @pl.when(stage != source_stage)
        def _():
            got = extra_recv[0 if source_stage == 0 else 1]
            extra_copy(source_stage, 1, got).wait_recv()
            out[...] = got[...]

        @pl.when(stage == source_stage)
        def _():
            for offset in range(1, stages):
                extra_copy(source_stage, offset, extra_recv[0]).wait_send()

    vec_drain()
    for kind, drain in drains:
        if kind == "extra":
            gated([drain])()
        else:
            drain()


def run_gradients(stages, devices, saved, vec, token_ids):
    dims = line_dims(devices)
    micros, tokens, width = saved[0].shape
    hid, vocab = saved[3].shape[2], saved[8].shape[2]
    plan = chunk_plan(width, hid, vocab, stages, devices)
    saved = [member.reshape(micros * tokens, member.shape[2]) for member in saved]
    vmem = pl.BlockSpec(memory_space=pltpu.VMEM)
    hbm = pl.BlockSpec(memory_space=pl.ANY)
    bits = devices.bit_length() - 1
    share = vocab // (stages * devices)
    scratch = [pltpu.VMEM(member.shape, BF16) for member in saved]
    scratch += [pltpu.SemaphoreType.DMA((len(saved),))]
    scratch += [pltpu.VMEM((width, micros * tokens), BF16), pltpu.VMEM((vocab, micros * tokens), BF16)]
    scratch += [
        pltpu.VMEM((bits + 1,) + vec.shape, F32),
        pltpu.VMEM((bits,) + vec.shape, F32),
        pltpu.SemaphoreType.DMA((bits,)),
        pltpu.SemaphoreType.DMA((bits,)),
        pltpu.VMEM((8, width), F32),
        pltpu.VMEM((8, width), F32),
        pltpu.SemaphoreType.DMA((stages,)),
        pltpu.SemaphoreType.DMA((1,)),
        pltpu.VMEM((stages, share, width), F32),
        pltpu.SemaphoreType.DMA((stages,)),
        pltpu.SemaphoreType.DMA((2,)),
        pltpu.VMEM((share, width), F32),
        pltpu.VMEM((share, width), F32),
    ]
    sizes = [size for size, _ in reversed(dims)]
    for _, _, block, turned in plan:
        scratch.append(pltpu.VMEM(tuple(sizes) + block, BF16))
        remain = list(reversed(dims))
        for size, stride in dims[::-1] if turned else dims:
            remain.remove((size, stride))
            piece = tuple(other for other, _ in remain) + block
            scratch.append(pltpu.VMEM((1 if size == 2 else 2, size - 1) + piece, BF16))
            scratch += [pltpu.SemaphoreType.DMA((2, size - 1))] * 2
    return pl.pallas_call(
        functools.partial(gradient_kernel, stages, devices, plan),
        out_shape=[
            jax.ShapeDtypeStruct((width // devices, 3 * width), F32),
            jax.ShapeDtypeStruct((width // devices, width), F32),
            jax.ShapeDtypeStruct((width // devices, hid), F32),
            jax.ShapeDtypeStruct((hid // devices, width), F32),
            jax.ShapeDtypeStruct((share, width), F32),
            jax.ShapeDtypeStruct((share, width), F32),
            jax.ShapeDtypeStruct(vec.shape, F32),
        ],
        in_specs=[hbm] * len(saved) + [vmem] * 2,
        out_specs=[vmem] * 7,
        scratch_shapes=scratch,
        compiler_params=pltpu.CompilerParams(
            collective_id=1, has_side_effects=True, vmem_limit_bytes=62 * 1024 * 1024
        ),
        name="gradients",
    )(*saved, vec, token_ids)


def finish_kernel(devices, embed_g, qkv_g, out_g, in_g, down_g, head_g, vec, *outs):
    place = lax.axis_index("dp")
    width = vec.shape[1]
    (embed_o, qkv_o, qv_o, out_o, outb_o, in_o, inb_o, down_o, gain_o, shift_o, fg_o, fb_o, head_o) = outs
    embed_o[...] = embed_g[...]
    head_o[...] = head_g[...]
    for source, target in ((qkv_g, qkv_o), (out_g, out_o), (in_g, in_o), (down_g, down_o)):
        target[0] = source[...]
    lanes = width // devices
    turned = pltpu.roll(vec[0:8, :], lax.rem(width - place * lanes, width), 1)
    for row, out in ((V_QUERY, qv_o), (V_BRANCH, outb_o), (V_GAIN1, gain_o), (V_SHIFT1, shift_o)):
        out[0] = turned[row : row + 2, 0:lanes]
    share = inb_o.shape[1]
    first = place * share
    row = vec[pl.ds(V_HIDDEN + first // width, 1), :]
    wide = jnp.broadcast_to(row, (8, width))
    inb_o[...] = pltpu.roll(wide, lax.rem(width - lax.rem(first, width), width), 1)[0:1, 0:share]
    fg_o[...] = vec[V_FINAL_GAIN : V_FINAL_GAIN + 1, :]
    fb_o[...] = vec[V_FINAL_BIAS : V_FINAL_BIAS + 1, :]


def run_finish(devices, embed_g, qkv_g, out_g, in_g, down_g, head_g, vec):
    vmem = pl.BlockSpec(memory_space=pltpu.VMEM)
    width = vec.shape[1]
    lanes = width // devices

    def shape(*sizes):
        return jax.ShapeDtypeStruct(sizes, F32)

    pair = shape(1, 2, lanes)
    return pl.pallas_call(
        functools.partial(finish_kernel, devices),
        out_shape=[
            shape(*embed_g.shape),
            shape(1, *qkv_g.shape),
            pair,
            shape(1, *out_g.shape),
            pair,
            shape(1, *in_g.shape),
            shape(1, in_g.shape[1] // devices),
            shape(1, *down_g.shape),
            pair,
            pair,
            shape(1, width),
            shape(1, width),
            shape(*head_g.shape),
        ],
        in_specs=[vmem] * 7,
        out_specs=[vmem] * 13,
        name="finish",
    )(embed_g, qkv_g, out_g, in_g, down_g, head_g, vec)


def on_device(
    token_ids,
    segment_ids,
    target_ids,
    embed_table,
    qkv_weight,
    qv_bias,
    out_weight,
    out_biases,
    ff_in,
    ff_in_bias,
    ff_out,
    norm_gains,
    norm_biases,
    final_gain,
    final_bias,
    head_weight,
):
    stages = lax.axis_size("pipe")
    devices = lax.axis_size("dp")
    params = (
        embed_table,
        qkv_weight[0],
        qv_bias[0],
        out_weight[0],
        out_biases[0],
        ff_in[0],
        ff_in_bias,
        ff_out[0],
        norm_gains[0],
        norm_biases[0],
        final_gain[None],
        final_bias[None],
        head_weight,
    )
    *saved, vec = run_pipeline(stages, token_ids, segment_ids, target_ids, params)
    qkv_g, out_g, in_g, down_g, embed_g, head_g, sums = run_gradients(stages, devices, saved, vec, token_ids)
    done = list(run_finish(devices, embed_g, qkv_g, out_g, in_g, down_g, head_g, sums))
    done[10], done[11] = done[10][0], done[11][0]
    return tuple(done)


def solution(mesh):
    layer3 = P("pipe", None, None)
    return jax.shard_map(
        on_device,
        mesh=mesh,
        in_specs=(
            P("dp", None),
            P("dp", None),
            P("dp", None),
            P(),
            layer3,
            layer3,
            layer3,
            layer3,
            layer3,
            P("pipe", None),
            layer3,
            layer3,
            layer3,
            P(),
            P(),
            P(),
        ),
        out_specs=(
            P(("pipe", "dp"), None),
            P("pipe", "dp", None),
            P("pipe", None, "dp"),
            P("pipe", "dp", None),
            P("pipe", None, "dp"),
            P("pipe", "dp", None),
            P("pipe", "dp"),
            P("pipe", "dp", None),
            P("pipe", None, "dp"),
            P("pipe", None, "dp"),
            P(),
            P(),
            P(("pipe", "dp"), None),
        ),
        check_vma=False,
    )
```

```python
import functools

import jax
import jax.numpy as jnp
from jax import lax
from jax.experimental import pallas as pl
from jax.experimental.pallas import tpu as pltpu
from jax.sharding import PartitionSpec as P

HEADS = 8
FRAME = 6
ROW = 128
GROUP = 2
MASKED = -1e30
GELU_A = 0.7978845608
GELU_B = 0.044715
MESH = pl.DeviceIdType.MESH
F32 = jnp.float32
BF16 = jnp.bfloat16

VEC_ROWS = 16
V_QUERY, V_VALUE, V_BRANCH, V_RESULT, V_GAIN1, V_GAIN2, V_SHIFT1, V_SHIFT2 = range(8)
V_HIDDEN = 8
V_FINAL_GAIN, V_FINAL_BIAS = 12, 13


def dot(a, b):
    return lax.dot_general(a, b, (((1,), (0,)), ((), ())), preferred_element_type=F32)


def dot_nt(a, b):
    return lax.dot_general(a, b, (((1,), (1,)), ((), ())), preferred_element_type=F32)


def dot_tn(a, b):
    return lax.dot_general(a, b, (((0,), (0,)), ((), ())), preferred_element_type=F32)


def normalise(values):
    centre = jnp.mean(values, axis=-1, keepdims=True)
    centered = values - centre
    spread = jnp.mean(centered * centered, axis=-1, keepdims=True)
    scale = lax.rsqrt(spread + 1e-05)
    return centered * scale, scale


def norm_backward(grad, normal, scale, gain):
    grad_n = grad * gain
    mean_grad = jnp.mean(grad_n, axis=-1, keepdims=True)
    mean_proj = jnp.mean(grad_n * normal, axis=-1, keepdims=True)
    return scale * (grad_n - mean_grad - normal * mean_proj)


def column_sum(values):
    return jnp.sum(values, axis=0, keepdims=True)


def stack_pair(pair, low_lanes):
    zero = jnp.zeros_like(pair)
    return jnp.concatenate(
        [jnp.where(low_lanes, pair, zero), jnp.where(low_lanes, zero, pair)], axis=0
    )


def join_pair(stacked, low_lanes):
    half = stacked.shape[0] // 2
    return jnp.where(low_lanes, stacked[:half], stacked[half:])


def pipeline_kernel(
    stages,
    sizes,
    token_ids,
    segment_ids,
    target_ids,
    embed,
    qkv_w,
    qv_b,
    out_w,
    out_b,
    in_w,
    in_b,
    down_w,
    gains,
    shifts,
    fin_gain,
    fin_bias,
    head_w,
    normed_o,
    mixed_o,
    normed2_o,
    active_o,
    gres_o,
    ghid_o,
    gbr_o,
    gproj_o,
    xl_o,
    xr_o,
    vec,
    instream,
    outb,
    gin,
    gs,
    normed,
    proj,
    probs,
    mixed,
    middle,
    normed2,
    active,
    slope,
    lo,
    go,
    gmid,
    s_gres,
    s_ghid,
    s_gbr,
    s_gproj,
    s_xl,
    ids,
    frames,
    fsend,
    frecv,
    bsend,
    brecv,
    osem,
):
    stage = lax.axis_index("pipe")
    width = instream.shape[2]
    micros = len(sizes)
    hidden_n = in_b.shape[1]
    vocab = head_w.shape[0]
    pairs = width // ROW
    chunk = 512
    is_first = stage == 0
    is_last = stage == stages - 1
    up = jnp.minimum(stage + 1, stages - 1)
    down = jnp.maximum(stage - 1, 0)

    barrier = pltpu.get_barrier_semaphore()

    @pl.when(jnp.logical_not(is_first))
    def _():
        pl.semaphore_signal(barrier, inc=1, device_id={"pipe": down}, device_id_type=MESH)

    @pl.when(jnp.logical_not(is_last))
    def _():
        pl.semaphore_signal(barrier, inc=1, device_id={"pipe": up}, device_id_type=MESH)

    pl.semaphore_wait(barrier, jnp.where(is_first | is_last, 1, 2))
    vec[...] = jnp.zeros_like(vec)
    rows_n, seq = token_ids.shape
    for index, member in enumerate((token_ids, segment_ids, target_ids)):
        ids[index] = jnp.full(ids.shape[1:], 4.0 if index == 1 else -1.0, F32)
        ids[index, 0:rows_n, 0:seq] = member[...].astype(F32)
    at_query = lax.broadcasted_iota(jnp.int32, (ROW, ROW), 1)
    at_key = lax.broadcasted_iota(jnp.int32, (ROW, ROW), 0)
    frames[...] = jnp.where(at_key < ((at_query * 43) // 256) * FRAME + FRAME, 1.0, 0.0)

    def column(index, row):
        values = jnp.broadcast_to(ids[index, pl.ds(row, 1), :], (8, ROW))
        return values.T[:, 0:1]

    def hot_rows(index, row, group):
        values = jnp.concatenate([column(index, row + r) for r in range(group)], axis=0)
        places = lax.broadcasted_iota(jnp.int32, (group * ROW, vocab), 1).astype(F32)
        return values, jnp.where(values == places, 1.0, 0.0)

    def get(ref, row, group, cols=slice(None)):
        block = ref[pl.ds(row, group), :, cols]
        return block.reshape(group * ROW, block.shape[2])

    def put(ref, row, group, value, cols=slice(None)):
        ref[pl.ds(row, group), :, cols] = value.reshape(group, ROW, value.shape[1])

    def forward_copy(m, row, group):
        return pltpu.make_async_remote_copy(
            src_ref=outb.at[pl.ds(row, group)],
            dst_ref=instream.at[pl.ds(row, group)],
            send_sem=fsend.at[m],
            recv_sem=frecv.at[m],
            device_id={"pipe": up},
            device_id_type=MESH,
        )

    def backward_copy(m, row, group):
        return pltpu.make_async_remote_copy(
            src_ref=gs.at[pl.ds(row, group)],
            dst_ref=gin.at[pl.ds(row, group)],
            send_sem=bsend.at[m],
            recv_sem=brecv.at[m],
            device_id={"pipe": down},
            device_id_type=MESH,
        )

    def save(index, src, dst, m, row, group):
        return pltpu.make_async_copy(src, dst.at[pl.ds(row, group)], osem.at[index, m])

    def saves_forward(m, row, group):
        rows = pl.ds(row, group)
        return [
            save(0, normed.at[rows], normed_o, m, row, group),
            save(1, mixed.at[rows], mixed_o, m, row, group),
            save(2, normed2.at[rows], normed2_o, m, row, group),
            save(3, active.at[rows], active_o, m, row, group),
        ]

    def ring(m, group):
        return pl.ds(pl.multiple_of(lax.rem(m, 2) * GROUP, GROUP), group)

    def saves_backward(m, row, group):
        rows = ring(m, group)
        return [
            save(4, s_gres.at[rows], gres_o, m, row, group),
            save(5, s_ghid.at[rows], ghid_o, m, row, group),
            save(6, s_gbr.at[rows], gbr_o, m, row, group),
            save(7, s_gproj.at[rows], gproj_o, m, row, group),
        ]

    def save_xl(m, row, group):
        return save(8, s_xl.at[ring(m, group)], xl_o, m, row, group)

    def row_of(m):
        return sum(jnp.where(m > i, size, 0) for i, size in enumerate(sizes))

    def by_size(m, run):
        for group in sorted(set(sizes)):
            held = [i for i, size in enumerate(sizes) if size == group]

            @pl.when(functools.reduce(jnp.logical_or, [m == i for i in held]))
            def _():
                run(group)

    def free_slot(m, copies):
        @pl.when(m >= 2)
        def _():
            def run(group):
                made = copies(m - 2, row_of(m - 2), group)
                for copy in made if isinstance(made, list) else [made]:
                    copy.wait()

            by_size(m - 2, run)

    lane_low = lax.broadcasted_iota(jnp.int32, (ROW, ROW), 1) < ROW // 2

    def forward(m, group):
        row = row_of(m)
        tokens = group * ROW

        @pl.when(is_first)
        def _():
            hot = hot_rows(0, row, group)[1].astype(BF16)
            put(instream, row, group, dot(hot, embed[...]).astype(BF16))

        @pl.when(jnp.logical_not(is_first))
        def _():
            forward_copy(m, row, group).wait_recv()

        normal, _ = normalise(get(instream, row, group).astype(F32))
        low = (normal * gains[0:1, :] + shifts[0:1, :]).astype(BF16)
        put(normed, row, group, low)
        queries = dot(low, qkv_w[:, 0:width]) + qv_b[0:1, :]
        put(proj, row, group, (queries * (ROW // 2) ** -0.5).astype(BF16), slice(0, width))
        keys = dot(low, qkv_w[:, width : 2 * width])
        put(proj, row, group, keys.astype(BF16), slice(width, 2 * width))
        values = dot(low, qkv_w[:, 2 * width : 3 * width]) + qv_b[1:2, :]
        put(proj, row, group, values.astype(BF16), slice(2 * width, 3 * width))
        masks, scores = [], []
        for r in range(group):
            kinds = lax.broadcasted_iota(jnp.int32, (16, ROW), 0).astype(F32)
            member = jnp.where(ids[1, pl.ds(row + r, 1), :] == kinds, 1.0, 0.0).astype(BF16)
            mask = jnp.where(dot_tn(member, member) * frames[...] > 0.5, 0.0, MASKED)
            masks.append(jnp.concatenate([mask, mask], axis=1))
            for p in range(pairs):
                q = stack_pair(proj[row + r, :, p * ROW : (p + 1) * ROW], lane_low)
                k = proj[row + r, :, width + p * ROW : width + (p + 1) * ROW]
                scores.append(dot_nt(k, q))

        def mix(unit):
            r, p = unit // pairs, unit % pairs
            v = proj[row + r, :, 2 * width + p * ROW : 2 * width + (p + 1) * ROW]
            both = dot_tn(probs[row + r, p], v)
            mixed[row + r, :, p * ROW : (p + 1) * ROW] = join_pair(both, lane_low).astype(BF16)

        for unit in range(group * pairs):
            masked = scores[unit] + masks[unit // pairs]
            expo = jnp.exp(masked - jnp.max(masked, axis=0, keepdims=True))
            total = jnp.sum(expo, axis=0, keepdims=True)
            probs[row + unit // pairs, unit % pairs] = (expo * (1.0 / total)).astype(BF16)
            if unit:
                mix(unit - 1)
        mix(group * pairs - 1)
        mid = get(instream, row, group).astype(F32)
        mid = mid + (dot(get(mixed, row, group), out_w[...]) + out_b[0:1, :])
        put(middle, row, group, mid)
        normal2, _ = normalise(mid)
        low2 = (normal2 * gains[1:2, :] + shifts[1:2, :]).astype(BF16)
        put(normed2, row, group, low2)
        parts = hidden_n // chunk

        def spread(c):
            return dot(low2, in_w[:, c * chunk : (c + 1) * chunk])

        total, ahead = None, spread(0)
        for c in range(parts):
            cols = slice(c * chunk, (c + 1) * chunk)
            hid = ahead + in_b[0:1, cols]
            if c + 1 < parts:
                ahead = spread(c + 1)
            square = hid * hid
            tan = jnp.tanh(hid * (GELU_A + (GELU_A * GELU_B) * square))
            half = 0.5 + 0.5 * tan
            act = (hid * half).astype(BF16)
            put(active, row, group, act, cols)
            rise = (1.0 - tan * tan) * (0.5 * GELU_A + (1.5 * GELU_A * GELU_B) * square)
            put(slope, row, group, (half + hid * rise).astype(BF16), cols)
            term = dot(act, down_w[cols, :])
            total = term if total is None else total + term
        for copy in saves_forward(m, row, group):
            copy.start()
        lo[0:tokens, :] = get(middle, row, group) + (total + out_b[1:2, :])

        @pl.when(jnp.logical_not(is_last))
        def _():
            put(outb, row, group, lo[0:tokens, :].astype(BF16))
            forward_copy(m, row, group).start()

    def head(m, group):
        row = row_of(m)
        tokens = group * ROW
        normal, scale = normalise(lo[0:tokens, :])
        final = (normal * fin_gain[...] + fin_bias[...]).astype(BF16)
        put(outb, row, group, final)
        save(9, outb.at[pl.ds(row, group)], xr_o, m, row, group).start()
        logits = dot_nt(final, head_w[...])
        top = jnp.max(logits, axis=-1, keepdims=True)
        expo = jnp.exp(logits - top)
        total = jnp.sum(expo, axis=-1, keepdims=True)
        target, hot = hot_rows(2, row, group)
        grad_logits = jnp.where(target >= 0.0, expo * (1.0 / total) - hot, 0.0).astype(BF16)
        free_slot(m, save_xl)
        s_xl[ring(m, group)] = grad_logits.reshape(group, ROW, vocab)
        save_xl(m, row, group).start()
        grad_final = dot(grad_logits, head_w[...])
        vec[V_FINAL_GAIN : V_FINAL_GAIN + 1, :] += column_sum(grad_final * normal)
        vec[V_FINAL_BIAS : V_FINAL_BIAS + 1, :] += column_sum(grad_final)
        go[0:tokens, :] = norm_backward(grad_final, normal, scale, fin_gain[...])

    def backward(m, group):
        row = row_of(m)
        tokens = group * ROW
        slot = ring(m, group)
        base = lax.rem(m, 2) * GROUP
        free_slot(m, saves_backward)

        @pl.when(jnp.logical_not(is_last))
        def _():
            backward_copy(m, row, group).wait_recv()
            go[0:tokens, :] = get(gin, row, group).astype(F32)

        gres = go[0:tokens, :].astype(BF16)
        s_gres[slot] = gres.reshape(group, ROW, width)
        parts = hidden_n // chunk

        def spread(c):
            return dot_nt(gres, down_w[c * chunk : (c + 1) * chunk, :])

        total, ahead = None, spread(0)
        for c in range(parts):
            cols = slice(c * chunk, (c + 1) * chunk)
            gact = ahead
            if c + 1 < parts:
                ahead = spread(c + 1)
            ghid = (gact * get(slope, row, group, cols).astype(F32)).astype(BF16)
            s_ghid[slot, :, cols] = ghid.reshape(group, ROW, chunk)
            term = dot_nt(ghid, in_w[:, cols])
            total = term if total is None else total + term
        normal2, scale2 = normalise(get(middle, row, group))
        vec[V_GAIN2 : V_GAIN2 + 1, :] += column_sum(total * normal2)
        vec[V_SHIFT2 : V_SHIFT2 + 1, :] += column_sum(total)
        gmid[0:tokens, :] = go[0:tokens, :] + norm_backward(total, normal2, scale2, gains[1:2, :])
        gbr = gmid[0:tokens, :].astype(BF16)
        s_gbr[slot] = gbr.reshape(group, ROW, width)
        gmix = dot_nt(gbr, out_w[...]).astype(BF16)
        grads = []
        for r in range(group):
            lines = slice(r * ROW, (r + 1) * ROW)
            for p in range(pairs):
                gm = stack_pair(gmix[lines, p * ROW : (p + 1) * ROW], lane_low)
                vlanes = slice(2 * width + p * ROW, 2 * width + (p + 1) * ROW)
                grads.append(dot_nt(proj[row + r, :, vlanes], gm))
                s_gproj[base + r, :, vlanes] = dot(probs[row + r, p], gm).astype(BF16)

        def pull(unit, gsc):
            r, p = unit // pairs, unit % pairs
            lanes = slice(p * ROW, (p + 1) * ROW)
            klanes = slice(width + p * ROW, width + (p + 1) * ROW)
            q = stack_pair(proj[row + r, :, lanes], lane_low)
            s_gproj[base + r, :, klanes] = dot(gsc, q).astype(BF16)
            gq = join_pair(dot_tn(gsc, proj[row + r, :, klanes]), lane_low) * (ROW // 2) ** -0.5
            s_gproj[base + r, :, lanes] = gq.astype(BF16)

        waiting = None
        for unit in range(group * pairs):
            weights = probs[row + unit // pairs, unit % pairs].astype(F32)
            inner = jnp.sum(weights * grads[unit], axis=0, keepdims=True)
            gsc = (weights * (grads[unit] - inner)).astype(BF16)
            if waiting is not None:
                pull(unit - 1, waiting)
            waiting = gsc
        pull(group * pairs - 1, waiting)
        for copy in saves_backward(m, row, group):
            copy.start()
        gproj = s_gproj[slot].reshape(tokens, 3 * width)
        gnormed = dot_nt(gproj, qkv_w[...])
        normal, scale = normalise(get(instream, row, group).astype(F32))
        vec[V_GAIN1 : V_GAIN1 + 1, :] += column_sum(gnormed * normal)
        vec[V_SHIFT1 : V_SHIFT1 + 1, :] += column_sum(gnormed)
        gstream = gmid[0:tokens, :] + norm_backward(gnormed, normal, scale, gains[0:1, :])
        put(gs, row, group, gstream.astype(BF16))

        @pl.when(is_first)
        def _():
            save(9, gs.at[pl.ds(row, group)], xr_o, m, row, group).start()

        @pl.when(jnp.logical_not(is_first))
        def _():
            backward_copy(m, row, group).start()

    def tick(t, carry):
        m_forward = t - stage
        m_backward = t - (2 * (stages - 1) - stage)

        @pl.when((m_forward >= 0) & (m_forward < micros))
        def _():
            by_size(m_forward, lambda group: forward(m_forward, group))

        @pl.when((m_backward >= 0) & (m_backward < micros))
        def _():
            @pl.when(is_last)
            def _():
                by_size(m_backward, lambda group: head(m_backward, group))

            by_size(m_backward, lambda group: backward(m_backward, group))

        return carry

    lax.fori_loop(0, micros + 2 * (stages - 1), tick, 0)

    for m, group in enumerate(sizes):
        row = sum(sizes[:m])
        for copy in saves_forward(m, row, group):
            copy.wait()

        @pl.when(jnp.logical_not(is_last))
        def _():
            forward_copy(m, row, group).wait_send()

        @pl.when(jnp.logical_not(is_first))
        def _():
            backward_copy(m, row, group).wait_send()

        @pl.when(is_first)
        def _():
            save(9, gs.at[pl.ds(row, group)], xr_o, m, row, group).wait()

        @pl.when(is_last)
        def _():
            save(9, outb.at[pl.ds(row, group)], xr_o, m, row, group).wait()

        if m >= micros - 2:
            for copy in saves_backward(m, row, group):
                copy.wait()

            @pl.when(is_last)
            def _():
                save_xl(m, row, group).wait()


def group_sizes(rows):
    if rows % 2 == 0 and rows > 2:
        return [1] + [2] * (rows // 2 - 1) + [1]
    return [1] * rows


def run_pipeline(stages, token_ids, segment_ids, target_ids, params):
    embed, in_w, head_w = params[0], params[5], params[12]
    width = embed.shape[1]
    vocab = head_w.shape[0]
    hid = in_w.shape[1]
    rows = token_ids.shape[0]
    sizes = group_sizes(rows)
    micros = len(sizes)
    pairs = width // ROW
    vmem = pl.BlockSpec(memory_space=pltpu.VMEM)
    hbm = pl.BlockSpec(memory_space=pl.ANY)

    def kept(columns):
        return jax.ShapeDtypeStruct((rows, ROW, columns), BF16)

    def scratch(lead, columns, kind=BF16):
        return pltpu.VMEM((lead, ROW, columns), kind)

    out_shape = [
        kept(width),
        kept(width),
        kept(width),
        kept(hid),
        kept(width),
        kept(hid),
        kept(width),
        kept(3 * width),
        kept(vocab),
        kept(width),
        jax.ShapeDtypeStruct((VEC_ROWS, width), F32),
    ]
    return pl.pallas_call(
        functools.partial(pipeline_kernel, stages, sizes),
        out_shape=out_shape,
        in_specs=[vmem] * 16,
        out_specs=[hbm] * 10 + [vmem],
        scratch_shapes=[
            scratch(rows, width),
            scratch(rows, width),
            scratch(rows, width),
            scratch(rows, width),
            scratch(rows, width),
            scratch(rows, 3 * width),
            pltpu.VMEM((rows, pairs, ROW, 2 * ROW), BF16),
            scratch(rows, width),
            scratch(rows, width, F32),
            scratch(rows, width),
            scratch(rows, hid),
            scratch(rows, hid),
            pltpu.VMEM((GROUP * ROW, width), F32),
            pltpu.VMEM((GROUP * ROW, width), F32),
            pltpu.VMEM((GROUP * ROW, width), F32),
            scratch(2 * GROUP, width),
            scratch(2 * GROUP, hid),
            scratch(2 * GROUP, width),
            scratch(2 * GROUP, 3 * width),
            scratch(2 * GROUP, vocab),
            pltpu.VMEM((3, 16, ROW), F32),
            pltpu.VMEM((ROW, ROW), F32),
            pltpu.SemaphoreType.DMA((micros,)),
            pltpu.SemaphoreType.DMA((micros,)),
            pltpu.SemaphoreType.DMA((micros,)),
            pltpu.SemaphoreType.DMA((micros,)),
            pltpu.SemaphoreType.DMA((10, micros)),
        ],
        compiler_params=pltpu.CompilerParams(
            collective_id=0, has_side_effects=True, vmem_limit_bytes=62 * 1024 * 1024
        ),
        name="pipeline",
    )(token_ids, segment_ids, target_ids, *params)


def line_dims(devices):
    dims, stride = [], 1
    if devices == 8:
        return [(2, 1), (4, 2)]
    while devices > 1:
        size = 4 if devices % 4 == 0 else 2
        dims.append((size, stride))
        stride *= size
        devices //= size
    return dims


def chunk_plan(width, hid, vocab, stages, devices):
    slim, deep = width // devices, hid // devices
    plan = [("out", 0, (slim, width), True)]
    for c in range(4):
        plan.append(("down", c, (deep, width // 4), c == 2))
    for c in range(2):
        plan.append(("extra", c, (stages, vocab // (stages * devices), width // 2), False))
    for c in range(hid // width):
        plan.append(("in", c, (slim, width), c == 0))
    for c in range(3):
        plan.append(("qkv", c, (slim, width), False))
    return plan


def gradient_kernel(stages, devices, plan, *refs):
    dims = line_dims(devices)
    refs = list(refs)

    def take(amount):
        head, refs[:] = refs[:amount], refs[amount:]
        return head

    inputs = take(10)
    vec_in, token_ids = take(2)
    qkv_out, out_out, in_out, down_out, embed_out, head_out, vec_out = take(7)
    local = take(10)
    in_sem = take(1)[0]
    turned_left, turned_xl = take(2)
    mats = dict(
        zip(
            ("normed", "mixed", "normed2", "active", "gres", "ghid", "gbr", "gproj", "xl", "xr"),
            local,
        )
    )
    names = list(mats)
    stage = lax.axis_index("pipe")
    place = lax.axis_index("dp")
    is_extra = (stage == 0) | (stage == stages - 1)
    width = mats["normed"].shape[1]
    where = [lax.rem(place // stride, size) for size, stride in dims]

    barrier = pltpu.get_barrier_semaphore()

    def greet(offset, carry):
        peer = lax.rem(place + offset, devices)
        pl.semaphore_signal(barrier, inc=1, device_id={"dp": peer}, device_id_type=MESH)
        return carry

    def greet_stage(offset, carry):
        peer = lax.rem(stage + offset, stages)
        pl.semaphore_signal(barrier, inc=1, device_id={"pipe": peer}, device_id_type=MESH)
        return carry

    lax.fori_loop(1, devices, greet, 0)
    lax.fori_loop(1, stages, greet_stage, 0)

    def load(name):
        i = names.index(name)
        return pltpu.make_async_copy(inputs[i], mats[name], in_sem.at[i])

    groups = [("mixed", "gbr"), ("gres", "active"), ("xr", "xl"), ("normed2", "ghid"), ("normed", "gproj")]

    def fetch(at):
        if at >= len(groups):
            return
        if groups[at] == ("xr", "xl"):
            @pl.when(is_extra)
            def _():
                load("xr").start()

            @pl.when(stage == stages - 1)
            def _():
                load("xl").start()

            at += 1
        for name in groups[at]:
            load(name).start()

    fetch(0)
    loaded = set()

    def need(*wanted):
        fresh = [name for name in wanted if name not in loaded]
        for name in fresh:
            loaded.add(name)
            load(name).wait()
        if fresh:
            at = [i for i, group in enumerate(groups) if group[0] == fresh[0]][0]
            fetch(at + 1)

    def identity(size):
        here = lax.broadcasted_iota(jnp.int32, (size, size), 0)
        there = lax.broadcasted_iota(jnp.int32, (size, size), 1)
        return jnp.where(here == there, 1.0, 0.0).astype(BF16)

    def turn(name):
        unit = identity(256)
        for q in range(width // 256):
            part = dot_nt(unit, mats[name][:, q * 256 : (q + 1) * 256])
            turned_left[q * 256 : (q + 1) * 256, :] = part.astype(BF16)

    bits = devices.bit_length() - 1
    vec_send, vec_recv = take(2)
    vec_sems = take(2)

    def vec_copy(k):
        peer = jnp.bitwise_xor(place, 1 << k)
        return pltpu.make_async_remote_copy(
            src_ref=vec_send.at[k],
            dst_ref=vec_recv.at[k],
            send_sem=vec_sems[0].at[k],
            recv_sem=vec_sems[1].at[k],
            device_id={"dp": peer},
            device_id_type=MESH,
        )

    def vec_step(k):
        def run():
            if k == 0:
                vec_send[0] = vec_in[...]
                ones = jnp.ones((16, mats["gres"].shape[0]), BF16)
                for name, start, row in (
                    ("gproj", 0, V_QUERY),
                    ("gproj", 2 * width, V_VALUE),
                    ("gbr", 0, V_BRANCH),
                    ("gres", 0, V_RESULT),
                ):
                    part = dot(ones, mats[name][:, start : start + width])
                    vec_send[0, row : row + 1, :] = part[0:1, :]
                for q in range(mats["ghid"].shape[1] // width):
                    part = dot(ones, mats["ghid"][:, q * width : (q + 1) * width])
                    vec_send[0, V_HIDDEN + q : V_HIDDEN + q + 1, :] = part[0:1, :]
            else:
                vec_copy(k - 1).wait_recv()
                vec_send[k] = vec_send[k - 1] + vec_recv[k - 1]
            if k < bits:
                vec_copy(k).start()

        return run

    final_send, final_recv = take(2)
    final_sems = take(2)

    def final_copy(offset):
        peer = lax.rem(stages - 1 + offset, stages)
        return pltpu.make_async_remote_copy(
            src_ref=final_send,
            dst_ref=final_recv,
            send_sem=final_sems[0].at[offset],
            recv_sem=final_sems[1].at[0],
            device_id={"pipe": peer},
            device_id_type=MESH,
        )

    def vec_last():
        vec_step(bits)()
        vec_out[...] = vec_send[bits]

        @pl.when(stage == stages - 1)
        def _():
            final_send[...] = vec_send[bits, 8:16, :]
            for offset in range(1, stages):
                final_copy(offset).start()

    def vec_finish():
        @pl.when(stage != stages - 1)
        def _():
            final_copy(1).wait_recv()
            vec_out[V_FINAL_GAIN : V_FINAL_BIAS + 1, :] = final_recv[
                V_FINAL_GAIN - 8 : V_FINAL_BIAS - 7, :
            ]

    def vec_drain():
        for k in range(bits):
            vec_copy(k).wait_send()

        @pl.when(stage == stages - 1)
        def _():
            for offset in range(1, stages):
                final_copy(offset).wait_send()

    extra_sum, extra_send_sem, extra_recv_sem = take(3)

    def extra_copy(source, offset, target):
        peer = lax.rem(source + offset, stages)
        return pltpu.make_async_remote_copy(
            src_ref=extra_sum.at[peer],
            dst_ref=target,
            send_sem=extra_send_sem.at[offset],
            recv_sem=extra_recv_sem.at[0 if source == 0 else 1],
            device_id={"pipe": peer},
            device_id_type=MESH,
        )

    def chunk_steps(kind, c, block, turned):
        order = list(range(len(dims)))
        if turned:
            order.reverse()
        full = take(1)[0]

        def compute():
            if kind == "down":
                need("gres", "active")
                if c == 0:
                    turn("gres")
                half, deep = width // 4, 256
                per = deep // block[0]
                unit = identity(deep)

                def body(i, carry):
                    lanes = pl.ds(pl.multiple_of(i * deep, deep), deep)
                    part = dot(turned_left[c * half : (c + 1) * half, :], mats["active"][:, lanes])
                    part = dot_nt(unit, part.astype(BF16)).astype(BF16)
                    put_blocks(full, i, per, part.reshape((per,) + block))
                    return carry

                lax.fori_loop(0, mats["active"].shape[1] // deep, body, 0)
            elif kind == "extra":
                vocab = turned_xl.shape[0]
                if c == 0:
                    load("xr").wait()

                @pl.when((stage == 0) & (c == 0))
                def _():
                    rows_n, seq = token_ids.shape
                    places = lax.broadcasted_iota(jnp.int32, (vocab, ROW), 0)
                    gap = jnp.full((1, ROW - seq), -1, jnp.int32)
                    for r in range(rows_n):
                        row = jnp.concatenate([token_ids[r : r + 1, :], gap], axis=1)
                        hot = jnp.where(places == row, 1.0, 0.0)
                        turned_xl[:, r * ROW : (r + 1) * ROW] = hot.astype(BF16)

                @pl.when((stage == stages - 1) & (c == 0))
                def _():
                    load("xl").wait()
                    unit = identity(256)
                    for q in range(vocab // 256):
                        part = dot_nt(unit, mats["xl"][:, q * 256 : (q + 1) * 256])
                        turned_xl[q * 256 : (q + 1) * 256, :] = part.astype(BF16)

                rows = vocab // stages
                for p in range(stages):
                    part = dot(
                        turned_xl[p * rows : (p + 1) * rows, :],
                        mats["xr"][:, c * (width // 2) : (c + 1) * (width // 2)],
                    )
                    part = part.astype(BF16).reshape((devices,) + block[1:])
                    for d in range(devices):
                        full[split(d) + (p,)] = part[d]
            else:
                left, right = {
                    "in": ("normed2", "ghid"),
                    "out": ("mixed", "gbr"),
                    "qkv": ("normed", "gproj"),
                }[kind]
                need(left, right)
                if c == 0:
                    turn(left)
                cols = slice(c * width, (c + 1) * width)
                per = 256 // block[0]

                def body(i, carry):
                    lines = pl.ds(pl.multiple_of(i * 256, 256), 256)
                    part = dot(turned_left[lines, :], mats[right][:, cols]).astype(BF16)
                    put_blocks(full, i, per, part.reshape((per,) + block))
                    return carry

                lax.fori_loop(0, width // 256, body, 0)

        def split(d):
            return tuple((d // stride) % size for size, stride in reversed(dims))

        def put_blocks(ref, i, per, values):
            for q in range(per):
                d = i * per + q
                index = tuple(lax.rem(d // stride, size) for size, stride in reversed(dims))
                ref[index] = values[q]

        steps = [[compute]]
        for at, phase in enumerate(order):
            size = dims[phase][0]
            buffers = take(3)
            done = order[:at]
            last = at == len(order) - 1
            steps[-1].append(functools.partial(line_step, phase, size, 1, full, buffers, done))
            for t in range(2, size):
                steps.append([functools.partial(line_step, phase, size, t, full, buffers, done)])
            drains.append((kind, functools.partial(line_drain, phase, size, full, buffers, done)))
            steps.append([functools.partial(line_final, kind, c, phase, size, full, buffers, done, last)])
        if kind == "extra":
            steps = [[gated([part]) for part in step] for step in steps]
        return steps

    def gated(step):
        def run():
            @pl.when(is_extra)
            def _():
                for part in step:
                    part()

        return run

    def block_of(full, phase, j, done):
        spot = [slice(None)] * len(dims)
        for other in done:
            spot[len(dims) - 1 - other] = where[other]
        spot[len(dims) - 1 - phase] = j
        return full.at[tuple(spot)]

    def line_copy(phase, size, t, side, full, buffers, done):
        recv, ssem, rsem = buffers
        i = where[phase]
        stride = dims[phase][1]
        if side == 0:
            j, peer = size - t + i, place + jnp.where(i < size - 1, stride, 0)
        else:
            j, peer = t - size + i, place - jnp.where(i > 0, stride, 0)
        return pltpu.make_async_remote_copy(
            src_ref=block_of(full, phase, jnp.clip(j, 0, size - 1), done),
            dst_ref=recv.at[0 if size == 2 else side, t - 1],
            send_sem=ssem.at[side, t - 1],
            recv_sem=rsem.at[side, t - 1],
            device_id={"dp": peer},
            device_id_type=MESH,
        )

    def sends(i, size, t, side):
        return (i <= t - 1) if side == 0 else (i >= size - t)

    def line_step(phase, size, t, full, buffers, done):
        i = where[phase]
        for side in range(2):
            at_end = (i == 0) if side == 0 else (i == size - 1)
            j = size - t + i if side == 0 else t - size + i
            j = jnp.clip(j, 0, size - 1)

            @pl.when(sends(i, size, t, side))
            def _():
                if t > 1:
                    @pl.when(jnp.logical_not(at_end))
                    def _():
                        line_copy(phase, size, t - 1, side, full, buffers, done).wait_recv()
                        own = block_of(full, phase, j, done)
                        got = buffers[0][0 if size == 2 else side, t - 2]
                        own[...] = (own[...].astype(F32) + got.astype(F32)).astype(BF16)

                line_copy(phase, size, t, side, full, buffers, done).start()

    def line_final(kind, c, phase, size, full, buffers, done, last):
        i = where[phase]
        own = block_of(full, phase, i, done)
        total = own
        if last:
            slots = {
                "qkv": lambda: qkv_out.at[:, c * width : (c + 1) * width],
                "in": lambda: in_out.at[:, c * width : (c + 1) * width],
                "out": lambda: out_out,
                "down": lambda: down_out.at[:, c * (width // 4) : (c + 1) * (width // 4)],
                "extra": lambda: extra_sum.at[:, :, c * (width // 2) : (c + 1) * (width // 2)],
            }
            total = slots[kind]()
        lower, upper = i > 0, i < size - 1

        def arrived(side):
            line_copy(phase, size, size - 1, side, full, buffers, done).wait_recv()
            return buffers[0][0 if size == 2 else side, size - 2].astype(F32)

        @pl.when(lower & upper)
        def _():
            total[...] = (own[...].astype(F32) + arrived(0) + arrived(1)).astype(total.dtype)

        @pl.when(lower & jnp.logical_not(upper))
        def _():
            total[...] = (own[...].astype(F32) + arrived(0)).astype(total.dtype)

        @pl.when(jnp.logical_not(lower))
        def _():
            total[...] = (own[...].astype(F32) + arrived(1)).astype(total.dtype)

        if last and kind == "extra" and c == 1:
            for source_stage, out in ((0, embed_out), (stages - 1, head_out)):
                @pl.when(stage == source_stage)
                def _():
                    for offset in range(1, stages):
                        extra_copy(source_stage, offset, extra_recv[0 if source_stage == 0 else 1]).start()
                    out[...] = extra_sum[source_stage]

    def line_drain(phase, size, full, buffers, done):
        i = where[phase]
        for side in range(2):
            for t in range(1, size):
                @pl.when(sends(i, size, t, side))
                def _():
                    line_copy(phase, size, t, side, full, buffers, done).wait_send()

    extra_recv = take(2)
    drains = []
    chains = [chunk_steps(*item) for item in plan]
    depth = len(chains[0])
    vec_chain = [vec_step(k) for k in range(bits)] + [vec_last]
    for r in range(len(chains) + depth - 1):
        for d in [0] + list(range(depth - 1, 0, -1)):
            if 0 <= r - d < len(chains):
                for n, part in enumerate(chains[r - d][d]):
                    part()
                    if r == d == n == 0:
                        pl.semaphore_wait(barrier, devices - 1 + stages - 1)
        if 0 <= r - (len(chains) - 3) < len(vec_chain):
            vec_chain[r - (len(chains) - 3)]()
    vec_finish()
    for source_stage, out in ((0, embed_out), (stages - 1, head_out)):
        @pl.when(stage != source_stage)
        def _():
            got = extra_recv[0 if source_stage == 0 else 1]
            extra_copy(source_stage, 1, got).wait_recv()
            out[...] = got[...]

        @pl.when(stage == source_stage)
        def _():
            for offset in range(1, stages):
                extra_copy(source_stage, offset, extra_recv[0]).wait_send()

    vec_drain()
    for kind, drain in drains:
        if kind == "extra":
            gated([drain])()
        else:
            drain()


def run_gradients(stages, devices, saved, vec, token_ids):
    dims = line_dims(devices)
    rows, tokens, width = saved[0].shape
    hid, vocab = saved[3].shape[2], saved[8].shape[2]
    plan = chunk_plan(width, hid, vocab, stages, devices)
    saved = [member.reshape(rows * tokens, member.shape[2]) for member in saved]
    vmem = pl.BlockSpec(memory_space=pltpu.VMEM)
    hbm = pl.BlockSpec(memory_space=pl.ANY)
    bits = devices.bit_length() - 1
    share = vocab // (stages * devices)
    scratch = [pltpu.VMEM(member.shape, BF16) for member in saved]
    scratch += [pltpu.SemaphoreType.DMA((len(saved),))]
    scratch += [pltpu.VMEM((width, rows * tokens), BF16), pltpu.VMEM((vocab, rows * tokens), BF16)]
    scratch += [
        pltpu.VMEM((bits + 1,) + vec.shape, F32),
        pltpu.VMEM((bits,) + vec.shape, F32),
        pltpu.SemaphoreType.DMA((bits,)),
        pltpu.SemaphoreType.DMA((bits,)),
        pltpu.VMEM((8, width), F32),
        pltpu.VMEM((8, width), F32),
        pltpu.SemaphoreType.DMA((stages,)),
        pltpu.SemaphoreType.DMA((1,)),
        pltpu.VMEM((stages, share, width), F32),
        pltpu.SemaphoreType.DMA((stages,)),
        pltpu.SemaphoreType.DMA((2,)),
        pltpu.VMEM((share, width), F32),
        pltpu.VMEM((share, width), F32),
    ]
    sizes = [size for size, _ in reversed(dims)]
    for _, _, block, turned in plan:
        scratch.append(pltpu.VMEM(tuple(sizes) + block, BF16))
        remain = list(reversed(dims))
        for size, stride in dims[::-1] if turned else dims:
            remain.remove((size, stride))
            piece = tuple(other for other, _ in remain) + block
            scratch.append(pltpu.VMEM((1 if size == 2 else 2, size - 1) + piece, BF16))
            scratch += [pltpu.SemaphoreType.DMA((2, size - 1))] * 2
    return pl.pallas_call(
        functools.partial(gradient_kernel, stages, devices, plan),
        out_shape=[
            jax.ShapeDtypeStruct((width // devices, 3 * width), F32),
            jax.ShapeDtypeStruct((width // devices, width), F32),
            jax.ShapeDtypeStruct((width // devices, hid), F32),
            jax.ShapeDtypeStruct((hid // devices, width), F32),
            jax.ShapeDtypeStruct((share, width), F32),
            jax.ShapeDtypeStruct((share, width), F32),
            jax.ShapeDtypeStruct(vec.shape, F32),
        ],
        in_specs=[hbm] * len(saved) + [vmem] * 2,
        out_specs=[vmem] * 7,
        scratch_shapes=scratch,
        compiler_params=pltpu.CompilerParams(
            collective_id=1, has_side_effects=True, vmem_limit_bytes=62 * 1024 * 1024
        ),
        name="gradients",
    )(*saved, vec, token_ids)


def finish_kernel(devices, embed_g, qkv_g, out_g, in_g, down_g, head_g, vec, *outs):
    place = lax.axis_index("dp")
    width = vec.shape[1]
    (embed_o, qkv_o, qv_o, out_o, outb_o, in_o, inb_o, down_o, gain_o, shift_o, fg_o, fb_o, head_o) = outs
    embed_o[...] = embed_g[...]
    head_o[...] = head_g[...]
    for source, target in ((qkv_g, qkv_o), (out_g, out_o), (in_g, in_o), (down_g, down_o)):
        target[0] = source[...]
    lanes = width // devices
    turned = pltpu.roll(vec[0:8, :], lax.rem(width - place * lanes, width), 1)
    for row, out in ((V_QUERY, qv_o), (V_BRANCH, outb_o), (V_GAIN1, gain_o), (V_SHIFT1, shift_o)):
        out[0] = turned[row : row + 2, 0:lanes]
    share = inb_o.shape[1]
    first = place * share
    row = vec[pl.ds(V_HIDDEN + first // width, 1), :]
    wide = jnp.broadcast_to(row, (8, width))
    inb_o[...] = pltpu.roll(wide, lax.rem(width - lax.rem(first, width), width), 1)[0:1, 0:share]
    fg_o[...] = vec[V_FINAL_GAIN : V_FINAL_GAIN + 1, :]
    fb_o[...] = vec[V_FINAL_BIAS : V_FINAL_BIAS + 1, :]


def run_finish(devices, embed_g, qkv_g, out_g, in_g, down_g, head_g, vec):
    vmem = pl.BlockSpec(memory_space=pltpu.VMEM)
    width = vec.shape[1]
    lanes = width // devices

    def shape(*sizes):
        return jax.ShapeDtypeStruct(sizes, F32)

    pair = shape(1, 2, lanes)
    return pl.pallas_call(
        functools.partial(finish_kernel, devices),
        out_shape=[
            shape(*embed_g.shape),
            shape(1, *qkv_g.shape),
            pair,
            shape(1, *out_g.shape),
            pair,
            shape(1, *in_g.shape),
            shape(1, in_g.shape[1] // devices),
            shape(1, *down_g.shape),
            pair,
            pair,
            shape(1, width),
            shape(1, width),
            shape(*head_g.shape),
        ],
        in_specs=[vmem] * 7,
        out_specs=[vmem] * 13,
        name="finish",
    )(embed_g, qkv_g, out_g, in_g, down_g, head_g, vec)


def on_device(
    token_ids,
    segment_ids,
    target_ids,
    embed_table,
    qkv_weight,
    qv_bias,
    out_weight,
    out_biases,
    ff_in,
    ff_in_bias,
    ff_out,
    norm_gains,
    norm_biases,
    final_gain,
    final_bias,
    head_weight,
):
    stages = lax.axis_size("pipe")
    devices = lax.axis_size("dp")
    params = (
        embed_table,
        qkv_weight[0],
        qv_bias[0],
        out_weight[0],
        out_biases[0],
        ff_in[0],
        ff_in_bias,
        ff_out[0],
        norm_gains[0],
        norm_biases[0],
        final_gain[None],
        final_bias[None],
        head_weight,
    )
    *saved, vec = run_pipeline(stages, token_ids, segment_ids, target_ids, params)
    qkv_g, out_g, in_g, down_g, embed_g, head_g, sums = run_gradients(stages, devices, saved, vec, token_ids)
    done = list(run_finish(devices, embed_g, qkv_g, out_g, in_g, down_g, head_g, sums))
    done[10], done[11] = done[10][0], done[11][0]
    return tuple(done)


def solution(mesh):
    layer3 = P("pipe", None, None)
    return jax.shard_map(
        on_device,
        mesh=mesh,
        in_specs=(
            P("dp", None),
            P("dp", None),
            P("dp", None),
            P(),
            layer3,
            layer3,
            layer3,
            layer3,
            layer3,
            P("pipe", None),
            layer3,
            layer3,
            layer3,
            P(),
            P(),
            P(),
        ),
        out_specs=(
            P(("pipe", "dp"), None),
            P("pipe", "dp", None),
            P("pipe", None, "dp"),
            P("pipe", "dp", None),
            P("pipe", None, "dp"),
            P("pipe", "dp", None),
            P("pipe", "dp"),
            P("pipe", "dp", None),
            P("pipe", None, "dp"),
            P("pipe", None, "dp"),
            P(),
            P(),
            P(("pipe", "dp"), None),
        ),
        check_vma=False,
    )
```

```python
import functools

import jax
import jax.numpy as jnp
from jax import lax
from jax.experimental import pallas as pl
from jax.experimental.pallas import tpu as pltpu
from jax.sharding import PartitionSpec as P

HEADS = 8
FRAME = 6
ROW = 128
GROUP = 2
MASKED = -1e30
GELU_A = 0.7978845608
GELU_B = 0.044715
MESH = pl.DeviceIdType.MESH
F32 = jnp.float32
BF16 = jnp.bfloat16

VEC_ROWS = 16
V_QUERY, V_VALUE, V_BRANCH, V_RESULT, V_GAIN1, V_GAIN2, V_SHIFT1, V_SHIFT2 = range(8)
V_HIDDEN = 8
V_FINAL_GAIN, V_FINAL_BIAS = 12, 13


def dot(a, b):
    return lax.dot_general(a, b, (((1,), (0,)), ((), ())), preferred_element_type=F32)


def dot_nt(a, b):
    return lax.dot_general(a, b, (((1,), (1,)), ((), ())), preferred_element_type=F32)


def dot_tn(a, b):
    return lax.dot_general(a, b, (((0,), (0,)), ((), ())), preferred_element_type=F32)


def normalise(values):
    centre = jnp.mean(values, axis=0, keepdims=True)
    centered = values - centre
    spread = jnp.mean(centered * centered, axis=0, keepdims=True)
    scale = lax.rsqrt(spread + 1e-05)
    return centered * scale, scale


def norm_backward(grad, normal, scale, gain):
    grad_n = grad * gain
    mean_grad = jnp.mean(grad_n, axis=0, keepdims=True)
    mean_proj = jnp.mean(grad_n * normal, axis=0, keepdims=True)
    return scale * (grad_n - mean_grad - normal * mean_proj)


def identity(size):
    here = lax.broadcasted_iota(jnp.int32, (size, size), 0)
    there = lax.broadcasted_iota(jnp.int32, (size, size), 1)
    return jnp.where(here == there, 1.0, 0.0).astype(BF16)


def column_sum(values):
    return jnp.sum(values, axis=0, keepdims=True)


def two_heads(pair):
    half = pair.shape[0] // 2
    zero = jnp.zeros((half, pair.shape[1]), pair.dtype)
    upper = jnp.concatenate([pair[:half], zero], axis=1)
    lower = jnp.concatenate([zero, pair[half:]], axis=1)
    return jnp.concatenate([upper, lower], axis=0)


def own_heads(both):
    half, lanes = both.shape[0] // 2, both.shape[1] // 2
    return jnp.concatenate([both[:half, :lanes], both[half:, lanes:]], axis=0)


def pipeline_kernel(
    stages,
    micros,
    group,
    token_ids,
    segment_ids,
    target_ids,
    qv_b,
    out_b,
    in_b,
    gains,
    shifts,
    fin_gain,
    fin_bias,
    embed_h,
    head_h,
    qkv_h,
    out_h,
    in_h,
    down_h,
    normed_o,
    mixed_o,
    normed2_o,
    active_o,
    gres_o,
    ghid_o,
    gbr_o,
    gproj_o,
    xl_o,
    xr_o,
    acc,
    side,
    qkv_w,
    out_w,
    in_w,
    down_w,
    side_t,
    qkv_t,
    out_t,
    in_t,
    down_t,
    spread_v,
    instream,
    outb,
    gin,
    gs,
    proj,
    probs,
    middle,
    slope,
    normed,
    mixed,
    normed2,
    active,
    s_gbr,
    s_xl,
    lo,
    go,
    gmid,
    ids,
    frames,
    fsend,
    frecv,
    bsend,
    brecv,
    osem,
    wsem,
):
    stage = lax.axis_index("pipe")
    width, tokens = instream.shape[1], instream.shape[2]
    hidden_n = in_b.shape[1]
    vocab = side.shape[0]
    pairs = width // ROW
    chunk = 512
    is_first = stage == 0
    is_last = stage == stages - 1
    up = jnp.minimum(stage + 1, stages - 1)
    down = jnp.maximum(stage - 1, 0)

    def bring(index, source, target):
        return pltpu.make_async_copy(source, target, wsem.at[index])

    weights = [
        bring(1, qkv_h, qkv_w),
        bring(2, out_h, out_w),
        bring(3, in_h, in_w),
        bring(4, down_h, down_w),
    ]

    @pl.when(is_first)
    def _():
        bring(0, embed_h, side).start()

    for copy in weights:
        copy.start()

    @pl.when(is_last)
    def _():
        bring(0, head_h, side).start()

    barrier = pltpu.get_barrier_semaphore()

    @pl.when(jnp.logical_not(is_first))
    def _():
        pl.semaphore_signal(barrier, inc=1, device_id={"pipe": down}, device_id_type=MESH)

    @pl.when(jnp.logical_not(is_last))
    def _():
        pl.semaphore_signal(barrier, inc=1, device_id={"pipe": up}, device_id_type=MESH)

    acc[...] = jnp.zeros_like(acc)
    rows_n, seq = token_ids.shape
    for index, member in enumerate((token_ids, segment_ids, target_ids)):
        ids[index] = jnp.full(ids.shape[1:], 4.0 if index == 1 else -1.0, F32)
        ids[index, 0:rows_n, 0:seq] = member[...].astype(F32)
    at_query = lax.broadcasted_iota(jnp.int32, (ROW, ROW), 1)
    at_key = lax.broadcasted_iota(jnp.int32, (ROW, ROW), 0)
    frames[...] = jnp.where(at_key < ((at_query * 43) // 256) * FRAME + FRAME, 1.0, 0.0)

    places = {}
    filled = 0
    for name, ref, row in (
        ("gain1", gains, 0),
        ("shift1", shifts, 0),
        ("query", qv_b, 0),
        ("value", qv_b, 1),
        ("branch", out_b, 0),
        ("gain2", gains, 1),
        ("shift2", shifts, 1),
        ("hidden", in_b, 0),
        ("result", out_b, 1),
        ("final_gain", fin_gain, 0),
        ("final_bias", fin_bias, 0),
    ):
        long = ref.shape[1]
        places[name] = filled
        for q in range(long // width):
            line = ref[row : row + 1, q * width : (q + 1) * width]
            spread_v[filled : filled + width, :] = jnp.broadcast_to(line, (ROW, width)).T
            filled += width

    def wide(name, start=0, size=width):
        first = places[name] + start
        return jnp.concatenate([spread_v[first : first + size, :]] * group, axis=1)

    def turn(source, target):
        unit = identity(256)
        for q in range(source.shape[1] // 256):
            part = dot_nt(unit, source[:, q * 256 : (q + 1) * 256])
            target[q * 256 : (q + 1) * 256, :] = part.astype(BF16)

    @pl.when(is_first | is_last)
    def _():
        bring(0, embed_h, side).wait()
        turn(side, side_t)

    for copy, source, target in zip(
        weights, (qkv_w, out_w, in_w, down_w), (qkv_t, out_t, in_t, down_t)
    ):
        copy.wait()
        turn(source, target)

    pl.semaphore_wait(barrier, jnp.where(is_first | is_last, 1, 2))

    def gather_row(index, m):
        return jnp.concatenate([ids[index, pl.ds(m * group + r, 1), :] for r in range(group)], axis=1)

    def hot_columns(index, m):
        values = gather_row(index, m)
        here = lax.broadcasted_iota(jnp.int32, (vocab, tokens), 0).astype(F32)
        return values, jnp.where(values == here, 1.0, 0.0)

    def fold(values):
        total = values[:, 0:ROW]
        for r in range(1, group):
            total = total + values[:, r * ROW : (r + 1) * ROW]
        return total

    def forward_copy(m):
        return pltpu.make_async_remote_copy(
            src_ref=outb.at[m],
            dst_ref=instream.at[m],
            send_sem=fsend.at[m],
            recv_sem=frecv.at[m],
            device_id={"pipe": up},
            device_id_type=MESH,
        )

    def backward_copy(m):
        return pltpu.make_async_remote_copy(
            src_ref=gs.at[m],
            dst_ref=gin.at[m],
            send_sem=bsend.at[m],
            recv_sem=brecv.at[m],
            device_id={"pipe": down},
            device_id_type=MESH,
        )

    def save(index, src, dst, m):
        lanes = pl.ds(pl.multiple_of(m * tokens, ROW), tokens)
        return pltpu.make_async_copy(src, dst.at[:, lanes], osem.at[index, m])

    def saves_forward(m):
        slot = lax.rem(m, 2)
        return [
            save(0, normed.at[slot], normed_o, m),
            save(1, mixed.at[slot], mixed_o, m),
            save(2, normed2.at[slot], normed2_o, m),
            save(3, active.at[slot], active_o, m),
        ]

    def save_gbr(m):
        return save(6, s_gbr.at[lax.rem(m, 2)], gbr_o, m)

    def saves_backward(m):
        return [
            save(4, gin.at[m], gres_o, m),
            save(5, slope.at[m], ghid_o, m),
            save(7, proj.at[m], gproj_o, m),
        ]

    def save_xl(m):
        return save(8, s_xl.at[lax.rem(m, 2)], xl_o, m)

    def free_slot(m, copies):
        @pl.when(m >= 2)
        def _():
            for copy in copies(m - 2):
                copy.wait()

    def forward(m):
        slot = lax.rem(m, 2)
        free_slot(m, saves_forward)

        @pl.when(is_first)
        def _():
            hot = hot_columns(0, m)[1].astype(BF16)
            free_slot(m, lambda k: [save_xl(k)])
            s_xl[slot] = hot
            save_xl(m).start()
            instream[m] = dot(side_t[...], hot).astype(BF16)

        @pl.when(jnp.logical_not(is_first))
        def _():
            forward_copy(m).wait_recv()

        normal, _ = normalise(instream[m].astype(F32))
        low = (normal * wide("gain1") + wide("shift1")).astype(BF16)
        normed[slot] = low
        queries = dot(qkv_t[0:width, :], low) + wide("query")
        proj[m, 0:width, :] = (queries * (ROW // 2) ** -0.5).astype(BF16)
        proj[m, width : 2 * width, :] = dot(qkv_t[width : 2 * width, :], low).astype(BF16)
        values = dot(qkv_t[2 * width : 3 * width, :], low) + wide("value")
        proj[m, 2 * width : 3 * width, :] = values.astype(BF16)
        masks, scores = [], []
        for r in range(group):
            lanes = slice(r * ROW, (r + 1) * ROW)
            kinds = lax.broadcasted_iota(jnp.int32, (16, ROW), 0).astype(F32)
            member = jnp.where(ids[1, pl.ds(m * group + r, 1), :] == kinds, 1.0, 0.0).astype(BF16)
            mask = jnp.where(dot_tn(member, member) * frames[...] > 0.5, 0.0, MASKED)
            masks.append(jnp.concatenate([mask, mask], axis=1))
            for p in range(pairs):
                q = two_heads(proj[m, p * ROW : (p + 1) * ROW, lanes])
                k = proj[m, width + p * ROW : width + (p + 1) * ROW, lanes]
                scores.append(dot_tn(k, q))

        def mix(unit):
            r, p = unit // pairs, unit % pairs
            lanes = slice(r * ROW, (r + 1) * ROW)
            v = proj[m, 2 * width + p * ROW : 2 * width + (p + 1) * ROW, lanes]
            both = own_heads(dot(v, probs[m, unit]))
            mixed[slot, p * ROW : (p + 1) * ROW, lanes] = both.astype(BF16)

        for unit in range(group * pairs):
            masked = scores[unit] + masks[unit // pairs]
            expo = jnp.exp(masked - jnp.max(masked, axis=0, keepdims=True))
            total = jnp.sum(expo, axis=0, keepdims=True)
            probs[m, unit] = (expo * (1.0 / total)).astype(BF16)
            if unit:
                mix(unit - 1)
        mix(group * pairs - 1)
        mid = instream[m].astype(F32) + (dot(out_t[...], mixed[slot]) + wide("branch"))
        middle[m] = mid
        normal2, _ = normalise(mid)
        low2 = (normal2 * wide("gain2") + wide("shift2")).astype(BF16)
        normed2[slot] = low2
        parts = hidden_n // chunk

        def spread(c):
            return dot(in_t[c * chunk : (c + 1) * chunk, :], low2)

        total, ahead = None, spread(0)
        for c in range(parts):
            cols = slice(c * chunk, (c + 1) * chunk)
            hid = ahead + wide("hidden", c * chunk, chunk)
            if c + 1 < parts:
                ahead = spread(c + 1)
            square = hid * hid
            tan = jnp.tanh(hid * (GELU_A + (GELU_A * GELU_B) * square))
            half = 0.5 + 0.5 * tan
            act = (hid * half).astype(BF16)
            active[slot, cols, :] = act
            rise = (1.0 - tan * tan) * (0.5 * GELU_A + (1.5 * GELU_A * GELU_B) * square)
            slope[m, cols, :] = (half + hid * rise).astype(BF16)
            term = dot(down_t[:, cols], act)
            total = term if total is None else total + term
        for copy in saves_forward(m):
            copy.start()
        lo[...] = middle[m] + (total + wide("result"))

        @pl.when(jnp.logical_not(is_last))
        def _():
            outb[m] = lo[...].astype(BF16)
            forward_copy(m).start()

    def head(m):
        normal, scale = normalise(lo[...])
        final = (normal * wide("final_gain") + wide("final_bias")).astype(BF16)
        outb[m] = final
        save(9, outb.at[m], xr_o, m).start()
        logits = dot(side[...], final)
        expo = jnp.exp(logits - jnp.max(logits, axis=0, keepdims=True))
        total = jnp.sum(expo, axis=0, keepdims=True)
        target, hot = hot_columns(2, m)
        grad_logits = jnp.where(target >= 0.0, expo * (1.0 / total) - hot, 0.0).astype(BF16)
        free_slot(m, lambda k: [save_xl(k)])
        s_xl[lax.rem(m, 2)] = grad_logits
        save_xl(m).start()
        grad_final = dot(side_t[...], grad_logits)
        acc[4] += fold(grad_final * normal)
        acc[5] += fold(grad_final)
        go[...] = norm_backward(grad_final, normal, scale, wide("final_gain"))

    def backward(m):
        slot = lax.rem(m, 2)
        free_slot(m, lambda k: [save_gbr(k)])

        @pl.when(is_last)
        def _():
            gin[m] = go[...].astype(BF16)

        @pl.when(jnp.logical_not(is_last))
        def _():
            backward_copy(m).wait_recv()
            go[...] = gin[m].astype(F32)

        gres = gin[m]
        parts = hidden_n // chunk

        def spread(c):
            return dot(down_w[c * chunk : (c + 1) * chunk, :], gres)

        total, ahead = None, spread(0)
        for c in range(parts):
            cols = slice(c * chunk, (c + 1) * chunk)
            gact = ahead
            if c + 1 < parts:
                ahead = spread(c + 1)
            ghid = (gact * slope[m, cols, :].astype(F32)).astype(BF16)
            slope[m, cols, :] = ghid
            term = dot(in_w[:, cols], ghid)
            total = term if total is None else total + term
        normal2, scale2 = normalise(middle[m])
        acc[2] += fold(total * normal2)
        acc[3] += fold(total)
        gmid[...] = go[...] + norm_backward(total, normal2, scale2, wide("gain2"))
        gbr = gmid[...].astype(BF16)
        s_gbr[slot] = gbr
        save_gbr(m).start()
        gmix = dot(out_w[...], gbr).astype(BF16)
        grads, grad_values = [], []
        for r in range(group):
            lanes = slice(r * ROW, (r + 1) * ROW)
            for p in range(pairs):
                gm = two_heads(gmix[p * ROW : (p + 1) * ROW, lanes])
                v = proj[m, 2 * width + p * ROW : 2 * width + (p + 1) * ROW, lanes]
                grads.append(dot_tn(v, gm))
                grad_values.append(dot_nt(gm, probs[m, r * pairs + p]).astype(BF16))

        def pull(unit, gsc):
            r, p = unit // pairs, unit % pairs
            lanes = slice(r * ROW, (r + 1) * ROW)
            lines = slice(p * ROW, (p + 1) * ROW)
            klines = slice(width + p * ROW, width + (p + 1) * ROW)
            q = two_heads(proj[m, lines, lanes])
            gk = dot_nt(q, gsc).astype(BF16)
            gq = own_heads(dot(proj[m, klines, lanes], gsc)) * (ROW // 2) ** -0.5
            proj[m, klines, lanes] = gk
            proj[m, lines, lanes] = gq.astype(BF16)
            vlines = slice(2 * width + p * ROW, 2 * width + (p + 1) * ROW)
            proj[m, vlines, lanes] = grad_values[unit]

        waiting = None
        for unit in range(group * pairs):
            chances = probs[m, unit].astype(F32)
            inner = jnp.sum(chances * grads[unit], axis=0, keepdims=True)
            gsc = (chances * (grads[unit] - inner)).astype(BF16)
            if waiting is not None:
                pull(unit - 1, waiting)
            waiting = gsc
        pull(group * pairs - 1, waiting)
        for copy in saves_backward(m):
            copy.start()
        gnormed = dot(qkv_w[...], proj[m])
        normal, scale = normalise(instream[m].astype(F32))
        acc[0] += fold(gnormed * normal)
        acc[1] += fold(gnormed)
        gstream = gmid[...] + norm_backward(gnormed, normal, scale, wide("gain1"))
        gs[m] = gstream.astype(BF16)

        @pl.when(is_first)
        def _():
            save(9, gs.at[m], xr_o, m).start()

        @pl.when(jnp.logical_not(is_first))
        def _():
            backward_copy(m).start()

    def tick(t, carry):
        m_forward = t - stage
        m_backward = t - (2 * (stages - 1) - stage)

        @pl.when((m_forward >= 0) & (m_forward < micros))
        def _():
            forward(m_forward)

        @pl.when((m_backward >= 0) & (m_backward < micros))
        def _():
            @pl.when(is_last)
            def _():
                head(m_backward)

            backward(m_backward)

        return carry

    lax.fori_loop(0, micros + 2 * (stages - 1), tick, 0)

    for m in range(micros):
        for copy in saves_backward(m):
            copy.wait()

        @pl.when(jnp.logical_not(is_last))
        def _():
            forward_copy(m).wait_send()

        @pl.when(jnp.logical_not(is_first))
        def _():
            backward_copy(m).wait_send()

        @pl.when(is_first)
        def _():
            save(9, gs.at[m], xr_o, m).wait()

        @pl.when(is_last)
        def _():
            save(9, outb.at[m], xr_o, m).wait()

        if m >= micros - 2:
            for copy in saves_forward(m) + [save_gbr(m)]:
                copy.wait()

            @pl.when(is_first | is_last)
            def _():
                save_xl(m).wait()


def run_pipeline(stages, token_ids, segment_ids, target_ids, params):
    embed, qkv_w, qv_b, out_w, out_b, in_w, in_b, down_w, gains, shifts, fg, fb, head_w = params
    width, hid, vocab = embed.shape[1], in_w.shape[1], head_w.shape[0]
    rows = token_ids.shape[0]
    group = GROUP if rows % GROUP == 0 else 1
    micros, tokens = rows // group, group * ROW
    pairs = width // ROW
    vmem = pl.BlockSpec(memory_space=pltpu.VMEM)
    hbm = pl.BlockSpec(memory_space=pl.ANY)

    def kept(features):
        return jax.ShapeDtypeStruct((features, micros * tokens), BF16)

    def scratch(lead, features, kind=BF16):
        return pltpu.VMEM((lead, features, tokens), kind)

    def plain(*shape):
        return pltpu.VMEM(shape, BF16)

    out_shape = [
        kept(width),
        kept(width),
        kept(width),
        kept(hid),
        kept(width),
        kept(hid),
        kept(width),
        kept(3 * width),
        kept(vocab),
        kept(width),
        jax.ShapeDtypeStruct((6, width, ROW), F32),
    ]
    return pl.pallas_call(
        functools.partial(pipeline_kernel, stages, micros, group),
        out_shape=out_shape,
        in_specs=[vmem] * 10 + [hbm] * 6,
        out_specs=[hbm] * 10 + [vmem],
        scratch_shapes=[
            plain(vocab, width),
            plain(width, 3 * width),
            plain(width, width),
            plain(width, hid),
            plain(hid, width),
            plain(width, vocab),
            plain(3 * width, width),
            plain(width, width),
            plain(hid, width),
            plain(width, hid),
            pltpu.VMEM((10 * width + hid, ROW), F32),
            scratch(micros, width),
            scratch(micros, width),
            scratch(micros, width),
            scratch(micros, width),
            scratch(micros, 3 * width),
            pltpu.VMEM((micros, group * pairs, ROW, 2 * ROW), BF16),
            scratch(micros, width, F32),
            scratch(micros, hid),
            scratch(2, width),
            scratch(2, width),
            scratch(2, width),
            scratch(2, hid),
            scratch(2, width),
            scratch(2, vocab),
            pltpu.VMEM((width, tokens), F32),
            pltpu.VMEM((width, tokens), F32),
            pltpu.VMEM((width, tokens), F32),
            pltpu.VMEM((3, 16, ROW), F32),
            pltpu.VMEM((ROW, ROW), F32),
            pltpu.SemaphoreType.DMA((micros,)),
            pltpu.SemaphoreType.DMA((micros,)),
            pltpu.SemaphoreType.DMA((micros,)),
            pltpu.SemaphoreType.DMA((micros,)),
            pltpu.SemaphoreType.DMA((10, micros)),
            pltpu.SemaphoreType.DMA((5,)),
        ],
        compiler_params=pltpu.CompilerParams(
            collective_id=0, has_side_effects=True, vmem_limit_bytes=62 * 1024 * 1024
        ),
        name="pipeline",
    )(
        token_ids,
        segment_ids,
        target_ids,
        qv_b,
        out_b,
        in_b,
        gains,
        shifts,
        fg,
        fb,
        embed,
        head_w,
        qkv_w,
        out_w,
        in_w,
        down_w,
    )


def line_dims(devices):
    dims, stride = [], 1
    if devices == 8:
        return [(2, 1), (4, 2)]
    while devices > 1:
        size = 4 if devices % 4 == 0 else 2
        dims.append((size, stride))
        stride *= size
        devices //= size
    return dims


def chunk_plan(width, hid, vocab, stages, devices):
    slim, deep = width // devices, hid // devices
    plan = [("out", 0, (slim, width), True)]
    for c in range(4):
        plan.append(("down", c, (deep, width // 4), c == 2))
    for c in range(2):
        plan.append(("extra", c, (stages, vocab // (stages * devices), width // 2), False))
    for c in range(hid // width):
        plan.append(("in", c, (slim, width), c == 0))
    for c in range(3):
        plan.append(("qkv", c, (slim, width), False))
    return plan


def gradient_kernel(stages, devices, plan, *refs):
    dims = line_dims(devices)
    refs = list(refs)

    def take(amount):
        head, refs[:] = refs[:amount], refs[amount:]
        return head

    inputs = take(10)
    vec_in = take(1)[0]
    qkv_out, out_out, in_out, down_out, embed_out, head_out, vec_out = take(7)
    local = take(10)
    in_sem = take(1)[0]
    mats = dict(
        zip(
            ("normed", "mixed", "normed2", "active", "gres", "ghid", "gbr", "gproj", "xl", "xr"),
            local,
        )
    )
    names = list(mats)
    stage = lax.axis_index("pipe")
    place = lax.axis_index("dp")
    is_extra = (stage == 0) | (stage == stages - 1)
    width = mats["normed"].shape[0]
    where = [lax.rem(place // stride, size) for size, stride in dims]

    barrier = pltpu.get_barrier_semaphore()

    def greet(offset, carry):
        peer = lax.rem(place + offset, devices)
        pl.semaphore_signal(barrier, inc=1, device_id={"dp": peer}, device_id_type=MESH)
        return carry

    def greet_stage(offset, carry):
        peer = lax.rem(stage + offset, stages)
        pl.semaphore_signal(barrier, inc=1, device_id={"pipe": peer}, device_id_type=MESH)
        return carry

    lax.fori_loop(1, devices, greet, 0)
    lax.fori_loop(1, stages, greet_stage, 0)

    def load(name):
        i = names.index(name)
        return pltpu.make_async_copy(inputs[i], mats[name], in_sem.at[i])

    groups = [("mixed", "gbr"), ("gres", "active"), ("xr", "xl"), ("normed2", "ghid"), ("normed", "gproj")]

    def fetch(at):
        if at >= len(groups):
            return
        if groups[at] == ("xr", "xl"):
            @pl.when(is_extra)
            def _():
                load("xr").start()
                load("xl").start()

            at += 1
        for name in groups[at]:
            load(name).start()

    fetch(0)
    loaded = set()

    def need(*wanted):
        fresh = [name for name in wanted if name not in loaded]
        for name in fresh:
            loaded.add(name)
            load(name).wait()
        if fresh:
            at = [i for i, group in enumerate(groups) if group[0] == fresh[0]][0]
            fetch(at + 1)

    bits = devices.bit_length() - 1
    vec_send, vec_recv = take(2)
    vec_sems = take(2)

    def vec_copy(k):
        peer = jnp.bitwise_xor(place, 1 << k)
        return pltpu.make_async_remote_copy(
            src_ref=vec_send.at[k],
            dst_ref=vec_recv.at[k],
            send_sem=vec_sems[0].at[k],
            recv_sem=vec_sems[1].at[k],
            device_id={"dp": peer},
            device_id_type=MESH,
        )

    def vec_step(k):
        def run():
            if k == 0:
                vec_send[0] = jnp.zeros(vec_send.shape[1:], F32)
                for at, row in enumerate(
                    (V_GAIN1, V_SHIFT1, V_GAIN2, V_SHIFT2, V_FINAL_GAIN, V_FINAL_BIAS)
                ):
                    vec_send[0, row : row + 1, :] = column_sum(vec_in[at].T)
                ones = jnp.ones((16, mats["gres"].shape[1]), BF16)
                for name, start, row in (
                    ("gproj", 0, V_QUERY),
                    ("gproj", 2 * width, V_VALUE),
                    ("gbr", 0, V_BRANCH),
                    ("gres", 0, V_RESULT),
                ):
                    part = dot_nt(ones, mats[name][start : start + width, :])
                    vec_send[0, row : row + 1, :] = part[0:1, :]
                for q in range(mats["ghid"].shape[0] // width):
                    part = dot_nt(ones, mats["ghid"][q * width : (q + 1) * width, :])
                    vec_send[0, V_HIDDEN + q : V_HIDDEN + q + 1, :] = part[0:1, :]
            else:
                vec_copy(k - 1).wait_recv()
                vec_send[k] = vec_send[k - 1] + vec_recv[k - 1]
            if k < bits:
                vec_copy(k).start()

        return run

    final_send, final_recv = take(2)
    final_sems = take(2)

    def final_copy(offset):
        peer = lax.rem(stages - 1 + offset, stages)
        return pltpu.make_async_remote_copy(
            src_ref=final_send,
            dst_ref=final_recv,
            send_sem=final_sems[0].at[offset],
            recv_sem=final_sems[1].at[0],
            device_id={"pipe": peer},
            device_id_type=MESH,
        )

    def vec_last():
        vec_step(bits)()
        vec_out[...] = vec_send[bits]

        @pl.when(stage == stages - 1)
        def _():
            final_send[...] = vec_send[bits, 8:16, :]
            for offset in range(1, stages):
                final_copy(offset).start()

    def vec_finish():
        @pl.when(stage != stages - 1)
        def _():
            final_copy(1).wait_recv()
            vec_out[V_FINAL_GAIN : V_FINAL_BIAS + 1, :] = final_recv[
                V_FINAL_GAIN - 8 : V_FINAL_BIAS - 7, :
            ]

    def vec_drain():
        for k in range(bits):
            vec_copy(k).wait_send()

        @pl.when(stage == stages - 1)
        def _():
            for offset in range(1, stages):
                final_copy(offset).wait_send()

    extra_sum, extra_send_sem, extra_recv_sem = take(3)

    def extra_copy(source, offset, target):
        peer = lax.rem(source + offset, stages)
        return pltpu.make_async_remote_copy(
            src_ref=extra_sum.at[peer],
            dst_ref=target,
            send_sem=extra_send_sem.at[offset],
            recv_sem=extra_recv_sem.at[0 if source == 0 else 1],
            device_id={"pipe": peer},
            device_id_type=MESH,
        )

    def chunk_steps(kind, c, block, turned):
        order = list(range(len(dims)))
        if turned:
            order.reverse()
        full = take(1)[0]

        def compute():
            if kind == "down":
                need("gres", "active")
                share = width // 4
                per = 256 // block[0]

                def body(i, carry):
                    lines = pl.ds(pl.multiple_of(i * 256, 256), 256)
                    part = dot_nt(mats["active"][lines, :], mats["gres"][c * share : (c + 1) * share, :])
                    put_blocks(full, i, per, part.astype(BF16).reshape((per,) + block))
                    return carry

                lax.fori_loop(0, mats["active"].shape[0] // 256, body, 0)
            elif kind == "extra":
                if c == 0:
                    load("xr").wait()
                    load("xl").wait()
                share, rows = width // 2, mats["xl"].shape[0] // stages
                for p in range(stages):
                    part = dot_nt(
                        mats["xl"][p * rows : (p + 1) * rows, :],
                        mats["xr"][c * share : (c + 1) * share, :],
                    )
                    part = part.astype(BF16).reshape((devices,) + block[1:])
                    for d in range(devices):
                        full[split(d) + (p,)] = part[d]
            else:
                left, right = {
                    "in": ("normed2", "ghid"),
                    "out": ("mixed", "gbr"),
                    "qkv": ("normed", "gproj"),
                }[kind]
                need(left, right)
                per = 256 // block[0]

                def body(i, carry):
                    lines = pl.ds(pl.multiple_of(i * 256, 256), 256)
                    part = dot_nt(mats[left][lines, :], mats[right][c * width : (c + 1) * width, :])
                    put_blocks(full, i, per, part.astype(BF16).reshape((per,) + block))
                    return carry

                lax.fori_loop(0, width // 256, body, 0)

        def split(d):
            return tuple((d // stride) % size for size, stride in reversed(dims))

        def put_blocks(ref, i, per, values):
            for q in range(per):
                d = i * per + q
                index = tuple(lax.rem(d // stride, size) for size, stride in reversed(dims))
                ref[index] = values[q]

        steps = [[compute]]
        for at, phase in enumerate(order):
            size = dims[phase][0]
            buffers = take(3)
            done = order[:at]
            last = at == len(order) - 1
            steps[-1].append(functools.partial(line_step, phase, size, 1, full, buffers, done))
            for t in range(2, size):
                steps.append([functools.partial(line_step, phase, size, t, full, buffers, done)])
            drains.append((kind, functools.partial(line_drain, phase, size, full, buffers, done)))
            steps.append([functools.partial(line_final, kind, c, phase, size, full, buffers, done, last)])
        if kind == "extra":
            steps = [[gated([part]) for part in step] for step in steps]
        return steps

    def gated(step):
        def run():
            @pl.when(is_extra)
            def _():
                for part in step:
                    part()

        return run

    def block_of(full, phase, j, done):
        spot = [slice(None)] * len(dims)
        for other in done:
            spot[len(dims) - 1 - other] = where[other]
        spot[len(dims) - 1 - phase] = j
        return full.at[tuple(spot)]

    def line_copy(phase, size, t, side, full, buffers, done):
        recv, ssem, rsem = buffers
        i = where[phase]
        stride = dims[phase][1]
        if side == 0:
            j, peer = size - t + i, place + jnp.where(i < size - 1, stride, 0)
        else:
            j, peer = t - size + i, place - jnp.where(i > 0, stride, 0)
        return pltpu.make_async_remote_copy(
            src_ref=block_of(full, phase, jnp.clip(j, 0, size - 1), done),
            dst_ref=recv.at[0 if size == 2 else side, t - 1],
            send_sem=ssem.at[side, t - 1],
            recv_sem=rsem.at[side, t - 1],
            device_id={"dp": peer},
            device_id_type=MESH,
        )

    def sends(i, size, t, side):
        return (i <= t - 1) if side == 0 else (i >= size - t)

    def line_step(phase, size, t, full, buffers, done):
        i = where[phase]
        for side in range(2):
            at_end = (i == 0) if side == 0 else (i == size - 1)
            j = size - t + i if side == 0 else t - size + i
            j = jnp.clip(j, 0, size - 1)

            @pl.when(sends(i, size, t, side))
            def _():
                if t > 1:
                    @pl.when(jnp.logical_not(at_end))
                    def _():
                        line_copy(phase, size, t - 1, side, full, buffers, done).wait_recv()
                        own = block_of(full, phase, j, done)
                        got = buffers[0][0 if size == 2 else side, t - 2]
                        own[...] = (own[...].astype(F32) + got.astype(F32)).astype(BF16)

                line_copy(phase, size, t, side, full, buffers, done).start()

    def line_final(kind, c, phase, size, full, buffers, done, last):
        i = where[phase]
        own = block_of(full, phase, i, done)
        total = own
        if last:
            slots = {
                "qkv": lambda: qkv_out.at[:, c * width : (c + 1) * width],
                "in": lambda: in_out.at[:, c * width : (c + 1) * width],
                "out": lambda: out_out,
                "down": lambda: down_out.at[:, c * (width // 4) : (c + 1) * (width // 4)],
                "extra": lambda: extra_sum.at[:, :, c * (width // 2) : (c + 1) * (width // 2)],
            }
            total = slots[kind]()
        lower, upper = i > 0, i < size - 1

        def arrived(side):
            line_copy(phase, size, size - 1, side, full, buffers, done).wait_recv()
            return buffers[0][0 if size == 2 else side, size - 2].astype(F32)

        @pl.when(lower & upper)
        def _():
            total[...] = (own[...].astype(F32) + arrived(0) + arrived(1)).astype(total.dtype)

        @pl.when(lower & jnp.logical_not(upper))
        def _():
            total[...] = (own[...].astype(F32) + arrived(0)).astype(total.dtype)

        @pl.when(jnp.logical_not(lower))
        def _():
            total[...] = (own[...].astype(F32) + arrived(1)).astype(total.dtype)

        if last and kind == "extra" and c == 1:
            for source_stage, out in ((0, embed_out), (stages - 1, head_out)):
                @pl.when(stage == source_stage)
                def _():
                    for offset in range(1, stages):
                        extra_copy(source_stage, offset, extra_recv[0 if source_stage == 0 else 1]).start()
                    out[...] = extra_sum[source_stage]

    def line_drain(phase, size, full, buffers, done):
        i = where[phase]
        for side in range(2):
            for t in range(1, size):
                @pl.when(sends(i, size, t, side))
                def _():
                    line_copy(phase, size, t, side, full, buffers, done).wait_send()

    extra_recv = take(2)
    drains = []
    chains = [chunk_steps(*item) for item in plan]
    depth = len(chains[0])
    vec_chain = [vec_step(k) for k in range(bits)] + [vec_last]
    for r in range(len(chains) + depth - 1):
        for d in [0] + list(range(depth - 1, 0, -1)):
            if 0 <= r - d < len(chains):
                for n, part in enumerate(chains[r - d][d]):
                    part()
                    if r == d == n == 0:
                        pl.semaphore_wait(barrier, devices - 1 + stages - 1)
        if 0 <= r - (len(chains) - 3) < len(vec_chain):
            vec_chain[r - (len(chains) - 3)]()
    vec_finish()
    for source_stage, out in ((0, embed_out), (stages - 1, head_out)):
        @pl.when(stage != source_stage)
        def _():
            got = extra_recv[0 if source_stage == 0 else 1]
            extra_copy(source_stage, 1, got).wait_recv()
            out[...] = got[...]

        @pl.when(stage == source_stage)
        def _():
            for offset in range(1, stages):
                extra_copy(source_stage, offset, extra_recv[0]).wait_send()

    vec_drain()
    for kind, drain in drains:
        if kind == "extra":
            gated([drain])()
        else:
            drain()


def run_gradients(stages, devices, saved, sums):
    dims = line_dims(devices)
    width, hid, vocab = saved[0].shape[0], saved[3].shape[0], saved[8].shape[0]
    plan = chunk_plan(width, hid, vocab, stages, devices)
    vmem = pl.BlockSpec(memory_space=pltpu.VMEM)
    hbm = pl.BlockSpec(memory_space=pl.ANY)
    bits = devices.bit_length() - 1
    share = vocab // (stages * devices)
    scratch = [pltpu.VMEM(member.shape, BF16) for member in saved]
    scratch += [pltpu.SemaphoreType.DMA((len(saved),))]
    scratch += [
        pltpu.VMEM((bits + 1, VEC_ROWS, width), F32),
        pltpu.VMEM((bits, VEC_ROWS, width), F32),
        pltpu.SemaphoreType.DMA((bits,)),
        pltpu.SemaphoreType.DMA((bits,)),
        pltpu.VMEM((8, width), F32),
        pltpu.VMEM((8, width), F32),
        pltpu.SemaphoreType.DMA((stages,)),
        pltpu.SemaphoreType.DMA((1,)),
        pltpu.VMEM((stages, share, width), F32),
        pltpu.SemaphoreType.DMA((stages,)),
        pltpu.SemaphoreType.DMA((2,)),
        pltpu.VMEM((share, width), F32),
        pltpu.VMEM((share, width), F32),
    ]
    sizes = [size for size, _ in reversed(dims)]
    for _, _, block, turned in plan:
        scratch.append(pltpu.VMEM(tuple(sizes) + block, BF16))
        remain = list(reversed(dims))
        for size, stride in dims[::-1] if turned else dims:
            remain.remove((size, stride))
            piece = tuple(other for other, _ in remain) + block
            scratch.append(pltpu.VMEM((1 if size == 2 else 2, size - 1) + piece, BF16))
            scratch += [pltpu.SemaphoreType.DMA((2, size - 1))] * 2
    return pl.pallas_call(
        functools.partial(gradient_kernel, stages, devices, plan),
        out_shape=[
            jax.ShapeDtypeStruct((width // devices, 3 * width), F32),
            jax.ShapeDtypeStruct((width // devices, width), F32),
            jax.ShapeDtypeStruct((width // devices, hid), F32),
            jax.ShapeDtypeStruct((hid // devices, width), F32),
            jax.ShapeDtypeStruct((share, width), F32),
            jax.ShapeDtypeStruct((share, width), F32),
            jax.ShapeDtypeStruct((VEC_ROWS, width), F32),
        ],
        in_specs=[hbm] * len(saved) + [vmem],
        out_specs=[vmem] * 7,
        scratch_shapes=scratch,
        compiler_params=pltpu.CompilerParams(
            collective_id=1, has_side_effects=True, vmem_limit_bytes=62 * 1024 * 1024
        ),
        name="gradients",
    )(*saved, sums)


def finish_kernel(devices, embed_g, qkv_g, out_g, in_g, down_g, head_g, vec, *outs):
    place = lax.axis_index("dp")
    width = vec.shape[1]
    (embed_o, qkv_o, qv_o, out_o, outb_o, in_o, inb_o, down_o, gain_o, shift_o, fg_o, fb_o, head_o) = outs
    embed_o[...] = embed_g[...]
    head_o[...] = head_g[...]
    for source, target in ((qkv_g, qkv_o), (out_g, out_o), (in_g, in_o), (down_g, down_o)):
        target[0] = source[...]
    lanes = width // devices
    turned = pltpu.roll(vec[0:8, :], lax.rem(width - place * lanes, width), 1)
    for row, out in ((V_QUERY, qv_o), (V_BRANCH, outb_o), (V_GAIN1, gain_o), (V_SHIFT1, shift_o)):
        out[0] = turned[row : row + 2, 0:lanes]
    share = inb_o.shape[1]
    first = place * share
    row = vec[pl.ds(V_HIDDEN + first // width, 1), :]
    wide = jnp.broadcast_to(row, (8, width))
    inb_o[...] = pltpu.roll(wide, lax.rem(width - lax.rem(first, width), width), 1)[0:1, 0:share]
    fg_o[...] = vec[V_FINAL_GAIN : V_FINAL_GAIN + 1, :]
    fb_o[...] = vec[V_FINAL_BIAS : V_FINAL_BIAS + 1, :]


def run_finish(devices, embed_g, qkv_g, out_g, in_g, down_g, head_g, vec):
    vmem = pl.BlockSpec(memory_space=pltpu.VMEM)
    width = vec.shape[1]
    lanes = width // devices

    def shape(*sizes):
        return jax.ShapeDtypeStruct(sizes, F32)

    pair = shape(1, 2, lanes)
    return pl.pallas_call(
        functools.partial(finish_kernel, devices),
        out_shape=[
            shape(*embed_g.shape),
            shape(1, *qkv_g.shape),
            pair,
            shape(1, *out_g.shape),
            pair,
            shape(1, *in_g.shape),
            shape(1, in_g.shape[1] // devices),
            shape(1, *down_g.shape),
            pair,
            pair,
            shape(1, width),
            shape(1, width),
            shape(*head_g.shape),
        ],
        in_specs=[vmem] * 7,
        out_specs=[vmem] * 13,
        name="finish",
    )(embed_g, qkv_g, out_g, in_g, down_g, head_g, vec)


def on_device(
    token_ids,
    segment_ids,
    target_ids,
    embed_table,
    qkv_weight,
    qv_bias,
    out_weight,
    out_biases,
    ff_in,
    ff_in_bias,
    ff_out,
    norm_gains,
    norm_biases,
    final_gain,
    final_bias,
    head_weight,
):
    stages = lax.axis_size("pipe")
    devices = lax.axis_size("dp")
    params = (
        embed_table,
        qkv_weight[0],
        qv_bias[0],
        out_weight[0],
        out_biases[0],
        ff_in[0],
        ff_in_bias,
        ff_out[0],
        norm_gains[0],
        norm_biases[0],
        final_gain[None],
        final_bias[None],
        head_weight,
    )
    *saved, vec = run_pipeline(stages, token_ids, segment_ids, target_ids, params)
    qkv_g, out_g, in_g, down_g, embed_g, head_g, sums = run_gradients(stages, devices, saved, vec)
    done = list(run_finish(devices, embed_g, qkv_g, out_g, in_g, down_g, head_g, sums))
    done[10], done[11] = done[10][0], done[11][0]
    return tuple(done)


def solution(mesh):
    layer3 = P("pipe", None, None)
    return jax.shard_map(
        on_device,
        mesh=mesh,
        in_specs=(
            P("dp", None),
            P("dp", None),
            P("dp", None),
            P(),
            layer3,
            layer3,
            layer3,
            layer3,
            layer3,
            P("pipe", None),
            layer3,
            layer3,
            layer3,
            P(),
            P(),
            P(),
        ),
        out_specs=(
            P(("pipe", "dp"), None),
            P("pipe", "dp", None),
            P("pipe", None, "dp"),
            P("pipe", "dp", None),
            P("pipe", None, "dp"),
            P("pipe", "dp", None),
            P("pipe", "dp"),
            P("pipe", "dp", None),
            P("pipe", None, "dp"),
            P("pipe", None, "dp"),
            P(),
            P(),
            P(("pipe", "dp"), None),
        ),
        check_vma=False,
    )
```

```python
import functools

import jax
import jax.numpy as jnp
from jax import lax
from jax.experimental import pallas as pl
from jax.experimental.pallas import tpu as pltpu
from jax.sharding import PartitionSpec as P

HEADS = 8
FRAME = 6
ROW = 128
GROUP = 2
MASKED = -1e30
GELU_A = 0.7978845608
GELU_B = 0.044715
MESH = pl.DeviceIdType.MESH
F32 = jnp.float32
BF16 = jnp.bfloat16

VEC_ROWS = 16
V_QUERY, V_VALUE, V_BRANCH, V_RESULT, V_GAIN1, V_GAIN2, V_SHIFT1, V_SHIFT2 = range(8)
V_HIDDEN = 8
V_FINAL_GAIN, V_FINAL_BIAS = 12, 13


def dot(a, b):
    return lax.dot_general(a, b, (((1,), (0,)), ((), ())), preferred_element_type=F32)


def dot_nt(a, b):
    return lax.dot_general(a, b, (((1,), (1,)), ((), ())), preferred_element_type=F32)


def dot_tn(a, b):
    return lax.dot_general(a, b, (((0,), (0,)), ((), ())), preferred_element_type=F32)


def normalise(values):
    centre = jnp.mean(values, axis=-1, keepdims=True)
    centered = values - centre
    spread = jnp.mean(centered * centered, axis=-1, keepdims=True)
    scale = lax.rsqrt(spread + 1e-05)
    return centered * scale, scale


def norm_backward(grad, normal, scale, gain):
    grad_n = grad * gain
    mean_grad = jnp.mean(grad_n, axis=-1, keepdims=True)
    mean_proj = jnp.mean(grad_n * normal, axis=-1, keepdims=True)
    return scale * (grad_n - mean_grad - normal * mean_proj)


def column_sum(values):
    return jnp.sum(values, axis=0, keepdims=True)


def stack_pair(pair, low_lanes):
    zero = jnp.zeros_like(pair)
    return jnp.concatenate(
        [jnp.where(low_lanes, pair, zero), jnp.where(low_lanes, zero, pair)], axis=0
    )


def join_pair(stacked, low_lanes):
    half = stacked.shape[0] // 2
    return jnp.where(low_lanes, stacked[:half], stacked[half:])


def pipeline_kernel(
    stages,
    micros,
    token_ids,
    segment_ids,
    target_ids,
    qv_b,
    out_b,
    in_b,
    gains,
    shifts,
    fin_gain,
    fin_bias,
    embed_h,
    head_h,
    qkv_h,
    out_h,
    in_h,
    down_h,
    normed_o,
    mixed_o,
    normed2_o,
    active_o,
    gres_o,
    ghid_o,
    gbr_o,
    gproj_o,
    xl_o,
    xr_o,
    vec,
    side,
    qkv_w,
    out_w,
    in_w,
    down_w,
    instream,
    outb,
    gin,
    gs,
    xr_l,
    normed,
    proj,
    probs,
    mixed,
    middle,
    normed2,
    active,
    slope,
    lo,
    go,
    gmid,
    s_gres,
    s_ghid,
    s_gbr,
    s_gproj,
    s_xl,
    ids,
    frames,
    fsend,
    frecv,
    bsend,
    brecv,
    osem,
    wsem,
):
    stage = lax.axis_index("pipe")
    tokens, width = instream.shape[1], instream.shape[2]
    hidden_n = in_b.shape[1]
    vocab = side.shape[0]
    pairs = width // ROW
    chunk = 512
    parts = hidden_n // chunk
    units = GROUP * pairs
    is_first = stage == 0
    is_last = stage == stages - 1
    up = jnp.minimum(stage + 1, stages - 1)
    down = jnp.maximum(stage - 1, 0)

    def bring(index, source, target):
        return pltpu.make_async_copy(source, target, wsem.at[index])

    weights = [
        bring(1, qkv_h, qkv_w),
        bring(2, out_h, out_w),
        bring(3, in_h, in_w),
        bring(4, down_h, down_w),
    ]

    @pl.when(is_first)
    def _():
        bring(0, embed_h, side).start()

    for copy in weights:
        copy.start()

    @pl.when(is_last)
    def _():
        bring(0, head_h, side).start()

    barrier = pltpu.get_barrier_semaphore()

    @pl.when(jnp.logical_not(is_first))
    def _():
        pl.semaphore_signal(barrier, inc=1, device_id={"pipe": down}, device_id_type=MESH)

    @pl.when(jnp.logical_not(is_last))
    def _():
        pl.semaphore_signal(barrier, inc=1, device_id={"pipe": up}, device_id_type=MESH)

    vec[...] = jnp.zeros_like(vec)
    rows_n, seq = token_ids.shape
    for index, member in enumerate((token_ids, segment_ids, target_ids)):
        ids[index] = jnp.full(ids.shape[1:], 4.0 if index == 1 else -1.0, F32)
        ids[index, 0:rows_n, 0:seq] = member[...].astype(F32)
    at_query = lax.broadcasted_iota(jnp.int32, (ROW, ROW), 1)
    at_key = lax.broadcasted_iota(jnp.int32, (ROW, ROW), 0)
    frames[...] = jnp.where(at_key < ((at_query * 43) // 256) * FRAME + FRAME, 1.0, 0.0)

    @pl.when(is_first | is_last)
    def _():
        bring(0, embed_h, side).wait()

    pl.semaphore_wait(barrier, jnp.where(is_first | is_last, 1, 2))

    def column(index, row):
        values = jnp.broadcast_to(ids[index, pl.ds(row, 1), :], (8, ROW))
        return values.T[:, 0:1]

    def hot_rows(index, m):
        values = jnp.concatenate([column(index, m * GROUP + r) for r in range(GROUP)], axis=0)
        places = lax.broadcasted_iota(jnp.int32, (tokens, vocab), 1).astype(F32)
        return values, jnp.where(values == places, 1.0, 0.0)

    def hop(source, target, send, recv, peer, m):
        return [
            pltpu.make_async_remote_copy(
                src_ref=source.at[m, pl.ds(r * ROW, ROW)],
                dst_ref=target.at[m, pl.ds(r * ROW, ROW)],
                send_sem=send.at[m, r],
                recv_sem=recv.at[m, r],
                device_id={"pipe": peer},
                device_id_type=MESH,
            )
            for r in range(GROUP)
        ]

    def forward_copies(m):
        return hop(outb, instream, fsend, frecv, up, m)

    def backward_copies(m):
        return hop(gs, gin, bsend, brecv, down, m)

    def save(index, src, dst, m):
        return pltpu.make_async_copy(src, dst.at[m], osem.at[index, m])

    def saves_forward(m):
        return [
            save(0, normed.at[m], normed_o, m),
            save(1, mixed.at[m], mixed_o, m),
            save(2, normed2.at[m], normed2_o, m),
            save(3, active.at[m], active_o, m),
        ]

    def saves_backward(m):
        slot = lax.rem(m, 2)
        return [
            save(4, s_gres.at[slot], gres_o, m),
            save(5, s_ghid.at[slot], ghid_o, m),
            save(6, s_gbr.at[slot], gbr_o, m),
            save(7, s_gproj.at[slot], gproj_o, m),
        ]

    def save_xl(m):
        return save(8, s_xl.at[lax.rem(m, 2)], xl_o, m)

    lane_low = lax.broadcasted_iota(jnp.int32, (ROW, ROW), 1) < ROW // 2

    def forward_begin(m):
        @pl.when(is_first)
        def _():
            hot = hot_rows(0, m)[1].astype(BF16)
            instream[m] = dot(hot, side[...]).astype(BF16)

        @pl.when(jnp.logical_not(is_first))
        def _():
            for copy in forward_copies(m):
                copy.wait_recv()

    def forward_front(m):
        normal, _ = normalise(instream[m].astype(F32))
        low = (normal * gains[0:1, :] + shifts[0:1, :]).astype(BF16)
        normed[m] = low
        queries = dot(low, qkv_w[:, 0:width]) + qv_b[0:1, :]
        yield
        proj[m, :, 0:width] = (queries * (ROW // 2) ** -0.5).astype(BF16)
        proj[m, :, width : 2 * width] = dot(low, qkv_w[:, width : 2 * width]).astype(BF16)
        yield
        proj[m, :, 2 * width : 3 * width] = (
            dot(low, qkv_w[:, 2 * width : 3 * width]) + qv_b[1:2, :]
        ).astype(BF16)
        masks, scores = [], []
        for r in range(GROUP):
            rows = slice(r * ROW, (r + 1) * ROW)
            kinds = lax.broadcasted_iota(jnp.int32, (16, ROW), 0).astype(F32)
            member = jnp.where(ids[1, pl.ds(m * GROUP + r, 1), :] == kinds, 1.0, 0.0).astype(BF16)
            mask = jnp.where(dot_tn(member, member) * frames[...] > 0.5, 0.0, MASKED)
            masks.append(jnp.concatenate([mask, mask], axis=1))
            for p in range(pairs):
                q = stack_pair(proj[m, rows, p * ROW : (p + 1) * ROW], lane_low)
                k = proj[m, rows, width + p * ROW : width + (p + 1) * ROW]
                scores.append(dot_nt(k, q))
            yield

        def mix(unit):
            r, p = unit // pairs, unit % pairs
            rows = slice(r * ROW, (r + 1) * ROW)
            v = proj[m, rows, 2 * width + p * ROW : 2 * width + (p + 1) * ROW]
            both = dot_tn(probs[m, unit], v)
            mixed[m, rows, p * ROW : (p + 1) * ROW] = join_pair(both, lane_low).astype(BF16)

        for unit in range(units):
            masked = scores[unit] + masks[unit // pairs]
            expo = jnp.exp(masked - jnp.max(masked, axis=0, keepdims=True))
            total = jnp.sum(expo, axis=0, keepdims=True)
            probs[m, unit] = (expo * (1.0 / total)).astype(BF16)
            if unit:
                mix(unit - 1)
            yield
        mix(units - 1)

    def forward_back(m):
        mid = instream[m].astype(F32) + (dot(mixed[m], out_w[...]) + out_b[0:1, :])
        middle[m] = mid
        normal2, _ = normalise(mid)
        low2 = (normal2 * gains[1:2, :] + shifts[1:2, :]).astype(BF16)
        normed2[m] = low2
        yield

        def spread(c):
            return dot(low2, in_w[:, c * chunk : (c + 1) * chunk])

        total, ahead = None, spread(0)
        for c in range(parts):
            cols = slice(c * chunk, (c + 1) * chunk)
            hid = ahead + in_b[0:1, cols]
            if c + 1 < parts:
                ahead = spread(c + 1)
            square = hid * hid
            tan = jnp.tanh(hid * (GELU_A + (GELU_A * GELU_B) * square))
            half = 0.5 + 0.5 * tan
            act = (hid * half).astype(BF16)
            active[m, :, cols] = act
            rise = (1.0 - tan * tan) * (0.5 * GELU_A + (1.5 * GELU_A * GELU_B) * square)
            slope[m, :, cols] = (half + hid * rise).astype(BF16)
            term = dot(act, down_w[cols, :])
            total = term if total is None else total + term
            yield
        result = middle[m] + (total + out_b[1:2, :])
        lo[...] = result
        outb[m] = result.astype(BF16)

    def forward_end(m):
        for copy in saves_forward(m):
            copy.start()

        @pl.when(jnp.logical_not(is_last))
        def _():
            for copy in forward_copies(m):
                copy.start()

    def head_begin(m):
        @pl.when(m >= 2)
        def _():
            save_xl(m - 2).wait()

    def head(m):
        normal, scale = normalise(lo[...])
        final = (normal * fin_gain[...] + fin_bias[...]).astype(BF16)
        xr_l[m] = final
        logits = dot_nt(final, side[...])
        yield
        top = jnp.max(logits, axis=-1, keepdims=True)
        expo = jnp.exp(logits - top)
        total = jnp.sum(expo, axis=-1, keepdims=True)
        target, hot = hot_rows(2, m)
        grad_logits = jnp.where(target >= 0.0, expo * (1.0 / total) - hot, 0.0).astype(BF16)
        s_xl[lax.rem(m, 2)] = grad_logits
        yield
        grad_final = dot(grad_logits, side[...])
        vec[V_FINAL_GAIN : V_FINAL_GAIN + 1, :] += column_sum(grad_final * normal)
        vec[V_FINAL_BIAS : V_FINAL_BIAS + 1, :] += column_sum(grad_final)
        go[...] = norm_backward(grad_final, normal, scale, fin_gain[...])
        yield

    def head_end(m):
        save_xl(m).start()
        save(9, xr_l.at[m], xr_o, m).start()

    def backward_begin(m):
        @pl.when(m >= 2)
        def _():
            for copy in saves_backward(m - 2):
                copy.wait()

    def backward_receive(m):
        for copy in backward_copies(m):
            copy.wait_recv()
        go[...] = gin[m].astype(F32)

    def backward(m):
        slot = lax.rem(m, 2)
        gres = go[...].astype(BF16)
        s_gres[slot] = gres

        def spread(c):
            return dot_nt(gres, down_w[c * chunk : (c + 1) * chunk, :])

        total, ahead = None, spread(0)
        for c in range(parts):
            cols = slice(c * chunk, (c + 1) * chunk)
            gact = ahead
            if c + 1 < parts:
                ahead = spread(c + 1)
            ghid = (gact * slope[m, :, cols].astype(F32)).astype(BF16)
            s_ghid[slot, :, cols] = ghid
            term = dot_nt(ghid, in_w[:, cols])
            total = term if total is None else total + term
            yield
        normal2, scale2 = normalise(middle[m])
        vec[V_GAIN2 : V_GAIN2 + 1, :] += column_sum(total * normal2)
        vec[V_SHIFT2 : V_SHIFT2 + 1, :] += column_sum(total)
        gmid[...] = go[...] + norm_backward(total, normal2, scale2, gains[1:2, :])
        gbr = gmid[...].astype(BF16)
        s_gbr[slot] = gbr
        gmix = dot_nt(gbr, out_w[...]).astype(BF16)
        yield
        grads = []
        for r in range(GROUP):
            rows = slice(r * ROW, (r + 1) * ROW)
            for p in range(pairs):
                gm = stack_pair(gmix[rows, p * ROW : (p + 1) * ROW], lane_low)
                vlanes = slice(2 * width + p * ROW, 2 * width + (p + 1) * ROW)
                grads.append(dot_nt(proj[m, rows, vlanes], gm))
                s_gproj[slot, rows, vlanes] = dot(probs[m, r * pairs + p], gm).astype(BF16)
            yield

        def pull(unit, gsc):
            r, p = unit // pairs, unit % pairs
            rows = slice(r * ROW, (r + 1) * ROW)
            lanes = slice(p * ROW, (p + 1) * ROW)
            klanes = slice(width + p * ROW, width + (p + 1) * ROW)
            q = stack_pair(proj[m, rows, lanes], lane_low)
            s_gproj[slot, rows, klanes] = dot(gsc, q).astype(BF16)
            gq = join_pair(dot_tn(gsc, proj[m, rows, klanes]), lane_low) * (ROW // 2) ** -0.5
            s_gproj[slot, rows, lanes] = gq.astype(BF16)

        waiting = None
        for unit in range(units):
            chances = probs[m, unit].astype(F32)
            inner = jnp.sum(chances * grads[unit], axis=0, keepdims=True)
            gsc = (chances * (grads[unit] - inner)).astype(BF16)
            if waiting is not None:
                pull(unit - 1, waiting)
            waiting = gsc
            yield
        pull(units - 1, waiting)
        gnormed = dot_nt(s_gproj[slot], qkv_w[...])
        yield
        normal, scale = normalise(instream[m].astype(F32))
        vec[V_GAIN1 : V_GAIN1 + 1, :] += column_sum(gnormed * normal)
        vec[V_SHIFT1 : V_SHIFT1 + 1, :] += column_sum(gnormed)
        gstream = gmid[...] + norm_backward(gnormed, normal, scale, gains[0:1, :])
        gs[m] = gstream.astype(BF16)

    def backward_end(m):
        @pl.when(is_first)
        def _():
            save(9, gs.at[m], xr_o, m).start()

        @pl.when(jnp.logical_not(is_first))
        def _():
            for copy in backward_copies(m):
                copy.start()

        for copy in saves_backward(m):
            copy.start()

    def run(*chains):
        chains = [chain for chain in chains]
        while chains:
            for chain in list(chains):
                try:
                    next(chain)
                except StopIteration:
                    chains.remove(chain)

    def both(*chains):
        for chain in chains:
            yield from chain

    def tick(t, carry):
        mf = t - stage
        mb = t - (2 * stages - 1 - stage)
        ahead = (mf >= 0) & (mf < micros)
        behind = (mb >= 0) & (mb < micros)

        @pl.when(ahead)
        def _():
            forward_begin(mf)

        @pl.when(behind)
        def _():
            backward_begin(mb)

            @pl.when(is_last)
            def _():
                head_begin(mb)

            @pl.when(jnp.logical_not(is_last))
            def _():
                backward_receive(mb)

        @pl.when(ahead & jnp.logical_not(behind))
        def _():
            @pl.when(mf == 0)
            def _():
                weights[0].wait()

            run(forward_front(mf))

            @pl.when(mf == 0)
            def _():
                for copy in weights[1:]:
                    copy.wait()

            run(forward_back(mf))

        @pl.when(ahead & behind & is_last)
        def _():
            run(both(head(mb), backward(mb)), both(forward_front(mf), forward_back(mf)))

        @pl.when(ahead & behind & jnp.logical_not(is_last))
        def _():
            run(backward(mb), both(forward_front(mf), forward_back(mf)))

        @pl.when(behind & jnp.logical_not(ahead))
        def _():
            @pl.when(is_last)
            def _():
                run(head(mb))

            run(backward(mb))

        @pl.when(behind)
        def _():
            backward_end(mb)

            @pl.when(is_last)
            def _():
                head_end(mb)

        @pl.when(ahead)
        def _():
            forward_end(mf)

        return carry

    lax.fori_loop(0, micros + 2 * stages - 1, tick, 0)

    for m in range(micros):
        for copy in saves_forward(m):
            copy.wait()

        @pl.when(jnp.logical_not(is_last))
        def _():
            for copy in forward_copies(m):
                copy.wait_send()

        @pl.when(jnp.logical_not(is_first))
        def _():
            for copy in backward_copies(m):
                copy.wait_send()

        @pl.when(is_first)
        def _():
            save(9, gs.at[m], xr_o, m).wait()

        @pl.when(is_last)
        def _():
            save(9, xr_l.at[m], xr_o, m).wait()

    for m in range(max(0, micros - 2), micros):
        for copy in saves_backward(m):
            copy.wait()

        @pl.when(is_last)
        def _():
            save_xl(m).wait()


def run_pipeline(stages, token_ids, segment_ids, target_ids, params):
    embed, qkv_w, qv_b, out_w, out_b, in_w, in_b, down_w, gains, shifts, fg, fb, head_w = params
    width, hid, vocab = embed.shape[1], in_w.shape[1], head_w.shape[0]
    tokens = GROUP * ROW
    micros = token_ids.shape[0] // GROUP
    pairs = width // ROW
    vmem = pl.BlockSpec(memory_space=pltpu.VMEM)
    hbm = pl.BlockSpec(memory_space=pl.ANY)

    def kept(columns):
        return jax.ShapeDtypeStruct((micros, tokens, columns), BF16)

    def scratch(lead, columns, kind=BF16):
        return pltpu.VMEM((lead, tokens, columns), kind)

    def plain(*shape):
        return pltpu.VMEM(shape, BF16)

    out_shape = [
        kept(width),
        kept(width),
        kept(width),
        kept(hid),
        kept(width),
        kept(hid),
        kept(width),
        kept(3 * width),
        kept(vocab),
        kept(width),
        jax.ShapeDtypeStruct((VEC_ROWS, width), F32),
    ]
    return pl.pallas_call(
        functools.partial(pipeline_kernel, stages, micros),
        out_shape=out_shape,
        in_specs=[vmem] * 10 + [hbm] * 6,
        out_specs=[hbm] * 10 + [vmem],
        scratch_shapes=[
            plain(vocab, width),
            plain(width, 3 * width),
            plain(width, width),
            plain(width, hid),
            plain(hid, width),
            scratch(micros, width),
            scratch(micros, width),
            scratch(micros, width),
            scratch(micros, width),
            scratch(micros, width),
            scratch(micros, width),
            scratch(micros, 3 * width),
            pltpu.VMEM((micros, GROUP * pairs, ROW, 2 * ROW), BF16),
            scratch(micros, width),
            scratch(micros, width, F32),
            scratch(micros, width),
            scratch(micros, hid),
            scratch(micros, hid),
            pltpu.VMEM((tokens, width), F32),
            pltpu.VMEM((tokens, width), F32),
            pltpu.VMEM((tokens, width), F32),
            scratch(2, width),
            scratch(2, hid),
            scratch(2, width),
            scratch(2, 3 * width),
            scratch(2, vocab),
            pltpu.VMEM((3, 16, ROW), F32),
            pltpu.VMEM((ROW, ROW), F32),
            pltpu.SemaphoreType.DMA((micros, GROUP)),
            pltpu.SemaphoreType.DMA((micros, GROUP)),
            pltpu.SemaphoreType.DMA((micros, GROUP)),
            pltpu.SemaphoreType.DMA((micros, GROUP)),
            pltpu.SemaphoreType.DMA((10, micros)),
            pltpu.SemaphoreType.DMA((5,)),
        ],
        compiler_params=pltpu.CompilerParams(
            collective_id=0, has_side_effects=True, vmem_limit_bytes=62 * 1024 * 1024
        ),
        name="pipeline",
    )(
        token_ids,
        segment_ids,
        target_ids,
        qv_b,
        out_b,
        in_b,
        gains,
        shifts,
        fg,
        fb,
        embed,
        head_w,
        qkv_w,
        out_w,
        in_w,
        down_w,
    )


def line_dims(devices):
    dims, stride = [], 1
    if devices == 8:
        return [(2, 1), (4, 2)]
    while devices > 1:
        size = 4 if devices % 4 == 0 else 2
        dims.append((size, stride))
        stride *= size
        devices //= size
    return dims


def chunk_plan(width, hid, vocab, stages, devices):
    slim, deep = width // devices, hid // devices
    plan = [("out", 0, (slim, width), False)]
    for c in range(4):
        plan.append(("down", c, (deep, width // 4), c in (0, 2)))
    for c in range(2):
        plan.append(("extra", c, (stages, vocab // (stages * devices), width // 2), False))
    for c in range(hid // width):
        plan.append(("in", c, (slim, width), c == 1))
    for c in range(3):
        plan.append(("qkv", c, (slim, width), False))
    return plan


def gradient_kernel(stages, devices, plan, *refs):
    dims = line_dims(devices)
    refs = list(refs)

    def take(amount):
        head, refs[:] = refs[:amount], refs[amount:]
        return head

    inputs = take(10)
    vec_in, token_ids = take(2)
    qkv_out, out_out, in_out, down_out, embed_out, head_out, vec_out = take(7)
    local = take(10)
    in_sem = take(1)[0]
    turned_left, turned_xl = take(2)
    mats = dict(
        zip(
            ("normed", "mixed", "normed2", "active", "gres", "ghid", "gbr", "gproj", "xl", "xr"),
            local,
        )
    )
    names = list(mats)
    stage = lax.axis_index("pipe")
    place = lax.axis_index("dp")
    is_extra = (stage == 0) | (stage == stages - 1)
    width = mats["normed"].shape[1]
    where = [lax.rem(place // stride, size) for size, stride in dims]

    barrier = pltpu.get_barrier_semaphore()

    def greet(offset, carry):
        peer = lax.rem(place + offset, devices)
        pl.semaphore_signal(barrier, inc=1, device_id={"dp": peer}, device_id_type=MESH)
        return carry

    def greet_stage(offset, carry):
        peer = lax.rem(stage + offset, stages)
        pl.semaphore_signal(barrier, inc=1, device_id={"pipe": peer}, device_id_type=MESH)
        return carry

    lax.fori_loop(1, devices, greet, 0)
    lax.fori_loop(1, stages, greet_stage, 0)

    def load(name):
        i = names.index(name)
        return pltpu.make_async_copy(inputs[i], mats[name], in_sem.at[i])

    groups = [("mixed", "gbr"), ("gres", "active"), ("xr", "xl"), ("normed2", "ghid"), ("normed", "gproj")]

    def fetch(at):
        if at >= len(groups):
            return
        if groups[at] == ("xr", "xl"):
            @pl.when(is_extra)
            def _():
                load("xr").start()

            @pl.when(stage == stages - 1)
            def _():
                load("xl").start()

            at += 1
        for name in groups[at]:
            load(name).start()

    fetch(0)
    loaded = set()

    def need(*wanted):
        fresh = [name for name in wanted if name not in loaded]
        for name in fresh:
            loaded.add(name)
            load(name).wait()
        if fresh:
            at = [i for i, group in enumerate(groups) if group[0] == fresh[0]][0]
            fetch(at + 1)

    def identity(size):
        here = lax.broadcasted_iota(jnp.int32, (size, size), 0)
        there = lax.broadcasted_iota(jnp.int32, (size, size), 1)
        return jnp.where(here == there, 1.0, 0.0).astype(BF16)

    held = []

    def turn(name):
        if held[-1:] == [name]:
            return
        held.append(name)
        unit = identity(256)
        for q in range(width // 256):
            part = dot_nt(unit, mats[name][:, q * 256 : (q + 1) * 256])
            turned_left[q * 256 : (q + 1) * 256, :] = part.astype(BF16)

    bits = devices.bit_length() - 1
    vec_send, vec_recv = take(2)
    vec_sems = take(2)

    def vec_copy(k):
        peer = jnp.bitwise_xor(place, 1 << k)
        return pltpu.make_async_remote_copy(
            src_ref=vec_send.at[k],
            dst_ref=vec_recv.at[k],
            send_sem=vec_sems[0].at[k],
            recv_sem=vec_sems[1].at[k],
            device_id={"dp": peer},
            device_id_type=MESH,
        )

    def vec_step(k):
        def run():
            if k == 0:
                vec_send[0] = vec_in[...]
                ones = jnp.ones((16, mats["gres"].shape[0]), BF16)
                for name, start, row in (
                    ("gproj", 0, V_QUERY),
                    ("gproj", 2 * width, V_VALUE),
                    ("gbr", 0, V_BRANCH),
                    ("gres", 0, V_RESULT),
                ):
                    part = dot(ones, mats[name][:, start : start + width])
                    vec_send[0, row : row + 1, :] = part[0:1, :]
                for q in range(mats["ghid"].shape[1] // width):
                    part = dot(ones, mats["ghid"][:, q * width : (q + 1) * width])
                    vec_send[0, V_HIDDEN + q : V_HIDDEN + q + 1, :] = part[0:1, :]
            else:
                vec_copy(k - 1).wait_recv()
                vec_send[k] = vec_send[k - 1] + vec_recv[k - 1]
            if k < bits:
                vec_copy(k).start()

        return run

    final_send, final_recv = take(2)
    final_sems = take(2)

    def final_copy(offset):
        peer = lax.rem(stages - 1 + offset, stages)
        return pltpu.make_async_remote_copy(
            src_ref=final_send,
            dst_ref=final_recv,
            send_sem=final_sems[0].at[offset],
            recv_sem=final_sems[1].at[0],
            device_id={"pipe": peer},
            device_id_type=MESH,
        )

    def vec_last():
        vec_step(bits)()
        vec_out[...] = vec_send[bits]

        @pl.when(stage == stages - 1)
        def _():
            final_send[...] = vec_send[bits, 8:16, :]
            for offset in range(1, stages):
                final_copy(offset).start()

    def vec_finish():
        @pl.when(stage != stages - 1)
        def _():
            final_copy(1).wait_recv()
            vec_out[V_FINAL_GAIN : V_FINAL_BIAS + 1, :] = final_recv[
                V_FINAL_GAIN - 8 : V_FINAL_BIAS - 7, :
            ]

    def vec_drain():
        for k in range(bits):
            vec_copy(k).wait_send()

        @pl.when(stage == stages - 1)
        def _():
            for offset in range(1, stages):
                final_copy(offset).wait_send()

    extra_sum, extra_send_sem, extra_recv_sem = take(3)

    def extra_copy(source, offset, target):
        peer = lax.rem(source + offset, stages)
        return pltpu.make_async_remote_copy(
            src_ref=extra_sum.at[peer],
            dst_ref=target,
            send_sem=extra_send_sem.at[offset],
            recv_sem=extra_recv_sem.at[0 if source == 0 else 1],
            device_id={"pipe": peer},
            device_id_type=MESH,
        )

    def chunk_steps(kind, c, block, turned):
        order = list(range(len(dims)))
        if turned:
            order.reverse()
        full = take(1)[0]

        def compute():
            if kind == "down":
                need("gres", "active")
                turn("gres")
                half, deep = width // 4, 256
                per = deep // block[0]
                unit = identity(deep)

                def body(i, carry):
                    lanes = pl.ds(pl.multiple_of(i * deep, deep), deep)
                    part = dot(turned_left[c * half : (c + 1) * half, :], mats["active"][:, lanes])
                    part = dot_nt(unit, part.astype(BF16)).astype(BF16)
                    put_blocks(full, i, per, part.reshape((per,) + block))
                    return carry

                lax.fori_loop(0, mats["active"].shape[1] // deep, body, 0)
            elif kind == "extra":
                vocab = turned_xl.shape[0]
                if c == 0:
                    load("xr").wait()

                @pl.when((stage == 0) & (c == 0))
                def _():
                    rows_n, seq = token_ids.shape
                    places = lax.broadcasted_iota(jnp.int32, (vocab, ROW), 0)
                    gap = jnp.full((1, ROW - seq), -1, jnp.int32)
                    for r in range(rows_n):
                        row = jnp.concatenate([token_ids[r : r + 1, :], gap], axis=1)
                        hot = jnp.where(places == row, 1.0, 0.0)
                        turned_xl[:, r * ROW : (r + 1) * ROW] = hot.astype(BF16)

                @pl.when((stage == stages - 1) & (c == 0))
                def _():
                    load("xl").wait()
                    unit = identity(256)
                    for q in range(vocab // 256):
                        part = dot_nt(unit, mats["xl"][:, q * 256 : (q + 1) * 256])
                        turned_xl[q * 256 : (q + 1) * 256, :] = part.astype(BF16)

                rows = vocab // stages
                for p in range(stages):
                    part = dot(
                        turned_xl[p * rows : (p + 1) * rows, :],
                        mats["xr"][:, c * (width // 2) : (c + 1) * (width // 2)],
                    )
                    part = part.astype(BF16).reshape((devices,) + block[1:])
                    for d in range(devices):
                        full[split(d) + (p,)] = part[d]
            else:
                left, right = {
                    "in": ("normed2", "ghid"),
                    "out": ("mixed", "gbr"),
                    "qkv": ("normed", "gproj"),
                }[kind]
                need(left, right)
                turn(left)
                cols = slice(c * width, (c + 1) * width)
                per = 256 // block[0]

                def body(i, carry):
                    lines = pl.ds(pl.multiple_of(i * 256, 256), 256)
                    part = dot(turned_left[lines, :], mats[right][:, cols]).astype(BF16)
                    put_blocks(full, i, per, part.reshape((per,) + block))
                    return carry

                lax.fori_loop(0, width // 256, body, 0)

        def split(d):
            return tuple((d // stride) % size for size, stride in reversed(dims))

        def put_blocks(ref, i, per, values):
            for q in range(per):
                d = i * per + q
                index = tuple(lax.rem(d // stride, size) for size, stride in reversed(dims))
                ref[index] = values[q]

        steps = [[compute]]
        for at, phase in enumerate(order):
            size = dims[phase][0]
            buffers = take(3)
            done = order[:at]
            last = at == len(order) - 1
            steps[-1].append(functools.partial(line_step, phase, size, 1, full, buffers, done))
            for t in range(2, size):
                steps.append([functools.partial(line_step, phase, size, t, full, buffers, done)])
            drains.append((kind, functools.partial(line_drain, phase, size, full, buffers, done)))
            steps.append([functools.partial(line_final, kind, c, phase, size, full, buffers, done, last)])
        if kind == "extra":
            steps = [[gated([part]) for part in step] for step in steps]
        return steps

    def gated(step):
        def run():
            @pl.when(is_extra)
            def _():
                for part in step:
                    part()

        return run

    def block_of(full, phase, j, done):
        spot = [slice(None)] * len(dims)
        for other in done:
            spot[len(dims) - 1 - other] = where[other]
        spot[len(dims) - 1 - phase] = j
        return full.at[tuple(spot)]

    def line_copy(phase, size, t, side, full, buffers, done):
        recv, ssem, rsem = buffers
        i = where[phase]
        stride = dims[phase][1]
        if side == 0:
            j, peer = size - t + i, place + jnp.where(i < size - 1, stride, 0)
        else:
            j, peer = t - size + i, place - jnp.where(i > 0, stride, 0)
        return pltpu.make_async_remote_copy(
            src_ref=block_of(full, phase, jnp.clip(j, 0, size - 1), done),
            dst_ref=recv.at[0 if size == 2 else side, t - 1],
            send_sem=ssem.at[side, t - 1],
            recv_sem=rsem.at[side, t - 1],
            device_id={"dp": peer},
            device_id_type=MESH,
        )

    def sends(i, size, t, side):
        return (i <= t - 1) if side == 0 else (i >= size - t)

    def line_step(phase, size, t, full, buffers, done):
        i = where[phase]
        for side in range(2):
            at_end = (i == 0) if side == 0 else (i == size - 1)
            j = size - t + i if side == 0 else t - size + i
            j = jnp.clip(j, 0, size - 1)

            @pl.when(sends(i, size, t, side))
            def _():
                if t > 1:
                    @pl.when(jnp.logical_not(at_end))
                    def _():
                        line_copy(phase, size, t - 1, side, full, buffers, done).wait_recv()
                        own = block_of(full, phase, j, done)
                        got = buffers[0][0 if size == 2 else side, t - 2]
                        own[...] = (own[...].astype(F32) + got.astype(F32)).astype(BF16)

                line_copy(phase, size, t, side, full, buffers, done).start()

    def line_final(kind, c, phase, size, full, buffers, done, last):
        i = where[phase]
        own = block_of(full, phase, i, done)
        total = own
        if last:
            slots = {
                "qkv": lambda: qkv_out.at[:, c * width : (c + 1) * width],
                "in": lambda: in_out.at[:, c * width : (c + 1) * width],
                "out": lambda: out_out,
                "down": lambda: down_out.at[:, c * (width // 4) : (c + 1) * (width // 4)],
                "extra": lambda: extra_sum.at[:, :, c * (width // 2) : (c + 1) * (width // 2)],
            }
            total = slots[kind]()
        lower, upper = i > 0, i < size - 1

        def arrived(side):
            line_copy(phase, size, size - 1, side, full, buffers, done).wait_recv()
            return buffers[0][0 if size == 2 else side, size - 2].astype(F32)

        @pl.when(lower & upper)
        def _():
            total[...] = (own[...].astype(F32) + arrived(0) + arrived(1)).astype(total.dtype)

        @pl.when(lower & jnp.logical_not(upper))
        def _():
            total[...] = (own[...].astype(F32) + arrived(0)).astype(total.dtype)

        @pl.when(jnp.logical_not(lower))
        def _():
            total[...] = (own[...].astype(F32) + arrived(1)).astype(total.dtype)

        if last and kind == "extra" and c == 1:
            for source_stage, out in ((0, embed_out), (stages - 1, head_out)):
                @pl.when(stage == source_stage)
                def _():
                    for offset in range(1, stages):
                        extra_copy(source_stage, offset, extra_recv[0 if source_stage == 0 else 1]).start()
                    out[...] = extra_sum[source_stage]

    def line_drain(phase, size, full, buffers, done):
        i = where[phase]
        for side in range(2):
            for t in range(1, size):
                @pl.when(sends(i, size, t, side))
                def _():
                    line_copy(phase, size, t, side, full, buffers, done).wait_send()

    extra_recv = take(2)
    drains = []
    chains = [chunk_steps(*item) for item in plan]
    depth = len(chains[0])
    vec_chain = [vec_step(k) for k in range(bits)] + [vec_last]
    starts, first, extra_rounds = [], 0, iter((0, 2, 5, 7))
    for item in plan:
        if item[3]:
            starts.append(next(extra_rounds))
        else:
            starts.append(first)
            first += 1
    begun = False
    loaded_at = max(start for start, item in zip(starts, plan) if item[0] == "qkv" and item[1] == 0)
    for r in range(max(starts) + depth):
        for d in [0] + list(range(depth - 1, 0, -1)):
            for start, chain in zip(starts, chains):
                if r - start != d:
                    continue
                for part in chain[d]:
                    part()
                    if not begun:
                        begun = True
                        pl.semaphore_wait(barrier, devices - 1 + stages - 1)
        if 0 <= r - loaded_at < len(vec_chain):
            vec_chain[r - loaded_at]()
    vec_finish()
    for source_stage, out in ((0, embed_out), (stages - 1, head_out)):
        @pl.when(stage != source_stage)
        def _():
            got = extra_recv[0 if source_stage == 0 else 1]
            extra_copy(source_stage, 1, got).wait_recv()
            out[...] = got[...]

        @pl.when(stage == source_stage)
        def _():
            for offset in range(1, stages):
                extra_copy(source_stage, offset, extra_recv[0]).wait_send()

    vec_drain()
    for kind, drain in drains:
        if kind == "extra":
            gated([drain])()
        else:
            drain()


def run_gradients(stages, devices, saved, vec, token_ids):
    dims = line_dims(devices)
    rows, tokens, width = saved[0].shape
    hid, vocab = saved[3].shape[2], saved[8].shape[2]
    plan = chunk_plan(width, hid, vocab, stages, devices)
    saved = [member.reshape(rows * tokens, member.shape[2]) for member in saved]
    vmem = pl.BlockSpec(memory_space=pltpu.VMEM)
    hbm = pl.BlockSpec(memory_space=pl.ANY)
    bits = devices.bit_length() - 1
    share = vocab // (stages * devices)
    scratch = [pltpu.VMEM(member.shape, BF16) for member in saved]
    scratch += [pltpu.SemaphoreType.DMA((len(saved),))]
    scratch += [pltpu.VMEM((width, rows * tokens), BF16), pltpu.VMEM((vocab, rows * tokens), BF16)]
    scratch += [
        pltpu.VMEM((bits + 1,) + vec.shape, F32),
        pltpu.VMEM((bits,) + vec.shape, F32),
        pltpu.SemaphoreType.DMA((bits,)),
        pltpu.SemaphoreType.DMA((bits,)),
        pltpu.VMEM((8, width), F32),
        pltpu.VMEM((8, width), F32),
        pltpu.SemaphoreType.DMA((stages,)),
        pltpu.SemaphoreType.DMA((1,)),
        pltpu.VMEM((stages, share, width), F32),
        pltpu.SemaphoreType.DMA((stages,)),
        pltpu.SemaphoreType.DMA((2,)),
        pltpu.VMEM((share, width), F32),
        pltpu.VMEM((share, width), F32),
    ]
    sizes = [size for size, _ in reversed(dims)]
    for _, _, block, turned in plan:
        scratch.append(pltpu.VMEM(tuple(sizes) + block, BF16))
        remain = list(reversed(dims))
        for size, stride in dims[::-1] if turned else dims:
            remain.remove((size, stride))
            piece = tuple(other for other, _ in remain) + block
            scratch.append(pltpu.VMEM((1 if size == 2 else 2, size - 1) + piece, BF16))
            scratch += [pltpu.SemaphoreType.DMA((2, size - 1))] * 2
    return pl.pallas_call(
        functools.partial(gradient_kernel, stages, devices, plan),
        out_shape=[
            jax.ShapeDtypeStruct((width // devices, 3 * width), F32),
            jax.ShapeDtypeStruct((width // devices, width), F32),
            jax.ShapeDtypeStruct((width // devices, hid), F32),
            jax.ShapeDtypeStruct((hid // devices, width), F32),
            jax.ShapeDtypeStruct((share, width), F32),
            jax.ShapeDtypeStruct((share, width), F32),
            jax.ShapeDtypeStruct(vec.shape, F32),
        ],
        in_specs=[hbm] * len(saved) + [vmem] * 2,
        out_specs=[vmem] * 7,
        scratch_shapes=scratch,
        compiler_params=pltpu.CompilerParams(
            collective_id=1, has_side_effects=True, vmem_limit_bytes=62 * 1024 * 1024
        ),
        name="gradients",
    )(*saved, vec, token_ids)


def finish_kernel(devices, embed_g, qkv_g, out_g, in_g, down_g, head_g, vec, *outs):
    place = lax.axis_index("dp")
    width = vec.shape[1]
    (embed_o, qkv_o, qv_o, out_o, outb_o, in_o, inb_o, down_o, gain_o, shift_o, fg_o, fb_o, head_o) = outs
    embed_o[...] = embed_g[...]
    head_o[...] = head_g[...]
    for source, target in ((qkv_g, qkv_o), (out_g, out_o), (in_g, in_o), (down_g, down_o)):
        target[0] = source[...]
    lanes = width // devices
    turned = pltpu.roll(vec[0:8, :], lax.rem(width - place * lanes, width), 1)
    for row, out in ((V_QUERY, qv_o), (V_BRANCH, outb_o), (V_GAIN1, gain_o), (V_SHIFT1, shift_o)):
        out[0] = turned[row : row + 2, 0:lanes]
    share = inb_o.shape[1]
    first = place * share
    row = vec[pl.ds(V_HIDDEN + first // width, 1), :]
    wide = jnp.broadcast_to(row, (8, width))
    inb_o[...] = pltpu.roll(wide, lax.rem(width - lax.rem(first, width), width), 1)[0:1, 0:share]
    fg_o[...] = vec[V_FINAL_GAIN : V_FINAL_GAIN + 1, :]
    fb_o[...] = vec[V_FINAL_BIAS : V_FINAL_BIAS + 1, :]


def run_finish(devices, embed_g, qkv_g, out_g, in_g, down_g, head_g, vec):
    vmem = pl.BlockSpec(memory_space=pltpu.VMEM)
    width = vec.shape[1]
    lanes = width // devices

    def shape(*sizes):
        return jax.ShapeDtypeStruct(sizes, F32)

    pair = shape(1, 2, lanes)
    return pl.pallas_call(
        functools.partial(finish_kernel, devices),
        out_shape=[
            shape(*embed_g.shape),
            shape(1, *qkv_g.shape),
            pair,
            shape(1, *out_g.shape),
            pair,
            shape(1, *in_g.shape),
            shape(1, in_g.shape[1] // devices),
            shape(1, *down_g.shape),
            pair,
            pair,
            shape(1, width),
            shape(1, width),
            shape(*head_g.shape),
        ],
        in_specs=[vmem] * 7,
        out_specs=[vmem] * 13,
        name="finish",
    )(embed_g, qkv_g, out_g, in_g, down_g, head_g, vec)


def on_device(
    token_ids,
    segment_ids,
    target_ids,
    embed_table,
    qkv_weight,
    qv_bias,
    out_weight,
    out_biases,
    ff_in,
    ff_in_bias,
    ff_out,
    norm_gains,
    norm_biases,
    final_gain,
    final_bias,
    head_weight,
):
    stages = lax.axis_size("pipe")
    devices = lax.axis_size("dp")
    params = (
        embed_table,
        qkv_weight[0],
        qv_bias[0],
        out_weight[0],
        out_biases[0],
        ff_in[0],
        ff_in_bias,
        ff_out[0],
        norm_gains[0],
        norm_biases[0],
        final_gain[None],
        final_bias[None],
        head_weight,
    )
    *saved, vec = run_pipeline(stages, token_ids, segment_ids, target_ids, params)
    qkv_g, out_g, in_g, down_g, embed_g, head_g, sums = run_gradients(stages, devices, saved, vec, token_ids)
    done = list(run_finish(devices, embed_g, qkv_g, out_g, in_g, down_g, head_g, sums))
    done[10], done[11] = done[10][0], done[11][0]
    return tuple(done)


def solution(mesh):
    layer3 = P("pipe", None, None)
    return jax.shard_map(
        on_device,
        mesh=mesh,
        in_specs=(
            P("dp", None),
            P("dp", None),
            P("dp", None),
            P(),
            layer3,
            layer3,
            layer3,
            layer3,
            layer3,
            P("pipe", None),
            layer3,
            layer3,
            layer3,
            P(),
            P(),
            P(),
        ),
        out_specs=(
            P(("pipe", "dp"), None),
            P("pipe", "dp", None),
            P("pipe", None, "dp"),
            P("pipe", "dp", None),
            P("pipe", None, "dp"),
            P("pipe", "dp", None),
            P("pipe", "dp"),
            P("pipe", "dp", None),
            P("pipe", None, "dp"),
            P("pipe", None, "dp"),
            P(),
            P(),
            P(("pipe", "dp"), None),
        ),
        check_vma=False,
    )
```

```python
import functools

import jax
import jax.numpy as jnp
from jax import lax
from jax.experimental import pallas as pl
from jax.experimental.pallas import tpu as pltpu
from jax.sharding import PartitionSpec as P

HEADS = 8
FRAME = 6
ROW = 128
GROUP = 2
MASKED = -1e30
GELU_A = 0.7978845608
GELU_B = 0.044715
MESH = pl.DeviceIdType.MESH
F32 = jnp.float32
BF16 = jnp.bfloat16

VEC_ROWS = 16
V_QUERY, V_VALUE, V_BRANCH, V_RESULT, V_GAIN1, V_GAIN2, V_SHIFT1, V_SHIFT2 = range(8)
V_HIDDEN = 8
V_FINAL_GAIN, V_FINAL_BIAS = 12, 13


def dot(a, b):
    return lax.dot_general(a, b, (((1,), (0,)), ((), ())), preferred_element_type=F32)


def dot_nt(a, b):
    return lax.dot_general(a, b, (((1,), (1,)), ((), ())), preferred_element_type=F32)


def dot_tn(a, b):
    return lax.dot_general(a, b, (((0,), (0,)), ((), ())), preferred_element_type=F32)


def normalise(values):
    centre = jnp.mean(values, axis=-1, keepdims=True)
    centered = values - centre
    spread = jnp.mean(centered * centered, axis=-1, keepdims=True)
    scale = lax.rsqrt(spread + 1e-05)
    return centered * scale, scale


def norm_backward(grad, normal, scale, gain):
    grad_n = grad * gain
    mean_grad = jnp.mean(grad_n, axis=-1, keepdims=True)
    mean_proj = jnp.mean(grad_n * normal, axis=-1, keepdims=True)
    return scale * (grad_n - mean_grad - normal * mean_proj)


def column_sum(values):
    return jnp.sum(values, axis=0, keepdims=True)


def stack_pair(pair, low_lanes):
    zero = jnp.zeros_like(pair)
    return jnp.concatenate(
        [jnp.where(low_lanes, pair, zero), jnp.where(low_lanes, zero, pair)], axis=0
    )


def join_pair(stacked, low_lanes):
    half = stacked.shape[0] // 2
    return jnp.where(low_lanes, stacked[:half], stacked[half:])


def pipeline_kernel(
    stages,
    micros,
    token_ids,
    segment_ids,
    target_ids,
    qv_b,
    out_b,
    in_b,
    gains,
    shifts,
    fin_gain,
    fin_bias,
    embed_h,
    head_h,
    qkv_h,
    out_h,
    in_h,
    down_h,
    normed_o,
    mixed_o,
    normed2_o,
    active_o,
    gres_o,
    ghid_o,
    gbr_o,
    gproj_o,
    xl_o,
    xr_o,
    vec,
    side,
    qkv_w,
    out_w,
    in_w,
    down_w,
    instream,
    outb,
    gin,
    gs,
    xr_l,
    normed,
    proj,
    probs,
    mixed,
    middle,
    normed2,
    active,
    slope,
    lo,
    go,
    gmid,
    s_gres,
    s_ghid,
    s_gbr,
    s_gproj,
    s_xl,
    s_gmix,
    s_gsc,
    ids,
    frames,
    fsend,
    frecv,
    bsend,
    brecv,
    osem,
    wsem,
):
    stage = lax.axis_index("pipe")
    tokens, width = instream.shape[1], instream.shape[2]
    hidden_n = in_b.shape[1]
    vocab = side.shape[0]
    pairs = width // ROW
    chunk = 512
    parts = hidden_n // chunk
    units = GROUP * pairs
    is_first = stage == 0
    is_last = stage == stages - 1
    up = jnp.minimum(stage + 1, stages - 1)
    down = jnp.maximum(stage - 1, 0)

    def bring(index, source, target):
        return pltpu.make_async_copy(source, target, wsem.at[index])

    weights = [
        bring(1, qkv_h, qkv_w),
        bring(2, out_h, out_w),
        bring(3, in_h, in_w),
        bring(4, down_h, down_w),
    ]

    @pl.when(is_first)
    def _():
        bring(0, embed_h, side).start()

    for copy in weights:
        copy.start()

    @pl.when(is_last)
    def _():
        bring(0, head_h, side).start()

    barrier = pltpu.get_barrier_semaphore()

    @pl.when(jnp.logical_not(is_first))
    def _():
        pl.semaphore_signal(barrier, inc=1, device_id={"pipe": down}, device_id_type=MESH)

    @pl.when(jnp.logical_not(is_last))
    def _():
        pl.semaphore_signal(barrier, inc=1, device_id={"pipe": up}, device_id_type=MESH)

    vec[...] = jnp.zeros_like(vec)
    rows_n, seq = token_ids.shape
    for index, member in enumerate((token_ids, segment_ids, target_ids)):
        ids[index] = jnp.full(ids.shape[1:], 4.0 if index == 1 else -1.0, F32)
        ids[index, 0:rows_n, 0:seq] = member[...].astype(F32)
    at_query = lax.broadcasted_iota(jnp.int32, (ROW, ROW), 1)
    at_key = lax.broadcasted_iota(jnp.int32, (ROW, ROW), 0)
    frames[...] = jnp.where(at_key < ((at_query * 43) // 256) * FRAME + FRAME, 1.0, 0.0)

    @pl.when(is_first | is_last)
    def _():
        bring(0, embed_h, side).wait()

    pl.semaphore_wait(barrier, jnp.where(is_first | is_last, 1, 2))

    def column(index, row):
        values = jnp.broadcast_to(ids[index, pl.ds(row, 1), :], (8, ROW))
        return values.T[:, 0:1]

    def hot_rows(index, m):
        values = jnp.concatenate([column(index, m * GROUP + r) for r in range(GROUP)], axis=0)
        places = lax.broadcasted_iota(jnp.int32, (tokens, vocab), 1).astype(F32)
        return values, jnp.where(values == places, 1.0, 0.0)

    def hop(source, target, send, recv, peer, m):
        return [
            pltpu.make_async_remote_copy(
                src_ref=source.at[m, pl.ds(r * ROW, ROW)],
                dst_ref=target.at[m, pl.ds(r * ROW, ROW)],
                send_sem=send.at[m, r],
                recv_sem=recv.at[m, r],
                device_id={"pipe": peer},
                device_id_type=MESH,
            )
            for r in range(GROUP)
        ]

    def forward_copies(m):
        return hop(outb, instream, fsend, frecv, up, m)

    def backward_copies(m):
        return hop(gs, gin, bsend, brecv, down, m)

    def save(index, src, dst, m):
        return pltpu.make_async_copy(src, dst.at[m], osem.at[index, m])

    def saves_forward(m):
        return [
            save(0, normed.at[m], normed_o, m),
            save(1, mixed.at[m], mixed_o, m),
            save(2, normed2.at[m], normed2_o, m),
            save(3, active.at[m], active_o, m),
        ]

    def saves_backward(m):
        slot = lax.rem(m, 2)
        return [
            save(4, s_gres.at[slot], gres_o, m),
            save(5, s_ghid.at[slot], ghid_o, m),
            save(6, s_gbr.at[slot], gbr_o, m),
            save(7, s_gproj.at[slot], gproj_o, m),
        ]

    def save_xl(m):
        return save(8, s_xl.at[lax.rem(m, 2)], xl_o, m)

    lane_low = lax.broadcasted_iota(jnp.int32, (ROW, ROW), 1) < ROW // 2

    def forward_begin(m):
        @pl.when(is_first)
        def _():
            hot = hot_rows(0, m)[1].astype(BF16)
            instream[m] = dot(hot, side[...]).astype(BF16)

        @pl.when(jnp.logical_not(is_first))
        def _():
            for copy in forward_copies(m):
                copy.wait_recv()

    def blocks(size):
        return [slice(i * size, (i + 1) * size) for i in range(tokens // size)]

    def partial(values):
        total = values[0:8]
        for i in range(1, values.shape[0] // 8):
            total = total + values[8 * i : 8 * i + 8]
        return total

    def forward_front(m):
        for rows in blocks(32):
            normal, _ = normalise(instream[m, rows, :].astype(F32))
            normed[m, rows, :] = (normal * gains[0:1, :] + shifts[0:1, :]).astype(BF16)
        low = normed[m]
        queries = dot(low, qkv_w[:, 0:width])
        keys = dot(low, qkv_w[:, width : 2 * width])
        values = dot(low, qkv_w[:, 2 * width : 3 * width])
        for rows in blocks(32):
            query = (queries[rows] + qv_b[0:1, :]) * (ROW // 2) ** -0.5
            proj[m, rows, 0:width] = query.astype(BF16)
            proj[m, rows, width : 2 * width] = keys[rows].astype(BF16)
            proj[m, rows, 2 * width : 3 * width] = (values[rows] + qv_b[1:2, :]).astype(BF16)
        masks, scores = [], []
        for r in range(GROUP):
            rows = slice(r * ROW, (r + 1) * ROW)
            kinds = lax.broadcasted_iota(jnp.int32, (16, ROW), 0).astype(F32)
            member = jnp.where(ids[1, pl.ds(m * GROUP + r, 1), :] == kinds, 1.0, 0.0).astype(BF16)
            masks.append(jnp.where(dot_tn(member, member) * frames[...] > 0.5, 0.0, MASKED))
            for p in range(pairs):
                q = stack_pair(proj[m, rows, p * ROW : (p + 1) * ROW], lane_low)
                k = proj[m, rows, width + p * ROW : width + (p + 1) * ROW]
                scores.append(dot_nt(k, q))

        def mix(unit):
            r, p = unit // pairs, unit % pairs
            rows = slice(r * ROW, (r + 1) * ROW)
            v = proj[m, rows, 2 * width + p * ROW : 2 * width + (p + 1) * ROW]
            both = dot_tn(probs[m, unit], v)
            mixed[m, rows, p * ROW : (p + 1) * ROW] = join_pair(both, lane_low).astype(BF16)

        for unit in range(units):
            for side_lanes in (slice(0, ROW), slice(ROW, 2 * ROW)):
                masked = scores[unit][:, side_lanes] + masks[unit // pairs]
                expo = jnp.exp(masked - jnp.max(masked, axis=0, keepdims=True))
                total = jnp.sum(expo, axis=0, keepdims=True)
                probs[m, unit, :, side_lanes] = (expo * (1.0 / total)).astype(BF16)
            if unit:
                mix(unit - 1)
        mix(units - 1)

    def forward_back(m):
        branch = dot(mixed[m], out_w[...])
        for rows in blocks(32):
            mid = instream[m, rows, :].astype(F32) + (branch[rows] + out_b[0:1, :])
            middle[m, rows, :] = mid
            normal2, _ = normalise(mid)
            normed2[m, rows, :] = (normal2 * gains[1:2, :] + shifts[1:2, :]).astype(BF16)
        low2 = normed2[m]

        def spread(c):
            return dot(low2, in_w[:, c * chunk : (c + 1) * chunk])

        total, ahead = None, spread(0)
        for c in range(parts):
            cols = slice(c * chunk, (c + 1) * chunk)
            now = ahead
            if c + 1 < parts:
                ahead = spread(c + 1)
            for rows in blocks(16):
                hid = now[rows] + in_b[0:1, cols]
                square = hid * hid
                tan = jnp.tanh(hid * (GELU_A + (GELU_A * GELU_B) * square))
                half = 0.5 + 0.5 * tan
                active[m, rows, cols] = (hid * half).astype(BF16)
                rise = (1.0 - tan * tan) * (0.5 * GELU_A + (1.5 * GELU_A * GELU_B) * square)
                slope[m, rows, cols] = (half + hid * rise).astype(BF16)
            term = dot(active[m, :, cols], down_w[cols, :])
            total = term if total is None else total + term
        for rows in blocks(32):
            result = middle[m, rows, :] + (total[rows] + out_b[1:2, :])
            lo[rows, :] = result
            outb[m, rows, :] = result.astype(BF16)

    def forward_end(m):
        for copy in saves_forward(m):
            copy.start()

        @pl.when(jnp.logical_not(is_last))
        def _():
            for copy in forward_copies(m):
                copy.start()

    def head_begin(m):
        @pl.when(m >= 2)
        def _():
            save_xl(m - 2).wait()

    def head(m):
        slot = lax.rem(m, 2)
        for rows in blocks(32):
            normal, _ = normalise(lo[rows, :])
            xr_l[m, rows, :] = (normal * fin_gain[...] + fin_bias[...]).astype(BF16)
        logits = dot_nt(xr_l[m], side[...])
        targets = jnp.concatenate([column(2, m * GROUP + r) for r in range(GROUP)], axis=0)
        places = lax.broadcasted_iota(jnp.int32, (16, vocab), 1).astype(F32)
        for rows in blocks(16):
            part = logits[rows]
            expo = jnp.exp(part - jnp.max(part, axis=-1, keepdims=True))
            total = jnp.sum(expo, axis=-1, keepdims=True)
            target = targets[rows]
            real = jnp.where(target >= 0.0, 1.0, 0.0)
            hot = jnp.where(target == places, 1.0, 0.0)
            s_xl[slot, rows, :] = (expo * (real / total) - hot).astype(BF16)
        grad_final = dot(s_xl[slot], side[...])
        gain_part, bias_part = None, None
        for rows in blocks(16):
            normal, scale = normalise(lo[rows, :])
            grad = grad_final[rows]
            first, second = partial(grad * normal), partial(grad)
            gain_part = first if gain_part is None else gain_part + first
            bias_part = second if bias_part is None else bias_part + second
            go[rows, :] = norm_backward(grad, normal, scale, fin_gain[...])
        vec[4] += gain_part
        vec[5] += bias_part

    def head_end(m):
        save_xl(m).start()
        save(9, xr_l.at[m], xr_o, m).start()

    def backward_begin(m):
        @pl.when(m >= 2)
        def _():
            for copy in saves_backward(m - 2):
                copy.wait()

    def backward_receive(m):
        for copy in backward_copies(m):
            copy.wait_recv()
        go[...] = gin[m].astype(F32)

    def backward(m):
        slot = lax.rem(m, 2)
        for rows in blocks(32):
            s_gres[slot, rows, :] = go[rows, :].astype(BF16)
        gres = s_gres[slot]

        def spread(c):
            return dot_nt(gres, down_w[c * chunk : (c + 1) * chunk, :])

        total, ahead = None, spread(0)
        for c in range(parts):
            cols = slice(c * chunk, (c + 1) * chunk)
            now = ahead
            if c + 1 < parts:
                ahead = spread(c + 1)
            for rows in blocks(32):
                ghid = now[rows] * slope[m, rows, cols].astype(F32)
                s_ghid[slot, rows, cols] = ghid.astype(BF16)
            term = dot_nt(s_ghid[slot, :, cols], in_w[:, cols])
            total = term if total is None else total + term
        gain_part, bias_part = None, None
        for rows in blocks(16):
            normal2, scale2 = normalise(middle[m, rows, :])
            grad = total[rows]
            first, second = partial(grad * normal2), partial(grad)
            gain_part = first if gain_part is None else gain_part + first
            bias_part = second if bias_part is None else bias_part + second
            grad = go[rows, :] + norm_backward(grad, normal2, scale2, gains[1:2, :])
            gmid[rows, :] = grad
            s_gbr[slot, rows, :] = grad.astype(BF16)
        vec[2] += gain_part
        vec[3] += bias_part
        gmix = dot_nt(s_gbr[slot], out_w[...])
        for rows in blocks(32):
            s_gmix[rows, :] = gmix[rows].astype(BF16)
        grads = []
        for r in range(GROUP):
            rows = slice(r * ROW, (r + 1) * ROW)
            for p in range(pairs):
                gm = stack_pair(s_gmix[rows, p * ROW : (p + 1) * ROW], lane_low)
                vlanes = slice(2 * width + p * ROW, 2 * width + (p + 1) * ROW)
                grads.append(dot_nt(proj[m, rows, vlanes], gm))
                s_gproj[slot, rows, vlanes] = dot(probs[m, r * pairs + p], gm).astype(BF16)

        def pull(unit):
            r, p = unit // pairs, unit % pairs
            rows = slice(r * ROW, (r + 1) * ROW)
            lanes = slice(p * ROW, (p + 1) * ROW)
            klanes = slice(width + p * ROW, width + (p + 1) * ROW)
            q = stack_pair(proj[m, rows, lanes], lane_low)
            gsc = s_gsc[unit]
            s_gproj[slot, rows, klanes] = dot(gsc, q).astype(BF16)
            gq = join_pair(dot_tn(gsc, proj[m, rows, klanes]), lane_low) * (ROW // 2) ** -0.5
            s_gproj[slot, rows, lanes] = gq.astype(BF16)

        for unit in range(units):
            for side_lanes in (slice(0, ROW), slice(ROW, 2 * ROW)):
                chances = probs[m, unit, :, side_lanes].astype(F32)
                part = grads[unit][:, side_lanes]
                inner = jnp.sum(chances * part, axis=0, keepdims=True)
                s_gsc[unit, :, side_lanes] = (chances * (part - inner)).astype(BF16)
            if unit:
                pull(unit - 1)
        pull(units - 1)
        gnormed = dot_nt(s_gproj[slot], qkv_w[...])
        gain_part, bias_part = None, None
        for rows in blocks(16):
            normal, scale = normalise(instream[m, rows, :].astype(F32))
            grad = gnormed[rows]
            first, second = partial(grad * normal), partial(grad)
            gain_part = first if gain_part is None else gain_part + first
            bias_part = second if bias_part is None else bias_part + second
            grad = gmid[rows, :] + norm_backward(grad, normal, scale, gains[0:1, :])
            gs[m, rows, :] = grad.astype(BF16)
        vec[0] += gain_part
        vec[1] += bias_part

    def backward_end(m):
        @pl.when(is_first)
        def _():
            save(9, gs.at[m], xr_o, m).start()

        @pl.when(jnp.logical_not(is_first))
        def _():
            for copy in backward_copies(m):
                copy.start()

        for copy in saves_backward(m):
            copy.start()

    def tick(t, carry):
        mf = t - stage
        mb = t - (2 * (stages - 1) - stage)

        @pl.when((mf >= 0) & (mf < micros))
        def _():
            forward_begin(mf)

            @pl.when(mf == 0)
            def _():
                weights[0].wait()

            forward_front(mf)

            @pl.when(mf == 0)
            def _():
                for copy in weights[1:]:
                    copy.wait()

            forward_back(mf)
            forward_end(mf)

        @pl.when((mb >= 0) & (mb < micros))
        def _():
            backward_begin(mb)

            @pl.when(is_last)
            def _():
                head_begin(mb)
                head(mb)
                head_end(mb)

            @pl.when(jnp.logical_not(is_last))
            def _():
                backward_receive(mb)

            backward(mb)
            backward_end(mb)

        return carry

    lax.fori_loop(0, micros + 2 * (stages - 1), tick, 0)

    for m in range(micros):
        for copy in saves_forward(m):
            copy.wait()

        @pl.when(jnp.logical_not(is_last))
        def _():
            for copy in forward_copies(m):
                copy.wait_send()

        @pl.when(jnp.logical_not(is_first))
        def _():
            for copy in backward_copies(m):
                copy.wait_send()

        @pl.when(is_first)
        def _():
            save(9, gs.at[m], xr_o, m).wait()

        @pl.when(is_last)
        def _():
            save(9, xr_l.at[m], xr_o, m).wait()

    for m in range(max(0, micros - 2), micros):
        for copy in saves_backward(m):
            copy.wait()

        @pl.when(is_last)
        def _():
            save_xl(m).wait()


def run_pipeline(stages, token_ids, segment_ids, target_ids, params):
    embed, qkv_w, qv_b, out_w, out_b, in_w, in_b, down_w, gains, shifts, fg, fb, head_w = params
    width, hid, vocab = embed.shape[1], in_w.shape[1], head_w.shape[0]
    tokens = GROUP * ROW
    micros = token_ids.shape[0] // GROUP
    pairs = width // ROW
    vmem = pl.BlockSpec(memory_space=pltpu.VMEM)
    hbm = pl.BlockSpec(memory_space=pl.ANY)

    def kept(columns):
        return jax.ShapeDtypeStruct((micros, tokens, columns), BF16)

    def scratch(lead, columns, kind=BF16):
        return pltpu.VMEM((lead, tokens, columns), kind)

    def plain(*shape):
        return pltpu.VMEM(shape, BF16)

    out_shape = [
        kept(width),
        kept(width),
        kept(width),
        kept(hid),
        kept(width),
        kept(hid),
        kept(width),
        kept(3 * width),
        kept(vocab),
        kept(width),
        jax.ShapeDtypeStruct((6, 8, width), F32),
    ]
    return pl.pallas_call(
        functools.partial(pipeline_kernel, stages, micros),
        out_shape=out_shape,
        in_specs=[vmem] * 10 + [hbm] * 6,
        out_specs=[hbm] * 10 + [vmem],
        scratch_shapes=[
            plain(vocab, width),
            plain(width, 3 * width),
            plain(width, width),
            plain(width, hid),
            plain(hid, width),
            scratch(micros, width),
            scratch(micros, width),
            scratch(micros, width),
            scratch(micros, width),
            scratch(micros, width),
            scratch(micros, width),
            scratch(micros, 3 * width),
            pltpu.VMEM((micros, GROUP * pairs, ROW, 2 * ROW), BF16),
            scratch(micros, width),
            scratch(micros, width, F32),
            scratch(micros, width),
            scratch(micros, hid),
            scratch(micros, hid),
            pltpu.VMEM((tokens, width), F32),
            pltpu.VMEM((tokens, width), F32),
            pltpu.VMEM((tokens, width), F32),
            scratch(2, width),
            scratch(2, hid),
            scratch(2, width),
            scratch(2, 3 * width),
            scratch(2, vocab),
            plain(tokens, width),
            plain(GROUP * pairs, ROW, 2 * ROW),
            pltpu.VMEM((3, 16, ROW), F32),
            pltpu.VMEM((ROW, ROW), F32),
            pltpu.SemaphoreType.DMA((micros, GROUP)),
            pltpu.SemaphoreType.DMA((micros, GROUP)),
            pltpu.SemaphoreType.DMA((micros, GROUP)),
            pltpu.SemaphoreType.DMA((micros, GROUP)),
            pltpu.SemaphoreType.DMA((10, micros)),
            pltpu.SemaphoreType.DMA((5,)),
        ],
        compiler_params=pltpu.CompilerParams(
            collective_id=0, has_side_effects=True, vmem_limit_bytes=62 * 1024 * 1024
        ),
        name="pipeline",
    )(
        token_ids,
        segment_ids,
        target_ids,
        qv_b,
        out_b,
        in_b,
        gains,
        shifts,
        fg,
        fb,
        embed,
        head_w,
        qkv_w,
        out_w,
        in_w,
        down_w,
    )


def line_dims(devices):
    dims, stride = [], 1
    if devices == 8:
        return [(2, 1), (4, 2)]
    while devices > 1:
        size = 4 if devices % 4 == 0 else 2
        dims.append((size, stride))
        stride *= size
        devices //= size
    return dims


def chunk_plan(width, hid, vocab, stages, devices):
    slim, deep = width // devices, hid // devices
    plan = [("out", 0, (slim, width), False)]
    for c in range(4):
        plan.append(("down", c, (deep, width // 4), c in (0, 2)))
    for c in range(2):
        plan.append(("extra", c, (stages, vocab // (stages * devices), width // 2), False))
    for c in range(hid // width):
        plan.append(("in", c, (slim, width), c == 1))
    for c in range(3):
        plan.append(("qkv", c, (slim, width), False))
    return plan


def gradient_kernel(stages, devices, plan, *refs):
    dims = line_dims(devices)
    refs = list(refs)

    def take(amount):
        head, refs[:] = refs[:amount], refs[amount:]
        return head

    inputs = take(10)
    vec_in, token_ids = take(2)
    qkv_out, out_out, in_out, down_out, embed_out, head_out, vec_out = take(7)
    local = take(10)
    in_sem = take(1)[0]
    turned_left, turned_xl = take(2)
    mats = dict(
        zip(
            ("normed", "mixed", "normed2", "active", "gres", "ghid", "gbr", "gproj", "xl", "xr"),
            local,
        )
    )
    names = list(mats)
    stage = lax.axis_index("pipe")
    place = lax.axis_index("dp")
    is_extra = (stage == 0) | (stage == stages - 1)
    width = mats["normed"].shape[1]
    where = [lax.rem(place // stride, size) for size, stride in dims]

    barrier = pltpu.get_barrier_semaphore()

    def greet(offset, carry):
        peer = lax.rem(place + offset, devices)
        pl.semaphore_signal(barrier, inc=1, device_id={"dp": peer}, device_id_type=MESH)
        return carry

    def greet_stage(offset, carry):
        peer = lax.rem(stage + offset, stages)
        pl.semaphore_signal(barrier, inc=1, device_id={"pipe": peer}, device_id_type=MESH)
        return carry

    lax.fori_loop(1, devices, greet, 0)
    lax.fori_loop(1, stages, greet_stage, 0)

    def load(name):
        i = names.index(name)
        return pltpu.make_async_copy(inputs[i], mats[name], in_sem.at[i])

    groups = [("mixed", "gbr"), ("gres", "active"), ("xr", "xl"), ("normed2", "ghid"), ("normed", "gproj")]

    def fetch(at):
        if at >= len(groups):
            return
        if groups[at] == ("xr", "xl"):
            @pl.when(is_extra)
            def _():
                load("xr").start()

            @pl.when(stage == stages - 1)
            def _():
                load("xl").start()

            at += 1
        for name in groups[at]:
            load(name).start()

    fetch(0)
    loaded = set()

    def need(*wanted):
        fresh = [name for name in wanted if name not in loaded]
        for name in fresh:
            loaded.add(name)
            load(name).wait()
        if fresh:
            at = [i for i, group in enumerate(groups) if group[0] == fresh[0]][0]
            fetch(at + 1)

    def identity(size):
        here = lax.broadcasted_iota(jnp.int32, (size, size), 0)
        there = lax.broadcasted_iota(jnp.int32, (size, size), 1)
        return jnp.where(here == there, 1.0, 0.0).astype(BF16)

    held = []

    def turn(name):
        if held[-1:] == [name]:
            return
        held.append(name)
        unit = identity(256)
        for q in range(width // 256):
            part = dot_nt(unit, mats[name][:, q * 256 : (q + 1) * 256])
            turned_left[q * 256 : (q + 1) * 256, :] = part.astype(BF16)

    bits = devices.bit_length() - 1
    vec_send, vec_recv = take(2)
    vec_sems = take(2)

    def vec_copy(k):
        peer = jnp.bitwise_xor(place, 1 << k)
        return pltpu.make_async_remote_copy(
            src_ref=vec_send.at[k],
            dst_ref=vec_recv.at[k],
            send_sem=vec_sems[0].at[k],
            recv_sem=vec_sems[1].at[k],
            device_id={"dp": peer},
            device_id_type=MESH,
        )

    def vec_step(k):
        def run():
            if k == 0:
                vec_send[0] = jnp.zeros(vec_send.shape[1:], F32)
                for at, row in enumerate(
                    (V_GAIN1, V_SHIFT1, V_GAIN2, V_SHIFT2, V_FINAL_GAIN, V_FINAL_BIAS)
                ):
                    vec_send[0, row : row + 1, :] = column_sum(vec_in[at])
                ones = jnp.ones((16, mats["gres"].shape[0]), BF16)
                for name, start, row in (
                    ("gproj", 0, V_QUERY),
                    ("gproj", 2 * width, V_VALUE),
                    ("gbr", 0, V_BRANCH),
                    ("gres", 0, V_RESULT),
                ):
                    part = dot(ones, mats[name][:, start : start + width])
                    vec_send[0, row : row + 1, :] = part[0:1, :]
                for q in range(mats["ghid"].shape[1] // width):
                    part = dot(ones, mats["ghid"][:, q * width : (q + 1) * width])
                    vec_send[0, V_HIDDEN + q : V_HIDDEN + q + 1, :] = part[0:1, :]
            else:
                vec_copy(k - 1).wait_recv()
                vec_send[k] = vec_send[k - 1] + vec_recv[k - 1]
            if k < bits:
                vec_copy(k).start()

        return run

    final_send, final_recv = take(2)
    final_sems = take(2)

    def final_copy(offset):
        peer = lax.rem(stages - 1 + offset, stages)
        return pltpu.make_async_remote_copy(
            src_ref=final_send,
            dst_ref=final_recv,
            send_sem=final_sems[0].at[offset],
            recv_sem=final_sems[1].at[0],
            device_id={"pipe": peer},
            device_id_type=MESH,
        )

    def vec_last():
        vec_step(bits)()
        vec_out[...] = vec_send[bits]

        @pl.when(stage == stages - 1)
        def _():
            final_send[...] = vec_send[bits, 8:16, :]
            for offset in range(1, stages):
                final_copy(offset).start()

    def vec_finish():
        @pl.when(stage != stages - 1)
        def _():
            final_copy(1).wait_recv()
            vec_out[V_FINAL_GAIN : V_FINAL_BIAS + 1, :] = final_recv[
                V_FINAL_GAIN - 8 : V_FINAL_BIAS - 7, :
            ]

    def vec_drain():
        for k in range(bits):
            vec_copy(k).wait_send()

        @pl.when(stage == stages - 1)
        def _():
            for offset in range(1, stages):
                final_copy(offset).wait_send()

    extra_sum, extra_send_sem, extra_recv_sem = take(3)

    def extra_copy(source, offset, target):
        peer = lax.rem(source + offset, stages)
        return pltpu.make_async_remote_copy(
            src_ref=extra_sum.at[peer],
            dst_ref=target,
            send_sem=extra_send_sem.at[offset],
            recv_sem=extra_recv_sem.at[0 if source == 0 else 1],
            device_id={"pipe": peer},
            device_id_type=MESH,
        )

    def chunk_steps(kind, c, block, turned):
        order = list(range(len(dims)))
        if turned:
            order.reverse()
        full = take(1)[0]

        def compute():
            if kind == "down":
                need("gres", "active")
                turn("gres")
                half, deep = width // 4, 256
                per = deep // block[0]
                unit = identity(deep)

                def body(i, carry):
                    lanes = pl.ds(pl.multiple_of(i * deep, deep), deep)
                    part = dot(turned_left[c * half : (c + 1) * half, :], mats["active"][:, lanes])
                    part = dot_nt(unit, part.astype(BF16)).astype(BF16)
                    put_blocks(full, i, per, part.reshape((per,) + block))
                    return carry

                lax.fori_loop(0, mats["active"].shape[1] // deep, body, 0)
            elif kind == "extra":
                vocab = turned_xl.shape[0]
                if c == 0:
                    load("xr").wait()

                @pl.when((stage == 0) & (c == 0))
                def _():
                    rows_n, seq = token_ids.shape
                    places = lax.broadcasted_iota(jnp.int32, (vocab, ROW), 0)
                    gap = jnp.full((1, ROW - seq), -1, jnp.int32)
                    for r in range(rows_n):
                        row = jnp.concatenate([token_ids[r : r + 1, :], gap], axis=1)
                        hot = jnp.where(places == row, 1.0, 0.0)
                        turned_xl[:, r * ROW : (r + 1) * ROW] = hot.astype(BF16)

                @pl.when((stage == stages - 1) & (c == 0))
                def _():
                    load("xl").wait()
                    unit = identity(256)
                    for q in range(vocab // 256):
                        part = dot_nt(unit, mats["xl"][:, q * 256 : (q + 1) * 256])
                        turned_xl[q * 256 : (q + 1) * 256, :] = part.astype(BF16)

                rows = vocab // stages
                for p in range(stages):
                    part = dot(
                        turned_xl[p * rows : (p + 1) * rows, :],
                        mats["xr"][:, c * (width // 2) : (c + 1) * (width // 2)],
                    )
                    part = part.astype(BF16).reshape((devices,) + block[1:])
                    for d in range(devices):
                        full[split(d) + (p,)] = part[d]
            else:
                left, right = {
                    "in": ("normed2", "ghid"),
                    "out": ("mixed", "gbr"),
                    "qkv": ("normed", "gproj"),
                }[kind]
                need(left, right)
                turn(left)
                cols = slice(c * width, (c + 1) * width)
                per = 256 // block[0]

                def body(i, carry):
                    lines = pl.ds(pl.multiple_of(i * 256, 256), 256)
                    part = dot(turned_left[lines, :], mats[right][:, cols]).astype(BF16)
                    put_blocks(full, i, per, part.reshape((per,) + block))
                    return carry

                lax.fori_loop(0, width // 256, body, 0)

        def split(d):
            return tuple((d // stride) % size for size, stride in reversed(dims))

        def put_blocks(ref, i, per, values):
            for q in range(per):
                d = i * per + q
                index = tuple(lax.rem(d // stride, size) for size, stride in reversed(dims))
                ref[index] = values[q]

        steps = [[compute]]
        for at, phase in enumerate(order):
            size = dims[phase][0]
            buffers = take(3)
            done = order[:at]
            last = at == len(order) - 1
            steps[-1].append(functools.partial(line_step, phase, size, 1, full, buffers, done))
            for t in range(2, size):
                steps.append([functools.partial(line_step, phase, size, t, full, buffers, done)])
            drains.append((kind, functools.partial(line_drain, phase, size, full, buffers, done)))
            steps.append([functools.partial(line_final, kind, c, phase, size, full, buffers, done, last)])
        if kind == "extra":
            steps = [[gated([part]) for part in step] for step in steps]
        return steps

    def gated(step):
        def run():
            @pl.when(is_extra)
            def _():
                for part in step:
                    part()

        return run

    def block_of(full, phase, j, done):
        spot = [slice(None)] * len(dims)
        for other in done:
            spot[len(dims) - 1 - other] = where[other]
        spot[len(dims) - 1 - phase] = j
        return full.at[tuple(spot)]

    def line_copy(phase, size, t, side, full, buffers, done):
        recv, ssem, rsem = buffers
        i = where[phase]
        stride = dims[phase][1]
        if side == 0:
            j, peer = size - t + i, place + jnp.where(i < size - 1, stride, 0)
        else:
            j, peer = t - size + i, place - jnp.where(i > 0, stride, 0)
        return pltpu.make_async_remote_copy(
            src_ref=block_of(full, phase, jnp.clip(j, 0, size - 1), done),
            dst_ref=recv.at[0 if size == 2 else side, t - 1],
            send_sem=ssem.at[side, t - 1],
            recv_sem=rsem.at[side, t - 1],
            device_id={"dp": peer},
            device_id_type=MESH,
        )

    def sends(i, size, t, side):
        return (i <= t - 1) if side == 0 else (i >= size - t)

    def line_step(phase, size, t, full, buffers, done):
        i = where[phase]
        for side in range(2):
            at_end = (i == 0) if side == 0 else (i == size - 1)
            j = size - t + i if side == 0 else t - size + i
            j = jnp.clip(j, 0, size - 1)

            @pl.when(sends(i, size, t, side))
            def _():
                if t > 1:
                    @pl.when(jnp.logical_not(at_end))
                    def _():
                        line_copy(phase, size, t - 1, side, full, buffers, done).wait_recv()
                        own = block_of(full, phase, j, done)
                        got = buffers[0][0 if size == 2 else side, t - 2]
                        own[...] = (own[...].astype(F32) + got.astype(F32)).astype(BF16)

                line_copy(phase, size, t, side, full, buffers, done).start()

    def line_final(kind, c, phase, size, full, buffers, done, last):
        i = where[phase]
        own = block_of(full, phase, i, done)
        total = own
        if last:
            slots = {
                "qkv": lambda: qkv_out.at[:, c * width : (c + 1) * width],
                "in": lambda: in_out.at[:, c * width : (c + 1) * width],
                "out": lambda: out_out,
                "down": lambda: down_out.at[:, c * (width // 4) : (c + 1) * (width // 4)],
                "extra": lambda: extra_sum.at[:, :, c * (width // 2) : (c + 1) * (width // 2)],
            }
            total = slots[kind]()
        lower, upper = i > 0, i < size - 1

        def arrived(side):
            line_copy(phase, size, size - 1, side, full, buffers, done).wait_recv()
            return buffers[0][0 if size == 2 else side, size - 2].astype(F32)

        @pl.when(lower & upper)
        def _():
            total[...] = (own[...].astype(F32) + arrived(0) + arrived(1)).astype(total.dtype)

        @pl.when(lower & jnp.logical_not(upper))
        def _():
            total[...] = (own[...].astype(F32) + arrived(0)).astype(total.dtype)

        @pl.when(jnp.logical_not(lower))
        def _():
            total[...] = (own[...].astype(F32) + arrived(1)).astype(total.dtype)

        if last and kind == "extra" and c == 1:
            for source_stage, out in ((0, embed_out), (stages - 1, head_out)):
                @pl.when(stage == source_stage)
                def _():
                    for offset in range(1, stages):
                        extra_copy(source_stage, offset, extra_recv[0 if source_stage == 0 else 1]).start()
                    out[...] = extra_sum[source_stage]

    def line_drain(phase, size, full, buffers, done):
        i = where[phase]
        for side in range(2):
            for t in range(1, size):
                @pl.when(sends(i, size, t, side))
                def _():
                    line_copy(phase, size, t, side, full, buffers, done).wait_send()

    extra_recv = take(2)
    drains = []
    chains = [chunk_steps(*item) for item in plan]
    depth = len(chains[0])
    vec_chain = [vec_step(k) for k in range(bits)] + [vec_last]
    starts, first, extra_rounds = [], 0, iter((0, 2, 5, 7))
    for item in plan:
        if item[3]:
            starts.append(next(extra_rounds))
        else:
            starts.append(first)
            first += 1
    begun = False
    loaded_at = max(start for start, item in zip(starts, plan) if item[0] == "qkv" and item[1] == 0)
    for r in range(max(starts) + depth):
        for d in [0] + list(range(depth - 1, 0, -1)):
            for start, chain in zip(starts, chains):
                if r - start != d:
                    continue
                for part in chain[d]:
                    part()
                    if not begun:
                        begun = True
                        pl.semaphore_wait(barrier, devices - 1 + stages - 1)
        if 0 <= r - loaded_at < len(vec_chain):
            vec_chain[r - loaded_at]()
    vec_finish()
    for source_stage, out in ((0, embed_out), (stages - 1, head_out)):
        @pl.when(stage != source_stage)
        def _():
            got = extra_recv[0 if source_stage == 0 else 1]
            extra_copy(source_stage, 1, got).wait_recv()
            out[...] = got[...]

        @pl.when(stage == source_stage)
        def _():
            for offset in range(1, stages):
                extra_copy(source_stage, offset, extra_recv[0]).wait_send()

    vec_drain()
    for kind, drain in drains:
        if kind == "extra":
            gated([drain])()
        else:
            drain()


def run_gradients(stages, devices, saved, vec, token_ids):
    dims = line_dims(devices)
    rows, tokens, width = saved[0].shape
    hid, vocab = saved[3].shape[2], saved[8].shape[2]
    plan = chunk_plan(width, hid, vocab, stages, devices)
    saved = [member.reshape(rows * tokens, member.shape[2]) for member in saved]
    vmem = pl.BlockSpec(memory_space=pltpu.VMEM)
    hbm = pl.BlockSpec(memory_space=pl.ANY)
    bits = devices.bit_length() - 1
    share = vocab // (stages * devices)
    scratch = [pltpu.VMEM(member.shape, BF16) for member in saved]
    scratch += [pltpu.SemaphoreType.DMA((len(saved),))]
    scratch += [pltpu.VMEM((width, rows * tokens), BF16), pltpu.VMEM((vocab, rows * tokens), BF16)]
    scratch += [
        pltpu.VMEM((bits + 1, VEC_ROWS, width), F32),
        pltpu.VMEM((bits, VEC_ROWS, width), F32),
        pltpu.SemaphoreType.DMA((bits,)),
        pltpu.SemaphoreType.DMA((bits,)),
        pltpu.VMEM((8, width), F32),
        pltpu.VMEM((8, width), F32),
        pltpu.SemaphoreType.DMA((stages,)),
        pltpu.SemaphoreType.DMA((1,)),
        pltpu.VMEM((stages, share, width), F32),
        pltpu.SemaphoreType.DMA((stages,)),
        pltpu.SemaphoreType.DMA((2,)),
        pltpu.VMEM((share, width), F32),
        pltpu.VMEM((share, width), F32),
    ]
    sizes = [size for size, _ in reversed(dims)]
    for _, _, block, turned in plan:
        scratch.append(pltpu.VMEM(tuple(sizes) + block, BF16))
        remain = list(reversed(dims))
        for size, stride in dims[::-1] if turned else dims:
            remain.remove((size, stride))
            piece = tuple(other for other, _ in remain) + block
            scratch.append(pltpu.VMEM((1 if size == 2 else 2, size - 1) + piece, BF16))
            scratch += [pltpu.SemaphoreType.DMA((2, size - 1))] * 2
    return pl.pallas_call(
        functools.partial(gradient_kernel, stages, devices, plan),
        out_shape=[
            jax.ShapeDtypeStruct((width // devices, 3 * width), F32),
            jax.ShapeDtypeStruct((width // devices, width), F32),
            jax.ShapeDtypeStruct((width // devices, hid), F32),
            jax.ShapeDtypeStruct((hid // devices, width), F32),
            jax.ShapeDtypeStruct((share, width), F32),
            jax.ShapeDtypeStruct((share, width), F32),
            jax.ShapeDtypeStruct((VEC_ROWS, width), F32),
        ],
        in_specs=[hbm] * len(saved) + [vmem] * 2,
        out_specs=[vmem] * 7,
        scratch_shapes=scratch,
        compiler_params=pltpu.CompilerParams(
            collective_id=1, has_side_effects=True, vmem_limit_bytes=62 * 1024 * 1024
        ),
        name="gradients",
    )(*saved, vec, token_ids)


def finish_kernel(devices, embed_g, qkv_g, out_g, in_g, down_g, head_g, vec, *outs):
    place = lax.axis_index("dp")
    width = vec.shape[1]
    (embed_o, qkv_o, qv_o, out_o, outb_o, in_o, inb_o, down_o, gain_o, shift_o, fg_o, fb_o, head_o) = outs
    embed_o[...] = embed_g[...]
    head_o[...] = head_g[...]
    for source, target in ((qkv_g, qkv_o), (out_g, out_o), (in_g, in_o), (down_g, down_o)):
        target[0] = source[...]
    lanes = width // devices
    turned = pltpu.roll(vec[0:8, :], lax.rem(width - place * lanes, width), 1)
    for row, out in ((V_QUERY, qv_o), (V_BRANCH, outb_o), (V_GAIN1, gain_o), (V_SHIFT1, shift_o)):
        out[0] = turned[row : row + 2, 0:lanes]
    share = inb_o.shape[1]
    first = place * share
    row = vec[pl.ds(V_HIDDEN + first // width, 1), :]
    wide = jnp.broadcast_to(row, (8, width))
    inb_o[...] = pltpu.roll(wide, lax.rem(width - lax.rem(first, width), width), 1)[0:1, 0:share]
    fg_o[...] = vec[V_FINAL_GAIN : V_FINAL_GAIN + 1, :]
    fb_o[...] = vec[V_FINAL_BIAS : V_FINAL_BIAS + 1, :]


def run_finish(devices, embed_g, qkv_g, out_g, in_g, down_g, head_g, vec):
    vmem = pl.BlockSpec(memory_space=pltpu.VMEM)
    width = vec.shape[1]
    lanes = width // devices

    def shape(*sizes):
        return jax.ShapeDtypeStruct(sizes, F32)

    pair = shape(1, 2, lanes)
    return pl.pallas_call(
        functools.partial(finish_kernel, devices),
        out_shape=[
            shape(*embed_g.shape),
            shape(1, *qkv_g.shape),
            pair,
            shape(1, *out_g.shape),
            pair,
            shape(1, *in_g.shape),
            shape(1, in_g.shape[1] // devices),
            shape(1, *down_g.shape),
            pair,
            pair,
            shape(1, width),
            shape(1, width),
            shape(*head_g.shape),
        ],
        in_specs=[vmem] * 7,
        out_specs=[vmem] * 13,
        name="finish",
    )(embed_g, qkv_g, out_g, in_g, down_g, head_g, vec)


def on_device(
    token_ids,
    segment_ids,
    target_ids,
    embed_table,
    qkv_weight,
    qv_bias,
    out_weight,
    out_biases,
    ff_in,
    ff_in_bias,
    ff_out,
    norm_gains,
    norm_biases,
    final_gain,
    final_bias,
    head_weight,
):
    stages = lax.axis_size("pipe")
    devices = lax.axis_size("dp")
    params = (
        embed_table,
        qkv_weight[0],
        qv_bias[0],
        out_weight[0],
        out_biases[0],
        ff_in[0],
        ff_in_bias,
        ff_out[0],
        norm_gains[0],
        norm_biases[0],
        final_gain[None],
        final_bias[None],
        head_weight,
    )
    *saved, vec = run_pipeline(stages, token_ids, segment_ids, target_ids, params)
    qkv_g, out_g, in_g, down_g, embed_g, head_g, sums = run_gradients(stages, devices, saved, vec, token_ids)
    done = list(run_finish(devices, embed_g, qkv_g, out_g, in_g, down_g, head_g, sums))
    done[10], done[11] = done[10][0], done[11][0]
    return tuple(done)


def solution(mesh):
    layer3 = P("pipe", None, None)
    return jax.shard_map(
        on_device,
        mesh=mesh,
        in_specs=(
            P("dp", None),
            P("dp", None),
            P("dp", None),
            P(),
            layer3,
            layer3,
            layer3,
            layer3,
            layer3,
            P("pipe", None),
            layer3,
            layer3,
            layer3,
            P(),
            P(),
            P(),
        ),
        out_specs=(
            P(("pipe", "dp"), None),
            P("pipe", "dp", None),
            P("pipe", None, "dp"),
            P("pipe", "dp", None),
            P("pipe", None, "dp"),
            P("pipe", "dp", None),
            P("pipe", "dp"),
            P("pipe", "dp", None),
            P("pipe", None, "dp"),
            P("pipe", None, "dp"),
            P(),
            P(),
            P(("pipe", "dp"), None),
        ),
        check_vma=False,
    )
```

```python
import functools

import jax
import jax.numpy as jnp
from jax import lax
from jax.experimental import pallas as pl
from jax.experimental.pallas import tpu as pltpu
from jax.sharding import PartitionSpec as P

HEADS = 8
FRAME = 6
ROW = 128
GROUP = 2
MASKED = -1e30
GELU_A = 0.7978845608
GELU_B = 0.044715
MESH = pl.DeviceIdType.MESH
F32 = jnp.float32
BF16 = jnp.bfloat16

VEC_ROWS = 16
V_QUERY, V_VALUE, V_BRANCH, V_RESULT, V_GAIN1, V_GAIN2, V_SHIFT1, V_SHIFT2 = range(8)
V_HIDDEN = 8
V_FINAL_GAIN, V_FINAL_BIAS = 12, 13


def dot(a, b):
    return lax.dot_general(a, b, (((1,), (0,)), ((), ())), preferred_element_type=F32)


def dot_nt(a, b):
    return lax.dot_general(a, b, (((1,), (1,)), ((), ())), preferred_element_type=F32)


def dot_tn(a, b):
    return lax.dot_general(a, b, (((0,), (0,)), ((), ())), preferred_element_type=F32)


def normalise(values):
    centre = jnp.mean(values, axis=-1, keepdims=True)
    centered = values - centre
    spread = jnp.mean(centered * centered, axis=-1, keepdims=True)
    scale = lax.rsqrt(spread + 1e-05)
    return centered * scale, scale


def norm_backward(grad, normal, scale, gain):
    grad_n = grad * gain
    mean_grad = jnp.mean(grad_n, axis=-1, keepdims=True)
    mean_proj = jnp.mean(grad_n * normal, axis=-1, keepdims=True)
    return scale * (grad_n - mean_grad - normal * mean_proj)


def column_sum(values):
    return jnp.sum(values, axis=0, keepdims=True)


def stack_pair(pair, low_lanes):
    zero = jnp.zeros_like(pair)
    return jnp.concatenate(
        [jnp.where(low_lanes, pair, zero), jnp.where(low_lanes, zero, pair)], axis=0
    )


def join_pair(stacked, low_lanes):
    half = stacked.shape[0] // 2
    return jnp.where(low_lanes, stacked[:half], stacked[half:])


def pipeline_kernel(
    stages,
    micros,
    token_ids,
    segment_ids,
    target_ids,
    qv_b,
    out_b,
    in_b,
    gains,
    shifts,
    fin_gain,
    fin_bias,
    embed_h,
    head_h,
    qkv_h,
    out_h,
    in_h,
    down_h,
    normed_o,
    mixed_o,
    normed2_o,
    active_o,
    gres_o,
    ghid_o,
    gbr_o,
    gproj_o,
    xl_o,
    xr_o,
    vec,
    side,
    qkv_w,
    out_w,
    in_w,
    down_w,
    instream,
    outb,
    gin,
    gs,
    xr_l,
    normed,
    proj,
    probs,
    mixed,
    middle,
    normed2,
    active,
    slope,
    lo,
    go,
    gmid,
    s_gres,
    s_ghid,
    s_gbr,
    s_gproj,
    s_xl,
    s_gmix,
    tmp,
    logits,
    wanted,
    masks,
    bias,
    ids,
    frames,
    fsend,
    frecv,
    bsend,
    brecv,
    osem,
    wsem,
):
    stage = lax.axis_index("pipe")
    tokens, width = instream.shape[1], instream.shape[2]
    hidden_n = in_b.shape[1]
    vocab = side.shape[0]
    pairs = width // ROW
    chunk = 512
    parts = hidden_n // chunk
    units = GROUP * pairs
    is_first = stage == 0
    is_last = stage == stages - 1
    up = jnp.minimum(stage + 1, stages - 1)
    down = jnp.maximum(stage - 1, 0)

    def bring(index, source, target):
        return pltpu.make_async_copy(source, target, wsem.at[index])

    weights = [
        bring(1, qkv_h, qkv_w),
        bring(2, out_h, out_w),
        bring(3, in_h, in_w),
        bring(4, down_h, down_w),
    ]

    @pl.when(is_first)
    def _():
        bring(0, embed_h, side).start()

    for copy in weights:
        copy.start()

    @pl.when(is_last)
    def _():
        bring(0, head_h, side).start()

    barrier = pltpu.get_barrier_semaphore()

    @pl.when(jnp.logical_not(is_first))
    def _():
        pl.semaphore_signal(barrier, inc=1, device_id={"pipe": down}, device_id_type=MESH)

    @pl.when(jnp.logical_not(is_last))
    def _():
        pl.semaphore_signal(barrier, inc=1, device_id={"pipe": up}, device_id_type=MESH)

    vec[...] = jnp.zeros_like(vec)
    bias[:, 0:width] = qv_b[0:1, :]
    bias[:, width : 2 * width] = jnp.zeros((1, width), F32)
    bias[:, 2 * width : 3 * width] = qv_b[1:2, :]
    rows_n, seq = token_ids.shape
    for index, member in enumerate((token_ids, segment_ids, target_ids)):
        ids[index] = jnp.full(ids.shape[1:], 4.0 if index == 1 else -1.0, F32)
        ids[index, 0:rows_n, 0:seq] = member[...].astype(F32)
    at_query = lax.broadcasted_iota(jnp.int32, (ROW, ROW), 1)
    at_key = lax.broadcasted_iota(jnp.int32, (ROW, ROW), 0)
    frames[...] = jnp.where(at_key < ((at_query * 43) // 256) * FRAME + FRAME, 1.0, 0.0)

    @pl.when(is_first | is_last)
    def _():
        bring(0, embed_h, side).wait()

    pl.semaphore_wait(barrier, jnp.where(is_first | is_last, 1, 2))

    def column(index, row):
        values = jnp.broadcast_to(ids[index, pl.ds(row, 1), :], (8, ROW))
        return values.T[:, 0:1]

    def hot_rows(index, m):
        values = jnp.concatenate([column(index, m * GROUP + r) for r in range(GROUP)], axis=0)
        places = lax.broadcasted_iota(jnp.int32, (tokens, vocab), 1).astype(F32)
        return values, jnp.where(values == places, 1.0, 0.0)

    def hop(source, target, send, recv, peer, m):
        return [
            pltpu.make_async_remote_copy(
                src_ref=source.at[m, pl.ds(r * ROW, ROW)],
                dst_ref=target.at[m, pl.ds(r * ROW, ROW)],
                send_sem=send.at[m, r],
                recv_sem=recv.at[m, r],
                device_id={"pipe": peer},
                device_id_type=MESH,
            )
            for r in range(GROUP)
        ]

    def forward_copies(m):
        return hop(outb, instream, fsend, frecv, up, m)

    def backward_copies(m):
        return hop(gs, gin, bsend, brecv, down, m)

    def save(index, src, dst, m):
        return pltpu.make_async_copy(src, dst.at[m], osem.at[index, m])

    def saves_forward(m):
        return [
            save(0, normed.at[m], normed_o, m),
            save(1, mixed.at[m], mixed_o, m),
            save(2, normed2.at[m], normed2_o, m),
            save(3, active.at[m], active_o, m),
        ]

    def saves_backward(m):
        slot = lax.rem(m, 2)
        return [
            save(4, s_gres.at[slot], gres_o, m),
            save(5, s_ghid.at[slot], ghid_o, m),
            save(6, s_gbr.at[slot], gbr_o, m),
            save(7, s_gproj.at[slot], gproj_o, m),
        ]

    def save_xl(m):
        return save(8, s_xl.at[lax.rem(m, 2)], xl_o, m)

    lane_low = lax.broadcasted_iota(jnp.int32, (ROW, ROW), 1) < ROW // 2

    def forward_begin(m):
        @pl.when(is_first)
        def _():
            hot = hot_rows(0, m)[1].astype(BF16)
            instream[m] = dot(hot, side[...]).astype(BF16)

        @pl.when(jnp.logical_not(is_first))
        def _():
            for copy in forward_copies(m):
                copy.wait_recv()

    def loop(count, body):
        def step(i, carry):
            body(i)
            return carry

        lax.fori_loop(0, count, step, 0)

    def span(i, size):
        return pl.ds(pl.multiple_of(i * size, size), size)

    def by_rows(size, body):
        loop(tokens // size, lambda i: body(span(i, size)))

    def partial(values):
        total = values[0:8]
        for i in range(1, values.shape[0] // 8):
            total = total + values[8 * i : 8 * i + 8]
        return total

    def forward_front(m):
        def enter(rows):
            normal, _ = normalise(instream[m, rows, :].astype(F32))
            normed[m, rows, :] = (normal * gains[0:1, :] + shifts[0:1, :]).astype(BF16)

        by_rows(64, enter)

        def project(c):
            cols = span(c, width)
            part = dot(normed[m], qkv_w[:, cols]) + bias[0:1, cols]
            proj[m, :, cols] = (part * jnp.where(c == 0, (ROW // 2) ** -0.5, 1.0)).astype(BF16)

        loop(3, project)

        def see(r):
            kinds = lax.broadcasted_iota(jnp.int32, (16, ROW), 0).astype(F32)
            member = jnp.where(ids[1, pl.ds(m * GROUP + r, 1), :] == kinds, 1.0, 0.0).astype(BF16)
            masks[r] = jnp.where(dot_tn(member, member) * frames[...] > 0.5, 0.0, MASKED)

        loop(GROUP, see)

        def attend(i):
            r = i * 2 // pairs
            rows = span(r, ROW)
            scores = []
            for j in range(2):
                p = lax.rem(2 * i + j, pairs)
                q = stack_pair(proj[m, rows, span(p, ROW)], lane_low)
                scores.append(dot_nt(proj[m, rows, span(pairs + p, ROW)], q))
            for j in range(2):
                p = lax.rem(2 * i + j, pairs)
                masked = scores[j] + jnp.concatenate([masks[r], masks[r]], axis=1)
                expo = jnp.exp(masked - jnp.max(masked, axis=0, keepdims=True))
                total = jnp.sum(expo, axis=0, keepdims=True)
                chances = (expo * (1.0 / total)).astype(BF16)
                probs[m, 2 * i + j] = chances
                both = dot_tn(chances, proj[m, rows, span(2 * pairs + p, ROW)])
                mixed[m, rows, span(p, ROW)] = join_pair(both, lane_low).astype(BF16)

        loop(units // 2, attend)

    def forward_back(m):
        tmp[...] = dot(mixed[m], out_w[...])

        def enter(rows):
            mid = instream[m, rows, :].astype(F32) + (tmp[rows, :] + out_b[0:1, :])
            middle[m, rows, :] = mid
            lo[rows, :] = mid + out_b[1:2, :]
            normal2, _ = normalise(mid)
            normed2[m, rows, :] = (normal2 * gains[1:2, :] + shifts[1:2, :]).astype(BF16)

        by_rows(64, enter)

        def feed(c):
            cols = span(c, chunk)
            hid = dot(normed2[m], in_w[:, cols]) + in_b[0:1, cols]
            square = hid * hid
            tan = jnp.tanh(hid * (GELU_A + (GELU_A * GELU_B) * square))
            half = 0.5 + 0.5 * tan
            act = (hid * half).astype(BF16)
            active[m, :, cols] = act
            rise = (1.0 - tan * tan) * (0.5 * GELU_A + (1.5 * GELU_A * GELU_B) * square)
            slope[m, :, cols] = (half + hid * rise).astype(BF16)
            lo[...] += dot(act, down_w[cols, :])

        loop(parts, feed)
        outb[m] = lo[...].astype(BF16)

    def forward_end(m):
        for copy in saves_forward(m):
            copy.start()

        @pl.when(jnp.logical_not(is_last))
        def _():
            for copy in forward_copies(m):
                copy.start()

    def head_begin(m):
        @pl.when(m >= 2)
        def _():
            save_xl(m - 2).wait()

    def head(m):
        slot = lax.rem(m, 2)

        def enter(rows):
            normal, _ = normalise(lo[rows, :])
            xr_l[m, rows, :] = (normal * fin_gain[...] + fin_bias[...]).astype(BF16)

        by_rows(64, enter)

        def guess(c):
            logits[:, span(c, chunk)] = dot_nt(xr_l[m], side[span(c, chunk), :])

        loop(vocab // chunk, guess)
        for r in range(GROUP):
            wanted[r * ROW : (r + 1) * ROW, :] = column(2, m * GROUP + r)

        def soften(rows):
            part = logits[rows, :]
            expo = jnp.exp(part - jnp.max(part, axis=-1, keepdims=True))
            total = jnp.sum(expo, axis=-1, keepdims=True)
            target = wanted[rows, :]
            places = lax.broadcasted_iota(jnp.int32, (32, vocab), 1).astype(F32)
            real = jnp.where(target >= 0.0, 1.0, 0.0)
            hot = jnp.where(target == places, 1.0, 0.0)
            s_xl[slot, rows, :] = (expo * (real / total) - hot).astype(BF16)

        by_rows(32, soften)
        tmp[...] = jnp.zeros_like(tmp)

        def pull(c):
            tmp[...] += dot(s_xl[slot, :, span(c, chunk)], side[span(c, chunk), :])

        loop(vocab // chunk, pull)

        def leave(rows):
            normal, scale = normalise(lo[rows, :])
            grad = tmp[rows, :]
            vec[4] += partial(grad * normal)
            vec[5] += partial(grad)
            go[rows, :] = norm_backward(grad, normal, scale, fin_gain[...])

        by_rows(32, leave)

    def head_end(m):
        save_xl(m).start()
        save(9, xr_l.at[m], xr_o, m).start()

    def backward_begin(m):
        @pl.when(m >= 2)
        def _():
            for copy in saves_backward(m - 2):
                copy.wait()

    def backward_receive(m):
        for copy in backward_copies(m):
            copy.wait_recv()
        go[...] = gin[m].astype(F32)

    def backward(m):
        slot = lax.rem(m, 2)
        s_gres[slot] = go[...].astype(BF16)
        tmp[...] = jnp.zeros_like(tmp)

        def feed(c):
            cols = span(c, chunk)
            gact = dot_nt(s_gres[slot], down_w[cols, :])
            ghid = (gact * slope[m, :, cols].astype(F32)).astype(BF16)
            s_ghid[slot, :, cols] = ghid
            tmp[...] += dot_nt(ghid, in_w[:, cols])

        loop(parts, feed)

        def middle_norm(rows):
            normal2, scale2 = normalise(middle[m, rows, :])
            grad = tmp[rows, :]
            vec[2] += partial(grad * normal2)
            vec[3] += partial(grad)
            grad = go[rows, :] + norm_backward(grad, normal2, scale2, gains[1:2, :])
            gmid[rows, :] = grad
            s_gbr[slot, rows, :] = grad.astype(BF16)

        by_rows(32, middle_norm)
        s_gmix[...] = dot_nt(s_gbr[slot], out_w[...]).astype(BF16)

        def attend(i):
            r = i * 2 // pairs
            rows = span(r, ROW)
            grads, heads = [], []
            for j in range(2):
                p = lax.rem(2 * i + j, pairs)
                gm = stack_pair(s_gmix[rows, span(p, ROW)], lane_low)
                vlanes = span(2 * pairs + p, ROW)
                grads.append(dot_nt(proj[m, rows, vlanes], gm))
                s_gproj[slot, rows, vlanes] = dot(probs[m, 2 * i + j], gm).astype(BF16)
            for j in range(2):
                chances = probs[m, 2 * i + j].astype(F32)
                inner = jnp.sum(chances * grads[j], axis=0, keepdims=True)
                gsc = (chances * (grads[j] - inner)).astype(BF16)
                p = lax.rem(2 * i + j, pairs)
                lanes, klanes = span(p, ROW), span(pairs + p, ROW)
                q = stack_pair(proj[m, rows, lanes], lane_low)
                s_gproj[slot, rows, klanes] = dot(gsc, q).astype(BF16)
                gq = join_pair(dot_tn(gsc, proj[m, rows, klanes]), lane_low)
                s_gproj[slot, rows, lanes] = (gq * (ROW // 2) ** -0.5).astype(BF16)

        loop(units // 2, attend)
        tmp[...] = jnp.zeros_like(tmp)

        def project(c):
            cols = span(c, width)
            tmp[...] += dot_nt(s_gproj[slot, :, cols], qkv_w[:, cols])

        loop(3, project)

        def leave(rows):
            normal, scale = normalise(instream[m, rows, :].astype(F32))
            grad = tmp[rows, :]
            vec[0] += partial(grad * normal)
            vec[1] += partial(grad)
            grad = gmid[rows, :] + norm_backward(grad, normal, scale, gains[0:1, :])
            gs[m, rows, :] = grad.astype(BF16)

        by_rows(32, leave)

    def backward_end(m):
        @pl.when(is_first)
        def _():
            save(9, gs.at[m], xr_o, m).start()

        @pl.when(jnp.logical_not(is_first))
        def _():
            for copy in backward_copies(m):
                copy.start()

        for copy in saves_backward(m):
            copy.start()

    def tick(t, carry):
        mf = t - stage
        mb = t - (2 * (stages - 1) - stage)

        @pl.when((mf >= 0) & (mf < micros))
        def _():
            forward_begin(mf)

            @pl.when(mf == 0)
            def _():
                weights[0].wait()

            forward_front(mf)

            @pl.when(mf == 0)
            def _():
                for copy in weights[1:]:
                    copy.wait()

            forward_back(mf)
            forward_end(mf)

        @pl.when((mb >= 0) & (mb < micros))
        def _():
            backward_begin(mb)

            @pl.when(is_last)
            def _():
                head_begin(mb)
                head(mb)
                head_end(mb)

            @pl.when(jnp.logical_not(is_last))
            def _():
                backward_receive(mb)

            backward(mb)
            backward_end(mb)

        return carry

    lax.fori_loop(0, micros + 2 * (stages - 1), tick, 0)

    for m in range(micros):
        for copy in saves_forward(m):
            copy.wait()

        @pl.when(jnp.logical_not(is_last))
        def _():
            for copy in forward_copies(m):
                copy.wait_send()

        @pl.when(jnp.logical_not(is_first))
        def _():
            for copy in backward_copies(m):
                copy.wait_send()

        @pl.when(is_first)
        def _():
            save(9, gs.at[m], xr_o, m).wait()

        @pl.when(is_last)
        def _():
            save(9, xr_l.at[m], xr_o, m).wait()

    for m in range(max(0, micros - 2), micros):
        for copy in saves_backward(m):
            copy.wait()

        @pl.when(is_last)
        def _():
            save_xl(m).wait()


def run_pipeline(stages, token_ids, segment_ids, target_ids, params):
    embed, qkv_w, qv_b, out_w, out_b, in_w, in_b, down_w, gains, shifts, fg, fb, head_w = params
    width, hid, vocab = embed.shape[1], in_w.shape[1], head_w.shape[0]
    tokens = GROUP * ROW
    micros = token_ids.shape[0] // GROUP
    pairs = width // ROW
    vmem = pl.BlockSpec(memory_space=pltpu.VMEM)
    hbm = pl.BlockSpec(memory_space=pl.ANY)

    def kept(columns):
        return jax.ShapeDtypeStruct((micros, tokens, columns), BF16)

    def scratch(lead, columns, kind=BF16):
        return pltpu.VMEM((lead, tokens, columns), kind)

    def plain(*shape):
        return pltpu.VMEM(shape, BF16)

    out_shape = [
        kept(width),
        kept(width),
        kept(width),
        kept(hid),
        kept(width),
        kept(hid),
        kept(width),
        kept(3 * width),
        kept(vocab),
        kept(width),
        jax.ShapeDtypeStruct((6, 8, width), F32),
    ]
    return pl.pallas_call(
        functools.partial(pipeline_kernel, stages, micros),
        out_shape=out_shape,
        in_specs=[vmem] * 10 + [hbm] * 6,
        out_specs=[hbm] * 10 + [vmem],
        scratch_shapes=[
            plain(vocab, width),
            plain(width, 3 * width),
            plain(width, width),
            plain(width, hid),
            plain(hid, width),
            scratch(micros, width),
            scratch(micros, width),
            scratch(micros, width),
            scratch(micros, width),
            scratch(micros, width),
            scratch(micros, width),
            scratch(micros, 3 * width),
            pltpu.VMEM((micros, GROUP * pairs, ROW, 2 * ROW), BF16),
            scratch(micros, width),
            scratch(micros, width, F32),
            scratch(micros, width),
            scratch(micros, hid),
            scratch(micros, hid),
            pltpu.VMEM((tokens, width), F32),
            pltpu.VMEM((tokens, width), F32),
            pltpu.VMEM((tokens, width), F32),
            scratch(2, width),
            scratch(2, hid),
            scratch(2, width),
            scratch(2, 3 * width),
            scratch(2, vocab),
            plain(tokens, width),
            pltpu.VMEM((tokens, width), F32),
            pltpu.VMEM((tokens, vocab), F32),
            pltpu.VMEM((tokens, 1), F32),
            pltpu.VMEM((GROUP, ROW, ROW), F32),
            pltpu.VMEM((1, 3 * width), F32),
            pltpu.VMEM((3, 16, ROW), F32),
            pltpu.VMEM((ROW, ROW), F32),
            pltpu.SemaphoreType.DMA((micros, GROUP)),
            pltpu.SemaphoreType.DMA((micros, GROUP)),
            pltpu.SemaphoreType.DMA((micros, GROUP)),
            pltpu.SemaphoreType.DMA((micros, GROUP)),
            pltpu.SemaphoreType.DMA((10, micros)),
            pltpu.SemaphoreType.DMA((5,)),
        ],
        compiler_params=pltpu.CompilerParams(
            collective_id=0, has_side_effects=True, vmem_limit_bytes=62 * 1024 * 1024
        ),
        name="pipeline",
    )(
        token_ids,
        segment_ids,
        target_ids,
        qv_b,
        out_b,
        in_b,
        gains,
        shifts,
        fg,
        fb,
        embed,
        head_w,
        qkv_w,
        out_w,
        in_w,
        down_w,
    )


def line_dims(devices):
    dims, stride = [], 1
    if devices == 8:
        return [(2, 1), (4, 2)]
    while devices > 1:
        size = 4 if devices % 4 == 0 else 2
        dims.append((size, stride))
        stride *= size
        devices //= size
    return dims


def chunk_plan(width, hid, vocab, stages, devices):
    slim, deep = width // devices, hid // devices
    plan = [("out", 0, (slim, width), False)]
    for c in range(4):
        plan.append(("down", c, (deep, width // 4), c in (0, 2)))
    for c in range(2):
        plan.append(("extra", c, (stages, vocab // (stages * devices), width // 2), False))
    for c in range(hid // width):
        plan.append(("in", c, (slim, width), c == 1))
    for c in range(3):
        plan.append(("qkv", c, (slim, width), False))
    return plan


def gradient_kernel(stages, devices, plan, *refs):
    dims = line_dims(devices)
    refs = list(refs)

    def take(amount):
        head, refs[:] = refs[:amount], refs[amount:]
        return head

    inputs = take(10)
    vec_in, token_ids = take(2)
    qkv_out, out_out, in_out, down_out, embed_out, head_out, vec_out = take(7)
    local = take(10)
    in_sem = take(1)[0]
    turned_left, turned_xl = take(2)
    mats = dict(
        zip(
            ("normed", "mixed", "normed2", "active", "gres", "ghid", "gbr", "gproj", "xl", "xr"),
            local,
        )
    )
    names = list(mats)
    stage = lax.axis_index("pipe")
    place = lax.axis_index("dp")
    is_extra = (stage == 0) | (stage == stages - 1)
    width = mats["normed"].shape[1]
    where = [lax.rem(place // stride, size) for size, stride in dims]

    barrier = pltpu.get_barrier_semaphore()

    def greet(offset, carry):
        peer = lax.rem(place + offset, devices)
        pl.semaphore_signal(barrier, inc=1, device_id={"dp": peer}, device_id_type=MESH)
        return carry

    def greet_stage(offset, carry):
        peer = lax.rem(stage + offset, stages)
        pl.semaphore_signal(barrier, inc=1, device_id={"pipe": peer}, device_id_type=MESH)
        return carry

    lax.fori_loop(1, devices, greet, 0)
    lax.fori_loop(1, stages, greet_stage, 0)

    def load(name):
        i = names.index(name)
        return pltpu.make_async_copy(inputs[i], mats[name], in_sem.at[i])

    groups = [("mixed", "gbr"), ("gres", "active"), ("xr", "xl"), ("normed2", "ghid"), ("normed", "gproj")]

    def fetch(at):
        if at >= len(groups):
            return
        if groups[at] == ("xr", "xl"):
            @pl.when(is_extra)
            def _():
                load("xr").start()

            @pl.when(stage == stages - 1)
            def _():
                load("xl").start()

            at += 1
        for name in groups[at]:
            load(name).start()

    fetch(0)
    loaded = set()

    def need(*wanted):
        fresh = [name for name in wanted if name not in loaded]
        for name in fresh:
            loaded.add(name)
            load(name).wait()
        if fresh:
            at = [i for i, group in enumerate(groups) if group[0] == fresh[0]][0]
            fetch(at + 1)

    def identity(size):
        here = lax.broadcasted_iota(jnp.int32, (size, size), 0)
        there = lax.broadcasted_iota(jnp.int32, (size, size), 1)
        return jnp.where(here == there, 1.0, 0.0).astype(BF16)

    held = []

    def turn(name):
        if held[-1:] == [name]:
            return
        held.append(name)
        unit = identity(256)
        for q in range(width // 256):
            part = dot_nt(unit, mats[name][:, q * 256 : (q + 1) * 256])
            turned_left[q * 256 : (q + 1) * 256, :] = part.astype(BF16)

    bits = devices.bit_length() - 1
    vec_send, vec_recv = take(2)
    vec_sems = take(2)

    def vec_copy(k):
        peer = jnp.bitwise_xor(place, 1 << k)
        return pltpu.make_async_remote_copy(
            src_ref=vec_send.at[k],
            dst_ref=vec_recv.at[k],
            send_sem=vec_sems[0].at[k],
            recv_sem=vec_sems[1].at[k],
            device_id={"dp": peer},
            device_id_type=MESH,
        )

    def vec_step(k):
        def run():
            if k == 0:
                vec_send[0] = jnp.zeros(vec_send.shape[1:], F32)
                for at, row in enumerate(
                    (V_GAIN1, V_SHIFT1, V_GAIN2, V_SHIFT2, V_FINAL_GAIN, V_FINAL_BIAS)
                ):
                    vec_send[0, row : row + 1, :] = column_sum(vec_in[at])
                ones = jnp.ones((16, mats["gres"].shape[0]), BF16)
                for name, start, row in (
                    ("gproj", 0, V_QUERY),
                    ("gproj", 2 * width, V_VALUE),
                    ("gbr", 0, V_BRANCH),
                    ("gres", 0, V_RESULT),
                ):
                    part = dot(ones, mats[name][:, start : start + width])
                    vec_send[0, row : row + 1, :] = part[0:1, :]
                for q in range(mats["ghid"].shape[1] // width):
                    part = dot(ones, mats["ghid"][:, q * width : (q + 1) * width])
                    vec_send[0, V_HIDDEN + q : V_HIDDEN + q + 1, :] = part[0:1, :]
            else:
                vec_copy(k - 1).wait_recv()
                vec_send[k] = vec_send[k - 1] + vec_recv[k - 1]
            if k < bits:
                vec_copy(k).start()

        return run

    final_send, final_recv = take(2)
    final_sems = take(2)

    def final_copy(offset):
        peer = lax.rem(stages - 1 + offset, stages)
        return pltpu.make_async_remote_copy(
            src_ref=final_send,
            dst_ref=final_recv,
            send_sem=final_sems[0].at[offset],
            recv_sem=final_sems[1].at[0],
            device_id={"pipe": peer},
            device_id_type=MESH,
        )

    def vec_last():
        vec_step(bits)()
        vec_out[...] = vec_send[bits]

        @pl.when(stage == stages - 1)
        def _():
            final_send[...] = vec_send[bits, 8:16, :]
            for offset in range(1, stages):
                final_copy(offset).start()

    def vec_finish():
        @pl.when(stage != stages - 1)
        def _():
            final_copy(1).wait_recv()
            vec_out[V_FINAL_GAIN : V_FINAL_BIAS + 1, :] = final_recv[
                V_FINAL_GAIN - 8 : V_FINAL_BIAS - 7, :
            ]

    def vec_drain():
        for k in range(bits):
            vec_copy(k).wait_send()

        @pl.when(stage == stages - 1)
        def _():
            for offset in range(1, stages):
                final_copy(offset).wait_send()

    extra_sum, extra_send_sem, extra_recv_sem = take(3)

    def extra_copy(source, offset, target):
        peer = lax.rem(source + offset, stages)
        return pltpu.make_async_remote_copy(
            src_ref=extra_sum.at[peer],
            dst_ref=target,
            send_sem=extra_send_sem.at[offset],
            recv_sem=extra_recv_sem.at[0 if source == 0 else 1],
            device_id={"pipe": peer},
            device_id_type=MESH,
        )

    def chunk_steps(kind, c, block, turned):
        order = list(range(len(dims)))
        if turned:
            order.reverse()
        full = take(1)[0]

        def compute():
            if kind == "down":
                need("gres", "active")
                turn("gres")
                half, deep = width // 4, 256
                per = deep // block[0]
                unit = identity(deep)

                def body(i, carry):
                    lanes = pl.ds(pl.multiple_of(i * deep, deep), deep)
                    part = dot(turned_left[c * half : (c + 1) * half, :], mats["active"][:, lanes])
                    part = dot_nt(unit, part.astype(BF16)).astype(BF16)
                    put_blocks(full, i, per, part.reshape((per,) + block))
                    return carry

                lax.fori_loop(0, mats["active"].shape[1] // deep, body, 0)
            elif kind == "extra":
                vocab = turned_xl.shape[0]
                if c == 0:
                    load("xr").wait()

                @pl.when((stage == 0) & (c == 0))
                def _():
                    rows_n, seq = token_ids.shape
                    places = lax.broadcasted_iota(jnp.int32, (vocab, ROW), 0)
                    gap = jnp.full((1, ROW - seq), -1, jnp.int32)
                    for r in range(rows_n):
                        row = jnp.concatenate([token_ids[r : r + 1, :], gap], axis=1)
                        hot = jnp.where(places == row, 1.0, 0.0)
                        turned_xl[:, r * ROW : (r + 1) * ROW] = hot.astype(BF16)

                @pl.when((stage == stages - 1) & (c == 0))
                def _():
                    load("xl").wait()
                    unit = identity(256)
                    for q in range(vocab // 256):
                        part = dot_nt(unit, mats["xl"][:, q * 256 : (q + 1) * 256])
                        turned_xl[q * 256 : (q + 1) * 256, :] = part.astype(BF16)

                rows = vocab // stages
                for p in range(stages):
                    part = dot(
                        turned_xl[p * rows : (p + 1) * rows, :],
                        mats["xr"][:, c * (width // 2) : (c + 1) * (width // 2)],
                    )
                    part = part.astype(BF16).reshape((devices,) + block[1:])
                    for d in range(devices):
                        full[split(d) + (p,)] = part[d]
            else:
                left, right = {
                    "in": ("normed2", "ghid"),
                    "out": ("mixed", "gbr"),
                    "qkv": ("normed", "gproj"),
                }[kind]
                need(left, right)
                turn(left)
                cols = slice(c * width, (c + 1) * width)
                per = 256 // block[0]

                def body(i, carry):
                    lines = pl.ds(pl.multiple_of(i * 256, 256), 256)
                    part = dot(turned_left[lines, :], mats[right][:, cols]).astype(BF16)
                    put_blocks(full, i, per, part.reshape((per,) + block))
                    return carry

                lax.fori_loop(0, width // 256, body, 0)

        def split(d):
            return tuple((d // stride) % size for size, stride in reversed(dims))

        def put_blocks(ref, i, per, values):
            for q in range(per):
                d = i * per + q
                index = tuple(lax.rem(d // stride, size) for size, stride in reversed(dims))
                ref[index] = values[q]

        steps = [[compute]]
        for at, phase in enumerate(order):
            size = dims[phase][0]
            buffers = take(3)
            done = order[:at]
            last = at == len(order) - 1
            steps[-1].append(functools.partial(line_step, phase, size, 1, full, buffers, done))
            for t in range(2, size):
                steps.append([functools.partial(line_step, phase, size, t, full, buffers, done)])
            drains.append((kind, functools.partial(line_drain, phase, size, full, buffers, done)))
            steps.append([functools.partial(line_final, kind, c, phase, size, full, buffers, done, last)])
        if kind == "extra":
            steps = [[gated([part]) for part in step] for step in steps]
        return steps

    def gated(step):
        def run():
            @pl.when(is_extra)
            def _():
                for part in step:
                    part()

        return run

    def block_of(full, phase, j, done):
        spot = [slice(None)] * len(dims)
        for other in done:
            spot[len(dims) - 1 - other] = where[other]
        spot[len(dims) - 1 - phase] = j
        return full.at[tuple(spot)]

    def line_copy(phase, size, t, side, full, buffers, done):
        recv, ssem, rsem = buffers
        i = where[phase]
        stride = dims[phase][1]
        if side == 0:
            j, peer = size - t + i, place + jnp.where(i < size - 1, stride, 0)
        else:
            j, peer = t - size + i, place - jnp.where(i > 0, stride, 0)
        return pltpu.make_async_remote_copy(
            src_ref=block_of(full, phase, jnp.clip(j, 0, size - 1), done),
            dst_ref=recv.at[0 if size == 2 else side, t - 1],
            send_sem=ssem.at[side, t - 1],
            recv_sem=rsem.at[side, t - 1],
            device_id={"dp": peer},
            device_id_type=MESH,
        )

    def sends(i, size, t, side):
        return (i <= t - 1) if side == 0 else (i >= size - t)

    def line_step(phase, size, t, full, buffers, done):
        i = where[phase]
        for side in range(2):
            at_end = (i == 0) if side == 0 else (i == size - 1)
            j = size - t + i if side == 0 else t - size + i
            j = jnp.clip(j, 0, size - 1)

            @pl.when(sends(i, size, t, side))
            def _():
                if t > 1:
                    @pl.when(jnp.logical_not(at_end))
                    def _():
                        line_copy(phase, size, t - 1, side, full, buffers, done).wait_recv()
                        own = block_of(full, phase, j, done)
                        got = buffers[0][0 if size == 2 else side, t - 2]
                        own[...] = (own[...].astype(F32) + got.astype(F32)).astype(BF16)

                line_copy(phase, size, t, side, full, buffers, done).start()

    def line_final(kind, c, phase, size, full, buffers, done, last):
        i = where[phase]
        own = block_of(full, phase, i, done)
        total = own
        if last:
            slots = {
                "qkv": lambda: qkv_out.at[:, c * width : (c + 1) * width],
                "in": lambda: in_out.at[:, c * width : (c + 1) * width],
                "out": lambda: out_out,
                "down": lambda: down_out.at[:, c * (width // 4) : (c + 1) * (width // 4)],
                "extra": lambda: extra_sum.at[:, :, c * (width // 2) : (c + 1) * (width // 2)],
            }
            total = slots[kind]()
        lower, upper = i > 0, i < size - 1

        def arrived(side):
            line_copy(phase, size, size - 1, side, full, buffers, done).wait_recv()
            return buffers[0][0 if size == 2 else side, size - 2].astype(F32)

        @pl.when(lower & upper)
        def _():
            total[...] = (own[...].astype(F32) + arrived(0) + arrived(1)).astype(total.dtype)

        @pl.when(lower & jnp.logical_not(upper))
        def _():
            total[...] = (own[...].astype(F32) + arrived(0)).astype(total.dtype)

        @pl.when(jnp.logical_not(lower))
        def _():
            total[...] = (own[...].astype(F32) + arrived(1)).astype(total.dtype)

        if last and kind == "extra" and c == 1:
            for source_stage, out in ((0, embed_out), (stages - 1, head_out)):
                @pl.when(stage == source_stage)
                def _():
                    for offset in range(1, stages):
                        extra_copy(source_stage, offset, extra_recv[0 if source_stage == 0 else 1]).start()
                    out[...] = extra_sum[source_stage]

    def line_drain(phase, size, full, buffers, done):
        i = where[phase]
        for side in range(2):
            for t in range(1, size):
                @pl.when(sends(i, size, t, side))
                def _():
                    line_copy(phase, size, t, side, full, buffers, done).wait_send()

    extra_recv = take(2)
    drains = []
    chains = [chunk_steps(*item) for item in plan]
    depth = len(chains[0])
    vec_chain = [vec_step(k) for k in range(bits)] + [vec_last]
    starts, first, extra_rounds = [], 0, iter((0, 2, 5, 7))
    for item in plan:
        if item[3]:
            starts.append(next(extra_rounds))
        else:
            starts.append(first)
            first += 1
    begun = False
    loaded_at = max(start for start, item in zip(starts, plan) if item[0] == "qkv" and item[1] == 0)
    for r in range(max(starts) + depth):
        for d in [0] + list(range(depth - 1, 0, -1)):
            for start, chain in zip(starts, chains):
                if r - start != d:
                    continue
                for part in chain[d]:
                    part()
                    if not begun:
                        begun = True
                        pl.semaphore_wait(barrier, devices - 1 + stages - 1)
        if 0 <= r - loaded_at < len(vec_chain):
            vec_chain[r - loaded_at]()
    vec_finish()
    for source_stage, out in ((0, embed_out), (stages - 1, head_out)):
        @pl.when(stage != source_stage)
        def _():
            got = extra_recv[0 if source_stage == 0 else 1]
            extra_copy(source_stage, 1, got).wait_recv()
            out[...] = got[...]

        @pl.when(stage == source_stage)
        def _():
            for offset in range(1, stages):
                extra_copy(source_stage, offset, extra_recv[0]).wait_send()

    vec_drain()
    for kind, drain in drains:
        if kind == "extra":
            gated([drain])()
        else:
            drain()


def run_gradients(stages, devices, saved, vec, token_ids):
    dims = line_dims(devices)
    rows, tokens, width = saved[0].shape
    hid, vocab = saved[3].shape[2], saved[8].shape[2]
    plan = chunk_plan(width, hid, vocab, stages, devices)
    saved = [member.reshape(rows * tokens, member.shape[2]) for member in saved]
    vmem = pl.BlockSpec(memory_space=pltpu.VMEM)
    hbm = pl.BlockSpec(memory_space=pl.ANY)
    bits = devices.bit_length() - 1
    share = vocab // (stages * devices)
    scratch = [pltpu.VMEM(member.shape, BF16) for member in saved]
    scratch += [pltpu.SemaphoreType.DMA((len(saved),))]
    scratch += [pltpu.VMEM((width, rows * tokens), BF16), pltpu.VMEM((vocab, rows * tokens), BF16)]
    scratch += [
        pltpu.VMEM((bits + 1, VEC_ROWS, width), F32),
        pltpu.VMEM((bits, VEC_ROWS, width), F32),
        pltpu.SemaphoreType.DMA((bits,)),
        pltpu.SemaphoreType.DMA((bits,)),
        pltpu.VMEM((8, width), F32),
        pltpu.VMEM((8, width), F32),
        pltpu.SemaphoreType.DMA((stages,)),
        pltpu.SemaphoreType.DMA((1,)),
        pltpu.VMEM((stages, share, width), F32),
        pltpu.SemaphoreType.DMA((stages,)),
        pltpu.SemaphoreType.DMA((2,)),
        pltpu.VMEM((share, width), F32),
        pltpu.VMEM((share, width), F32),
    ]
    sizes = [size for size, _ in reversed(dims)]
    for _, _, block, turned in plan:
        scratch.append(pltpu.VMEM(tuple(sizes) + block, BF16))
        remain = list(reversed(dims))
        for size, stride in dims[::-1] if turned else dims:
            remain.remove((size, stride))
            piece = tuple(other for other, _ in remain) + block
            scratch.append(pltpu.VMEM((1 if size == 2 else 2, size - 1) + piece, BF16))
            scratch += [pltpu.SemaphoreType.DMA((2, size - 1))] * 2
    return pl.pallas_call(
        functools.partial(gradient_kernel, stages, devices, plan),
        out_shape=[
            jax.ShapeDtypeStruct((width // devices, 3 * width), F32),
            jax.ShapeDtypeStruct((width // devices, width), F32),
            jax.ShapeDtypeStruct((width // devices, hid), F32),
            jax.ShapeDtypeStruct((hid // devices, width), F32),
            jax.ShapeDtypeStruct((share, width), F32),
            jax.ShapeDtypeStruct((share, width), F32),
            jax.ShapeDtypeStruct((VEC_ROWS, width), F32),
        ],
        in_specs=[hbm] * len(saved) + [vmem] * 2,
        out_specs=[vmem] * 7,
        scratch_shapes=scratch,
        compiler_params=pltpu.CompilerParams(
            collective_id=1, has_side_effects=True, vmem_limit_bytes=62 * 1024 * 1024
        ),
        name="gradients",
    )(*saved, vec, token_ids)


def finish_kernel(devices, embed_g, qkv_g, out_g, in_g, down_g, head_g, vec, *outs):
    place = lax.axis_index("dp")
    width = vec.shape[1]
    (embed_o, qkv_o, qv_o, out_o, outb_o, in_o, inb_o, down_o, gain_o, shift_o, fg_o, fb_o, head_o) = outs
    embed_o[...] = embed_g[...]
    head_o[...] = head_g[...]
    for source, target in ((qkv_g, qkv_o), (out_g, out_o), (in_g, in_o), (down_g, down_o)):
        target[0] = source[...]
    lanes = width // devices
    turned = pltpu.roll(vec[0:8, :], lax.rem(width - place * lanes, width), 1)
    for row, out in ((V_QUERY, qv_o), (V_BRANCH, outb_o), (V_GAIN1, gain_o), (V_SHIFT1, shift_o)):
        out[0] = turned[row : row + 2, 0:lanes]
    share = inb_o.shape[1]
    first = place * share
    row = vec[pl.ds(V_HIDDEN + first // width, 1), :]
    wide = jnp.broadcast_to(row, (8, width))
    inb_o[...] = pltpu.roll(wide, lax.rem(width - lax.rem(first, width), width), 1)[0:1, 0:share]
    fg_o[...] = vec[V_FINAL_GAIN : V_FINAL_GAIN + 1, :]
    fb_o[...] = vec[V_FINAL_BIAS : V_FINAL_BIAS + 1, :]


def run_finish(devices, embed_g, qkv_g, out_g, in_g, down_g, head_g, vec):
    vmem = pl.BlockSpec(memory_space=pltpu.VMEM)
    width = vec.shape[1]
    lanes = width // devices

    def shape(*sizes):
        return jax.ShapeDtypeStruct(sizes, F32)

    pair = shape(1, 2, lanes)
    return pl.pallas_call(
        functools.partial(finish_kernel, devices),
        out_shape=[
            shape(*embed_g.shape),
            shape(1, *qkv_g.shape),
            pair,
            shape(1, *out_g.shape),
            pair,
            shape(1, *in_g.shape),
            shape(1, in_g.shape[1] // devices),
            shape(1, *down_g.shape),
            pair,
            pair,
            shape(1, width),
            shape(1, width),
            shape(*head_g.shape),
        ],
        in_specs=[vmem] * 7,
        out_specs=[vmem] * 13,
        name="finish",
    )(embed_g, qkv_g, out_g, in_g, down_g, head_g, vec)


def on_device(
    token_ids,
    segment_ids,
    target_ids,
    embed_table,
    qkv_weight,
    qv_bias,
    out_weight,
    out_biases,
    ff_in,
    ff_in_bias,
    ff_out,
    norm_gains,
    norm_biases,
    final_gain,
    final_bias,
    head_weight,
):
    stages = lax.axis_size("pipe")
    devices = lax.axis_size("dp")
    params = (
        embed_table,
        qkv_weight[0],
        qv_bias[0],
        out_weight[0],
        out_biases[0],
        ff_in[0],
        ff_in_bias,
        ff_out[0],
        norm_gains[0],
        norm_biases[0],
        final_gain[None],
        final_bias[None],
        head_weight,
    )
    *saved, vec = run_pipeline(stages, token_ids, segment_ids, target_ids, params)
    qkv_g, out_g, in_g, down_g, embed_g, head_g, sums = run_gradients(stages, devices, saved, vec, token_ids)
    done = list(run_finish(devices, embed_g, qkv_g, out_g, in_g, down_g, head_g, sums))
    done[10], done[11] = done[10][0], done[11][0]
    return tuple(done)


def solution(mesh):
    layer3 = P("pipe", None, None)
    return jax.shard_map(
        on_device,
        mesh=mesh,
        in_specs=(
            P("dp", None),
            P("dp", None),
            P("dp", None),
            P(),
            layer3,
            layer3,
            layer3,
            layer3,
            layer3,
            P("pipe", None),
            layer3,
            layer3,
            layer3,
            P(),
            P(),
            P(),
        ),
        out_specs=(
            P(("pipe", "dp"), None),
            P("pipe", "dp", None),
            P("pipe", None, "dp"),
            P("pipe", "dp", None),
            P("pipe", None, "dp"),
            P("pipe", "dp", None),
            P("pipe", "dp"),
            P("pipe", "dp", None),
            P("pipe", None, "dp"),
            P("pipe", None, "dp"),
            P(),
            P(),
            P(("pipe", "dp"), None),
        ),
        check_vma=False,
    )
```

```python
import functools

import jax
import jax.numpy as jnp
from jax import lax
from jax.experimental import pallas as pl
from jax.experimental.pallas import tpu as pltpu
from jax.sharding import PartitionSpec as P

HEADS = 8
FRAME = 6
ROW = 128
GROUP = 2
MASKED = -1e30
GELU_A = 0.7978845608
GELU_B = 0.044715
MESH = pl.DeviceIdType.MESH
F32 = jnp.float32
BF16 = jnp.bfloat16

VEC_ROWS = 16
V_QUERY, V_VALUE, V_BRANCH, V_RESULT, V_GAIN1, V_GAIN2, V_SHIFT1, V_SHIFT2 = range(8)
V_HIDDEN = 8
V_FINAL_GAIN, V_FINAL_BIAS = 12, 13


def dot(a, b):
    return lax.dot_general(a, b, (((1,), (0,)), ((), ())), preferred_element_type=F32)


def dot_nt(a, b):
    return lax.dot_general(a, b, (((1,), (1,)), ((), ())), preferred_element_type=F32)


def dot_tn(a, b):
    return lax.dot_general(a, b, (((0,), (0,)), ((), ())), preferred_element_type=F32)


def normalise(values):
    centre = jnp.mean(values, axis=-1, keepdims=True)
    centered = values - centre
    spread = jnp.mean(centered * centered, axis=-1, keepdims=True)
    scale = lax.rsqrt(spread + 1e-05)
    return centered * scale, scale


def norm_backward(grad, normal, scale, gain):
    grad_n = grad * gain
    mean_grad = jnp.mean(grad_n, axis=-1, keepdims=True)
    mean_proj = jnp.mean(grad_n * normal, axis=-1, keepdims=True)
    return scale * (grad_n - mean_grad - normal * mean_proj)


def column_sum(values):
    return jnp.sum(values, axis=0, keepdims=True)


def stack_pair(pair, low_lanes):
    zero = jnp.zeros_like(pair)
    return jnp.concatenate(
        [jnp.where(low_lanes, pair, zero), jnp.where(low_lanes, zero, pair)], axis=0
    )


def join_pair(stacked, low_lanes):
    half = stacked.shape[0] // 2
    return jnp.where(low_lanes, stacked[:half], stacked[half:])


def pipeline_kernel(
    stages,
    micros,
    token_ids,
    segment_ids,
    target_ids,
    embed,
    qkv_w,
    qv_b,
    out_w,
    out_b,
    in_w,
    in_b,
    down_w,
    gains,
    shifts,
    fin_gain,
    fin_bias,
    head_w,
    normed_o,
    mixed_o,
    normed2_o,
    active_o,
    gres_o,
    ghid_o,
    gbr_o,
    gproj_o,
    xl_o,
    xr_o,
    vec,
    instream,
    outb,
    gin,
    gs,
    normed,
    proj,
    probs,
    mixed,
    middle,
    normed2,
    active,
    slope,
    lo,
    go,
    gmid,
    s_gres,
    s_ghid,
    s_gbr,
    s_gproj,
    s_xl,
    ids,
    frames,
    fsend,
    frecv,
    bsend,
    brecv,
    osem,
):
    stage = lax.axis_index("pipe")
    tokens, width = instream.shape[1], instream.shape[2]
    hidden_n = in_b.shape[1]
    vocab = head_w.shape[0]
    pairs = width // ROW
    chunk = 512
    is_first = stage == 0
    is_last = stage == stages - 1
    up = jnp.minimum(stage + 1, stages - 1)
    down = jnp.maximum(stage - 1, 0)

    barrier = pltpu.get_barrier_semaphore()

    @pl.when(jnp.logical_not(is_first))
    def _():
        pl.semaphore_signal(barrier, inc=1, device_id={"pipe": down}, device_id_type=MESH)

    @pl.when(jnp.logical_not(is_last))
    def _():
        pl.semaphore_signal(barrier, inc=1, device_id={"pipe": up}, device_id_type=MESH)

    pl.semaphore_wait(barrier, jnp.where(is_first | is_last, 1, 2))
    vec[...] = jnp.zeros_like(vec)
    rows_n, seq = token_ids.shape
    for index, member in enumerate((token_ids, segment_ids, target_ids)):
        ids[index] = jnp.full(ids.shape[1:], 4.0 if index == 1 else -1.0, F32)
        ids[index, 0:rows_n, 0:seq] = member[...].astype(F32)
    at_query = lax.broadcasted_iota(jnp.int32, (ROW, ROW), 1)
    at_key = lax.broadcasted_iota(jnp.int32, (ROW, ROW), 0)
    frames[...] = jnp.where(at_key < ((at_query * 43) // 256) * FRAME + FRAME, 1.0, 0.0)

    def column(index, row):
        values = jnp.broadcast_to(ids[index, pl.ds(row, 1), :], (8, ROW))
        return values.T[:, 0:1]

    def hot_rows(index, m):
        parts = [column(index, m * GROUP + r) for r in range(GROUP)]
        values = jnp.concatenate(parts, axis=0)
        places = lax.broadcasted_iota(jnp.int32, (tokens, vocab), 1).astype(F32)
        return values, jnp.where(values == places, 1.0, 0.0)

    def forward_copy(m):
        return pltpu.make_async_remote_copy(
            src_ref=outb.at[m],
            dst_ref=instream.at[m],
            send_sem=fsend.at[m],
            recv_sem=frecv.at[m],
            device_id={"pipe": up},
            device_id_type=MESH,
        )

    def backward_copy(m):
        return pltpu.make_async_remote_copy(
            src_ref=gs.at[m],
            dst_ref=gin.at[m],
            send_sem=bsend.at[m],
            recv_sem=brecv.at[m],
            device_id={"pipe": down},
            device_id_type=MESH,
        )

    def save(index, src, dst, m):
        return pltpu.make_async_copy(src, dst.at[m], osem.at[index, m])

    def saves_forward(m):
        return [
            save(0, normed.at[m], normed_o, m),
            save(1, mixed.at[m], mixed_o, m),
            save(2, normed2.at[m], normed2_o, m),
            save(3, active.at[m], active_o, m),
        ]

    def saves_backward(m):
        slot = lax.rem(m, 2)
        return [
            save(4, s_gres.at[slot], gres_o, m),
            save(5, s_ghid.at[slot], ghid_o, m),
            save(6, s_gbr.at[slot], gbr_o, m),
            save(7, s_gproj.at[slot], gproj_o, m),
        ]

    def save_xl(m):
        return save(8, s_xl.at[lax.rem(m, 2)], xl_o, m)

    def put_xl(m, value):
        @pl.when(m >= 2)
        def _():
            save_xl(m - 2).wait()

        s_xl[lax.rem(m, 2)] = value
        save_xl(m).start()

    lane_low = lax.broadcasted_iota(jnp.int32, (ROW, ROW), 1) < ROW // 2

    def forward(m):
        @pl.when(is_first)
        def _():
            hot = hot_rows(0, m)[1].astype(BF16)
            instream[m] = dot(hot, embed[...]).astype(BF16)

        @pl.when(jnp.logical_not(is_first))
        def _():
            forward_copy(m).wait_recv()

        normal, _ = normalise(instream[m].astype(F32))
        normed[m] = (normal * gains[0:1, :] + shifts[0:1, :]).astype(BF16)
        low = normed[m]
        queries = dot(low, qkv_w[:, 0:width]) + qv_b[0:1, :]
        proj[m, :, 0:width] = (queries * (ROW // 2) ** -0.5).astype(BF16)
        proj[m, :, width : 2 * width] = dot(low, qkv_w[:, width : 2 * width]).astype(BF16)
        proj[m, :, 2 * width : 3 * width] = (
            dot(low, qkv_w[:, 2 * width : 3 * width]) + qv_b[1:2, :]
        ).astype(BF16)
        masks, scores = [], []
        for r in range(GROUP):
            rows = slice(r * ROW, (r + 1) * ROW)
            kinds = lax.broadcasted_iota(jnp.int32, (16, ROW), 0).astype(F32)
            member = jnp.where(ids[1, pl.ds(m * GROUP + r, 1), :] == kinds, 1.0, 0.0).astype(BF16)
            mask = jnp.where(dot_tn(member, member) * frames[...] > 0.5, 0.0, MASKED)
            masks.append(jnp.concatenate([mask, mask], axis=1))
            for p in range(pairs):
                q = stack_pair(proj[m, rows, p * ROW : (p + 1) * ROW], lane_low)
                k = proj[m, rows, width + p * ROW : width + (p + 1) * ROW]
                scores.append(dot_nt(k, q))

        def mix(unit):
            r, p = unit // pairs, unit % pairs
            rows = slice(r * ROW, (r + 1) * ROW)
            v = proj[m, rows, 2 * width + p * ROW : 2 * width + (p + 1) * ROW]
            both = dot_tn(probs[m, unit], v)
            mixed[m, rows, p * ROW : (p + 1) * ROW] = join_pair(both, lane_low).astype(BF16)

        for unit in range(GROUP * pairs):
            masked = scores[unit] + masks[unit // pairs]
            expo = jnp.exp(masked - jnp.max(masked, axis=0, keepdims=True))
            total = jnp.sum(expo, axis=0, keepdims=True)
            probs[m, unit] = (expo * (1.0 / total)).astype(BF16)
            if unit:
                mix(unit - 1)
        mix(GROUP * pairs - 1)
        mid = instream[m].astype(F32) + (dot(mixed[m], out_w[...]) + out_b[0:1, :])
        middle[m] = mid
        normal2, _ = normalise(mid)
        normed2[m] = (normal2 * gains[1:2, :] + shifts[1:2, :]).astype(BF16)
        low2 = normed2[m]
        parts = hidden_n // chunk

        def spread(c):
            return dot(low2, in_w[:, c * chunk : (c + 1) * chunk])

        total, ahead = None, spread(0)
        for c in range(parts):
            cols = slice(c * chunk, (c + 1) * chunk)
            hid = ahead + in_b[0:1, cols]
            if c + 1 < parts:
                ahead = spread(c + 1)
            square = hid * hid
            tan = jnp.tanh(hid * (GELU_A + (GELU_A * GELU_B) * square))
            half = 0.5 + 0.5 * tan
            act = (hid * half).astype(BF16)
            active[m, :, cols] = act
            rise = (1.0 - tan * tan) * (0.5 * GELU_A + (1.5 * GELU_A * GELU_B) * square)
            slope[m, :, cols] = (half + hid * rise).astype(BF16)
            term = dot(act, down_w[cols, :])
            total = term if total is None else total + term
        for copy in saves_forward(m):
            copy.start()
        lo[...] = middle[m] + (total + out_b[1:2, :])

        @pl.when(jnp.logical_not(is_last))
        def _():
            outb[m] = lo[...].astype(BF16)
            forward_copy(m).start()

    def head(m):
        normal, scale = normalise(lo[...])
        outb[m] = (normal * fin_gain[...] + fin_bias[...]).astype(BF16)
        save(9, outb.at[m], xr_o, m).start()
        logits = dot_nt(outb[m], head_w[...])
        top = jnp.max(logits, axis=-1, keepdims=True)
        expo = jnp.exp(logits - top)
        total = jnp.sum(expo, axis=-1, keepdims=True)
        target, hot = hot_rows(2, m)
        grad_logits = jnp.where(target >= 0.0, expo * (1.0 / total) - hot, 0.0).astype(BF16)
        put_xl(m, grad_logits)
        grad_final = dot(grad_logits, head_w[...])
        vec[V_FINAL_GAIN : V_FINAL_GAIN + 1, :] += column_sum(grad_final * normal)
        vec[V_FINAL_BIAS : V_FINAL_BIAS + 1, :] += column_sum(grad_final)
        go[...] = norm_backward(grad_final, normal, scale, fin_gain[...])

    def backward(m):
        slot = lax.rem(m, 2)

        @pl.when(m >= 2)
        def _():
            for copy in saves_backward(m - 2):
                copy.wait()

        @pl.when(jnp.logical_not(is_last))
        def _():
            backward_copy(m).wait_recv()
            go[...] = gin[m].astype(F32)

        s_gres[slot] = go[...].astype(BF16)
        gres = s_gres[slot]
        parts = hidden_n // chunk

        def spread(c):
            return dot_nt(gres, down_w[c * chunk : (c + 1) * chunk, :])

        total, ahead = None, spread(0)
        for c in range(parts):
            cols = slice(c * chunk, (c + 1) * chunk)
            gact = ahead
            if c + 1 < parts:
                ahead = spread(c + 1)
            ghid = (gact * slope[m, :, cols].astype(F32)).astype(BF16)
            s_ghid[slot, :, cols] = ghid
            term = dot_nt(ghid, in_w[:, cols])
            total = term if total is None else total + term
        normal2, scale2 = normalise(middle[m])
        vec[V_GAIN2 : V_GAIN2 + 1, :] += column_sum(total * normal2)
        vec[V_SHIFT2 : V_SHIFT2 + 1, :] += column_sum(total)
        gmid[...] = go[...] + norm_backward(total, normal2, scale2, gains[1:2, :])
        s_gbr[slot] = gmid[...].astype(BF16)
        gbr = s_gbr[slot]
        gmix = dot_nt(gbr, out_w[...]).astype(BF16)
        grads = []
        for r in range(GROUP):
            rows = slice(r * ROW, (r + 1) * ROW)
            for p in range(pairs):
                gm = stack_pair(gmix[rows, p * ROW : (p + 1) * ROW], lane_low)
                vlanes = slice(2 * width + p * ROW, 2 * width + (p + 1) * ROW)
                grads.append(dot_nt(proj[m, rows, vlanes], gm))
                s_gproj[slot, rows, vlanes] = dot(probs[m, r * pairs + p], gm).astype(BF16)

        def pull(unit, gsc):
            r, p = unit // pairs, unit % pairs
            rows = slice(r * ROW, (r + 1) * ROW)
            lanes = slice(p * ROW, (p + 1) * ROW)
            klanes = slice(width + p * ROW, width + (p + 1) * ROW)
            q = stack_pair(proj[m, rows, lanes], lane_low)
            s_gproj[slot, rows, klanes] = dot(gsc, q).astype(BF16)
            gq = join_pair(dot_tn(gsc, proj[m, rows, klanes]), lane_low) * (ROW // 2) ** -0.5
            s_gproj[slot, rows, lanes] = gq.astype(BF16)

        waiting = None
        for unit in range(GROUP * pairs):
            weights = probs[m, unit].astype(F32)
            inner = jnp.sum(weights * grads[unit], axis=0, keepdims=True)
            gsc = (weights * (grads[unit] - inner)).astype(BF16)
            if waiting is not None:
                pull(unit - 1, waiting)
            waiting = gsc
        pull(GROUP * pairs - 1, waiting)
        for copy in saves_backward(m):
            copy.start()
        gproj = s_gproj[slot]
        gnormed = dot_nt(gproj, qkv_w[...])
        normal, scale = normalise(instream[m].astype(F32))
        vec[V_GAIN1 : V_GAIN1 + 1, :] += column_sum(gnormed * normal)
        vec[V_SHIFT1 : V_SHIFT1 + 1, :] += column_sum(gnormed)
        gs[m] = (gmid[...] + norm_backward(gnormed, normal, scale, gains[0:1, :])).astype(BF16)

        @pl.when(is_first)
        def _():
            save(9, gs.at[m], xr_o, m).start()

        @pl.when(jnp.logical_not(is_first))
        def _():
            backward_copy(m).start()

    def tick(t, carry):
        m_forward = t - stage
        m_backward = t - (2 * (stages - 1) - stage)

        @pl.when((m_forward >= 0) & (m_forward < micros))
        def _():
            forward(m_forward)

        @pl.when((m_backward >= 0) & (m_backward < micros))
        def _():
            @pl.when(is_last)
            def _():
                head(m_backward)

            backward(m_backward)

        return carry

    lax.fori_loop(0, micros + 2 * (stages - 1), tick, 0)

    for m in range(micros):
        for copy in saves_forward(m):
            copy.wait()

        @pl.when(jnp.logical_not(is_last))
        def _():
            forward_copy(m).wait_send()

        @pl.when(jnp.logical_not(is_first))
        def _():
            backward_copy(m).wait_send()

        @pl.when(is_first)
        def _():
            save(9, gs.at[m], xr_o, m).wait()

        @pl.when(is_last)
        def _():
            save(9, outb.at[m], xr_o, m).wait()

    for m in range(max(0, micros - 2), micros):
        for copy in saves_backward(m):
            copy.wait()

        @pl.when(is_last)
        def _():
            save_xl(m).wait()


def run_pipeline(stages, token_ids, segment_ids, target_ids, params):
    embed, in_w, head_w = params[0], params[5], params[12]
    width = embed.shape[1]
    vocab = head_w.shape[0]
    hid = in_w.shape[1]
    tokens = GROUP * ROW
    micros = token_ids.shape[0] // GROUP
    pairs = width // ROW
    vmem = pl.BlockSpec(memory_space=pltpu.VMEM)
    hbm = pl.BlockSpec(memory_space=pl.ANY)

    def kept(columns):
        return jax.ShapeDtypeStruct((micros, tokens, columns), BF16)

    def scratch(lead, columns, kind=BF16):
        return pltpu.VMEM((lead, tokens, columns), kind)

    out_shape = [
        kept(width),
        kept(width),
        kept(width),
        kept(hid),
        kept(width),
        kept(hid),
        kept(width),
        kept(3 * width),
        kept(vocab),
        kept(width),
        jax.ShapeDtypeStruct((VEC_ROWS, width), F32),
    ]
    return pl.pallas_call(
        functools.partial(pipeline_kernel, stages, micros),
        out_shape=out_shape,
        in_specs=[vmem] * 16,
        out_specs=[hbm] * 10 + [vmem],
        scratch_shapes=[
            scratch(micros, width),
            scratch(micros, width),
            scratch(micros, width),
            scratch(micros, width),
            scratch(micros, width),
            scratch(micros, 3 * width),
            pltpu.VMEM((micros, GROUP * pairs, ROW, 2 * ROW), BF16),
            scratch(micros, width),
            scratch(micros, width, F32),
            scratch(micros, width),
            scratch(micros, hid),
            scratch(micros, hid),
            pltpu.VMEM((tokens, width), F32),
            pltpu.VMEM((tokens, width), F32),
            pltpu.VMEM((tokens, width), F32),
            scratch(2, width),
            scratch(2, hid),
            scratch(2, width),
            scratch(2, 3 * width),
            scratch(2, vocab),
            pltpu.VMEM((3, 16, ROW), F32),
            pltpu.VMEM((ROW, ROW), F32),
            pltpu.SemaphoreType.DMA((micros,)),
            pltpu.SemaphoreType.DMA((micros,)),
            pltpu.SemaphoreType.DMA((micros,)),
            pltpu.SemaphoreType.DMA((micros,)),
            pltpu.SemaphoreType.DMA((10, micros)),
        ],
        compiler_params=pltpu.CompilerParams(
            collective_id=0, has_side_effects=True, vmem_limit_bytes=62 * 1024 * 1024
        ),
        name="pipeline",
    )(token_ids, segment_ids, target_ids, *params)


def line_dims(devices):
    dims, stride = [], 1
    if devices == 8:
        return [(2, 1), (4, 2)]
    while devices > 1:
        size = 4 if devices % 4 == 0 else 2
        dims.append((size, stride))
        stride *= size
        devices //= size
    return dims


def chunk_plan(width, hid, vocab, stages, devices):
    slim, deep = width // devices, hid // devices
    plan = [("out", 0, (slim, width), False)]
    for c in range(4):
        plan.append(("down", c, (deep, width // 4), c in (1, 3)))
    for c in range(2):
        plan.append(("extra", c, (stages, vocab // (stages * devices), width // 2), False))
    for c in range(hid // width):
        plan.append(("in", c, (slim, width), c == 1))
    for c in range(3):
        plan.append(("qkv", c, (slim, width), False))
    return plan


def gradient_kernel(stages, devices, plan, *refs):
    dims = line_dims(devices)
    refs = list(refs)

    def take(amount):
        head, refs[:] = refs[:amount], refs[amount:]
        return head

    inputs = take(10)
    vec_in, token_ids = take(2)
    qkv_out, out_out, in_out, down_out, embed_out, head_out, vec_out = take(7)
    local = take(10)
    in_sem = take(1)[0]
    turned_left, turned_xl = take(2)
    mats = dict(
        zip(
            ("normed", "mixed", "normed2", "active", "gres", "ghid", "gbr", "gproj", "xl", "xr"),
            local,
        )
    )
    names = list(mats)
    stage = lax.axis_index("pipe")
    place = lax.axis_index("dp")
    is_extra = (stage == 0) | (stage == stages - 1)
    width = mats["normed"].shape[1]
    where = [lax.rem(place // stride, size) for size, stride in dims]

    barrier = pltpu.get_barrier_semaphore()

    def greet(offset, carry):
        peer = lax.rem(place + offset, devices)
        pl.semaphore_signal(barrier, inc=1, device_id={"dp": peer}, device_id_type=MESH)
        return carry

    def greet_stage(offset, carry):
        peer = lax.rem(stage + offset, stages)
        pl.semaphore_signal(barrier, inc=1, device_id={"pipe": peer}, device_id_type=MESH)
        return carry

    lax.fori_loop(1, devices, greet, 0)
    lax.fori_loop(1, stages, greet_stage, 0)

    def load(name):
        i = names.index(name)
        return pltpu.make_async_copy(inputs[i], mats[name], in_sem.at[i])

    groups = [("mixed", "gbr"), ("gres", "active"), ("xr", "xl"), ("normed2", "ghid"), ("normed", "gproj")]

    def fetch(at):
        if at >= len(groups):
            return
        if groups[at] == ("xr", "xl"):
            @pl.when(is_extra)
            def _():
                load("xr").start()

            @pl.when(stage == stages - 1)
            def _():
                load("xl").start()

            at += 1
        for name in groups[at]:
            load(name).start()

    fetch(0)
    loaded = set()

    def need(*wanted):
        fresh = [name for name in wanted if name not in loaded]
        for name in fresh:
            loaded.add(name)
            load(name).wait()
        if fresh:
            at = [i for i, group in enumerate(groups) if group[0] == fresh[0]][0]
            fetch(at + 1)

    def identity(size):
        here = lax.broadcasted_iota(jnp.int32, (size, size), 0)
        there = lax.broadcasted_iota(jnp.int32, (size, size), 1)
        return jnp.where(here == there, 1.0, 0.0).astype(BF16)

    held = []

    def turn(name):
        if held[-1:] == [name]:
            return
        held.append(name)
        unit = identity(256)
        for q in range(width // 256):
            part = dot_nt(unit, mats[name][:, q * 256 : (q + 1) * 256])
            turned_left[q * 256 : (q + 1) * 256, :] = part.astype(BF16)

    bits = devices.bit_length() - 1
    vec_send, vec_recv = take(2)
    vec_sems = take(2)

    def vec_copy(k):
        peer = jnp.bitwise_xor(place, 1 << k)
        return pltpu.make_async_remote_copy(
            src_ref=vec_send.at[k],
            dst_ref=vec_recv.at[k],
            send_sem=vec_sems[0].at[k],
            recv_sem=vec_sems[1].at[k],
            device_id={"dp": peer},
            device_id_type=MESH,
        )

    def vec_step(k):
        def run():
            if k == 0:
                vec_send[0] = vec_in[...]
                ones = jnp.ones((16, mats["gres"].shape[0]), BF16)
                for name, start, row in (
                    ("gproj", 0, V_QUERY),
                    ("gproj", 2 * width, V_VALUE),
                    ("gbr", 0, V_BRANCH),
                    ("gres", 0, V_RESULT),
                ):
                    part = dot(ones, mats[name][:, start : start + width])
                    vec_send[0, row : row + 1, :] = part[0:1, :]
                for q in range(mats["ghid"].shape[1] // width):
                    part = dot(ones, mats["ghid"][:, q * width : (q + 1) * width])
                    vec_send[0, V_HIDDEN + q : V_HIDDEN + q + 1, :] = part[0:1, :]
            else:
                vec_copy(k - 1).wait_recv()
                vec_send[k] = vec_send[k - 1] + vec_recv[k - 1]
            if k < bits:
                vec_copy(k).start()

        return run

    final_send, final_recv = take(2)
    final_sems = take(2)

    def final_copy(offset):
        peer = lax.rem(stages - 1 + offset, stages)
        return pltpu.make_async_remote_copy(
            src_ref=final_send,
            dst_ref=final_recv,
            send_sem=final_sems[0].at[offset],
            recv_sem=final_sems[1].at[0],
            device_id={"pipe": peer},
            device_id_type=MESH,
        )

    def vec_last():
        vec_step(bits)()
        vec_out[...] = vec_send[bits]

        @pl.when(stage == stages - 1)
        def _():
            final_send[...] = vec_send[bits, 8:16, :]
            for offset in range(1, stages):
                final_copy(offset).start()

    def vec_finish():
        @pl.when(stage != stages - 1)
        def _():
            final_copy(1).wait_recv()
            vec_out[V_FINAL_GAIN : V_FINAL_BIAS + 1, :] = final_recv[
                V_FINAL_GAIN - 8 : V_FINAL_BIAS - 7, :
            ]

    def vec_drain():
        for k in range(bits):
            vec_copy(k).wait_send()

        @pl.when(stage == stages - 1)
        def _():
            for offset in range(1, stages):
                final_copy(offset).wait_send()

    extra_sum, extra_send_sem, extra_recv_sem = take(3)

    def extra_copy(source, offset, target):
        peer = lax.rem(source + offset, stages)
        return pltpu.make_async_remote_copy(
            src_ref=extra_sum.at[peer],
            dst_ref=target,
            send_sem=extra_send_sem.at[offset],
            recv_sem=extra_recv_sem.at[0 if source == 0 else 1],
            device_id={"pipe": peer},
            device_id_type=MESH,
        )

    down_full = {}

    def chunk_steps(kind, c, block, turned):
        order = list(range(len(dims)))
        if turned:
            order.reverse()
        full = take(1)[0]

        def compute():
            if kind == "down":
                need("gres", "active")
                turn("gres")
                if c % 2 == 1:
                    return
                half = width // 2
                lines = slice((c // 2) * half, (c // 2 + 1) * half)
                parts = dot(turned_left[lines, :], mats["active"][...]).astype(BF16)
                depth = block[0]
                unit = identity(depth)
                for d in range(devices):
                    back = dot_nt(unit, parts[:, d * depth : (d + 1) * depth]).astype(BF16)
                    down_full[c][split(d)] = back[:, 0 : half // 2]
                    down_full[c + 1][split(d)] = back[:, half // 2 : half]
            elif kind == "extra":
                vocab = turned_xl.shape[0]
                if c == 0:
                    load("xr").wait()

                @pl.when((stage == 0) & (c == 0))
                def _():
                    rows_n, seq = token_ids.shape
                    places = lax.broadcasted_iota(jnp.int32, (vocab, ROW), 0)
                    gap = jnp.full((1, ROW - seq), -1, jnp.int32)
                    for r in range(rows_n):
                        row = jnp.concatenate([token_ids[r : r + 1, :], gap], axis=1)
                        hot = jnp.where(places == row, 1.0, 0.0)
                        turned_xl[:, r * ROW : (r + 1) * ROW] = hot.astype(BF16)

                @pl.when((stage == stages - 1) & (c == 0))
                def _():
                    load("xl").wait()
                    unit = identity(256)
                    for q in range(vocab // 256):
                        part = dot_nt(unit, mats["xl"][:, q * 256 : (q + 1) * 256])
                        turned_xl[q * 256 : (q + 1) * 256, :] = part.astype(BF16)

                rows = vocab // stages
                for p in range(stages):
                    part = dot(
                        turned_xl[p * rows : (p + 1) * rows, :],
                        mats["xr"][:, c * (width // 2) : (c + 1) * (width // 2)],
                    )
                    part = part.astype(BF16).reshape((devices,) + block[1:])
                    for d in range(devices):
                        full[split(d) + (p,)] = part[d]
            else:
                left, right = {
                    "in": ("normed2", "ghid"),
                    "out": ("mixed", "gbr"),
                    "qkv": ("normed", "gproj"),
                }[kind]
                need(left, right)
                turn(left)
                cols = slice(c * width, (c + 1) * width)
                part = dot(turned_left[...], mats[right][:, cols]).astype(BF16)
                part = part.reshape((devices,) + block)
                for d in range(devices):
                    full[split(d)] = part[d]

        def split(d):
            return tuple((d // stride) % size for size, stride in reversed(dims))

        if kind == "down":
            down_full[c] = full
        steps = [[compute]]
        for at, phase in enumerate(order):
            size = dims[phase][0]
            buffers = take(3)
            done = order[:at]
            last = at == len(order) - 1
            steps[-1].append(functools.partial(line_step, phase, size, 1, full, buffers, done))
            for t in range(2, size):
                steps.append([functools.partial(line_step, phase, size, t, full, buffers, done)])
            drains.append((kind, functools.partial(line_drain, phase, size, full, buffers, done)))
            steps.append([functools.partial(line_final, kind, c, phase, size, full, buffers, done, last)])
        if kind == "extra":
            steps = [[gated([part]) for part in step] for step in steps]
        return steps

    def gated(step):
        def run():
            @pl.when(is_extra)
            def _():
                for part in step:
                    part()

        return run

    def block_of(full, phase, j, done):
        spot = [slice(None)] * len(dims)
        for other in done:
            spot[len(dims) - 1 - other] = where[other]
        spot[len(dims) - 1 - phase] = j
        return full.at[tuple(spot)]

    def line_copy(phase, size, t, side, full, buffers, done):
        recv, ssem, rsem = buffers
        i = where[phase]
        stride = dims[phase][1]
        if side == 0:
            j, peer = size - t + i, place + jnp.where(i < size - 1, stride, 0)
        else:
            j, peer = t - size + i, place - jnp.where(i > 0, stride, 0)
        return pltpu.make_async_remote_copy(
            src_ref=block_of(full, phase, jnp.clip(j, 0, size - 1), done),
            dst_ref=recv.at[0 if size == 2 else side, t - 1],
            send_sem=ssem.at[side, t - 1],
            recv_sem=rsem.at[side, t - 1],
            device_id={"dp": peer},
            device_id_type=MESH,
        )

    def sends(i, size, t, side):
        return (i <= t - 1) if side == 0 else (i >= size - t)

    def line_step(phase, size, t, full, buffers, done):
        i = where[phase]
        for side in range(2):
            at_end = (i == 0) if side == 0 else (i == size - 1)
            j = size - t + i if side == 0 else t - size + i
            j = jnp.clip(j, 0, size - 1)

            @pl.when(sends(i, size, t, side))
            def _():
                if t > 1:
                    @pl.when(jnp.logical_not(at_end))
                    def _():
                        line_copy(phase, size, t - 1, side, full, buffers, done).wait_recv()
                        own = block_of(full, phase, j, done)
                        got = buffers[0][0 if size == 2 else side, t - 2]
                        own[...] = (own[...].astype(F32) + got.astype(F32)).astype(BF16)

                line_copy(phase, size, t, side, full, buffers, done).start()

    def line_final(kind, c, phase, size, full, buffers, done, last):
        i = where[phase]
        own = block_of(full, phase, i, done)
        total = own
        if last:
            slots = {
                "qkv": lambda: qkv_out.at[:, c * width : (c + 1) * width],
                "in": lambda: in_out.at[:, c * width : (c + 1) * width],
                "out": lambda: out_out,
                "down": lambda: down_out.at[:, c * (width // 4) : (c + 1) * (width // 4)],
                "extra": lambda: extra_sum.at[:, :, c * (width // 2) : (c + 1) * (width // 2)],
            }
            total = slots[kind]()
        lower, upper = i > 0, i < size - 1

        def arrived(side):
            line_copy(phase, size, size - 1, side, full, buffers, done).wait_recv()
            return buffers[0][0 if size == 2 else side, size - 2].astype(F32)

        @pl.when(lower & upper)
        def _():
            total[...] = (own[...].astype(F32) + arrived(0) + arrived(1)).astype(total.dtype)

        @pl.when(lower & jnp.logical_not(upper))
        def _():
            total[...] = (own[...].astype(F32) + arrived(0)).astype(total.dtype)

        @pl.when(jnp.logical_not(lower))
        def _():
            total[...] = (own[...].astype(F32) + arrived(1)).astype(total.dtype)

        if last and kind == "extra" and c == 1:
            for source_stage, out in ((0, embed_out), (stages - 1, head_out)):
                @pl.when(stage == source_stage)
                def _():
                    for offset in range(1, stages):
                        extra_copy(source_stage, offset, extra_recv[0 if source_stage == 0 else 1]).start()
                    out[...] = extra_sum[source_stage]

    def line_drain(phase, size, full, buffers, done):
        i = where[phase]
        for side in range(2):
            for t in range(1, size):
                @pl.when(sends(i, size, t, side))
                def _():
                    line_copy(phase, size, t, side, full, buffers, done).wait_send()

    extra_recv = take(2)
    drains = []
    chains = [chunk_steps(*item) for item in plan]
    depth = len(chains[0])
    vec_chain = [vec_step(k) for k in range(bits)] + [vec_last]
    starts, first, extra_rounds = [], 0, iter((1, 3, 6, 8))
    for item in plan:
        if item[3]:
            starts.append(next(extra_rounds))
        else:
            starts.append(first)
            first += 1
    begun = False
    loaded_at = max(start for start, item in zip(starts, plan) if item[0] == "qkv" and item[1] == 0)
    for r in range(max(starts) + depth):
        for d in [0] + list(range(depth - 1, 0, -1)):
            for start, chain in zip(starts, chains):
                if r - start != d:
                    continue
                for part in chain[d]:
                    part()
                    if not begun:
                        begun = True
                        pl.semaphore_wait(barrier, devices - 1 + stages - 1)
        if 0 <= r - loaded_at < len(vec_chain):
            vec_chain[r - loaded_at]()
    vec_finish()
    for source_stage, out in ((0, embed_out), (stages - 1, head_out)):
        @pl.when(stage != source_stage)
        def _():
            got = extra_recv[0 if source_stage == 0 else 1]
            extra_copy(source_stage, 1, got).wait_recv()
            out[...] = got[...]

        @pl.when(stage == source_stage)
        def _():
            for offset in range(1, stages):
                extra_copy(source_stage, offset, extra_recv[0]).wait_send()

    vec_drain()
    for kind, drain in drains:
        if kind == "extra":
            gated([drain])()
        else:
            drain()


def run_gradients(stages, devices, saved, vec, token_ids):
    dims = line_dims(devices)
    rows, tokens, width = saved[0].shape
    hid, vocab = saved[3].shape[2], saved[8].shape[2]
    plan = chunk_plan(width, hid, vocab, stages, devices)
    saved = [member.reshape(rows * tokens, member.shape[2]) for member in saved]
    vmem = pl.BlockSpec(memory_space=pltpu.VMEM)
    hbm = pl.BlockSpec(memory_space=pl.ANY)
    bits = devices.bit_length() - 1
    share = vocab // (stages * devices)
    scratch = [pltpu.VMEM(member.shape, BF16) for member in saved]
    scratch += [pltpu.SemaphoreType.DMA((len(saved),))]
    scratch += [pltpu.VMEM((width, rows * tokens), BF16), pltpu.VMEM((vocab, rows * tokens), BF16)]
    scratch += [
        pltpu.VMEM((bits + 1,) + vec.shape, F32),
        pltpu.VMEM((bits,) + vec.shape, F32),
        pltpu.SemaphoreType.DMA((bits,)),
        pltpu.SemaphoreType.DMA((bits,)),
        pltpu.VMEM((8, width), F32),
        pltpu.VMEM((8, width), F32),
        pltpu.SemaphoreType.DMA((stages,)),
        pltpu.SemaphoreType.DMA((1,)),
        pltpu.VMEM((stages, share, width), F32),
        pltpu.SemaphoreType.DMA((stages,)),
        pltpu.SemaphoreType.DMA((2,)),
        pltpu.VMEM((share, width), F32),
        pltpu.VMEM((share, width), F32),
    ]
    sizes = [size for size, _ in reversed(dims)]
    for _, _, block, turned in plan:
        scratch.append(pltpu.VMEM(tuple(sizes) + block, BF16))
        remain = list(reversed(dims))
        for size, stride in dims[::-1] if turned else dims:
            remain.remove((size, stride))
            piece = tuple(other for other, _ in remain) + block
            scratch.append(pltpu.VMEM((1 if size == 2 else 2, size - 1) + piece, BF16))
            scratch += [pltpu.SemaphoreType.DMA((2, size - 1))] * 2
    return pl.pallas_call(
        functools.partial(gradient_kernel, stages, devices, plan),
        out_shape=[
            jax.ShapeDtypeStruct((width // devices, 3 * width), F32),
            jax.ShapeDtypeStruct((width // devices, width), F32),
            jax.ShapeDtypeStruct((width // devices, hid), F32),
            jax.ShapeDtypeStruct((hid // devices, width), F32),
            jax.ShapeDtypeStruct((share, width), F32),
            jax.ShapeDtypeStruct((share, width), F32),
            jax.ShapeDtypeStruct(vec.shape, F32),
        ],
        in_specs=[hbm] * len(saved) + [vmem] * 2,
        out_specs=[vmem] * 7,
        scratch_shapes=scratch,
        compiler_params=pltpu.CompilerParams(
            collective_id=1, has_side_effects=True, vmem_limit_bytes=62 * 1024 * 1024
        ),
        name="gradients",
    )(*saved, vec, token_ids)


def finish_kernel(devices, embed_g, qkv_g, out_g, in_g, down_g, head_g, vec, *outs):
    place = lax.axis_index("dp")
    width = vec.shape[1]
    (embed_o, qkv_o, qv_o, out_o, outb_o, in_o, inb_o, down_o, gain_o, shift_o, fg_o, fb_o, head_o) = outs
    embed_o[...] = embed_g[...]
    head_o[...] = head_g[...]
    for source, target in ((qkv_g, qkv_o), (out_g, out_o), (in_g, in_o), (down_g, down_o)):
        target[0] = source[...]
    lanes = width // devices
    turned = pltpu.roll(vec[0:8, :], lax.rem(width - place * lanes, width), 1)
    for row, out in ((V_QUERY, qv_o), (V_BRANCH, outb_o), (V_GAIN1, gain_o), (V_SHIFT1, shift_o)):
        out[0] = turned[row : row + 2, 0:lanes]
    share = inb_o.shape[1]
    first = place * share
    row = vec[pl.ds(V_HIDDEN + first // width, 1), :]
    wide = jnp.broadcast_to(row, (8, width))
    inb_o[...] = pltpu.roll(wide, lax.rem(width - lax.rem(first, width), width), 1)[0:1, 0:share]
    fg_o[...] = vec[V_FINAL_GAIN : V_FINAL_GAIN + 1, :]
    fb_o[...] = vec[V_FINAL_BIAS : V_FINAL_BIAS + 1, :]


def run_finish(devices, embed_g, qkv_g, out_g, in_g, down_g, head_g, vec):
    vmem = pl.BlockSpec(memory_space=pltpu.VMEM)
    width = vec.shape[1]
    lanes = width // devices

    def shape(*sizes):
        return jax.ShapeDtypeStruct(sizes, F32)

    pair = shape(1, 2, lanes)
    return pl.pallas_call(
        functools.partial(finish_kernel, devices),
        out_shape=[
            shape(*embed_g.shape),
            shape(1, *qkv_g.shape),
            pair,
            shape(1, *out_g.shape),
            pair,
            shape(1, *in_g.shape),
            shape(1, in_g.shape[1] // devices),
            shape(1, *down_g.shape),
            pair,
            pair,
            shape(1, width),
            shape(1, width),
            shape(*head_g.shape),
        ],
        in_specs=[vmem] * 7,
        out_specs=[vmem] * 13,
        name="finish",
    )(embed_g, qkv_g, out_g, in_g, down_g, head_g, vec)


def on_device(
    token_ids,
    segment_ids,
    target_ids,
    embed_table,
    qkv_weight,
    qv_bias,
    out_weight,
    out_biases,
    ff_in,
    ff_in_bias,
    ff_out,
    norm_gains,
    norm_biases,
    final_gain,
    final_bias,
    head_weight,
):
    stages = lax.axis_size("pipe")
    devices = lax.axis_size("dp")
    params = (
        embed_table,
        qkv_weight[0],
        qv_bias[0],
        out_weight[0],
        out_biases[0],
        ff_in[0],
        ff_in_bias,
        ff_out[0],
        norm_gains[0],
        norm_biases[0],
        final_gain[None],
        final_bias[None],
        head_weight,
    )
    *saved, vec = run_pipeline(stages, token_ids, segment_ids, target_ids, params)
    qkv_g, out_g, in_g, down_g, embed_g, head_g, sums = run_gradients(stages, devices, saved, vec, token_ids)
    done = list(run_finish(devices, embed_g, qkv_g, out_g, in_g, down_g, head_g, sums))
    done[10], done[11] = done[10][0], done[11][0]
    return tuple(done)


def solution(mesh):
    layer3 = P("pipe", None, None)
    return jax.shard_map(
        on_device,
        mesh=mesh,
        in_specs=(
            P("dp", None),
            P("dp", None),
            P("dp", None),
            P(),
            layer3,
            layer3,
            layer3,
            layer3,
            layer3,
            P("pipe", None),
            layer3,
            layer3,
            layer3,
            P(),
            P(),
            P(),
        ),
        out_specs=(
            P(("pipe", "dp"), None),
            P("pipe", "dp", None),
            P("pipe", None, "dp"),
            P("pipe", "dp", None),
            P("pipe", None, "dp"),
            P("pipe", "dp", None),
            P("pipe", "dp"),
            P("pipe", "dp", None),
            P("pipe", None, "dp"),
            P("pipe", None, "dp"),
            P(),
            P(),
            P(("pipe", "dp"), None),
        ),
        check_vma=False,
    )
```

```python
import functools

import jax
import jax.numpy as jnp
from jax import lax
from jax.experimental import pallas as pl
from jax.experimental.pallas import tpu as pltpu
from jax.sharding import PartitionSpec as P

HEADS = 8
FRAME = 6
ROW = 128
GROUP = 2
MASKED = -1e30
GELU_A = 0.7978845608
GELU_B = 0.044715
MESH = pl.DeviceIdType.MESH
F32 = jnp.float32
BF16 = jnp.bfloat16

VEC_ROWS = 16
V_QUERY, V_VALUE, V_BRANCH, V_RESULT, V_GAIN1, V_GAIN2, V_SHIFT1, V_SHIFT2 = range(8)
V_HIDDEN = 8
V_FINAL_GAIN, V_FINAL_BIAS = 12, 13


def dot(a, b):
    return lax.dot_general(a, b, (((1,), (0,)), ((), ())), preferred_element_type=F32)


def dot_nt(a, b):
    return lax.dot_general(a, b, (((1,), (1,)), ((), ())), preferred_element_type=F32)


def dot_tn(a, b):
    return lax.dot_general(a, b, (((0,), (0,)), ((), ())), preferred_element_type=F32)


def normalise(values):
    centre = jnp.mean(values, axis=-1, keepdims=True)
    centered = values - centre
    spread = jnp.mean(centered * centered, axis=-1, keepdims=True)
    scale = lax.rsqrt(spread + 1e-05)
    return centered * scale, scale


def norm_backward(grad, normal, scale, gain):
    grad_n = grad * gain
    mean_grad = jnp.mean(grad_n, axis=-1, keepdims=True)
    mean_proj = jnp.mean(grad_n * normal, axis=-1, keepdims=True)
    return scale * (grad_n - mean_grad - normal * mean_proj)


def column_sum(values):
    return jnp.sum(values, axis=0, keepdims=True)


def stack_pair(pair, low_lanes):
    zero = jnp.zeros_like(pair)
    return jnp.concatenate(
        [jnp.where(low_lanes, pair, zero), jnp.where(low_lanes, zero, pair)], axis=0
    )


def join_pair(stacked, low_lanes):
    half = stacked.shape[0] // 2
    return jnp.where(low_lanes, stacked[:half], stacked[half:])


def pipeline_kernel(
    stages,
    micros,
    token_ids,
    segment_ids,
    target_ids,
    embed,
    qkv_w,
    qv_b,
    out_w,
    out_b,
    in_w,
    in_b,
    down_w,
    gains,
    shifts,
    fin_gain,
    fin_bias,
    head_w,
    normed_o,
    mixed_o,
    normed2_o,
    active_o,
    gres_o,
    ghid_o,
    gbr_o,
    gproj_o,
    xl_o,
    xr_o,
    vec,
    instream,
    outb,
    gin,
    gs,
    normed,
    proj,
    probs,
    mixed,
    middle,
    normed2,
    active,
    slope,
    lo,
    go,
    gmid,
    s_gres,
    s_ghid,
    s_gbr,
    s_gproj,
    s_xl,
    ids,
    frames,
    fsend,
    frecv,
    bsend,
    brecv,
    osem,
):
    stage = lax.axis_index("pipe")
    tokens, width = instream.shape[1], instream.shape[2]
    hidden_n = in_b.shape[1]
    vocab = head_w.shape[0]
    pairs = width // ROW
    chunk = 512
    is_first = stage == 0
    is_last = stage == stages - 1
    up = jnp.minimum(stage + 1, stages - 1)
    down = jnp.maximum(stage - 1, 0)

    barrier = pltpu.get_barrier_semaphore()

    @pl.when(jnp.logical_not(is_first))
    def _():
        pl.semaphore_signal(barrier, inc=1, device_id={"pipe": down}, device_id_type=MESH)

    @pl.when(jnp.logical_not(is_last))
    def _():
        pl.semaphore_signal(barrier, inc=1, device_id={"pipe": up}, device_id_type=MESH)

    pl.semaphore_wait(barrier, jnp.where(is_first | is_last, 1, 2))
    vec[...] = jnp.zeros_like(vec)
    rows_n, seq = token_ids.shape
    for index, member in enumerate((token_ids, segment_ids, target_ids)):
        ids[index] = jnp.full(ids.shape[1:], 4.0 if index == 1 else -1.0, F32)
        ids[index, 0:rows_n, 0:seq] = member[...].astype(F32)
    at_query = lax.broadcasted_iota(jnp.int32, (ROW, ROW), 1)
    at_key = lax.broadcasted_iota(jnp.int32, (ROW, ROW), 0)
    frames[...] = jnp.where(at_key < ((at_query * 43) // 256) * FRAME + FRAME, 1.0, 0.0)

    def column(index, row):
        values = jnp.broadcast_to(ids[index, pl.ds(row, 1), :], (8, ROW))
        return values.T[:, 0:1]

    def hot_rows(index, m):
        parts = [column(index, m * GROUP + r) for r in range(GROUP)]
        values = jnp.concatenate(parts, axis=0)
        places = lax.broadcasted_iota(jnp.int32, (tokens, vocab), 1).astype(F32)
        return values, jnp.where(values == places, 1.0, 0.0)

    def forward_copy(m):
        return pltpu.make_async_remote_copy(
            src_ref=outb.at[m],
            dst_ref=instream.at[m],
            send_sem=fsend.at[m],
            recv_sem=frecv.at[m],
            device_id={"pipe": up},
            device_id_type=MESH,
        )

    def backward_copy(m):
        return pltpu.make_async_remote_copy(
            src_ref=gs.at[m],
            dst_ref=gin.at[m],
            send_sem=bsend.at[m],
            recv_sem=brecv.at[m],
            device_id={"pipe": down},
            device_id_type=MESH,
        )

    def save(index, src, dst, m):
        return pltpu.make_async_copy(src, dst.at[m], osem.at[index, m])

    def saves_forward(m):
        return [
            save(0, normed.at[m], normed_o, m),
            save(1, mixed.at[m], mixed_o, m),
            save(2, normed2.at[m], normed2_o, m),
            save(3, active.at[m], active_o, m),
        ]

    def saves_backward(m):
        slot = lax.rem(m, 2)
        return [
            save(4, s_gres.at[slot], gres_o, m),
            save(5, s_ghid.at[slot], ghid_o, m),
            save(6, s_gbr.at[slot], gbr_o, m),
            save(7, s_gproj.at[slot], gproj_o, m),
        ]

    def save_xl(m):
        return save(8, s_xl.at[lax.rem(m, 2)], xl_o, m)

    def put_xl(m, value):
        @pl.when(m >= 2)
        def _():
            save_xl(m - 2).wait()

        s_xl[lax.rem(m, 2)] = value
        save_xl(m).start()

    lane_low = lax.broadcasted_iota(jnp.int32, (ROW, ROW), 1) < ROW // 2

    def forward(m):
        @pl.when(is_first)
        def _():
            hot = hot_rows(0, m)[1].astype(BF16)
            instream[m] = dot(hot, embed[...]).astype(BF16)

        @pl.when(jnp.logical_not(is_first))
        def _():
            forward_copy(m).wait_recv()

        normal, _ = normalise(instream[m].astype(F32))
        normed[m] = (normal * gains[0:1, :] + shifts[0:1, :]).astype(BF16)
        low = normed[m]
        queries = dot(low, qkv_w[:, 0:width]) + qv_b[0:1, :]
        proj[m, :, 0:width] = (queries * (ROW // 2) ** -0.5).astype(BF16)
        proj[m, :, width : 2 * width] = dot(low, qkv_w[:, width : 2 * width]).astype(BF16)
        proj[m, :, 2 * width : 3 * width] = (
            dot(low, qkv_w[:, 2 * width : 3 * width]) + qv_b[1:2, :]
        ).astype(BF16)
        masks, scores = [], []
        for r in range(GROUP):
            rows = slice(r * ROW, (r + 1) * ROW)
            kinds = lax.broadcasted_iota(jnp.int32, (16, ROW), 0).astype(F32)
            member = jnp.where(ids[1, pl.ds(m * GROUP + r, 1), :] == kinds, 1.0, 0.0).astype(BF16)
            mask = jnp.where(dot_tn(member, member) * frames[...] > 0.5, 0.0, MASKED)
            masks.append(jnp.concatenate([mask, mask], axis=1))
            for p in range(pairs):
                q = stack_pair(proj[m, rows, p * ROW : (p + 1) * ROW], lane_low)
                k = proj[m, rows, width + p * ROW : width + (p + 1) * ROW]
                scores.append(dot_nt(k, q))

        def mix(unit):
            r, p = unit // pairs, unit % pairs
            rows = slice(r * ROW, (r + 1) * ROW)
            v = proj[m, rows, 2 * width + p * ROW : 2 * width + (p + 1) * ROW]
            both = dot_tn(probs[m, unit], v)
            mixed[m, rows, p * ROW : (p + 1) * ROW] = join_pair(both, lane_low).astype(BF16)

        for unit in range(GROUP * pairs):
            masked = scores[unit] + masks[unit // pairs]
            expo = jnp.exp(masked - jnp.max(masked, axis=0, keepdims=True))
            total = jnp.sum(expo, axis=0, keepdims=True)
            probs[m, unit] = (expo * (1.0 / total)).astype(BF16)
            if unit:
                mix(unit - 1)
        mix(GROUP * pairs - 1)
        mid = instream[m].astype(F32) + (dot(mixed[m], out_w[...]) + out_b[0:1, :])
        middle[m] = mid
        normal2, _ = normalise(mid)
        normed2[m] = (normal2 * gains[1:2, :] + shifts[1:2, :]).astype(BF16)
        low2 = normed2[m]
        parts = hidden_n // chunk

        def spread(c):
            return dot(low2, in_w[:, c * chunk : (c + 1) * chunk])

        total, ahead = None, spread(0)
        for c in range(parts):
            cols = slice(c * chunk, (c + 1) * chunk)
            hid = ahead + in_b[0:1, cols]
            if c + 1 < parts:
                ahead = spread(c + 1)
            square = hid * hid
            tan = jnp.tanh(hid * (GELU_A + (GELU_A * GELU_B) * square))
            half = 0.5 + 0.5 * tan
            act = (hid * half).astype(BF16)
            active[m, :, cols] = act
            rise = (1.0 - tan * tan) * (0.5 * GELU_A + (1.5 * GELU_A * GELU_B) * square)
            slope[m, :, cols] = (half + hid * rise).astype(BF16)
            term = dot(act, down_w[cols, :])
            total = term if total is None else total + term
        for copy in saves_forward(m):
            copy.start()
        lo[...] = middle[m] + (total + out_b[1:2, :])

        @pl.when(jnp.logical_not(is_last))
        def _():
            outb[m] = lo[...].astype(BF16)
            forward_copy(m).start()

    def head(m):
        normal, scale = normalise(lo[...])
        outb[m] = (normal * fin_gain[...] + fin_bias[...]).astype(BF16)
        save(9, outb.at[m], xr_o, m).start()
        logits = dot_nt(outb[m], head_w[...])
        top = jnp.max(logits, axis=-1, keepdims=True)
        expo = jnp.exp(logits - top)
        total = jnp.sum(expo, axis=-1, keepdims=True)
        target, hot = hot_rows(2, m)
        grad_logits = jnp.where(target >= 0.0, expo * (1.0 / total) - hot, 0.0).astype(BF16)
        put_xl(m, grad_logits)
        grad_final = dot(grad_logits, head_w[...])
        vec[V_FINAL_GAIN : V_FINAL_GAIN + 1, :] += column_sum(grad_final * normal)
        vec[V_FINAL_BIAS : V_FINAL_BIAS + 1, :] += column_sum(grad_final)
        go[...] = norm_backward(grad_final, normal, scale, fin_gain[...])

    def backward(m):
        slot = lax.rem(m, 2)

        @pl.when(m >= 2)
        def _():
            for copy in saves_backward(m - 2):
                copy.wait()

        @pl.when(jnp.logical_not(is_last))
        def _():
            backward_copy(m).wait_recv()
            go[...] = gin[m].astype(F32)

        s_gres[slot] = go[...].astype(BF16)
        gres = s_gres[slot]
        parts = hidden_n // chunk

        def spread(c):
            return dot_nt(gres, down_w[c * chunk : (c + 1) * chunk, :])

        total, ahead = None, spread(0)
        for c in range(parts):
            cols = slice(c * chunk, (c + 1) * chunk)
            gact = ahead
            if c + 1 < parts:
                ahead = spread(c + 1)
            ghid = (gact * slope[m, :, cols].astype(F32)).astype(BF16)
            s_ghid[slot, :, cols] = ghid
            term = dot_nt(ghid, in_w[:, cols])
            total = term if total is None else total + term
        normal2, scale2 = normalise(middle[m])
        vec[V_GAIN2 : V_GAIN2 + 1, :] += column_sum(total * normal2)
        vec[V_SHIFT2 : V_SHIFT2 + 1, :] += column_sum(total)
        gmid[...] = go[...] + norm_backward(total, normal2, scale2, gains[1:2, :])
        s_gbr[slot] = gmid[...].astype(BF16)
        gbr = s_gbr[slot]
        gmix = dot_nt(gbr, out_w[...]).astype(BF16)
        grads = []
        for r in range(GROUP):
            rows = slice(r * ROW, (r + 1) * ROW)
            for p in range(pairs):
                gm = stack_pair(gmix[rows, p * ROW : (p + 1) * ROW], lane_low)
                vlanes = slice(2 * width + p * ROW, 2 * width + (p + 1) * ROW)
                grads.append(dot_nt(proj[m, rows, vlanes], gm))
                s_gproj[slot, rows, vlanes] = dot(probs[m, r * pairs + p], gm).astype(BF16)

        def pull(unit, gsc):
            r, p = unit // pairs, unit % pairs
            rows = slice(r * ROW, (r + 1) * ROW)
            lanes = slice(p * ROW, (p + 1) * ROW)
            klanes = slice(width + p * ROW, width + (p + 1) * ROW)
            q = stack_pair(proj[m, rows, lanes], lane_low)
            s_gproj[slot, rows, klanes] = dot(gsc, q).astype(BF16)
            gq = join_pair(dot_tn(gsc, proj[m, rows, klanes]), lane_low) * (ROW // 2) ** -0.5
            s_gproj[slot, rows, lanes] = gq.astype(BF16)

        waiting = None
        for unit in range(GROUP * pairs):
            weights = probs[m, unit].astype(F32)
            inner = jnp.sum(weights * grads[unit], axis=0, keepdims=True)
            gsc = (weights * (grads[unit] - inner)).astype(BF16)
            if waiting is not None:
                pull(unit - 1, waiting)
            waiting = gsc
        pull(GROUP * pairs - 1, waiting)
        for copy in saves_backward(m):
            copy.start()
        gproj = s_gproj[slot]
        gnormed = dot_nt(gproj, qkv_w[...])
        normal, scale = normalise(instream[m].astype(F32))
        vec[V_GAIN1 : V_GAIN1 + 1, :] += column_sum(gnormed * normal)
        vec[V_SHIFT1 : V_SHIFT1 + 1, :] += column_sum(gnormed)
        gs[m] = (gmid[...] + norm_backward(gnormed, normal, scale, gains[0:1, :])).astype(BF16)

        @pl.when(is_first)
        def _():
            save(9, gs.at[m], xr_o, m).start()

        @pl.when(jnp.logical_not(is_first))
        def _():
            backward_copy(m).start()

    def tick(t, carry):
        m_forward = t - stage
        m_backward = t - (2 * (stages - 1) - stage)

        @pl.when((m_forward >= 0) & (m_forward < micros))
        def _():
            forward(m_forward)

        @pl.when((m_backward >= 0) & (m_backward < micros))
        def _():
            @pl.when(is_last)
            def _():
                head(m_backward)

            backward(m_backward)

        return carry

    lax.fori_loop(0, micros + 2 * (stages - 1), tick, 0)

    for m in range(micros):
        for copy in saves_forward(m):
            copy.wait()

        @pl.when(jnp.logical_not(is_last))
        def _():
            forward_copy(m).wait_send()

        @pl.when(jnp.logical_not(is_first))
        def _():
            backward_copy(m).wait_send()

        @pl.when(is_first)
        def _():
            save(9, gs.at[m], xr_o, m).wait()

        @pl.when(is_last)
        def _():
            save(9, outb.at[m], xr_o, m).wait()

    for m in range(max(0, micros - 2), micros):
        for copy in saves_backward(m):
            copy.wait()

        @pl.when(is_last)
        def _():
            save_xl(m).wait()


def run_pipeline(stages, token_ids, segment_ids, target_ids, params):
    embed, in_w, head_w = params[0], params[5], params[12]
    width = embed.shape[1]
    vocab = head_w.shape[0]
    hid = in_w.shape[1]
    tokens = GROUP * ROW
    micros = token_ids.shape[0] // GROUP
    pairs = width // ROW
    vmem = pl.BlockSpec(memory_space=pltpu.VMEM)
    hbm = pl.BlockSpec(memory_space=pl.ANY)

    def kept(columns):
        return jax.ShapeDtypeStruct((micros, tokens, columns), BF16)

    def scratch(lead, columns, kind=BF16):
        return pltpu.VMEM((lead, tokens, columns), kind)

    out_shape = [
        kept(width),
        kept(width),
        kept(width),
        kept(hid),
        kept(width),
        kept(hid),
        kept(width),
        kept(3 * width),
        kept(vocab),
        kept(width),
        jax.ShapeDtypeStruct((VEC_ROWS, width), F32),
    ]
    return pl.pallas_call(
        functools.partial(pipeline_kernel, stages, micros),
        out_shape=out_shape,
        in_specs=[vmem] * 16,
        out_specs=[hbm] * 10 + [vmem],
        scratch_shapes=[
            scratch(micros, width),
            scratch(micros, width),
            scratch(micros, width),
            scratch(micros, width),
            scratch(micros, width),
            scratch(micros, 3 * width),
            pltpu.VMEM((micros, GROUP * pairs, ROW, 2 * ROW), BF16),
            scratch(micros, width),
            scratch(micros, width, F32),
            scratch(micros, width),
            scratch(micros, hid),
            scratch(micros, hid),
            pltpu.VMEM((tokens, width), F32),
            pltpu.VMEM((tokens, width), F32),
            pltpu.VMEM((tokens, width), F32),
            scratch(2, width),
            scratch(2, hid),
            scratch(2, width),
            scratch(2, 3 * width),
            scratch(2, vocab),
            pltpu.VMEM((3, 16, ROW), F32),
            pltpu.VMEM((ROW, ROW), F32),
            pltpu.SemaphoreType.DMA((micros,)),
            pltpu.SemaphoreType.DMA((micros,)),
            pltpu.SemaphoreType.DMA((micros,)),
            pltpu.SemaphoreType.DMA((micros,)),
            pltpu.SemaphoreType.DMA((10, micros)),
        ],
        compiler_params=pltpu.CompilerParams(
            collective_id=0, has_side_effects=True, vmem_limit_bytes=62 * 1024 * 1024
        ),
        name="pipeline",
    )(token_ids, segment_ids, target_ids, *params)


def line_dims(devices):
    dims, stride = [], 1
    if devices == 8:
        return [(2, 1), (4, 2)]
    while devices > 1:
        size = 4 if devices % 4 == 0 else 2
        dims.append((size, stride))
        stride *= size
        devices //= size
    return dims


def chunk_plan(width, hid, vocab, stages, devices):
    slim, deep = width // devices, hid // devices
    plan = [("out", 0, (slim, width), False)]
    for c in range(4):
        plan.append(("down", c, (deep, width // 4), c == 1))
    for c in range(2):
        plan.append(("extra", c, (stages, vocab // (stages * devices), width // 2), False))
    for c in range(hid // width):
        plan.append(("in", c, (slim, width), c == 1))
    for c in range(3):
        plan.append(("qkv", c, (slim, width), False))
    return plan


def gradient_kernel(stages, devices, plan, *refs):
    dims = line_dims(devices)
    refs = list(refs)

    def take(amount):
        head, refs[:] = refs[:amount], refs[amount:]
        return head

    inputs = take(10)
    vec_in, token_ids = take(2)
    qkv_out, out_out, in_out, down_out, embed_out, head_out, vec_out = take(7)
    local = take(10)
    in_sem = take(1)[0]
    turned_left, turned_xl = take(2)
    mats = dict(
        zip(
            ("normed", "mixed", "normed2", "active", "gres", "ghid", "gbr", "gproj", "xl", "xr"),
            local,
        )
    )
    names = list(mats)
    stage = lax.axis_index("pipe")
    place = lax.axis_index("dp")
    is_extra = (stage == 0) | (stage == stages - 1)
    width = mats["normed"].shape[1]
    where = [lax.rem(place // stride, size) for size, stride in dims]

    barrier = pltpu.get_barrier_semaphore()

    def greet(offset, carry):
        peer = lax.rem(place + offset, devices)
        pl.semaphore_signal(barrier, inc=1, device_id={"dp": peer}, device_id_type=MESH)
        return carry

    def greet_stage(offset, carry):
        peer = lax.rem(stage + offset, stages)
        pl.semaphore_signal(barrier, inc=1, device_id={"pipe": peer}, device_id_type=MESH)
        return carry

    lax.fori_loop(1, devices, greet, 0)
    lax.fori_loop(1, stages, greet_stage, 0)

    def load(name):
        i = names.index(name)
        return pltpu.make_async_copy(inputs[i], mats[name], in_sem.at[i])

    groups = [("mixed", "gbr"), ("gres", "active"), ("xr", "xl"), ("normed2", "ghid"), ("normed", "gproj")]

    def fetch(at):
        if at >= len(groups):
            return
        if groups[at] == ("xr", "xl"):
            @pl.when(is_extra)
            def _():
                load("xr").start()

            @pl.when(stage == stages - 1)
            def _():
                load("xl").start()

            at += 1
        for name in groups[at]:
            load(name).start()

    fetch(0)
    loaded = set()

    def need(*wanted):
        fresh = [name for name in wanted if name not in loaded]
        for name in fresh:
            loaded.add(name)
            load(name).wait()
        if fresh:
            at = [i for i, group in enumerate(groups) if group[0] == fresh[0]][0]
            fetch(at + 1)

    def identity(size):
        here = lax.broadcasted_iota(jnp.int32, (size, size), 0)
        there = lax.broadcasted_iota(jnp.int32, (size, size), 1)
        return jnp.where(here == there, 1.0, 0.0).astype(BF16)

    held = []

    def turn(name):
        if held[-1:] == [name]:
            return
        held.append(name)
        unit = identity(256)
        for q in range(width // 256):
            part = dot_nt(unit, mats[name][:, q * 256 : (q + 1) * 256])
            turned_left[q * 256 : (q + 1) * 256, :] = part.astype(BF16)

    bits = devices.bit_length() - 1
    vec_send, vec_recv = take(2)
    vec_sems = take(2)

    def vec_copy(k):
        peer = jnp.bitwise_xor(place, 1 << k)
        return pltpu.make_async_remote_copy(
            src_ref=vec_send.at[k],
            dst_ref=vec_recv.at[k],
            send_sem=vec_sems[0].at[k],
            recv_sem=vec_sems[1].at[k],
            device_id={"dp": peer},
            device_id_type=MESH,
        )

    def vec_step(k):
        def run():
            if k == 0:
                vec_send[0] = vec_in[...]
                ones = jnp.ones((16, mats["gres"].shape[0]), BF16)
                for name, start, row in (
                    ("gproj", 0, V_QUERY),
                    ("gproj", 2 * width, V_VALUE),
                    ("gbr", 0, V_BRANCH),
                    ("gres", 0, V_RESULT),
                ):
                    part = dot(ones, mats[name][:, start : start + width])
                    vec_send[0, row : row + 1, :] = part[0:1, :]
                for q in range(mats["ghid"].shape[1] // width):
                    part = dot(ones, mats["ghid"][:, q * width : (q + 1) * width])
                    vec_send[0, V_HIDDEN + q : V_HIDDEN + q + 1, :] = part[0:1, :]
            else:
                vec_copy(k - 1).wait_recv()
                vec_send[k] = vec_send[k - 1] + vec_recv[k - 1]
            if k < bits:
                vec_copy(k).start()

        return run

    final_send, final_recv = take(2)
    final_sems = take(2)

    def final_copy(offset):
        peer = lax.rem(stages - 1 + offset, stages)
        return pltpu.make_async_remote_copy(
            src_ref=final_send,
            dst_ref=final_recv,
            send_sem=final_sems[0].at[offset],
            recv_sem=final_sems[1].at[0],
            device_id={"pipe": peer},
            device_id_type=MESH,
        )

    def vec_last():
        vec_step(bits)()
        vec_out[...] = vec_send[bits]

        @pl.when(stage == stages - 1)
        def _():
            final_send[...] = vec_send[bits, 8:16, :]
            for offset in range(1, stages):
                final_copy(offset).start()

    def vec_finish():
        @pl.when(stage != stages - 1)
        def _():
            final_copy(1).wait_recv()
            vec_out[V_FINAL_GAIN : V_FINAL_BIAS + 1, :] = final_recv[
                V_FINAL_GAIN - 8 : V_FINAL_BIAS - 7, :
            ]

    def vec_drain():
        for k in range(bits):
            vec_copy(k).wait_send()

        @pl.when(stage == stages - 1)
        def _():
            for offset in range(1, stages):
                final_copy(offset).wait_send()

    extra_sum, extra_send_sem, extra_recv_sem = take(3)

    def extra_copy(source, offset, target):
        peer = lax.rem(source + offset, stages)
        return pltpu.make_async_remote_copy(
            src_ref=extra_sum.at[peer],
            dst_ref=target,
            send_sem=extra_send_sem.at[offset],
            recv_sem=extra_recv_sem.at[0 if source == 0 else 1],
            device_id={"pipe": peer},
            device_id_type=MESH,
        )

    down_full = {}

    def chunk_steps(kind, c, block, turned):
        order = list(range(len(dims)))
        if turned:
            order.reverse()
        full = take(1)[0]

        def compute():
            if kind == "down":
                need("gres", "active")
                turn("gres")
                if c % 2 == 1:
                    return
                half = width // 2
                lines = slice((c // 2) * half, (c // 2 + 1) * half)
                parts = dot(turned_left[lines, :], mats["active"][...]).astype(BF16)
                depth = block[0]
                unit = identity(depth)
                for d in range(devices):
                    back = dot_nt(unit, parts[:, d * depth : (d + 1) * depth]).astype(BF16)
                    down_full[c][split(d)] = back[:, 0 : half // 2]
                    down_full[c + 1][split(d)] = back[:, half // 2 : half]
            elif kind == "extra":
                vocab = turned_xl.shape[0]
                if c == 0:
                    load("xr").wait()

                @pl.when((stage == 0) & (c == 0))
                def _():
                    rows_n, seq = token_ids.shape
                    places = lax.broadcasted_iota(jnp.int32, (vocab, ROW), 0)
                    gap = jnp.full((1, ROW - seq), -1, jnp.int32)
                    for r in range(rows_n):
                        row = jnp.concatenate([token_ids[r : r + 1, :], gap], axis=1)
                        hot = jnp.where(places == row, 1.0, 0.0)
                        turned_xl[:, r * ROW : (r + 1) * ROW] = hot.astype(BF16)

                @pl.when((stage == stages - 1) & (c == 0))
                def _():
                    load("xl").wait()
                    unit = identity(256)
                    for q in range(vocab // 256):
                        part = dot_nt(unit, mats["xl"][:, q * 256 : (q + 1) * 256])
                        turned_xl[q * 256 : (q + 1) * 256, :] = part.astype(BF16)

                rows = vocab // stages
                for p in range(stages):
                    part = dot(
                        turned_xl[p * rows : (p + 1) * rows, :],
                        mats["xr"][:, c * (width // 2) : (c + 1) * (width // 2)],
                    )
                    part = part.astype(BF16).reshape((devices,) + block[1:])
                    for d in range(devices):
                        full[split(d) + (p,)] = part[d]
            else:
                left, right = {
                    "in": ("normed2", "ghid"),
                    "out": ("mixed", "gbr"),
                    "qkv": ("normed", "gproj"),
                }[kind]
                need(left, right)
                turn(left)
                cols = slice(c * width, (c + 1) * width)
                part = dot(turned_left[...], mats[right][:, cols]).astype(BF16)
                part = part.reshape((devices,) + block)
                for d in range(devices):
                    full[split(d)] = part[d]

        def split(d):
            return tuple((d // stride) % size for size, stride in reversed(dims))

        if kind == "down":
            down_full[c] = full
        steps = [[compute]]
        for at, phase in enumerate(order):
            size = dims[phase][0]
            buffers = take(3)
            done = order[:at]
            last = at == len(order) - 1
            steps[-1].append(functools.partial(line_step, phase, size, 1, full, buffers, done))
            for t in range(2, size):
                steps.append([functools.partial(line_step, phase, size, t, full, buffers, done)])
            drains.append((kind, functools.partial(line_drain, phase, size, full, buffers, done)))
            steps.append([functools.partial(line_final, kind, c, phase, size, full, buffers, done, last)])
        if kind == "extra":
            steps = [[gated([part]) for part in step] for step in steps]
        return steps

    def gated(step):
        def run():
            @pl.when(is_extra)
            def _():
                for part in step:
                    part()

        return run

    def block_of(full, phase, j, done):
        spot = [slice(None)] * len(dims)
        for other in done:
            spot[len(dims) - 1 - other] = where[other]
        spot[len(dims) - 1 - phase] = j
        return full.at[tuple(spot)]

    def line_copy(phase, size, t, side, full, buffers, done):
        recv, ssem, rsem = buffers
        i = where[phase]
        stride = dims[phase][1]
        if side == 0:
            j, peer = size - t + i, place + jnp.where(i < size - 1, stride, 0)
        else:
            j, peer = t - size + i, place - jnp.where(i > 0, stride, 0)
        source = block_of(full, phase, jnp.clip(j, 0, size - 1), done)
        target = recv.at[0 if size == 2 else side, t - 1]
        pieces = 1 if done or phase else dims[1][0]
        return [
            pltpu.make_async_remote_copy(
                src_ref=source.at[q] if pieces > 1 else source,
                dst_ref=target.at[q] if pieces > 1 else target,
                send_sem=ssem.at[side, t - 1, q],
                recv_sem=rsem.at[side, t - 1, q],
                device_id={"dp": peer},
                device_id_type=MESH,
            )
            for q in range(pieces)
        ]

    def sends(i, size, t, side):
        return (i <= t - 1) if side == 0 else (i >= size - t)

    def line_step(phase, size, t, full, buffers, done):
        i = where[phase]
        for side in range(2):
            at_end = (i == 0) if side == 0 else (i == size - 1)
            j = size - t + i if side == 0 else t - size + i
            j = jnp.clip(j, 0, size - 1)

            @pl.when(sends(i, size, t, side))
            def _():
                if t > 1:
                    @pl.when(jnp.logical_not(at_end))
                    def _():
                        for copy in line_copy(phase, size, t - 1, side, full, buffers, done):
                            copy.wait_recv()
                        own = block_of(full, phase, j, done)
                        got = buffers[0][0 if size == 2 else side, t - 2]
                        own[...] = (own[...].astype(F32) + got.astype(F32)).astype(BF16)

                for copy in line_copy(phase, size, t, side, full, buffers, done):
                    copy.start()

    def line_final(kind, c, phase, size, full, buffers, done, last):
        i = where[phase]
        own = block_of(full, phase, i, done)
        total = own
        if last:
            slots = {
                "qkv": lambda: qkv_out.at[:, c * width : (c + 1) * width],
                "in": lambda: in_out.at[:, c * width : (c + 1) * width],
                "out": lambda: out_out,
                "down": lambda: down_out.at[:, c * (width // 4) : (c + 1) * (width // 4)],
                "extra": lambda: extra_sum.at[:, :, c * (width // 2) : (c + 1) * (width // 2)],
            }
            total = slots[kind]()
        lower, upper = i > 0, i < size - 1

        def arrived(side):
            for copy in line_copy(phase, size, size - 1, side, full, buffers, done):
                copy.wait_recv()
            return buffers[0][0 if size == 2 else side, size - 2].astype(F32)

        @pl.when(lower & upper)
        def _():
            total[...] = (own[...].astype(F32) + arrived(0) + arrived(1)).astype(total.dtype)

        @pl.when(lower & jnp.logical_not(upper))
        def _():
            total[...] = (own[...].astype(F32) + arrived(0)).astype(total.dtype)

        @pl.when(jnp.logical_not(lower))
        def _():
            total[...] = (own[...].astype(F32) + arrived(1)).astype(total.dtype)

        if last and kind == "extra" and c == 1:
            for source_stage, out in ((0, embed_out), (stages - 1, head_out)):
                @pl.when(stage == source_stage)
                def _():
                    for offset in range(1, stages):
                        extra_copy(source_stage, offset, extra_recv[0 if source_stage == 0 else 1]).start()
                    out[...] = extra_sum[source_stage]

    def line_drain(phase, size, full, buffers, done):
        i = where[phase]
        for side in range(2):
            for t in range(1, size):
                @pl.when(sends(i, size, t, side))
                def _():
                    for copy in line_copy(phase, size, t, side, full, buffers, done):
                        copy.wait_send()

    extra_recv = take(2)
    drains = []
    chains = [chunk_steps(*item) for item in plan]
    depth = len(chains[0])
    vec_chain = [vec_step(k) for k in range(bits)] + [vec_last]
    starts, first, extra_rounds = [], 0, iter((1, 7, 9))
    for item in plan:
        if item[3]:
            starts.append(next(extra_rounds))
        else:
            starts.append(first)
            first += 1
    begun = False
    loaded_at = max(start for start, item in zip(starts, plan) if item[0] == "qkv" and item[1] == 0)
    for r in range(max(starts) + depth):
        for d in list(range(depth - 1, 1, -1)) + [0, 1]:
            for start, chain in zip(starts, chains):
                if r - start != d:
                    continue
                for part in chain[d]:
                    part()
                    if not begun:
                        begun = True
                        pl.semaphore_wait(barrier, devices - 1 + stages - 1)
        if 0 <= r - loaded_at < len(vec_chain):
            vec_chain[r - loaded_at]()
    vec_finish()
    for source_stage, out in ((0, embed_out), (stages - 1, head_out)):
        @pl.when(stage != source_stage)
        def _():
            got = extra_recv[0 if source_stage == 0 else 1]
            extra_copy(source_stage, 1, got).wait_recv()
            out[...] = got[...]

        @pl.when(stage == source_stage)
        def _():
            for offset in range(1, stages):
                extra_copy(source_stage, offset, extra_recv[0]).wait_send()

    vec_drain()
    for kind, drain in drains:
        if kind == "extra":
            gated([drain])()
        else:
            drain()


def run_gradients(stages, devices, saved, vec, token_ids):
    dims = line_dims(devices)
    rows, tokens, width = saved[0].shape
    hid, vocab = saved[3].shape[2], saved[8].shape[2]
    plan = chunk_plan(width, hid, vocab, stages, devices)
    saved = [member.reshape(rows * tokens, member.shape[2]) for member in saved]
    vmem = pl.BlockSpec(memory_space=pltpu.VMEM)
    hbm = pl.BlockSpec(memory_space=pl.ANY)
    bits = devices.bit_length() - 1
    share = vocab // (stages * devices)
    scratch = [pltpu.VMEM(member.shape, BF16) for member in saved]
    scratch += [pltpu.SemaphoreType.DMA((len(saved),))]
    scratch += [pltpu.VMEM((width, rows * tokens), BF16), pltpu.VMEM((vocab, rows * tokens), BF16)]
    scratch += [
        pltpu.VMEM((bits + 1,) + vec.shape, F32),
        pltpu.VMEM((bits,) + vec.shape, F32),
        pltpu.SemaphoreType.DMA((bits,)),
        pltpu.SemaphoreType.DMA((bits,)),
        pltpu.VMEM((8, width), F32),
        pltpu.VMEM((8, width), F32),
        pltpu.SemaphoreType.DMA((stages,)),
        pltpu.SemaphoreType.DMA((1,)),
        pltpu.VMEM((stages, share, width), F32),
        pltpu.SemaphoreType.DMA((stages,)),
        pltpu.SemaphoreType.DMA((2,)),
        pltpu.VMEM((share, width), F32),
        pltpu.VMEM((share, width), F32),
    ]
    sizes = [size for size, _ in reversed(dims)]
    for _, _, block, turned in plan:
        scratch.append(pltpu.VMEM(tuple(sizes) + block, BF16))
        remain = list(reversed(dims))
        for size, stride in dims[::-1] if turned else dims:
            remain.remove((size, stride))
            piece = tuple(other for other, _ in remain) + block
            scratch.append(pltpu.VMEM((1 if size == 2 else 2, size - 1) + piece, BF16))
            scratch += [pltpu.SemaphoreType.DMA((2, size - 1, 4))] * 2
    return pl.pallas_call(
        functools.partial(gradient_kernel, stages, devices, plan),
        out_shape=[
            jax.ShapeDtypeStruct((width // devices, 3 * width), F32),
            jax.ShapeDtypeStruct((width // devices, width), F32),
            jax.ShapeDtypeStruct((width // devices, hid), F32),
            jax.ShapeDtypeStruct((hid // devices, width), F32),
            jax.ShapeDtypeStruct((share, width), F32),
            jax.ShapeDtypeStruct((share, width), F32),
            jax.ShapeDtypeStruct(vec.shape, F32),
        ],
        in_specs=[hbm] * len(saved) + [vmem] * 2,
        out_specs=[vmem] * 7,
        scratch_shapes=scratch,
        compiler_params=pltpu.CompilerParams(
            collective_id=1, has_side_effects=True, vmem_limit_bytes=62 * 1024 * 1024
        ),
        name="gradients",
    )(*saved, vec, token_ids)


def finish_kernel(devices, embed_g, qkv_g, out_g, in_g, down_g, head_g, vec, *outs):
    place = lax.axis_index("dp")
    width = vec.shape[1]
    (embed_o, qkv_o, qv_o, out_o, outb_o, in_o, inb_o, down_o, gain_o, shift_o, fg_o, fb_o, head_o) = outs
    embed_o[...] = embed_g[...]
    head_o[...] = head_g[...]
    for source, target in ((qkv_g, qkv_o), (out_g, out_o), (in_g, in_o), (down_g, down_o)):
        target[0] = source[...]
    lanes = width // devices
    turned = pltpu.roll(vec[0:8, :], lax.rem(width - place * lanes, width), 1)
    for row, out in ((V_QUERY, qv_o), (V_BRANCH, outb_o), (V_GAIN1, gain_o), (V_SHIFT1, shift_o)):
        out[0] = turned[row : row + 2, 0:lanes]
    share = inb_o.shape[1]
    first = place * share
    row = vec[pl.ds(V_HIDDEN + first // width, 1), :]
    wide = jnp.broadcast_to(row, (8, width))
    inb_o[...] = pltpu.roll(wide, lax.rem(width - lax.rem(first, width), width), 1)[0:1, 0:share]
    fg_o[...] = vec[V_FINAL_GAIN : V_FINAL_GAIN + 1, :]
    fb_o[...] = vec[V_FINAL_BIAS : V_FINAL_BIAS + 1, :]


def run_finish(devices, embed_g, qkv_g, out_g, in_g, down_g, head_g, vec):
    vmem = pl.BlockSpec(memory_space=pltpu.VMEM)
    width = vec.shape[1]
    lanes = width // devices

    def shape(*sizes):
        return jax.ShapeDtypeStruct(sizes, F32)

    pair = shape(1, 2, lanes)
    return pl.pallas_call(
        functools.partial(finish_kernel, devices),
        out_shape=[
            shape(*embed_g.shape),
            shape(1, *qkv_g.shape),
            pair,
            shape(1, *out_g.shape),
            pair,
            shape(1, *in_g.shape),
            shape(1, in_g.shape[1] // devices),
            shape(1, *down_g.shape),
            pair,
            pair,
            shape(1, width),
            shape(1, width),
            shape(*head_g.shape),
        ],
        in_specs=[vmem] * 7,
        out_specs=[vmem] * 13,
        name="finish",
    )(embed_g, qkv_g, out_g, in_g, down_g, head_g, vec)


def on_device(
    token_ids,
    segment_ids,
    target_ids,
    embed_table,
    qkv_weight,
    qv_bias,
    out_weight,
    out_biases,
    ff_in,
    ff_in_bias,
    ff_out,
    norm_gains,
    norm_biases,
    final_gain,
    final_bias,
    head_weight,
):
    stages = lax.axis_size("pipe")
    devices = lax.axis_size("dp")
    params = (
        embed_table,
        qkv_weight[0],
        qv_bias[0],
        out_weight[0],
        out_biases[0],
        ff_in[0],
        ff_in_bias,
        ff_out[0],
        norm_gains[0],
        norm_biases[0],
        final_gain[None],
        final_bias[None],
        head_weight,
    )
    *saved, vec = run_pipeline(stages, token_ids, segment_ids, target_ids, params)
    qkv_g, out_g, in_g, down_g, embed_g, head_g, sums = run_gradients(stages, devices, saved, vec, token_ids)
    done = list(run_finish(devices, embed_g, qkv_g, out_g, in_g, down_g, head_g, sums))
    done[10], done[11] = done[10][0], done[11][0]
    return tuple(done)


def solution(mesh):
    layer3 = P("pipe", None, None)
    return jax.shard_map(
        on_device,
        mesh=mesh,
        in_specs=(
            P("dp", None),
            P("dp", None),
            P("dp", None),
            P(),
            layer3,
            layer3,
            layer3,
            layer3,
            layer3,
            P("pipe", None),
            layer3,
            layer3,
            layer3,
            P(),
            P(),
            P(),
        ),
        out_specs=(
            P(("pipe", "dp"), None),
            P("pipe", "dp", None),
            P("pipe", None, "dp"),
            P("pipe", "dp", None),
            P("pipe", None, "dp"),
            P("pipe", "dp", None),
            P("pipe", "dp"),
            P("pipe", "dp", None),
            P("pipe", None, "dp"),
            P("pipe", None, "dp"),
            P(),
            P(),
            P(("pipe", "dp"), None),
        ),
        check_vma=False,
    )
```

```python
import functools

import jax
import jax.numpy as jnp
from jax import lax
from jax.experimental import pallas as pl
from jax.experimental.pallas import tpu as pltpu
from jax.sharding import PartitionSpec as P

HEADS = 8
FRAME = 6
ROW = 128
GROUP = 2
MASKED = -1e30
GELU_A = 0.7978845608
GELU_B = 0.044715
MESH = pl.DeviceIdType.MESH
F32 = jnp.float32
BF16 = jnp.bfloat16

VEC_ROWS = 16
V_QUERY, V_VALUE, V_BRANCH, V_RESULT, V_GAIN1, V_GAIN2, V_SHIFT1, V_SHIFT2 = range(8)
V_HIDDEN = 8
V_FINAL_GAIN, V_FINAL_BIAS = 12, 13


def dot(a, b):
    return lax.dot_general(a, b, (((1,), (0,)), ((), ())), preferred_element_type=F32)


def dot_nt(a, b):
    return lax.dot_general(a, b, (((1,), (1,)), ((), ())), preferred_element_type=F32)


def dot_tn(a, b):
    return lax.dot_general(a, b, (((0,), (0,)), ((), ())), preferred_element_type=F32)


def normalise(values):
    centre = jnp.mean(values, axis=-1, keepdims=True)
    centered = values - centre
    spread = jnp.mean(centered * centered, axis=-1, keepdims=True)
    scale = lax.rsqrt(spread + 1e-05)
    return centered * scale, scale


def norm_backward(grad, normal, scale, gain):
    grad_n = grad * gain
    mean_grad = jnp.mean(grad_n, axis=-1, keepdims=True)
    mean_proj = jnp.mean(grad_n * normal, axis=-1, keepdims=True)
    return scale * (grad_n - mean_grad - normal * mean_proj)


def column_sum(values):
    return jnp.sum(values, axis=0, keepdims=True)


def stack_pair(pair, low_lanes):
    zero = jnp.zeros_like(pair)
    return jnp.concatenate(
        [jnp.where(low_lanes, pair, zero), jnp.where(low_lanes, zero, pair)], axis=0
    )


def join_pair(stacked, low_lanes):
    half = stacked.shape[0] // 2
    return jnp.where(low_lanes, stacked[:half], stacked[half:])


def pipeline_kernel(
    stages,
    micros,
    token_ids,
    segment_ids,
    target_ids,
    embed,
    qkv_w,
    qv_b,
    out_w,
    out_b,
    in_w,
    in_b,
    down_w,
    gains,
    shifts,
    fin_gain,
    fin_bias,
    head_w,
    normed_o,
    mixed_o,
    normed2_o,
    active_o,
    gres_o,
    ghid_o,
    gbr_o,
    gproj_o,
    xl_o,
    xr_o,
    vec,
    instream,
    outb,
    gin,
    gs,
    normed,
    proj,
    probs,
    mixed,
    middle,
    normed2,
    active,
    slope,
    lo,
    go,
    gmid,
    s_gres,
    s_ghid,
    s_gbr,
    s_gproj,
    s_xl,
    ids,
    frames,
    fsend,
    frecv,
    bsend,
    brecv,
    osem,
):
    stage = lax.axis_index("pipe")
    tokens, width = instream.shape[1], instream.shape[2]
    hidden_n = in_b.shape[1]
    vocab = head_w.shape[0]
    pairs = width // ROW
    chunk = 512
    is_first = stage == 0
    is_last = stage == stages - 1
    up = jnp.minimum(stage + 1, stages - 1)
    down = jnp.maximum(stage - 1, 0)

    barrier = pltpu.get_barrier_semaphore()

    @pl.when(jnp.logical_not(is_first))
    def _():
        pl.semaphore_signal(barrier, inc=1, device_id={"pipe": down}, device_id_type=MESH)

    @pl.when(jnp.logical_not(is_last))
    def _():
        pl.semaphore_signal(barrier, inc=1, device_id={"pipe": up}, device_id_type=MESH)

    pl.semaphore_wait(barrier, jnp.where(is_first | is_last, 1, 2))
    vec[...] = jnp.zeros_like(vec)
    rows_n, seq = token_ids.shape
    for index, member in enumerate((token_ids, segment_ids, target_ids)):
        ids[index] = jnp.full(ids.shape[1:], 4.0 if index == 1 else -1.0, F32)
        ids[index, 0:rows_n, 0:seq] = member[...].astype(F32)
    at_query = lax.broadcasted_iota(jnp.int32, (ROW, ROW), 1)
    at_key = lax.broadcasted_iota(jnp.int32, (ROW, ROW), 0)
    frames[...] = jnp.where(at_key < ((at_query * 43) // 256) * FRAME + FRAME, 1.0, 0.0)

    def column(index, row):
        values = jnp.broadcast_to(ids[index, pl.ds(row, 1), :], (8, ROW))
        return values.T[:, 0:1]

    def hot_rows(index, m):
        parts = [column(index, m * GROUP + r) for r in range(GROUP)]
        values = jnp.concatenate(parts, axis=0)
        places = lax.broadcasted_iota(jnp.int32, (tokens, vocab), 1).astype(F32)
        return values, jnp.where(values == places, 1.0, 0.0)

    def forward_copy(m):
        return pltpu.make_async_remote_copy(
            src_ref=outb.at[m],
            dst_ref=instream.at[m],
            send_sem=fsend.at[m],
            recv_sem=frecv.at[m],
            device_id={"pipe": up},
            device_id_type=MESH,
        )

    def backward_copy(m):
        return pltpu.make_async_remote_copy(
            src_ref=gs.at[m],
            dst_ref=gin.at[m],
            send_sem=bsend.at[m],
            recv_sem=brecv.at[m],
            device_id={"pipe": down},
            device_id_type=MESH,
        )

    def save(index, src, dst, m):
        return pltpu.make_async_copy(src, dst.at[m], osem.at[index, m])

    def saves_forward(m):
        return [
            save(0, normed.at[m], normed_o, m),
            save(1, mixed.at[m], mixed_o, m),
            save(2, normed2.at[m], normed2_o, m),
            save(3, active.at[m], active_o, m),
        ]

    def saves_backward(m):
        slot = lax.rem(m, 2)
        return [
            save(4, s_gres.at[slot], gres_o, m),
            save(5, s_ghid.at[slot], ghid_o, m),
            save(6, s_gbr.at[slot], gbr_o, m),
            save(7, s_gproj.at[slot], gproj_o, m),
        ]

    def save_xl(m):
        return save(8, s_xl.at[lax.rem(m, 2)], xl_o, m)

    def put_xl(m, value):
        @pl.when(m >= 2)
        def _():
            save_xl(m - 2).wait()

        s_xl[lax.rem(m, 2)] = value
        save_xl(m).start()

    lane_low = lax.broadcasted_iota(jnp.int32, (ROW, ROW), 1) < ROW // 2

    def forward(m):
        @pl.when(is_first)
        def _():
            hot = hot_rows(0, m)[1].astype(BF16)
            instream[m] = dot(hot, embed[...]).astype(BF16)

        @pl.when(jnp.logical_not(is_first))
        def _():
            forward_copy(m).wait_recv()

        normal, _ = normalise(instream[m].astype(F32))
        normed[m] = (normal * gains[0:1, :] + shifts[0:1, :]).astype(BF16)
        low = normed[m]
        queries = dot(low, qkv_w[:, 0:width]) + qv_b[0:1, :]
        proj[m, :, 0:width] = (queries * (ROW // 2) ** -0.5).astype(BF16)
        proj[m, :, width : 2 * width] = dot(low, qkv_w[:, width : 2 * width]).astype(BF16)
        proj[m, :, 2 * width : 3 * width] = (
            dot(low, qkv_w[:, 2 * width : 3 * width]) + qv_b[1:2, :]
        ).astype(BF16)
        masks, scores = [], []
        for r in range(GROUP):
            rows = slice(r * ROW, (r + 1) * ROW)
            kinds = lax.broadcasted_iota(jnp.int32, (16, ROW), 0).astype(F32)
            member = jnp.where(ids[1, pl.ds(m * GROUP + r, 1), :] == kinds, 1.0, 0.0).astype(BF16)
            mask = jnp.where(dot_tn(member, member) * frames[...] > 0.5, 0.0, MASKED)
            masks.append(jnp.concatenate([mask, mask], axis=1))
            for p in range(pairs):
                q = stack_pair(proj[m, rows, p * ROW : (p + 1) * ROW], lane_low)
                k = proj[m, rows, width + p * ROW : width + (p + 1) * ROW]
                scores.append(dot_nt(k, q))

        def mix(unit):
            r, p = unit // pairs, unit % pairs
            rows = slice(r * ROW, (r + 1) * ROW)
            v = proj[m, rows, 2 * width + p * ROW : 2 * width + (p + 1) * ROW]
            both = dot_tn(probs[m, unit], v)
            mixed[m, rows, p * ROW : (p + 1) * ROW] = join_pair(both, lane_low).astype(BF16)

        for unit in range(GROUP * pairs):
            masked = scores[unit] + masks[unit // pairs]
            expo = jnp.exp(masked - jnp.max(masked, axis=0, keepdims=True))
            total = jnp.sum(expo, axis=0, keepdims=True)
            probs[m, unit] = (expo * (1.0 / total)).astype(BF16)
            if unit:
                mix(unit - 1)
        mix(GROUP * pairs - 1)
        mid = instream[m].astype(F32) + (dot(mixed[m], out_w[...]) + out_b[0:1, :])
        middle[m] = mid
        normal2, _ = normalise(mid)
        normed2[m] = (normal2 * gains[1:2, :] + shifts[1:2, :]).astype(BF16)
        low2 = normed2[m]
        parts = hidden_n // chunk

        def spread(c):
            return dot(low2, in_w[:, c * chunk : (c + 1) * chunk])

        total, ahead = None, spread(0)
        for c in range(parts):
            cols = slice(c * chunk, (c + 1) * chunk)
            hid = ahead + in_b[0:1, cols]
            if c + 1 < parts:
                ahead = spread(c + 1)
            square = hid * hid
            tan = jnp.tanh(hid * (GELU_A + (GELU_A * GELU_B) * square))
            half = 0.5 + 0.5 * tan
            act = (hid * half).astype(BF16)
            active[m, :, cols] = act
            rise = (1.0 - tan * tan) * (0.5 * GELU_A + (1.5 * GELU_A * GELU_B) * square)
            slope[m, :, cols] = (half + hid * rise).astype(BF16)
            term = dot(act, down_w[cols, :])
            total = term if total is None else total + term
        for copy in saves_forward(m):
            copy.start()
        lo[...] = middle[m] + (total + out_b[1:2, :])

        @pl.when(jnp.logical_not(is_last))
        def _():
            outb[m] = lo[...].astype(BF16)
            forward_copy(m).start()

    def head(m):
        normal, scale = normalise(lo[...])
        outb[m] = (normal * fin_gain[...] + fin_bias[...]).astype(BF16)
        save(9, outb.at[m], xr_o, m).start()
        logits = dot_nt(outb[m], head_w[...])
        top = jnp.max(logits, axis=-1, keepdims=True)
        expo = jnp.exp(logits - top)
        total = jnp.sum(expo, axis=-1, keepdims=True)
        target, hot = hot_rows(2, m)
        grad_logits = jnp.where(target >= 0.0, expo * (1.0 / total) - hot, 0.0).astype(BF16)
        put_xl(m, grad_logits)
        grad_final = dot(grad_logits, head_w[...])
        vec[V_FINAL_GAIN : V_FINAL_GAIN + 1, :] += column_sum(grad_final * normal)
        vec[V_FINAL_BIAS : V_FINAL_BIAS + 1, :] += column_sum(grad_final)
        go[...] = norm_backward(grad_final, normal, scale, fin_gain[...])

    def backward(m):
        slot = lax.rem(m, 2)

        @pl.when(m >= 2)
        def _():
            for copy in saves_backward(m - 2):
                copy.wait()

        @pl.when(jnp.logical_not(is_last))
        def _():
            backward_copy(m).wait_recv()
            go[...] = gin[m].astype(F32)

        s_gres[slot] = go[...].astype(BF16)
        gres = s_gres[slot]
        parts = hidden_n // chunk

        def spread(c):
            return dot_nt(gres, down_w[c * chunk : (c + 1) * chunk, :])

        total, ahead = None, spread(0)
        for c in range(parts):
            cols = slice(c * chunk, (c + 1) * chunk)
            gact = ahead
            if c + 1 < parts:
                ahead = spread(c + 1)
            ghid = (gact * slope[m, :, cols].astype(F32)).astype(BF16)
            s_ghid[slot, :, cols] = ghid
            term = dot_nt(ghid, in_w[:, cols])
            total = term if total is None else total + term
        normal2, scale2 = normalise(middle[m])
        vec[V_GAIN2 : V_GAIN2 + 1, :] += column_sum(total * normal2)
        vec[V_SHIFT2 : V_SHIFT2 + 1, :] += column_sum(total)
        gmid[...] = go[...] + norm_backward(total, normal2, scale2, gains[1:2, :])
        s_gbr[slot] = gmid[...].astype(BF16)
        gbr = s_gbr[slot]
        gmix = dot_nt(gbr, out_w[...]).astype(BF16)
        grads = []
        for r in range(GROUP):
            rows = slice(r * ROW, (r + 1) * ROW)
            for p in range(pairs):
                gm = stack_pair(gmix[rows, p * ROW : (p + 1) * ROW], lane_low)
                vlanes = slice(2 * width + p * ROW, 2 * width + (p + 1) * ROW)
                grads.append(dot_nt(proj[m, rows, vlanes], gm))
                s_gproj[slot, rows, vlanes] = dot(probs[m, r * pairs + p], gm).astype(BF16)

        def pull(unit, gsc):
            r, p = unit // pairs, unit % pairs
            rows = slice(r * ROW, (r + 1) * ROW)
            lanes = slice(p * ROW, (p + 1) * ROW)
            klanes = slice(width + p * ROW, width + (p + 1) * ROW)
            q = stack_pair(proj[m, rows, lanes], lane_low)
            s_gproj[slot, rows, klanes] = dot(gsc, q).astype(BF16)
            gq = join_pair(dot_tn(gsc, proj[m, rows, klanes]), lane_low) * (ROW // 2) ** -0.5
            s_gproj[slot, rows, lanes] = gq.astype(BF16)

        waiting = None
        for unit in range(GROUP * pairs):
            weights = probs[m, unit].astype(F32)
            inner = jnp.sum(weights * grads[unit], axis=0, keepdims=True)
            gsc = (weights * (grads[unit] - inner)).astype(BF16)
            if waiting is not None:
                pull(unit - 1, waiting)
            waiting = gsc
        pull(GROUP * pairs - 1, waiting)
        for copy in saves_backward(m):
            copy.start()
        gproj = s_gproj[slot]
        gnormed = dot_nt(gproj, qkv_w[...])
        normal, scale = normalise(instream[m].astype(F32))
        vec[V_GAIN1 : V_GAIN1 + 1, :] += column_sum(gnormed * normal)
        vec[V_SHIFT1 : V_SHIFT1 + 1, :] += column_sum(gnormed)
        gs[m] = (gmid[...] + norm_backward(gnormed, normal, scale, gains[0:1, :])).astype(BF16)

        @pl.when(is_first)
        def _():
            save(9, gs.at[m], xr_o, m).start()

        @pl.when(jnp.logical_not(is_first))
        def _():
            backward_copy(m).start()

    def tick(t, carry):
        m_forward = t - stage
        m_backward = t - (2 * (stages - 1) - stage)

        @pl.when((m_forward >= 0) & (m_forward < micros))
        def _():
            forward(m_forward)

        @pl.when((m_backward >= 0) & (m_backward < micros))
        def _():
            @pl.when(is_last)
            def _():
                head(m_backward)

            backward(m_backward)

        return carry

    lax.fori_loop(0, micros + 2 * (stages - 1), tick, 0)

    for m in range(micros):
        for copy in saves_forward(m):
            copy.wait()

        @pl.when(jnp.logical_not(is_last))
        def _():
            forward_copy(m).wait_send()

        @pl.when(jnp.logical_not(is_first))
        def _():
            backward_copy(m).wait_send()

        @pl.when(is_first)
        def _():
            save(9, gs.at[m], xr_o, m).wait()

        @pl.when(is_last)
        def _():
            save(9, outb.at[m], xr_o, m).wait()

    for m in range(max(0, micros - 2), micros):
        for copy in saves_backward(m):
            copy.wait()

        @pl.when(is_last)
        def _():
            save_xl(m).wait()


def run_pipeline(stages, token_ids, segment_ids, target_ids, params):
    embed, in_w, head_w = params[0], params[5], params[12]
    width = embed.shape[1]
    vocab = head_w.shape[0]
    hid = in_w.shape[1]
    tokens = GROUP * ROW
    micros = token_ids.shape[0] // GROUP
    pairs = width // ROW
    vmem = pl.BlockSpec(memory_space=pltpu.VMEM)
    hbm = pl.BlockSpec(memory_space=pl.ANY)

    def kept(columns):
        return jax.ShapeDtypeStruct((micros, tokens, columns), BF16)

    def scratch(lead, columns, kind=BF16):
        return pltpu.VMEM((lead, tokens, columns), kind)

    out_shape = [
        kept(width),
        kept(width),
        kept(width),
        kept(hid),
        kept(width),
        kept(hid),
        kept(width),
        kept(3 * width),
        kept(vocab),
        kept(width),
        jax.ShapeDtypeStruct((VEC_ROWS, width), F32),
    ]
    return pl.pallas_call(
        functools.partial(pipeline_kernel, stages, micros),
        out_shape=out_shape,
        in_specs=[vmem] * 16,
        out_specs=[hbm] * 10 + [vmem],
        scratch_shapes=[
            scratch(micros, width),
            scratch(micros, width),
            scratch(micros, width),
            scratch(micros, width),
            scratch(micros, width),
            scratch(micros, 3 * width),
            pltpu.VMEM((micros, GROUP * pairs, ROW, 2 * ROW), BF16),
            scratch(micros, width),
            scratch(micros, width, F32),
            scratch(micros, width),
            scratch(micros, hid),
            scratch(micros, hid),
            pltpu.VMEM((tokens, width), F32),
            pltpu.VMEM((tokens, width), F32),
            pltpu.VMEM((tokens, width), F32),
            scratch(2, width),
            scratch(2, hid),
            scratch(2, width),
            scratch(2, 3 * width),
            scratch(2, vocab),
            pltpu.VMEM((3, 16, ROW), F32),
            pltpu.VMEM((ROW, ROW), F32),
            pltpu.SemaphoreType.DMA((micros,)),
            pltpu.SemaphoreType.DMA((micros,)),
            pltpu.SemaphoreType.DMA((micros,)),
            pltpu.SemaphoreType.DMA((micros,)),
            pltpu.SemaphoreType.DMA((10, micros)),
        ],
        compiler_params=pltpu.CompilerParams(
            collective_id=0, has_side_effects=True, vmem_limit_bytes=62 * 1024 * 1024
        ),
        name="pipeline",
    )(token_ids, segment_ids, target_ids, *params)


def line_dims(devices):
    dims, stride = [], 1
    if devices == 8:
        return [(2, 1), (4, 2)]
    while devices > 1:
        size = 4 if devices % 4 == 0 else 2
        dims.append((size, stride))
        stride *= size
        devices //= size
    return dims


def chunk_plan(width, hid, vocab, stages, devices):
    slim, deep = width // devices, hid // devices
    plan = [("out", 0, (slim, width), False)]
    for c in range(4):
        plan.append(("down", c, (deep, width // 4), c in (1, 3)))
    for c in range(2):
        plan.append(("extra", c, (stages, vocab // (stages * devices), width // 2), False))
    for c in range(hid // width):
        plan.append(("in", c, (slim, width), c % 2 == 1))
    for c in range(3):
        plan.append(("qkv", c, (slim, width), c == 1))
    return plan


def gradient_kernel(stages, devices, plan, *refs):
    dims = line_dims(devices)
    refs = list(refs)

    def take(amount):
        head, refs[:] = refs[:amount], refs[amount:]
        return head

    inputs = take(10)
    vec_in, token_ids = take(2)
    qkv_out, out_out, in_out, down_out, embed_out, head_out, vec_out = take(7)
    local = take(10)
    in_sem = take(1)[0]
    turned_left, turned_xl = take(2)
    mats = dict(
        zip(
            ("normed", "mixed", "normed2", "active", "gres", "ghid", "gbr", "gproj", "xl", "xr"),
            local,
        )
    )
    names = list(mats)
    stage = lax.axis_index("pipe")
    place = lax.axis_index("dp")
    is_extra = (stage == 0) | (stage == stages - 1)
    width = mats["normed"].shape[1]
    where = [lax.rem(place // stride, size) for size, stride in dims]

    barrier = pltpu.get_barrier_semaphore()

    def greet(offset, carry):
        peer = lax.rem(place + offset, devices)
        pl.semaphore_signal(barrier, inc=1, device_id={"dp": peer}, device_id_type=MESH)
        return carry

    def greet_stage(offset, carry):
        peer = lax.rem(stage + offset, stages)
        pl.semaphore_signal(barrier, inc=1, device_id={"pipe": peer}, device_id_type=MESH)
        return carry

    lax.fori_loop(1, devices, greet, 0)
    lax.fori_loop(1, stages, greet_stage, 0)

    def load(name):
        i = names.index(name)
        return pltpu.make_async_copy(inputs[i], mats[name], in_sem.at[i])

    groups = [("mixed", "gbr"), ("gres", "active"), ("xr", "xl"), ("normed2", "ghid"), ("normed", "gproj")]

    def fetch(at):
        if at >= len(groups):
            return
        if groups[at] == ("xr", "xl"):
            @pl.when(is_extra)
            def _():
                load("xr").start()

            @pl.when(stage == stages - 1)
            def _():
                load("xl").start()

            at += 1
        for name in groups[at]:
            load(name).start()

    fetch(0)
    loaded = set()

    def need(*wanted):
        fresh = [name for name in wanted if name not in loaded]
        for name in fresh:
            loaded.add(name)
            load(name).wait()
        if fresh:
            at = [i for i, group in enumerate(groups) if group[0] == fresh[0]][0]
            fetch(at + 1)

    def identity(size):
        here = lax.broadcasted_iota(jnp.int32, (size, size), 0)
        there = lax.broadcasted_iota(jnp.int32, (size, size), 1)
        return jnp.where(here == there, 1.0, 0.0).astype(BF16)

    held = []

    def turn(name):
        if held[-1:] == [name]:
            return
        held.append(name)
        unit = identity(256)
        for q in range(width // 256):
            part = dot_nt(unit, mats[name][:, q * 256 : (q + 1) * 256])
            turned_left[q * 256 : (q + 1) * 256, :] = part.astype(BF16)

    bits = devices.bit_length() - 1
    vec_send, vec_recv = take(2)
    vec_sems = take(2)

    def vec_copy(k):
        peer = jnp.bitwise_xor(place, 1 << k)
        return pltpu.make_async_remote_copy(
            src_ref=vec_send.at[k],
            dst_ref=vec_recv.at[k],
            send_sem=vec_sems[0].at[k],
            recv_sem=vec_sems[1].at[k],
            device_id={"dp": peer},
            device_id_type=MESH,
        )

    def vec_step(k):
        def run():
            if k == 0:
                vec_send[0] = vec_in[...]
                ones = jnp.ones((16, mats["gres"].shape[0]), BF16)
                for name, start, row in (
                    ("gproj", 0, V_QUERY),
                    ("gproj", 2 * width, V_VALUE),
                    ("gbr", 0, V_BRANCH),
                    ("gres", 0, V_RESULT),
                ):
                    part = dot(ones, mats[name][:, start : start + width])
                    vec_send[0, row : row + 1, :] = part[0:1, :]
                for q in range(mats["ghid"].shape[1] // width):
                    part = dot(ones, mats["ghid"][:, q * width : (q + 1) * width])
                    vec_send[0, V_HIDDEN + q : V_HIDDEN + q + 1, :] = part[0:1, :]
            else:
                vec_copy(k - 1).wait_recv()
                vec_send[k] = vec_send[k - 1] + vec_recv[k - 1]
            if k < bits:
                vec_copy(k).start()

        return run

    final_send, final_recv = take(2)
    final_sems = take(2)

    def final_copy(offset):
        peer = lax.rem(stages - 1 + offset, stages)
        return pltpu.make_async_remote_copy(
            src_ref=final_send,
            dst_ref=final_recv,
            send_sem=final_sems[0].at[offset],
            recv_sem=final_sems[1].at[0],
            device_id={"pipe": peer},
            device_id_type=MESH,
        )

    def vec_last():
        vec_step(bits)()
        vec_out[...] = vec_send[bits]

        @pl.when(stage == stages - 1)
        def _():
            final_send[...] = vec_send[bits, 8:16, :]
            for offset in range(1, stages):
                final_copy(offset).start()

    def vec_finish():
        @pl.when(stage != stages - 1)
        def _():
            final_copy(1).wait_recv()
            vec_out[V_FINAL_GAIN : V_FINAL_BIAS + 1, :] = final_recv[
                V_FINAL_GAIN - 8 : V_FINAL_BIAS - 7, :
            ]

    def vec_drain():
        for k in range(bits):
            vec_copy(k).wait_send()

        @pl.when(stage == stages - 1)
        def _():
            for offset in range(1, stages):
                final_copy(offset).wait_send()

    extra_sum, extra_send_sem, extra_recv_sem = take(3)

    def extra_copy(source, offset, target):
        peer = lax.rem(source + offset, stages)
        return pltpu.make_async_remote_copy(
            src_ref=extra_sum.at[peer],
            dst_ref=target,
            send_sem=extra_send_sem.at[offset],
            recv_sem=extra_recv_sem.at[0 if source == 0 else 1],
            device_id={"pipe": peer},
            device_id_type=MESH,
        )

    down_full = {}

    def chunk_steps(kind, c, block, turned):
        order = list(range(len(dims)))
        if turned:
            order.reverse()
        full = take(1)[0]

        def compute():
            if kind == "down":
                need("gres", "active")
                turn("gres")
                if c % 2 == 1:
                    return
                half = width // 2
                lines = slice((c // 2) * half, (c // 2 + 1) * half)
                parts = dot(turned_left[lines, :], mats["active"][...]).astype(BF16)
                depth = block[0]
                unit = identity(depth)
                for d in range(devices):
                    back = dot_nt(unit, parts[:, d * depth : (d + 1) * depth]).astype(BF16)
                    down_full[c][split(d)] = back[:, 0 : half // 2]
                    down_full[c + 1][split(d)] = back[:, half // 2 : half]
            elif kind == "extra":
                vocab = turned_xl.shape[0]
                if c == 0:
                    load("xr").wait()

                @pl.when((stage == 0) & (c == 0))
                def _():
                    rows_n, seq = token_ids.shape
                    places = lax.broadcasted_iota(jnp.int32, (vocab, ROW), 0)
                    gap = jnp.full((1, ROW - seq), -1, jnp.int32)
                    for r in range(rows_n):
                        row = jnp.concatenate([token_ids[r : r + 1, :], gap], axis=1)
                        hot = jnp.where(places == row, 1.0, 0.0)
                        turned_xl[:, r * ROW : (r + 1) * ROW] = hot.astype(BF16)

                @pl.when((stage == stages - 1) & (c == 0))
                def _():
                    load("xl").wait()
                    unit = identity(256)
                    for q in range(vocab // 256):
                        part = dot_nt(unit, mats["xl"][:, q * 256 : (q + 1) * 256])
                        turned_xl[q * 256 : (q + 1) * 256, :] = part.astype(BF16)

                rows = vocab // stages
                for p in range(stages):
                    part = dot(
                        turned_xl[p * rows : (p + 1) * rows, :],
                        mats["xr"][:, c * (width // 2) : (c + 1) * (width // 2)],
                    )
                    part = part.astype(BF16).reshape((devices,) + block[1:])
                    for d in range(devices):
                        full[split(d) + (p,)] = part[d]
            else:
                left, right = {
                    "in": ("normed2", "ghid"),
                    "out": ("mixed", "gbr"),
                    "qkv": ("normed", "gproj"),
                }[kind]
                need(left, right)
                turn(left)
                cols = slice(c * width, (c + 1) * width)
                part = dot(turned_left[...], mats[right][:, cols]).astype(BF16)
                part = part.reshape((devices,) + block)
                for d in range(devices):
                    full[split(d)] = part[d]

        def split(d):
            return tuple((d // stride) % size for size, stride in reversed(dims))

        if kind == "down":
            down_full[c] = full
        steps = [[compute]]
        for at, phase in enumerate(order):
            size = dims[phase][0]
            buffers = take(3)
            done = order[:at]
            last = at == len(order) - 1
            steps[-1].append(functools.partial(line_step, phase, size, 1, full, buffers, done))
            for t in range(2, size):
                steps.append([functools.partial(line_step, phase, size, t, full, buffers, done)])
            drains.append((kind, functools.partial(line_drain, phase, size, full, buffers, done)))
            steps.append([functools.partial(line_final, kind, c, phase, size, full, buffers, done, last)])
        if kind == "extra":
            steps = [[gated([part]) for part in step] for step in steps]
        return steps

    def gated(step):
        def run():
            @pl.when(is_extra)
            def _():
                for part in step:
                    part()

        return run

    def block_of(full, phase, j, done):
        spot = [slice(None)] * len(dims)
        for other in done:
            spot[len(dims) - 1 - other] = where[other]
        spot[len(dims) - 1 - phase] = j
        return full.at[tuple(spot)]

    def line_copy(phase, size, t, side, full, buffers, done):
        recv, ssem, rsem = buffers
        i = where[phase]
        stride = dims[phase][1]
        if side == 0:
            j, peer = size - t + i, place + jnp.where(i < size - 1, stride, 0)
        else:
            j, peer = t - size + i, place - jnp.where(i > 0, stride, 0)
        return pltpu.make_async_remote_copy(
            src_ref=block_of(full, phase, jnp.clip(j, 0, size - 1), done),
            dst_ref=recv.at[0 if size == 2 else side, t - 1],
            send_sem=ssem.at[side, t - 1],
            recv_sem=rsem.at[side, t - 1],
            device_id={"dp": peer},
            device_id_type=MESH,
        )

    def sends(i, size, t, side):
        return (i <= t - 1) if side == 0 else (i >= size - t)

    def line_step(phase, size, t, full, buffers, done):
        i = where[phase]
        for side in range(2):
            at_end = (i == 0) if side == 0 else (i == size - 1)
            j = size - t + i if side == 0 else t - size + i
            j = jnp.clip(j, 0, size - 1)

            @pl.when(sends(i, size, t, side))
            def _():
                if t > 1:
                    @pl.when(jnp.logical_not(at_end))
                    def _():
                        line_copy(phase, size, t - 1, side, full, buffers, done).wait_recv()
                        own = block_of(full, phase, j, done)
                        got = buffers[0][0 if size == 2 else side, t - 2]
                        own[...] = (own[...].astype(F32) + got.astype(F32)).astype(BF16)

                line_copy(phase, size, t, side, full, buffers, done).start()

    def line_final(kind, c, phase, size, full, buffers, done, last):
        i = where[phase]
        own = block_of(full, phase, i, done)
        total = own
        if last:
            slots = {
                "qkv": lambda: qkv_out.at[:, c * width : (c + 1) * width],
                "in": lambda: in_out.at[:, c * width : (c + 1) * width],
                "out": lambda: out_out,
                "down": lambda: down_out.at[:, c * (width // 4) : (c + 1) * (width // 4)],
                "extra": lambda: extra_sum.at[:, :, c * (width // 2) : (c + 1) * (width // 2)],
            }
            total = slots[kind]()
        lower, upper = i > 0, i < size - 1

        def arrived(side):
            line_copy(phase, size, size - 1, side, full, buffers, done).wait_recv()
            return buffers[0][0 if size == 2 else side, size - 2].astype(F32)

        @pl.when(lower & upper)
        def _():
            total[...] = (own[...].astype(F32) + arrived(0) + arrived(1)).astype(total.dtype)

        @pl.when(lower & jnp.logical_not(upper))
        def _():
            total[...] = (own[...].astype(F32) + arrived(0)).astype(total.dtype)

        @pl.when(jnp.logical_not(lower))
        def _():
            total[...] = (own[...].astype(F32) + arrived(1)).astype(total.dtype)

        if last and kind == "extra" and c == 1:
            for source_stage, out in ((0, embed_out), (stages - 1, head_out)):
                @pl.when(stage == source_stage)
                def _():
                    for offset in range(1, stages):
                        extra_copy(source_stage, offset, extra_recv[0 if source_stage == 0 else 1]).start()
                    out[...] = extra_sum[source_stage]

    def line_drain(phase, size, full, buffers, done):
        i = where[phase]
        for side in range(2):
            for t in range(1, size):
                @pl.when(sends(i, size, t, side))
                def _():
                    line_copy(phase, size, t, side, full, buffers, done).wait_send()

    extra_recv = take(2)
    drains = []
    chains = [chunk_steps(*item) for item in plan]
    depth = len(chains[0])
    vec_chain = [vec_step(k) for k in range(bits)] + [vec_last]
    starts, first, extra_rounds = [], 0, iter((1, 3, 5, 6, 7))
    for item in plan:
        if item[3]:
            starts.append(next(extra_rounds))
        else:
            starts.append(first)
            first += 1
    begun = False
    loaded_at = max(start for start, item in zip(starts, plan) if item[0] == "qkv" and item[1] == 0)
    for r in range(max(starts) + depth):
        for d in [0] + list(range(depth - 1, 0, -1)):
            for start, chain in zip(starts, chains):
                if r - start != d:
                    continue
                for part in chain[d]:
                    part()
                    if not begun:
                        begun = True
                        pl.semaphore_wait(barrier, devices - 1 + stages - 1)
        if 0 <= r - loaded_at < len(vec_chain):
            vec_chain[r - loaded_at]()
    vec_finish()
    for source_stage, out in ((0, embed_out), (stages - 1, head_out)):
        @pl.when(stage != source_stage)
        def _():
            got = extra_recv[0 if source_stage == 0 else 1]
            extra_copy(source_stage, 1, got).wait_recv()
            out[...] = got[...]

        @pl.when(stage == source_stage)
        def _():
            for offset in range(1, stages):
                extra_copy(source_stage, offset, extra_recv[0]).wait_send()

    vec_drain()
    for kind, drain in drains:
        if kind == "extra":
            gated([drain])()
        else:
            drain()


def run_gradients(stages, devices, saved, vec, token_ids):
    dims = line_dims(devices)
    rows, tokens, width = saved[0].shape
    hid, vocab = saved[3].shape[2], saved[8].shape[2]
    plan = chunk_plan(width, hid, vocab, stages, devices)
    saved = [member.reshape(rows * tokens, member.shape[2]) for member in saved]
    vmem = pl.BlockSpec(memory_space=pltpu.VMEM)
    hbm = pl.BlockSpec(memory_space=pl.ANY)
    bits = devices.bit_length() - 1
    share = vocab // (stages * devices)
    scratch = [pltpu.VMEM(member.shape, BF16) for member in saved]
    scratch += [pltpu.SemaphoreType.DMA((len(saved),))]
    scratch += [pltpu.VMEM((width, rows * tokens), BF16), pltpu.VMEM((vocab, rows * tokens), BF16)]
    scratch += [
        pltpu.VMEM((bits + 1,) + vec.shape, F32),
        pltpu.VMEM((bits,) + vec.shape, F32),
        pltpu.SemaphoreType.DMA((bits,)),
        pltpu.SemaphoreType.DMA((bits,)),
        pltpu.VMEM((8, width), F32),
        pltpu.VMEM((8, width), F32),
        pltpu.SemaphoreType.DMA((stages,)),
        pltpu.SemaphoreType.DMA((1,)),
        pltpu.VMEM((stages, share, width), F32),
        pltpu.SemaphoreType.DMA((stages,)),
        pltpu.SemaphoreType.DMA((2,)),
        pltpu.VMEM((share, width), F32),
        pltpu.VMEM((share, width), F32),
    ]
    sizes = [size for size, _ in reversed(dims)]
    for _, _, block, turned in plan:
        scratch.append(pltpu.VMEM(tuple(sizes) + block, BF16))
        remain = list(reversed(dims))
        for size, stride in dims[::-1] if turned else dims:
            remain.remove((size, stride))
            piece = tuple(other for other, _ in remain) + block
            scratch.append(pltpu.VMEM((1 if size == 2 else 2, size - 1) + piece, BF16))
            scratch += [pltpu.SemaphoreType.DMA((2, size - 1))] * 2
    return pl.pallas_call(
        functools.partial(gradient_kernel, stages, devices, plan),
        out_shape=[
            jax.ShapeDtypeStruct((width // devices, 3 * width), F32),
            jax.ShapeDtypeStruct((width // devices, width), F32),
            jax.ShapeDtypeStruct((width // devices, hid), F32),
            jax.ShapeDtypeStruct((hid // devices, width), F32),
            jax.ShapeDtypeStruct((share, width), F32),
            jax.ShapeDtypeStruct((share, width), F32),
            jax.ShapeDtypeStruct(vec.shape, F32),
        ],
        in_specs=[hbm] * len(saved) + [vmem] * 2,
        out_specs=[vmem] * 7,
        scratch_shapes=scratch,
        compiler_params=pltpu.CompilerParams(
            collective_id=1, has_side_effects=True, vmem_limit_bytes=62 * 1024 * 1024
        ),
        name="gradients",
    )(*saved, vec, token_ids)


def finish_kernel(devices, embed_g, qkv_g, out_g, in_g, down_g, head_g, vec, *outs):
    place = lax.axis_index("dp")
    width = vec.shape[1]
    (embed_o, qkv_o, qv_o, out_o, outb_o, in_o, inb_o, down_o, gain_o, shift_o, fg_o, fb_o, head_o) = outs
    embed_o[...] = embed_g[...]
    head_o[...] = head_g[...]
    for source, target in ((qkv_g, qkv_o), (out_g, out_o), (in_g, in_o), (down_g, down_o)):
        target[0] = source[...]
    lanes = width // devices
    turned = pltpu.roll(vec[0:8, :], lax.rem(width - place * lanes, width), 1)
    for row, out in ((V_QUERY, qv_o), (V_BRANCH, outb_o), (V_GAIN1, gain_o), (V_SHIFT1, shift_o)):
        out[0] = turned[row : row + 2, 0:lanes]
    share = inb_o.shape[1]
    first = place * share
    row = vec[pl.ds(V_HIDDEN + first // width, 1), :]
    wide = jnp.broadcast_to(row, (8, width))
    inb_o[...] = pltpu.roll(wide, lax.rem(width - lax.rem(first, width), width), 1)[0:1, 0:share]
    fg_o[...] = vec[V_FINAL_GAIN : V_FINAL_GAIN + 1, :]
    fb_o[...] = vec[V_FINAL_BIAS : V_FINAL_BIAS + 1, :]


def run_finish(devices, embed_g, qkv_g, out_g, in_g, down_g, head_g, vec):
    vmem = pl.BlockSpec(memory_space=pltpu.VMEM)
    width = vec.shape[1]
    lanes = width // devices

    def shape(*sizes):
        return jax.ShapeDtypeStruct(sizes, F32)

    pair = shape(1, 2, lanes)
    return pl.pallas_call(
        functools.partial(finish_kernel, devices),
        out_shape=[
            shape(*embed_g.shape),
            shape(1, *qkv_g.shape),
            pair,
            shape(1, *out_g.shape),
            pair,
            shape(1, *in_g.shape),
            shape(1, in_g.shape[1] // devices),
            shape(1, *down_g.shape),
            pair,
            pair,
            shape(1, width),
            shape(1, width),
            shape(*head_g.shape),
        ],
        in_specs=[vmem] * 7,
        out_specs=[vmem] * 13,
        name="finish",
    )(embed_g, qkv_g, out_g, in_g, down_g, head_g, vec)


def on_device(
    token_ids,
    segment_ids,
    target_ids,
    embed_table,
    qkv_weight,
    qv_bias,
    out_weight,
    out_biases,
    ff_in,
    ff_in_bias,
    ff_out,
    norm_gains,
    norm_biases,
    final_gain,
    final_bias,
    head_weight,
):
    stages = lax.axis_size("pipe")
    devices = lax.axis_size("dp")
    params = (
        embed_table,
        qkv_weight[0],
        qv_bias[0],
        out_weight[0],
        out_biases[0],
        ff_in[0],
        ff_in_bias,
        ff_out[0],
        norm_gains[0],
        norm_biases[0],
        final_gain[None],
        final_bias[None],
        head_weight,
    )
    *saved, vec = run_pipeline(stages, token_ids, segment_ids, target_ids, params)
    qkv_g, out_g, in_g, down_g, embed_g, head_g, sums = run_gradients(stages, devices, saved, vec, token_ids)
    done = list(run_finish(devices, embed_g, qkv_g, out_g, in_g, down_g, head_g, sums))
    done[10], done[11] = done[10][0], done[11][0]
    return tuple(done)


def solution(mesh):
    layer3 = P("pipe", None, None)
    return jax.shard_map(
        on_device,
        mesh=mesh,
        in_specs=(
            P("dp", None),
            P("dp", None),
            P("dp", None),
            P(),
            layer3,
            layer3,
            layer3,
            layer3,
            layer3,
            P("pipe", None),
            layer3,
            layer3,
            layer3,
            P(),
            P(),
            P(),
        ),
        out_specs=(
            P(("pipe", "dp"), None),
            P("pipe", "dp", None),
            P("pipe", None, "dp"),
            P("pipe", "dp", None),
            P("pipe", None, "dp"),
            P("pipe", "dp", None),
            P("pipe", "dp"),
            P("pipe", "dp", None),
            P("pipe", None, "dp"),
            P("pipe", None, "dp"),
            P(),
            P(),
            P(("pipe", "dp"), None),
        ),
        check_vma=False,
    )
```

```python
import functools

import jax
import jax.numpy as jnp
from jax import lax
from jax.experimental import pallas as pl
from jax.experimental.pallas import tpu as pltpu
from jax.sharding import PartitionSpec as P

HEADS = 8
FRAME = 6
ROW = 128
GROUP = 2
MASKED = -1e30
GELU_A = 0.7978845608
GELU_B = 0.044715
MESH = pl.DeviceIdType.MESH
F32 = jnp.float32
BF16 = jnp.bfloat16

VEC_ROWS = 16
V_QUERY, V_VALUE, V_BRANCH, V_RESULT, V_GAIN1, V_GAIN2, V_SHIFT1, V_SHIFT2 = range(8)
V_HIDDEN = 8
V_FINAL_GAIN, V_FINAL_BIAS = 12, 13


def dot(a, b):
    return lax.dot_general(a, b, (((1,), (0,)), ((), ())), preferred_element_type=F32)


def dot_nt(a, b):
    return lax.dot_general(a, b, (((1,), (1,)), ((), ())), preferred_element_type=F32)


def dot_tn(a, b):
    return lax.dot_general(a, b, (((0,), (0,)), ((), ())), preferred_element_type=F32)


def normalise(values):
    centre = jnp.mean(values, axis=-1, keepdims=True)
    centered = values - centre
    spread = jnp.mean(centered * centered, axis=-1, keepdims=True)
    scale = lax.rsqrt(spread + 1e-05)
    return centered * scale, scale


def norm_backward(grad, normal, scale, gain):
    grad_n = grad * gain
    mean_grad = jnp.mean(grad_n, axis=-1, keepdims=True)
    mean_proj = jnp.mean(grad_n * normal, axis=-1, keepdims=True)
    return scale * (grad_n - mean_grad - normal * mean_proj)


def column_sum(values):
    return jnp.sum(values, axis=0, keepdims=True)


def stack_pair(pair, low_lanes):
    zero = jnp.zeros_like(pair)
    return jnp.concatenate(
        [jnp.where(low_lanes, pair, zero), jnp.where(low_lanes, zero, pair)], axis=0
    )


def join_pair(stacked, low_lanes):
    half = stacked.shape[0] // 2
    return jnp.where(low_lanes, stacked[:half], stacked[half:])


def pipeline_kernel(
    stages,
    micros,
    token_ids,
    segment_ids,
    target_ids,
    embed,
    qkv_w,
    qv_b,
    out_w,
    out_b,
    in_w,
    in_b,
    down_w,
    gains,
    shifts,
    fin_gain,
    fin_bias,
    head_w,
    normed_o,
    mixed_o,
    normed2_o,
    active_o,
    gres_o,
    ghid_o,
    gbr_o,
    gproj_o,
    xl_o,
    xr_o,
    vec,
    instream,
    outb,
    gin,
    gs,
    normed,
    proj,
    probs,
    mixed,
    middle,
    normed2,
    active,
    slope,
    lo,
    go,
    gmid,
    s_gres,
    s_ghid,
    s_gbr,
    s_gproj,
    s_xl,
    ids,
    frames,
    fsend,
    frecv,
    bsend,
    brecv,
    osem,
):
    stage = lax.axis_index("pipe")
    tokens, width = instream.shape[1], instream.shape[2]
    hidden_n = in_b.shape[1]
    vocab = head_w.shape[0]
    pairs = width // ROW
    chunk = 512
    is_first = stage == 0
    is_last = stage == stages - 1
    up = jnp.minimum(stage + 1, stages - 1)
    down = jnp.maximum(stage - 1, 0)

    barrier = pltpu.get_barrier_semaphore()

    @pl.when(jnp.logical_not(is_first))
    def _():
        pl.semaphore_signal(barrier, inc=1, device_id={"pipe": down}, device_id_type=MESH)

    @pl.when(jnp.logical_not(is_last))
    def _():
        pl.semaphore_signal(barrier, inc=1, device_id={"pipe": up}, device_id_type=MESH)

    pl.semaphore_wait(barrier, jnp.where(is_first | is_last, 1, 2))
    vec[...] = jnp.zeros_like(vec)
    rows_n, seq = token_ids.shape
    for index, member in enumerate((token_ids, segment_ids, target_ids)):
        ids[index] = jnp.full(ids.shape[1:], 4.0 if index == 1 else -1.0, F32)
        ids[index, 0:rows_n, 0:seq] = member[...].astype(F32)
    at_query = lax.broadcasted_iota(jnp.int32, (ROW, ROW), 1)
    at_key = lax.broadcasted_iota(jnp.int32, (ROW, ROW), 0)
    frames[...] = jnp.where(at_key < ((at_query * 43) // 256) * FRAME + FRAME, 1.0, 0.0)

    def column(index, row):
        values = jnp.broadcast_to(ids[index, pl.ds(row, 1), :], (8, ROW))
        return values.T[:, 0:1]

    def hot_rows(index, m):
        parts = [column(index, m * GROUP + r) for r in range(GROUP)]
        values = jnp.concatenate(parts, axis=0)
        places = lax.broadcasted_iota(jnp.int32, (tokens, vocab), 1).astype(F32)
        return values, jnp.where(values == places, 1.0, 0.0)

    def forward_copy(m):
        return pltpu.make_async_remote_copy(
            src_ref=outb.at[m],
            dst_ref=instream.at[m],
            send_sem=fsend.at[m],
            recv_sem=frecv.at[m],
            device_id={"pipe": up},
            device_id_type=MESH,
        )

    def backward_copy(m):
        return pltpu.make_async_remote_copy(
            src_ref=gs.at[m],
            dst_ref=gin.at[m],
            send_sem=bsend.at[m],
            recv_sem=brecv.at[m],
            device_id={"pipe": down},
            device_id_type=MESH,
        )

    def save(index, src, dst, m):
        return pltpu.make_async_copy(src, dst.at[m], osem.at[index, m])

    def saves_forward(m):
        return [
            save(0, normed.at[m], normed_o, m),
            save(1, mixed.at[m], mixed_o, m),
            save(2, normed2.at[m], normed2_o, m),
            save(3, active.at[m], active_o, m),
        ]

    def saves_backward(m):
        slot = lax.rem(m, 2)
        return [
            save(4, s_gres.at[slot], gres_o, m),
            save(5, s_ghid.at[slot], ghid_o, m),
            save(6, s_gbr.at[slot], gbr_o, m),
            save(7, s_gproj.at[slot], gproj_o, m),
        ]

    def save_xl(m):
        return save(8, s_xl.at[lax.rem(m, 2)], xl_o, m)

    def put_xl(m, value):
        @pl.when(m >= 2)
        def _():
            save_xl(m - 2).wait()

        s_xl[lax.rem(m, 2)] = value
        save_xl(m).start()

    lane_low = lax.broadcasted_iota(jnp.int32, (ROW, ROW), 1) < ROW // 2

    def forward(m):
        @pl.when(is_first)
        def _():
            hot = hot_rows(0, m)[1].astype(BF16)
            instream[m] = dot(hot, embed[...]).astype(BF16)

        @pl.when(jnp.logical_not(is_first))
        def _():
            forward_copy(m).wait_recv()

        normal, _ = normalise(instream[m].astype(F32))
        normed[m] = (normal * gains[0:1, :] + shifts[0:1, :]).astype(BF16)
        low = normed[m]
        queries = dot(low, qkv_w[:, 0:width]) + qv_b[0:1, :]
        proj[m, :, 0:width] = (queries * (ROW // 2) ** -0.5).astype(BF16)
        proj[m, :, width : 2 * width] = dot(low, qkv_w[:, width : 2 * width]).astype(BF16)
        proj[m, :, 2 * width : 3 * width] = (
            dot(low, qkv_w[:, 2 * width : 3 * width]) + qv_b[1:2, :]
        ).astype(BF16)
        masks, scores = [], []
        for r in range(GROUP):
            rows = slice(r * ROW, (r + 1) * ROW)
            kinds = lax.broadcasted_iota(jnp.int32, (16, ROW), 0).astype(F32)
            member = jnp.where(ids[1, pl.ds(m * GROUP + r, 1), :] == kinds, 1.0, 0.0).astype(BF16)
            mask = jnp.where(dot_tn(member, member) * frames[...] > 0.5, 0.0, MASKED)
            masks.append(jnp.concatenate([mask, mask], axis=1))
            for p in range(pairs):
                q = stack_pair(proj[m, rows, p * ROW : (p + 1) * ROW], lane_low)
                k = proj[m, rows, width + p * ROW : width + (p + 1) * ROW]
                scores.append(dot_nt(k, q))

        def mix(unit):
            r, p = unit // pairs, unit % pairs
            rows = slice(r * ROW, (r + 1) * ROW)
            v = proj[m, rows, 2 * width + p * ROW : 2 * width + (p + 1) * ROW]
            both = dot_tn(probs[m, unit], v)
            mixed[m, rows, p * ROW : (p + 1) * ROW] = join_pair(both, lane_low).astype(BF16)

        for unit in range(GROUP * pairs):
            masked = scores[unit] + masks[unit // pairs]
            expo = jnp.exp(masked - jnp.max(masked, axis=0, keepdims=True))
            total = jnp.sum(expo, axis=0, keepdims=True)
            probs[m, unit] = (expo * (1.0 / total)).astype(BF16)
            if unit:
                mix(unit - 1)
        mix(GROUP * pairs - 1)
        mid = instream[m].astype(F32) + (dot(mixed[m], out_w[...]) + out_b[0:1, :])
        middle[m] = mid
        normal2, _ = normalise(mid)
        normed2[m] = (normal2 * gains[1:2, :] + shifts[1:2, :]).astype(BF16)
        low2 = normed2[m]
        parts = hidden_n // chunk

        def spread(c):
            return dot(low2, in_w[:, c * chunk : (c + 1) * chunk])

        total, ahead = None, spread(0)
        for c in range(parts):
            cols = slice(c * chunk, (c + 1) * chunk)
            hid = ahead + in_b[0:1, cols]
            if c + 1 < parts:
                ahead = spread(c + 1)
            square = hid * hid
            tan = jnp.tanh(hid * (GELU_A + (GELU_A * GELU_B) * square))
            half = 0.5 + 0.5 * tan
            act = (hid * half).astype(BF16)
            active[m, :, cols] = act
            rise = (1.0 - tan * tan) * (0.5 * GELU_A + (1.5 * GELU_A * GELU_B) * square)
            slope[m, :, cols] = (half + hid * rise).astype(BF16)
            term = dot(act, down_w[cols, :])
            total = term if total is None else total + term
        for copy in saves_forward(m):
            copy.start()
        lo[...] = middle[m] + (total + out_b[1:2, :])

        @pl.when(jnp.logical_not(is_last))
        def _():
            outb[m] = lo[...].astype(BF16)
            forward_copy(m).start()

    def head(m):
        normal, scale = normalise(lo[...])
        outb[m] = (normal * fin_gain[...] + fin_bias[...]).astype(BF16)
        save(9, outb.at[m], xr_o, m).start()
        logits = dot_nt(outb[m], head_w[...])
        top = jnp.max(logits, axis=-1, keepdims=True)
        expo = jnp.exp(logits - top)
        total = jnp.sum(expo, axis=-1, keepdims=True)
        target, hot = hot_rows(2, m)
        grad_logits = jnp.where(target >= 0.0, expo * (1.0 / total) - hot, 0.0).astype(BF16)
        put_xl(m, grad_logits)
        grad_final = dot(grad_logits, head_w[...])
        vec[V_FINAL_GAIN : V_FINAL_GAIN + 1, :] += column_sum(grad_final * normal)
        vec[V_FINAL_BIAS : V_FINAL_BIAS + 1, :] += column_sum(grad_final)
        go[...] = norm_backward(grad_final, normal, scale, fin_gain[...])

    def backward(m):
        slot = lax.rem(m, 2)

        @pl.when(m >= 2)
        def _():
            for copy in saves_backward(m - 2):
                copy.wait()

        @pl.when(jnp.logical_not(is_last))
        def _():
            backward_copy(m).wait_recv()
            go[...] = gin[m].astype(F32)

        s_gres[slot] = go[...].astype(BF16)
        gres = s_gres[slot]
        parts = hidden_n // chunk

        def spread(c):
            return dot_nt(gres, down_w[c * chunk : (c + 1) * chunk, :])

        total, ahead = None, spread(0)
        for c in range(parts):
            cols = slice(c * chunk, (c + 1) * chunk)
            gact = ahead
            if c + 1 < parts:
                ahead = spread(c + 1)
            ghid = (gact * slope[m, :, cols].astype(F32)).astype(BF16)
            s_ghid[slot, :, cols] = ghid
            term = dot_nt(ghid, in_w[:, cols])
            total = term if total is None else total + term
        normal2, scale2 = normalise(middle[m])
        vec[V_GAIN2 : V_GAIN2 + 1, :] += column_sum(total * normal2)
        vec[V_SHIFT2 : V_SHIFT2 + 1, :] += column_sum(total)
        gmid[...] = go[...] + norm_backward(total, normal2, scale2, gains[1:2, :])
        s_gbr[slot] = gmid[...].astype(BF16)
        gbr = s_gbr[slot]
        gmix = dot_nt(gbr, out_w[...]).astype(BF16)
        grads = []
        for r in range(GROUP):
            rows = slice(r * ROW, (r + 1) * ROW)
            for p in range(pairs):
                gm = stack_pair(gmix[rows, p * ROW : (p + 1) * ROW], lane_low)
                vlanes = slice(2 * width + p * ROW, 2 * width + (p + 1) * ROW)
                grads.append(dot_nt(proj[m, rows, vlanes], gm))
                s_gproj[slot, rows, vlanes] = dot(probs[m, r * pairs + p], gm).astype(BF16)

        def pull(unit, gsc):
            r, p = unit // pairs, unit % pairs
            rows = slice(r * ROW, (r + 1) * ROW)
            lanes = slice(p * ROW, (p + 1) * ROW)
            klanes = slice(width + p * ROW, width + (p + 1) * ROW)
            q = stack_pair(proj[m, rows, lanes], lane_low)
            s_gproj[slot, rows, klanes] = dot(gsc, q).astype(BF16)
            gq = join_pair(dot_tn(gsc, proj[m, rows, klanes]), lane_low) * (ROW // 2) ** -0.5
            s_gproj[slot, rows, lanes] = gq.astype(BF16)

        waiting = None
        for unit in range(GROUP * pairs):
            weights = probs[m, unit].astype(F32)
            inner = jnp.sum(weights * grads[unit], axis=0, keepdims=True)
            gsc = (weights * (grads[unit] - inner)).astype(BF16)
            if waiting is not None:
                pull(unit - 1, waiting)
            waiting = gsc
        pull(GROUP * pairs - 1, waiting)
        for copy in saves_backward(m):
            copy.start()
        gproj = s_gproj[slot]
        gnormed = dot_nt(gproj, qkv_w[...])
        normal, scale = normalise(instream[m].astype(F32))
        vec[V_GAIN1 : V_GAIN1 + 1, :] += column_sum(gnormed * normal)
        vec[V_SHIFT1 : V_SHIFT1 + 1, :] += column_sum(gnormed)
        gs[m] = (gmid[...] + norm_backward(gnormed, normal, scale, gains[0:1, :])).astype(BF16)

        @pl.when(is_first)
        def _():
            save(9, gs.at[m], xr_o, m).start()

        @pl.when(jnp.logical_not(is_first))
        def _():
            backward_copy(m).start()

    def tick(t, carry):
        m_forward = t - stage
        m_backward = t - (2 * (stages - 1) - stage)

        @pl.when((m_forward >= 0) & (m_forward < micros))
        def _():
            forward(m_forward)

        @pl.when((m_backward >= 0) & (m_backward < micros))
        def _():
            @pl.when(is_last)
            def _():
                head(m_backward)

            backward(m_backward)

        return carry

    lax.fori_loop(0, micros + 2 * (stages - 1), tick, 0)

    for m in range(micros):
        for copy in saves_forward(m):
            copy.wait()

        @pl.when(jnp.logical_not(is_last))
        def _():
            forward_copy(m).wait_send()

        @pl.when(jnp.logical_not(is_first))
        def _():
            backward_copy(m).wait_send()

        @pl.when(is_first)
        def _():
            save(9, gs.at[m], xr_o, m).wait()

        @pl.when(is_last)
        def _():
            save(9, outb.at[m], xr_o, m).wait()

    for m in range(max(0, micros - 2), micros):
        for copy in saves_backward(m):
            copy.wait()

        @pl.when(is_last)
        def _():
            save_xl(m).wait()


def run_pipeline(stages, token_ids, segment_ids, target_ids, params):
    embed, in_w, head_w = params[0], params[5], params[12]
    width = embed.shape[1]
    vocab = head_w.shape[0]
    hid = in_w.shape[1]
    tokens = GROUP * ROW
    micros = token_ids.shape[0] // GROUP
    pairs = width // ROW
    vmem = pl.BlockSpec(memory_space=pltpu.VMEM)
    hbm = pl.BlockSpec(memory_space=pl.ANY)

    def kept(columns):
        return jax.ShapeDtypeStruct((micros, tokens, columns), BF16)

    def scratch(lead, columns, kind=BF16):
        return pltpu.VMEM((lead, tokens, columns), kind)

    out_shape = [
        kept(width),
        kept(width),
        kept(width),
        kept(hid),
        kept(width),
        kept(hid),
        kept(width),
        kept(3 * width),
        kept(vocab),
        kept(width),
        jax.ShapeDtypeStruct((VEC_ROWS, width), F32),
    ]
    return pl.pallas_call(
        functools.partial(pipeline_kernel, stages, micros),
        out_shape=out_shape,
        in_specs=[vmem] * 16,
        out_specs=[hbm] * 10 + [vmem],
        scratch_shapes=[
            scratch(micros, width),
            scratch(micros, width),
            scratch(micros, width),
            scratch(micros, width),
            scratch(micros, width),
            scratch(micros, 3 * width),
            pltpu.VMEM((micros, GROUP * pairs, ROW, 2 * ROW), BF16),
            scratch(micros, width),
            scratch(micros, width, F32),
            scratch(micros, width),
            scratch(micros, hid),
            scratch(micros, hid),
            pltpu.VMEM((tokens, width), F32),
            pltpu.VMEM((tokens, width), F32),
            pltpu.VMEM((tokens, width), F32),
            scratch(2, width),
            scratch(2, hid),
            scratch(2, width),
            scratch(2, 3 * width),
            scratch(2, vocab),
            pltpu.VMEM((3, 16, ROW), F32),
            pltpu.VMEM((ROW, ROW), F32),
            pltpu.SemaphoreType.DMA((micros,)),
            pltpu.SemaphoreType.DMA((micros,)),
            pltpu.SemaphoreType.DMA((micros,)),
            pltpu.SemaphoreType.DMA((micros,)),
            pltpu.SemaphoreType.DMA((10, micros)),
        ],
        compiler_params=pltpu.CompilerParams(
            collective_id=0, has_side_effects=True, vmem_limit_bytes=62 * 1024 * 1024
        ),
        name="pipeline",
    )(token_ids, segment_ids, target_ids, *params)


def line_dims(devices):
    dims, stride = [], 1
    if devices == 8:
        return [(2, 1), (4, 2)]
    while devices > 1:
        size = 4 if devices % 4 == 0 else 2
        dims.append((size, stride))
        stride *= size
        devices //= size
    return dims


def chunk_plan(width, hid, vocab, stages, devices):
    slim, deep = width // devices, hid // devices
    plan = [("out", 0, (slim, width), False)]
    for c in range(4):
        plan.append(("down", c, (deep, width // 4), c in (1, 3)))
    for c in range(2):
        plan.append(("extra", c, (stages, vocab // (stages * devices), width // 2), False))
    for c in range(hid // width):
        plan.append(("in", c, (slim, width), c == 1))
    for c in range(3):
        plan.append(("qkv", c, (slim, width), False))
    return plan


def gradient_kernel(stages, devices, plan, *refs):
    dims = line_dims(devices)
    refs = list(refs)

    def take(amount):
        head, refs[:] = refs[:amount], refs[amount:]
        return head

    inputs = take(10)
    vec_in, token_ids = take(2)
    qkv_out, out_out, in_out, down_out, embed_out, head_out, vec_out = take(7)
    local = take(10)
    in_sem = take(1)[0]
    turned_left, turned_xl = take(2)
    mats = dict(
        zip(
            ("normed", "mixed", "normed2", "active", "gres", "ghid", "gbr", "gproj", "xl", "xr"),
            local,
        )
    )
    names = list(mats)
    stage = lax.axis_index("pipe")
    place = lax.axis_index("dp")
    is_extra = (stage == 0) | (stage == stages - 1)
    width = mats["normed"].shape[1]
    where = [lax.rem(place // stride, size) for size, stride in dims]

    barrier = pltpu.get_barrier_semaphore()

    def greet(offset, carry):
        peer = lax.rem(place + offset, devices)
        pl.semaphore_signal(barrier, inc=1, device_id={"dp": peer}, device_id_type=MESH)
        return carry

    def greet_stage(offset, carry):
        peer = lax.rem(stage + offset, stages)
        pl.semaphore_signal(barrier, inc=1, device_id={"pipe": peer}, device_id_type=MESH)
        return carry

    lax.fori_loop(1, devices, greet, 0)
    lax.fori_loop(1, stages, greet_stage, 0)

    def load(name):
        i = names.index(name)
        return pltpu.make_async_copy(inputs[i], mats[name], in_sem.at[i])

    groups = [("mixed", "gbr"), ("gres", "active"), ("xr", "xl"), ("normed2", "ghid"), ("normed", "gproj")]

    def fetch(at):
        if at >= len(groups):
            return
        if groups[at] == ("xr", "xl"):
            @pl.when(is_extra)
            def _():
                load("xr").start()

            @pl.when(stage == stages - 1)
            def _():
                load("xl").start()

            at += 1
        for name in groups[at]:
            load(name).start()

    fetch(0)
    loaded = set()

    def need(*wanted):
        fresh = [name for name in wanted if name not in loaded]
        for name in fresh:
            loaded.add(name)
            load(name).wait()
        if fresh:
            at = [i for i, group in enumerate(groups) if group[0] == fresh[0]][0]
            fetch(at + 1)

    def identity(size):
        here = lax.broadcasted_iota(jnp.int32, (size, size), 0)
        there = lax.broadcasted_iota(jnp.int32, (size, size), 1)
        return jnp.where(here == there, 1.0, 0.0).astype(BF16)

    held = []

    def turn(name):
        if held[-1:] == [name]:
            return
        held.append(name)
        unit = identity(256)
        for q in range(width // 256):
            part = dot_nt(unit, mats[name][:, q * 256 : (q + 1) * 256])
            turned_left[q * 256 : (q + 1) * 256, :] = part.astype(BF16)

    bits = devices.bit_length() - 1
    vec_send, vec_recv = take(2)
    vec_sems = take(2)

    def vec_copy(k):
        peer = jnp.bitwise_xor(place, 1 << k)
        return pltpu.make_async_remote_copy(
            src_ref=vec_send.at[k],
            dst_ref=vec_recv.at[k],
            send_sem=vec_sems[0].at[k],
            recv_sem=vec_sems[1].at[k],
            device_id={"dp": peer},
            device_id_type=MESH,
        )

    def vec_step(k):
        def run():
            if k == 0:
                vec_send[0] = vec_in[...]
                ones = jnp.ones((16, mats["gres"].shape[0]), BF16)
                for name, start, row in (
                    ("gproj", 0, V_QUERY),
                    ("gproj", 2 * width, V_VALUE),
                    ("gbr", 0, V_BRANCH),
                    ("gres", 0, V_RESULT),
                ):
                    part = dot(ones, mats[name][:, start : start + width])
                    vec_send[0, row : row + 1, :] = part[0:1, :]
                for q in range(mats["ghid"].shape[1] // width):
                    part = dot(ones, mats["ghid"][:, q * width : (q + 1) * width])
                    vec_send[0, V_HIDDEN + q : V_HIDDEN + q + 1, :] = part[0:1, :]
            else:
                vec_copy(k - 1).wait_recv()
                vec_send[k] = vec_send[k - 1] + vec_recv[k - 1]
            if k < bits:
                vec_copy(k).start()

        return run

    final_send, final_recv = take(2)
    final_sems = take(2)

    def final_copy(offset):
        peer = lax.rem(stages - 1 + offset, stages)
        return pltpu.make_async_remote_copy(
            src_ref=final_send,
            dst_ref=final_recv,
            send_sem=final_sems[0].at[offset],
            recv_sem=final_sems[1].at[0],
            device_id={"pipe": peer},
            device_id_type=MESH,
        )

    def vec_last():
        vec_step(bits)()
        vec_out[...] = vec_send[bits]

        @pl.when(stage == stages - 1)
        def _():
            final_send[...] = vec_send[bits, 8:16, :]
            for offset in range(1, stages):
                final_copy(offset).start()

    def vec_finish():
        @pl.when(stage != stages - 1)
        def _():
            final_copy(1).wait_recv()
            vec_out[V_FINAL_GAIN : V_FINAL_BIAS + 1, :] = final_recv[
                V_FINAL_GAIN - 8 : V_FINAL_BIAS - 7, :
            ]

    def vec_drain():
        for k in range(bits):
            vec_copy(k).wait_send()

        @pl.when(stage == stages - 1)
        def _():
            for offset in range(1, stages):
                final_copy(offset).wait_send()

    extra_sum, extra_send_sem, extra_recv_sem = take(3)

    def extra_copy(source, offset, target):
        peer = lax.rem(source + offset, stages)
        return pltpu.make_async_remote_copy(
            src_ref=extra_sum.at[peer],
            dst_ref=target,
            send_sem=extra_send_sem.at[offset],
            recv_sem=extra_recv_sem.at[0 if source == 0 else 1],
            device_id={"pipe": peer},
            device_id_type=MESH,
        )

    down_full = {}

    def chunk_steps(kind, c, block, turned):
        order = list(range(len(dims)))
        if turned:
            order.reverse()
        full = take(1)[0]

        def compute():
            if kind == "down":
                need("gres", "active")
                turn("gres")
                if c % 2 == 1:
                    return
                half = width // 2
                lines = slice((c // 2) * half, (c // 2 + 1) * half)
                parts = dot(turned_left[lines, :], mats["active"][...]).astype(BF16)
                depth = block[0]
                unit = identity(depth)
                for d in range(devices):
                    back = dot_nt(unit, parts[:, d * depth : (d + 1) * depth]).astype(BF16)
                    down_full[c][split(d)] = back[:, 0 : half // 2]
                    down_full[c + 1][split(d)] = back[:, half // 2 : half]
            elif kind == "extra":
                vocab = turned_xl.shape[0]
                if c == 0:
                    load("xr").wait()

                @pl.when((stage == 0) & (c == 0))
                def _():
                    rows_n, seq = token_ids.shape
                    places = lax.broadcasted_iota(jnp.int32, (vocab, ROW), 0)
                    gap = jnp.full((1, ROW - seq), -1, jnp.int32)
                    for r in range(rows_n):
                        row = jnp.concatenate([token_ids[r : r + 1, :], gap], axis=1)
                        hot = jnp.where(places == row, 1.0, 0.0)
                        turned_xl[:, r * ROW : (r + 1) * ROW] = hot.astype(BF16)

                @pl.when((stage == stages - 1) & (c == 0))
                def _():
                    load("xl").wait()
                    unit = identity(256)
                    for q in range(vocab // 256):
                        part = dot_nt(unit, mats["xl"][:, q * 256 : (q + 1) * 256])
                        turned_xl[q * 256 : (q + 1) * 256, :] = part.astype(BF16)

                rows = vocab // stages
                for p in range(stages):
                    part = dot(
                        turned_xl[p * rows : (p + 1) * rows, :],
                        mats["xr"][:, c * (width // 2) : (c + 1) * (width // 2)],
                    )
                    part = part.astype(BF16).reshape((devices,) + block[1:])
                    for d in range(devices):
                        full[split(d) + (p,)] = part[d]
            else:
                left, right = {
                    "in": ("normed2", "ghid"),
                    "out": ("mixed", "gbr"),
                    "qkv": ("normed", "gproj"),
                }[kind]
                need(left, right)
                turn(left)
                cols = slice(c * width, (c + 1) * width)
                part = dot(turned_left[...], mats[right][:, cols]).astype(BF16)
                part = part.reshape((devices,) + block)
                for d in range(devices):
                    full[split(d)] = part[d]

        def split(d):
            return tuple((d // stride) % size for size, stride in reversed(dims))

        if kind == "down":
            down_full[c] = full
        steps = [[compute]]
        for at, phase in enumerate(order):
            size = dims[phase][0]
            buffers = take(3)
            done = order[:at]
            last = at == len(order) - 1
            steps[-1].append(functools.partial(line_step, phase, size, 1, full, buffers, done))
            for t in range(2, size):
                steps.append([functools.partial(line_step, phase, size, t, full, buffers, done)])
            drains.append((kind, functools.partial(line_drain, phase, size, full, buffers, done)))
            steps.append([functools.partial(line_final, kind, c, phase, size, full, buffers, done, last)])
        if kind == "extra":
            steps = [[gated([part]) for part in step] for step in steps]
        return steps

    def gated(step):
        def run():
            @pl.when(is_extra)
            def _():
                for part in step:
                    part()

        return run

    def block_of(full, phase, j, done):
        spot = [slice(None)] * len(dims)
        for other in done:
            spot[len(dims) - 1 - other] = where[other]
        spot[len(dims) - 1 - phase] = j
        return full.at[tuple(spot)]

    def line_copy(phase, size, t, side, full, buffers, done):
        recv, ssem, rsem = buffers
        i = where[phase]
        stride = dims[phase][1]
        if side == 0:
            j, peer = size - t + i, place + jnp.where(i < size - 1, stride, 0)
        else:
            j, peer = t - size + i, place - jnp.where(i > 0, stride, 0)
        return pltpu.make_async_remote_copy(
            src_ref=block_of(full, phase, jnp.clip(j, 0, size - 1), done),
            dst_ref=recv.at[0 if size == 2 else side, t - 1],
            send_sem=ssem.at[side, t - 1],
            recv_sem=rsem.at[side, t - 1],
            device_id={"dp": peer},
            device_id_type=MESH,
        )

    def sends(i, size, t, side):
        return (i <= t - 1) if side == 0 else (i >= size - t)

    def line_step(phase, size, t, full, buffers, done):
        i = where[phase]
        for side in range(2):
            at_end = (i == 0) if side == 0 else (i == size - 1)
            j = size - t + i if side == 0 else t - size + i
            j = jnp.clip(j, 0, size - 1)

            @pl.when(sends(i, size, t, side))
            def _():
                if t > 1:
                    @pl.when(jnp.logical_not(at_end))
                    def _():
                        line_copy(phase, size, t - 1, side, full, buffers, done).wait_recv()
                        own = block_of(full, phase, j, done)
                        got = buffers[0][0 if size == 2 else side, t - 2]
                        own[...] = (own[...].astype(F32) + got.astype(F32)).astype(BF16)

                line_copy(phase, size, t, side, full, buffers, done).start()

    def line_final(kind, c, phase, size, full, buffers, done, last):
        i = where[phase]
        own = block_of(full, phase, i, done)
        total = own
        if last:
            slots = {
                "qkv": lambda: qkv_out.at[:, c * width : (c + 1) * width],
                "in": lambda: in_out.at[:, c * width : (c + 1) * width],
                "out": lambda: out_out,
                "down": lambda: down_out.at[:, c * (width // 4) : (c + 1) * (width // 4)],
                "extra": lambda: extra_sum.at[:, :, c * (width // 2) : (c + 1) * (width // 2)],
            }
            total = slots[kind]()
        lower, upper = i > 0, i < size - 1

        def arrived(side):
            line_copy(phase, size, size - 1, side, full, buffers, done).wait_recv()
            return buffers[0][0 if size == 2 else side, size - 2].astype(F32)

        @pl.when(lower & upper)
        def _():
            total[...] = (own[...].astype(F32) + arrived(0) + arrived(1)).astype(total.dtype)

        @pl.when(lower & jnp.logical_not(upper))
        def _():
            total[...] = (own[...].astype(F32) + arrived(0)).astype(total.dtype)

        @pl.when(jnp.logical_not(lower))
        def _():
            total[...] = (own[...].astype(F32) + arrived(1)).astype(total.dtype)

        if last and kind == "extra" and c == 1:
            for source_stage, out in ((0, embed_out), (stages - 1, head_out)):
                @pl.when(stage == source_stage)
                def _():
                    for offset in range(1, stages):
                        extra_copy(source_stage, offset, extra_recv[0 if source_stage == 0 else 1]).start()
                    out[...] = extra_sum[source_stage]

    def line_drain(phase, size, full, buffers, done):
        i = where[phase]
        for side in range(2):
            for t in range(1, size):
                @pl.when(sends(i, size, t, side))
                def _():
                    line_copy(phase, size, t, side, full, buffers, done).wait_send()

    extra_recv = take(2)
    drains = []
    chains = [chunk_steps(*item) for item in plan]
    depth = len(chains[0])
    vec_chain = [vec_step(k) for k in range(bits)] + [vec_last]
    starts, first, extra_rounds = [], 0, iter((1, 3, 6, 8))
    for item in plan:
        if item[3]:
            starts.append(next(extra_rounds))
        else:
            starts.append(first)
            first += 1
    begun = False
    loaded_at = max(start for start, item in zip(starts, plan) if item[0] == "qkv" and item[1] == 0)
    for r in range(max(starts) + depth):
        for d in [0] + list(range(depth - 1, 0, -1)):
            for start, chain in zip(starts, chains):
                if r - start != d:
                    continue
                for part in chain[d]:
                    part()
                    if not begun:
                        begun = True
                        pl.semaphore_wait(barrier, devices - 1 + stages - 1)
        if 0 <= r - loaded_at < len(vec_chain):
            vec_chain[r - loaded_at]()
    vec_finish()
    for source_stage, out in ((0, embed_out), (stages - 1, head_out)):
        @pl.when(stage != source_stage)
        def _():
            got = extra_recv[0 if source_stage == 0 else 1]
            extra_copy(source_stage, 1, got).wait_recv()
            out[...] = got[...]

        @pl.when(stage == source_stage)
        def _():
            for offset in range(1, stages):
                extra_copy(source_stage, offset, extra_recv[0]).wait_send()

    vec_drain()
    for kind, drain in drains:
        if kind == "extra":
            gated([drain])()
        else:
            drain()


def run_gradients(stages, devices, saved, vec, token_ids):
    dims = line_dims(devices)
    rows, tokens, width = saved[0].shape
    hid, vocab = saved[3].shape[2], saved[8].shape[2]
    plan = chunk_plan(width, hid, vocab, stages, devices)
    saved = [member.reshape(rows * tokens, member.shape[2]) for member in saved]
    vmem = pl.BlockSpec(memory_space=pltpu.VMEM)
    hbm = pl.BlockSpec(memory_space=pl.ANY)
    bits = devices.bit_length() - 1
    share = vocab // (stages * devices)
    scratch = [pltpu.VMEM(member.shape, BF16) for member in saved]
    scratch += [pltpu.SemaphoreType.DMA((len(saved),))]
    scratch += [pltpu.VMEM((width, rows * tokens), BF16), pltpu.VMEM((vocab, rows * tokens), BF16)]
    scratch += [
        pltpu.VMEM((bits + 1,) + vec.shape, F32),
        pltpu.VMEM((bits,) + vec.shape, F32),
        pltpu.SemaphoreType.DMA((bits,)),
        pltpu.SemaphoreType.DMA((bits,)),
        pltpu.VMEM((8, width), F32),
        pltpu.VMEM((8, width), F32),
        pltpu.SemaphoreType.DMA((stages,)),
        pltpu.SemaphoreType.DMA((1,)),
        pltpu.VMEM((stages, share, width), F32),
        pltpu.SemaphoreType.DMA((stages,)),
        pltpu.SemaphoreType.DMA((2,)),
        pltpu.VMEM((share, width), F32),
        pltpu.VMEM((share, width), F32),
    ]
    sizes = [size for size, _ in reversed(dims)]
    for _, _, block, turned in plan:
        scratch.append(pltpu.VMEM(tuple(sizes) + block, BF16))
        remain = list(reversed(dims))
        for size, stride in dims[::-1] if turned else dims:
            remain.remove((size, stride))
            piece = tuple(other for other, _ in remain) + block
            scratch.append(pltpu.VMEM((1 if size == 2 else 2, size - 1) + piece, BF16))
            scratch += [pltpu.SemaphoreType.DMA((2, size - 1))] * 2
    return pl.pallas_call(
        functools.partial(gradient_kernel, stages, devices, plan),
        out_shape=[
            jax.ShapeDtypeStruct((width // devices, 3 * width), F32),
            jax.ShapeDtypeStruct((width // devices, width), F32),
            jax.ShapeDtypeStruct((width // devices, hid), F32),
            jax.ShapeDtypeStruct((hid // devices, width), F32),
            jax.ShapeDtypeStruct((share, width), F32),
            jax.ShapeDtypeStruct((share, width), F32),
            jax.ShapeDtypeStruct(vec.shape, F32),
        ],
        in_specs=[hbm] * len(saved) + [vmem] * 2,
        out_specs=[vmem] * 7,
        scratch_shapes=scratch,
        compiler_params=pltpu.CompilerParams(
            collective_id=1, has_side_effects=True, vmem_limit_bytes=62 * 1024 * 1024
        ),
        name="gradients",
    )(*saved, vec, token_ids)


def step_kernel(stages, micros, devices, plan, *refs):
    refs = list(refs)

    def take(amount):
        head, refs[:] = refs[:amount], refs[amount:]
        return head

    token_ids, segment_ids, target_ids = take(3)
    qv_b, out_b, in_b, gains, shifts, fin_gain, fin_bias = take(7)
    embed_h, head_h, qkv_h, out_h, in_h, down_h = take(6)
    qkv_out, out_out, in_out, down_out, embed_out, head_out, vec_out = take(7)
    side, qkv_w, out_w = take(3)
    in_w, down_w = take(4), take(4)
    instream, outb, gin, gs, proj, probs, mixed, middle, active, slope = take(10)
    lo, gmid, s_gbr, s_xl, vec, ids, frames = take(7)
    fsend, frecv, bsend, brecv, wsem = take(5)
    go = lo
    place = lax.axis_index("dp")
    stage = lax.axis_index("pipe")
    tokens, width = instream.shape[1], instream.shape[2]
    hidden_n = in_b.shape[1]
    vocab = side.shape[0]
    pairs = width // ROW
    chunk = 512
    is_first = stage == 0
    is_last = stage == stages - 1
    up = jnp.minimum(stage + 1, stages - 1)
    down = jnp.maximum(stage - 1, 0)

    def bring(index, source, target):
        return pltpu.make_async_copy(source, target, wsem.at[index])

    weights = [bring(1, qkv_h, qkv_w), bring(2, out_h, out_w)]
    for c in range(4):
        lanes = pl.ds(c * chunk, chunk)
        weights.append(bring(3 + c, in_h.at[:, :, :, lanes], in_w[c]))
        weights.append(bring(7 + c, down_h.at[c], down_w[c]))

    @pl.when(is_first)
    def _():
        bring(0, embed_h, side).start()

    for copy in weights:
        copy.start()

    @pl.when(is_last)
    def _():
        bring(0, head_h, side).start()

    barrier = pltpu.get_barrier_semaphore()

    def greet(offset, carry):
        peer = lax.rem(place + offset, devices)
        pl.semaphore_signal(barrier, inc=1, device_id={"dp": peer}, device_id_type=MESH)
        return carry

    def greet_stage(offset, carry):
        peer = lax.rem(stage + offset, stages)
        pl.semaphore_signal(barrier, inc=1, device_id={"pipe": peer}, device_id_type=MESH)
        return carry

    lax.fori_loop(1, devices, greet, 0)
    lax.fori_loop(1, stages, greet_stage, 0)

    def whole(part):
        return part[...].reshape(width, width)

    vec[...] = jnp.zeros_like(vec)
    rows_n, seq = token_ids.shape
    for index, member in enumerate((token_ids, segment_ids, target_ids)):
        ids[index] = jnp.full(ids.shape[1:], 4.0 if index == 1 else -1.0, F32)
        ids[index, 0:rows_n, 0:seq] = member[...].astype(F32)
    at_query = lax.broadcasted_iota(jnp.int32, (ROW, ROW), 1)
    at_key = lax.broadcasted_iota(jnp.int32, (ROW, ROW), 0)
    frames[...] = jnp.where(at_key < ((at_query * 43) // 256) * FRAME + FRAME, 1.0, 0.0)

    def column(index, row):
        values = jnp.broadcast_to(ids[index, pl.ds(row, 1), :], (8, ROW))
        return values.T[:, 0:1]

    def hot_rows(index, m):
        parts = [column(index, m * GROUP + r) for r in range(GROUP)]
        values = jnp.concatenate(parts, axis=0)
        places = lax.broadcasted_iota(jnp.int32, (tokens, vocab), 1).astype(F32)
        return values, jnp.where(values == places, 1.0, 0.0)

    def forward_copy(m):
        return pltpu.make_async_remote_copy(
            src_ref=outb.at[m],
            dst_ref=instream.at[m],
            send_sem=fsend.at[m],
            recv_sem=frecv.at[m],
            device_id={"pipe": up},
            device_id_type=MESH,
        )

    def backward_copy(m):
        return pltpu.make_async_remote_copy(
            src_ref=gs.at[m],
            dst_ref=gin.at[m],
            send_sem=bsend.at[m],
            recv_sem=brecv.at[m],
            device_id={"pipe": down},
            device_id_type=MESH,
        )

    @pl.when(is_first | is_last)
    def _():
        bring(0, embed_h, side).wait()

    for copy in weights:
        copy.wait()
    pl.semaphore_wait(barrier, devices - 1 + stages - 1)

    lane_low = lax.broadcasted_iota(jnp.int32, (ROW, ROW), 1) < ROW // 2

    def forward(m):
        @pl.when(is_first)
        def _():
            hot = hot_rows(0, m)[1].astype(BF16)
            instream[m] = dot(hot, side[...]).astype(BF16)

        @pl.when(jnp.logical_not(is_first))
        def _():
            forward_copy(m).wait_recv()

        normal, _ = normalise(instream[m].astype(F32))
        low = (normal * gains[0:1, :] + shifts[0:1, :]).astype(BF16)
        queries = dot(low, qkv_w[:, 0:width]) + qv_b[0:1, :]
        proj[m, :, 0:width] = (queries * (ROW // 2) ** -0.5).astype(BF16)
        proj[m, :, width : 2 * width] = dot(low, qkv_w[:, width : 2 * width]).astype(BF16)
        proj[m, :, 2 * width : 3 * width] = (
            dot(low, qkv_w[:, 2 * width : 3 * width]) + qv_b[1:2, :]
        ).astype(BF16)
        masks, scores = [], []
        for r in range(GROUP):
            rows = slice(r * ROW, (r + 1) * ROW)
            kinds = lax.broadcasted_iota(jnp.int32, (16, ROW), 0).astype(F32)
            member = jnp.where(ids[1, pl.ds(m * GROUP + r, 1), :] == kinds, 1.0, 0.0).astype(BF16)
            mask = jnp.where(dot_tn(member, member) * frames[...] > 0.5, 0.0, MASKED)
            masks.append(jnp.concatenate([mask, mask], axis=1))
            for p in range(pairs):
                q = stack_pair(proj[m, rows, p * ROW : (p + 1) * ROW], lane_low)
                k = proj[m, rows, width + p * ROW : width + (p + 1) * ROW]
                scores.append(dot_nt(k, q))

        def mix(unit):
            r, p = unit // pairs, unit % pairs
            rows = slice(r * ROW, (r + 1) * ROW)
            v = proj[m, rows, 2 * width + p * ROW : 2 * width + (p + 1) * ROW]
            both = dot_tn(probs[m, unit // 2, unit % 2], v)
            mixed[m, rows, p * ROW : (p + 1) * ROW] = join_pair(both, lane_low).astype(BF16)

        for unit in range(GROUP * pairs):
            masked = scores[unit] + masks[unit // pairs]
            expo = jnp.exp(masked - jnp.max(masked, axis=0, keepdims=True))
            total = jnp.sum(expo, axis=0, keepdims=True)
            probs[m, unit // 2, unit % 2] = (expo * (1.0 / total)).astype(BF16)
            if unit:
                mix(unit - 1)
        mix(GROUP * pairs - 1)
        mid = instream[m].astype(F32) + (dot(mixed[m], out_w[...]) + out_b[0:1, :])
        middle[m] = mid
        normal2, _ = normalise(mid)
        low2 = (normal2 * gains[1:2, :] + shifts[1:2, :]).astype(BF16)
        parts = hidden_n // chunk

        def spread(c):
            return dot(low2, whole(in_w[c]))

        total, ahead = None, spread(0)
        for c in range(parts):
            cols = slice(c * chunk, (c + 1) * chunk)
            hid = ahead + in_b[0:1, cols]
            if c + 1 < parts:
                ahead = spread(c + 1)
            square = hid * hid
            tan = jnp.tanh(hid * (GELU_A + (GELU_A * GELU_B) * square))
            half = 0.5 + 0.5 * tan
            act = (hid * half).astype(BF16)
            active[m, :, cols] = act
            rise = (1.0 - tan * tan) * (0.5 * GELU_A + (1.5 * GELU_A * GELU_B) * square)
            slope[m, :, cols] = (half + hid * rise).astype(BF16)
            term = dot(act, whole(down_w[c]))
            total = term if total is None else total + term
        lo[...] = middle[m] + (total + out_b[1:2, :])

        @pl.when(jnp.logical_not(is_last))
        def _():
            outb[m] = lo[...].astype(BF16)
            forward_copy(m).start()

    def head(m):
        normal, scale = normalise(lo[...])
        outb[m] = (normal * fin_gain[...] + fin_bias[...]).astype(BF16)
        logits = dot_nt(outb[m], side[...])
        top = jnp.max(logits, axis=-1, keepdims=True)
        expo = jnp.exp(logits - top)
        total = jnp.sum(expo, axis=-1, keepdims=True)
        target, hot = hot_rows(2, m)
        grad_logits = jnp.where(target >= 0.0, expo * (1.0 / total) - hot, 0.0).astype(BF16)
        s_xl[m] = grad_logits
        grad_final = dot(grad_logits, side[...])
        vec[V_FINAL_GAIN : V_FINAL_GAIN + 1, :] += column_sum(grad_final * normal)
        vec[V_FINAL_BIAS : V_FINAL_BIAS + 1, :] += column_sum(grad_final)
        go[...] = norm_backward(grad_final, normal, scale, fin_gain[...])

    def backward(m):
        @pl.when(jnp.logical_not(is_last))
        def _():
            backward_copy(m).wait_recv()
            go[...] = gin[m].astype(F32)

        gres = go[...].astype(BF16)
        gin[m] = gres
        parts = hidden_n // chunk

        def spread(c):
            return dot_nt(gres, whole(down_w[c]))

        total, ahead = None, spread(0)
        for c in range(parts):
            cols = slice(c * chunk, (c + 1) * chunk)
            gact = ahead
            if c + 1 < parts:
                ahead = spread(c + 1)
            ghid = (gact * slope[m, :, cols].astype(F32)).astype(BF16)
            slope[m, :, cols] = ghid
            term = dot_nt(ghid, whole(in_w[c]))
            total = term if total is None else total + term
        normal2, scale2 = normalise(middle[m])
        vec[V_GAIN2 : V_GAIN2 + 1, :] += column_sum(total * normal2)
        vec[V_SHIFT2 : V_SHIFT2 + 1, :] += column_sum(total)
        gmid[...] = go[...] + norm_backward(total, normal2, scale2, gains[1:2, :])
        gbr = gmid[...].astype(BF16)
        s_gbr[m] = gbr
        gmix = dot_nt(gbr, out_w[...]).astype(BF16)
        grads = []
        for r in range(GROUP):
            rows = slice(r * ROW, (r + 1) * ROW)
            for p in range(pairs):
                gm = stack_pair(gmix[rows, p * ROW : (p + 1) * ROW], lane_low)
                vlanes = slice(2 * width + p * ROW, 2 * width + (p + 1) * ROW)
                grads.append(dot_nt(proj[m, rows, vlanes], gm))
                unit = r * pairs + p
                proj[m, rows, vlanes] = dot(probs[m, unit // 2, unit % 2], gm).astype(BF16)

        def pull(unit, gsc):
            r, p = unit // pairs, unit % pairs
            rows = slice(r * ROW, (r + 1) * ROW)
            lanes = slice(p * ROW, (p + 1) * ROW)
            klanes = slice(width + p * ROW, width + (p + 1) * ROW)
            q = stack_pair(proj[m, rows, lanes], lane_low)
            gq = join_pair(dot_tn(gsc, proj[m, rows, klanes]), lane_low) * (ROW // 2) ** -0.5
            gk = dot(gsc, q)
            proj[m, rows, klanes] = gk.astype(BF16)
            proj[m, rows, lanes] = gq.astype(BF16)

        waiting = None
        for unit in range(GROUP * pairs):
            weights = probs[m, unit // 2, unit % 2].astype(F32)
            inner = jnp.sum(weights * grads[unit], axis=0, keepdims=True)
            gsc = (weights * (grads[unit] - inner)).astype(BF16)
            if waiting is not None:
                pull(unit - 1, waiting)
            waiting = gsc
        pull(GROUP * pairs - 1, waiting)
        gproj = proj[m]
        gnormed = dot_nt(gproj, qkv_w[...])
        normal, scale = normalise(instream[m].astype(F32))
        vec[V_GAIN1 : V_GAIN1 + 1, :] += column_sum(gnormed * normal)
        vec[V_SHIFT1 : V_SHIFT1 + 1, :] += column_sum(gnormed)
        gs[m] = (gmid[...] + norm_backward(gnormed, normal, scale, gains[0:1, :])).astype(BF16)

        @pl.when(jnp.logical_not(is_first))
        def _():
            backward_copy(m).start()

    def tick(t, carry):
        m_forward = t - stage
        m_backward = t - (2 * (stages - 1) - stage)

        @pl.when((m_forward >= 0) & (m_forward < micros))
        def _():
            forward(m_forward)

        @pl.when((m_backward >= 0) & (m_backward < micros))
        def _():
            @pl.when(is_last)
            def _():
                head(m_backward)

            backward(m_backward)

        return carry

    lax.fori_loop(0, micros + 2 * (stages - 1), tick, 0)

    is_extra = is_first | is_last
    dims = line_dims(devices)
    turned_left = qkv_w
    mats = {
        "mixed": mixed,
        "active": active,
        "gres": gin,
        "ghid": slope,
        "gbr": s_gbr,
        "gproj": proj,
    }

    def mat(name, lanes=slice(None)):
        value = mats[name][:, :, lanes]
        return value.reshape(micros * tokens, value.shape[2])

    where = [lax.rem(place // stride, size) for size, stride in dims]

    def identity(size):
        here = lax.broadcasted_iota(jnp.int32, (size, size), 0)
        there = lax.broadcasted_iota(jnp.int32, (size, size), 1)
        return jnp.where(here == there, 1.0, 0.0).astype(BF16)

    held = []

    def turn(name):
        if held[-1:] == [name]:
            return
        held.append(name)
        unit = identity(256)
        if name in ("normed", "normed2"):
            row = 0 if name == "normed" else 1
            source = instream if name == "normed" else middle
            for m in range(micros):
                normal, _ = normalise(source[m].astype(F32))
                again = (normal * gains[row : row + 1, :] + shifts[row : row + 1, :]).astype(BF16)
                for q in range(width // 256):
                    part = dot_nt(unit, again[:, q * 256 : (q + 1) * 256])
                    turned_left[q * 256 : (q + 1) * 256, m * tokens : (m + 1) * tokens] = part.astype(BF16)
            return
        for q in range(width // 256):
            part = dot_nt(unit, mat(name, slice(q * 256, (q + 1) * 256)))
            turned_left[q * 256 : (q + 1) * 256, :] = part.astype(BF16)

    bits = devices.bit_length() - 1
    vec_send, vec_recv = take(2)
    vec_sems = take(2)

    def vec_copy(k):
        peer = jnp.bitwise_xor(place, 1 << k)
        return pltpu.make_async_remote_copy(
            src_ref=vec_send.at[k],
            dst_ref=vec_recv.at[k],
            send_sem=vec_sems[0].at[k],
            recv_sem=vec_sems[1].at[k],
            device_id={"dp": peer},
            device_id_type=MESH,
        )

    def vec_step(k):
        def run():
            if k == 0:
                vec_send[0] = vec[...]
                ones = jnp.ones((16, micros * tokens), BF16)
                for name, start, row in (
                    ("gproj", 0, V_QUERY),
                    ("gproj", 2 * width, V_VALUE),
                    ("gbr", 0, V_BRANCH),
                    ("gres", 0, V_RESULT),
                ):
                    part = dot(ones, mat(name, slice(start, start + width)))
                    vec_send[0, row : row + 1, :] = part[0:1, :]
                for q in range(hidden_n // width):
                    part = dot(ones, mat("ghid", slice(q * width, (q + 1) * width)))
                    vec_send[0, V_HIDDEN + q : V_HIDDEN + q + 1, :] = part[0:1, :]
            else:
                vec_copy(k - 1).wait_recv()
                vec_send[k] = vec_send[k - 1] + vec_recv[k - 1]
            if k < bits:
                vec_copy(k).start()

        return run

    final_send, final_recv = take(2)
    final_sems = take(2)

    def final_copy(offset):
        peer = lax.rem(stages - 1 + offset, stages)
        return pltpu.make_async_remote_copy(
            src_ref=final_send,
            dst_ref=final_recv,
            send_sem=final_sems[0].at[offset],
            recv_sem=final_sems[1].at[0],
            device_id={"pipe": peer},
            device_id_type=MESH,
        )

    def vec_last():
        vec_step(bits)()
        vec_out[...] = vec_send[bits]

        @pl.when(stage == stages - 1)
        def _():
            final_send[...] = vec_send[bits, 8:16, :]
            for offset in range(1, stages):
                final_copy(offset).start()

    def vec_finish():
        @pl.when(stage != stages - 1)
        def _():
            final_copy(1).wait_recv()
            vec_out[V_FINAL_GAIN : V_FINAL_BIAS + 1, :] = final_recv[
                V_FINAL_GAIN - 8 : V_FINAL_BIAS - 7, :
            ]

    def vec_drain():
        for k in range(bits):
            vec_copy(k).wait_send()

        @pl.when(stage == stages - 1)
        def _():
            for offset in range(1, stages):
                final_copy(offset).wait_send()

    extra_sum, extra_send_sem, extra_recv_sem, last_sum = take(4)
    share = embed_out.shape[0]

    def extra_copy(source, offset, target):
        peer = lax.rem(source + offset, stages)
        return pltpu.make_async_remote_copy(
            src_ref=extra_sum.at[pl.ds(pl.multiple_of(peer * share, share), share)],
            dst_ref=target,
            send_sem=extra_send_sem.at[offset],
            recv_sem=extra_recv_sem.at[0 if source == 0 else 1],
            device_id={"pipe": peer},
            device_id_type=MESH,
        )

    def chunk_steps(kind, c, block, turned):
        order = list(range(len(dims)))
        if turned:
            order.reverse()
        if kind == "down":
            full = probs.at[c]
        elif kind == "extra":
            full = probs.at[4 + c]
        else:
            full = (down_w + in_w)[{"out": 0, "in": 1, "qkv": 5}[kind] + c]

        def compute():
            if kind == "down":
                if c % 2 == 1:
                    return
                turn("gres")
                half = width // 2
                lines = slice((c // 2) * half, (c // 2 + 1) * half)
                parts = dot(turned_left[lines, :], mat("active")).astype(BF16)
                depth = hidden_n // devices
                unit = identity(depth)
                for d in range(devices):
                    back = dot_nt(unit, parts[:, d * depth : (d + 1) * depth]).astype(BF16)
                    for k in range(2):
                        piece = back[:, k * ROW : (k + 1) * ROW]
                        piece = jnp.concatenate([piece[: depth // 2], piece[depth // 2 :]], axis=1)
                        probs[(c + k,) + split(d)] = piece
            elif kind == "extra":
                if c == 1:
                    return
                rows = vocab // stages
                share = rows // devices
                half = width // 2

                def fill(left, right):
                    for p in range(stages):
                        part = left(p, right).astype(BF16).reshape(devices, share, width)
                        for d in range(devices):
                            for k in range(2):
                                lines = slice(p * share, (p + 1) * share)
                                probs[(4 + k,) + split(d) + (lines,)] = part[
                                    d, :, k * half : (k + 1) * half
                                ]

                def flat(ref):
                    return ref[...].reshape(micros * tokens, ref.shape[2])

                @pl.when(is_first)
                def _():
                    def hot_part(p, right):
                        here = lax.broadcasted_iota(jnp.int32, (rows, ROW), 0).astype(F32) + p * rows
                        hot = [
                            jnp.where(ids[0, r : r + 1, :] == here, 1.0, 0.0).astype(BF16)
                            for r in range(rows_n)
                        ]
                        return dot(jnp.concatenate(hot, axis=1), right)

                    fill(hot_part, flat(gs))

                @pl.when(is_last)
                def _():
                    def soft_part(p, right):
                        left = s_xl[:, :, p * rows : (p + 1) * rows]
                        return dot_tn(left.reshape(micros * tokens, rows), right)

                    fill(soft_part, flat(outb))
            else:
                left, right = {
                    "in": ("normed2", "ghid"),
                    "out": ("mixed", "gbr"),
                    "qkv": ("normed", "gproj"),
                }[kind]
                turn(left)
                part = dot(turned_left[...], mat(right, slice(c * width, (c + 1) * width)))
                part = part.astype(BF16).reshape((devices,) + block)
                for d in range(devices):
                    full[split(d)] = part[d]

        def split(d):
            return tuple((d // stride) % size for size, stride in reversed(dims))

        steps = [[compute]]
        for at, phase in enumerate(order):
            size = dims[phase][0]
            buffers = take(3)
            done = order[:at]
            last = at == len(order) - 1
            steps[-1].append(functools.partial(line_step, phase, size, 1, full, buffers, done))
            for t in range(2, size):
                steps.append([functools.partial(line_step, phase, size, t, full, buffers, done)])
            drains.append((kind, functools.partial(line_drain, phase, size, full, buffers, done)))
            steps.append([functools.partial(line_final, kind, c, phase, size, full, buffers, done, last)])
        if kind == "extra":
            steps = [[gated([part]) for part in step] for step in steps]
        return steps

    def gated(step):
        def run():
            @pl.when(is_extra)
            def _():
                for part in step:
                    part()

        return run

    def block_of(full, phase, j, done):
        spot = [slice(None)] * len(dims)
        for other in done:
            spot[len(dims) - 1 - other] = where[other]
        spot[len(dims) - 1 - phase] = j
        return full.at[tuple(spot)]

    def line_copy(phase, size, t, side, full, buffers, done):
        recv, ssem, rsem = buffers
        i = where[phase]
        stride = dims[phase][1]
        if side == 0:
            j, peer = size - t + i, place + jnp.where(i < size - 1, stride, 0)
        else:
            j, peer = t - size + i, place - jnp.where(i > 0, stride, 0)
        return pltpu.make_async_remote_copy(
            src_ref=block_of(full, phase, jnp.clip(j, 0, size - 1), done),
            dst_ref=recv.at[0 if size == 2 else side, t - 1],
            send_sem=ssem.at[side, t - 1],
            recv_sem=rsem.at[side, t - 1],
            device_id={"dp": peer},
            device_id_type=MESH,
        )

    def sends(i, size, t, side):
        return (i <= t - 1) if side == 0 else (i >= size - t)

    def line_step(phase, size, t, full, buffers, done):
        i = where[phase]
        for side in range(2):
            at_end = (i == 0) if side == 0 else (i == size - 1)
            j = size - t + i if side == 0 else t - size + i
            j = jnp.clip(j, 0, size - 1)

            @pl.when(sends(i, size, t, side))
            def _():
                if t > 1:
                    @pl.when(jnp.logical_not(at_end))
                    def _():
                        line_copy(phase, size, t - 1, side, full, buffers, done).wait_recv()
                        own = block_of(full, phase, j, done)
                        got = buffers[0][0 if size == 2 else side, t - 2]
                        own[...] = (own[...].astype(F32) + got.astype(F32)).astype(BF16)

                line_copy(phase, size, t, side, full, buffers, done).start()

    def line_final(kind, c, phase, size, full, buffers, done, last):
        i = where[phase]
        own = block_of(full, phase, i, done)
        total = own
        if last:
            lanes = slice(c * width, (c + 1) * width)
            slots = {
                "qkv": lambda: qkv_out.at[:, lanes],
                "in": lambda: in_out.at[:, lanes],
                "out": lambda: out_out,
                "down": lambda: last_sum,
                "extra": lambda: extra_sum.at[:, c * (width // 2) : (c + 1) * (width // 2)],
            }
            total = slots[kind]()
        lower, upper = i > 0, i < size - 1

        def arrived(side):
            line_copy(phase, size, size - 1, side, full, buffers, done).wait_recv()
            return buffers[0][0 if size == 2 else side, size - 2].astype(F32)

        @pl.when(lower & upper)
        def _():
            total[...] = (own[...].astype(F32) + arrived(0) + arrived(1)).astype(total.dtype)

        @pl.when(lower & jnp.logical_not(upper))
        def _():
            total[...] = (own[...].astype(F32) + arrived(0)).astype(total.dtype)

        @pl.when(jnp.logical_not(lower))
        def _():
            total[...] = (own[...].astype(F32) + arrived(1)).astype(total.dtype)

        if last and kind == "down":
            deep = down_out.shape[0] // 2
            lanes = slice(c * ROW, (c + 1) * ROW)
            down_out[0:deep, lanes] = last_sum[:, 0:ROW]
            down_out[deep : 2 * deep, lanes] = last_sum[:, ROW : 2 * ROW]
        if last and kind == "extra" and c == 1:
            for source_stage, out in ((0, embed_out), (stages - 1, head_out)):
                @pl.when(stage == source_stage)
                def _():
                    for offset in range(1, stages):
                        extra_copy(source_stage, offset, extra_recv[0 if source_stage == 0 else 1]).start()
                    out[...] = extra_sum[source_stage * share : (source_stage + 1) * share, :]

    def line_drain(phase, size, full, buffers, done):
        i = where[phase]
        for side in range(2):
            for t in range(1, size):
                @pl.when(sends(i, size, t, side))
                def _():
                    line_copy(phase, size, t, side, full, buffers, done).wait_send()

    extra_recv = take(2)
    drains = []
    chains = [chunk_steps(*item) for item in plan]
    depth = len(chains[0])
    vec_chain = [vec_step(k) for k in range(bits)] + [vec_last]
    starts, first, extra_rounds = [], 0, iter((1, 3, 6, 8))
    for item in plan:
        if item[3]:
            starts.append(next(extra_rounds))
        else:
            starts.append(first)
            first += 1
    loaded_at = max(start for start, item in zip(starts, plan) if item[0] == "qkv" and item[1] == 0)
    for r in range(max(starts) + depth):
        for d in [0] + list(range(depth - 1, 0, -1)):
            for start, chain in zip(starts, chains):
                if r - start != d:
                    continue
                for part in chain[d]:
                    part()
        if 0 <= r - loaded_at < len(vec_chain):
            vec_chain[r - loaded_at]()
    vec_finish()
    for source_stage, out in ((0, embed_out), (stages - 1, head_out)):
        @pl.when(stage != source_stage)
        def _():
            got = extra_recv[0 if source_stage == 0 else 1]
            extra_copy(source_stage, 1, got).wait_recv()
            out[...] = got[...]

        @pl.when(stage == source_stage)
        def _():
            for offset in range(1, stages):
                extra_copy(source_stage, offset, extra_recv[0]).wait_send()

    vec_drain()
    for kind, drain in drains:
        if kind == "extra":
            gated([drain])()
        else:
            drain()

    for m in range(micros):
        @pl.when(jnp.logical_not(is_last))
        def _():
            forward_copy(m).wait_send()

        @pl.when(jnp.logical_not(is_first))
        def _():
            backward_copy(m).wait_send()


def step_plan(width, hid, vocab, stages, devices):
    plan = []
    for kind, c, _, turned in chunk_plan(width, hid, vocab, stages, devices):
        wide = kind in ("down", "extra")
        plan.append((kind, c, (ROW, 2 * ROW) if wide else (width // devices, width), turned))
    return plan


def run_step(stages, devices, token_ids, segment_ids, target_ids, params):
    embed, qkv_w, qv_b, out_w, out_b, in_w, in_b, down_w, gains, shifts, fg, fb, head_w = params
    dims = line_dims(devices)
    width, hid, vocab = embed.shape[1], in_w.shape[1], head_w.shape[0]
    tokens = GROUP * ROW
    micros = token_ids.shape[0] // GROUP
    vmem = pl.BlockSpec(memory_space=pltpu.VMEM)
    hbm = pl.BlockSpec(memory_space=pl.ANY)
    sizes = tuple(size for size, _ in reversed(dims))
    slim = width // devices
    share = vocab // (stages * devices)
    plan = step_plan(width, hid, vocab, stages, devices)
    bits = devices.bit_length() - 1

    def scratch(lead, columns, kind=BF16):
        return pltpu.VMEM((lead, tokens, columns), kind)

    def sums(*shape):
        return pltpu.VMEM(shape, F32)

    dma = pltpu.SemaphoreType.DMA
    scratch_shapes = [
        pltpu.VMEM((vocab, width), BF16),
        pltpu.VMEM((width, 3 * width), BF16),
        pltpu.VMEM((width, width), BF16),
    ]
    scratch_shapes += [pltpu.VMEM(sizes + (slim, width), BF16)] * 8
    scratch_shapes += [
        scratch(micros, width),
        scratch(micros, width),
        scratch(micros, width),
        scratch(micros, width),
        scratch(micros, 3 * width),
        pltpu.VMEM((micros,) + sizes + (ROW, 2 * ROW), BF16),
        scratch(micros, width),
        scratch(micros, width, F32),
        scratch(micros, hid),
        scratch(micros, hid),
        sums(tokens, width),
        sums(tokens, width),
        scratch(micros, width),
        scratch(micros, vocab),
        sums(VEC_ROWS, width),
        sums(3, 16, ROW),
        sums(ROW, ROW),
        dma((micros,)),
        dma((micros,)),
        dma((micros,)),
        dma((micros,)),
        dma((11,)),
        sums(bits + 1, VEC_ROWS, width),
        sums(bits, VEC_ROWS, width),
        dma((bits,)),
        dma((bits,)),
        sums(8, width),
        sums(8, width),
        dma((stages,)),
        dma((1,)),
        sums(stages * share, width),
        dma((stages,)),
        dma((2,)),
        sums(ROW, 2 * ROW),
        sums(share, width),
        sums(share, width),
    ]
    for _, _, block, turned in plan:
        remain = list(reversed(dims))
        for size, stride in dims[::-1] if turned else dims:
            remain.remove((size, stride))
            piece = tuple(other for other, _ in remain) + block
            scratch_shapes.append(pltpu.VMEM((1 if size == 2 else 2, size - 1) + piece, BF16))
            scratch_shapes += [dma((2, size - 1))] * 2

    def result(*shape):
        return jax.ShapeDtypeStruct(shape, F32)

    return pl.pallas_call(
        functools.partial(step_kernel, stages, micros, devices, plan),
        out_shape=[
            result(slim, 3 * width),
            result(slim, width),
            result(slim, hid),
            result(hid // devices, width),
            result(share, width),
            result(share, width),
            result(VEC_ROWS, width),
        ],
        in_specs=[vmem] * 10 + [hbm] * 6,
        out_specs=[vmem] * 7,
        scratch_shapes=scratch_shapes,
        compiler_params=pltpu.CompilerParams(
            collective_id=2, has_side_effects=True, vmem_limit_bytes=63 * 1024 * 1024
        ),
        name="step",
    )(
        token_ids,
        segment_ids,
        target_ids,
        qv_b,
        out_b,
        in_b,
        gains,
        shifts,
        fg,
        fb,
        embed,
        head_w,
        qkv_w,
        out_w,
        in_w.reshape(sizes + (slim, hid)),
        down_w.reshape((hid // width,) + sizes + (slim, width)),
    )


def finish_kernel(devices, embed_g, qkv_g, out_g, in_g, down_g, head_g, vec, *outs):
    place = lax.axis_index("dp")
    width = vec.shape[1]
    (embed_o, qkv_o, qv_o, out_o, outb_o, in_o, inb_o, down_o, gain_o, shift_o, fg_o, fb_o, head_o) = outs
    embed_o[...] = embed_g[...]
    head_o[...] = head_g[...]
    for source, target in ((qkv_g, qkv_o), (out_g, out_o), (in_g, in_o), (down_g, down_o)):
        target[0] = source[...]
    lanes = width // devices
    turned = pltpu.roll(vec[0:8, :], lax.rem(width - place * lanes, width), 1)
    for row, out in ((V_QUERY, qv_o), (V_BRANCH, outb_o), (V_GAIN1, gain_o), (V_SHIFT1, shift_o)):
        out[0] = turned[row : row + 2, 0:lanes]
    share = inb_o.shape[1]
    first = place * share
    row = vec[pl.ds(V_HIDDEN + first // width, 1), :]
    wide = jnp.broadcast_to(row, (8, width))
    inb_o[...] = pltpu.roll(wide, lax.rem(width - lax.rem(first, width), width), 1)[0:1, 0:share]
    fg_o[...] = vec[V_FINAL_GAIN : V_FINAL_GAIN + 1, :]
    fb_o[...] = vec[V_FINAL_BIAS : V_FINAL_BIAS + 1, :]


def run_finish(devices, embed_g, qkv_g, out_g, in_g, down_g, head_g, vec):
    vmem = pl.BlockSpec(memory_space=pltpu.VMEM)
    width = vec.shape[1]
    lanes = width // devices

    def shape(*sizes):
        return jax.ShapeDtypeStruct(sizes, F32)

    pair = shape(1, 2, lanes)
    return pl.pallas_call(
        functools.partial(finish_kernel, devices),
        out_shape=[
            shape(*embed_g.shape),
            shape(1, *qkv_g.shape),
            pair,
            shape(1, *out_g.shape),
            pair,
            shape(1, *in_g.shape),
            shape(1, in_g.shape[1] // devices),
            shape(1, *down_g.shape),
            pair,
            pair,
            shape(1, width),
            shape(1, width),
            shape(*head_g.shape),
        ],
        in_specs=[vmem] * 7,
        out_specs=[vmem] * 13,
        name="finish",
    )(embed_g, qkv_g, out_g, in_g, down_g, head_g, vec)


def on_device(
    token_ids,
    segment_ids,
    target_ids,
    embed_table,
    qkv_weight,
    qv_bias,
    out_weight,
    out_biases,
    ff_in,
    ff_in_bias,
    ff_out,
    norm_gains,
    norm_biases,
    final_gain,
    final_bias,
    head_weight,
):
    stages = lax.axis_size("pipe")
    devices = lax.axis_size("dp")
    params = (
        embed_table,
        qkv_weight[0],
        qv_bias[0],
        out_weight[0],
        out_biases[0],
        ff_in[0],
        ff_in_bias,
        ff_out[0],
        norm_gains[0],
        norm_biases[0],
        final_gain[None],
        final_bias[None],
        head_weight,
    )
    if devices == 8:
        grads = run_step(stages, devices, token_ids, segment_ids, target_ids, params)
    else:
        *saved, vec = run_pipeline(stages, token_ids, segment_ids, target_ids, params)
        grads = run_gradients(stages, devices, saved, vec, token_ids)
    qkv_g, out_g, in_g, down_g, embed_g, head_g, sums = grads
    done = list(run_finish(devices, embed_g, qkv_g, out_g, in_g, down_g, head_g, sums))
    done[10], done[11] = done[10][0], done[11][0]
    return tuple(done)


def solution(mesh):
    layer3 = P("pipe", None, None)
    return jax.shard_map(
        on_device,
        mesh=mesh,
        in_specs=(
            P("dp", None),
            P("dp", None),
            P("dp", None),
            P(),
            layer3,
            layer3,
            layer3,
            layer3,
            layer3,
            P("pipe", None),
            layer3,
            layer3,
            layer3,
            P(),
            P(),
            P(),
        ),
        out_specs=(
            P(("pipe", "dp"), None),
            P("pipe", "dp", None),
            P("pipe", None, "dp"),
            P("pipe", "dp", None),
            P("pipe", None, "dp"),
            P("pipe", "dp", None),
            P("pipe", "dp"),
            P("pipe", "dp", None),
            P("pipe", None, "dp"),
            P("pipe", None, "dp"),
            P(),
            P(),
            P(("pipe", "dp"), None),
        ),
        check_vma=False,
    )
```

```python
import functools

import jax
import jax.numpy as jnp
from jax import lax
from jax.experimental import pallas as pl
from jax.experimental.pallas import tpu as pltpu
from jax.sharding import PartitionSpec as P

HEADS = 8
FRAME = 6
ROW = 128
GROUP = 2
MASKED = -1e30
GELU_A = 0.7978845608
GELU_B = 0.044715
MESH = pl.DeviceIdType.MESH
F32 = jnp.float32
BF16 = jnp.bfloat16

VEC_ROWS = 16
V_QUERY, V_VALUE, V_BRANCH, V_RESULT, V_GAIN1, V_GAIN2, V_SHIFT1, V_SHIFT2 = range(8)
V_HIDDEN = 8
V_FINAL_GAIN, V_FINAL_BIAS = 12, 13


def dot(a, b):
    return lax.dot_general(a, b, (((1,), (0,)), ((), ())), preferred_element_type=F32)


def dot_nt(a, b):
    return lax.dot_general(a, b, (((1,), (1,)), ((), ())), preferred_element_type=F32)


def dot_tn(a, b):
    return lax.dot_general(a, b, (((0,), (0,)), ((), ())), preferred_element_type=F32)


def normalise(values):
    centre = jnp.mean(values, axis=-1, keepdims=True)
    centered = values - centre
    spread = jnp.mean(centered * centered, axis=-1, keepdims=True)
    scale = lax.rsqrt(spread + 1e-05)
    return centered * scale, scale


def norm_backward(grad, normal, scale, gain):
    grad_n = grad * gain
    mean_grad = jnp.mean(grad_n, axis=-1, keepdims=True)
    mean_proj = jnp.mean(grad_n * normal, axis=-1, keepdims=True)
    return scale * (grad_n - mean_grad - normal * mean_proj)


def column_sum(values):
    return jnp.sum(values, axis=0, keepdims=True)


def stack_pair(pair, low_lanes):
    zero = jnp.zeros_like(pair)
    return jnp.concatenate(
        [jnp.where(low_lanes, pair, zero), jnp.where(low_lanes, zero, pair)], axis=0
    )


def join_pair(stacked, low_lanes):
    half = stacked.shape[0] // 2
    return jnp.where(low_lanes, stacked[:half], stacked[half:])


def pipeline_kernel(
    stages,
    micros,
    token_ids,
    segment_ids,
    target_ids,
    embed,
    qkv_w,
    qv_b,
    out_w,
    out_b,
    in_w,
    in_b,
    down_w,
    gains,
    shifts,
    fin_gain,
    fin_bias,
    head_w,
    normed_o,
    mixed_o,
    normed2_o,
    active_o,
    gres_o,
    ghid_o,
    gbr_o,
    gproj_o,
    xl_o,
    xr_o,
    vec,
    instream,
    outb,
    gin,
    gs,
    normed,
    proj,
    probs,
    mixed,
    middle,
    normed2,
    active,
    slope,
    lo,
    go,
    gmid,
    s_gres,
    s_ghid,
    s_gbr,
    s_gproj,
    s_xl,
    ids,
    frames,
    fsend,
    frecv,
    bsend,
    brecv,
    osem,
):
    stage = lax.axis_index("pipe")
    tokens, width = instream.shape[1], instream.shape[2]
    hidden_n = in_b.shape[1]
    vocab = head_w.shape[0]
    pairs = width // ROW
    chunk = 512
    is_first = stage == 0
    is_last = stage == stages - 1
    up = jnp.minimum(stage + 1, stages - 1)
    down = jnp.maximum(stage - 1, 0)

    barrier = pltpu.get_barrier_semaphore()

    @pl.when(jnp.logical_not(is_first))
    def _():
        pl.semaphore_signal(barrier, inc=1, device_id={"pipe": down}, device_id_type=MESH)

    @pl.when(jnp.logical_not(is_last))
    def _():
        pl.semaphore_signal(barrier, inc=1, device_id={"pipe": up}, device_id_type=MESH)

    pl.semaphore_wait(barrier, jnp.where(is_first | is_last, 1, 2))
    vec[...] = jnp.zeros_like(vec)
    rows_n, seq = token_ids.shape
    for index, member in enumerate((token_ids, segment_ids, target_ids)):
        ids[index] = jnp.full(ids.shape[1:], 4.0 if index == 1 else -1.0, F32)
        ids[index, 0:rows_n, 0:seq] = member[...].astype(F32)
    at_query = lax.broadcasted_iota(jnp.int32, (ROW, ROW), 1)
    at_key = lax.broadcasted_iota(jnp.int32, (ROW, ROW), 0)
    frames[...] = jnp.where(at_key < ((at_query * 43) // 256) * FRAME + FRAME, 1.0, 0.0)

    def column(index, row):
        values = jnp.broadcast_to(ids[index, pl.ds(row, 1), :], (8, ROW))
        return values.T[:, 0:1]

    def hot_rows(index, m):
        parts = [column(index, m * GROUP + r) for r in range(GROUP)]
        values = jnp.concatenate(parts, axis=0)
        places = lax.broadcasted_iota(jnp.int32, (tokens, vocab), 1).astype(F32)
        return values, jnp.where(values == places, 1.0, 0.0)

    def forward_copy(m):
        return pltpu.make_async_remote_copy(
            src_ref=outb.at[m],
            dst_ref=instream.at[m],
            send_sem=fsend.at[m],
            recv_sem=frecv.at[m],
            device_id={"pipe": up},
            device_id_type=MESH,
        )

    def backward_copy(m):
        return pltpu.make_async_remote_copy(
            src_ref=gs.at[m],
            dst_ref=gin.at[m],
            send_sem=bsend.at[m],
            recv_sem=brecv.at[m],
            device_id={"pipe": down},
            device_id_type=MESH,
        )

    def save(index, src, dst, m):
        return pltpu.make_async_copy(src, dst.at[m], osem.at[index, m])

    def saves_forward(m):
        return [
            save(0, normed.at[m], normed_o, m),
            save(1, mixed.at[m], mixed_o, m),
            save(2, normed2.at[m], normed2_o, m),
            save(3, active.at[m], active_o, m),
        ]

    def saves_backward(m):
        slot = lax.rem(m, 2)
        return [
            save(4, s_gres.at[slot], gres_o, m),
            save(5, s_ghid.at[slot], ghid_o, m),
            save(6, s_gbr.at[slot], gbr_o, m),
            save(7, s_gproj.at[slot], gproj_o, m),
        ]

    def save_xl(m):
        return save(8, s_xl.at[lax.rem(m, 2)], xl_o, m)

    def put_xl(m, value):
        @pl.when(m >= 2)
        def _():
            save_xl(m - 2).wait()

        s_xl[lax.rem(m, 2)] = value
        save_xl(m).start()

    lane_low = lax.broadcasted_iota(jnp.int32, (ROW, ROW), 1) < ROW // 2

    def forward(m):
        @pl.when(is_first)
        def _():
            hot = hot_rows(0, m)[1].astype(BF16)
            instream[m] = dot(hot, embed[...]).astype(BF16)

        @pl.when(jnp.logical_not(is_first))
        def _():
            forward_copy(m).wait_recv()

        normal, _ = normalise(instream[m].astype(F32))
        normed[m] = (normal * gains[0:1, :] + shifts[0:1, :]).astype(BF16)
        low = normed[m]
        queries = dot(low, qkv_w[:, 0:width]) + qv_b[0:1, :]
        proj[m, :, 0:width] = (queries * (ROW // 2) ** -0.5).astype(BF16)
        proj[m, :, width : 2 * width] = dot(low, qkv_w[:, width : 2 * width]).astype(BF16)
        proj[m, :, 2 * width : 3 * width] = (
            dot(low, qkv_w[:, 2 * width : 3 * width]) + qv_b[1:2, :]
        ).astype(BF16)
        masks, scores = [], []
        for r in range(GROUP):
            rows = slice(r * ROW, (r + 1) * ROW)
            kinds = lax.broadcasted_iota(jnp.int32, (16, ROW), 0).astype(F32)
            member = jnp.where(ids[1, pl.ds(m * GROUP + r, 1), :] == kinds, 1.0, 0.0).astype(BF16)
            mask = jnp.where(dot_tn(member, member) * frames[...] > 0.5, 0.0, MASKED)
            masks.append(jnp.concatenate([mask, mask], axis=1))
            for p in range(pairs):
                q = stack_pair(proj[m, rows, p * ROW : (p + 1) * ROW], lane_low)
                k = proj[m, rows, width + p * ROW : width + (p + 1) * ROW]
                scores.append(dot_nt(k, q))

        def mix(unit):
            r, p = unit // pairs, unit % pairs
            rows = slice(r * ROW, (r + 1) * ROW)
            v = proj[m, rows, 2 * width + p * ROW : 2 * width + (p + 1) * ROW]
            both = dot_tn(probs[m, unit], v)
            mixed[m, rows, p * ROW : (p + 1) * ROW] = join_pair(both, lane_low).astype(BF16)

        for unit in range(GROUP * pairs):
            masked = scores[unit] + masks[unit // pairs]
            expo = jnp.exp(masked - jnp.max(masked, axis=0, keepdims=True))
            total = jnp.sum(expo, axis=0, keepdims=True)
            probs[m, unit] = (expo * (1.0 / total)).astype(BF16)
            if unit:
                mix(unit - 1)
        mix(GROUP * pairs - 1)
        mid = instream[m].astype(F32) + (dot(mixed[m], out_w[...]) + out_b[0:1, :])
        middle[m] = mid
        normal2, _ = normalise(mid)
        normed2[m] = (normal2 * gains[1:2, :] + shifts[1:2, :]).astype(BF16)
        low2 = normed2[m]
        parts = hidden_n // chunk

        def spread(c):
            return dot(low2, in_w[:, c * chunk : (c + 1) * chunk])

        total, ahead = None, spread(0)
        for c in range(parts):
            cols = slice(c * chunk, (c + 1) * chunk)
            hid = ahead + in_b[0:1, cols]
            if c + 1 < parts:
                ahead = spread(c + 1)
            square = hid * hid
            tan = jnp.tanh(hid * (GELU_A + (GELU_A * GELU_B) * square))
            half = 0.5 + 0.5 * tan
            act = (hid * half).astype(BF16)
            active[m, :, cols] = act
            rise = (1.0 - tan * tan) * (0.5 * GELU_A + (1.5 * GELU_A * GELU_B) * square)
            slope[m, :, cols] = (half + hid * rise).astype(BF16)
            term = dot(act, down_w[cols, :])
            total = term if total is None else total + term
        for copy in saves_forward(m):
            copy.start()
        lo[...] = middle[m] + (total + out_b[1:2, :])

        @pl.when(jnp.logical_not(is_last))
        def _():
            outb[m] = lo[...].astype(BF16)
            forward_copy(m).start()

    def head(m):
        normal, scale = normalise(lo[...])
        outb[m] = (normal * fin_gain[...] + fin_bias[...]).astype(BF16)
        save(9, outb.at[m], xr_o, m).start()
        logits = dot_nt(outb[m], head_w[...])
        top = jnp.max(logits, axis=-1, keepdims=True)
        expo = jnp.exp(logits - top)
        total = jnp.sum(expo, axis=-1, keepdims=True)
        target, hot = hot_rows(2, m)
        grad_logits = jnp.where(target >= 0.0, expo * (1.0 / total) - hot, 0.0).astype(BF16)
        put_xl(m, grad_logits)
        grad_final = dot(grad_logits, head_w[...])
        vec[V_FINAL_GAIN : V_FINAL_GAIN + 1, :] += column_sum(grad_final * normal)
        vec[V_FINAL_BIAS : V_FINAL_BIAS + 1, :] += column_sum(grad_final)
        go[...] = norm_backward(grad_final, normal, scale, fin_gain[...])

    def backward(m):
        slot = lax.rem(m, 2)

        @pl.when(m >= 2)
        def _():
            for copy in saves_backward(m - 2):
                copy.wait()

        @pl.when(jnp.logical_not(is_last))
        def _():
            backward_copy(m).wait_recv()
            go[...] = gin[m].astype(F32)

        s_gres[slot] = go[...].astype(BF16)
        gres = s_gres[slot]
        parts = hidden_n // chunk

        def spread(c):
            return dot_nt(gres, down_w[c * chunk : (c + 1) * chunk, :])

        total, ahead = None, spread(0)
        for c in range(parts):
            cols = slice(c * chunk, (c + 1) * chunk)
            gact = ahead
            if c + 1 < parts:
                ahead = spread(c + 1)
            ghid = (gact * slope[m, :, cols].astype(F32)).astype(BF16)
            s_ghid[slot, :, cols] = ghid
            term = dot_nt(ghid, in_w[:, cols])
            total = term if total is None else total + term
        normal2, scale2 = normalise(middle[m])
        vec[V_GAIN2 : V_GAIN2 + 1, :] += column_sum(total * normal2)
        vec[V_SHIFT2 : V_SHIFT2 + 1, :] += column_sum(total)
        gmid[...] = go[...] + norm_backward(total, normal2, scale2, gains[1:2, :])
        s_gbr[slot] = gmid[...].astype(BF16)
        gbr = s_gbr[slot]
        gmix = dot_nt(gbr, out_w[...]).astype(BF16)
        grads = []
        for r in range(GROUP):
            rows = slice(r * ROW, (r + 1) * ROW)
            for p in range(pairs):
                gm = stack_pair(gmix[rows, p * ROW : (p + 1) * ROW], lane_low)
                vlanes = slice(2 * width + p * ROW, 2 * width + (p + 1) * ROW)
                grads.append(dot_nt(proj[m, rows, vlanes], gm))
                s_gproj[slot, rows, vlanes] = dot(probs[m, r * pairs + p], gm).astype(BF16)

        def pull(unit, gsc):
            r, p = unit // pairs, unit % pairs
            rows = slice(r * ROW, (r + 1) * ROW)
            lanes = slice(p * ROW, (p + 1) * ROW)
            klanes = slice(width + p * ROW, width + (p + 1) * ROW)
            q = stack_pair(proj[m, rows, lanes], lane_low)
            s_gproj[slot, rows, klanes] = dot(gsc, q).astype(BF16)
            gq = join_pair(dot_tn(gsc, proj[m, rows, klanes]), lane_low) * (ROW // 2) ** -0.5
            s_gproj[slot, rows, lanes] = gq.astype(BF16)

        waiting = None
        for unit in range(GROUP * pairs):
            weights = probs[m, unit].astype(F32)
            inner = jnp.sum(weights * grads[unit], axis=0, keepdims=True)
            gsc = (weights * (grads[unit] - inner)).astype(BF16)
            if waiting is not None:
                pull(unit - 1, waiting)
            waiting = gsc
        pull(GROUP * pairs - 1, waiting)
        for copy in saves_backward(m):
            copy.start()
        gproj = s_gproj[slot]
        gnormed = dot_nt(gproj, qkv_w[...])
        normal, scale = normalise(instream[m].astype(F32))
        vec[V_GAIN1 : V_GAIN1 + 1, :] += column_sum(gnormed * normal)
        vec[V_SHIFT1 : V_SHIFT1 + 1, :] += column_sum(gnormed)
        gs[m] = (gmid[...] + norm_backward(gnormed, normal, scale, gains[0:1, :])).astype(BF16)

        @pl.when(is_first)
        def _():
            save(9, gs.at[m], xr_o, m).start()

        @pl.when(jnp.logical_not(is_first))
        def _():
            backward_copy(m).start()

    def tick(t, carry):
        m_forward = t - stage
        m_backward = t - (2 * (stages - 1) - stage)

        @pl.when((m_forward >= 0) & (m_forward < micros))
        def _():
            forward(m_forward)

        @pl.when((m_backward >= 0) & (m_backward < micros))
        def _():
            @pl.when(is_last)
            def _():
                head(m_backward)

            backward(m_backward)

        return carry

    lax.fori_loop(0, micros + 2 * (stages - 1), tick, 0)

    for m in range(micros):
        for copy in saves_forward(m):
            copy.wait()

        @pl.when(jnp.logical_not(is_last))
        def _():
            forward_copy(m).wait_send()

        @pl.when(jnp.logical_not(is_first))
        def _():
            backward_copy(m).wait_send()

        @pl.when(is_first)
        def _():
            save(9, gs.at[m], xr_o, m).wait()

        @pl.when(is_last)
        def _():
            save(9, outb.at[m], xr_o, m).wait()

    for m in range(max(0, micros - 2), micros):
        for copy in saves_backward(m):
            copy.wait()

        @pl.when(is_last)
        def _():
            save_xl(m).wait()


def run_pipeline(stages, token_ids, segment_ids, target_ids, params):
    embed, in_w, head_w = params[0], params[5], params[12]
    width = embed.shape[1]
    vocab = head_w.shape[0]
    hid = in_w.shape[1]
    tokens = GROUP * ROW
    micros = token_ids.shape[0] // GROUP
    pairs = width // ROW
    vmem = pl.BlockSpec(memory_space=pltpu.VMEM)
    hbm = pl.BlockSpec(memory_space=pl.ANY)

    def kept(columns):
        return jax.ShapeDtypeStruct((micros, tokens, columns), BF16)

    def scratch(lead, columns, kind=BF16):
        return pltpu.VMEM((lead, tokens, columns), kind)

    out_shape = [
        kept(width),
        kept(width),
        kept(width),
        kept(hid),
        kept(width),
        kept(hid),
        kept(width),
        kept(3 * width),
        kept(vocab),
        kept(width),
        jax.ShapeDtypeStruct((VEC_ROWS, width), F32),
    ]
    return pl.pallas_call(
        functools.partial(pipeline_kernel, stages, micros),
        out_shape=out_shape,
        in_specs=[vmem] * 16,
        out_specs=[hbm] * 10 + [vmem],
        scratch_shapes=[
            scratch(micros, width),
            scratch(micros, width),
            scratch(micros, width),
            scratch(micros, width),
            scratch(micros, width),
            scratch(micros, 3 * width),
            pltpu.VMEM((micros, GROUP * pairs, ROW, 2 * ROW), BF16),
            scratch(micros, width),
            scratch(micros, width, F32),
            scratch(micros, width),
            scratch(micros, hid),
            scratch(micros, hid),
            pltpu.VMEM((tokens, width), F32),
            pltpu.VMEM((tokens, width), F32),
            pltpu.VMEM((tokens, width), F32),
            scratch(2, width),
            scratch(2, hid),
            scratch(2, width),
            scratch(2, 3 * width),
            scratch(2, vocab),
            pltpu.VMEM((3, 16, ROW), F32),
            pltpu.VMEM((ROW, ROW), F32),
            pltpu.SemaphoreType.DMA((micros,)),
            pltpu.SemaphoreType.DMA((micros,)),
            pltpu.SemaphoreType.DMA((micros,)),
            pltpu.SemaphoreType.DMA((micros,)),
            pltpu.SemaphoreType.DMA((10, micros)),
        ],
        compiler_params=pltpu.CompilerParams(
            collective_id=0, has_side_effects=True, vmem_limit_bytes=62 * 1024 * 1024
        ),
        name="pipeline",
    )(token_ids, segment_ids, target_ids, *params)


def line_dims(devices):
    dims, stride = [], 1
    if devices == 8:
        return [(2, 1), (4, 2)]
    while devices > 1:
        size = 4 if devices % 4 == 0 else 2
        dims.append((size, stride))
        stride *= size
        devices //= size
    return dims


def chunk_plan(width, hid, vocab, stages, devices):
    slim, deep = width // devices, hid // devices
    plan = [("out", 0, (slim, width), False)]
    for c in range(4):
        plan.append(("down", c, (deep, width // 4), c in (1, 3)))
    for c in range(2):
        plan.append(("extra", c, (stages, vocab // (stages * devices), width // 2), False))
    for c in range(hid // width):
        plan.append(("in", c, (slim, width), c == 1))
    for c in range(3):
        plan.append(("qkv", c, (slim, width), False))
    return plan


def gradient_kernel(stages, devices, plan, *refs):
    dims = line_dims(devices)
    refs = list(refs)

    def take(amount):
        head, refs[:] = refs[:amount], refs[amount:]
        return head

    inputs = take(10)
    vec_in, token_ids = take(2)
    qkv_out, out_out, in_out, down_out, embed_out, head_out, vec_out = take(7)
    local = take(10)
    in_sem = take(1)[0]
    turned_left, turned_xl = take(2)
    mats = dict(
        zip(
            ("normed", "mixed", "normed2", "active", "gres", "ghid", "gbr", "gproj", "xl", "xr"),
            local,
        )
    )
    names = list(mats)
    stage = lax.axis_index("pipe")
    place = lax.axis_index("dp")
    is_extra = (stage == 0) | (stage == stages - 1)
    width = mats["normed"].shape[1]
    where = [lax.rem(place // stride, size) for size, stride in dims]

    barrier = pltpu.get_barrier_semaphore()

    def greet(offset, carry):
        peer = lax.rem(place + offset, devices)
        pl.semaphore_signal(barrier, inc=1, device_id={"dp": peer}, device_id_type=MESH)
        return carry

    def greet_stage(offset, carry):
        peer = lax.rem(stage + offset, stages)
        pl.semaphore_signal(barrier, inc=1, device_id={"pipe": peer}, device_id_type=MESH)
        return carry

    lax.fori_loop(1, devices, greet, 0)
    lax.fori_loop(1, stages, greet_stage, 0)

    def load(name):
        i = names.index(name)
        return pltpu.make_async_copy(inputs[i], mats[name], in_sem.at[i])

    groups = [("mixed", "gbr"), ("gres", "active"), ("xr", "xl"), ("normed2", "ghid"), ("normed", "gproj")]

    def fetch(at):
        if at >= len(groups):
            return
        if groups[at] == ("xr", "xl"):
            @pl.when(is_extra)
            def _():
                load("xr").start()

            @pl.when(stage == stages - 1)
            def _():
                load("xl").start()

            at += 1
        for name in groups[at]:
            load(name).start()

    fetch(0)
    loaded = set()

    def need(*wanted):
        fresh = [name for name in wanted if name not in loaded]
        for name in fresh:
            loaded.add(name)
            load(name).wait()
        if fresh:
            at = [i for i, group in enumerate(groups) if group[0] == fresh[0]][0]
            fetch(at + 1)

    def identity(size):
        here = lax.broadcasted_iota(jnp.int32, (size, size), 0)
        there = lax.broadcasted_iota(jnp.int32, (size, size), 1)
        return jnp.where(here == there, 1.0, 0.0).astype(BF16)

    held = []

    def turn(name):
        if held[-1:] == [name]:
            return
        held.append(name)
        unit = identity(256)
        for q in range(width // 256):
            part = dot_nt(unit, mats[name][:, q * 256 : (q + 1) * 256])
            turned_left[q * 256 : (q + 1) * 256, :] = part.astype(BF16)

    bits = devices.bit_length() - 1
    vec_send, vec_recv = take(2)
    vec_sems = take(2)

    def vec_copy(k):
        peer = jnp.bitwise_xor(place, 1 << k)
        return pltpu.make_async_remote_copy(
            src_ref=vec_send.at[k],
            dst_ref=vec_recv.at[k],
            send_sem=vec_sems[0].at[k],
            recv_sem=vec_sems[1].at[k],
            device_id={"dp": peer},
            device_id_type=MESH,
        )

    def vec_step(k):
        def run():
            if k == 0:
                vec_send[0] = vec_in[...]
                ones = jnp.ones((16, mats["gres"].shape[0]), BF16)
                for name, start, row in (
                    ("gproj", 0, V_QUERY),
                    ("gproj", 2 * width, V_VALUE),
                    ("gbr", 0, V_BRANCH),
                    ("gres", 0, V_RESULT),
                ):
                    part = dot(ones, mats[name][:, start : start + width])
                    vec_send[0, row : row + 1, :] = part[0:1, :]
                for q in range(mats["ghid"].shape[1] // width):
                    part = dot(ones, mats["ghid"][:, q * width : (q + 1) * width])
                    vec_send[0, V_HIDDEN + q : V_HIDDEN + q + 1, :] = part[0:1, :]
            else:
                vec_copy(k - 1).wait_recv()
                vec_send[k] = vec_send[k - 1] + vec_recv[k - 1]
            if k < bits:
                vec_copy(k).start()

        return run

    final_send, final_recv = take(2)
    final_sems = take(2)

    def final_copy(offset):
        peer = lax.rem(stages - 1 + offset, stages)
        return pltpu.make_async_remote_copy(
            src_ref=final_send,
            dst_ref=final_recv,
            send_sem=final_sems[0].at[offset],
            recv_sem=final_sems[1].at[0],
            device_id={"pipe": peer},
            device_id_type=MESH,
        )

    def vec_last():
        vec_step(bits)()
        vec_out[...] = vec_send[bits]

        @pl.when(stage == stages - 1)
        def _():
            final_send[...] = vec_send[bits, 8:16, :]
            for offset in range(1, stages):
                final_copy(offset).start()

    def vec_finish():
        @pl.when(stage != stages - 1)
        def _():
            final_copy(1).wait_recv()
            vec_out[V_FINAL_GAIN : V_FINAL_BIAS + 1, :] = final_recv[
                V_FINAL_GAIN - 8 : V_FINAL_BIAS - 7, :
            ]

    def vec_drain():
        for k in range(bits):
            vec_copy(k).wait_send()

        @pl.when(stage == stages - 1)
        def _():
            for offset in range(1, stages):
                final_copy(offset).wait_send()

    extra_sum, extra_send_sem, extra_recv_sem = take(3)

    def extra_copy(source, offset, target):
        peer = lax.rem(source + offset, stages)
        return pltpu.make_async_remote_copy(
            src_ref=extra_sum.at[peer],
            dst_ref=target,
            send_sem=extra_send_sem.at[offset],
            recv_sem=extra_recv_sem.at[0 if source == 0 else 1],
            device_id={"pipe": peer},
            device_id_type=MESH,
        )

    down_full = {}

    def chunk_steps(kind, c, block, turned):
        order = list(range(len(dims)))
        if turned:
            order.reverse()
        full = take(1)[0]

        def compute():
            if kind == "down":
                need("gres", "active")
                turn("gres")
                if c % 2 == 1:
                    return
                half = width // 2
                lines = slice((c // 2) * half, (c // 2 + 1) * half)
                parts = dot(turned_left[lines, :], mats["active"][...]).astype(BF16)
                depth = block[0]
                unit = identity(depth)
                for d in range(devices):
                    back = dot_nt(unit, parts[:, d * depth : (d + 1) * depth]).astype(BF16)
                    down_full[c][split(d)] = back[:, 0 : half // 2]
                    down_full[c + 1][split(d)] = back[:, half // 2 : half]
            elif kind == "extra":
                vocab = turned_xl.shape[0]
                if c == 0:
                    load("xr").wait()

                @pl.when((stage == 0) & (c == 0))
                def _():
                    rows_n, seq = token_ids.shape
                    places = lax.broadcasted_iota(jnp.int32, (vocab, ROW), 0)
                    gap = jnp.full((1, ROW - seq), -1, jnp.int32)
                    for r in range(rows_n):
                        row = jnp.concatenate([token_ids[r : r + 1, :], gap], axis=1)
                        hot = jnp.where(places == row, 1.0, 0.0)
                        turned_xl[:, r * ROW : (r + 1) * ROW] = hot.astype(BF16)

                @pl.when((stage == stages - 1) & (c == 0))
                def _():
                    load("xl").wait()
                    unit = identity(256)
                    for q in range(vocab // 256):
                        part = dot_nt(unit, mats["xl"][:, q * 256 : (q + 1) * 256])
                        turned_xl[q * 256 : (q + 1) * 256, :] = part.astype(BF16)

                rows = vocab // stages
                for p in range(stages):
                    part = dot(
                        turned_xl[p * rows : (p + 1) * rows, :],
                        mats["xr"][:, c * (width // 2) : (c + 1) * (width // 2)],
                    )
                    part = part.astype(BF16).reshape((devices,) + block[1:])
                    for d in range(devices):
                        full[split(d) + (p,)] = part[d]
            else:
                left, right = {
                    "in": ("normed2", "ghid"),
                    "out": ("mixed", "gbr"),
                    "qkv": ("normed", "gproj"),
                }[kind]
                need(left, right)
                turn(left)
                cols = slice(c * width, (c + 1) * width)
                part = dot(turned_left[...], mats[right][:, cols]).astype(BF16)
                part = part.reshape((devices,) + block)
                for d in range(devices):
                    full[split(d)] = part[d]

        def split(d):
            return tuple((d // stride) % size for size, stride in reversed(dims))

        if kind == "down":
            down_full[c] = full
        steps = [[compute]]
        for at, phase in enumerate(order):
            size = dims[phase][0]
            buffers = take(3)
            done = order[:at]
            last = at == len(order) - 1
            steps[-1].append(functools.partial(line_step, phase, size, 1, full, buffers, done))
            for t in range(2, size):
                steps.append([functools.partial(line_step, phase, size, t, full, buffers, done)])
            drains.append((kind, functools.partial(line_drain, phase, size, full, buffers, done)))
            steps.append([functools.partial(line_final, kind, c, phase, size, full, buffers, done, last)])
        if kind == "extra":
            steps = [[gated([part]) for part in step] for step in steps]
        return steps

    def gated(step):
        def run():
            @pl.when(is_extra)
            def _():
                for part in step:
                    part()

        return run

    def block_of(full, phase, j, done):
        spot = [slice(None)] * len(dims)
        for other in done:
            spot[len(dims) - 1 - other] = where[other]
        spot[len(dims) - 1 - phase] = j
        return full.at[tuple(spot)]

    def line_copy(phase, size, t, side, full, buffers, done):
        recv, ssem, rsem = buffers
        i = where[phase]
        stride = dims[phase][1]
        if side == 0:
            j, peer = size - t + i, place + jnp.where(i < size - 1, stride, 0)
        else:
            j, peer = t - size + i, place - jnp.where(i > 0, stride, 0)
        return pltpu.make_async_remote_copy(
            src_ref=block_of(full, phase, jnp.clip(j, 0, size - 1), done),
            dst_ref=recv.at[0 if size == 2 else side, t - 1],
            send_sem=ssem.at[side, t - 1],
            recv_sem=rsem.at[side, t - 1],
            device_id={"dp": peer},
            device_id_type=MESH,
        )

    def sends(i, size, t, side):
        return (i <= t - 1) if side == 0 else (i >= size - t)

    def line_step(phase, size, t, full, buffers, done):
        i = where[phase]
        for side in range(2):
            at_end = (i == 0) if side == 0 else (i == size - 1)
            j = size - t + i if side == 0 else t - size + i
            j = jnp.clip(j, 0, size - 1)

            @pl.when(sends(i, size, t, side))
            def _():
                if t > 1:
                    @pl.when(jnp.logical_not(at_end))
                    def _():
                        line_copy(phase, size, t - 1, side, full, buffers, done).wait_recv()
                        own = block_of(full, phase, j, done)
                        got = buffers[0][0 if size == 2 else side, t - 2]
                        own[...] = (own[...].astype(F32) + got.astype(F32)).astype(BF16)

                line_copy(phase, size, t, side, full, buffers, done).start()

    def line_final(kind, c, phase, size, full, buffers, done, last):
        i = where[phase]
        own = block_of(full, phase, i, done)
        total = own
        if last:
            slots = {
                "qkv": lambda: qkv_out.at[:, c * width : (c + 1) * width],
                "in": lambda: in_out.at[:, c * width : (c + 1) * width],
                "out": lambda: out_out,
                "down": lambda: down_out.at[:, c * (width // 4) : (c + 1) * (width // 4)],
                "extra": lambda: extra_sum.at[:, :, c * (width // 2) : (c + 1) * (width // 2)],
            }
            total = slots[kind]()
        lower, upper = i > 0, i < size - 1

        def arrived(side):
            line_copy(phase, size, size - 1, side, full, buffers, done).wait_recv()
            return buffers[0][0 if size == 2 else side, size - 2].astype(F32)

        @pl.when(lower & upper)
        def _():
            total[...] = (own[...].astype(F32) + arrived(0) + arrived(1)).astype(total.dtype)

        @pl.when(lower & jnp.logical_not(upper))
        def _():
            total[...] = (own[...].astype(F32) + arrived(0)).astype(total.dtype)

        @pl.when(jnp.logical_not(lower))
        def _():
            total[...] = (own[...].astype(F32) + arrived(1)).astype(total.dtype)

        if last and kind == "extra" and c == 1:
            for source_stage, out in ((0, embed_out), (stages - 1, head_out)):
                @pl.when(stage == source_stage)
                def _():
                    for offset in range(1, stages):
                        extra_copy(source_stage, offset, extra_recv[0 if source_stage == 0 else 1]).start()
                    out[...] = extra_sum[source_stage]

    def line_drain(phase, size, full, buffers, done):
        i = where[phase]
        for side in range(2):
            for t in range(1, size):
                @pl.when(sends(i, size, t, side))
                def _():
                    line_copy(phase, size, t, side, full, buffers, done).wait_send()

    extra_recv = take(2)
    drains = []
    chains = [chunk_steps(*item) for item in plan]
    depth = len(chains[0])
    vec_chain = [vec_step(k) for k in range(bits)] + [vec_last]
    starts, first, extra_rounds = [], 0, iter((1, 3, 6, 8))
    for item in plan:
        if item[3]:
            starts.append(next(extra_rounds))
        else:
            starts.append(first)
            first += 1
    begun = False
    loaded_at = max(start for start, item in zip(starts, plan) if item[0] == "qkv" and item[1] == 0)
    for r in range(max(starts) + depth):
        for d in [0] + list(range(depth - 1, 0, -1)):
            for start, chain in zip(starts, chains):
                if r - start != d:
                    continue
                for part in chain[d]:
                    part()
                    if not begun:
                        begun = True
                        pl.semaphore_wait(barrier, devices - 1 + stages - 1)
        if 0 <= r - loaded_at < len(vec_chain):
            vec_chain[r - loaded_at]()
    vec_finish()
    for source_stage, out in ((0, embed_out), (stages - 1, head_out)):
        @pl.when(stage != source_stage)
        def _():
            got = extra_recv[0 if source_stage == 0 else 1]
            extra_copy(source_stage, 1, got).wait_recv()
            out[...] = got[...]

        @pl.when(stage == source_stage)
        def _():
            for offset in range(1, stages):
                extra_copy(source_stage, offset, extra_recv[0]).wait_send()

    vec_drain()
    for kind, drain in drains:
        if kind == "extra":
            gated([drain])()
        else:
            drain()


def run_gradients(stages, devices, saved, vec, token_ids):
    dims = line_dims(devices)
    rows, tokens, width = saved[0].shape
    hid, vocab = saved[3].shape[2], saved[8].shape[2]
    plan = chunk_plan(width, hid, vocab, stages, devices)
    saved = [member.reshape(rows * tokens, member.shape[2]) for member in saved]
    vmem = pl.BlockSpec(memory_space=pltpu.VMEM)
    hbm = pl.BlockSpec(memory_space=pl.ANY)
    bits = devices.bit_length() - 1
    share = vocab // (stages * devices)
    scratch = [pltpu.VMEM(member.shape, BF16) for member in saved]
    scratch += [pltpu.SemaphoreType.DMA((len(saved),))]
    scratch += [pltpu.VMEM((width, rows * tokens), BF16), pltpu.VMEM((vocab, rows * tokens), BF16)]
    scratch += [
        pltpu.VMEM((bits + 1,) + vec.shape, F32),
        pltpu.VMEM((bits,) + vec.shape, F32),
        pltpu.SemaphoreType.DMA((bits,)),
        pltpu.SemaphoreType.DMA((bits,)),
        pltpu.VMEM((8, width), F32),
        pltpu.VMEM((8, width), F32),
        pltpu.SemaphoreType.DMA((stages,)),
        pltpu.SemaphoreType.DMA((1,)),
        pltpu.VMEM((stages, share, width), F32),
        pltpu.SemaphoreType.DMA((stages,)),
        pltpu.SemaphoreType.DMA((2,)),
        pltpu.VMEM((share, width), F32),
        pltpu.VMEM((share, width), F32),
    ]
    sizes = [size for size, _ in reversed(dims)]
    for _, _, block, turned in plan:
        scratch.append(pltpu.VMEM(tuple(sizes) + block, BF16))
        remain = list(reversed(dims))
        for size, stride in dims[::-1] if turned else dims:
            remain.remove((size, stride))
            piece = tuple(other for other, _ in remain) + block
            scratch.append(pltpu.VMEM((1 if size == 2 else 2, size - 1) + piece, BF16))
            scratch += [pltpu.SemaphoreType.DMA((2, size - 1))] * 2
    return pl.pallas_call(
        functools.partial(gradient_kernel, stages, devices, plan),
        out_shape=[
            jax.ShapeDtypeStruct((width // devices, 3 * width), F32),
            jax.ShapeDtypeStruct((width // devices, width), F32),
            jax.ShapeDtypeStruct((width // devices, hid), F32),
            jax.ShapeDtypeStruct((hid // devices, width), F32),
            jax.ShapeDtypeStruct((share, width), F32),
            jax.ShapeDtypeStruct((share, width), F32),
            jax.ShapeDtypeStruct(vec.shape, F32),
        ],
        in_specs=[hbm] * len(saved) + [vmem] * 2,
        out_specs=[vmem] * 7,
        scratch_shapes=scratch,
        compiler_params=pltpu.CompilerParams(
            collective_id=1, has_side_effects=True, vmem_limit_bytes=62 * 1024 * 1024
        ),
        name="gradients",
    )(*saved, vec, token_ids)


def step_kernel(stages, micros, devices, plan, *refs):
    refs = list(refs)

    def take(amount):
        head, refs[:] = refs[:amount], refs[amount:]
        return head

    token_ids, segment_ids, target_ids = take(3)
    qv_b, out_b, in_b, gains, shifts, fin_gain, fin_bias = take(7)
    embed_h, head_h, qkv_h, out_h, in_h, down_h = take(6)
    qkv_out, out_out, in_out, down_out, embed_out, head_out, vec_out = take(7)
    side, qkv_w, out_w = take(3)
    in_w, down_w = take(4), take(4)
    instream, outb, gin, gs, proj, probs, mixed, middle, active, slope = take(10)
    lo, gmid, s_gbr, s_xl, vec, ids, frames = take(7)
    fsend, frecv, bsend, brecv, wsem = take(5)
    go = lo
    place = lax.axis_index("dp")
    stage = lax.axis_index("pipe")
    tokens, width = instream.shape[1], instream.shape[2]
    hidden_n = in_b.shape[1]
    vocab = side.shape[0]
    pairs = width // ROW
    chunk = 512
    is_first = stage == 0
    is_last = stage == stages - 1
    up = jnp.minimum(stage + 1, stages - 1)
    down = jnp.maximum(stage - 1, 0)

    def bring(index, source, target):
        return pltpu.make_async_copy(source, target, wsem.at[index])

    weights = [bring(1, qkv_h, qkv_w), bring(2, out_h, out_w)]
    for c in range(4):
        lanes = pl.ds(c * chunk, chunk)
        weights.append(bring(3 + c, in_h.at[:, :, :, lanes], in_w[c]))
        weights.append(bring(7 + c, down_h.at[c], down_w[c]))

    @pl.when(is_first)
    def _():
        bring(0, embed_h, side).start()

    for copy in weights:
        copy.start()

    @pl.when(is_last)
    def _():
        bring(0, head_h, side).start()

    barrier = pltpu.get_barrier_semaphore()

    def greet(offset, carry):
        peer = lax.rem(place + offset, devices)
        pl.semaphore_signal(barrier, inc=1, device_id={"dp": peer}, device_id_type=MESH)
        return carry

    def greet_stage(offset, carry):
        peer = lax.rem(stage + offset, stages)
        pl.semaphore_signal(barrier, inc=1, device_id={"pipe": peer}, device_id_type=MESH)
        return carry

    lax.fori_loop(1, devices, greet, 0)
    lax.fori_loop(1, stages, greet_stage, 0)

    def whole(part):
        return part[...].reshape(width, width)

    vec[...] = jnp.zeros_like(vec)
    rows_n, seq = token_ids.shape
    for index, member in enumerate((token_ids, segment_ids, target_ids)):
        ids[index] = jnp.full(ids.shape[1:], 4.0 if index == 1 else -1.0, F32)
        ids[index, 0:rows_n, 0:seq] = member[...].astype(F32)
    at_query = lax.broadcasted_iota(jnp.int32, (ROW, ROW), 1)
    at_key = lax.broadcasted_iota(jnp.int32, (ROW, ROW), 0)
    frames[...] = jnp.where(at_key < ((at_query * 43) // 256) * FRAME + FRAME, 1.0, 0.0)

    def column(index, row):
        values = jnp.broadcast_to(ids[index, pl.ds(row, 1), :], (8, ROW))
        return values.T[:, 0:1]

    def hot_rows(index, m):
        parts = [column(index, m * GROUP + r) for r in range(GROUP)]
        values = jnp.concatenate(parts, axis=0)
        places = lax.broadcasted_iota(jnp.int32, (tokens, vocab), 1).astype(F32)
        return values, jnp.where(values == places, 1.0, 0.0)

    def forward_copy(m):
        return pltpu.make_async_remote_copy(
            src_ref=outb.at[m],
            dst_ref=instream.at[m],
            send_sem=fsend.at[m],
            recv_sem=frecv.at[m],
            device_id={"pipe": up},
            device_id_type=MESH,
        )

    def backward_copy(m):
        return pltpu.make_async_remote_copy(
            src_ref=gs.at[m],
            dst_ref=gin.at[m],
            send_sem=bsend.at[m],
            recv_sem=brecv.at[m],
            device_id={"pipe": down},
            device_id_type=MESH,
        )

    @pl.when(is_first | is_last)
    def _():
        bring(0, embed_h, side).wait()

    for copy in weights:
        copy.wait()
    pl.semaphore_wait(barrier, devices - 1 + stages - 1)

    lane_low = lax.broadcasted_iota(jnp.int32, (ROW, ROW), 1) < ROW // 2

    def forward(m):
        @pl.when(is_first)
        def _():
            hot = hot_rows(0, m)[1].astype(BF16)
            instream[m] = dot(hot, side[...]).astype(BF16)

        @pl.when(jnp.logical_not(is_first))
        def _():
            forward_copy(m).wait_recv()

        normal, _ = normalise(instream[m].astype(F32))
        low = (normal * gains[0:1, :] + shifts[0:1, :]).astype(BF16)
        queries = dot(low, qkv_w[:, 0:width]) + qv_b[0:1, :]
        proj[m, :, 0:width] = (queries * (ROW // 2) ** -0.5).astype(BF16)
        proj[m, :, width : 2 * width] = dot(low, qkv_w[:, width : 2 * width]).astype(BF16)
        proj[m, :, 2 * width : 3 * width] = (
            dot(low, qkv_w[:, 2 * width : 3 * width]) + qv_b[1:2, :]
        ).astype(BF16)
        masks, scores = [], []
        for r in range(GROUP):
            rows = slice(r * ROW, (r + 1) * ROW)
            kinds = lax.broadcasted_iota(jnp.int32, (16, ROW), 0).astype(F32)
            member = jnp.where(ids[1, pl.ds(m * GROUP + r, 1), :] == kinds, 1.0, 0.0).astype(BF16)
            mask = jnp.where(dot_tn(member, member) * frames[...] > 0.5, 0.0, MASKED)
            masks.append(jnp.concatenate([mask, mask], axis=1))
            for p in range(pairs):
                q = stack_pair(proj[m, rows, p * ROW : (p + 1) * ROW], lane_low)
                k = proj[m, rows, width + p * ROW : width + (p + 1) * ROW]
                scores.append(dot_nt(k, q))

        def mix(unit):
            r, p = unit // pairs, unit % pairs
            rows = slice(r * ROW, (r + 1) * ROW)
            v = proj[m, rows, 2 * width + p * ROW : 2 * width + (p + 1) * ROW]
            both = dot_tn(probs[m, unit // 2, unit % 2], v)
            mixed[m, rows, p * ROW : (p + 1) * ROW] = join_pair(both, lane_low).astype(BF16)

        for unit in range(GROUP * pairs):
            masked = scores[unit] + masks[unit // pairs]
            expo = jnp.exp(masked - jnp.max(masked, axis=0, keepdims=True))
            total = jnp.sum(expo, axis=0, keepdims=True)
            probs[m, unit // 2, unit % 2] = (expo * (1.0 / total)).astype(BF16)
            if unit:
                mix(unit - 1)
        mix(GROUP * pairs - 1)
        mid = instream[m].astype(F32) + (dot(mixed[m], out_w[...]) + out_b[0:1, :])
        middle[m] = mid
        normal2, _ = normalise(mid)
        low2 = (normal2 * gains[1:2, :] + shifts[1:2, :]).astype(BF16)
        parts = hidden_n // chunk

        def spread(c):
            return dot(low2, whole(in_w[c]))

        total, ahead = None, spread(0)
        for c in range(parts):
            cols = slice(c * chunk, (c + 1) * chunk)
            hid = ahead + in_b[0:1, cols]
            if c + 1 < parts:
                ahead = spread(c + 1)
            square = hid * hid
            tan = jnp.tanh(hid * (GELU_A + (GELU_A * GELU_B) * square))
            half = 0.5 + 0.5 * tan
            act = (hid * half).astype(BF16)
            active[m, :, cols] = act
            rise = (1.0 - tan * tan) * (0.5 * GELU_A + (1.5 * GELU_A * GELU_B) * square)
            slope[m, :, cols] = (half + hid * rise).astype(BF16)
            term = dot(act, whole(down_w[c]))
            total = term if total is None else total + term
        lo[...] = middle[m] + (total + out_b[1:2, :])

        @pl.when(jnp.logical_not(is_last))
        def _():
            outb[m] = lo[...].astype(BF16)
            forward_copy(m).start()

    def head(m):
        normal, scale = normalise(lo[...])
        outb[m] = (normal * fin_gain[...] + fin_bias[...]).astype(BF16)
        logits = dot_nt(outb[m], side[...])
        top = jnp.max(logits, axis=-1, keepdims=True)
        expo = jnp.exp(logits - top)
        total = jnp.sum(expo, axis=-1, keepdims=True)
        target, hot = hot_rows(2, m)
        grad_logits = jnp.where(target >= 0.0, expo * (1.0 / total) - hot, 0.0).astype(BF16)
        s_xl[m] = grad_logits
        grad_final = dot(grad_logits, side[...])
        vec[V_FINAL_GAIN : V_FINAL_GAIN + 1, :] += column_sum(grad_final * normal)
        vec[V_FINAL_BIAS : V_FINAL_BIAS + 1, :] += column_sum(grad_final)
        go[...] = norm_backward(grad_final, normal, scale, fin_gain[...])

    def backward(m):
        @pl.when(jnp.logical_not(is_last))
        def _():
            backward_copy(m).wait_recv()
            go[...] = gin[m].astype(F32)

        gres = go[...].astype(BF16)
        gin[m] = gres
        parts = hidden_n // chunk

        def spread(c):
            return dot_nt(gres, whole(down_w[c]))

        total, ahead = None, spread(0)
        for c in range(parts):
            cols = slice(c * chunk, (c + 1) * chunk)
            gact = ahead
            if c + 1 < parts:
                ahead = spread(c + 1)
            ghid = (gact * slope[m, :, cols].astype(F32)).astype(BF16)
            slope[m, :, cols] = ghid
            term = dot_nt(ghid, whole(in_w[c]))
            total = term if total is None else total + term
        normal2, scale2 = normalise(middle[m])
        vec[V_GAIN2 : V_GAIN2 + 1, :] += column_sum(total * normal2)
        vec[V_SHIFT2 : V_SHIFT2 + 1, :] += column_sum(total)
        gmid[...] = go[...] + norm_backward(total, normal2, scale2, gains[1:2, :])
        gbr = gmid[...].astype(BF16)
        s_gbr[m] = gbr
        gmix = dot_nt(gbr, out_w[...]).astype(BF16)
        grads = []
        for r in range(GROUP):
            rows = slice(r * ROW, (r + 1) * ROW)
            for p in range(pairs):
                gm = stack_pair(gmix[rows, p * ROW : (p + 1) * ROW], lane_low)
                vlanes = slice(2 * width + p * ROW, 2 * width + (p + 1) * ROW)
                grads.append(dot_nt(proj[m, rows, vlanes], gm))
                unit = r * pairs + p
                proj[m, rows, vlanes] = dot(probs[m, unit // 2, unit % 2], gm).astype(BF16)

        def pull(unit, gsc):
            r, p = unit // pairs, unit % pairs
            rows = slice(r * ROW, (r + 1) * ROW)
            lanes = slice(p * ROW, (p + 1) * ROW)
            klanes = slice(width + p * ROW, width + (p + 1) * ROW)
            q = stack_pair(proj[m, rows, lanes], lane_low)
            gq = join_pair(dot_tn(gsc, proj[m, rows, klanes]), lane_low) * (ROW // 2) ** -0.5
            gk = dot(gsc, q)
            proj[m, rows, klanes] = gk.astype(BF16)
            proj[m, rows, lanes] = gq.astype(BF16)

        waiting = None
        for unit in range(GROUP * pairs):
            weights = probs[m, unit // 2, unit % 2].astype(F32)
            inner = jnp.sum(weights * grads[unit], axis=0, keepdims=True)
            gsc = (weights * (grads[unit] - inner)).astype(BF16)
            if waiting is not None:
                pull(unit - 1, waiting)
            waiting = gsc
        pull(GROUP * pairs - 1, waiting)
        gproj = proj[m]
        gnormed = dot_nt(gproj, qkv_w[...])
        normal, scale = normalise(instream[m].astype(F32))
        vec[V_GAIN1 : V_GAIN1 + 1, :] += column_sum(gnormed * normal)
        vec[V_SHIFT1 : V_SHIFT1 + 1, :] += column_sum(gnormed)
        gs[m] = (gmid[...] + norm_backward(gnormed, normal, scale, gains[0:1, :])).astype(BF16)

        @pl.when(jnp.logical_not(is_first))
        def _():
            backward_copy(m).start()

    def tick(t, carry):
        m_forward = t - stage
        m_backward = t - (2 * (stages - 1) - stage)

        @pl.when((m_forward >= 0) & (m_forward < micros))
        def _():
            forward(m_forward)

        @pl.when((m_backward >= 0) & (m_backward < micros))
        def _():
            @pl.when(is_last)
            def _():
                head(m_backward)

            backward(m_backward)

        return carry

    lax.fori_loop(0, micros + 2 * (stages - 1), tick, 0)

    embed_stage = stages - 2
    is_extra = (stage == embed_stage) | is_last
    dims = line_dims(devices)
    turned_left = qkv_w
    mats = {
        "mixed": mixed,
        "active": active,
        "gres": gin,
        "ghid": slope,
        "gbr": s_gbr,
        "gproj": proj,
    }

    def mat(name, lanes=slice(None)):
        value = mats[name][:, :, lanes]
        return value.reshape(micros * tokens, value.shape[2])

    where = [lax.rem(place // stride, size) for size, stride in dims]

    def identity(size):
        here = lax.broadcasted_iota(jnp.int32, (size, size), 0)
        there = lax.broadcasted_iota(jnp.int32, (size, size), 1)
        return jnp.where(here == there, 1.0, 0.0).astype(BF16)

    held = []

    def turn(name):
        if held[-1:] == [name]:
            return
        held.append(name)
        unit = identity(256)
        if name in ("normed", "normed2"):
            row = 0 if name == "normed" else 1
            source = instream if name == "normed" else middle
            for m in range(micros):
                normal, _ = normalise(source[m].astype(F32))
                again = (normal * gains[row : row + 1, :] + shifts[row : row + 1, :]).astype(BF16)
                for q in range(width // 256):
                    part = dot_nt(unit, again[:, q * 256 : (q + 1) * 256])
                    turned_left[q * 256 : (q + 1) * 256, m * tokens : (m + 1) * tokens] = part.astype(BF16)
            return
        for q in range(width // 256):
            part = dot_nt(unit, mat(name, slice(q * 256, (q + 1) * 256)))
            turned_left[q * 256 : (q + 1) * 256, :] = part.astype(BF16)

    bits = devices.bit_length() - 1
    vec_send, vec_recv = take(2)
    vec_sems = take(2)

    def vec_copy(k):
        peer = jnp.bitwise_xor(place, 1 << k)
        return pltpu.make_async_remote_copy(
            src_ref=vec_send.at[k],
            dst_ref=vec_recv.at[k],
            send_sem=vec_sems[0].at[k],
            recv_sem=vec_sems[1].at[k],
            device_id={"dp": peer},
            device_id_type=MESH,
        )

    def vec_step(k):
        def run():
            if k == 0:
                vec_send[0] = vec[...]
                ones = jnp.ones((16, micros * tokens), BF16)
                for name, start, row in (
                    ("gproj", 0, V_QUERY),
                    ("gproj", 2 * width, V_VALUE),
                    ("gbr", 0, V_BRANCH),
                    ("gres", 0, V_RESULT),
                ):
                    part = dot(ones, mat(name, slice(start, start + width)))
                    vec_send[0, row : row + 1, :] = part[0:1, :]
                for q in range(hidden_n // width):
                    part = dot(ones, mat("ghid", slice(q * width, (q + 1) * width)))
                    vec_send[0, V_HIDDEN + q : V_HIDDEN + q + 1, :] = part[0:1, :]
            else:
                vec_copy(k - 1).wait_recv()
                vec_send[k] = vec_send[k - 1] + vec_recv[k - 1]
            if k < bits:
                vec_copy(k).start()

        return run

    final_send, final_recv = take(2)
    final_sems = take(2)

    def final_copy(offset):
        peer = lax.rem(stages - 1 + offset, stages)
        return pltpu.make_async_remote_copy(
            src_ref=final_send,
            dst_ref=final_recv,
            send_sem=final_sems[0].at[offset],
            recv_sem=final_sems[1].at[0],
            device_id={"pipe": peer},
            device_id_type=MESH,
        )

    def vec_last():
        vec_step(bits)()
        vec_out[...] = vec_send[bits]

        @pl.when(stage == stages - 1)
        def _():
            final_send[...] = vec_send[bits, 8:16, :]
            for offset in range(1, stages):
                final_copy(offset).start()

    def vec_finish():
        @pl.when(stage != stages - 1)
        def _():
            final_copy(1).wait_recv()
            vec_out[V_FINAL_GAIN : V_FINAL_BIAS + 1, :] = final_recv[
                V_FINAL_GAIN - 8 : V_FINAL_BIAS - 7, :
            ]

    def vec_drain():
        for k in range(bits):
            vec_copy(k).wait_send()

        @pl.when(stage == stages - 1)
        def _():
            for offset in range(1, stages):
                final_copy(offset).wait_send()

    def ship():
        return pltpu.make_async_remote_copy(
            src_ref=s_xl.at[pl.ds(0, 2)],
            dst_ref=s_xl.at[pl.ds(0, 2)],
            send_sem=ship_sem.at[0],
            recv_sem=ship_sem.at[1],
            device_id={"pipe": embed_stage},
            device_id_type=MESH,
        )

    def ship_embed():
        rows, half = vocab // stages, width // 2

        @pl.when(is_first)
        def _():
            right = gs[...].reshape(micros * tokens, width)
            for p in range(stages):
                here = lax.broadcasted_iota(jnp.int32, (rows, ROW), 0).astype(F32) + p * rows
                hot = [
                    jnp.where(ids[0, r : r + 1, :] == here, 1.0, 0.0).astype(BF16) for r in range(rows_n)
                ]
                part = dot(jnp.concatenate(hot, axis=1), right).astype(BF16)
                for k in range(2):
                    s_xl[k, :, p * half : (p + 1) * half] = part[:, k * half : (k + 1) * half]
            ship().start()

    extra_sum, extra_send_sem, extra_recv_sem, last_sum, ship_sem = take(5)
    share = embed_out.shape[0]

    def extra_copy(source, offset, target):
        peer = lax.rem(source + offset, stages)
        return pltpu.make_async_remote_copy(
            src_ref=extra_sum.at[pl.ds(pl.multiple_of(peer * share, share), share)],
            dst_ref=target,
            send_sem=extra_send_sem.at[offset],
            recv_sem=extra_recv_sem.at[0 if source == embed_stage else 1],
            device_id={"pipe": peer},
            device_id_type=MESH,
        )

    def chunk_steps(kind, c, block, turned):
        order = list(range(len(dims)))
        if turned:
            order.reverse()
        if kind == "down":
            full = probs.at[c]
        elif kind == "extra":
            full = probs.at[4 + c]
        else:
            full = (down_w + in_w)[{"out": 0, "in": 1, "qkv": 5}[kind] + c]

        def compute():
            if kind == "down":
                if c % 2 == 1:
                    return
                turn("gres")
                half = width // 2
                lines = slice((c // 2) * half, (c // 2 + 1) * half)
                parts = dot(turned_left[lines, :], mat("active")).astype(BF16)
                depth = hidden_n // devices
                unit = identity(depth)
                for d in range(devices):
                    back = dot_nt(unit, parts[:, d * depth : (d + 1) * depth]).astype(BF16)
                    for k in range(2):
                        piece = back[:, k * ROW : (k + 1) * ROW]
                        piece = jnp.concatenate([piece[: depth // 2], piece[depth // 2 :]], axis=1)
                        probs[(c + k,) + split(d)] = piece
            elif kind == "extra":
                if c == 1:
                    return
                rows = vocab // stages
                share = rows // devices
                half = width // 2

                def fill(left, right):
                    for p in range(stages):
                        part = left(p, right).astype(BF16).reshape(devices, share, width)
                        for d in range(devices):
                            for k in range(2):
                                lines = slice(p * share, (p + 1) * share)
                                probs[(4 + k,) + split(d) + (lines,)] = part[
                                    d, :, k * half : (k + 1) * half
                                ]

                def flat(ref):
                    return ref[...].reshape(micros * tokens, ref.shape[2])

                @pl.when(stage == embed_stage)
                def _():
                    ship().wait_recv()
                    for d in range(devices):
                        for k in range(2):
                            for p in range(stages):
                                lines = slice(p * share, (p + 1) * share)
                                probs[(4 + k,) + split(d) + (lines,)] = s_xl[
                                    k, d * share : (d + 1) * share, p * half : (p + 1) * half
                                ]

                @pl.when(is_last)
                def _():
                    def soft_part(p, right):
                        left = s_xl[:, :, p * rows : (p + 1) * rows]
                        return dot_tn(left.reshape(micros * tokens, rows), right)

                    fill(soft_part, flat(outb))
            else:
                left, right = {
                    "in": ("normed2", "ghid"),
                    "out": ("mixed", "gbr"),
                    "qkv": ("normed", "gproj"),
                }[kind]
                turn(left)
                part = dot(turned_left[...], mat(right, slice(c * width, (c + 1) * width)))
                part = part.astype(BF16).reshape((devices,) + block)
                for d in range(devices):
                    full[split(d)] = part[d]

        def split(d):
            return tuple((d // stride) % size for size, stride in reversed(dims))

        steps = [[compute]]
        for at, phase in enumerate(order):
            size = dims[phase][0]
            buffers = take(3)
            done = order[:at]
            last = at == len(order) - 1
            steps[-1].append(functools.partial(line_step, phase, size, 1, full, buffers, done))
            for t in range(2, size):
                steps.append([functools.partial(line_step, phase, size, t, full, buffers, done)])
            drains.append((kind, functools.partial(line_drain, phase, size, full, buffers, done)))
            steps.append([functools.partial(line_final, kind, c, phase, size, full, buffers, done, last)])
        if kind == "extra":
            steps = [[gated([part]) for part in step] for step in steps]
        return steps

    def gated(step):
        def run():
            @pl.when(is_extra)
            def _():
                for part in step:
                    part()

        return run

    def block_of(full, phase, j, done):
        spot = [slice(None)] * len(dims)
        for other in done:
            spot[len(dims) - 1 - other] = where[other]
        spot[len(dims) - 1 - phase] = j
        return full.at[tuple(spot)]

    def line_copy(phase, size, t, side, full, buffers, done):
        recv, ssem, rsem = buffers
        i = where[phase]
        stride = dims[phase][1]
        if side == 0:
            j, peer = size - t + i, place + jnp.where(i < size - 1, stride, 0)
        else:
            j, peer = t - size + i, place - jnp.where(i > 0, stride, 0)
        return pltpu.make_async_remote_copy(
            src_ref=block_of(full, phase, jnp.clip(j, 0, size - 1), done),
            dst_ref=recv.at[0 if size == 2 else side, t - 1],
            send_sem=ssem.at[side, t - 1],
            recv_sem=rsem.at[side, t - 1],
            device_id={"dp": peer},
            device_id_type=MESH,
        )

    def sends(i, size, t, side):
        return (i <= t - 1) if side == 0 else (i >= size - t)

    def line_step(phase, size, t, full, buffers, done):
        i = where[phase]
        for side in range(2):
            at_end = (i == 0) if side == 0 else (i == size - 1)
            j = size - t + i if side == 0 else t - size + i
            j = jnp.clip(j, 0, size - 1)

            @pl.when(sends(i, size, t, side))
            def _():
                if t > 1:
                    @pl.when(jnp.logical_not(at_end))
                    def _():
                        line_copy(phase, size, t - 1, side, full, buffers, done).wait_recv()
                        own = block_of(full, phase, j, done)
                        got = buffers[0][0 if size == 2 else side, t - 2]
                        own[...] = (own[...].astype(F32) + got.astype(F32)).astype(BF16)

                line_copy(phase, size, t, side, full, buffers, done).start()

    def line_final(kind, c, phase, size, full, buffers, done, last):
        i = where[phase]
        own = block_of(full, phase, i, done)
        total = own
        if last:
            lanes = slice(c * width, (c + 1) * width)
            slots = {
                "qkv": lambda: qkv_out.at[:, lanes],
                "in": lambda: in_out.at[:, lanes],
                "out": lambda: out_out,
                "down": lambda: last_sum,
                "extra": lambda: extra_sum.at[:, c * (width // 2) : (c + 1) * (width // 2)],
            }
            total = slots[kind]()
        lower, upper = i > 0, i < size - 1

        def arrived(side):
            line_copy(phase, size, size - 1, side, full, buffers, done).wait_recv()
            return buffers[0][0 if size == 2 else side, size - 2].astype(F32)

        @pl.when(lower & upper)
        def _():
            total[...] = (own[...].astype(F32) + arrived(0) + arrived(1)).astype(total.dtype)

        @pl.when(lower & jnp.logical_not(upper))
        def _():
            total[...] = (own[...].astype(F32) + arrived(0)).astype(total.dtype)

        @pl.when(jnp.logical_not(lower))
        def _():
            total[...] = (own[...].astype(F32) + arrived(1)).astype(total.dtype)

        if last and kind == "down":
            deep = down_out.shape[0] // 2
            lanes = slice(c * ROW, (c + 1) * ROW)
            down_out[0:deep, lanes] = last_sum[:, 0:ROW]
            down_out[deep : 2 * deep, lanes] = last_sum[:, ROW : 2 * ROW]
        if last and kind == "extra" and c == 1:
            for source_stage, out in ((embed_stage, embed_out), (stages - 1, head_out)):
                @pl.when(stage == source_stage)
                def _():
                    for offset in range(1, stages):
                        extra_copy(source_stage, offset, extra_recv[0 if source_stage == embed_stage else 1]).start()
                    out[...] = extra_sum[source_stage * share : (source_stage + 1) * share, :]

    def line_drain(phase, size, full, buffers, done):
        i = where[phase]
        for side in range(2):
            for t in range(1, size):
                @pl.when(sends(i, size, t, side))
                def _():
                    line_copy(phase, size, t, side, full, buffers, done).wait_send()

    extra_recv = take(2)
    drains = []
    chains = [chunk_steps(*item) for item in plan]
    depth = len(chains[0])
    vec_chain = [vec_step(k) for k in range(bits)] + [vec_last]
    starts, first, extra_rounds = [], 0, iter((1, 3, 5, 7))
    for item in plan:
        if item[3]:
            starts.append(next(extra_rounds))
        else:
            starts.append(first)
            first += 1
    loaded_at = max(start for start, item in zip(starts, plan) if item[0] == "qkv" and item[1] == 0)
    for r in range(max(starts) + depth):
        for d in [0] + list(range(depth - 1, 0, -1)):
            for start, chain in zip(starts, chains):
                if r - start != d:
                    continue
                for part in chain[d]:
                    part()
            if r == d == 0:
                ship_embed()
        if 0 <= r - loaded_at < len(vec_chain):
            vec_chain[r - loaded_at]()
    vec_finish()
    for source_stage, out in ((embed_stage, embed_out), (stages - 1, head_out)):
        @pl.when(stage != source_stage)
        def _():
            got = extra_recv[0 if source_stage == embed_stage else 1]
            extra_copy(source_stage, 1, got).wait_recv()
            out[...] = got[...]

        @pl.when(stage == source_stage)
        def _():
            for offset in range(1, stages):
                extra_copy(source_stage, offset, extra_recv[0]).wait_send()

    vec_drain()
    for kind, drain in drains:
        if kind == "extra":
            gated([drain])()
        else:
            drain()

    @pl.when(is_first)
    def _():
        ship().wait_send()

    for m in range(micros):
        @pl.when(jnp.logical_not(is_last))
        def _():
            forward_copy(m).wait_send()

        @pl.when(jnp.logical_not(is_first))
        def _():
            backward_copy(m).wait_send()


def step_plan(width, hid, vocab, stages, devices):
    plan = []
    for kind, c, _, turned in chunk_plan(width, hid, vocab, stages, devices):
        wide = kind in ("down", "extra")
        plan.append((kind, c, (ROW, 2 * ROW) if wide else (width // devices, width), turned))
    extra = [item for item in plan if item[0] == "extra"]
    rest = [item for item in plan if item[0] != "extra"]
    return rest[:-3] + extra + rest[-3:]


def run_step(stages, devices, token_ids, segment_ids, target_ids, params):
    embed, qkv_w, qv_b, out_w, out_b, in_w, in_b, down_w, gains, shifts, fg, fb, head_w = params
    dims = line_dims(devices)
    width, hid, vocab = embed.shape[1], in_w.shape[1], head_w.shape[0]
    tokens = GROUP * ROW
    micros = token_ids.shape[0] // GROUP
    vmem = pl.BlockSpec(memory_space=pltpu.VMEM)
    hbm = pl.BlockSpec(memory_space=pl.ANY)
    sizes = tuple(size for size, _ in reversed(dims))
    slim = width // devices
    share = vocab // (stages * devices)
    plan = step_plan(width, hid, vocab, stages, devices)
    bits = devices.bit_length() - 1

    def scratch(lead, columns, kind=BF16):
        return pltpu.VMEM((lead, tokens, columns), kind)

    def sums(*shape):
        return pltpu.VMEM(shape, F32)

    dma = pltpu.SemaphoreType.DMA
    scratch_shapes = [
        pltpu.VMEM((vocab, width), BF16),
        pltpu.VMEM((width, 3 * width), BF16),
        pltpu.VMEM((width, width), BF16),
    ]
    scratch_shapes += [pltpu.VMEM(sizes + (slim, width), BF16)] * 8
    scratch_shapes += [
        scratch(micros, width),
        scratch(micros, width),
        scratch(micros, width),
        scratch(micros, width),
        scratch(micros, 3 * width),
        pltpu.VMEM((micros,) + sizes + (ROW, 2 * ROW), BF16),
        scratch(micros, width),
        scratch(micros, width, F32),
        scratch(micros, hid),
        scratch(micros, hid),
        sums(tokens, width),
        sums(tokens, width),
        scratch(micros, width),
        scratch(micros, vocab),
        sums(VEC_ROWS, width),
        sums(3, 16, ROW),
        sums(ROW, ROW),
        dma((micros,)),
        dma((micros,)),
        dma((micros,)),
        dma((micros,)),
        dma((11,)),
        sums(bits + 1, VEC_ROWS, width),
        sums(bits, VEC_ROWS, width),
        dma((bits,)),
        dma((bits,)),
        sums(8, width),
        sums(8, width),
        dma((stages,)),
        dma((1,)),
        sums(stages * share, width),
        dma((stages,)),
        dma((2,)),
        sums(ROW, 2 * ROW),
        dma((2,)),
        sums(share, width),
        sums(share, width),
    ]
    for _, _, block, turned in plan:
        remain = list(reversed(dims))
        for size, stride in dims[::-1] if turned else dims:
            remain.remove((size, stride))
            piece = tuple(other for other, _ in remain) + block
            scratch_shapes.append(pltpu.VMEM((1 if size == 2 else 2, size - 1) + piece, BF16))
            scratch_shapes += [dma((2, size - 1))] * 2

    def result(*shape):
        return jax.ShapeDtypeStruct(shape, F32)

    return pl.pallas_call(
        functools.partial(step_kernel, stages, micros, devices, plan),
        out_shape=[
            result(slim, 3 * width),
            result(slim, width),
            result(slim, hid),
            result(hid // devices, width),
            result(share, width),
            result(share, width),
            result(VEC_ROWS, width),
        ],
        in_specs=[vmem] * 10 + [hbm] * 6,
        out_specs=[vmem] * 7,
        scratch_shapes=scratch_shapes,
        compiler_params=pltpu.CompilerParams(
            collective_id=2, has_side_effects=True, vmem_limit_bytes=63 * 1024 * 1024
        ),
        name="step",
    )(
        token_ids,
        segment_ids,
        target_ids,
        qv_b,
        out_b,
        in_b,
        gains,
        shifts,
        fg,
        fb,
        embed,
        head_w,
        qkv_w,
        out_w,
        in_w.reshape(sizes + (slim, hid)),
        down_w.reshape((hid // width,) + sizes + (slim, width)),
    )


def finish_kernel(devices, embed_g, qkv_g, out_g, in_g, down_g, head_g, vec, *outs):
    place = lax.axis_index("dp")
    width = vec.shape[1]
    (embed_o, qkv_o, qv_o, out_o, outb_o, in_o, inb_o, down_o, gain_o, shift_o, fg_o, fb_o, head_o) = outs
    embed_o[...] = embed_g[...]
    head_o[...] = head_g[...]
    for source, target in ((qkv_g, qkv_o), (out_g, out_o), (in_g, in_o), (down_g, down_o)):
        target[0] = source[...]
    lanes = width // devices
    turned = pltpu.roll(vec[0:8, :], lax.rem(width - place * lanes, width), 1)
    for row, out in ((V_QUERY, qv_o), (V_BRANCH, outb_o), (V_GAIN1, gain_o), (V_SHIFT1, shift_o)):
        out[0] = turned[row : row + 2, 0:lanes]
    share = inb_o.shape[1]
    first = place * share
    row = vec[pl.ds(V_HIDDEN + first // width, 1), :]
    wide = jnp.broadcast_to(row, (8, width))
    inb_o[...] = pltpu.roll(wide, lax.rem(width - lax.rem(first, width), width), 1)[0:1, 0:share]
    fg_o[...] = vec[V_FINAL_GAIN : V_FINAL_GAIN + 1, :]
    fb_o[...] = vec[V_FINAL_BIAS : V_FINAL_BIAS + 1, :]


def run_finish(devices, embed_g, qkv_g, out_g, in_g, down_g, head_g, vec):
    vmem = pl.BlockSpec(memory_space=pltpu.VMEM)
    width = vec.shape[1]
    lanes = width // devices

    def shape(*sizes):
        return jax.ShapeDtypeStruct(sizes, F32)

    pair = shape(1, 2, lanes)
    return pl.pallas_call(
        functools.partial(finish_kernel, devices),
        out_shape=[
            shape(*embed_g.shape),
            shape(1, *qkv_g.shape),
            pair,
            shape(1, *out_g.shape),
            pair,
            shape(1, *in_g.shape),
            shape(1, in_g.shape[1] // devices),
            shape(1, *down_g.shape),
            pair,
            pair,
            shape(1, width),
            shape(1, width),
            shape(*head_g.shape),
        ],
        in_specs=[vmem] * 7,
        out_specs=[vmem] * 13,
        name="finish",
    )(embed_g, qkv_g, out_g, in_g, down_g, head_g, vec)


def on_device(
    token_ids,
    segment_ids,
    target_ids,
    embed_table,
    qkv_weight,
    qv_bias,
    out_weight,
    out_biases,
    ff_in,
    ff_in_bias,
    ff_out,
    norm_gains,
    norm_biases,
    final_gain,
    final_bias,
    head_weight,
):
    stages = lax.axis_size("pipe")
    devices = lax.axis_size("dp")
    params = (
        embed_table,
        qkv_weight[0],
        qv_bias[0],
        out_weight[0],
        out_biases[0],
        ff_in[0],
        ff_in_bias,
        ff_out[0],
        norm_gains[0],
        norm_biases[0],
        final_gain[None],
        final_bias[None],
        head_weight,
    )
    if devices == 8:
        grads = run_step(stages, devices, token_ids, segment_ids, target_ids, params)
    else:
        *saved, vec = run_pipeline(stages, token_ids, segment_ids, target_ids, params)
        grads = run_gradients(stages, devices, saved, vec, token_ids)
    qkv_g, out_g, in_g, down_g, embed_g, head_g, sums = grads
    done = list(run_finish(devices, embed_g, qkv_g, out_g, in_g, down_g, head_g, sums))
    done[10], done[11] = done[10][0], done[11][0]
    return tuple(done)


def solution(mesh):
    layer3 = P("pipe", None, None)
    return jax.shard_map(
        on_device,
        mesh=mesh,
        in_specs=(
            P("dp", None),
            P("dp", None),
            P("dp", None),
            P(),
            layer3,
            layer3,
            layer3,
            layer3,
            layer3,
            P("pipe", None),
            layer3,
            layer3,
            layer3,
            P(),
            P(),
            P(),
        ),
        out_specs=(
            P(("pipe", "dp"), None),
            P("pipe", "dp", None),
            P("pipe", None, "dp"),
            P("pipe", "dp", None),
            P("pipe", None, "dp"),
            P("pipe", "dp", None),
            P("pipe", "dp"),
            P("pipe", "dp", None),
            P("pipe", None, "dp"),
            P("pipe", None, "dp"),
            P(),
            P(),
            P(("pipe", "dp"), None),
        ),
        check_vma=False,
    )
```

```python
import functools

import jax
import jax.numpy as jnp
from jax import lax
from jax.experimental import pallas as pl
from jax.experimental.pallas import tpu as pltpu
from jax.sharding import PartitionSpec as P

HEADS = 8
FRAME = 6
ROW = 128
GROUP = 2
MASKED = -1e30
GELU_A = 0.7978845608
GELU_B = 0.044715
MESH = pl.DeviceIdType.MESH
F32 = jnp.float32
BF16 = jnp.bfloat16

VEC_ROWS = 16
V_QUERY, V_VALUE, V_BRANCH, V_RESULT, V_GAIN1, V_GAIN2, V_SHIFT1, V_SHIFT2 = range(8)
V_HIDDEN = 8
V_FINAL_GAIN, V_FINAL_BIAS = 12, 13


def dot(a, b):
    return lax.dot_general(a, b, (((1,), (0,)), ((), ())), preferred_element_type=F32)


def dot_nt(a, b):
    return lax.dot_general(a, b, (((1,), (1,)), ((), ())), preferred_element_type=F32)


def dot_tn(a, b):
    return lax.dot_general(a, b, (((0,), (0,)), ((), ())), preferred_element_type=F32)


def normalise(values):
    centre = jnp.mean(values, axis=-1, keepdims=True)
    centered = values - centre
    spread = jnp.mean(centered * centered, axis=-1, keepdims=True)
    scale = lax.rsqrt(spread + 1e-05)
    return centered * scale, scale


def norm_backward(grad, normal, scale, gain):
    grad_n = grad * gain
    mean_grad = jnp.mean(grad_n, axis=-1, keepdims=True)
    mean_proj = jnp.mean(grad_n * normal, axis=-1, keepdims=True)
    return scale * (grad_n - mean_grad - normal * mean_proj)


def column_sum(values):
    return jnp.sum(values, axis=0, keepdims=True)


def stack_pair(pair, low_lanes):
    zero = jnp.zeros_like(pair)
    return jnp.concatenate(
        [jnp.where(low_lanes, pair, zero), jnp.where(low_lanes, zero, pair)], axis=0
    )


def join_pair(stacked, low_lanes):
    half = stacked.shape[0] // 2
    return jnp.where(low_lanes, stacked[:half], stacked[half:])


def pipeline_kernel(
    stages,
    micros,
    token_ids,
    segment_ids,
    target_ids,
    embed,
    qkv_w,
    qv_b,
    out_w,
    out_b,
    in_w,
    in_b,
    down_w,
    gains,
    shifts,
    fin_gain,
    fin_bias,
    head_w,
    normed_o,
    mixed_o,
    normed2_o,
    active_o,
    gres_o,
    ghid_o,
    gbr_o,
    gproj_o,
    xl_o,
    xr_o,
    vec,
    instream,
    outb,
    gin,
    gs,
    normed,
    proj,
    probs,
    mixed,
    middle,
    normed2,
    active,
    slope,
    lo,
    go,
    gmid,
    s_gres,
    s_ghid,
    s_gbr,
    s_gproj,
    s_xl,
    ids,
    frames,
    fsend,
    frecv,
    bsend,
    brecv,
    osem,
):
    stage = lax.axis_index("pipe")
    tokens, width = instream.shape[1], instream.shape[2]
    hidden_n = in_b.shape[1]
    vocab = head_w.shape[0]
    pairs = width // ROW
    chunk = 512
    is_first = stage == 0
    is_last = stage == stages - 1
    up = jnp.minimum(stage + 1, stages - 1)
    down = jnp.maximum(stage - 1, 0)

    barrier = pltpu.get_barrier_semaphore()

    @pl.when(jnp.logical_not(is_first))
    def _():
        pl.semaphore_signal(barrier, inc=1, device_id={"pipe": down}, device_id_type=MESH)

    @pl.when(jnp.logical_not(is_last))
    def _():
        pl.semaphore_signal(barrier, inc=1, device_id={"pipe": up}, device_id_type=MESH)

    pl.semaphore_wait(barrier, jnp.where(is_first | is_last, 1, 2))
    vec[...] = jnp.zeros_like(vec)
    rows_n, seq = token_ids.shape
    for index, member in enumerate((token_ids, segment_ids, target_ids)):
        ids[index] = jnp.full(ids.shape[1:], 4.0 if index == 1 else -1.0, F32)
        ids[index, 0:rows_n, 0:seq] = member[...].astype(F32)
    at_query = lax.broadcasted_iota(jnp.int32, (ROW, ROW), 1)
    at_key = lax.broadcasted_iota(jnp.int32, (ROW, ROW), 0)
    frames[...] = jnp.where(at_key < ((at_query * 43) // 256) * FRAME + FRAME, 1.0, 0.0)

    def column(index, row):
        values = jnp.broadcast_to(ids[index, pl.ds(row, 1), :], (8, ROW))
        return values.T[:, 0:1]

    def hot_rows(index, m):
        parts = [column(index, m * GROUP + r) for r in range(GROUP)]
        values = jnp.concatenate(parts, axis=0)
        places = lax.broadcasted_iota(jnp.int32, (tokens, vocab), 1).astype(F32)
        return values, jnp.where(values == places, 1.0, 0.0)

    def forward_copy(m):
        return pltpu.make_async_remote_copy(
            src_ref=outb.at[m],
            dst_ref=instream.at[m],
            send_sem=fsend.at[m],
            recv_sem=frecv.at[m],
            device_id={"pipe": up},
            device_id_type=MESH,
        )

    def backward_copy(m):
        return pltpu.make_async_remote_copy(
            src_ref=gs.at[m],
            dst_ref=gin.at[m],
            send_sem=bsend.at[m],
            recv_sem=brecv.at[m],
            device_id={"pipe": down},
            device_id_type=MESH,
        )

    def save(index, src, dst, m):
        return pltpu.make_async_copy(src, dst.at[m], osem.at[index, m])

    def saves_forward(m):
        return [
            save(0, normed.at[m], normed_o, m),
            save(1, mixed.at[m], mixed_o, m),
            save(2, normed2.at[m], normed2_o, m),
            save(3, active.at[m], active_o, m),
        ]

    def saves_backward(m):
        slot = lax.rem(m, 2)
        return [
            save(4, s_gres.at[slot], gres_o, m),
            save(5, s_ghid.at[slot], ghid_o, m),
            save(6, s_gbr.at[slot], gbr_o, m),
            save(7, s_gproj.at[slot], gproj_o, m),
        ]

    def save_xl(m):
        return save(8, s_xl.at[lax.rem(m, 2)], xl_o, m)

    def put_xl(m, value):
        @pl.when(m >= 2)
        def _():
            save_xl(m - 2).wait()

        s_xl[lax.rem(m, 2)] = value
        save_xl(m).start()

    lane_low = lax.broadcasted_iota(jnp.int32, (ROW, ROW), 1) < ROW // 2

    def forward(m):
        @pl.when(is_first)
        def _():
            hot = hot_rows(0, m)[1].astype(BF16)
            instream[m] = dot(hot, embed[...]).astype(BF16)

        @pl.when(jnp.logical_not(is_first))
        def _():
            forward_copy(m).wait_recv()

        normal, _ = normalise(instream[m].astype(F32))
        normed[m] = (normal * gains[0:1, :] + shifts[0:1, :]).astype(BF16)
        low = normed[m]
        queries = dot(low, qkv_w[:, 0:width]) + qv_b[0:1, :]
        proj[m, :, 0:width] = (queries * (ROW // 2) ** -0.5).astype(BF16)
        proj[m, :, width : 2 * width] = dot(low, qkv_w[:, width : 2 * width]).astype(BF16)
        proj[m, :, 2 * width : 3 * width] = (
            dot(low, qkv_w[:, 2 * width : 3 * width]) + qv_b[1:2, :]
        ).astype(BF16)
        masks, scores = [], []
        for r in range(GROUP):
            rows = slice(r * ROW, (r + 1) * ROW)
            kinds = lax.broadcasted_iota(jnp.int32, (16, ROW), 0).astype(F32)
            member = jnp.where(ids[1, pl.ds(m * GROUP + r, 1), :] == kinds, 1.0, 0.0).astype(BF16)
            mask = jnp.where(dot_tn(member, member) * frames[...] > 0.5, 0.0, MASKED)
            masks.append(jnp.concatenate([mask, mask], axis=1))
            for p in range(pairs):
                q = stack_pair(proj[m, rows, p * ROW : (p + 1) * ROW], lane_low)
                k = proj[m, rows, width + p * ROW : width + (p + 1) * ROW]
                scores.append(dot_nt(k, q))

        def mix(unit):
            r, p = unit // pairs, unit % pairs
            rows = slice(r * ROW, (r + 1) * ROW)
            v = proj[m, rows, 2 * width + p * ROW : 2 * width + (p + 1) * ROW]
            both = dot_tn(probs[m, unit], v)
            mixed[m, rows, p * ROW : (p + 1) * ROW] = join_pair(both, lane_low).astype(BF16)

        for unit in range(GROUP * pairs):
            masked = scores[unit] + masks[unit // pairs]
            expo = jnp.exp(masked - jnp.max(masked, axis=0, keepdims=True))
            total = jnp.sum(expo, axis=0, keepdims=True)
            probs[m, unit] = (expo * (1.0 / total)).astype(BF16)
            if unit:
                mix(unit - 1)
        mix(GROUP * pairs - 1)
        mid = instream[m].astype(F32) + (dot(mixed[m], out_w[...]) + out_b[0:1, :])
        middle[m] = mid
        normal2, _ = normalise(mid)
        normed2[m] = (normal2 * gains[1:2, :] + shifts[1:2, :]).astype(BF16)
        low2 = normed2[m]
        parts = hidden_n // chunk

        def spread(c):
            return dot(low2, in_w[:, c * chunk : (c + 1) * chunk])

        total, ahead = None, spread(0)
        for c in range(parts):
            cols = slice(c * chunk, (c + 1) * chunk)
            hid = ahead + in_b[0:1, cols]
            if c + 1 < parts:
                ahead = spread(c + 1)
            square = hid * hid
            tan = jnp.tanh(hid * (GELU_A + (GELU_A * GELU_B) * square))
            half = 0.5 + 0.5 * tan
            act = (hid * half).astype(BF16)
            active[m, :, cols] = act
            rise = (1.0 - tan * tan) * (0.5 * GELU_A + (1.5 * GELU_A * GELU_B) * square)
            slope[m, :, cols] = (half + hid * rise).astype(BF16)
            term = dot(act, down_w[cols, :])
            total = term if total is None else total + term
        for copy in saves_forward(m):
            copy.start()
        lo[...] = middle[m] + (total + out_b[1:2, :])

        @pl.when(jnp.logical_not(is_last))
        def _():
            outb[m] = lo[...].astype(BF16)
            forward_copy(m).start()

    def head(m):
        normal, scale = normalise(lo[...])
        outb[m] = (normal * fin_gain[...] + fin_bias[...]).astype(BF16)
        save(9, outb.at[m], xr_o, m).start()
        logits = dot_nt(outb[m], head_w[...])
        top = jnp.max(logits, axis=-1, keepdims=True)
        expo = jnp.exp(logits - top)
        total = jnp.sum(expo, axis=-1, keepdims=True)
        target, hot = hot_rows(2, m)
        grad_logits = jnp.where(target >= 0.0, expo * (1.0 / total) - hot, 0.0).astype(BF16)
        put_xl(m, grad_logits)
        grad_final = dot(grad_logits, head_w[...])
        vec[V_FINAL_GAIN : V_FINAL_GAIN + 1, :] += column_sum(grad_final * normal)
        vec[V_FINAL_BIAS : V_FINAL_BIAS + 1, :] += column_sum(grad_final)
        go[...] = norm_backward(grad_final, normal, scale, fin_gain[...])

    def backward(m):
        slot = lax.rem(m, 2)

        @pl.when(m >= 2)
        def _():
            for copy in saves_backward(m - 2):
                copy.wait()

        @pl.when(jnp.logical_not(is_last))
        def _():
            backward_copy(m).wait_recv()
            go[...] = gin[m].astype(F32)

        s_gres[slot] = go[...].astype(BF16)
        gres = s_gres[slot]
        parts = hidden_n // chunk

        def spread(c):
            return dot_nt(gres, down_w[c * chunk : (c + 1) * chunk, :])

        total, ahead = None, spread(0)
        for c in range(parts):
            cols = slice(c * chunk, (c + 1) * chunk)
            gact = ahead
            if c + 1 < parts:
                ahead = spread(c + 1)
            ghid = (gact * slope[m, :, cols].astype(F32)).astype(BF16)
            s_ghid[slot, :, cols] = ghid
            term = dot_nt(ghid, in_w[:, cols])
            total = term if total is None else total + term
        normal2, scale2 = normalise(middle[m])
        vec[V_GAIN2 : V_GAIN2 + 1, :] += column_sum(total * normal2)
        vec[V_SHIFT2 : V_SHIFT2 + 1, :] += column_sum(total)
        gmid[...] = go[...] + norm_backward(total, normal2, scale2, gains[1:2, :])
        s_gbr[slot] = gmid[...].astype(BF16)
        gbr = s_gbr[slot]
        gmix = dot_nt(gbr, out_w[...]).astype(BF16)
        grads = []
        for r in range(GROUP):
            rows = slice(r * ROW, (r + 1) * ROW)
            for p in range(pairs):
                gm = stack_pair(gmix[rows, p * ROW : (p + 1) * ROW], lane_low)
                vlanes = slice(2 * width + p * ROW, 2 * width + (p + 1) * ROW)
                grads.append(dot_nt(proj[m, rows, vlanes], gm))
                s_gproj[slot, rows, vlanes] = dot(probs[m, r * pairs + p], gm).astype(BF16)

        def pull(unit, gsc):
            r, p = unit // pairs, unit % pairs
            rows = slice(r * ROW, (r + 1) * ROW)
            lanes = slice(p * ROW, (p + 1) * ROW)
            klanes = slice(width + p * ROW, width + (p + 1) * ROW)
            q = stack_pair(proj[m, rows, lanes], lane_low)
            s_gproj[slot, rows, klanes] = dot(gsc, q).astype(BF16)
            gq = join_pair(dot_tn(gsc, proj[m, rows, klanes]), lane_low) * (ROW // 2) ** -0.5
            s_gproj[slot, rows, lanes] = gq.astype(BF16)

        waiting = None
        for unit in range(GROUP * pairs):
            weights = probs[m, unit].astype(F32)
            inner = jnp.sum(weights * grads[unit], axis=0, keepdims=True)
            gsc = (weights * (grads[unit] - inner)).astype(BF16)
            if waiting is not None:
                pull(unit - 1, waiting)
            waiting = gsc
        pull(GROUP * pairs - 1, waiting)
        for copy in saves_backward(m):
            copy.start()
        gproj = s_gproj[slot]
        gnormed = dot_nt(gproj, qkv_w[...])
        normal, scale = normalise(instream[m].astype(F32))
        vec[V_GAIN1 : V_GAIN1 + 1, :] += column_sum(gnormed * normal)
        vec[V_SHIFT1 : V_SHIFT1 + 1, :] += column_sum(gnormed)
        gs[m] = (gmid[...] + norm_backward(gnormed, normal, scale, gains[0:1, :])).astype(BF16)

        @pl.when(is_first)
        def _():
            save(9, gs.at[m], xr_o, m).start()

        @pl.when(jnp.logical_not(is_first))
        def _():
            backward_copy(m).start()

    def tick(t, carry):
        m_forward = t - stage
        m_backward = t - (2 * (stages - 1) - stage)

        @pl.when((m_forward >= 0) & (m_forward < micros))
        def _():
            forward(m_forward)

        @pl.when((m_backward >= 0) & (m_backward < micros))
        def _():
            @pl.when(is_last)
            def _():
                head(m_backward)

            backward(m_backward)

        return carry

    lax.fori_loop(0, micros + 2 * (stages - 1), tick, 0)

    for m in range(micros):
        for copy in saves_forward(m):
            copy.wait()

        @pl.when(jnp.logical_not(is_last))
        def _():
            forward_copy(m).wait_send()

        @pl.when(jnp.logical_not(is_first))
        def _():
            backward_copy(m).wait_send()

        @pl.when(is_first)
        def _():
            save(9, gs.at[m], xr_o, m).wait()

        @pl.when(is_last)
        def _():
            save(9, outb.at[m], xr_o, m).wait()

    for m in range(max(0, micros - 2), micros):
        for copy in saves_backward(m):
            copy.wait()

        @pl.when(is_last)
        def _():
            save_xl(m).wait()


def run_pipeline(stages, token_ids, segment_ids, target_ids, params):
    embed, in_w, head_w = params[0], params[5], params[12]
    width = embed.shape[1]
    vocab = head_w.shape[0]
    hid = in_w.shape[1]
    tokens = GROUP * ROW
    micros = token_ids.shape[0] // GROUP
    pairs = width // ROW
    vmem = pl.BlockSpec(memory_space=pltpu.VMEM)
    hbm = pl.BlockSpec(memory_space=pl.ANY)

    def kept(columns):
        return jax.ShapeDtypeStruct((micros, tokens, columns), BF16)

    def scratch(lead, columns, kind=BF16):
        return pltpu.VMEM((lead, tokens, columns), kind)

    out_shape = [
        kept(width),
        kept(width),
        kept(width),
        kept(hid),
        kept(width),
        kept(hid),
        kept(width),
        kept(3 * width),
        kept(vocab),
        kept(width),
        jax.ShapeDtypeStruct((VEC_ROWS, width), F32),
    ]
    return pl.pallas_call(
        functools.partial(pipeline_kernel, stages, micros),
        out_shape=out_shape,
        in_specs=[vmem] * 16,
        out_specs=[hbm] * 10 + [vmem],
        scratch_shapes=[
            scratch(micros, width),
            scratch(micros, width),
            scratch(micros, width),
            scratch(micros, width),
            scratch(micros, width),
            scratch(micros, 3 * width),
            pltpu.VMEM((micros, GROUP * pairs, ROW, 2 * ROW), BF16),
            scratch(micros, width),
            scratch(micros, width, F32),
            scratch(micros, width),
            scratch(micros, hid),
            scratch(micros, hid),
            pltpu.VMEM((tokens, width), F32),
            pltpu.VMEM((tokens, width), F32),
            pltpu.VMEM((tokens, width), F32),
            scratch(2, width),
            scratch(2, hid),
            scratch(2, width),
            scratch(2, 3 * width),
            scratch(2, vocab),
            pltpu.VMEM((3, 16, ROW), F32),
            pltpu.VMEM((ROW, ROW), F32),
            pltpu.SemaphoreType.DMA((micros,)),
            pltpu.SemaphoreType.DMA((micros,)),
            pltpu.SemaphoreType.DMA((micros,)),
            pltpu.SemaphoreType.DMA((micros,)),
            pltpu.SemaphoreType.DMA((10, micros)),
        ],
        compiler_params=pltpu.CompilerParams(
            collective_id=0, has_side_effects=True, vmem_limit_bytes=62 * 1024 * 1024
        ),
        name="pipeline",
    )(token_ids, segment_ids, target_ids, *params)


def line_dims(devices):
    dims, stride = [], 1
    if devices == 8:
        return [(2, 1), (4, 2)]
    while devices > 1:
        size = 4 if devices % 4 == 0 else 2
        dims.append((size, stride))
        stride *= size
        devices //= size
    return dims


def chunk_plan(width, hid, vocab, stages, devices):
    slim, deep = width // devices, hid // devices
    plan = [("out", 0, (slim, width), False)]
    for c in range(4):
        plan.append(("down", c, (deep, width // 4), c in (1, 3)))
    for c in range(2):
        plan.append(("extra", c, (stages, vocab // (stages * devices), width // 2), False))
    for c in range(hid // width):
        plan.append(("in", c, (slim, width), c == 1))
    for c in range(3):
        plan.append(("qkv", c, (slim, width), False))
    return plan


def gradient_kernel(stages, devices, plan, *refs):
    dims = line_dims(devices)
    refs = list(refs)

    def take(amount):
        head, refs[:] = refs[:amount], refs[amount:]
        return head

    inputs = take(10)
    vec_in, token_ids = take(2)
    qkv_out, out_out, in_out, down_out, embed_out, head_out, vec_out = take(7)
    local = take(10)
    in_sem = take(1)[0]
    turned_left, turned_xl = take(2)
    mats = dict(
        zip(
            ("normed", "mixed", "normed2", "active", "gres", "ghid", "gbr", "gproj", "xl", "xr"),
            local,
        )
    )
    names = list(mats)
    stage = lax.axis_index("pipe")
    place = lax.axis_index("dp")
    is_extra = (stage == 0) | (stage == stages - 1)
    width = mats["normed"].shape[1]
    where = [lax.rem(place // stride, size) for size, stride in dims]

    barrier = pltpu.get_barrier_semaphore()

    def greet(offset, carry):
        peer = lax.rem(place + offset, devices)
        pl.semaphore_signal(barrier, inc=1, device_id={"dp": peer}, device_id_type=MESH)
        return carry

    def greet_stage(offset, carry):
        peer = lax.rem(stage + offset, stages)
        pl.semaphore_signal(barrier, inc=1, device_id={"pipe": peer}, device_id_type=MESH)
        return carry

    lax.fori_loop(1, devices, greet, 0)
    lax.fori_loop(1, stages, greet_stage, 0)

    def load(name):
        i = names.index(name)
        return pltpu.make_async_copy(inputs[i], mats[name], in_sem.at[i])

    groups = [("mixed", "gbr"), ("gres", "active"), ("xr", "xl"), ("normed2", "ghid"), ("normed", "gproj")]

    def fetch(at):
        if at >= len(groups):
            return
        if groups[at] == ("xr", "xl"):
            @pl.when(is_extra)
            def _():
                load("xr").start()

            @pl.when(stage == stages - 1)
            def _():
                load("xl").start()

            at += 1
        for name in groups[at]:
            load(name).start()

    fetch(0)
    loaded = set()

    def need(*wanted):
        fresh = [name for name in wanted if name not in loaded]
        for name in fresh:
            loaded.add(name)
            load(name).wait()
        if fresh:
            at = [i for i, group in enumerate(groups) if group[0] == fresh[0]][0]
            fetch(at + 1)

    def identity(size):
        here = lax.broadcasted_iota(jnp.int32, (size, size), 0)
        there = lax.broadcasted_iota(jnp.int32, (size, size), 1)
        return jnp.where(here == there, 1.0, 0.0).astype(BF16)

    held = []

    def turn(name):
        if held[-1:] == [name]:
            return
        held.append(name)
        unit = identity(256)
        for q in range(width // 256):
            part = dot_nt(unit, mats[name][:, q * 256 : (q + 1) * 256])
            turned_left[q * 256 : (q + 1) * 256, :] = part.astype(BF16)

    bits = devices.bit_length() - 1
    vec_send, vec_recv = take(2)
    vec_sems = take(2)

    def vec_copy(k):
        peer = jnp.bitwise_xor(place, 1 << k)
        return pltpu.make_async_remote_copy(
            src_ref=vec_send.at[k],
            dst_ref=vec_recv.at[k],
            send_sem=vec_sems[0].at[k],
            recv_sem=vec_sems[1].at[k],
            device_id={"dp": peer},
            device_id_type=MESH,
        )

    def vec_step(k):
        def run():
            if k == 0:
                vec_send[0] = vec_in[...]
                ones = jnp.ones((16, mats["gres"].shape[0]), BF16)
                for name, start, row in (
                    ("gproj", 0, V_QUERY),
                    ("gproj", 2 * width, V_VALUE),
                    ("gbr", 0, V_BRANCH),
                    ("gres", 0, V_RESULT),
                ):
                    part = dot(ones, mats[name][:, start : start + width])
                    vec_send[0, row : row + 1, :] = part[0:1, :]
                for q in range(mats["ghid"].shape[1] // width):
                    part = dot(ones, mats["ghid"][:, q * width : (q + 1) * width])
                    vec_send[0, V_HIDDEN + q : V_HIDDEN + q + 1, :] = part[0:1, :]
            else:
                vec_copy(k - 1).wait_recv()
                vec_send[k] = vec_send[k - 1] + vec_recv[k - 1]
            if k < bits:
                vec_copy(k).start()

        return run

    final_send, final_recv = take(2)
    final_sems = take(2)

    def final_copy(offset):
        peer = lax.rem(stages - 1 + offset, stages)
        return pltpu.make_async_remote_copy(
            src_ref=final_send,
            dst_ref=final_recv,
            send_sem=final_sems[0].at[offset],
            recv_sem=final_sems[1].at[0],
            device_id={"pipe": peer},
            device_id_type=MESH,
        )

    def vec_last():
        vec_step(bits)()
        vec_out[...] = vec_send[bits]

        @pl.when(stage == stages - 1)
        def _():
            final_send[...] = vec_send[bits, 8:16, :]
            for offset in range(1, stages):
                final_copy(offset).start()

    def vec_finish():
        @pl.when(stage != stages - 1)
        def _():
            final_copy(1).wait_recv()
            vec_out[V_FINAL_GAIN : V_FINAL_BIAS + 1, :] = final_recv[
                V_FINAL_GAIN - 8 : V_FINAL_BIAS - 7, :
            ]

    def vec_drain():
        for k in range(bits):
            vec_copy(k).wait_send()

        @pl.when(stage == stages - 1)
        def _():
            for offset in range(1, stages):
                final_copy(offset).wait_send()

    extra_sum, extra_send_sem, extra_recv_sem = take(3)

    def extra_copy(source, offset, target):
        peer = lax.rem(source + offset, stages)
        return pltpu.make_async_remote_copy(
            src_ref=extra_sum.at[peer],
            dst_ref=target,
            send_sem=extra_send_sem.at[offset],
            recv_sem=extra_recv_sem.at[0 if source == 0 else 1],
            device_id={"pipe": peer},
            device_id_type=MESH,
        )

    down_full = {}

    def chunk_steps(kind, c, block, turned):
        order = list(range(len(dims)))
        if turned:
            order.reverse()
        full = take(1)[0]

        def compute():
            if kind == "down":
                need("gres", "active")
                turn("gres")
                if c % 2 == 1:
                    return
                half = width // 2
                lines = slice((c // 2) * half, (c // 2 + 1) * half)
                parts = dot(turned_left[lines, :], mats["active"][...]).astype(BF16)
                depth = block[0]
                unit = identity(depth)
                for d in range(devices):
                    back = dot_nt(unit, parts[:, d * depth : (d + 1) * depth]).astype(BF16)
                    down_full[c][split(d)] = back[:, 0 : half // 2]
                    down_full[c + 1][split(d)] = back[:, half // 2 : half]
            elif kind == "extra":
                vocab = turned_xl.shape[0]
                if c == 0:
                    load("xr").wait()

                @pl.when((stage == 0) & (c == 0))
                def _():
                    rows_n, seq = token_ids.shape
                    places = lax.broadcasted_iota(jnp.int32, (vocab, ROW), 0)
                    gap = jnp.full((1, ROW - seq), -1, jnp.int32)
                    for r in range(rows_n):
                        row = jnp.concatenate([token_ids[r : r + 1, :], gap], axis=1)
                        hot = jnp.where(places == row, 1.0, 0.0)
                        turned_xl[:, r * ROW : (r + 1) * ROW] = hot.astype(BF16)

                @pl.when((stage == stages - 1) & (c == 0))
                def _():
                    load("xl").wait()
                    unit = identity(256)
                    for q in range(vocab // 256):
                        part = dot_nt(unit, mats["xl"][:, q * 256 : (q + 1) * 256])
                        turned_xl[q * 256 : (q + 1) * 256, :] = part.astype(BF16)

                rows = vocab // stages
                for p in range(stages):
                    part = dot(
                        turned_xl[p * rows : (p + 1) * rows, :],
                        mats["xr"][:, c * (width // 2) : (c + 1) * (width // 2)],
                    )
                    part = part.astype(BF16).reshape((devices,) + block[1:])
                    for d in range(devices):
                        full[split(d) + (p,)] = part[d]
            else:
                left, right = {
                    "in": ("normed2", "ghid"),
                    "out": ("mixed", "gbr"),
                    "qkv": ("normed", "gproj"),
                }[kind]
                need(left, right)
                turn(left)
                cols = slice(c * width, (c + 1) * width)
                part = dot(turned_left[...], mats[right][:, cols]).astype(BF16)
                part = part.reshape((devices,) + block)
                for d in range(devices):
                    full[split(d)] = part[d]

        def split(d):
            return tuple((d // stride) % size for size, stride in reversed(dims))

        if kind == "down":
            down_full[c] = full
        steps = [[compute]]
        for at, phase in enumerate(order):
            size = dims[phase][0]
            buffers = take(3)
            done = order[:at]
            last = at == len(order) - 1
            steps[-1].append(functools.partial(line_step, phase, size, 1, full, buffers, done))
            for t in range(2, size):
                steps.append([functools.partial(line_step, phase, size, t, full, buffers, done)])
            drains.append((kind, functools.partial(line_drain, phase, size, full, buffers, done)))
            steps.append([functools.partial(line_final, kind, c, phase, size, full, buffers, done, last)])
        if kind == "extra":
            steps = [[gated([part]) for part in step] for step in steps]
        return steps

    def gated(step):
        def run():
            @pl.when(is_extra)
            def _():
                for part in step:
                    part()

        return run

    def block_of(full, phase, j, done):
        spot = [slice(None)] * len(dims)
        for other in done:
            spot[len(dims) - 1 - other] = where[other]
        spot[len(dims) - 1 - phase] = j
        return full.at[tuple(spot)]

    def line_copy(phase, size, t, side, full, buffers, done):
        recv, ssem, rsem = buffers
        i = where[phase]
        stride = dims[phase][1]
        if side == 0:
            j, peer = size - t + i, place + jnp.where(i < size - 1, stride, 0)
        else:
            j, peer = t - size + i, place - jnp.where(i > 0, stride, 0)
        return pltpu.make_async_remote_copy(
            src_ref=block_of(full, phase, jnp.clip(j, 0, size - 1), done),
            dst_ref=recv.at[0 if size == 2 else side, t - 1],
            send_sem=ssem.at[side, t - 1],
            recv_sem=rsem.at[side, t - 1],
            device_id={"dp": peer},
            device_id_type=MESH,
        )

    def sends(i, size, t, side):
        return (i <= t - 1) if side == 0 else (i >= size - t)

    def line_step(phase, size, t, full, buffers, done):
        i = where[phase]
        for side in range(2):
            at_end = (i == 0) if side == 0 else (i == size - 1)
            j = size - t + i if side == 0 else t - size + i
            j = jnp.clip(j, 0, size - 1)

            @pl.when(sends(i, size, t, side))
            def _():
                if t > 1:
                    @pl.when(jnp.logical_not(at_end))
                    def _():
                        line_copy(phase, size, t - 1, side, full, buffers, done).wait_recv()
                        own = block_of(full, phase, j, done)
                        got = buffers[0][0 if size == 2 else side, t - 2]
                        own[...] = (own[...].astype(F32) + got.astype(F32)).astype(BF16)

                line_copy(phase, size, t, side, full, buffers, done).start()

    def line_final(kind, c, phase, size, full, buffers, done, last):
        i = where[phase]
        own = block_of(full, phase, i, done)
        total = own
        if last:
            slots = {
                "qkv": lambda: qkv_out.at[:, c * width : (c + 1) * width],
                "in": lambda: in_out.at[:, c * width : (c + 1) * width],
                "out": lambda: out_out,
                "down": lambda: down_out.at[:, c * (width // 4) : (c + 1) * (width // 4)],
                "extra": lambda: extra_sum.at[:, :, c * (width // 2) : (c + 1) * (width // 2)],
            }
            total = slots[kind]()
        lower, upper = i > 0, i < size - 1

        def arrived(side):
            line_copy(phase, size, size - 1, side, full, buffers, done).wait_recv()
            return buffers[0][0 if size == 2 else side, size - 2].astype(F32)

        @pl.when(lower & upper)
        def _():
            total[...] = (own[...].astype(F32) + arrived(0) + arrived(1)).astype(total.dtype)

        @pl.when(lower & jnp.logical_not(upper))
        def _():
            total[...] = (own[...].astype(F32) + arrived(0)).astype(total.dtype)

        @pl.when(jnp.logical_not(lower))
        def _():
            total[...] = (own[...].astype(F32) + arrived(1)).astype(total.dtype)

        if last and kind == "extra" and c == 1:
            for source_stage, out in ((0, embed_out), (stages - 1, head_out)):
                @pl.when(stage == source_stage)
                def _():
                    for offset in range(1, stages):
                        extra_copy(source_stage, offset, extra_recv[0 if source_stage == 0 else 1]).start()
                    out[...] = extra_sum[source_stage]

    def line_drain(phase, size, full, buffers, done):
        i = where[phase]
        for side in range(2):
            for t in range(1, size):
                @pl.when(sends(i, size, t, side))
                def _():
                    line_copy(phase, size, t, side, full, buffers, done).wait_send()

    extra_recv = take(2)
    drains = []
    chains = [chunk_steps(*item) for item in plan]
    depth = len(chains[0])
    vec_chain = [vec_step(k) for k in range(bits)] + [vec_last]
    starts, first, extra_rounds = [], 0, iter((1, 3, 6, 8))
    for item in plan:
        if item[3]:
            starts.append(next(extra_rounds))
        else:
            starts.append(first)
            first += 1
    begun = False
    loaded_at = max(start for start, item in zip(starts, plan) if item[0] == "qkv" and item[1] == 0)
    for r in range(max(starts) + depth):
        for d in [0] + list(range(depth - 1, 0, -1)):
            for start, chain in zip(starts, chains):
                if r - start != d:
                    continue
                for part in chain[d]:
                    part()
                    if not begun:
                        begun = True
                        pl.semaphore_wait(barrier, devices - 1 + stages - 1)
        if 0 <= r - loaded_at < len(vec_chain):
            vec_chain[r - loaded_at]()
    vec_finish()
    for source_stage, out in ((0, embed_out), (stages - 1, head_out)):
        @pl.when(stage != source_stage)
        def _():
            got = extra_recv[0 if source_stage == 0 else 1]
            extra_copy(source_stage, 1, got).wait_recv()
            out[...] = got[...]

        @pl.when(stage == source_stage)
        def _():
            for offset in range(1, stages):
                extra_copy(source_stage, offset, extra_recv[0]).wait_send()

    vec_drain()
    for kind, drain in drains:
        if kind == "extra":
            gated([drain])()
        else:
            drain()


def run_gradients(stages, devices, saved, vec, token_ids):
    dims = line_dims(devices)
    rows, tokens, width = saved[0].shape
    hid, vocab = saved[3].shape[2], saved[8].shape[2]
    plan = chunk_plan(width, hid, vocab, stages, devices)
    saved = [member.reshape(rows * tokens, member.shape[2]) for member in saved]
    vmem = pl.BlockSpec(memory_space=pltpu.VMEM)
    hbm = pl.BlockSpec(memory_space=pl.ANY)
    bits = devices.bit_length() - 1
    share = vocab // (stages * devices)
    scratch = [pltpu.VMEM(member.shape, BF16) for member in saved]
    scratch += [pltpu.SemaphoreType.DMA((len(saved),))]
    scratch += [pltpu.VMEM((width, rows * tokens), BF16), pltpu.VMEM((vocab, rows * tokens), BF16)]
    scratch += [
        pltpu.VMEM((bits + 1,) + vec.shape, F32),
        pltpu.VMEM((bits,) + vec.shape, F32),
        pltpu.SemaphoreType.DMA((bits,)),
        pltpu.SemaphoreType.DMA((bits,)),
        pltpu.VMEM((8, width), F32),
        pltpu.VMEM((8, width), F32),
        pltpu.SemaphoreType.DMA((stages,)),
        pltpu.SemaphoreType.DMA((1,)),
        pltpu.VMEM((stages, share, width), F32),
        pltpu.SemaphoreType.DMA((stages,)),
        pltpu.SemaphoreType.DMA((2,)),
        pltpu.VMEM((share, width), F32),
        pltpu.VMEM((share, width), F32),
    ]
    sizes = [size for size, _ in reversed(dims)]
    for _, _, block, turned in plan:
        scratch.append(pltpu.VMEM(tuple(sizes) + block, BF16))
        remain = list(reversed(dims))
        for size, stride in dims[::-1] if turned else dims:
            remain.remove((size, stride))
            piece = tuple(other for other, _ in remain) + block
            scratch.append(pltpu.VMEM((1 if size == 2 else 2, size - 1) + piece, BF16))
            scratch += [pltpu.SemaphoreType.DMA((2, size - 1))] * 2
    return pl.pallas_call(
        functools.partial(gradient_kernel, stages, devices, plan),
        out_shape=[
            jax.ShapeDtypeStruct((width // devices, 3 * width), F32),
            jax.ShapeDtypeStruct((width // devices, width), F32),
            jax.ShapeDtypeStruct((width // devices, hid), F32),
            jax.ShapeDtypeStruct((hid // devices, width), F32),
            jax.ShapeDtypeStruct((share, width), F32),
            jax.ShapeDtypeStruct((share, width), F32),
            jax.ShapeDtypeStruct(vec.shape, F32),
        ],
        in_specs=[hbm] * len(saved) + [vmem] * 2,
        out_specs=[vmem] * 7,
        scratch_shapes=scratch,
        compiler_params=pltpu.CompilerParams(
            collective_id=1, has_side_effects=True, vmem_limit_bytes=62 * 1024 * 1024
        ),
        name="gradients",
    )(*saved, vec, token_ids)


def step_kernel(stages, micros, devices, plan, *refs):
    refs = list(refs)

    def take(amount):
        head, refs[:] = refs[:amount], refs[amount:]
        return head

    token_ids, segment_ids, target_ids = take(3)
    qv_b, out_b, in_b, gains, shifts, fin_gain, fin_bias = take(7)
    embed_h, head_h, qkv_h, out_h, in_h, down_h = take(6)
    qkv_out, out_out, in_out, down_out, embed_out, head_out, vec_out = take(7)
    side, qkv_w, out_w = take(3)
    in_w, down_w = take(4), take(4)
    instream, outb, gin, gs, proj, probs, mixed, middle, active, slope = take(10)
    lo, gmid, s_gbr, s_xl, vec, ids, frames = take(7)
    fsend, frecv, bsend, brecv, wsem = take(5)
    go = lo
    place = lax.axis_index("dp")
    stage = lax.axis_index("pipe")
    tokens, width = instream.shape[1], instream.shape[2]
    hidden_n = in_b.shape[1]
    vocab = side.shape[0]
    pairs = width // ROW
    chunk = 512
    is_first = stage == 0
    is_last = stage == stages - 1
    up = jnp.minimum(stage + 1, stages - 1)
    down = jnp.maximum(stage - 1, 0)

    def bring(index, source, target):
        return pltpu.make_async_copy(source, target, wsem.at[index])

    weights = [bring(1, qkv_h, qkv_w), bring(2, out_h, out_w)]
    for c in range(4):
        lanes = pl.ds(c * chunk, chunk)
        weights.append(bring(3 + c, in_h.at[:, :, :, lanes], in_w[c]))
        weights.append(bring(7 + c, down_h.at[c], down_w[c]))

    @pl.when(is_first)
    def _():
        bring(0, embed_h, side).start()

    for copy in weights:
        copy.start()

    @pl.when(is_last)
    def _():
        bring(0, head_h, side).start()

    barrier = pltpu.get_barrier_semaphore()

    def greet(offset, carry):
        peer = lax.rem(place + offset, devices)
        pl.semaphore_signal(barrier, inc=1, device_id={"dp": peer}, device_id_type=MESH)
        return carry

    def greet_stage(offset, carry):
        peer = lax.rem(stage + offset, stages)
        pl.semaphore_signal(barrier, inc=1, device_id={"pipe": peer}, device_id_type=MESH)
        return carry

    lax.fori_loop(1, devices, greet, 0)
    lax.fori_loop(1, stages, greet_stage, 0)

    def whole(part):
        return part[...].reshape(width, width)

    vec[...] = jnp.zeros_like(vec)
    rows_n, seq = token_ids.shape
    for index, member in enumerate((token_ids, segment_ids, target_ids)):
        ids[index] = jnp.full(ids.shape[1:], 4.0 if index == 1 else -1.0, F32)
        ids[index, 0:rows_n, 0:seq] = member[...].astype(F32)
    at_query = lax.broadcasted_iota(jnp.int32, (ROW, ROW), 1)
    at_key = lax.broadcasted_iota(jnp.int32, (ROW, ROW), 0)
    frames[...] = jnp.where(at_key < ((at_query * 43) // 256) * FRAME + FRAME, 1.0, 0.0)

    def column(index, row):
        values = jnp.broadcast_to(ids[index, pl.ds(row, 1), :], (8, ROW))
        return values.T[:, 0:1]

    def hot_rows(index, m):
        parts = [column(index, m * GROUP + r) for r in range(GROUP)]
        values = jnp.concatenate(parts, axis=0)
        places = lax.broadcasted_iota(jnp.int32, (tokens, vocab), 1).astype(F32)
        return values, jnp.where(values == places, 1.0, 0.0)

    def forward_copy(m):
        return pltpu.make_async_remote_copy(
            src_ref=outb.at[m],
            dst_ref=instream.at[m],
            send_sem=fsend.at[m],
            recv_sem=frecv.at[m],
            device_id={"pipe": up},
            device_id_type=MESH,
        )

    def backward_copy(m):
        return pltpu.make_async_remote_copy(
            src_ref=gs.at[m],
            dst_ref=gin.at[m],
            send_sem=bsend.at[m],
            recv_sem=brecv.at[m],
            device_id={"pipe": down},
            device_id_type=MESH,
        )

    @pl.when(is_first | is_last)
    def _():
        bring(0, embed_h, side).wait()

    for copy in weights:
        copy.wait()
    pl.semaphore_wait(barrier, devices - 1 + stages - 1)

    lane_low = lax.broadcasted_iota(jnp.int32, (ROW, ROW), 1) < ROW // 2

    def forward(m):
        @pl.when(is_first)
        def _():
            hot = hot_rows(0, m)[1].astype(BF16)
            instream[m] = dot(hot, side[...]).astype(BF16)

        @pl.when(jnp.logical_not(is_first))
        def _():
            forward_copy(m).wait_recv()

        normal, _ = normalise(instream[m].astype(F32))
        low = (normal * gains[0:1, :] + shifts[0:1, :]).astype(BF16)
        queries = dot(low, qkv_w[:, 0:width]) + qv_b[0:1, :]
        proj[m, :, 0:width] = (queries * (ROW // 2) ** -0.5).astype(BF16)
        proj[m, :, width : 2 * width] = dot(low, qkv_w[:, width : 2 * width]).astype(BF16)
        proj[m, :, 2 * width : 3 * width] = (
            dot(low, qkv_w[:, 2 * width : 3 * width]) + qv_b[1:2, :]
        ).astype(BF16)
        masks, scores = [], []
        for r in range(GROUP):
            rows = slice(r * ROW, (r + 1) * ROW)
            kinds = lax.broadcasted_iota(jnp.int32, (16, ROW), 0).astype(F32)
            member = jnp.where(ids[1, pl.ds(m * GROUP + r, 1), :] == kinds, 1.0, 0.0).astype(BF16)
            mask = jnp.where(dot_tn(member, member) * frames[...] > 0.5, 0.0, MASKED)
            masks.append(jnp.concatenate([mask, mask], axis=1))
            for p in range(pairs):
                q = stack_pair(proj[m, rows, p * ROW : (p + 1) * ROW], lane_low)
                k = proj[m, rows, width + p * ROW : width + (p + 1) * ROW]
                scores.append(dot_nt(k, q))

        def mix(unit):
            r, p = unit // pairs, unit % pairs
            rows = slice(r * ROW, (r + 1) * ROW)
            v = proj[m, rows, 2 * width + p * ROW : 2 * width + (p + 1) * ROW]
            both = dot_tn(probs[m, unit // 2, unit % 2], v)
            mixed[m, rows, p * ROW : (p + 1) * ROW] = join_pair(both, lane_low).astype(BF16)

        for unit in range(GROUP * pairs):
            masked = scores[unit] + masks[unit // pairs]
            expo = jnp.exp(masked - jnp.max(masked, axis=0, keepdims=True))
            total = jnp.sum(expo, axis=0, keepdims=True)
            probs[m, unit // 2, unit % 2] = (expo * (1.0 / total)).astype(BF16)
            if unit:
                mix(unit - 1)
        mix(GROUP * pairs - 1)
        mid = instream[m].astype(F32) + (dot(mixed[m], out_w[...]) + out_b[0:1, :])
        middle[m] = mid
        normal2, _ = normalise(mid)
        low2 = (normal2 * gains[1:2, :] + shifts[1:2, :]).astype(BF16)
        parts = hidden_n // chunk

        def spread(c):
            return dot(low2, whole(in_w[c]))

        total, ahead = None, spread(0)
        for c in range(parts):
            cols = slice(c * chunk, (c + 1) * chunk)
            hid = ahead + in_b[0:1, cols]
            if c + 1 < parts:
                ahead = spread(c + 1)
            square = hid * hid
            tan = jnp.tanh(hid * (GELU_A + (GELU_A * GELU_B) * square))
            half = 0.5 + 0.5 * tan
            act = (hid * half).astype(BF16)
            active[m, :, cols] = act
            rise = (1.0 - tan * tan) * (0.5 * GELU_A + (1.5 * GELU_A * GELU_B) * square)
            slope[m, :, cols] = (half + hid * rise).astype(BF16)
            term = dot(act, whole(down_w[c]))
            total = term if total is None else total + term
        lo[...] = middle[m] + (total + out_b[1:2, :])

        @pl.when(jnp.logical_not(is_last))
        def _():
            outb[m] = lo[...].astype(BF16)
            forward_copy(m).start()

    def head(m):
        normal, scale = normalise(lo[...])
        outb[m] = (normal * fin_gain[...] + fin_bias[...]).astype(BF16)
        logits = dot_nt(outb[m], side[...])
        top = jnp.max(logits, axis=-1, keepdims=True)
        expo = jnp.exp(logits - top)
        total = jnp.sum(expo, axis=-1, keepdims=True)
        target, hot = hot_rows(2, m)
        grad_logits = jnp.where(target >= 0.0, expo * (1.0 / total) - hot, 0.0).astype(BF16)
        s_xl[m] = grad_logits
        grad_final = dot(grad_logits, side[...])
        vec[V_FINAL_GAIN : V_FINAL_GAIN + 1, :] += column_sum(grad_final * normal)
        vec[V_FINAL_BIAS : V_FINAL_BIAS + 1, :] += column_sum(grad_final)
        go[...] = norm_backward(grad_final, normal, scale, fin_gain[...])

    def backward(m):
        @pl.when(jnp.logical_not(is_last))
        def _():
            backward_copy(m).wait_recv()
            go[...] = gin[m].astype(F32)

        gres = go[...].astype(BF16)
        gin[m] = gres
        parts = hidden_n // chunk

        def spread(c):
            return dot_nt(gres, whole(down_w[c]))

        total, ahead = None, spread(0)
        for c in range(parts):
            cols = slice(c * chunk, (c + 1) * chunk)
            gact = ahead
            if c + 1 < parts:
                ahead = spread(c + 1)
            ghid = (gact * slope[m, :, cols].astype(F32)).astype(BF16)
            slope[m, :, cols] = ghid
            term = dot_nt(ghid, whole(in_w[c]))
            total = term if total is None else total + term
        normal2, scale2 = normalise(middle[m])
        vec[V_GAIN2 : V_GAIN2 + 1, :] += column_sum(total * normal2)
        vec[V_SHIFT2 : V_SHIFT2 + 1, :] += column_sum(total)
        gmid[...] = go[...] + norm_backward(total, normal2, scale2, gains[1:2, :])
        gbr = gmid[...].astype(BF16)
        s_gbr[m] = gbr
        gmix = dot_nt(gbr, out_w[...]).astype(BF16)
        grads = []
        for r in range(GROUP):
            rows = slice(r * ROW, (r + 1) * ROW)
            for p in range(pairs):
                gm = stack_pair(gmix[rows, p * ROW : (p + 1) * ROW], lane_low)
                vlanes = slice(2 * width + p * ROW, 2 * width + (p + 1) * ROW)
                grads.append(dot_nt(proj[m, rows, vlanes], gm))
                unit = r * pairs + p
                proj[m, rows, vlanes] = dot(probs[m, unit // 2, unit % 2], gm).astype(BF16)

        def pull(unit, gsc):
            r, p = unit // pairs, unit % pairs
            rows = slice(r * ROW, (r + 1) * ROW)
            lanes = slice(p * ROW, (p + 1) * ROW)
            klanes = slice(width + p * ROW, width + (p + 1) * ROW)
            q = stack_pair(proj[m, rows, lanes], lane_low)
            gq = join_pair(dot_tn(gsc, proj[m, rows, klanes]), lane_low) * (ROW // 2) ** -0.5
            gk = dot(gsc, q)
            proj[m, rows, klanes] = gk.astype(BF16)
            proj[m, rows, lanes] = gq.astype(BF16)

        waiting = None
        for unit in range(GROUP * pairs):
            weights = probs[m, unit // 2, unit % 2].astype(F32)
            inner = jnp.sum(weights * grads[unit], axis=0, keepdims=True)
            gsc = (weights * (grads[unit] - inner)).astype(BF16)
            if waiting is not None:
                pull(unit - 1, waiting)
            waiting = gsc
        pull(GROUP * pairs - 1, waiting)
        gproj = proj[m]
        gnormed = dot_nt(gproj, qkv_w[...])
        normal, scale = normalise(instream[m].astype(F32))
        vec[V_GAIN1 : V_GAIN1 + 1, :] += column_sum(gnormed * normal)
        vec[V_SHIFT1 : V_SHIFT1 + 1, :] += column_sum(gnormed)
        gs[m] = (gmid[...] + norm_backward(gnormed, normal, scale, gains[0:1, :])).astype(BF16)

        @pl.when(jnp.logical_not(is_first))
        def _():
            backward_copy(m).start()

    def tick(t, carry):
        m_forward = t - stage
        m_backward = t - (2 * (stages - 1) - stage)

        @pl.when((m_forward >= 0) & (m_forward < micros))
        def _():
            forward(m_forward)

        @pl.when((m_backward >= 0) & (m_backward < micros))
        def _():
            @pl.when(is_last)
            def _():
                head(m_backward)

            backward(m_backward)

        return carry

    lax.fori_loop(0, micros + 2 * (stages - 1), tick, 0)

    embed_stage = stages - 2
    is_extra = (stage == embed_stage) | is_last
    dims = line_dims(devices)
    turned_left = qkv_w
    mats = {
        "mixed": mixed,
        "active": active,
        "gres": gin,
        "ghid": slope,
        "gbr": s_gbr,
        "gproj": proj,
    }

    def mat(name, lanes=slice(None)):
        value = mats[name][:, :, lanes]
        return value.reshape(micros * tokens, value.shape[2])

    where = [lax.rem(place // stride, size) for size, stride in dims]

    def identity(size):
        here = lax.broadcasted_iota(jnp.int32, (size, size), 0)
        there = lax.broadcasted_iota(jnp.int32, (size, size), 1)
        return jnp.where(here == there, 1.0, 0.0).astype(BF16)

    held = []

    def turn(name):
        if held[-1:] == [name]:
            return
        held.append(name)
        unit = identity(256)
        if name in ("normed", "normed2"):
            row = 0 if name == "normed" else 1
            source = instream if name == "normed" else middle
            for m in range(micros):
                normal, _ = normalise(source[m].astype(F32))
                again = (normal * gains[row : row + 1, :] + shifts[row : row + 1, :]).astype(BF16)
                for q in range(width // 256):
                    part = dot_nt(unit, again[:, q * 256 : (q + 1) * 256])
                    turned_left[q * 256 : (q + 1) * 256, m * tokens : (m + 1) * tokens] = part.astype(BF16)
            return
        for q in range(width // 256):
            part = dot_nt(unit, mat(name, slice(q * 256, (q + 1) * 256)))
            turned_left[q * 256 : (q + 1) * 256, :] = part.astype(BF16)

    bits = devices.bit_length() - 1
    vec_send, vec_recv = take(2)
    vec_sems = take(2)

    def vec_copy(k):
        peer = jnp.bitwise_xor(place, 1 << k)
        return pltpu.make_async_remote_copy(
            src_ref=vec_send.at[k],
            dst_ref=vec_recv.at[k],
            send_sem=vec_sems[0].at[k],
            recv_sem=vec_sems[1].at[k],
            device_id={"dp": peer},
            device_id_type=MESH,
        )

    def vec_step(k):
        def run():
            if k == 0:
                vec_send[0] = vec[...]
                ones = jnp.ones((16, micros * tokens), BF16)
                for name, start, row in (
                    ("gproj", 0, V_QUERY),
                    ("gproj", 2 * width, V_VALUE),
                    ("gbr", 0, V_BRANCH),
                    ("gres", 0, V_RESULT),
                ):
                    part = dot(ones, mat(name, slice(start, start + width)))
                    vec_send[0, row : row + 1, :] = part[0:1, :]
                for q in range(hidden_n // width):
                    part = dot(ones, mat("ghid", slice(q * width, (q + 1) * width)))
                    vec_send[0, V_HIDDEN + q : V_HIDDEN + q + 1, :] = part[0:1, :]
            else:
                vec_copy(k - 1).wait_recv()
                vec_send[k] = vec_send[k - 1] + vec_recv[k - 1]
            if k < bits:
                vec_copy(k).start()

        return run

    final_send, final_recv = take(2)
    final_sems = take(2)

    def final_copy(offset):
        peer = lax.rem(stages - 1 + offset, stages)
        return pltpu.make_async_remote_copy(
            src_ref=final_send,
            dst_ref=final_recv,
            send_sem=final_sems[0].at[offset],
            recv_sem=final_sems[1].at[0],
            device_id={"pipe": peer},
            device_id_type=MESH,
        )

    def vec_last():
        vec_step(bits)()
        vec_out[...] = vec_send[bits]

        @pl.when(stage == stages - 1)
        def _():
            final_send[...] = vec_send[bits, 8:16, :]
            for offset in range(1, stages):
                final_copy(offset).start()

    def vec_finish():
        @pl.when(stage != stages - 1)
        def _():
            final_copy(1).wait_recv()
            vec_out[V_FINAL_GAIN : V_FINAL_BIAS + 1, :] = final_recv[
                V_FINAL_GAIN - 8 : V_FINAL_BIAS - 7, :
            ]

    def vec_drain():
        for k in range(bits):
            vec_copy(k).wait_send()

        @pl.when(stage == stages - 1)
        def _():
            for offset in range(1, stages):
                final_copy(offset).wait_send()

    def ship():
        return pltpu.make_async_remote_copy(
            src_ref=s_xl.at[pl.ds(0, 2)],
            dst_ref=s_xl.at[pl.ds(0, 2)],
            send_sem=ship_sem.at[0],
            recv_sem=ship_sem.at[1],
            device_id={"pipe": embed_stage},
            device_id_type=MESH,
        )

    def ship_embed():
        rows, half = vocab // stages, width // 2

        @pl.when(is_first)
        def _():
            right = gs[...].reshape(micros * tokens, width)
            for p in range(stages):
                here = lax.broadcasted_iota(jnp.int32, (rows, ROW), 0).astype(F32) + p * rows
                hot = [
                    jnp.where(ids[0, r : r + 1, :] == here, 1.0, 0.0).astype(BF16) for r in range(rows_n)
                ]
                part = dot(jnp.concatenate(hot, axis=1), right).astype(BF16)
                for k in range(2):
                    s_xl[k, :, p * half : (p + 1) * half] = part[:, k * half : (k + 1) * half]
            ship().start()

    extra_sum, extra_send_sem, extra_recv_sem, last_sum, ship_sem = take(5)
    share = embed_out.shape[0]

    def extra_copy(source, offset, target):
        peer = lax.rem(source + offset, stages)
        return pltpu.make_async_remote_copy(
            src_ref=extra_sum.at[pl.ds(pl.multiple_of(peer * share, share), share)],
            dst_ref=target,
            send_sem=extra_send_sem.at[offset],
            recv_sem=extra_recv_sem.at[0 if source == embed_stage else 1],
            device_id={"pipe": peer},
            device_id_type=MESH,
        )

    def chunk_steps(kind, c, block, turned):
        order = list(range(len(dims)))
        if turned:
            order.reverse()
        if kind == "down":
            full = probs.at[c]
        elif kind == "extra":
            full = probs.at[4 + c]
        else:
            full = (down_w + in_w)[{"out": 0, "in": 1, "qkv": 5}[kind] + c]

        def compute():
            if kind == "down":
                if c % 2 == 1:
                    return
                turn("gres")
                half = width // 2
                lines = slice((c // 2) * half, (c // 2 + 1) * half)
                parts = dot(turned_left[lines, :], mat("active")).astype(BF16)
                depth = hidden_n // devices
                unit = identity(depth)
                for d in range(devices):
                    back = dot_nt(unit, parts[:, d * depth : (d + 1) * depth]).astype(BF16)
                    for k in range(2):
                        piece = back[:, k * ROW : (k + 1) * ROW]
                        piece = jnp.concatenate([piece[: depth // 2], piece[depth // 2 :]], axis=1)
                        probs[(c + k,) + split(d)] = piece
            elif kind == "extra":
                if c == 1:
                    return
                rows = vocab // stages
                share = rows // devices
                half = width // 2

                def fill(left, right):
                    for p in range(stages):
                        part = left(p, right).astype(BF16).reshape(devices, share, width)
                        for d in range(devices):
                            for k in range(2):
                                lines = slice(p * share, (p + 1) * share)
                                probs[(4 + k,) + split(d) + (lines,)] = part[
                                    d, :, k * half : (k + 1) * half
                                ]

                def flat(ref):
                    return ref[...].reshape(micros * tokens, ref.shape[2])

                @pl.when(stage == embed_stage)
                def _():
                    ship().wait_recv()
                    for d in range(devices):
                        for k in range(2):
                            for p in range(stages):
                                lines = slice(p * share, (p + 1) * share)
                                probs[(4 + k,) + split(d) + (lines,)] = s_xl[
                                    k, d * share : (d + 1) * share, p * half : (p + 1) * half
                                ]

                @pl.when(is_last)
                def _():
                    def soft_part(p, right):
                        left = s_xl[:, :, p * rows : (p + 1) * rows]
                        return dot_tn(left.reshape(micros * tokens, rows), right)

                    fill(soft_part, flat(outb))
            else:
                left, right = {
                    "in": ("normed2", "ghid"),
                    "out": ("mixed", "gbr"),
                    "qkv": ("normed", "gproj"),
                }[kind]
                turn(left)
                part = dot(turned_left[...], mat(right, slice(c * width, (c + 1) * width)))
                part = part.astype(BF16).reshape((devices,) + block)
                for d in range(devices):
                    full[split(d)] = part[d]

        def split(d):
            return tuple((d // stride) % size for size, stride in reversed(dims))

        steps = [[compute]]
        for at, phase in enumerate(order):
            size = dims[phase][0]
            buffers = take(3)
            done = order[:at]
            last = at == len(order) - 1
            steps[-1].append(functools.partial(line_step, phase, size, 1, full, buffers, done))
            for t in range(2, size):
                steps.append([functools.partial(line_step, phase, size, t, full, buffers, done)])
            drains.append((kind, functools.partial(line_drain, phase, size, full, buffers, done)))
            steps.append([functools.partial(line_final, kind, c, phase, size, full, buffers, done, last)])
        if kind == "extra":
            steps = [[gated([part]) for part in step] for step in steps]
        return steps

    def gated(step):
        def run():
            @pl.when(is_extra)
            def _():
                for part in step:
                    part()

        return run

    def block_of(full, phase, j, done):
        spot = [slice(None)] * len(dims)
        for other in done:
            spot[len(dims) - 1 - other] = where[other]
        spot[len(dims) - 1 - phase] = j
        return full.at[tuple(spot)]

    def line_copy(phase, size, t, side, full, buffers, done):
        recv, ssem, rsem = buffers
        i = where[phase]
        stride = dims[phase][1]
        if side == 0:
            j, peer = size - t + i, place + jnp.where(i < size - 1, stride, 0)
        else:
            j, peer = t - size + i, place - jnp.where(i > 0, stride, 0)
        return pltpu.make_async_remote_copy(
            src_ref=block_of(full, phase, jnp.clip(j, 0, size - 1), done),
            dst_ref=recv.at[0 if size == 2 else side, t - 1],
            send_sem=ssem.at[side, t - 1],
            recv_sem=rsem.at[side, t - 1],
            device_id={"dp": peer},
            device_id_type=MESH,
        )

    def sends(i, size, t, side):
        return (i <= t - 1) if side == 0 else (i >= size - t)

    def line_step(phase, size, t, full, buffers, done):
        i = where[phase]
        for side in range(2):
            at_end = (i == 0) if side == 0 else (i == size - 1)
            j = size - t + i if side == 0 else t - size + i
            j = jnp.clip(j, 0, size - 1)

            @pl.when(sends(i, size, t, side))
            def _():
                if t > 1:
                    @pl.when(jnp.logical_not(at_end))
                    def _():
                        line_copy(phase, size, t - 1, side, full, buffers, done).wait_recv()
                        own = block_of(full, phase, j, done)
                        got = buffers[0][0 if size == 2 else side, t - 2]
                        own[...] = (own[...].astype(F32) + got.astype(F32)).astype(BF16)

                line_copy(phase, size, t, side, full, buffers, done).start()

    def line_final(kind, c, phase, size, full, buffers, done, last):
        i = where[phase]
        own = block_of(full, phase, i, done)
        total = own
        if last:
            lanes = slice(c * width, (c + 1) * width)
            slots = {
                "qkv": lambda: qkv_out.at[:, lanes],
                "in": lambda: in_out.at[:, lanes],
                "out": lambda: out_out,
                "down": lambda: last_sum,
                "extra": lambda: extra_sum.at[:, c * (width // 2) : (c + 1) * (width // 2)],
            }
            total = slots[kind]()
        lower, upper = i > 0, i < size - 1

        def arrived(side):
            line_copy(phase, size, size - 1, side, full, buffers, done).wait_recv()
            return buffers[0][0 if size == 2 else side, size - 2].astype(F32)

        @pl.when(lower & upper)
        def _():
            total[...] = (own[...].astype(F32) + arrived(0) + arrived(1)).astype(total.dtype)

        @pl.when(lower & jnp.logical_not(upper))
        def _():
            total[...] = (own[...].astype(F32) + arrived(0)).astype(total.dtype)

        @pl.when(jnp.logical_not(lower))
        def _():
            total[...] = (own[...].astype(F32) + arrived(1)).astype(total.dtype)

        if last and kind == "down":
            deep = down_out.shape[0] // 2
            lanes = slice(c * ROW, (c + 1) * ROW)
            down_out[0:deep, lanes] = last_sum[:, 0:ROW]
            down_out[deep : 2 * deep, lanes] = last_sum[:, ROW : 2 * ROW]
        if last and kind == "extra" and c == 1:
            for source_stage, out in ((embed_stage, embed_out), (stages - 1, head_out)):
                @pl.when(stage == source_stage)
                def _():
                    for offset in range(1, stages):
                        extra_copy(source_stage, offset, extra_recv[0 if source_stage == embed_stage else 1]).start()
                    out[...] = extra_sum[source_stage * share : (source_stage + 1) * share, :]

    def line_drain(phase, size, full, buffers, done):
        i = where[phase]
        for side in range(2):
            for t in range(1, size):
                @pl.when(sends(i, size, t, side))
                def _():
                    line_copy(phase, size, t, side, full, buffers, done).wait_send()

    extra_recv = take(2)
    drains = []
    chains = [chunk_steps(*item) for item in plan]
    depth = len(chains[0])
    vec_chain = [vec_step(k) for k in range(bits)] + [vec_last]
    starts, first, extra_rounds = [], 0, iter((1, 3, 5, 7))
    for item in plan:
        if item[3]:
            starts.append(next(extra_rounds))
        else:
            starts.append(first)
            first += 1
    loaded_at = max(start for start, item in zip(starts, plan) if item[0] == "qkv" and item[1] == 0)
    for r in range(max(starts) + depth):
        for d in [0] + list(range(depth - 1, 0, -1)):
            for start, chain in zip(starts, chains):
                if r - start != d:
                    continue
                for part in chain[d]:
                    part()
            if r == d == 0:
                ship_embed()
        if 0 <= r - loaded_at < len(vec_chain):
            vec_chain[r - loaded_at]()
    vec_finish()
    for source_stage, out in ((embed_stage, embed_out), (stages - 1, head_out)):
        @pl.when(stage != source_stage)
        def _():
            got = extra_recv[0 if source_stage == embed_stage else 1]
            extra_copy(source_stage, 1, got).wait_recv()
            out[...] = got[...]

        @pl.when(stage == source_stage)
        def _():
            for offset in range(1, stages):
                extra_copy(source_stage, offset, extra_recv[0]).wait_send()

    vec_drain()
    for kind, drain in drains:
        if kind == "extra":
            gated([drain])()
        else:
            drain()

    @pl.when(is_first)
    def _():
        ship().wait_send()

    for m in range(micros):
        @pl.when(jnp.logical_not(is_last))
        def _():
            forward_copy(m).wait_send()

        @pl.when(jnp.logical_not(is_first))
        def _():
            backward_copy(m).wait_send()


def step_plan(width, hid, vocab, stages, devices):
    plan = []
    for kind, c, _, turned in chunk_plan(width, hid, vocab, stages, devices):
        wide = kind in ("down", "extra")
        plan.append((kind, c, (ROW, 2 * ROW) if wide else (width // devices, width), turned))
    extra = [item for item in plan if item[0] == "extra"]
    rest = [item for item in plan if item[0] != "extra"]
    return rest + extra


def run_step(stages, devices, token_ids, segment_ids, target_ids, params):
    embed, qkv_w, qv_b, out_w, out_b, in_w, in_b, down_w, gains, shifts, fg, fb, head_w = params
    dims = line_dims(devices)
    width, hid, vocab = embed.shape[1], in_w.shape[1], head_w.shape[0]
    tokens = GROUP * ROW
    micros = token_ids.shape[0] // GROUP
    vmem = pl.BlockSpec(memory_space=pltpu.VMEM)
    hbm = pl.BlockSpec(memory_space=pl.ANY)
    sizes = tuple(size for size, _ in reversed(dims))
    slim = width // devices
    share = vocab // (stages * devices)
    plan = step_plan(width, hid, vocab, stages, devices)
    bits = devices.bit_length() - 1

    def scratch(lead, columns, kind=BF16):
        return pltpu.VMEM((lead, tokens, columns), kind)

    def sums(*shape):
        return pltpu.VMEM(shape, F32)

    dma = pltpu.SemaphoreType.DMA
    scratch_shapes = [
        pltpu.VMEM((vocab, width), BF16),
        pltpu.VMEM((width, 3 * width), BF16),
        pltpu.VMEM((width, width), BF16),
    ]
    scratch_shapes += [pltpu.VMEM(sizes + (slim, width), BF16)] * 8
    scratch_shapes += [
        scratch(micros, width),
        scratch(micros, width),
        scratch(micros, width),
        scratch(micros, width),
        scratch(micros, 3 * width),
        pltpu.VMEM((micros,) + sizes + (ROW, 2 * ROW), BF16),
        scratch(micros, width),
        scratch(micros, width, F32),
        scratch(micros, hid),
        scratch(micros, hid),
        sums(tokens, width),
        sums(tokens, width),
        scratch(micros, width),
        scratch(micros, vocab),
        sums(VEC_ROWS, width),
        sums(3, 16, ROW),
        sums(ROW, ROW),
        dma((micros,)),
        dma((micros,)),
        dma((micros,)),
        dma((micros,)),
        dma((11,)),
        sums(bits + 1, VEC_ROWS, width),
        sums(bits, VEC_ROWS, width),
        dma((bits,)),
        dma((bits,)),
        sums(8, width),
        sums(8, width),
        dma((stages,)),
        dma((1,)),
        sums(stages * share, width),
        dma((stages,)),
        dma((2,)),
        sums(ROW, 2 * ROW),
        dma((2,)),
        sums(share, width),
        sums(share, width),
    ]
    for _, _, block, turned in plan:
        remain = list(reversed(dims))
        for size, stride in dims[::-1] if turned else dims:
            remain.remove((size, stride))
            piece = tuple(other for other, _ in remain) + block
            scratch_shapes.append(pltpu.VMEM((1 if size == 2 else 2, size - 1) + piece, BF16))
            scratch_shapes += [dma((2, size - 1))] * 2

    def result(*shape):
        return jax.ShapeDtypeStruct(shape, F32)

    return pl.pallas_call(
        functools.partial(step_kernel, stages, micros, devices, plan),
        out_shape=[
            result(slim, 3 * width),
            result(slim, width),
            result(slim, hid),
            result(hid // devices, width),
            result(share, width),
            result(share, width),
            result(VEC_ROWS, width),
        ],
        in_specs=[vmem] * 10 + [hbm] * 6,
        out_specs=[vmem] * 7,
        scratch_shapes=scratch_shapes,
        compiler_params=pltpu.CompilerParams(
            collective_id=2, has_side_effects=True, vmem_limit_bytes=63 * 1024 * 1024
        ),
        name="step",
    )(
        token_ids,
        segment_ids,
        target_ids,
        qv_b,
        out_b,
        in_b,
        gains,
        shifts,
        fg,
        fb,
        embed,
        head_w,
        qkv_w,
        out_w,
        in_w.reshape(sizes + (slim, hid)),
        down_w.reshape((hid // width,) + sizes + (slim, width)),
    )


def finish_kernel(devices, embed_g, qkv_g, out_g, in_g, down_g, head_g, vec, *outs):
    place = lax.axis_index("dp")
    width = vec.shape[1]
    (embed_o, qkv_o, qv_o, out_o, outb_o, in_o, inb_o, down_o, gain_o, shift_o, fg_o, fb_o, head_o) = outs
    embed_o[...] = embed_g[...]
    head_o[...] = head_g[...]
    for source, target in ((qkv_g, qkv_o), (out_g, out_o), (in_g, in_o), (down_g, down_o)):
        target[0] = source[...]
    lanes = width // devices
    turned = pltpu.roll(vec[0:8, :], lax.rem(width - place * lanes, width), 1)
    for row, out in ((V_QUERY, qv_o), (V_BRANCH, outb_o), (V_GAIN1, gain_o), (V_SHIFT1, shift_o)):
        out[0] = turned[row : row + 2, 0:lanes]
    share = inb_o.shape[1]
    first = place * share
    row = vec[pl.ds(V_HIDDEN + first // width, 1), :]
    wide = jnp.broadcast_to(row, (8, width))
    inb_o[...] = pltpu.roll(wide, lax.rem(width - lax.rem(first, width), width), 1)[0:1, 0:share]
    fg_o[...] = vec[V_FINAL_GAIN : V_FINAL_GAIN + 1, :]
    fb_o[...] = vec[V_FINAL_BIAS : V_FINAL_BIAS + 1, :]


def run_finish(devices, embed_g, qkv_g, out_g, in_g, down_g, head_g, vec):
    vmem = pl.BlockSpec(memory_space=pltpu.VMEM)
    width = vec.shape[1]
    lanes = width // devices

    def shape(*sizes):
        return jax.ShapeDtypeStruct(sizes, F32)

    pair = shape(1, 2, lanes)
    return pl.pallas_call(
        functools.partial(finish_kernel, devices),
        out_shape=[
            shape(*embed_g.shape),
            shape(1, *qkv_g.shape),
            pair,
            shape(1, *out_g.shape),
            pair,
            shape(1, *in_g.shape),
            shape(1, in_g.shape[1] // devices),
            shape(1, *down_g.shape),
            pair,
            pair,
            shape(1, width),
            shape(1, width),
            shape(*head_g.shape),
        ],
        in_specs=[vmem] * 7,
        out_specs=[vmem] * 13,
        name="finish",
    )(embed_g, qkv_g, out_g, in_g, down_g, head_g, vec)


def on_device(
    token_ids,
    segment_ids,
    target_ids,
    embed_table,
    qkv_weight,
    qv_bias,
    out_weight,
    out_biases,
    ff_in,
    ff_in_bias,
    ff_out,
    norm_gains,
    norm_biases,
    final_gain,
    final_bias,
    head_weight,
):
    stages = lax.axis_size("pipe")
    devices = lax.axis_size("dp")
    params = (
        embed_table,
        qkv_weight[0],
        qv_bias[0],
        out_weight[0],
        out_biases[0],
        ff_in[0],
        ff_in_bias,
        ff_out[0],
        norm_gains[0],
        norm_biases[0],
        final_gain[None],
        final_bias[None],
        head_weight,
    )
    if devices == 8:
        grads = run_step(stages, devices, token_ids, segment_ids, target_ids, params)
    else:
        *saved, vec = run_pipeline(stages, token_ids, segment_ids, target_ids, params)
        grads = run_gradients(stages, devices, saved, vec, token_ids)
    qkv_g, out_g, in_g, down_g, embed_g, head_g, sums = grads
    done = list(run_finish(devices, embed_g, qkv_g, out_g, in_g, down_g, head_g, sums))
    done[10], done[11] = done[10][0], done[11][0]
    return tuple(done)


def solution(mesh):
    layer3 = P("pipe", None, None)
    return jax.shard_map(
        on_device,
        mesh=mesh,
        in_specs=(
            P("dp", None),
            P("dp", None),
            P("dp", None),
            P(),
            layer3,
            layer3,
            layer3,
            layer3,
            layer3,
            P("pipe", None),
            layer3,
            layer3,
            layer3,
            P(),
            P(),
            P(),
        ),
        out_specs=(
            P(("pipe", "dp"), None),
            P("pipe", "dp", None),
            P("pipe", None, "dp"),
            P("pipe", "dp", None),
            P("pipe", None, "dp"),
            P("pipe", "dp", None),
            P("pipe", "dp"),
            P("pipe", "dp", None),
            P("pipe", None, "dp"),
            P("pipe", None, "dp"),
            P(),
            P(),
            P(("pipe", "dp"), None),
        ),
        check_vma=False,
    )
```

```python
import functools

import jax
import jax.numpy as jnp
from jax import lax
from jax.experimental import pallas as pl
from jax.experimental.pallas import tpu as pltpu
from jax.sharding import PartitionSpec as P

HEADS = 8
FRAME = 6
ROW = 128
GROUP = 2
MASKED = -1e30
GELU_A = 0.7978845608
GELU_B = 0.044715
MESH = pl.DeviceIdType.MESH
F32 = jnp.float32
BF16 = jnp.bfloat16

VEC_ROWS = 16
V_QUERY, V_VALUE, V_BRANCH, V_RESULT, V_GAIN1, V_GAIN2, V_SHIFT1, V_SHIFT2 = range(8)
V_HIDDEN = 8
V_FINAL_GAIN, V_FINAL_BIAS = 12, 13


def dot(a, b):
    return lax.dot_general(a, b, (((1,), (0,)), ((), ())), preferred_element_type=F32)


def dot_nt(a, b):
    return lax.dot_general(a, b, (((1,), (1,)), ((), ())), preferred_element_type=F32)


def dot_tn(a, b):
    return lax.dot_general(a, b, (((0,), (0,)), ((), ())), preferred_element_type=F32)


def normalise(values):
    centre = jnp.mean(values, axis=-1, keepdims=True)
    centered = values - centre
    spread = jnp.mean(centered * centered, axis=-1, keepdims=True)
    scale = lax.rsqrt(spread + 1e-05)
    return centered * scale, scale


def norm_backward(grad, normal, scale, gain):
    grad_n = grad * gain
    mean_grad = jnp.mean(grad_n, axis=-1, keepdims=True)
    mean_proj = jnp.mean(grad_n * normal, axis=-1, keepdims=True)
    return scale * (grad_n - mean_grad - normal * mean_proj)


def column_sum(values):
    return jnp.sum(values, axis=0, keepdims=True)


def stack_pair(pair, low_lanes):
    zero = jnp.zeros_like(pair)
    return jnp.concatenate(
        [jnp.where(low_lanes, pair, zero), jnp.where(low_lanes, zero, pair)], axis=0
    )


def join_pair(stacked, low_lanes):
    half = stacked.shape[0] // 2
    return jnp.where(low_lanes, stacked[:half], stacked[half:])


def pipeline_kernel(
    stages,
    micros,
    token_ids,
    segment_ids,
    target_ids,
    embed,
    qkv_w,
    qv_b,
    out_w,
    out_b,
    in_w,
    in_b,
    down_w,
    gains,
    shifts,
    fin_gain,
    fin_bias,
    head_w,
    normed_o,
    mixed_o,
    normed2_o,
    active_o,
    gres_o,
    ghid_o,
    gbr_o,
    gproj_o,
    xl_o,
    xr_o,
    vec,
    instream,
    outb,
    gin,
    gs,
    normed,
    proj,
    probs,
    mixed,
    middle,
    normed2,
    active,
    slope,
    lo,
    go,
    gmid,
    s_gres,
    s_ghid,
    s_gbr,
    s_gproj,
    s_xl,
    ids,
    frames,
    fsend,
    frecv,
    bsend,
    brecv,
    osem,
):
    stage = lax.axis_index("pipe")
    tokens, width = instream.shape[1], instream.shape[2]
    hidden_n = in_b.shape[1]
    vocab = head_w.shape[0]
    pairs = width // ROW
    chunk = 512
    is_first = stage == 0
    is_last = stage == stages - 1
    up = jnp.minimum(stage + 1, stages - 1)
    down = jnp.maximum(stage - 1, 0)

    barrier = pltpu.get_barrier_semaphore()

    @pl.when(jnp.logical_not(is_first))
    def _():
        pl.semaphore_signal(barrier, inc=1, device_id={"pipe": down}, device_id_type=MESH)

    @pl.when(jnp.logical_not(is_last))
    def _():
        pl.semaphore_signal(barrier, inc=1, device_id={"pipe": up}, device_id_type=MESH)

    pl.semaphore_wait(barrier, jnp.where(is_first | is_last, 1, 2))
    vec[...] = jnp.zeros_like(vec)
    rows_n, seq = token_ids.shape
    for index, member in enumerate((token_ids, segment_ids, target_ids)):
        ids[index] = jnp.full(ids.shape[1:], 4.0 if index == 1 else -1.0, F32)
        ids[index, 0:rows_n, 0:seq] = member[...].astype(F32)
    at_query = lax.broadcasted_iota(jnp.int32, (ROW, ROW), 1)
    at_key = lax.broadcasted_iota(jnp.int32, (ROW, ROW), 0)
    frames[...] = jnp.where(at_key < ((at_query * 43) // 256) * FRAME + FRAME, 1.0, 0.0)

    def column(index, row):
        values = jnp.broadcast_to(ids[index, pl.ds(row, 1), :], (8, ROW))
        return values.T[:, 0:1]

    def hot_rows(index, m):
        parts = [column(index, m * GROUP + r) for r in range(GROUP)]
        values = jnp.concatenate(parts, axis=0)
        places = lax.broadcasted_iota(jnp.int32, (tokens, vocab), 1).astype(F32)
        return values, jnp.where(values == places, 1.0, 0.0)

    def forward_copy(m):
        return pltpu.make_async_remote_copy(
            src_ref=outb.at[m],
            dst_ref=instream.at[m],
            send_sem=fsend.at[m],
            recv_sem=frecv.at[m],
            device_id={"pipe": up},
            device_id_type=MESH,
        )

    def backward_copy(m):
        return pltpu.make_async_remote_copy(
            src_ref=gs.at[m],
            dst_ref=gin.at[m],
            send_sem=bsend.at[m],
            recv_sem=brecv.at[m],
            device_id={"pipe": down},
            device_id_type=MESH,
        )

    def save(index, src, dst, m):
        return pltpu.make_async_copy(src, dst.at[m], osem.at[index, m])

    def saves_forward(m):
        return [
            save(0, normed.at[m], normed_o, m),
            save(1, mixed.at[m], mixed_o, m),
            save(2, normed2.at[m], normed2_o, m),
            save(3, active.at[m], active_o, m),
        ]

    def saves_backward(m):
        slot = lax.rem(m, 2)
        return [
            save(4, s_gres.at[slot], gres_o, m),
            save(5, s_ghid.at[slot], ghid_o, m),
            save(6, s_gbr.at[slot], gbr_o, m),
            save(7, s_gproj.at[slot], gproj_o, m),
        ]

    def save_xl(m):
        return save(8, s_xl.at[lax.rem(m, 2)], xl_o, m)

    def put_xl(m, value):
        @pl.when(m >= 2)
        def _():
            save_xl(m - 2).wait()

        s_xl[lax.rem(m, 2)] = value
        save_xl(m).start()

    lane_low = lax.broadcasted_iota(jnp.int32, (ROW, ROW), 1) < ROW // 2

    def forward(m):
        @pl.when(is_first)
        def _():
            hot = hot_rows(0, m)[1].astype(BF16)
            instream[m] = dot(hot, embed[...]).astype(BF16)

        @pl.when(jnp.logical_not(is_first))
        def _():
            forward_copy(m).wait_recv()

        normal, _ = normalise(instream[m].astype(F32))
        normed[m] = (normal * gains[0:1, :] + shifts[0:1, :]).astype(BF16)
        low = normed[m]
        queries = dot(low, qkv_w[:, 0:width]) + qv_b[0:1, :]
        proj[m, :, 0:width] = (queries * (ROW // 2) ** -0.5).astype(BF16)
        proj[m, :, width : 2 * width] = dot(low, qkv_w[:, width : 2 * width]).astype(BF16)
        proj[m, :, 2 * width : 3 * width] = (
            dot(low, qkv_w[:, 2 * width : 3 * width]) + qv_b[1:2, :]
        ).astype(BF16)
        masks, scores = [], []
        for r in range(GROUP):
            rows = slice(r * ROW, (r + 1) * ROW)
            kinds = lax.broadcasted_iota(jnp.int32, (16, ROW), 0).astype(F32)
            member = jnp.where(ids[1, pl.ds(m * GROUP + r, 1), :] == kinds, 1.0, 0.0).astype(BF16)
            mask = jnp.where(dot_tn(member, member) * frames[...] > 0.5, 0.0, MASKED)
            masks.append(jnp.concatenate([mask, mask], axis=1))
            for p in range(pairs):
                q = stack_pair(proj[m, rows, p * ROW : (p + 1) * ROW], lane_low)
                k = proj[m, rows, width + p * ROW : width + (p + 1) * ROW]
                scores.append(dot_nt(k, q))

        def mix(unit):
            r, p = unit // pairs, unit % pairs
            rows = slice(r * ROW, (r + 1) * ROW)
            v = proj[m, rows, 2 * width + p * ROW : 2 * width + (p + 1) * ROW]
            both = dot_tn(probs[m, unit], v)
            mixed[m, rows, p * ROW : (p + 1) * ROW] = join_pair(both, lane_low).astype(BF16)

        for unit in range(GROUP * pairs):
            masked = scores[unit] + masks[unit // pairs]
            expo = jnp.exp(masked - jnp.max(masked, axis=0, keepdims=True))
            total = jnp.sum(expo, axis=0, keepdims=True)
            probs[m, unit] = (expo * (1.0 / total)).astype(BF16)
            if unit:
                mix(unit - 1)
        mix(GROUP * pairs - 1)
        mid = instream[m].astype(F32) + (dot(mixed[m], out_w[...]) + out_b[0:1, :])
        middle[m] = mid
        normal2, _ = normalise(mid)
        normed2[m] = (normal2 * gains[1:2, :] + shifts[1:2, :]).astype(BF16)
        low2 = normed2[m]
        parts = hidden_n // chunk

        def spread(c):
            return dot(low2, in_w[:, c * chunk : (c + 1) * chunk])

        total, ahead = None, spread(0)
        for c in range(parts):
            cols = slice(c * chunk, (c + 1) * chunk)
            hid = ahead + in_b[0:1, cols]
            if c + 1 < parts:
                ahead = spread(c + 1)
            square = hid * hid
            tan = jnp.tanh(hid * (GELU_A + (GELU_A * GELU_B) * square))
            half = 0.5 + 0.5 * tan
            act = (hid * half).astype(BF16)
            active[m, :, cols] = act
            rise = (1.0 - tan * tan) * (0.5 * GELU_A + (1.5 * GELU_A * GELU_B) * square)
            slope[m, :, cols] = (half + hid * rise).astype(BF16)
            term = dot(act, down_w[cols, :])
            total = term if total is None else total + term
        for copy in saves_forward(m):
            copy.start()
        lo[...] = middle[m] + (total + out_b[1:2, :])

        @pl.when(jnp.logical_not(is_last))
        def _():
            outb[m] = lo[...].astype(BF16)
            forward_copy(m).start()

    def head(m):
        normal, scale = normalise(lo[...])
        outb[m] = (normal * fin_gain[...] + fin_bias[...]).astype(BF16)
        save(9, outb.at[m], xr_o, m).start()
        logits = dot_nt(outb[m], head_w[...])
        top = jnp.max(logits, axis=-1, keepdims=True)
        expo = jnp.exp(logits - top)
        total = jnp.sum(expo, axis=-1, keepdims=True)
        target, hot = hot_rows(2, m)
        grad_logits = jnp.where(target >= 0.0, expo * (1.0 / total) - hot, 0.0).astype(BF16)
        put_xl(m, grad_logits)
        grad_final = dot(grad_logits, head_w[...])
        vec[V_FINAL_GAIN : V_FINAL_GAIN + 1, :] += column_sum(grad_final * normal)
        vec[V_FINAL_BIAS : V_FINAL_BIAS + 1, :] += column_sum(grad_final)
        go[...] = norm_backward(grad_final, normal, scale, fin_gain[...])

    def backward(m):
        slot = lax.rem(m, 2)

        @pl.when(m >= 2)
        def _():
            for copy in saves_backward(m - 2):
                copy.wait()

        @pl.when(jnp.logical_not(is_last))
        def _():
            backward_copy(m).wait_recv()
            go[...] = gin[m].astype(F32)

        s_gres[slot] = go[...].astype(BF16)
        gres = s_gres[slot]
        parts = hidden_n // chunk

        def spread(c):
            return dot_nt(gres, down_w[c * chunk : (c + 1) * chunk, :])

        total, ahead = None, spread(0)
        for c in range(parts):
            cols = slice(c * chunk, (c + 1) * chunk)
            gact = ahead
            if c + 1 < parts:
                ahead = spread(c + 1)
            ghid = (gact * slope[m, :, cols].astype(F32)).astype(BF16)
            s_ghid[slot, :, cols] = ghid
            term = dot_nt(ghid, in_w[:, cols])
            total = term if total is None else total + term
        normal2, scale2 = normalise(middle[m])
        vec[V_GAIN2 : V_GAIN2 + 1, :] += column_sum(total * normal2)
        vec[V_SHIFT2 : V_SHIFT2 + 1, :] += column_sum(total)
        gmid[...] = go[...] + norm_backward(total, normal2, scale2, gains[1:2, :])
        s_gbr[slot] = gmid[...].astype(BF16)
        gbr = s_gbr[slot]
        gmix = dot_nt(gbr, out_w[...]).astype(BF16)
        grads = []
        for r in range(GROUP):
            rows = slice(r * ROW, (r + 1) * ROW)
            for p in range(pairs):
                gm = stack_pair(gmix[rows, p * ROW : (p + 1) * ROW], lane_low)
                vlanes = slice(2 * width + p * ROW, 2 * width + (p + 1) * ROW)
                grads.append(dot_nt(proj[m, rows, vlanes], gm))
                s_gproj[slot, rows, vlanes] = dot(probs[m, r * pairs + p], gm).astype(BF16)

        def pull(unit, gsc):
            r, p = unit // pairs, unit % pairs
            rows = slice(r * ROW, (r + 1) * ROW)
            lanes = slice(p * ROW, (p + 1) * ROW)
            klanes = slice(width + p * ROW, width + (p + 1) * ROW)
            q = stack_pair(proj[m, rows, lanes], lane_low)
            s_gproj[slot, rows, klanes] = dot(gsc, q).astype(BF16)
            gq = join_pair(dot_tn(gsc, proj[m, rows, klanes]), lane_low) * (ROW // 2) ** -0.5
            s_gproj[slot, rows, lanes] = gq.astype(BF16)

        waiting = None
        for unit in range(GROUP * pairs):
            weights = probs[m, unit].astype(F32)
            inner = jnp.sum(weights * grads[unit], axis=0, keepdims=True)
            gsc = (weights * (grads[unit] - inner)).astype(BF16)
            if waiting is not None:
                pull(unit - 1, waiting)
            waiting = gsc
        pull(GROUP * pairs - 1, waiting)
        for copy in saves_backward(m):
            copy.start()
        gproj = s_gproj[slot]
        gnormed = dot_nt(gproj, qkv_w[...])
        normal, scale = normalise(instream[m].astype(F32))
        vec[V_GAIN1 : V_GAIN1 + 1, :] += column_sum(gnormed * normal)
        vec[V_SHIFT1 : V_SHIFT1 + 1, :] += column_sum(gnormed)
        gs[m] = (gmid[...] + norm_backward(gnormed, normal, scale, gains[0:1, :])).astype(BF16)

        @pl.when(is_first)
        def _():
            save(9, gs.at[m], xr_o, m).start()

        @pl.when(jnp.logical_not(is_first))
        def _():
            backward_copy(m).start()

    def tick(t, carry):
        m_forward = t - stage
        m_backward = t - (2 * (stages - 1) - stage)

        @pl.when((m_forward >= 0) & (m_forward < micros))
        def _():
            forward(m_forward)

        @pl.when((m_backward >= 0) & (m_backward < micros))
        def _():
            @pl.when(is_last)
            def _():
                head(m_backward)

            backward(m_backward)

        return carry

    lax.fori_loop(0, micros + 2 * (stages - 1), tick, 0)

    for m in range(micros):
        for copy in saves_forward(m):
            copy.wait()

        @pl.when(jnp.logical_not(is_last))
        def _():
            forward_copy(m).wait_send()

        @pl.when(jnp.logical_not(is_first))
        def _():
            backward_copy(m).wait_send()

        @pl.when(is_first)
        def _():
            save(9, gs.at[m], xr_o, m).wait()

        @pl.when(is_last)
        def _():
            save(9, outb.at[m], xr_o, m).wait()

    for m in range(max(0, micros - 2), micros):
        for copy in saves_backward(m):
            copy.wait()

        @pl.when(is_last)
        def _():
            save_xl(m).wait()


def run_pipeline(stages, token_ids, segment_ids, target_ids, params):
    embed, in_w, head_w = params[0], params[5], params[12]
    width = embed.shape[1]
    vocab = head_w.shape[0]
    hid = in_w.shape[1]
    tokens = GROUP * ROW
    micros = token_ids.shape[0] // GROUP
    pairs = width // ROW
    vmem = pl.BlockSpec(memory_space=pltpu.VMEM)
    hbm = pl.BlockSpec(memory_space=pl.ANY)

    def kept(columns):
        return jax.ShapeDtypeStruct((micros, tokens, columns), BF16)

    def scratch(lead, columns, kind=BF16):
        return pltpu.VMEM((lead, tokens, columns), kind)

    out_shape = [
        kept(width),
        kept(width),
        kept(width),
        kept(hid),
        kept(width),
        kept(hid),
        kept(width),
        kept(3 * width),
        kept(vocab),
        kept(width),
        jax.ShapeDtypeStruct((VEC_ROWS, width), F32),
    ]
    return pl.pallas_call(
        functools.partial(pipeline_kernel, stages, micros),
        out_shape=out_shape,
        in_specs=[vmem] * 16,
        out_specs=[hbm] * 10 + [vmem],
        scratch_shapes=[
            scratch(micros, width),
            scratch(micros, width),
            scratch(micros, width),
            scratch(micros, width),
            scratch(micros, width),
            scratch(micros, 3 * width),
            pltpu.VMEM((micros, GROUP * pairs, ROW, 2 * ROW), BF16),
            scratch(micros, width),
            scratch(micros, width, F32),
            scratch(micros, width),
            scratch(micros, hid),
            scratch(micros, hid),
            pltpu.VMEM((tokens, width), F32),
            pltpu.VMEM((tokens, width), F32),
            pltpu.VMEM((tokens, width), F32),
            scratch(2, width),
            scratch(2, hid),
            scratch(2, width),
            scratch(2, 3 * width),
            scratch(2, vocab),
            pltpu.VMEM((3, 16, ROW), F32),
            pltpu.VMEM((ROW, ROW), F32),
            pltpu.SemaphoreType.DMA((micros,)),
            pltpu.SemaphoreType.DMA((micros,)),
            pltpu.SemaphoreType.DMA((micros,)),
            pltpu.SemaphoreType.DMA((micros,)),
            pltpu.SemaphoreType.DMA((10, micros)),
        ],
        compiler_params=pltpu.CompilerParams(
            collective_id=0, has_side_effects=True, vmem_limit_bytes=62 * 1024 * 1024
        ),
        name="pipeline",
    )(token_ids, segment_ids, target_ids, *params)


def line_dims(devices):
    dims, stride = [], 1
    if devices == 8:
        return [(2, 1), (4, 2)]
    while devices > 1:
        size = 4 if devices % 4 == 0 else 2
        dims.append((size, stride))
        stride *= size
        devices //= size
    return dims


def chunk_plan(width, hid, vocab, stages, devices):
    slim, deep = width // devices, hid // devices
    plan = [("out", 0, (slim, width), False)]
    for c in range(4):
        plan.append(("down", c, (deep, width // 4), c in (1, 3)))
    for c in range(2):
        plan.append(("extra", c, (stages, vocab // (stages * devices), width // 2), False))
    for c in range(hid // width):
        plan.append(("in", c, (slim, width), c == 1))
    for c in range(3):
        plan.append(("qkv", c, (slim, width), False))
    return plan


def gradient_kernel(stages, devices, plan, *refs):
    dims = line_dims(devices)
    refs = list(refs)

    def take(amount):
        head, refs[:] = refs[:amount], refs[amount:]
        return head

    inputs = take(10)
    vec_in, token_ids = take(2)
    qkv_out, out_out, in_out, down_out, embed_out, head_out, vec_out = take(7)
    local = take(10)
    in_sem = take(1)[0]
    turned_left, turned_xl = take(2)
    mats = dict(
        zip(
            ("normed", "mixed", "normed2", "active", "gres", "ghid", "gbr", "gproj", "xl", "xr"),
            local,
        )
    )
    names = list(mats)
    stage = lax.axis_index("pipe")
    place = lax.axis_index("dp")
    is_extra = (stage == 0) | (stage == stages - 1)
    width = mats["normed"].shape[1]
    where = [lax.rem(place // stride, size) for size, stride in dims]

    barrier = pltpu.get_barrier_semaphore()

    def greet(offset, carry):
        peer = lax.rem(place + offset, devices)
        pl.semaphore_signal(barrier, inc=1, device_id={"dp": peer}, device_id_type=MESH)
        return carry

    def greet_stage(offset, carry):
        peer = lax.rem(stage + offset, stages)
        pl.semaphore_signal(barrier, inc=1, device_id={"pipe": peer}, device_id_type=MESH)
        return carry

    lax.fori_loop(1, devices, greet, 0)
    lax.fori_loop(1, stages, greet_stage, 0)

    def load(name):
        i = names.index(name)
        return pltpu.make_async_copy(inputs[i], mats[name], in_sem.at[i])

    groups = [("mixed", "gbr"), ("gres", "active"), ("xr", "xl"), ("normed2", "ghid"), ("normed", "gproj")]

    def fetch(at):
        if at >= len(groups):
            return
        if groups[at] == ("xr", "xl"):
            @pl.when(is_extra)
            def _():
                load("xr").start()

            @pl.when(stage == stages - 1)
            def _():
                load("xl").start()

            at += 1
        for name in groups[at]:
            load(name).start()

    fetch(0)
    loaded = set()

    def need(*wanted):
        fresh = [name for name in wanted if name not in loaded]
        for name in fresh:
            loaded.add(name)
            load(name).wait()
        if fresh:
            at = [i for i, group in enumerate(groups) if group[0] == fresh[0]][0]
            fetch(at + 1)

    def identity(size):
        here = lax.broadcasted_iota(jnp.int32, (size, size), 0)
        there = lax.broadcasted_iota(jnp.int32, (size, size), 1)
        return jnp.where(here == there, 1.0, 0.0).astype(BF16)

    held = []

    def turn(name):
        if held[-1:] == [name]:
            return
        held.append(name)
        unit = identity(256)
        for q in range(width // 256):
            part = dot_nt(unit, mats[name][:, q * 256 : (q + 1) * 256])
            turned_left[q * 256 : (q + 1) * 256, :] = part.astype(BF16)

    bits = devices.bit_length() - 1
    vec_send, vec_recv = take(2)
    vec_sems = take(2)

    def vec_copy(k):
        peer = jnp.bitwise_xor(place, 1 << k)
        return pltpu.make_async_remote_copy(
            src_ref=vec_send.at[k],
            dst_ref=vec_recv.at[k],
            send_sem=vec_sems[0].at[k],
            recv_sem=vec_sems[1].at[k],
            device_id={"dp": peer},
            device_id_type=MESH,
        )

    def vec_step(k):
        def run():
            if k == 0:
                vec_send[0] = vec_in[...]
                ones = jnp.ones((16, mats["gres"].shape[0]), BF16)
                for name, start, row in (
                    ("gproj", 0, V_QUERY),
                    ("gproj", 2 * width, V_VALUE),
                    ("gbr", 0, V_BRANCH),
                    ("gres", 0, V_RESULT),
                ):
                    part = dot(ones, mats[name][:, start : start + width])
                    vec_send[0, row : row + 1, :] = part[0:1, :]
                for q in range(mats["ghid"].shape[1] // width):
                    part = dot(ones, mats["ghid"][:, q * width : (q + 1) * width])
                    vec_send[0, V_HIDDEN + q : V_HIDDEN + q + 1, :] = part[0:1, :]
            else:
                vec_copy(k - 1).wait_recv()
                vec_send[k] = vec_send[k - 1] + vec_recv[k - 1]
            if k < bits:
                vec_copy(k).start()

        return run

    final_send, final_recv = take(2)
    final_sems = take(2)

    def final_copy(offset):
        peer = lax.rem(stages - 1 + offset, stages)
        return pltpu.make_async_remote_copy(
            src_ref=final_send,
            dst_ref=final_recv,
            send_sem=final_sems[0].at[offset],
            recv_sem=final_sems[1].at[0],
            device_id={"pipe": peer},
            device_id_type=MESH,
        )

    def vec_last():
        vec_step(bits)()
        vec_out[...] = vec_send[bits]

        @pl.when(stage == stages - 1)
        def _():
            final_send[...] = vec_send[bits, 8:16, :]
            for offset in range(1, stages):
                final_copy(offset).start()

    def vec_finish():
        @pl.when(stage != stages - 1)
        def _():
            final_copy(1).wait_recv()
            vec_out[V_FINAL_GAIN : V_FINAL_BIAS + 1, :] = final_recv[
                V_FINAL_GAIN - 8 : V_FINAL_BIAS - 7, :
            ]

    def vec_drain():
        for k in range(bits):
            vec_copy(k).wait_send()

        @pl.when(stage == stages - 1)
        def _():
            for offset in range(1, stages):
                final_copy(offset).wait_send()

    extra_sum, extra_send_sem, extra_recv_sem = take(3)

    def extra_copy(source, offset, target):
        peer = lax.rem(source + offset, stages)
        return pltpu.make_async_remote_copy(
            src_ref=extra_sum.at[peer],
            dst_ref=target,
            send_sem=extra_send_sem.at[offset],
            recv_sem=extra_recv_sem.at[0 if source == 0 else 1],
            device_id={"pipe": peer},
            device_id_type=MESH,
        )

    down_full = {}

    def chunk_steps(kind, c, block, turned):
        order = list(range(len(dims)))
        if turned:
            order.reverse()
        full = take(1)[0]

        def compute():
            if kind == "down":
                need("gres", "active")
                turn("gres")
                if c % 2 == 1:
                    return
                half = width // 2
                lines = slice((c // 2) * half, (c // 2 + 1) * half)
                parts = dot(turned_left[lines, :], mats["active"][...]).astype(BF16)
                depth = block[0]
                unit = identity(depth)
                for d in range(devices):
                    back = dot_nt(unit, parts[:, d * depth : (d + 1) * depth]).astype(BF16)
                    down_full[c][split(d)] = back[:, 0 : half // 2]
                    down_full[c + 1][split(d)] = back[:, half // 2 : half]
            elif kind == "extra":
                vocab = turned_xl.shape[0]
                if c == 0:
                    load("xr").wait()

                @pl.when((stage == 0) & (c == 0))
                def _():
                    rows_n, seq = token_ids.shape
                    places = lax.broadcasted_iota(jnp.int32, (vocab, ROW), 0)
                    gap = jnp.full((1, ROW - seq), -1, jnp.int32)
                    for r in range(rows_n):
                        row = jnp.concatenate([token_ids[r : r + 1, :], gap], axis=1)
                        hot = jnp.where(places == row, 1.0, 0.0)
                        turned_xl[:, r * ROW : (r + 1) * ROW] = hot.astype(BF16)

                @pl.when((stage == stages - 1) & (c == 0))
                def _():
                    load("xl").wait()
                    unit = identity(256)
                    for q in range(vocab // 256):
                        part = dot_nt(unit, mats["xl"][:, q * 256 : (q + 1) * 256])
                        turned_xl[q * 256 : (q + 1) * 256, :] = part.astype(BF16)

                rows = vocab // stages
                for p in range(stages):
                    part = dot(
                        turned_xl[p * rows : (p + 1) * rows, :],
                        mats["xr"][:, c * (width // 2) : (c + 1) * (width // 2)],
                    )
                    part = part.astype(BF16).reshape((devices,) + block[1:])
                    for d in range(devices):
                        full[split(d) + (p,)] = part[d]
            else:
                left, right = {
                    "in": ("normed2", "ghid"),
                    "out": ("mixed", "gbr"),
                    "qkv": ("normed", "gproj"),
                }[kind]
                need(left, right)
                turn(left)
                cols = slice(c * width, (c + 1) * width)
                part = dot(turned_left[...], mats[right][:, cols]).astype(BF16)
                part = part.reshape((devices,) + block)
                for d in range(devices):
                    full[split(d)] = part[d]

        def split(d):
            return tuple((d // stride) % size for size, stride in reversed(dims))

        if kind == "down":
            down_full[c] = full
        steps = [[compute]]
        for at, phase in enumerate(order):
            size = dims[phase][0]
            buffers = take(3)
            done = order[:at]
            last = at == len(order) - 1
            steps[-1].append(functools.partial(line_step, phase, size, 1, full, buffers, done))
            for t in range(2, size):
                steps.append([functools.partial(line_step, phase, size, t, full, buffers, done)])
            drains.append((kind, functools.partial(line_drain, phase, size, full, buffers, done)))
            steps.append([functools.partial(line_final, kind, c, phase, size, full, buffers, done, last)])
        if kind == "extra":
            steps = [[gated([part]) for part in step] for step in steps]
        return steps

    def gated(step):
        def run():
            @pl.when(is_extra)
            def _():
                for part in step:
                    part()

        return run

    def block_of(full, phase, j, done):
        spot = [slice(None)] * len(dims)
        for other in done:
            spot[len(dims) - 1 - other] = where[other]
        spot[len(dims) - 1 - phase] = j
        return full.at[tuple(spot)]

    def line_copy(phase, size, t, side, full, buffers, done):
        recv, ssem, rsem = buffers
        i = where[phase]
        stride = dims[phase][1]
        if side == 0:
            j, peer = size - t + i, place + jnp.where(i < size - 1, stride, 0)
        else:
            j, peer = t - size + i, place - jnp.where(i > 0, stride, 0)
        return pltpu.make_async_remote_copy(
            src_ref=block_of(full, phase, jnp.clip(j, 0, size - 1), done),
            dst_ref=recv.at[0 if size == 2 else side, t - 1],
            send_sem=ssem.at[side, t - 1],
            recv_sem=rsem.at[side, t - 1],
            device_id={"dp": peer},
            device_id_type=MESH,
        )

    def sends(i, size, t, side):
        return (i <= t - 1) if side == 0 else (i >= size - t)

    def line_step(phase, size, t, full, buffers, done):
        i = where[phase]
        for side in range(2):
            at_end = (i == 0) if side == 0 else (i == size - 1)
            j = size - t + i if side == 0 else t - size + i
            j = jnp.clip(j, 0, size - 1)

            @pl.when(sends(i, size, t, side))
            def _():
                if t > 1:
                    @pl.when(jnp.logical_not(at_end))
                    def _():
                        line_copy(phase, size, t - 1, side, full, buffers, done).wait_recv()
                        own = block_of(full, phase, j, done)
                        got = buffers[0][0 if size == 2 else side, t - 2]
                        own[...] = (own[...].astype(F32) + got.astype(F32)).astype(BF16)

                line_copy(phase, size, t, side, full, buffers, done).start()

    def line_final(kind, c, phase, size, full, buffers, done, last):
        i = where[phase]
        own = block_of(full, phase, i, done)
        total = own
        if last:
            slots = {
                "qkv": lambda: qkv_out.at[:, c * width : (c + 1) * width],
                "in": lambda: in_out.at[:, c * width : (c + 1) * width],
                "out": lambda: out_out,
                "down": lambda: down_out.at[:, c * (width // 4) : (c + 1) * (width // 4)],
                "extra": lambda: extra_sum.at[:, :, c * (width // 2) : (c + 1) * (width // 2)],
            }
            total = slots[kind]()
        lower, upper = i > 0, i < size - 1

        def arrived(side):
            line_copy(phase, size, size - 1, side, full, buffers, done).wait_recv()
            return buffers[0][0 if size == 2 else side, size - 2].astype(F32)

        @pl.when(lower & upper)
        def _():
            total[...] = (own[...].astype(F32) + arrived(0) + arrived(1)).astype(total.dtype)

        @pl.when(lower & jnp.logical_not(upper))
        def _():
            total[...] = (own[...].astype(F32) + arrived(0)).astype(total.dtype)

        @pl.when(jnp.logical_not(lower))
        def _():
            total[...] = (own[...].astype(F32) + arrived(1)).astype(total.dtype)

        if last and kind == "extra" and c == 1:
            for source_stage, out in ((0, embed_out), (stages - 1, head_out)):
                @pl.when(stage == source_stage)
                def _():
                    for offset in range(1, stages):
                        extra_copy(source_stage, offset, extra_recv[0 if source_stage == 0 else 1]).start()
                    out[...] = extra_sum[source_stage]

    def line_drain(phase, size, full, buffers, done):
        i = where[phase]
        for side in range(2):
            for t in range(1, size):
                @pl.when(sends(i, size, t, side))
                def _():
                    line_copy(phase, size, t, side, full, buffers, done).wait_send()

    extra_recv = take(2)
    drains = []
    chains = [chunk_steps(*item) for item in plan]
    depth = len(chains[0])
    vec_chain = [vec_step(k) for k in range(bits)] + [vec_last]
    starts, first, extra_rounds = [], 0, iter((1, 3, 6, 8))
    for item in plan:
        if item[3]:
            starts.append(next(extra_rounds))
        else:
            starts.append(first)
            first += 1
    begun = False
    loaded_at = max(start for start, item in zip(starts, plan) if item[0] == "qkv" and item[1] == 0)
    for r in range(max(starts) + depth):
        for d in [0] + list(range(depth - 1, 0, -1)):
            for start, chain in zip(starts, chains):
                if r - start != d:
                    continue
                for part in chain[d]:
                    part()
                    if not begun:
                        begun = True
                        pl.semaphore_wait(barrier, devices - 1 + stages - 1)
        if 0 <= r - loaded_at < len(vec_chain):
            vec_chain[r - loaded_at]()
    vec_finish()
    for source_stage, out in ((0, embed_out), (stages - 1, head_out)):
        @pl.when(stage != source_stage)
        def _():
            got = extra_recv[0 if source_stage == 0 else 1]
            extra_copy(source_stage, 1, got).wait_recv()
            out[...] = got[...]

        @pl.when(stage == source_stage)
        def _():
            for offset in range(1, stages):
                extra_copy(source_stage, offset, extra_recv[0]).wait_send()

    vec_drain()
    for kind, drain in drains:
        if kind == "extra":
            gated([drain])()
        else:
            drain()


def run_gradients(stages, devices, saved, vec, token_ids):
    dims = line_dims(devices)
    rows, tokens, width = saved[0].shape
    hid, vocab = saved[3].shape[2], saved[8].shape[2]
    plan = chunk_plan(width, hid, vocab, stages, devices)
    saved = [member.reshape(rows * tokens, member.shape[2]) for member in saved]
    vmem = pl.BlockSpec(memory_space=pltpu.VMEM)
    hbm = pl.BlockSpec(memory_space=pl.ANY)
    bits = devices.bit_length() - 1
    share = vocab // (stages * devices)
    scratch = [pltpu.VMEM(member.shape, BF16) for member in saved]
    scratch += [pltpu.SemaphoreType.DMA((len(saved),))]
    scratch += [pltpu.VMEM((width, rows * tokens), BF16), pltpu.VMEM((vocab, rows * tokens), BF16)]
    scratch += [
        pltpu.VMEM((bits + 1,) + vec.shape, F32),
        pltpu.VMEM((bits,) + vec.shape, F32),
        pltpu.SemaphoreType.DMA((bits,)),
        pltpu.SemaphoreType.DMA((bits,)),
        pltpu.VMEM((8, width), F32),
        pltpu.VMEM((8, width), F32),
        pltpu.SemaphoreType.DMA((stages,)),
        pltpu.SemaphoreType.DMA((1,)),
        pltpu.VMEM((stages, share, width), F32),
        pltpu.SemaphoreType.DMA((stages,)),
        pltpu.SemaphoreType.DMA((2,)),
        pltpu.VMEM((share, width), F32),
        pltpu.VMEM((share, width), F32),
    ]
    sizes = [size for size, _ in reversed(dims)]
    for _, _, block, turned in plan:
        scratch.append(pltpu.VMEM(tuple(sizes) + block, BF16))
        remain = list(reversed(dims))
        for size, stride in dims[::-1] if turned else dims:
            remain.remove((size, stride))
            piece = tuple(other for other, _ in remain) + block
            scratch.append(pltpu.VMEM((1 if size == 2 else 2, size - 1) + piece, BF16))
            scratch += [pltpu.SemaphoreType.DMA((2, size - 1))] * 2
    return pl.pallas_call(
        functools.partial(gradient_kernel, stages, devices, plan),
        out_shape=[
            jax.ShapeDtypeStruct((width // devices, 3 * width), F32),
            jax.ShapeDtypeStruct((width // devices, width), F32),
            jax.ShapeDtypeStruct((width // devices, hid), F32),
            jax.ShapeDtypeStruct((hid // devices, width), F32),
            jax.ShapeDtypeStruct((share, width), F32),
            jax.ShapeDtypeStruct((share, width), F32),
            jax.ShapeDtypeStruct(vec.shape, F32),
        ],
        in_specs=[hbm] * len(saved) + [vmem] * 2,
        out_specs=[vmem] * 7,
        scratch_shapes=scratch,
        compiler_params=pltpu.CompilerParams(
            collective_id=1, has_side_effects=True, vmem_limit_bytes=62 * 1024 * 1024
        ),
        name="gradients",
    )(*saved, vec, token_ids)


def step_kernel(stages, micros, devices, plan, *refs):
    refs = list(refs)

    def take(amount):
        head, refs[:] = refs[:amount], refs[amount:]
        return head

    token_ids, segment_ids, target_ids = take(3)
    qv_b, out_b, in_b, gains, shifts, fin_gain, fin_bias = take(7)
    embed_h, head_h, qkv_h, out_h, in_h, down_h = take(6)
    qkv_out, out_out, in_out, down_out, embed_out, head_out, vec_out = take(7)
    side, qkv_w, out_w = take(3)
    in_w, down_w = take(4), take(4)
    instream, outb, gin, gs, proj, probs, mixed, middle, active, slope = take(10)
    lo, gmid, s_gbr, s_xl, vec, ids, frames = take(7)
    fsend, frecv, bsend, brecv, wsem = take(5)
    go = lo
    place = lax.axis_index("dp")
    stage = lax.axis_index("pipe")
    tokens, width = instream.shape[1], instream.shape[2]
    hidden_n = in_b.shape[1]
    vocab = side.shape[0]
    pairs = width // ROW
    chunk = 512
    is_first = stage == 0
    is_last = stage == stages - 1
    up = jnp.minimum(stage + 1, stages - 1)
    down = jnp.maximum(stage - 1, 0)

    def bring(index, source, target):
        return pltpu.make_async_copy(source, target, wsem.at[index])

    weights = [bring(1, qkv_h, qkv_w), bring(2, out_h, out_w)]
    for c in range(4):
        lanes = pl.ds(c * chunk, chunk)
        weights.append(bring(3 + c, in_h.at[:, :, :, lanes], in_w[c]))
        weights.append(bring(7 + c, down_h.at[c], down_w[c]))

    @pl.when(is_first)
    def _():
        bring(0, embed_h, side).start()

    for copy in weights:
        copy.start()

    @pl.when(is_last)
    def _():
        bring(0, head_h, side).start()

    barrier = pltpu.get_barrier_semaphore()

    def greet(offset, carry):
        peer = lax.rem(place + offset, devices)
        pl.semaphore_signal(barrier, inc=1, device_id={"dp": peer}, device_id_type=MESH)
        return carry

    def greet_stage(offset, carry):
        peer = lax.rem(stage + offset, stages)
        pl.semaphore_signal(barrier, inc=1, device_id={"pipe": peer}, device_id_type=MESH)
        return carry

    lax.fori_loop(1, devices, greet, 0)
    lax.fori_loop(1, stages, greet_stage, 0)

    def whole(part):
        return part[...].reshape(width, width)

    vec[...] = jnp.zeros_like(vec)
    rows_n, seq = token_ids.shape
    for index, member in enumerate((token_ids, segment_ids, target_ids)):
        ids[index] = jnp.full(ids.shape[1:], 4.0 if index == 1 else -1.0, F32)
        ids[index, 0:rows_n, 0:seq] = member[...].astype(F32)
    at_query = lax.broadcasted_iota(jnp.int32, (ROW, ROW), 1)
    at_key = lax.broadcasted_iota(jnp.int32, (ROW, ROW), 0)
    frames[...] = jnp.where(at_key < ((at_query * 43) // 256) * FRAME + FRAME, 1.0, 0.0)

    def column(index, row):
        values = jnp.broadcast_to(ids[index, pl.ds(row, 1), :], (8, ROW))
        return values.T[:, 0:1]

    def hot_rows(index, m):
        parts = [column(index, m * GROUP + r) for r in range(GROUP)]
        values = jnp.concatenate(parts, axis=0)
        places = lax.broadcasted_iota(jnp.int32, (tokens, vocab), 1).astype(F32)
        return values, jnp.where(values == places, 1.0, 0.0)

    def forward_copy(m):
        return pltpu.make_async_remote_copy(
            src_ref=outb.at[m],
            dst_ref=instream.at[m],
            send_sem=fsend.at[m],
            recv_sem=frecv.at[m],
            device_id={"pipe": up},
            device_id_type=MESH,
        )

    def backward_copy(m):
        return pltpu.make_async_remote_copy(
            src_ref=gs.at[m],
            dst_ref=gin.at[m],
            send_sem=bsend.at[m],
            recv_sem=brecv.at[m],
            device_id={"pipe": down},
            device_id_type=MESH,
        )

    @pl.when(is_first | is_last)
    def _():
        bring(0, embed_h, side).wait()

    for copy in weights:
        copy.wait()
    pl.semaphore_wait(barrier, devices - 1 + stages - 1)

    lane_low = lax.broadcasted_iota(jnp.int32, (ROW, ROW), 1) < ROW // 2

    def forward(m):
        @pl.when(is_first)
        def _():
            hot = hot_rows(0, m)[1].astype(BF16)
            instream[m] = dot(hot, side[...]).astype(BF16)

        @pl.when(jnp.logical_not(is_first))
        def _():
            forward_copy(m).wait_recv()

        normal, _ = normalise(instream[m].astype(F32))
        low = (normal * gains[0:1, :] + shifts[0:1, :]).astype(BF16)
        queries = dot(low, qkv_w[:, 0:width]) + qv_b[0:1, :]
        proj[m, :, 0:width] = (queries * (ROW // 2) ** -0.5).astype(BF16)
        proj[m, :, width : 2 * width] = dot(low, qkv_w[:, width : 2 * width]).astype(BF16)
        proj[m, :, 2 * width : 3 * width] = (
            dot(low, qkv_w[:, 2 * width : 3 * width]) + qv_b[1:2, :]
        ).astype(BF16)
        masks, scores = [], []
        for r in range(GROUP):
            rows = slice(r * ROW, (r + 1) * ROW)
            kinds = lax.broadcasted_iota(jnp.int32, (16, ROW), 0).astype(F32)
            member = jnp.where(ids[1, pl.ds(m * GROUP + r, 1), :] == kinds, 1.0, 0.0).astype(BF16)
            mask = jnp.where(dot_tn(member, member) * frames[...] > 0.5, 0.0, MASKED)
            masks.append(jnp.concatenate([mask, mask], axis=1))
            for p in range(pairs):
                q = stack_pair(proj[m, rows, p * ROW : (p + 1) * ROW], lane_low)
                k = proj[m, rows, width + p * ROW : width + (p + 1) * ROW]
                scores.append(dot_nt(k, q))

        def mix(unit):
            r, p = unit // pairs, unit % pairs
            rows = slice(r * ROW, (r + 1) * ROW)
            v = proj[m, rows, 2 * width + p * ROW : 2 * width + (p + 1) * ROW]
            both = dot_tn(probs[m, unit // 2, unit % 2], v)
            mixed[m, rows, p * ROW : (p + 1) * ROW] = join_pair(both, lane_low).astype(BF16)

        for unit in range(GROUP * pairs):
            masked = scores[unit] + masks[unit // pairs]
            expo = jnp.exp(masked - jnp.max(masked, axis=0, keepdims=True))
            total = jnp.sum(expo, axis=0, keepdims=True)
            probs[m, unit // 2, unit % 2] = (expo * (1.0 / total)).astype(BF16)
            if unit:
                mix(unit - 1)
        mix(GROUP * pairs - 1)
        mid = instream[m].astype(F32) + (dot(mixed[m], out_w[...]) + out_b[0:1, :])
        middle[m] = mid
        normal2, _ = normalise(mid)
        low2 = (normal2 * gains[1:2, :] + shifts[1:2, :]).astype(BF16)
        parts = hidden_n // chunk

        def spread(c):
            return dot(low2, whole(in_w[c]))

        total, ahead = None, spread(0)
        for c in range(parts):
            cols = slice(c * chunk, (c + 1) * chunk)
            hid = ahead + in_b[0:1, cols]
            if c + 1 < parts:
                ahead = spread(c + 1)
            square = hid * hid
            tan = jnp.tanh(hid * (GELU_A + (GELU_A * GELU_B) * square))
            half = 0.5 + 0.5 * tan
            act = (hid * half).astype(BF16)
            active[m, :, cols] = act
            rise = (1.0 - tan * tan) * (0.5 * GELU_A + (1.5 * GELU_A * GELU_B) * square)
            slope[m, :, cols] = (half + hid * rise).astype(BF16)
            term = dot(act, whole(down_w[c]))
            total = term if total is None else total + term
        lo[...] = middle[m] + (total + out_b[1:2, :])

        @pl.when(jnp.logical_not(is_last))
        def _():
            outb[m] = lo[...].astype(BF16)
            forward_copy(m).start()

    def head(m):
        normal, scale = normalise(lo[...])
        outb[m] = (normal * fin_gain[...] + fin_bias[...]).astype(BF16)
        logits = dot_nt(outb[m], side[...])
        top = jnp.max(logits, axis=-1, keepdims=True)
        expo = jnp.exp(logits - top)
        total = jnp.sum(expo, axis=-1, keepdims=True)
        target, hot = hot_rows(2, m)
        grad_logits = jnp.where(target >= 0.0, expo * (1.0 / total) - hot, 0.0).astype(BF16)
        s_xl[m] = grad_logits
        grad_final = dot(grad_logits, side[...])
        vec[V_FINAL_GAIN : V_FINAL_GAIN + 1, :] += column_sum(grad_final * normal)
        vec[V_FINAL_BIAS : V_FINAL_BIAS + 1, :] += column_sum(grad_final)
        go[...] = norm_backward(grad_final, normal, scale, fin_gain[...])

    def backward(m):
        @pl.when(jnp.logical_not(is_last))
        def _():
            backward_copy(m).wait_recv()
            go[...] = gin[m].astype(F32)

        gres = go[...].astype(BF16)
        gin[m] = gres
        parts = hidden_n // chunk

        def spread(c):
            return dot_nt(gres, whole(down_w[c]))

        total, ahead = None, spread(0)
        for c in range(parts):
            cols = slice(c * chunk, (c + 1) * chunk)
            gact = ahead
            if c + 1 < parts:
                ahead = spread(c + 1)
            ghid = (gact * slope[m, :, cols].astype(F32)).astype(BF16)
            slope[m, :, cols] = ghid
            term = dot_nt(ghid, whole(in_w[c]))
            total = term if total is None else total + term
        normal2, scale2 = normalise(middle[m])
        vec[V_GAIN2 : V_GAIN2 + 1, :] += column_sum(total * normal2)
        vec[V_SHIFT2 : V_SHIFT2 + 1, :] += column_sum(total)
        gmid[...] = go[...] + norm_backward(total, normal2, scale2, gains[1:2, :])
        gbr = gmid[...].astype(BF16)
        s_gbr[m] = gbr
        gmix = dot_nt(gbr, out_w[...]).astype(BF16)
        grads = []
        for r in range(GROUP):
            rows = slice(r * ROW, (r + 1) * ROW)
            for p in range(pairs):
                gm = stack_pair(gmix[rows, p * ROW : (p + 1) * ROW], lane_low)
                vlanes = slice(2 * width + p * ROW, 2 * width + (p + 1) * ROW)
                grads.append(dot_nt(proj[m, rows, vlanes], gm))
                unit = r * pairs + p
                proj[m, rows, vlanes] = dot(probs[m, unit // 2, unit % 2], gm).astype(BF16)

        def pull(unit, gsc):
            r, p = unit // pairs, unit % pairs
            rows = slice(r * ROW, (r + 1) * ROW)
            lanes = slice(p * ROW, (p + 1) * ROW)
            klanes = slice(width + p * ROW, width + (p + 1) * ROW)
            q = stack_pair(proj[m, rows, lanes], lane_low)
            gq = join_pair(dot_tn(gsc, proj[m, rows, klanes]), lane_low) * (ROW // 2) ** -0.5
            gk = dot(gsc, q)
            proj[m, rows, klanes] = gk.astype(BF16)
            proj[m, rows, lanes] = gq.astype(BF16)

        waiting = None
        for unit in range(GROUP * pairs):
            weights = probs[m, unit // 2, unit % 2].astype(F32)
            inner = jnp.sum(weights * grads[unit], axis=0, keepdims=True)
            gsc = (weights * (grads[unit] - inner)).astype(BF16)
            if waiting is not None:
                pull(unit - 1, waiting)
            waiting = gsc
        pull(GROUP * pairs - 1, waiting)
        gproj = proj[m]
        gnormed = dot_nt(gproj, qkv_w[...])
        normal, scale = normalise(instream[m].astype(F32))
        vec[V_GAIN1 : V_GAIN1 + 1, :] += column_sum(gnormed * normal)
        vec[V_SHIFT1 : V_SHIFT1 + 1, :] += column_sum(gnormed)
        gs[m] = (gmid[...] + norm_backward(gnormed, normal, scale, gains[0:1, :])).astype(BF16)

        @pl.when(jnp.logical_not(is_first))
        def _():
            backward_copy(m).start()

    def tick(t, carry):
        m_forward = t - stage
        m_backward = t - (2 * (stages - 1) - stage)

        @pl.when((m_forward >= 0) & (m_forward < micros))
        def _():
            forward(m_forward)

        @pl.when((m_backward >= 0) & (m_backward < micros))
        def _():
            @pl.when(is_last)
            def _():
                head(m_backward)

            backward(m_backward)

        return carry

    lax.fori_loop(0, micros + 2 * (stages - 1), tick, 0)

    embed_stage = stages - 2
    is_extra = (stage == embed_stage) | is_last
    dims = line_dims(devices)
    turned_left = qkv_w
    mats = {
        "mixed": mixed,
        "active": active,
        "gres": gin,
        "ghid": slope,
        "gbr": s_gbr,
        "gproj": proj,
    }

    def mat(name, lanes=slice(None)):
        value = mats[name][:, :, lanes]
        return value.reshape(micros * tokens, value.shape[2])

    where = [lax.rem(place // stride, size) for size, stride in dims]

    def identity(size):
        here = lax.broadcasted_iota(jnp.int32, (size, size), 0)
        there = lax.broadcasted_iota(jnp.int32, (size, size), 1)
        return jnp.where(here == there, 1.0, 0.0).astype(BF16)

    held = []

    def turn(name):
        if held[-1:] == [name]:
            return
        held.append(name)
        unit = identity(256)
        if name in ("normed", "normed2"):
            row = 0 if name == "normed" else 1
            source = instream if name == "normed" else middle
            for m in range(micros):
                normal, _ = normalise(source[m].astype(F32))
                again = (normal * gains[row : row + 1, :] + shifts[row : row + 1, :]).astype(BF16)
                for q in range(width // 256):
                    part = dot_nt(unit, again[:, q * 256 : (q + 1) * 256])
                    turned_left[q * 256 : (q + 1) * 256, m * tokens : (m + 1) * tokens] = part.astype(BF16)
            return
        for q in range(width // 256):
            part = dot_nt(unit, mat(name, slice(q * 256, (q + 1) * 256)))
            turned_left[q * 256 : (q + 1) * 256, :] = part.astype(BF16)

    bits = devices.bit_length() - 1
    vec_send, vec_recv = take(2)
    vec_sems = take(2)

    def vec_copy(k):
        peer = jnp.bitwise_xor(place, 1 << k)
        return pltpu.make_async_remote_copy(
            src_ref=vec_send.at[k],
            dst_ref=vec_recv.at[k],
            send_sem=vec_sems[0].at[k],
            recv_sem=vec_sems[1].at[k],
            device_id={"dp": peer},
            device_id_type=MESH,
        )

    def vec_step(k):
        def run():
            if k == 0:
                vec_send[0] = vec[...]
                ones = jnp.ones((16, micros * tokens), BF16)
                for name, start, row in (
                    ("gproj", 0, V_QUERY),
                    ("gproj", 2 * width, V_VALUE),
                    ("gbr", 0, V_BRANCH),
                    ("gres", 0, V_RESULT),
                ):
                    part = dot(ones, mat(name, slice(start, start + width)))
                    vec_send[0, row : row + 1, :] = part[0:1, :]
                for q in range(hidden_n // width):
                    part = dot(ones, mat("ghid", slice(q * width, (q + 1) * width)))
                    vec_send[0, V_HIDDEN + q : V_HIDDEN + q + 1, :] = part[0:1, :]
            else:
                vec_copy(k - 1).wait_recv()
                vec_send[k] = vec_send[k - 1] + vec_recv[k - 1]
            if k < bits:
                vec_copy(k).start()

        return run

    final_send, final_recv = take(2)
    final_sems = take(2)

    def final_copy(offset):
        peer = lax.rem(stages - 1 + offset, stages)
        return pltpu.make_async_remote_copy(
            src_ref=final_send,
            dst_ref=final_recv,
            send_sem=final_sems[0].at[offset],
            recv_sem=final_sems[1].at[0],
            device_id={"pipe": peer},
            device_id_type=MESH,
        )

    def vec_last():
        vec_step(bits)()
        vec_out[...] = vec_send[bits]

        @pl.when(stage == stages - 1)
        def _():
            final_send[...] = vec_send[bits, 8:16, :]
            for offset in range(1, stages):
                final_copy(offset).start()

    def vec_finish():
        @pl.when(stage != stages - 1)
        def _():
            final_copy(1).wait_recv()
            vec_out[V_FINAL_GAIN : V_FINAL_BIAS + 1, :] = final_recv[
                V_FINAL_GAIN - 8 : V_FINAL_BIAS - 7, :
            ]

    def vec_drain():
        for k in range(bits):
            vec_copy(k).wait_send()

        @pl.when(stage == stages - 1)
        def _():
            for offset in range(1, stages):
                final_copy(offset).wait_send()

    def ship():
        return pltpu.make_async_remote_copy(
            src_ref=s_xl.at[pl.ds(0, 2)],
            dst_ref=s_xl.at[pl.ds(0, 2)],
            send_sem=ship_sem.at[0],
            recv_sem=ship_sem.at[1],
            device_id={"pipe": embed_stage},
            device_id_type=MESH,
        )

    def ship_embed():
        rows, half = vocab // stages, width // 2

        @pl.when(is_first)
        def _():
            right = gs[...].reshape(micros * tokens, width)
            for p in range(stages):
                here = lax.broadcasted_iota(jnp.int32, (rows, ROW), 0).astype(F32) + p * rows
                hot = [
                    jnp.where(ids[0, r : r + 1, :] == here, 1.0, 0.0).astype(BF16) for r in range(rows_n)
                ]
                part = dot(jnp.concatenate(hot, axis=1), right).astype(BF16)
                for k in range(2):
                    s_xl[k, :, p * half : (p + 1) * half] = part[:, k * half : (k + 1) * half]
            ship().start()

    extra_sum, extra_send_sem, extra_recv_sem, last_sum, ship_sem = take(5)
    share = embed_out.shape[0]

    def extra_copy(source, offset, target):
        peer = lax.rem(source + offset, stages)
        return pltpu.make_async_remote_copy(
            src_ref=extra_sum.at[pl.ds(pl.multiple_of(peer * share, share), share)],
            dst_ref=target,
            send_sem=extra_send_sem.at[offset],
            recv_sem=extra_recv_sem.at[0 if source == embed_stage else 1],
            device_id={"pipe": peer},
            device_id_type=MESH,
        )

    def chunk_steps(kind, c, block, turned):
        order = list(range(len(dims)))
        if turned:
            order.reverse()
        if kind == "down":
            full = probs.at[c]
        elif kind == "extra":
            full = probs.at[4 + c]
        else:
            full = (down_w + in_w)[{"out": 0, "in": 1, "qkv": 5}[kind] + c]

        def compute():
            if kind == "down":
                if c % 2 == 1:
                    return
                turn("gres")
                half = width // 2
                lines = slice((c // 2) * half, (c // 2 + 1) * half)
                parts = dot(turned_left[lines, :], mat("active")).astype(BF16)
                depth = hidden_n // devices
                unit = identity(depth)
                for d in range(devices):
                    back = dot_nt(unit, parts[:, d * depth : (d + 1) * depth]).astype(BF16)
                    for k in range(2):
                        piece = back[:, k * ROW : (k + 1) * ROW]
                        piece = jnp.concatenate([piece[: depth // 2], piece[depth // 2 :]], axis=1)
                        probs[(c + k,) + split(d)] = piece
            elif kind == "extra":
                if c == 1:
                    return
                rows = vocab // stages
                share = rows // devices
                half = width // 2

                def fill(left, right):
                    for p in range(stages):
                        part = left(p, right).astype(BF16).reshape(devices, share, width)
                        for d in range(devices):
                            for k in range(2):
                                lines = slice(p * share, (p + 1) * share)
                                probs[(4 + k,) + split(d) + (lines,)] = part[
                                    d, :, k * half : (k + 1) * half
                                ]

                def flat(ref):
                    return ref[...].reshape(micros * tokens, ref.shape[2])

                @pl.when(stage == embed_stage)
                def _():
                    ship().wait_recv()
                    for d in range(devices):
                        for k in range(2):
                            for p in range(stages):
                                lines = slice(p * share, (p + 1) * share)
                                probs[(4 + k,) + split(d) + (lines,)] = s_xl[
                                    k, d * share : (d + 1) * share, p * half : (p + 1) * half
                                ]

                @pl.when(is_last)
                def _():
                    def soft_part(p, right):
                        left = s_xl[:, :, p * rows : (p + 1) * rows]
                        return dot_tn(left.reshape(micros * tokens, rows), right)

                    fill(soft_part, flat(outb))
            else:
                left, right = {
                    "in": ("normed2", "ghid"),
                    "out": ("mixed", "gbr"),
                    "qkv": ("normed", "gproj"),
                }[kind]
                turn(left)
                part = dot(turned_left[...], mat(right, slice(c * width, (c + 1) * width)))
                part = part.astype(BF16).reshape((devices,) + block)
                for d in range(devices):
                    full[split(d)] = part[d]

        def split(d):
            return tuple((d // stride) % size for size, stride in reversed(dims))

        steps = [[compute]]
        for at, phase in enumerate(order):
            size = dims[phase][0]
            buffers = take(3)
            done = order[:at]
            last = at == len(order) - 1
            steps[-1].append(functools.partial(line_step, phase, size, 1, full, buffers, done))
            for t in range(2, size):
                steps.append([functools.partial(line_step, phase, size, t, full, buffers, done)])
            drains.append((kind, functools.partial(line_drain, phase, size, full, buffers, done)))
            steps.append([functools.partial(line_final, kind, c, phase, size, full, buffers, done, last)])
        if kind == "extra":
            steps = [[gated([part]) for part in step] for step in steps]
        return steps

    def gated(step):
        def run():
            @pl.when(is_extra)
            def _():
                for part in step:
                    part()

        return run

    def block_of(full, phase, j, done):
        spot = [slice(None)] * len(dims)
        for other in done:
            spot[len(dims) - 1 - other] = where[other]
        spot[len(dims) - 1 - phase] = j
        return full.at[tuple(spot)]

    def line_copy(phase, size, t, side, full, buffers, done):
        recv, ssem, rsem = buffers
        i = where[phase]
        stride = dims[phase][1]
        if side == 0:
            j, peer = size - t + i, place + jnp.where(i < size - 1, stride, 0)
        else:
            j, peer = t - size + i, place - jnp.where(i > 0, stride, 0)
        return pltpu.make_async_remote_copy(
            src_ref=block_of(full, phase, jnp.clip(j, 0, size - 1), done),
            dst_ref=recv.at[0 if size == 2 else side, t - 1],
            send_sem=ssem.at[side, t - 1],
            recv_sem=rsem.at[side, t - 1],
            device_id={"dp": peer},
            device_id_type=MESH,
        )

    def sends(i, size, t, side):
        return (i <= t - 1) if side == 0 else (i >= size - t)

    def line_step(phase, size, t, full, buffers, done):
        i = where[phase]
        for side in range(2):
            at_end = (i == 0) if side == 0 else (i == size - 1)
            j = size - t + i if side == 0 else t - size + i
            j = jnp.clip(j, 0, size - 1)

            @pl.when(sends(i, size, t, side))
            def _():
                if t > 1:
                    @pl.when(jnp.logical_not(at_end))
                    def _():
                        line_copy(phase, size, t - 1, side, full, buffers, done).wait_recv()
                        own = block_of(full, phase, j, done)
                        got = buffers[0][0 if size == 2 else side, t - 2]
                        own[...] = (own[...].astype(F32) + got.astype(F32)).astype(BF16)

                line_copy(phase, size, t, side, full, buffers, done).start()

    def line_final(kind, c, phase, size, full, buffers, done, last):
        i = where[phase]
        own = block_of(full, phase, i, done)
        total = own
        if last:
            lanes = slice(c * width, (c + 1) * width)
            slots = {
                "qkv": lambda: qkv_out.at[:, lanes],
                "in": lambda: in_out.at[:, lanes],
                "out": lambda: out_out,
                "down": lambda: last_sum,
                "extra": lambda: extra_sum.at[:, c * (width // 2) : (c + 1) * (width // 2)],
            }
            total = slots[kind]()
        lower, upper = i > 0, i < size - 1

        def arrived(side):
            line_copy(phase, size, size - 1, side, full, buffers, done).wait_recv()
            return buffers[0][0 if size == 2 else side, size - 2].astype(F32)

        @pl.when(lower & upper)
        def _():
            total[...] = (own[...].astype(F32) + arrived(0) + arrived(1)).astype(total.dtype)

        @pl.when(lower & jnp.logical_not(upper))
        def _():
            total[...] = (own[...].astype(F32) + arrived(0)).astype(total.dtype)

        @pl.when(jnp.logical_not(lower))
        def _():
            total[...] = (own[...].astype(F32) + arrived(1)).astype(total.dtype)

        if last and kind == "down":
            deep = down_out.shape[0] // 2
            lanes = slice(c * ROW, (c + 1) * ROW)
            down_out[0:deep, lanes] = last_sum[:, 0:ROW]
            down_out[deep : 2 * deep, lanes] = last_sum[:, ROW : 2 * ROW]
        if last and kind == "extra" and c == 1:
            for source_stage, out in ((embed_stage, embed_out), (stages - 1, head_out)):
                @pl.when(stage == source_stage)
                def _():
                    for offset in range(1, stages):
                        extra_copy(source_stage, offset, extra_recv[0 if source_stage == embed_stage else 1]).start()
                    out[...] = extra_sum[source_stage * share : (source_stage + 1) * share, :]

    def line_drain(phase, size, full, buffers, done):
        i = where[phase]
        for side in range(2):
            for t in range(1, size):
                @pl.when(sends(i, size, t, side))
                def _():
                    line_copy(phase, size, t, side, full, buffers, done).wait_send()

    extra_recv = take(2)
    drains = []
    chains = [chunk_steps(*item) for item in plan]
    depth = len(chains[0])
    vec_chain = [vec_step(k) for k in range(bits)] + [vec_last]
    starts, first, extra_rounds = [], 0, iter((1, 3, 5, 7))
    for item in plan:
        if item[0] == "extra":
            starts.append(6 + item[1])
        elif item[3]:
            starts.append(next(extra_rounds))
        else:
            starts.append(first)
            first += 1
    loaded_at = max(start for start, item in zip(starts, plan) if item[0] == "qkv" and item[1] == 0)
    for r in range(max(starts) + depth):
        for d in [0] + list(range(depth - 1, 0, -1)):
            for start, chain in zip(starts, chains):
                if r - start != d:
                    continue
                for part in chain[d]:
                    part()
            if r == d == 0:
                ship_embed()
        if 0 <= r - loaded_at < len(vec_chain):
            vec_chain[r - loaded_at]()
    vec_finish()
    for source_stage, out in ((embed_stage, embed_out), (stages - 1, head_out)):
        @pl.when(stage != source_stage)
        def _():
            got = extra_recv[0 if source_stage == embed_stage else 1]
            extra_copy(source_stage, 1, got).wait_recv()
            out[...] = got[...]

        @pl.when(stage == source_stage)
        def _():
            for offset in range(1, stages):
                extra_copy(source_stage, offset, extra_recv[0]).wait_send()

    vec_drain()
    for kind, drain in drains:
        if kind == "extra":
            gated([drain])()
        else:
            drain()

    @pl.when(is_first)
    def _():
        ship().wait_send()

    for m in range(micros):
        @pl.when(jnp.logical_not(is_last))
        def _():
            forward_copy(m).wait_send()

        @pl.when(jnp.logical_not(is_first))
        def _():
            backward_copy(m).wait_send()


def step_plan(width, hid, vocab, stages, devices):
    plan = []
    for kind, c, _, turned in chunk_plan(width, hid, vocab, stages, devices):
        wide = kind in ("down", "extra")
        plan.append((kind, c, (ROW, 2 * ROW) if wide else (width // devices, width), turned))
    extra = [item for item in plan if item[0] == "extra"]
    rest = [item for item in plan if item[0] != "extra"]
    return rest + extra


def run_step(stages, devices, token_ids, segment_ids, target_ids, params):
    embed, qkv_w, qv_b, out_w, out_b, in_w, in_b, down_w, gains, shifts, fg, fb, head_w = params
    dims = line_dims(devices)
    width, hid, vocab = embed.shape[1], in_w.shape[1], head_w.shape[0]
    tokens = GROUP * ROW
    micros = token_ids.shape[0] // GROUP
    vmem = pl.BlockSpec(memory_space=pltpu.VMEM)
    hbm = pl.BlockSpec(memory_space=pl.ANY)
    sizes = tuple(size for size, _ in reversed(dims))
    slim = width // devices
    share = vocab // (stages * devices)
    plan = step_plan(width, hid, vocab, stages, devices)
    bits = devices.bit_length() - 1

    def scratch(lead, columns, kind=BF16):
        return pltpu.VMEM((lead, tokens, columns), kind)

    def sums(*shape):
        return pltpu.VMEM(shape, F32)

    dma = pltpu.SemaphoreType.DMA
    scratch_shapes = [
        pltpu.VMEM((vocab, width), BF16),
        pltpu.VMEM((width, 3 * width), BF16),
        pltpu.VMEM((width, width), BF16),
    ]
    scratch_shapes += [pltpu.VMEM(sizes + (slim, width), BF16)] * 8
    scratch_shapes += [
        scratch(micros, width),
        scratch(micros, width),
        scratch(micros, width),
        scratch(micros, width),
        scratch(micros, 3 * width),
        pltpu.VMEM((micros,) + sizes + (ROW, 2 * ROW), BF16),
        scratch(micros, width),
        scratch(micros, width, F32),
        scratch(micros, hid),
        scratch(micros, hid),
        sums(tokens, width),
        sums(tokens, width),
        scratch(micros, width),
        scratch(micros, vocab),
        sums(VEC_ROWS, width),
        sums(3, 16, ROW),
        sums(ROW, ROW),
        dma((micros,)),
        dma((micros,)),
        dma((micros,)),
        dma((micros,)),
        dma((11,)),
        sums(bits + 1, VEC_ROWS, width),
        sums(bits, VEC_ROWS, width),
        dma((bits,)),
        dma((bits,)),
        sums(8, width),
        sums(8, width),
        dma((stages,)),
        dma((1,)),
        sums(stages * share, width),
        dma((stages,)),
        dma((2,)),
        sums(ROW, 2 * ROW),
        dma((2,)),
        sums(share, width),
        sums(share, width),
    ]
    for _, _, block, turned in plan:
        remain = list(reversed(dims))
        for size, stride in dims[::-1] if turned else dims:
            remain.remove((size, stride))
            piece = tuple(other for other, _ in remain) + block
            scratch_shapes.append(pltpu.VMEM((1 if size == 2 else 2, size - 1) + piece, BF16))
            scratch_shapes += [dma((2, size - 1))] * 2

    def result(*shape):
        return jax.ShapeDtypeStruct(shape, F32)

    return pl.pallas_call(
        functools.partial(step_kernel, stages, micros, devices, plan),
        out_shape=[
            result(slim, 3 * width),
            result(slim, width),
            result(slim, hid),
            result(hid // devices, width),
            result(share, width),
            result(share, width),
            result(VEC_ROWS, width),
        ],
        in_specs=[vmem] * 10 + [hbm] * 6,
        out_specs=[vmem] * 7,
        scratch_shapes=scratch_shapes,
        compiler_params=pltpu.CompilerParams(
            collective_id=2, has_side_effects=True, vmem_limit_bytes=63 * 1024 * 1024
        ),
        name="step",
    )(
        token_ids,
        segment_ids,
        target_ids,
        qv_b,
        out_b,
        in_b,
        gains,
        shifts,
        fg,
        fb,
        embed,
        head_w,
        qkv_w,
        out_w,
        in_w.reshape(sizes + (slim, hid)),
        down_w.reshape((hid // width,) + sizes + (slim, width)),
    )


def finish_kernel(devices, embed_g, qkv_g, out_g, in_g, down_g, head_g, vec, *outs):
    place = lax.axis_index("dp")
    width = vec.shape[1]
    (embed_o, qkv_o, qv_o, out_o, outb_o, in_o, inb_o, down_o, gain_o, shift_o, fg_o, fb_o, head_o) = outs
    embed_o[...] = embed_g[...]
    head_o[...] = head_g[...]
    for source, target in ((qkv_g, qkv_o), (out_g, out_o), (in_g, in_o), (down_g, down_o)):
        target[0] = source[...]
    lanes = width // devices
    turned = pltpu.roll(vec[0:8, :], lax.rem(width - place * lanes, width), 1)
    for row, out in ((V_QUERY, qv_o), (V_BRANCH, outb_o), (V_GAIN1, gain_o), (V_SHIFT1, shift_o)):
        out[0] = turned[row : row + 2, 0:lanes]
    share = inb_o.shape[1]
    first = place * share
    row = vec[pl.ds(V_HIDDEN + first // width, 1), :]
    wide = jnp.broadcast_to(row, (8, width))
    inb_o[...] = pltpu.roll(wide, lax.rem(width - lax.rem(first, width), width), 1)[0:1, 0:share]
    fg_o[...] = vec[V_FINAL_GAIN : V_FINAL_GAIN + 1, :]
    fb_o[...] = vec[V_FINAL_BIAS : V_FINAL_BIAS + 1, :]


def run_finish(devices, embed_g, qkv_g, out_g, in_g, down_g, head_g, vec):
    vmem = pl.BlockSpec(memory_space=pltpu.VMEM)
    width = vec.shape[1]
    lanes = width // devices

    def shape(*sizes):
        return jax.ShapeDtypeStruct(sizes, F32)

    pair = shape(1, 2, lanes)
    return pl.pallas_call(
        functools.partial(finish_kernel, devices),
        out_shape=[
            shape(*embed_g.shape),
            shape(1, *qkv_g.shape),
            pair,
            shape(1, *out_g.shape),
            pair,
            shape(1, *in_g.shape),
            shape(1, in_g.shape[1] // devices),
            shape(1, *down_g.shape),
            pair,
            pair,
            shape(1, width),
            shape(1, width),
            shape(*head_g.shape),
        ],
        in_specs=[vmem] * 7,
        out_specs=[vmem] * 13,
        name="finish",
    )(embed_g, qkv_g, out_g, in_g, down_g, head_g, vec)


def on_device(
    token_ids,
    segment_ids,
    target_ids,
    embed_table,
    qkv_weight,
    qv_bias,
    out_weight,
    out_biases,
    ff_in,
    ff_in_bias,
    ff_out,
    norm_gains,
    norm_biases,
    final_gain,
    final_bias,
    head_weight,
):
    stages = lax.axis_size("pipe")
    devices = lax.axis_size("dp")
    params = (
        embed_table,
        qkv_weight[0],
        qv_bias[0],
        out_weight[0],
        out_biases[0],
        ff_in[0],
        ff_in_bias,
        ff_out[0],
        norm_gains[0],
        norm_biases[0],
        final_gain[None],
        final_bias[None],
        head_weight,
    )
    if devices == 8:
        grads = run_step(stages, devices, token_ids, segment_ids, target_ids, params)
    else:
        *saved, vec = run_pipeline(stages, token_ids, segment_ids, target_ids, params)
        grads = run_gradients(stages, devices, saved, vec, token_ids)
    qkv_g, out_g, in_g, down_g, embed_g, head_g, sums = grads
    done = list(run_finish(devices, embed_g, qkv_g, out_g, in_g, down_g, head_g, sums))
    done[10], done[11] = done[10][0], done[11][0]
    return tuple(done)


def solution(mesh):
    layer3 = P("pipe", None, None)
    return jax.shard_map(
        on_device,
        mesh=mesh,
        in_specs=(
            P("dp", None),
            P("dp", None),
            P("dp", None),
            P(),
            layer3,
            layer3,
            layer3,
            layer3,
            layer3,
            P("pipe", None),
            layer3,
            layer3,
            layer3,
            P(),
            P(),
            P(),
        ),
        out_specs=(
            P(("pipe", "dp"), None),
            P("pipe", "dp", None),
            P("pipe", None, "dp"),
            P("pipe", "dp", None),
            P("pipe", None, "dp"),
            P("pipe", "dp", None),
            P("pipe", "dp"),
            P("pipe", "dp", None),
            P("pipe", None, "dp"),
            P("pipe", None, "dp"),
            P(),
            P(),
            P(("pipe", "dp"), None),
        ),
        check_vma=False,
    )
```

```python
import functools

import jax
import jax.numpy as jnp
from jax import lax
from jax.experimental import pallas as pl
from jax.experimental.pallas import tpu as pltpu
from jax.sharding import PartitionSpec as P

HEADS = 8
FRAME = 6
ROW = 128
GROUP = 2
MASKED = -1e30
GELU_A = 0.7978845608
GELU_B = 0.044715
MESH = pl.DeviceIdType.MESH
F32 = jnp.float32
BF16 = jnp.bfloat16

VEC_ROWS = 16
V_QUERY, V_VALUE, V_BRANCH, V_RESULT, V_GAIN1, V_GAIN2, V_SHIFT1, V_SHIFT2 = range(8)
V_HIDDEN = 8
V_FINAL_GAIN, V_FINAL_BIAS = 12, 13


def dot(a, b):
    return lax.dot_general(a, b, (((1,), (0,)), ((), ())), preferred_element_type=F32)


def dot_nt(a, b):
    return lax.dot_general(a, b, (((1,), (1,)), ((), ())), preferred_element_type=F32)


def dot_tn(a, b):
    return lax.dot_general(a, b, (((0,), (0,)), ((), ())), preferred_element_type=F32)


def normalise(values):
    centre = jnp.mean(values, axis=-1, keepdims=True)
    centered = values - centre
    spread = jnp.mean(centered * centered, axis=-1, keepdims=True)
    scale = lax.rsqrt(spread + 1e-05)
    return centered * scale, scale


def norm_backward(grad, normal, scale, gain):
    grad_n = grad * gain
    mean_grad = jnp.mean(grad_n, axis=-1, keepdims=True)
    mean_proj = jnp.mean(grad_n * normal, axis=-1, keepdims=True)
    return scale * (grad_n - mean_grad - normal * mean_proj)


def column_sum(values):
    return jnp.sum(values, axis=0, keepdims=True)


def stack_pair(pair, low_lanes):
    zero = jnp.zeros_like(pair)
    return jnp.concatenate(
        [jnp.where(low_lanes, pair, zero), jnp.where(low_lanes, zero, pair)], axis=0
    )


def join_pair(stacked, low_lanes):
    half = stacked.shape[0] // 2
    return jnp.where(low_lanes, stacked[:half], stacked[half:])


def pipeline_kernel(
    stages,
    micros,
    token_ids,
    segment_ids,
    target_ids,
    embed,
    qkv_w,
    qv_b,
    out_w,
    out_b,
    in_w,
    in_b,
    down_w,
    gains,
    shifts,
    fin_gain,
    fin_bias,
    head_w,
    normed_o,
    mixed_o,
    normed2_o,
    active_o,
    gres_o,
    ghid_o,
    gbr_o,
    gproj_o,
    xl_o,
    xr_o,
    vec,
    instream,
    outb,
    gin,
    gs,
    normed,
    proj,
    probs,
    mixed,
    middle,
    normed2,
    active,
    slope,
    lo,
    go,
    gmid,
    s_gres,
    s_ghid,
    s_gbr,
    s_gproj,
    s_xl,
    ids,
    frames,
    fsend,
    frecv,
    bsend,
    brecv,
    osem,
):
    stage = lax.axis_index("pipe")
    tokens, width = instream.shape[1], instream.shape[2]
    hidden_n = in_b.shape[1]
    vocab = head_w.shape[0]
    pairs = width // ROW
    chunk = 512
    is_first = stage == 0
    is_last = stage == stages - 1
    up = jnp.minimum(stage + 1, stages - 1)
    down = jnp.maximum(stage - 1, 0)

    barrier = pltpu.get_barrier_semaphore()

    @pl.when(jnp.logical_not(is_first))
    def _():
        pl.semaphore_signal(barrier, inc=1, device_id={"pipe": down}, device_id_type=MESH)

    @pl.when(jnp.logical_not(is_last))
    def _():
        pl.semaphore_signal(barrier, inc=1, device_id={"pipe": up}, device_id_type=MESH)

    pl.semaphore_wait(barrier, jnp.where(is_first | is_last, 1, 2))
    vec[...] = jnp.zeros_like(vec)
    rows_n, seq = token_ids.shape
    for index, member in enumerate((token_ids, segment_ids, target_ids)):
        ids[index] = jnp.full(ids.shape[1:], 4.0 if index == 1 else -1.0, F32)
        ids[index, 0:rows_n, 0:seq] = member[...].astype(F32)
    at_query = lax.broadcasted_iota(jnp.int32, (ROW, ROW), 1)
    at_key = lax.broadcasted_iota(jnp.int32, (ROW, ROW), 0)
    frames[...] = jnp.where(at_key < ((at_query * 43) // 256) * FRAME + FRAME, 1.0, 0.0)

    def column(index, row):
        values = jnp.broadcast_to(ids[index, pl.ds(row, 1), :], (8, ROW))
        return values.T[:, 0:1]

    def hot_rows(index, m):
        parts = [column(index, m * GROUP + r) for r in range(GROUP)]
        values = jnp.concatenate(parts, axis=0)
        places = lax.broadcasted_iota(jnp.int32, (tokens, vocab), 1).astype(F32)
        return values, jnp.where(values == places, 1.0, 0.0)

    def forward_copy(m):
        return pltpu.make_async_remote_copy(
            src_ref=outb.at[m],
            dst_ref=instream.at[m],
            send_sem=fsend.at[m],
            recv_sem=frecv.at[m],
            device_id={"pipe": up},
            device_id_type=MESH,
        )

    def backward_copy(m):
        return pltpu.make_async_remote_copy(
            src_ref=gs.at[m],
            dst_ref=gin.at[m],
            send_sem=bsend.at[m],
            recv_sem=brecv.at[m],
            device_id={"pipe": down},
            device_id_type=MESH,
        )

    def save(index, src, dst, m):
        return pltpu.make_async_copy(src, dst.at[m], osem.at[index, m])

    def saves_forward(m):
        return [
            save(0, normed.at[m], normed_o, m),
            save(1, mixed.at[m], mixed_o, m),
            save(2, normed2.at[m], normed2_o, m),
            save(3, active.at[m], active_o, m),
        ]

    def saves_backward(m):
        slot = lax.rem(m, 2)
        return [
            save(4, s_gres.at[slot], gres_o, m),
            save(5, s_ghid.at[slot], ghid_o, m),
            save(6, s_gbr.at[slot], gbr_o, m),
            save(7, s_gproj.at[slot], gproj_o, m),
        ]

    def save_xl(m):
        return save(8, s_xl.at[lax.rem(m, 2)], xl_o, m)

    def put_xl(m, value):
        @pl.when(m >= 2)
        def _():
            save_xl(m - 2).wait()

        s_xl[lax.rem(m, 2)] = value
        save_xl(m).start()

    lane_low = lax.broadcasted_iota(jnp.int32, (ROW, ROW), 1) < ROW // 2

    def forward(m):
        @pl.when(is_first)
        def _():
            hot = hot_rows(0, m)[1].astype(BF16)
            instream[m] = dot(hot, embed[...]).astype(BF16)

        @pl.when(jnp.logical_not(is_first))
        def _():
            forward_copy(m).wait_recv()

        normal, _ = normalise(instream[m].astype(F32))
        normed[m] = (normal * gains[0:1, :] + shifts[0:1, :]).astype(BF16)
        low = normed[m]
        queries = dot(low, qkv_w[:, 0:width]) + qv_b[0:1, :]
        proj[m, :, 0:width] = (queries * (ROW // 2) ** -0.5).astype(BF16)
        proj[m, :, width : 2 * width] = dot(low, qkv_w[:, width : 2 * width]).astype(BF16)
        proj[m, :, 2 * width : 3 * width] = (
            dot(low, qkv_w[:, 2 * width : 3 * width]) + qv_b[1:2, :]
        ).astype(BF16)
        masks, scores = [], []
        for r in range(GROUP):
            rows = slice(r * ROW, (r + 1) * ROW)
            kinds = lax.broadcasted_iota(jnp.int32, (16, ROW), 0).astype(F32)
            member = jnp.where(ids[1, pl.ds(m * GROUP + r, 1), :] == kinds, 1.0, 0.0).astype(BF16)
            mask = jnp.where(dot_tn(member, member) * frames[...] > 0.5, 0.0, MASKED)
            masks.append(jnp.concatenate([mask, mask], axis=1))
            for p in range(pairs):
                q = stack_pair(proj[m, rows, p * ROW : (p + 1) * ROW], lane_low)
                k = proj[m, rows, width + p * ROW : width + (p + 1) * ROW]
                scores.append(dot_nt(k, q))

        def mix(unit):
            r, p = unit // pairs, unit % pairs
            rows = slice(r * ROW, (r + 1) * ROW)
            v = proj[m, rows, 2 * width + p * ROW : 2 * width + (p + 1) * ROW]
            both = dot_tn(probs[m, unit], v)
            mixed[m, rows, p * ROW : (p + 1) * ROW] = join_pair(both, lane_low).astype(BF16)

        for unit in range(GROUP * pairs):
            masked = scores[unit] + masks[unit // pairs]
            expo = jnp.exp(masked - jnp.max(masked, axis=0, keepdims=True))
            total = jnp.sum(expo, axis=0, keepdims=True)
            probs[m, unit] = (expo * (1.0 / total)).astype(BF16)
            if unit:
                mix(unit - 1)
        mix(GROUP * pairs - 1)
        mid = instream[m].astype(F32) + (dot(mixed[m], out_w[...]) + out_b[0:1, :])
        middle[m] = mid
        normal2, _ = normalise(mid)
        normed2[m] = (normal2 * gains[1:2, :] + shifts[1:2, :]).astype(BF16)
        low2 = normed2[m]
        parts = hidden_n // chunk

        def spread(c):
            return dot(low2, in_w[:, c * chunk : (c + 1) * chunk])

        total, ahead = None, spread(0)
        for c in range(parts):
            cols = slice(c * chunk, (c + 1) * chunk)
            hid = ahead + in_b[0:1, cols]
            if c + 1 < parts:
                ahead = spread(c + 1)
            square = hid * hid
            tan = jnp.tanh(hid * (GELU_A + (GELU_A * GELU_B) * square))
            half = 0.5 + 0.5 * tan
            act = (hid * half).astype(BF16)
            active[m, :, cols] = act
            rise = (1.0 - tan * tan) * (0.5 * GELU_A + (1.5 * GELU_A * GELU_B) * square)
            slope[m, :, cols] = (half + hid * rise).astype(BF16)
            term = dot(act, down_w[cols, :])
            total = term if total is None else total + term
        for copy in saves_forward(m):
            copy.start()
        lo[...] = middle[m] + (total + out_b[1:2, :])

        @pl.when(jnp.logical_not(is_last))
        def _():
            outb[m] = lo[...].astype(BF16)
            forward_copy(m).start()

    def head(m):
        normal, scale = normalise(lo[...])
        outb[m] = (normal * fin_gain[...] + fin_bias[...]).astype(BF16)
        save(9, outb.at[m], xr_o, m).start()
        logits = dot_nt(outb[m], head_w[...])
        top = jnp.max(logits, axis=-1, keepdims=True)
        expo = jnp.exp(logits - top)
        total = jnp.sum(expo, axis=-1, keepdims=True)
        target, hot = hot_rows(2, m)
        grad_logits = jnp.where(target >= 0.0, expo * (1.0 / total) - hot, 0.0).astype(BF16)
        put_xl(m, grad_logits)
        grad_final = dot(grad_logits, head_w[...])
        vec[V_FINAL_GAIN : V_FINAL_GAIN + 1, :] += column_sum(grad_final * normal)
        vec[V_FINAL_BIAS : V_FINAL_BIAS + 1, :] += column_sum(grad_final)
        go[...] = norm_backward(grad_final, normal, scale, fin_gain[...])

    def backward(m):
        slot = lax.rem(m, 2)

        @pl.when(m >= 2)
        def _():
            for copy in saves_backward(m - 2):
                copy.wait()

        @pl.when(jnp.logical_not(is_last))
        def _():
            backward_copy(m).wait_recv()
            go[...] = gin[m].astype(F32)

        s_gres[slot] = go[...].astype(BF16)
        gres = s_gres[slot]
        parts = hidden_n // chunk

        def spread(c):
            return dot_nt(gres, down_w[c * chunk : (c + 1) * chunk, :])

        total, ahead = None, spread(0)
        for c in range(parts):
            cols = slice(c * chunk, (c + 1) * chunk)
            gact = ahead
            if c + 1 < parts:
                ahead = spread(c + 1)
            ghid = (gact * slope[m, :, cols].astype(F32)).astype(BF16)
            s_ghid[slot, :, cols] = ghid
            term = dot_nt(ghid, in_w[:, cols])
            total = term if total is None else total + term
        normal2, scale2 = normalise(middle[m])
        vec[V_GAIN2 : V_GAIN2 + 1, :] += column_sum(total * normal2)
        vec[V_SHIFT2 : V_SHIFT2 + 1, :] += column_sum(total)
        gmid[...] = go[...] + norm_backward(total, normal2, scale2, gains[1:2, :])
        s_gbr[slot] = gmid[...].astype(BF16)
        gbr = s_gbr[slot]
        gmix = dot_nt(gbr, out_w[...]).astype(BF16)
        grads = []
        for r in range(GROUP):
            rows = slice(r * ROW, (r + 1) * ROW)
            for p in range(pairs):
                gm = stack_pair(gmix[rows, p * ROW : (p + 1) * ROW], lane_low)
                vlanes = slice(2 * width + p * ROW, 2 * width + (p + 1) * ROW)
                grads.append(dot_nt(proj[m, rows, vlanes], gm))
                s_gproj[slot, rows, vlanes] = dot(probs[m, r * pairs + p], gm).astype(BF16)

        def pull(unit, gsc):
            r, p = unit // pairs, unit % pairs
            rows = slice(r * ROW, (r + 1) * ROW)
            lanes = slice(p * ROW, (p + 1) * ROW)
            klanes = slice(width + p * ROW, width + (p + 1) * ROW)
            q = stack_pair(proj[m, rows, lanes], lane_low)
            s_gproj[slot, rows, klanes] = dot(gsc, q).astype(BF16)
            gq = join_pair(dot_tn(gsc, proj[m, rows, klanes]), lane_low) * (ROW // 2) ** -0.5
            s_gproj[slot, rows, lanes] = gq.astype(BF16)

        waiting = None
        for unit in range(GROUP * pairs):
            weights = probs[m, unit].astype(F32)
            inner = jnp.sum(weights * grads[unit], axis=0, keepdims=True)
            gsc = (weights * (grads[unit] - inner)).astype(BF16)
            if waiting is not None:
                pull(unit - 1, waiting)
            waiting = gsc
        pull(GROUP * pairs - 1, waiting)
        for copy in saves_backward(m):
            copy.start()
        gproj = s_gproj[slot]
        gnormed = dot_nt(gproj, qkv_w[...])
        normal, scale = normalise(instream[m].astype(F32))
        vec[V_GAIN1 : V_GAIN1 + 1, :] += column_sum(gnormed * normal)
        vec[V_SHIFT1 : V_SHIFT1 + 1, :] += column_sum(gnormed)
        gs[m] = (gmid[...] + norm_backward(gnormed, normal, scale, gains[0:1, :])).astype(BF16)

        @pl.when(is_first)
        def _():
            save(9, gs.at[m], xr_o, m).start()

        @pl.when(jnp.logical_not(is_first))
        def _():
            backward_copy(m).start()

    def tick(t, carry):
        m_forward = t - stage
        m_backward = t - (2 * (stages - 1) - stage)

        @pl.when((m_forward >= 0) & (m_forward < micros))
        def _():
            forward(m_forward)

        @pl.when((m_backward >= 0) & (m_backward < micros))
        def _():
            @pl.when(is_last)
            def _():
                head(m_backward)

            backward(m_backward)

        return carry

    lax.fori_loop(0, micros + 2 * (stages - 1), tick, 0)

    for m in range(micros):
        for copy in saves_forward(m):
            copy.wait()

        @pl.when(jnp.logical_not(is_last))
        def _():
            forward_copy(m).wait_send()

        @pl.when(jnp.logical_not(is_first))
        def _():
            backward_copy(m).wait_send()

        @pl.when(is_first)
        def _():
            save(9, gs.at[m], xr_o, m).wait()

        @pl.when(is_last)
        def _():
            save(9, outb.at[m], xr_o, m).wait()

    for m in range(max(0, micros - 2), micros):
        for copy in saves_backward(m):
            copy.wait()

        @pl.when(is_last)
        def _():
            save_xl(m).wait()


def run_pipeline(stages, token_ids, segment_ids, target_ids, params):
    embed, in_w, head_w = params[0], params[5], params[12]
    width = embed.shape[1]
    vocab = head_w.shape[0]
    hid = in_w.shape[1]
    tokens = GROUP * ROW
    micros = token_ids.shape[0] // GROUP
    pairs = width // ROW
    vmem = pl.BlockSpec(memory_space=pltpu.VMEM)
    hbm = pl.BlockSpec(memory_space=pl.ANY)

    def kept(columns):
        return jax.ShapeDtypeStruct((micros, tokens, columns), BF16)

    def scratch(lead, columns, kind=BF16):
        return pltpu.VMEM((lead, tokens, columns), kind)

    out_shape = [
        kept(width),
        kept(width),
        kept(width),
        kept(hid),
        kept(width),
        kept(hid),
        kept(width),
        kept(3 * width),
        kept(vocab),
        kept(width),
        jax.ShapeDtypeStruct((VEC_ROWS, width), F32),
    ]
    return pl.pallas_call(
        functools.partial(pipeline_kernel, stages, micros),
        out_shape=out_shape,
        in_specs=[vmem] * 16,
        out_specs=[hbm] * 10 + [vmem],
        scratch_shapes=[
            scratch(micros, width),
            scratch(micros, width),
            scratch(micros, width),
            scratch(micros, width),
            scratch(micros, width),
            scratch(micros, 3 * width),
            pltpu.VMEM((micros, GROUP * pairs, ROW, 2 * ROW), BF16),
            scratch(micros, width),
            scratch(micros, width, F32),
            scratch(micros, width),
            scratch(micros, hid),
            scratch(micros, hid),
            pltpu.VMEM((tokens, width), F32),
            pltpu.VMEM((tokens, width), F32),
            pltpu.VMEM((tokens, width), F32),
            scratch(2, width),
            scratch(2, hid),
            scratch(2, width),
            scratch(2, 3 * width),
            scratch(2, vocab),
            pltpu.VMEM((3, 16, ROW), F32),
            pltpu.VMEM((ROW, ROW), F32),
            pltpu.SemaphoreType.DMA((micros,)),
            pltpu.SemaphoreType.DMA((micros,)),
            pltpu.SemaphoreType.DMA((micros,)),
            pltpu.SemaphoreType.DMA((micros,)),
            pltpu.SemaphoreType.DMA((10, micros)),
        ],
        compiler_params=pltpu.CompilerParams(
            collective_id=0, has_side_effects=True, vmem_limit_bytes=62 * 1024 * 1024
        ),
        name="pipeline",
    )(token_ids, segment_ids, target_ids, *params)


def line_dims(devices):
    dims, stride = [], 1
    if devices == 8:
        return [(2, 1), (4, 2)]
    while devices > 1:
        size = 4 if devices % 4 == 0 else 2
        dims.append((size, stride))
        stride *= size
        devices //= size
    return dims


def chunk_plan(width, hid, vocab, stages, devices):
    slim, deep = width // devices, hid // devices
    plan = [("out", 0, (slim, width), False)]
    for c in range(4):
        plan.append(("down", c, (deep, width // 4), c in (1, 3)))
    for c in range(2):
        plan.append(("extra", c, (stages, vocab // (stages * devices), width // 2), False))
    for c in range(hid // width):
        plan.append(("in", c, (slim, width), c == 1))
    for c in range(3):
        plan.append(("qkv", c, (slim, width), False))
    return plan


def gradient_kernel(stages, devices, plan, *refs):
    dims = line_dims(devices)
    refs = list(refs)

    def take(amount):
        head, refs[:] = refs[:amount], refs[amount:]
        return head

    inputs = take(10)
    vec_in, token_ids = take(2)
    qkv_out, out_out, in_out, down_out, embed_out, head_out, vec_out = take(7)
    local = take(10)
    in_sem = take(1)[0]
    turned_left, turned_xl = take(2)
    mats = dict(
        zip(
            ("normed", "mixed", "normed2", "active", "gres", "ghid", "gbr", "gproj", "xl", "xr"),
            local,
        )
    )
    names = list(mats)
    stage = lax.axis_index("pipe")
    place = lax.axis_index("dp")
    is_extra = (stage == 0) | (stage == stages - 1)
    width = mats["normed"].shape[1]
    where = [lax.rem(place // stride, size) for size, stride in dims]

    barrier = pltpu.get_barrier_semaphore()

    def greet(offset, carry):
        peer = lax.rem(place + offset, devices)
        pl.semaphore_signal(barrier, inc=1, device_id={"dp": peer}, device_id_type=MESH)
        return carry

    def greet_stage(offset, carry):
        peer = lax.rem(stage + offset, stages)
        pl.semaphore_signal(barrier, inc=1, device_id={"pipe": peer}, device_id_type=MESH)
        return carry

    lax.fori_loop(1, devices, greet, 0)
    lax.fori_loop(1, stages, greet_stage, 0)

    def load(name):
        i = names.index(name)
        return pltpu.make_async_copy(inputs[i], mats[name], in_sem.at[i])

    groups = [("mixed", "gbr"), ("gres", "active"), ("xr", "xl"), ("normed2", "ghid"), ("normed", "gproj")]

    def fetch(at):
        if at >= len(groups):
            return
        if groups[at] == ("xr", "xl"):
            @pl.when(is_extra)
            def _():
                load("xr").start()

            @pl.when(stage == stages - 1)
            def _():
                load("xl").start()

            at += 1
        for name in groups[at]:
            load(name).start()

    fetch(0)
    loaded = set()

    def need(*wanted):
        fresh = [name for name in wanted if name not in loaded]
        for name in fresh:
            loaded.add(name)
            load(name).wait()
        if fresh:
            at = [i for i, group in enumerate(groups) if group[0] == fresh[0]][0]
            fetch(at + 1)

    def identity(size):
        here = lax.broadcasted_iota(jnp.int32, (size, size), 0)
        there = lax.broadcasted_iota(jnp.int32, (size, size), 1)
        return jnp.where(here == there, 1.0, 0.0).astype(BF16)

    held = []

    def turn(name):
        if held[-1:] == [name]:
            return
        held.append(name)
        unit = identity(256)
        for q in range(width // 256):
            part = dot_nt(unit, mats[name][:, q * 256 : (q + 1) * 256])
            turned_left[q * 256 : (q + 1) * 256, :] = part.astype(BF16)

    bits = devices.bit_length() - 1
    vec_send, vec_recv = take(2)
    vec_sems = take(2)

    def vec_copy(k):
        peer = jnp.bitwise_xor(place, 1 << k)
        return pltpu.make_async_remote_copy(
            src_ref=vec_send.at[k],
            dst_ref=vec_recv.at[k],
            send_sem=vec_sems[0].at[k],
            recv_sem=vec_sems[1].at[k],
            device_id={"dp": peer},
            device_id_type=MESH,
        )

    def vec_step(k):
        def run():
            if k == 0:
                vec_send[0] = vec_in[...]
                ones = jnp.ones((16, mats["gres"].shape[0]), BF16)
                for name, start, row in (
                    ("gproj", 0, V_QUERY),
                    ("gproj", 2 * width, V_VALUE),
                    ("gbr", 0, V_BRANCH),
                    ("gres", 0, V_RESULT),
                ):
                    part = dot(ones, mats[name][:, start : start + width])
                    vec_send[0, row : row + 1, :] = part[0:1, :]
                for q in range(mats["ghid"].shape[1] // width):
                    part = dot(ones, mats["ghid"][:, q * width : (q + 1) * width])
                    vec_send[0, V_HIDDEN + q : V_HIDDEN + q + 1, :] = part[0:1, :]
            else:
                vec_copy(k - 1).wait_recv()
                vec_send[k] = vec_send[k - 1] + vec_recv[k - 1]
            if k < bits:
                vec_copy(k).start()

        return run

    final_send, final_recv = take(2)
    final_sems = take(2)

    def final_copy(offset):
        peer = lax.rem(stages - 1 + offset, stages)
        return pltpu.make_async_remote_copy(
            src_ref=final_send,
            dst_ref=final_recv,
            send_sem=final_sems[0].at[offset],
            recv_sem=final_sems[1].at[0],
            device_id={"pipe": peer},
            device_id_type=MESH,
        )

    def vec_last():
        vec_step(bits)()
        vec_out[...] = vec_send[bits]

        @pl.when(stage == stages - 1)
        def _():
            final_send[...] = vec_send[bits, 8:16, :]
            for offset in range(1, stages):
                final_copy(offset).start()

    def vec_finish():
        @pl.when(stage != stages - 1)
        def _():
            final_copy(1).wait_recv()
            vec_out[V_FINAL_GAIN : V_FINAL_BIAS + 1, :] = final_recv[
                V_FINAL_GAIN - 8 : V_FINAL_BIAS - 7, :
            ]

    def vec_drain():
        for k in range(bits):
            vec_copy(k).wait_send()

        @pl.when(stage == stages - 1)
        def _():
            for offset in range(1, stages):
                final_copy(offset).wait_send()

    extra_sum, extra_send_sem, extra_recv_sem = take(3)

    def extra_copy(source, offset, target):
        peer = lax.rem(source + offset, stages)
        return pltpu.make_async_remote_copy(
            src_ref=extra_sum.at[peer],
            dst_ref=target,
            send_sem=extra_send_sem.at[offset],
            recv_sem=extra_recv_sem.at[0 if source == 0 else 1],
            device_id={"pipe": peer},
            device_id_type=MESH,
        )

    down_full = {}

    def chunk_steps(kind, c, block, turned):
        order = list(range(len(dims)))
        if turned:
            order.reverse()
        full = take(1)[0]

        def compute():
            if kind == "down":
                need("gres", "active")
                turn("gres")
                if c % 2 == 1:
                    return
                half = width // 2
                lines = slice((c // 2) * half, (c // 2 + 1) * half)
                parts = dot(turned_left[lines, :], mats["active"][...]).astype(BF16)
                depth = block[0]
                unit = identity(depth)
                for d in range(devices):
                    back = dot_nt(unit, parts[:, d * depth : (d + 1) * depth]).astype(BF16)
                    down_full[c][split(d)] = back[:, 0 : half // 2]
                    down_full[c + 1][split(d)] = back[:, half // 2 : half]
            elif kind == "extra":
                vocab = turned_xl.shape[0]
                if c == 0:
                    load("xr").wait()

                @pl.when((stage == 0) & (c == 0))
                def _():
                    rows_n, seq = token_ids.shape
                    places = lax.broadcasted_iota(jnp.int32, (vocab, ROW), 0)
                    gap = jnp.full((1, ROW - seq), -1, jnp.int32)
                    for r in range(rows_n):
                        row = jnp.concatenate([token_ids[r : r + 1, :], gap], axis=1)
                        hot = jnp.where(places == row, 1.0, 0.0)
                        turned_xl[:, r * ROW : (r + 1) * ROW] = hot.astype(BF16)

                @pl.when((stage == stages - 1) & (c == 0))
                def _():
                    load("xl").wait()
                    unit = identity(256)
                    for q in range(vocab // 256):
                        part = dot_nt(unit, mats["xl"][:, q * 256 : (q + 1) * 256])
                        turned_xl[q * 256 : (q + 1) * 256, :] = part.astype(BF16)

                rows = vocab // stages
                for p in range(stages):
                    part = dot(
                        turned_xl[p * rows : (p + 1) * rows, :],
                        mats["xr"][:, c * (width // 2) : (c + 1) * (width // 2)],
                    )
                    part = part.astype(BF16).reshape((devices,) + block[1:])
                    for d in range(devices):
                        full[split(d) + (p,)] = part[d]
            else:
                left, right = {
                    "in": ("normed2", "ghid"),
                    "out": ("mixed", "gbr"),
                    "qkv": ("normed", "gproj"),
                }[kind]
                need(left, right)
                turn(left)
                cols = slice(c * width, (c + 1) * width)
                part = dot(turned_left[...], mats[right][:, cols]).astype(BF16)
                part = part.reshape((devices,) + block)
                for d in range(devices):
                    full[split(d)] = part[d]

        def split(d):
            return tuple((d // stride) % size for size, stride in reversed(dims))

        if kind == "down":
            down_full[c] = full
        steps = [[compute]]
        for at, phase in enumerate(order):
            size = dims[phase][0]
            buffers = take(3)
            done = order[:at]
            last = at == len(order) - 1
            steps[-1].append(functools.partial(line_step, phase, size, 1, full, buffers, done))
            for t in range(2, size):
                steps.append([functools.partial(line_step, phase, size, t, full, buffers, done)])
            drains.append((kind, functools.partial(line_drain, phase, size, full, buffers, done)))
            steps.append([functools.partial(line_final, kind, c, phase, size, full, buffers, done, last)])
        if kind == "extra":
            steps = [[gated([part]) for part in step] for step in steps]
        return steps

    def gated(step):
        def run():
            @pl.when(is_extra)
            def _():
                for part in step:
                    part()

        return run

    def block_of(full, phase, j, done):
        spot = [slice(None)] * len(dims)
        for other in done:
            spot[len(dims) - 1 - other] = where[other]
        spot[len(dims) - 1 - phase] = j
        return full.at[tuple(spot)]

    def line_copy(phase, size, t, side, full, buffers, done):
        recv, ssem, rsem = buffers
        i = where[phase]
        stride = dims[phase][1]
        if side == 0:
            j, peer = size - t + i, place + jnp.where(i < size - 1, stride, 0)
        else:
            j, peer = t - size + i, place - jnp.where(i > 0, stride, 0)
        return pltpu.make_async_remote_copy(
            src_ref=block_of(full, phase, jnp.clip(j, 0, size - 1), done),
            dst_ref=recv.at[0 if size == 2 else side, t - 1],
            send_sem=ssem.at[side, t - 1],
            recv_sem=rsem.at[side, t - 1],
            device_id={"dp": peer},
            device_id_type=MESH,
        )

    def sends(i, size, t, side):
        return (i <= t - 1) if side == 0 else (i >= size - t)

    def line_step(phase, size, t, full, buffers, done):
        i = where[phase]
        for side in range(2):
            at_end = (i == 0) if side == 0 else (i == size - 1)
            j = size - t + i if side == 0 else t - size + i
            j = jnp.clip(j, 0, size - 1)

            @pl.when(sends(i, size, t, side))
            def _():
                if t > 1:
                    @pl.when(jnp.logical_not(at_end))
                    def _():
                        line_copy(phase, size, t - 1, side, full, buffers, done).wait_recv()
                        own = block_of(full, phase, j, done)
                        got = buffers[0][0 if size == 2 else side, t - 2]
                        own[...] = (own[...].astype(F32) + got.astype(F32)).astype(BF16)

                line_copy(phase, size, t, side, full, buffers, done).start()

    def line_final(kind, c, phase, size, full, buffers, done, last):
        i = where[phase]
        own = block_of(full, phase, i, done)
        total = own
        if last:
            slots = {
                "qkv": lambda: qkv_out.at[:, c * width : (c + 1) * width],
                "in": lambda: in_out.at[:, c * width : (c + 1) * width],
                "out": lambda: out_out,
                "down": lambda: down_out.at[:, c * (width // 4) : (c + 1) * (width // 4)],
                "extra": lambda: extra_sum.at[:, :, c * (width // 2) : (c + 1) * (width // 2)],
            }
            total = slots[kind]()
        lower, upper = i > 0, i < size - 1

        def arrived(side):
            line_copy(phase, size, size - 1, side, full, buffers, done).wait_recv()
            return buffers[0][0 if size == 2 else side, size - 2].astype(F32)

        @pl.when(lower & upper)
        def _():
            total[...] = (own[...].astype(F32) + arrived(0) + arrived(1)).astype(total.dtype)

        @pl.when(lower & jnp.logical_not(upper))
        def _():
            total[...] = (own[...].astype(F32) + arrived(0)).astype(total.dtype)

        @pl.when(jnp.logical_not(lower))
        def _():
            total[...] = (own[...].astype(F32) + arrived(1)).astype(total.dtype)

        if last and kind == "extra" and c == 1:
            for source_stage, out in ((0, embed_out), (stages - 1, head_out)):
                @pl.when(stage == source_stage)
                def _():
                    for offset in range(1, stages):
                        extra_copy(source_stage, offset, extra_recv[0 if source_stage == 0 else 1]).start()
                    out[...] = extra_sum[source_stage]

    def line_drain(phase, size, full, buffers, done):
        i = where[phase]
        for side in range(2):
            for t in range(1, size):
                @pl.when(sends(i, size, t, side))
                def _():
                    line_copy(phase, size, t, side, full, buffers, done).wait_send()

    extra_recv = take(2)
    drains = []
    chains = [chunk_steps(*item) for item in plan]
    depth = len(chains[0])
    vec_chain = [vec_step(k) for k in range(bits)] + [vec_last]
    starts, first, extra_rounds = [], 0, iter((1, 3, 6, 8))
    for item in plan:
        if item[3]:
            starts.append(next(extra_rounds))
        else:
            starts.append(first)
            first += 1
    begun = False
    loaded_at = max(start for start, item in zip(starts, plan) if item[0] == "qkv" and item[1] == 0)
    for r in range(max(starts) + depth):
        for d in [0] + list(range(depth - 1, 0, -1)):
            for start, chain in zip(starts, chains):
                if r - start != d:
                    continue
                for part in chain[d]:
                    part()
                    if not begun:
                        begun = True
                        pl.semaphore_wait(barrier, devices - 1 + stages - 1)
        if 0 <= r - loaded_at < len(vec_chain):
            vec_chain[r - loaded_at]()
    vec_finish()
    for source_stage, out in ((0, embed_out), (stages - 1, head_out)):
        @pl.when(stage != source_stage)
        def _():
            got = extra_recv[0 if source_stage == 0 else 1]
            extra_copy(source_stage, 1, got).wait_recv()
            out[...] = got[...]

        @pl.when(stage == source_stage)
        def _():
            for offset in range(1, stages):
                extra_copy(source_stage, offset, extra_recv[0]).wait_send()

    vec_drain()
    for kind, drain in drains:
        if kind == "extra":
            gated([drain])()
        else:
            drain()


def run_gradients(stages, devices, saved, vec, token_ids):
    dims = line_dims(devices)
    rows, tokens, width = saved[0].shape
    hid, vocab = saved[3].shape[2], saved[8].shape[2]
    plan = chunk_plan(width, hid, vocab, stages, devices)
    saved = [member.reshape(rows * tokens, member.shape[2]) for member in saved]
    vmem = pl.BlockSpec(memory_space=pltpu.VMEM)
    hbm = pl.BlockSpec(memory_space=pl.ANY)
    bits = devices.bit_length() - 1
    share = vocab // (stages * devices)
    scratch = [pltpu.VMEM(member.shape, BF16) for member in saved]
    scratch += [pltpu.SemaphoreType.DMA((len(saved),))]
    scratch += [pltpu.VMEM((width, rows * tokens), BF16), pltpu.VMEM((vocab, rows * tokens), BF16)]
    scratch += [
        pltpu.VMEM((bits + 1,) + vec.shape, F32),
        pltpu.VMEM((bits,) + vec.shape, F32),
        pltpu.SemaphoreType.DMA((bits,)),
        pltpu.SemaphoreType.DMA((bits,)),
        pltpu.VMEM((8, width), F32),
        pltpu.VMEM((8, width), F32),
        pltpu.SemaphoreType.DMA((stages,)),
        pltpu.SemaphoreType.DMA((1,)),
        pltpu.VMEM((stages, share, width), F32),
        pltpu.SemaphoreType.DMA((stages,)),
        pltpu.SemaphoreType.DMA((2,)),
        pltpu.VMEM((share, width), F32),
        pltpu.VMEM((share, width), F32),
    ]
    sizes = [size for size, _ in reversed(dims)]
    for _, _, block, turned in plan:
        scratch.append(pltpu.VMEM(tuple(sizes) + block, BF16))
        remain = list(reversed(dims))
        for size, stride in dims[::-1] if turned else dims:
            remain.remove((size, stride))
            piece = tuple(other for other, _ in remain) + block
            scratch.append(pltpu.VMEM((1 if size == 2 else 2, size - 1) + piece, BF16))
            scratch += [pltpu.SemaphoreType.DMA((2, size - 1))] * 2
    return pl.pallas_call(
        functools.partial(gradient_kernel, stages, devices, plan),
        out_shape=[
            jax.ShapeDtypeStruct((width // devices, 3 * width), F32),
            jax.ShapeDtypeStruct((width // devices, width), F32),
            jax.ShapeDtypeStruct((width // devices, hid), F32),
            jax.ShapeDtypeStruct((hid // devices, width), F32),
            jax.ShapeDtypeStruct((share, width), F32),
            jax.ShapeDtypeStruct((share, width), F32),
            jax.ShapeDtypeStruct(vec.shape, F32),
        ],
        in_specs=[hbm] * len(saved) + [vmem] * 2,
        out_specs=[vmem] * 7,
        scratch_shapes=scratch,
        compiler_params=pltpu.CompilerParams(
            collective_id=1, has_side_effects=True, vmem_limit_bytes=62 * 1024 * 1024
        ),
        name="gradients",
    )(*saved, vec, token_ids)


def step_kernel(stages, micros, devices, plan, *refs):
    refs = list(refs)

    def take(amount):
        head, refs[:] = refs[:amount], refs[amount:]
        return head

    token_ids, segment_ids, target_ids = take(3)
    qv_b, out_b, in_b, gains, shifts, fin_gain, fin_bias = take(7)
    embed_h, head_h, qkv_h, out_h, in_h, down_h = take(6)
    qkv_out, out_out, in_out, down_out, embed_out, head_out, vec_out = take(7)
    side, qkv_w, out_w = take(3)
    in_w, down_w = take(4), take(4)
    instream, outb, gin, gs, proj, probs, mixed, middle, active, slope = take(10)
    lo, gmid, s_gbr, s_xl, vec, ids, frames = take(7)
    fsend, frecv, bsend, brecv, wsem = take(5)
    go = lo
    place = lax.axis_index("dp")
    stage = lax.axis_index("pipe")
    tokens, width = instream.shape[1], instream.shape[2]
    hidden_n = in_b.shape[1]
    vocab = side.shape[0]
    pairs = width // ROW
    chunk = 512
    is_first = stage == 0
    is_last = stage == stages - 1
    up = jnp.minimum(stage + 1, stages - 1)
    down = jnp.maximum(stage - 1, 0)

    def bring(index, source, target):
        return pltpu.make_async_copy(source, target, wsem.at[index])

    weights = [bring(1, qkv_h, qkv_w), bring(2, out_h, out_w)]
    for c in range(4):
        lanes = pl.ds(c * chunk, chunk)
        weights.append(bring(3 + c, in_h.at[:, :, :, lanes], in_w[c]))
        weights.append(bring(7 + c, down_h.at[c], down_w[c]))

    @pl.when(is_first)
    def _():
        bring(0, embed_h, side).start()

    for copy in weights:
        copy.start()

    @pl.when(is_last)
    def _():
        bring(0, head_h, side).start()

    barrier = pltpu.get_barrier_semaphore()

    def greet(offset, carry):
        peer = lax.rem(place + offset, devices)
        pl.semaphore_signal(barrier, inc=1, device_id={"dp": peer}, device_id_type=MESH)
        return carry

    def greet_stage(offset, carry):
        peer = lax.rem(stage + offset, stages)
        pl.semaphore_signal(barrier, inc=1, device_id={"pipe": peer}, device_id_type=MESH)
        return carry

    lax.fori_loop(1, devices, greet, 0)
    lax.fori_loop(1, stages, greet_stage, 0)

    def whole(part):
        return part[...].reshape(width, width)

    vec[...] = jnp.zeros_like(vec)
    rows_n, seq = token_ids.shape
    for index, member in enumerate((token_ids, segment_ids, target_ids)):
        ids[index] = jnp.full(ids.shape[1:], 4.0 if index == 1 else -1.0, F32)
        ids[index, 0:rows_n, 0:seq] = member[...].astype(F32)
    at_query = lax.broadcasted_iota(jnp.int32, (ROW, ROW), 1)
    at_key = lax.broadcasted_iota(jnp.int32, (ROW, ROW), 0)
    frames[...] = jnp.where(at_key < ((at_query * 43) // 256) * FRAME + FRAME, 1.0, 0.0)

    def column(index, row):
        values = jnp.broadcast_to(ids[index, pl.ds(row, 1), :], (8, ROW))
        return values.T[:, 0:1]

    def hot_rows(index, m):
        parts = [column(index, m * GROUP + r) for r in range(GROUP)]
        values = jnp.concatenate(parts, axis=0)
        places = lax.broadcasted_iota(jnp.int32, (tokens, vocab), 1).astype(F32)
        return values, jnp.where(values == places, 1.0, 0.0)

    def forward_copy(m):
        return pltpu.make_async_remote_copy(
            src_ref=outb.at[m],
            dst_ref=instream.at[m],
            send_sem=fsend.at[m],
            recv_sem=frecv.at[m],
            device_id={"pipe": up},
            device_id_type=MESH,
        )

    def backward_copy(m):
        return pltpu.make_async_remote_copy(
            src_ref=gs.at[m],
            dst_ref=gin.at[m],
            send_sem=bsend.at[m],
            recv_sem=brecv.at[m],
            device_id={"pipe": down},
            device_id_type=MESH,
        )

    @pl.when(is_first | is_last)
    def _():
        bring(0, embed_h, side).wait()

    for copy in weights:
        copy.wait()
    pl.semaphore_wait(barrier, devices - 1 + stages - 1)

    lane_low = lax.broadcasted_iota(jnp.int32, (ROW, ROW), 1) < ROW // 2

    def forward(m):
        @pl.when(is_first)
        def _():
            hot = hot_rows(0, m)[1].astype(BF16)
            instream[m] = dot(hot, side[...]).astype(BF16)

        @pl.when(jnp.logical_not(is_first))
        def _():
            forward_copy(m).wait_recv()

        normal, _ = normalise(instream[m].astype(F32))
        low = (normal * gains[0:1, :] + shifts[0:1, :]).astype(BF16)
        queries = dot(low, qkv_w[:, 0:width]) + qv_b[0:1, :]
        proj[m, :, 0:width] = (queries * (ROW // 2) ** -0.5).astype(BF16)
        proj[m, :, width : 2 * width] = dot(low, qkv_w[:, width : 2 * width]).astype(BF16)
        proj[m, :, 2 * width : 3 * width] = (
            dot(low, qkv_w[:, 2 * width : 3 * width]) + qv_b[1:2, :]
        ).astype(BF16)
        masks, scores = [], []
        for r in range(GROUP):
            rows = slice(r * ROW, (r + 1) * ROW)
            kinds = lax.broadcasted_iota(jnp.int32, (16, ROW), 0).astype(F32)
            member = jnp.where(ids[1, pl.ds(m * GROUP + r, 1), :] == kinds, 1.0, 0.0).astype(BF16)
            mask = jnp.where(dot_tn(member, member) * frames[...] > 0.5, 0.0, MASKED)
            masks.append(jnp.concatenate([mask, mask], axis=1))
            for p in range(pairs):
                q = stack_pair(proj[m, rows, p * ROW : (p + 1) * ROW], lane_low)
                k = proj[m, rows, width + p * ROW : width + (p + 1) * ROW]
                scores.append(dot_nt(k, q))

        def mix(unit):
            r, p = unit // pairs, unit % pairs
            rows = slice(r * ROW, (r + 1) * ROW)
            v = proj[m, rows, 2 * width + p * ROW : 2 * width + (p + 1) * ROW]
            both = dot_tn(probs[m, unit // 2, unit % 2], v)
            mixed[m, rows, p * ROW : (p + 1) * ROW] = join_pair(both, lane_low).astype(BF16)

        for unit in range(GROUP * pairs):
            masked = scores[unit] + masks[unit // pairs]
            expo = jnp.exp(masked - jnp.max(masked, axis=0, keepdims=True))
            total = jnp.sum(expo, axis=0, keepdims=True)
            probs[m, unit // 2, unit % 2] = (expo * (1.0 / total)).astype(BF16)
            if unit:
                mix(unit - 1)
        mix(GROUP * pairs - 1)
        mid = instream[m].astype(F32) + (dot(mixed[m], out_w[...]) + out_b[0:1, :])
        middle[m] = mid
        normal2, _ = normalise(mid)
        low2 = (normal2 * gains[1:2, :] + shifts[1:2, :]).astype(BF16)
        parts = hidden_n // chunk

        def spread(c):
            return dot(low2, whole(in_w[c]))

        total, ahead = None, spread(0)
        for c in range(parts):
            cols = slice(c * chunk, (c + 1) * chunk)
            hid = ahead + in_b[0:1, cols]
            if c + 1 < parts:
                ahead = spread(c + 1)
            square = hid * hid
            tan = jnp.tanh(hid * (GELU_A + (GELU_A * GELU_B) * square))
            half = 0.5 + 0.5 * tan
            act = (hid * half).astype(BF16)
            active[m, :, cols] = act
            rise = (1.0 - tan * tan) * (0.5 * GELU_A + (1.5 * GELU_A * GELU_B) * square)
            slope[m, :, cols] = (half + hid * rise).astype(BF16)
            term = dot(act, whole(down_w[c]))
            total = term if total is None else total + term
        lo[...] = middle[m] + (total + out_b[1:2, :])

        @pl.when(jnp.logical_not(is_last))
        def _():
            outb[m] = lo[...].astype(BF16)
            forward_copy(m).start()

    def head(m):
        normal, scale = normalise(lo[...])
        outb[m] = (normal * fin_gain[...] + fin_bias[...]).astype(BF16)
        logits = dot_nt(outb[m], side[...])
        top = jnp.max(logits, axis=-1, keepdims=True)
        expo = jnp.exp(logits - top)
        total = jnp.sum(expo, axis=-1, keepdims=True)
        target, hot = hot_rows(2, m)
        grad_logits = jnp.where(target >= 0.0, expo * (1.0 / total) - hot, 0.0).astype(BF16)
        s_xl[m] = grad_logits
        grad_final = dot(grad_logits, side[...])
        vec[V_FINAL_GAIN : V_FINAL_GAIN + 1, :] += column_sum(grad_final * normal)
        vec[V_FINAL_BIAS : V_FINAL_BIAS + 1, :] += column_sum(grad_final)
        go[...] = norm_backward(grad_final, normal, scale, fin_gain[...])

    def backward(m):
        @pl.when(jnp.logical_not(is_last))
        def _():
            backward_copy(m).wait_recv()
            go[...] = gin[m].astype(F32)

        gres = go[...].astype(BF16)
        gin[m] = gres
        parts = hidden_n // chunk

        def spread(c):
            return dot_nt(gres, whole(down_w[c]))

        total, ahead = None, spread(0)
        for c in range(parts):
            cols = slice(c * chunk, (c + 1) * chunk)
            gact = ahead
            if c + 1 < parts:
                ahead = spread(c + 1)
            ghid = (gact * slope[m, :, cols].astype(F32)).astype(BF16)
            slope[m, :, cols] = ghid
            term = dot_nt(ghid, whole(in_w[c]))
            total = term if total is None else total + term
        normal2, scale2 = normalise(middle[m])
        vec[V_GAIN2 : V_GAIN2 + 1, :] += column_sum(total * normal2)
        vec[V_SHIFT2 : V_SHIFT2 + 1, :] += column_sum(total)
        gmid[...] = go[...] + norm_backward(total, normal2, scale2, gains[1:2, :])
        gbr = gmid[...].astype(BF16)
        s_gbr[m] = gbr
        gmix = dot_nt(gbr, out_w[...]).astype(BF16)
        grads = []
        for r in range(GROUP):
            rows = slice(r * ROW, (r + 1) * ROW)
            for p in range(pairs):
                gm = stack_pair(gmix[rows, p * ROW : (p + 1) * ROW], lane_low)
                vlanes = slice(2 * width + p * ROW, 2 * width + (p + 1) * ROW)
                grads.append(dot_nt(proj[m, rows, vlanes], gm))
                unit = r * pairs + p
                proj[m, rows, vlanes] = dot(probs[m, unit // 2, unit % 2], gm).astype(BF16)

        def pull(unit, gsc):
            r, p = unit // pairs, unit % pairs
            rows = slice(r * ROW, (r + 1) * ROW)
            lanes = slice(p * ROW, (p + 1) * ROW)
            klanes = slice(width + p * ROW, width + (p + 1) * ROW)
            q = stack_pair(proj[m, rows, lanes], lane_low)
            gq = join_pair(dot_tn(gsc, proj[m, rows, klanes]), lane_low) * (ROW // 2) ** -0.5
            gk = dot(gsc, q)
            proj[m, rows, klanes] = gk.astype(BF16)
            proj[m, rows, lanes] = gq.astype(BF16)

        waiting = None
        for unit in range(GROUP * pairs):
            weights = probs[m, unit // 2, unit % 2].astype(F32)
            inner = jnp.sum(weights * grads[unit], axis=0, keepdims=True)
            gsc = (weights * (grads[unit] - inner)).astype(BF16)
            if waiting is not None:
                pull(unit - 1, waiting)
            waiting = gsc
        pull(GROUP * pairs - 1, waiting)
        gproj = proj[m]
        gnormed = dot_nt(gproj, qkv_w[...])
        normal, scale = normalise(instream[m].astype(F32))
        vec[V_GAIN1 : V_GAIN1 + 1, :] += column_sum(gnormed * normal)
        vec[V_SHIFT1 : V_SHIFT1 + 1, :] += column_sum(gnormed)
        gs[m] = (gmid[...] + norm_backward(gnormed, normal, scale, gains[0:1, :])).astype(BF16)

        @pl.when(jnp.logical_not(is_first))
        def _():
            backward_copy(m).start()

    def tick(t, carry):
        m_forward = t - stage
        m_backward = t - (2 * (stages - 1) - stage)

        @pl.when((m_forward >= 0) & (m_forward < micros))
        def _():
            forward(m_forward)

        @pl.when((m_backward >= 0) & (m_backward < micros))
        def _():
            @pl.when(is_last)
            def _():
                head(m_backward)

            backward(m_backward)

        return carry

    lax.fori_loop(0, micros + 2 * (stages - 1), tick, 0)

    embed_stage = stages - 2
    is_extra = (stage == embed_stage) | is_last
    dims = line_dims(devices)
    turned_left = qkv_w
    mats = {
        "mixed": mixed,
        "active": active,
        "gres": gin,
        "ghid": slope,
        "gbr": s_gbr,
        "gproj": proj,
    }

    def mat(name, lanes=slice(None)):
        value = mats[name][:, :, lanes]
        return value.reshape(micros * tokens, value.shape[2])

    where = [lax.rem(place // stride, size) for size, stride in dims]

    def identity(size):
        here = lax.broadcasted_iota(jnp.int32, (size, size), 0)
        there = lax.broadcasted_iota(jnp.int32, (size, size), 1)
        return jnp.where(here == there, 1.0, 0.0).astype(BF16)

    held = []

    def turn(name):
        if held[-1:] == [name]:
            return
        held.append(name)
        unit = identity(256)
        if name in ("normed", "normed2"):
            row = 0 if name == "normed" else 1
            source = instream if name == "normed" else middle
            for m in range(micros):
                normal, _ = normalise(source[m].astype(F32))
                again = (normal * gains[row : row + 1, :] + shifts[row : row + 1, :]).astype(BF16)
                for q in range(width // 256):
                    part = dot_nt(unit, again[:, q * 256 : (q + 1) * 256])
                    turned_left[q * 256 : (q + 1) * 256, m * tokens : (m + 1) * tokens] = part.astype(BF16)
            return
        for q in range(width // 256):
            part = dot_nt(unit, mat(name, slice(q * 256, (q + 1) * 256)))
            turned_left[q * 256 : (q + 1) * 256, :] = part.astype(BF16)

    bits = devices.bit_length() - 1
    vec_send, vec_recv = take(2)
    vec_sems = take(2)

    def vec_copy(k):
        peer = jnp.bitwise_xor(place, 1 << k)
        return pltpu.make_async_remote_copy(
            src_ref=vec_send.at[k],
            dst_ref=vec_recv.at[k],
            send_sem=vec_sems[0].at[k],
            recv_sem=vec_sems[1].at[k],
            device_id={"dp": peer},
            device_id_type=MESH,
        )

    def vec_step(k):
        def run():
            if k == 0:
                vec_send[0] = vec[...]
                ones = jnp.ones((16, micros * tokens), BF16)
                for name, start, row in (
                    ("gproj", 0, V_QUERY),
                    ("gproj", 2 * width, V_VALUE),
                    ("gbr", 0, V_BRANCH),
                    ("gres", 0, V_RESULT),
                ):
                    part = dot(ones, mat(name, slice(start, start + width)))
                    vec_send[0, row : row + 1, :] = part[0:1, :]
                for q in range(hidden_n // width):
                    part = dot(ones, mat("ghid", slice(q * width, (q + 1) * width)))
                    vec_send[0, V_HIDDEN + q : V_HIDDEN + q + 1, :] = part[0:1, :]
            else:
                vec_copy(k - 1).wait_recv()
                vec_send[k] = vec_send[k - 1] + vec_recv[k - 1]
            if k < bits:
                vec_copy(k).start()

        return run

    final_send, final_recv = take(2)
    final_sems = take(2)

    def final_copy(offset):
        peer = lax.rem(stages - 1 + offset, stages)
        return pltpu.make_async_remote_copy(
            src_ref=final_send,
            dst_ref=final_recv,
            send_sem=final_sems[0].at[offset],
            recv_sem=final_sems[1].at[0],
            device_id={"pipe": peer},
            device_id_type=MESH,
        )

    def vec_last():
        vec_step(bits)()
        vec_out[...] = vec_send[bits]

        @pl.when(stage == stages - 1)
        def _():
            final_send[...] = vec_send[bits, 8:16, :]
            for offset in range(1, stages):
                final_copy(offset).start()

    def vec_finish():
        @pl.when(stage != stages - 1)
        def _():
            final_copy(1).wait_recv()
            vec_out[V_FINAL_GAIN : V_FINAL_BIAS + 1, :] = final_recv[
                V_FINAL_GAIN - 8 : V_FINAL_BIAS - 7, :
            ]

    def vec_drain():
        for k in range(bits):
            vec_copy(k).wait_send()

        @pl.when(stage == stages - 1)
        def _():
            for offset in range(1, stages):
                final_copy(offset).wait_send()

    def ship():
        return pltpu.make_async_remote_copy(
            src_ref=s_xl.at[pl.ds(0, 2)],
            dst_ref=s_xl.at[pl.ds(0, 2)],
            send_sem=ship_sem.at[0],
            recv_sem=ship_sem.at[1],
            device_id={"pipe": embed_stage},
            device_id_type=MESH,
        )

    def ship_embed():
        rows, half = vocab // stages, width // 2

        @pl.when(is_first)
        def _():
            right = gs[...].reshape(micros * tokens, width)
            for p in range(stages):
                here = lax.broadcasted_iota(jnp.int32, (rows, ROW), 0).astype(F32) + p * rows
                hot = [
                    jnp.where(ids[0, r : r + 1, :] == here, 1.0, 0.0).astype(BF16) for r in range(rows_n)
                ]
                part = dot(jnp.concatenate(hot, axis=1), right).astype(BF16)
                for k in range(2):
                    s_xl[k, :, p * half : (p + 1) * half] = part[:, k * half : (k + 1) * half]
            ship().start()

    extra_sum, extra_send_sem, extra_recv_sem, last_sum, ship_sem = take(5)
    share = embed_out.shape[0]

    def extra_copy(source, offset, target):
        peer = lax.rem(source + offset, stages)
        return pltpu.make_async_remote_copy(
            src_ref=extra_sum.at[pl.ds(pl.multiple_of(peer * share, share), share)],
            dst_ref=target,
            send_sem=extra_send_sem.at[offset],
            recv_sem=extra_recv_sem.at[0 if source == embed_stage else 1],
            device_id={"pipe": peer},
            device_id_type=MESH,
        )

    def chunk_steps(kind, c, block, turned):
        order = list(range(len(dims)))
        if turned:
            order.reverse()
        if kind == "down":
            full = probs.at[c]
        elif kind == "extra":
            full = probs.at[4 + c]
        else:
            full = (down_w + in_w)[{"out": 0, "in": 1, "qkv": 5}[kind] + c]

        def compute():
            if kind == "down":
                if c % 2 == 1:
                    return
                turn("gres")
                half = width // 2
                lines = slice((c // 2) * half, (c // 2 + 1) * half)
                parts = dot(turned_left[lines, :], mat("active")).astype(BF16)
                depth = hidden_n // devices
                unit = identity(depth)
                for d in range(devices):
                    back = dot_nt(unit, parts[:, d * depth : (d + 1) * depth]).astype(BF16)
                    for k in range(2):
                        piece = back[:, k * ROW : (k + 1) * ROW]
                        piece = jnp.concatenate([piece[: depth // 2], piece[depth // 2 :]], axis=1)
                        probs[(c + k,) + split(d)] = piece
            elif kind == "extra":
                if c == 1:
                    return
                rows = vocab // stages
                share = rows // devices
                half = width // 2

                def fill(left, right):
                    for p in range(stages):
                        part = left(p, right).astype(BF16).reshape(devices, share, width)
                        for d in range(devices):
                            for k in range(2):
                                lines = slice(p * share, (p + 1) * share)
                                probs[(4 + k,) + split(d) + (lines,)] = part[
                                    d, :, k * half : (k + 1) * half
                                ]

                def flat(ref):
                    return ref[...].reshape(micros * tokens, ref.shape[2])

                @pl.when(stage == embed_stage)
                def _():
                    ship().wait_recv()
                    for d in range(devices):
                        for k in range(2):
                            for p in range(stages):
                                lines = slice(p * share, (p + 1) * share)
                                probs[(4 + k,) + split(d) + (lines,)] = s_xl[
                                    k, d * share : (d + 1) * share, p * half : (p + 1) * half
                                ]

                @pl.when(is_last)
                def _():
                    def soft_part(p, right):
                        left = s_xl[:, :, p * rows : (p + 1) * rows]
                        return dot_tn(left.reshape(micros * tokens, rows), right)

                    fill(soft_part, flat(outb))
            else:
                left, right = {
                    "in": ("normed2", "ghid"),
                    "out": ("mixed", "gbr"),
                    "qkv": ("normed", "gproj"),
                }[kind]
                turn(left)
                part = dot(turned_left[...], mat(right, slice(c * width, (c + 1) * width)))
                part = part.astype(BF16).reshape((devices,) + block)
                for d in range(devices):
                    full[split(d)] = part[d]

        def split(d):
            return tuple((d // stride) % size for size, stride in reversed(dims))

        steps = [[compute]]
        for at, phase in enumerate(order):
            size = dims[phase][0]
            buffers = take(3)
            done = order[:at]
            last = at == len(order) - 1
            steps[-1].append(functools.partial(line_step, phase, size, 1, full, buffers, done))
            for t in range(2, size):
                steps.append([functools.partial(line_step, phase, size, t, full, buffers, done)])
            drains.append((kind, functools.partial(line_drain, phase, size, full, buffers, done)))
            steps.append([functools.partial(line_final, kind, c, phase, size, full, buffers, done, last)])
        if kind == "extra":
            steps = [[gated([part]) for part in step] for step in steps]
        return steps

    def gated(step):
        def run():
            @pl.when(is_extra)
            def _():
                for part in step:
                    part()

        return run

    def block_of(full, phase, j, done):
        spot = [slice(None)] * len(dims)
        for other in done:
            spot[len(dims) - 1 - other] = where[other]
        spot[len(dims) - 1 - phase] = j
        return full.at[tuple(spot)]

    def line_copy(phase, size, t, side, full, buffers, done):
        recv, ssem, rsem = buffers
        i = where[phase]
        stride = dims[phase][1]
        if side == 0:
            j, peer = size - t + i, place + jnp.where(i < size - 1, stride, 0)
        else:
            j, peer = t - size + i, place - jnp.where(i > 0, stride, 0)
        return pltpu.make_async_remote_copy(
            src_ref=block_of(full, phase, jnp.clip(j, 0, size - 1), done),
            dst_ref=recv.at[0 if size == 2 else side, t - 1],
            send_sem=ssem.at[side, t - 1],
            recv_sem=rsem.at[side, t - 1],
            device_id={"dp": peer},
            device_id_type=MESH,
        )

    def sends(i, size, t, side):
        return (i <= t - 1) if side == 0 else (i >= size - t)

    def line_step(phase, size, t, full, buffers, done):
        i = where[phase]
        for side in range(2):
            at_end = (i == 0) if side == 0 else (i == size - 1)
            j = size - t + i if side == 0 else t - size + i
            j = jnp.clip(j, 0, size - 1)

            @pl.when(sends(i, size, t, side))
            def _():
                if t > 1:
                    @pl.when(jnp.logical_not(at_end))
                    def _():
                        line_copy(phase, size, t - 1, side, full, buffers, done).wait_recv()
                        own = block_of(full, phase, j, done)
                        got = buffers[0][0 if size == 2 else side, t - 2]
                        own[...] = (own[...].astype(F32) + got.astype(F32)).astype(BF16)

                line_copy(phase, size, t, side, full, buffers, done).start()

    def line_final(kind, c, phase, size, full, buffers, done, last):
        i = where[phase]
        own = block_of(full, phase, i, done)
        total = own
        if last:
            lanes = slice(c * width, (c + 1) * width)
            slots = {
                "qkv": lambda: qkv_out.at[:, lanes],
                "in": lambda: in_out.at[:, lanes],
                "out": lambda: out_out,
                "down": lambda: last_sum,
                "extra": lambda: extra_sum.at[:, c * (width // 2) : (c + 1) * (width // 2)],
            }
            total = slots[kind]()
        lower, upper = i > 0, i < size - 1

        def arrived(side):
            line_copy(phase, size, size - 1, side, full, buffers, done).wait_recv()
            return buffers[0][0 if size == 2 else side, size - 2].astype(F32)

        @pl.when(lower & upper)
        def _():
            total[...] = (own[...].astype(F32) + arrived(0) + arrived(1)).astype(total.dtype)

        @pl.when(lower & jnp.logical_not(upper))
        def _():
            total[...] = (own[...].astype(F32) + arrived(0)).astype(total.dtype)

        @pl.when(jnp.logical_not(lower))
        def _():
            total[...] = (own[...].astype(F32) + arrived(1)).astype(total.dtype)

        if last and kind == "down":
            deep = down_out.shape[0] // 2
            lanes = slice(c * ROW, (c + 1) * ROW)
            down_out[0:deep, lanes] = last_sum[:, 0:ROW]
            down_out[deep : 2 * deep, lanes] = last_sum[:, ROW : 2 * ROW]
        if last and kind == "extra" and c == 1:
            for source_stage, out in ((embed_stage, embed_out), (stages - 1, head_out)):
                @pl.when(stage == source_stage)
                def _():
                    for offset in range(1, stages):
                        extra_copy(source_stage, offset, extra_recv[0 if source_stage == embed_stage else 1]).start()
                    out[...] = extra_sum[source_stage * share : (source_stage + 1) * share, :]

    def line_drain(phase, size, full, buffers, done):
        i = where[phase]
        for side in range(2):
            for t in range(1, size):
                @pl.when(sends(i, size, t, side))
                def _():
                    line_copy(phase, size, t, side, full, buffers, done).wait_send()

    extra_recv = take(2)
    drains = []
    chains = [chunk_steps(*item) for item in plan]
    depth = len(chains[0])
    vec_chain = [vec_step(k) for k in range(bits)] + [vec_last]
    starts, first, extra_rounds = [], 0, iter((1, 3, 5, 7))
    for item in plan:
        if item[0] == "extra":
            starts.append(7 + item[1])
        elif item[3]:
            starts.append(next(extra_rounds))
        else:
            starts.append(first)
            first += 1
    loaded_at = max(start for start, item in zip(starts, plan) if item[0] == "qkv" and item[1] == 0)
    for r in range(max(starts) + depth):
        for d in [0] + list(range(depth - 1, 0, -1)):
            for start, chain in zip(starts, chains):
                if r - start != d:
                    continue
                for part in chain[d]:
                    part()
            if r == 1 and d == 0:
                ship_embed()
        if 0 <= r - loaded_at < len(vec_chain):
            vec_chain[r - loaded_at]()
    vec_finish()
    for source_stage, out in ((embed_stage, embed_out), (stages - 1, head_out)):
        @pl.when(stage != source_stage)
        def _():
            got = extra_recv[0 if source_stage == embed_stage else 1]
            extra_copy(source_stage, 1, got).wait_recv()
            out[...] = got[...]

        @pl.when(stage == source_stage)
        def _():
            for offset in range(1, stages):
                extra_copy(source_stage, offset, extra_recv[0]).wait_send()

    vec_drain()
    for kind, drain in drains:
        if kind == "extra":
            gated([drain])()
        else:
            drain()

    @pl.when(is_first)
    def _():
        ship().wait_send()

    for m in range(micros):
        @pl.when(jnp.logical_not(is_last))
        def _():
            forward_copy(m).wait_send()

        @pl.when(jnp.logical_not(is_first))
        def _():
            backward_copy(m).wait_send()


def step_plan(width, hid, vocab, stages, devices):
    plan = []
    for kind, c, _, turned in chunk_plan(width, hid, vocab, stages, devices):
        wide = kind in ("down", "extra")
        plan.append((kind, c, (ROW, 2 * ROW) if wide else (width // devices, width), turned))
    extra = [item for item in plan if item[0] == "extra"]
    rest = [item for item in plan if item[0] != "extra"]
    return rest + extra


def run_step(stages, devices, token_ids, segment_ids, target_ids, params):
    embed, qkv_w, qv_b, out_w, out_b, in_w, in_b, down_w, gains, shifts, fg, fb, head_w = params
    dims = line_dims(devices)
    width, hid, vocab = embed.shape[1], in_w.shape[1], head_w.shape[0]
    tokens = GROUP * ROW
    micros = token_ids.shape[0] // GROUP
    vmem = pl.BlockSpec(memory_space=pltpu.VMEM)
    hbm = pl.BlockSpec(memory_space=pl.ANY)
    sizes = tuple(size for size, _ in reversed(dims))
    slim = width // devices
    share = vocab // (stages * devices)
    plan = step_plan(width, hid, vocab, stages, devices)
    bits = devices.bit_length() - 1

    def scratch(lead, columns, kind=BF16):
        return pltpu.VMEM((lead, tokens, columns), kind)

    def sums(*shape):
        return pltpu.VMEM(shape, F32)

    dma = pltpu.SemaphoreType.DMA
    scratch_shapes = [
        pltpu.VMEM((vocab, width), BF16),
        pltpu.VMEM((width, 3 * width), BF16),
        pltpu.VMEM((width, width), BF16),
    ]
    scratch_shapes += [pltpu.VMEM(sizes + (slim, width), BF16)] * 8
    scratch_shapes += [
        scratch(micros, width),
        scratch(micros, width),
        scratch(micros, width),
        scratch(micros, width),
        scratch(micros, 3 * width),
        pltpu.VMEM((micros,) + sizes + (ROW, 2 * ROW), BF16),
        scratch(micros, width),
        scratch(micros, width, F32),
        scratch(micros, hid),
        scratch(micros, hid),
        sums(tokens, width),
        sums(tokens, width),
        scratch(micros, width),
        scratch(micros, vocab),
        sums(VEC_ROWS, width),
        sums(3, 16, ROW),
        sums(ROW, ROW),
        dma((micros,)),
        dma((micros,)),
        dma((micros,)),
        dma((micros,)),
        dma((11,)),
        sums(bits + 1, VEC_ROWS, width),
        sums(bits, VEC_ROWS, width),
        dma((bits,)),
        dma((bits,)),
        sums(8, width),
        sums(8, width),
        dma((stages,)),
        dma((1,)),
        sums(stages * share, width),
        dma((stages,)),
        dma((2,)),
        sums(ROW, 2 * ROW),
        dma((2,)),
        sums(share, width),
        sums(share, width),
    ]
    for _, _, block, turned in plan:
        remain = list(reversed(dims))
        for size, stride in dims[::-1] if turned else dims:
            remain.remove((size, stride))
            piece = tuple(other for other, _ in remain) + block
            scratch_shapes.append(pltpu.VMEM((1 if size == 2 else 2, size - 1) + piece, BF16))
            scratch_shapes += [dma((2, size - 1))] * 2

    def result(*shape):
        return jax.ShapeDtypeStruct(shape, F32)

    return pl.pallas_call(
        functools.partial(step_kernel, stages, micros, devices, plan),
        out_shape=[
            result(slim, 3 * width),
            result(slim, width),
            result(slim, hid),
            result(hid // devices, width),
            result(share, width),
            result(share, width),
            result(VEC_ROWS, width),
        ],
        in_specs=[vmem] * 10 + [hbm] * 6,
        out_specs=[vmem] * 7,
        scratch_shapes=scratch_shapes,
        compiler_params=pltpu.CompilerParams(
            collective_id=2, has_side_effects=True, vmem_limit_bytes=63 * 1024 * 1024
        ),
        name="step",
    )(
        token_ids,
        segment_ids,
        target_ids,
        qv_b,
        out_b,
        in_b,
        gains,
        shifts,
        fg,
        fb,
        embed,
        head_w,
        qkv_w,
        out_w,
        in_w.reshape(sizes + (slim, hid)),
        down_w.reshape((hid // width,) + sizes + (slim, width)),
    )


def finish_kernel(devices, embed_g, qkv_g, out_g, in_g, down_g, head_g, vec, *outs):
    place = lax.axis_index("dp")
    width = vec.shape[1]
    (embed_o, qkv_o, qv_o, out_o, outb_o, in_o, inb_o, down_o, gain_o, shift_o, fg_o, fb_o, head_o) = outs
    embed_o[...] = embed_g[...]
    head_o[...] = head_g[...]
    for source, target in ((qkv_g, qkv_o), (out_g, out_o), (in_g, in_o), (down_g, down_o)):
        target[0] = source[...]
    lanes = width // devices
    turned = pltpu.roll(vec[0:8, :], lax.rem(width - place * lanes, width), 1)
    for row, out in ((V_QUERY, qv_o), (V_BRANCH, outb_o), (V_GAIN1, gain_o), (V_SHIFT1, shift_o)):
        out[0] = turned[row : row + 2, 0:lanes]
    share = inb_o.shape[1]
    first = place * share
    row = vec[pl.ds(V_HIDDEN + first // width, 1), :]
    wide = jnp.broadcast_to(row, (8, width))
    inb_o[...] = pltpu.roll(wide, lax.rem(width - lax.rem(first, width), width), 1)[0:1, 0:share]
    fg_o[...] = vec[V_FINAL_GAIN : V_FINAL_GAIN + 1, :]
    fb_o[...] = vec[V_FINAL_BIAS : V_FINAL_BIAS + 1, :]


def run_finish(devices, embed_g, qkv_g, out_g, in_g, down_g, head_g, vec):
    vmem = pl.BlockSpec(memory_space=pltpu.VMEM)
    width = vec.shape[1]
    lanes = width // devices

    def shape(*sizes):
        return jax.ShapeDtypeStruct(sizes, F32)

    pair = shape(1, 2, lanes)
    return pl.pallas_call(
        functools.partial(finish_kernel, devices),
        out_shape=[
            shape(*embed_g.shape),
            shape(1, *qkv_g.shape),
            pair,
            shape(1, *out_g.shape),
            pair,
            shape(1, *in_g.shape),
            shape(1, in_g.shape[1] // devices),
            shape(1, *down_g.shape),
            pair,
            pair,
            shape(1, width),
            shape(1, width),
            shape(*head_g.shape),
        ],
        in_specs=[vmem] * 7,
        out_specs=[vmem] * 13,
        name="finish",
    )(embed_g, qkv_g, out_g, in_g, down_g, head_g, vec)


def on_device(
    token_ids,
    segment_ids,
    target_ids,
    embed_table,
    qkv_weight,
    qv_bias,
    out_weight,
    out_biases,
    ff_in,
    ff_in_bias,
    ff_out,
    norm_gains,
    norm_biases,
    final_gain,
    final_bias,
    head_weight,
):
    stages = lax.axis_size("pipe")
    devices = lax.axis_size("dp")
    params = (
        embed_table,
        qkv_weight[0],
        qv_bias[0],
        out_weight[0],
        out_biases[0],
        ff_in[0],
        ff_in_bias,
        ff_out[0],
        norm_gains[0],
        norm_biases[0],
        final_gain[None],
        final_bias[None],
        head_weight,
    )
    if devices == 8:
        grads = run_step(stages, devices, token_ids, segment_ids, target_ids, params)
    else:
        *saved, vec = run_pipeline(stages, token_ids, segment_ids, target_ids, params)
        grads = run_gradients(stages, devices, saved, vec, token_ids)
    qkv_g, out_g, in_g, down_g, embed_g, head_g, sums = grads
    done = list(run_finish(devices, embed_g, qkv_g, out_g, in_g, down_g, head_g, sums))
    done[10], done[11] = done[10][0], done[11][0]
    return tuple(done)


def solution(mesh):
    layer3 = P("pipe", None, None)
    return jax.shard_map(
        on_device,
        mesh=mesh,
        in_specs=(
            P("dp", None),
            P("dp", None),
            P("dp", None),
            P(),
            layer3,
            layer3,
            layer3,
            layer3,
            layer3,
            P("pipe", None),
            layer3,
            layer3,
            layer3,
            P(),
            P(),
            P(),
        ),
        out_specs=(
            P(("pipe", "dp"), None),
            P("pipe", "dp", None),
            P("pipe", None, "dp"),
            P("pipe", "dp", None),
            P("pipe", None, "dp"),
            P("pipe", "dp", None),
            P("pipe", "dp"),
            P("pipe", "dp", None),
            P("pipe", None, "dp"),
            P("pipe", None, "dp"),
            P(),
            P(),
            P(("pipe", "dp"), None),
        ),
        check_vma=False,
    )
```

```python
import functools

import jax
import jax.numpy as jnp
from jax import lax
from jax.experimental import pallas as pl
from jax.experimental.pallas import tpu as pltpu
from jax.sharding import PartitionSpec as P

HEADS = 8
FRAME = 6
ROW = 128
GROUP = 2
MASKED = -1e30
GELU_A = 0.7978845608
GELU_B = 0.044715
MESH = pl.DeviceIdType.MESH
F32 = jnp.float32
BF16 = jnp.bfloat16

VEC_ROWS = 16
V_QUERY, V_VALUE, V_BRANCH, V_RESULT, V_GAIN1, V_GAIN2, V_SHIFT1, V_SHIFT2 = range(8)
V_HIDDEN = 8
V_FINAL_GAIN, V_FINAL_BIAS = 12, 13


def dot(a, b):
    return lax.dot_general(a, b, (((1,), (0,)), ((), ())), preferred_element_type=F32)


def dot_nt(a, b):
    return lax.dot_general(a, b, (((1,), (1,)), ((), ())), preferred_element_type=F32)


def dot_tn(a, b):
    return lax.dot_general(a, b, (((0,), (0,)), ((), ())), preferred_element_type=F32)


def normalise(values):
    centre = jnp.mean(values, axis=-1, keepdims=True)
    centered = values - centre
    spread = jnp.mean(centered * centered, axis=-1, keepdims=True)
    scale = lax.rsqrt(spread + 1e-05)
    return centered * scale, scale


def norm_backward(grad, normal, scale, gain):
    grad_n = grad * gain
    mean_grad = jnp.mean(grad_n, axis=-1, keepdims=True)
    mean_proj = jnp.mean(grad_n * normal, axis=-1, keepdims=True)
    return scale * (grad_n - mean_grad - normal * mean_proj)


def column_sum(values):
    return jnp.sum(values, axis=0, keepdims=True)


def stack_pair(pair, low_lanes):
    zero = jnp.zeros_like(pair)
    return jnp.concatenate(
        [jnp.where(low_lanes, pair, zero), jnp.where(low_lanes, zero, pair)], axis=0
    )


def join_pair(stacked, low_lanes):
    half = stacked.shape[0] // 2
    return jnp.where(low_lanes, stacked[:half], stacked[half:])


def pipeline_kernel(
    stages,
    micros,
    token_ids,
    segment_ids,
    target_ids,
    embed,
    qkv_w,
    qv_b,
    out_w,
    out_b,
    in_w,
    in_b,
    down_w,
    gains,
    shifts,
    fin_gain,
    fin_bias,
    head_w,
    normed_o,
    mixed_o,
    normed2_o,
    active_o,
    gres_o,
    ghid_o,
    gbr_o,
    gproj_o,
    xl_o,
    xr_o,
    vec,
    instream,
    outb,
    gin,
    gs,
    normed,
    proj,
    probs,
    mixed,
    middle,
    normed2,
    active,
    slope,
    lo,
    go,
    gmid,
    s_gres,
    s_ghid,
    s_gbr,
    s_gproj,
    s_xl,
    ids,
    frames,
    fsend,
    frecv,
    bsend,
    brecv,
    osem,
):
    stage = lax.axis_index("pipe")
    tokens, width = instream.shape[1], instream.shape[2]
    hidden_n = in_b.shape[1]
    vocab = head_w.shape[0]
    pairs = width // ROW
    chunk = 512
    is_first = stage == 0
    is_last = stage == stages - 1
    up = jnp.minimum(stage + 1, stages - 1)
    down = jnp.maximum(stage - 1, 0)

    barrier = pltpu.get_barrier_semaphore()

    @pl.when(jnp.logical_not(is_first))
    def _():
        pl.semaphore_signal(barrier, inc=1, device_id={"pipe": down}, device_id_type=MESH)

    @pl.when(jnp.logical_not(is_last))
    def _():
        pl.semaphore_signal(barrier, inc=1, device_id={"pipe": up}, device_id_type=MESH)

    pl.semaphore_wait(barrier, jnp.where(is_first | is_last, 1, 2))
    vec[...] = jnp.zeros_like(vec)
    rows_n, seq = token_ids.shape
    for index, member in enumerate((token_ids, segment_ids, target_ids)):
        ids[index] = jnp.full(ids.shape[1:], 4.0 if index == 1 else -1.0, F32)
        ids[index, 0:rows_n, 0:seq] = member[...].astype(F32)
    at_query = lax.broadcasted_iota(jnp.int32, (ROW, ROW), 1)
    at_key = lax.broadcasted_iota(jnp.int32, (ROW, ROW), 0)
    frames[...] = jnp.where(at_key < ((at_query * 43) // 256) * FRAME + FRAME, 1.0, 0.0)

    def column(index, row):
        values = jnp.broadcast_to(ids[index, pl.ds(row, 1), :], (8, ROW))
        return values.T[:, 0:1]

    def hot_rows(index, m):
        parts = [column(index, m * GROUP + r) for r in range(GROUP)]
        values = jnp.concatenate(parts, axis=0)
        places = lax.broadcasted_iota(jnp.int32, (tokens, vocab), 1).astype(F32)
        return values, jnp.where(values == places, 1.0, 0.0)

    def forward_copy(m):
        return pltpu.make_async_remote_copy(
            src_ref=outb.at[m],
            dst_ref=instream.at[m],
            send_sem=fsend.at[m],
            recv_sem=frecv.at[m],
            device_id={"pipe": up},
            device_id_type=MESH,
        )

    def backward_copy(m):
        return pltpu.make_async_remote_copy(
            src_ref=gs.at[m],
            dst_ref=gin.at[m],
            send_sem=bsend.at[m],
            recv_sem=brecv.at[m],
            device_id={"pipe": down},
            device_id_type=MESH,
        )

    def save(index, src, dst, m):
        return pltpu.make_async_copy(src, dst.at[m], osem.at[index, m])

    def saves_forward(m):
        return [
            save(0, normed.at[m], normed_o, m),
            save(1, mixed.at[m], mixed_o, m),
            save(2, normed2.at[m], normed2_o, m),
            save(3, active.at[m], active_o, m),
        ]

    def saves_backward(m):
        slot = lax.rem(m, 2)
        return [
            save(4, s_gres.at[slot], gres_o, m),
            save(5, s_ghid.at[slot], ghid_o, m),
            save(6, s_gbr.at[slot], gbr_o, m),
            save(7, s_gproj.at[slot], gproj_o, m),
        ]

    def save_xl(m):
        return save(8, s_xl.at[lax.rem(m, 2)], xl_o, m)

    def put_xl(m, value):
        @pl.when(m >= 2)
        def _():
            save_xl(m - 2).wait()

        s_xl[lax.rem(m, 2)] = value
        save_xl(m).start()

    lane_low = lax.broadcasted_iota(jnp.int32, (ROW, ROW), 1) < ROW // 2

    def forward(m):
        @pl.when(is_first)
        def _():
            hot = hot_rows(0, m)[1].astype(BF16)
            instream[m] = dot(hot, embed[...]).astype(BF16)

        @pl.when(jnp.logical_not(is_first))
        def _():
            forward_copy(m).wait_recv()

        normal, _ = normalise(instream[m].astype(F32))
        normed[m] = (normal * gains[0:1, :] + shifts[0:1, :]).astype(BF16)
        low = normed[m]
        queries = dot(low, qkv_w[:, 0:width]) + qv_b[0:1, :]
        proj[m, :, 0:width] = (queries * (ROW // 2) ** -0.5).astype(BF16)
        proj[m, :, width : 2 * width] = dot(low, qkv_w[:, width : 2 * width]).astype(BF16)
        proj[m, :, 2 * width : 3 * width] = (
            dot(low, qkv_w[:, 2 * width : 3 * width]) + qv_b[1:2, :]
        ).astype(BF16)
        masks, scores = [], []
        for r in range(GROUP):
            rows = slice(r * ROW, (r + 1) * ROW)
            kinds = lax.broadcasted_iota(jnp.int32, (16, ROW), 0).astype(F32)
            member = jnp.where(ids[1, pl.ds(m * GROUP + r, 1), :] == kinds, 1.0, 0.0).astype(BF16)
            mask = jnp.where(dot_tn(member, member) * frames[...] > 0.5, 0.0, MASKED)
            masks.append(jnp.concatenate([mask, mask], axis=1))
            for p in range(pairs):
                q = stack_pair(proj[m, rows, p * ROW : (p + 1) * ROW], lane_low)
                k = proj[m, rows, width + p * ROW : width + (p + 1) * ROW]
                scores.append(dot_nt(k, q))

        def mix(unit):
            r, p = unit // pairs, unit % pairs
            rows = slice(r * ROW, (r + 1) * ROW)
            v = proj[m, rows, 2 * width + p * ROW : 2 * width + (p + 1) * ROW]
            both = dot_tn(probs[m, unit], v)
            mixed[m, rows, p * ROW : (p + 1) * ROW] = join_pair(both, lane_low).astype(BF16)

        for unit in range(GROUP * pairs):
            masked = scores[unit] + masks[unit // pairs]
            expo = jnp.exp(masked - jnp.max(masked, axis=0, keepdims=True))
            total = jnp.sum(expo, axis=0, keepdims=True)
            probs[m, unit] = (expo * (1.0 / total)).astype(BF16)
            if unit:
                mix(unit - 1)
        mix(GROUP * pairs - 1)
        mid = instream[m].astype(F32) + (dot(mixed[m], out_w[...]) + out_b[0:1, :])
        middle[m] = mid
        normal2, _ = normalise(mid)
        normed2[m] = (normal2 * gains[1:2, :] + shifts[1:2, :]).astype(BF16)
        low2 = normed2[m]
        parts = hidden_n // chunk

        def spread(c):
            return dot(low2, in_w[:, c * chunk : (c + 1) * chunk])

        total, ahead = None, spread(0)
        for c in range(parts):
            cols = slice(c * chunk, (c + 1) * chunk)
            hid = ahead + in_b[0:1, cols]
            if c + 1 < parts:
                ahead = spread(c + 1)
            square = hid * hid
            tan = jnp.tanh(hid * (GELU_A + (GELU_A * GELU_B) * square))
            half = 0.5 + 0.5 * tan
            act = (hid * half).astype(BF16)
            active[m, :, cols] = act
            rise = (1.0 - tan * tan) * (0.5 * GELU_A + (1.5 * GELU_A * GELU_B) * square)
            slope[m, :, cols] = (half + hid * rise).astype(BF16)
            term = dot(act, down_w[cols, :])
            total = term if total is None else total + term
        for copy in saves_forward(m):
            copy.start()
        lo[...] = middle[m] + (total + out_b[1:2, :])

        @pl.when(jnp.logical_not(is_last))
        def _():
            outb[m] = lo[...].astype(BF16)
            forward_copy(m).start()

    def head(m):
        normal, scale = normalise(lo[...])
        outb[m] = (normal * fin_gain[...] + fin_bias[...]).astype(BF16)
        save(9, outb.at[m], xr_o, m).start()
        logits = dot_nt(outb[m], head_w[...])
        top = jnp.max(logits, axis=-1, keepdims=True)
        expo = jnp.exp(logits - top)
        total = jnp.sum(expo, axis=-1, keepdims=True)
        target, hot = hot_rows(2, m)
        grad_logits = jnp.where(target >= 0.0, expo * (1.0 / total) - hot, 0.0).astype(BF16)
        put_xl(m, grad_logits)
        grad_final = dot(grad_logits, head_w[...])
        vec[V_FINAL_GAIN : V_FINAL_GAIN + 1, :] += column_sum(grad_final * normal)
        vec[V_FINAL_BIAS : V_FINAL_BIAS + 1, :] += column_sum(grad_final)
        go[...] = norm_backward(grad_final, normal, scale, fin_gain[...])

    def backward(m):
        slot = lax.rem(m, 2)

        @pl.when(m >= 2)
        def _():
            for copy in saves_backward(m - 2):
                copy.wait()

        @pl.when(jnp.logical_not(is_last))
        def _():
            backward_copy(m).wait_recv()
            go[...] = gin[m].astype(F32)

        s_gres[slot] = go[...].astype(BF16)
        gres = s_gres[slot]
        parts = hidden_n // chunk

        def spread(c):
            return dot_nt(gres, down_w[c * chunk : (c + 1) * chunk, :])

        total, ahead = None, spread(0)
        for c in range(parts):
            cols = slice(c * chunk, (c + 1) * chunk)
            gact = ahead
            if c + 1 < parts:
                ahead = spread(c + 1)
            ghid = (gact * slope[m, :, cols].astype(F32)).astype(BF16)
            s_ghid[slot, :, cols] = ghid
            term = dot_nt(ghid, in_w[:, cols])
            total = term if total is None else total + term
        normal2, scale2 = normalise(middle[m])
        vec[V_GAIN2 : V_GAIN2 + 1, :] += column_sum(total * normal2)
        vec[V_SHIFT2 : V_SHIFT2 + 1, :] += column_sum(total)
        gmid[...] = go[...] + norm_backward(total, normal2, scale2, gains[1:2, :])
        s_gbr[slot] = gmid[...].astype(BF16)
        gbr = s_gbr[slot]
        gmix = dot_nt(gbr, out_w[...]).astype(BF16)
        grads = []
        for r in range(GROUP):
            rows = slice(r * ROW, (r + 1) * ROW)
            for p in range(pairs):
                gm = stack_pair(gmix[rows, p * ROW : (p + 1) * ROW], lane_low)
                vlanes = slice(2 * width + p * ROW, 2 * width + (p + 1) * ROW)
                grads.append(dot_nt(proj[m, rows, vlanes], gm))
                s_gproj[slot, rows, vlanes] = dot(probs[m, r * pairs + p], gm).astype(BF16)

        def pull(unit, gsc):
            r, p = unit // pairs, unit % pairs
            rows = slice(r * ROW, (r + 1) * ROW)
            lanes = slice(p * ROW, (p + 1) * ROW)
            klanes = slice(width + p * ROW, width + (p + 1) * ROW)
            q = stack_pair(proj[m, rows, lanes], lane_low)
            s_gproj[slot, rows, klanes] = dot(gsc, q).astype(BF16)
            gq = join_pair(dot_tn(gsc, proj[m, rows, klanes]), lane_low) * (ROW // 2) ** -0.5
            s_gproj[slot, rows, lanes] = gq.astype(BF16)

        waiting = None
        for unit in range(GROUP * pairs):
            weights = probs[m, unit].astype(F32)
            inner = jnp.sum(weights * grads[unit], axis=0, keepdims=True)
            gsc = (weights * (grads[unit] - inner)).astype(BF16)
            if waiting is not None:
                pull(unit - 1, waiting)
            waiting = gsc
        pull(GROUP * pairs - 1, waiting)
        for copy in saves_backward(m):
            copy.start()
        gproj = s_gproj[slot]
        gnormed = dot_nt(gproj, qkv_w[...])
        normal, scale = normalise(instream[m].astype(F32))
        vec[V_GAIN1 : V_GAIN1 + 1, :] += column_sum(gnormed * normal)
        vec[V_SHIFT1 : V_SHIFT1 + 1, :] += column_sum(gnormed)
        gs[m] = (gmid[...] + norm_backward(gnormed, normal, scale, gains[0:1, :])).astype(BF16)

        @pl.when(is_first)
        def _():
            save(9, gs.at[m], xr_o, m).start()

        @pl.when(jnp.logical_not(is_first))
        def _():
            backward_copy(m).start()

    def tick(t, carry):
        m_forward = t - stage
        m_backward = t - (2 * (stages - 1) - stage)

        @pl.when((m_forward >= 0) & (m_forward < micros))
        def _():
            forward(m_forward)

        @pl.when((m_backward >= 0) & (m_backward < micros))
        def _():
            @pl.when(is_last)
            def _():
                head(m_backward)

            backward(m_backward)

        return carry

    lax.fori_loop(0, micros + 2 * (stages - 1), tick, 0)

    for m in range(micros):
        for copy in saves_forward(m):
            copy.wait()

        @pl.when(jnp.logical_not(is_last))
        def _():
            forward_copy(m).wait_send()

        @pl.when(jnp.logical_not(is_first))
        def _():
            backward_copy(m).wait_send()

        @pl.when(is_first)
        def _():
            save(9, gs.at[m], xr_o, m).wait()

        @pl.when(is_last)
        def _():
            save(9, outb.at[m], xr_o, m).wait()

    for m in range(max(0, micros - 2), micros):
        for copy in saves_backward(m):
            copy.wait()

        @pl.when(is_last)
        def _():
            save_xl(m).wait()


def run_pipeline(stages, token_ids, segment_ids, target_ids, params):
    embed, in_w, head_w = params[0], params[5], params[12]
    width = embed.shape[1]
    vocab = head_w.shape[0]
    hid = in_w.shape[1]
    tokens = GROUP * ROW
    micros = token_ids.shape[0] // GROUP
    pairs = width // ROW
    vmem = pl.BlockSpec(memory_space=pltpu.VMEM)
    hbm = pl.BlockSpec(memory_space=pl.ANY)

    def kept(columns):
        return jax.ShapeDtypeStruct((micros, tokens, columns), BF16)

    def scratch(lead, columns, kind=BF16):
        return pltpu.VMEM((lead, tokens, columns), kind)

    out_shape = [
        kept(width),
        kept(width),
        kept(width),
        kept(hid),
        kept(width),
        kept(hid),
        kept(width),
        kept(3 * width),
        kept(vocab),
        kept(width),
        jax.ShapeDtypeStruct((VEC_ROWS, width), F32),
    ]
    return pl.pallas_call(
        functools.partial(pipeline_kernel, stages, micros),
        out_shape=out_shape,
        in_specs=[vmem] * 16,
        out_specs=[hbm] * 10 + [vmem],
        scratch_shapes=[
            scratch(micros, width),
            scratch(micros, width),
            scratch(micros, width),
            scratch(micros, width),
            scratch(micros, width),
            scratch(micros, 3 * width),
            pltpu.VMEM((micros, GROUP * pairs, ROW, 2 * ROW), BF16),
            scratch(micros, width),
            scratch(micros, width, F32),
            scratch(micros, width),
            scratch(micros, hid),
            scratch(micros, hid),
            pltpu.VMEM((tokens, width), F32),
            pltpu.VMEM((tokens, width), F32),
            pltpu.VMEM((tokens, width), F32),
            scratch(2, width),
            scratch(2, hid),
            scratch(2, width),
            scratch(2, 3 * width),
            scratch(2, vocab),
            pltpu.VMEM((3, 16, ROW), F32),
            pltpu.VMEM((ROW, ROW), F32),
            pltpu.SemaphoreType.DMA((micros,)),
            pltpu.SemaphoreType.DMA((micros,)),
            pltpu.SemaphoreType.DMA((micros,)),
            pltpu.SemaphoreType.DMA((micros,)),
            pltpu.SemaphoreType.DMA((10, micros)),
        ],
        compiler_params=pltpu.CompilerParams(
            collective_id=0, has_side_effects=True, vmem_limit_bytes=62 * 1024 * 1024
        ),
        name="pipeline",
    )(token_ids, segment_ids, target_ids, *params)


def line_dims(devices):
    dims, stride = [], 1
    if devices == 8:
        return [(2, 1), (4, 2)]
    while devices > 1:
        size = 4 if devices % 4 == 0 else 2
        dims.append((size, stride))
        stride *= size
        devices //= size
    return dims


def chunk_plan(width, hid, vocab, stages, devices):
    slim, deep = width // devices, hid // devices
    plan = [("out", 0, (slim, width), False)]
    for c in range(4):
        plan.append(("down", c, (deep, width // 4), c in (1, 3)))
    for c in range(2):
        plan.append(("extra", c, (stages, vocab // (stages * devices), width // 2), False))
    for c in range(hid // width):
        plan.append(("in", c, (slim, width), c == 1))
    for c in range(3):
        plan.append(("qkv", c, (slim, width), False))
    return plan


def gradient_kernel(stages, devices, plan, *refs):
    dims = line_dims(devices)
    refs = list(refs)

    def take(amount):
        head, refs[:] = refs[:amount], refs[amount:]
        return head

    inputs = take(10)
    vec_in, token_ids = take(2)
    qkv_out, out_out, in_out, down_out, embed_out, head_out, vec_out = take(7)
    local = take(10)
    in_sem = take(1)[0]
    turned_left, turned_xl = take(2)
    mats = dict(
        zip(
            ("normed", "mixed", "normed2", "active", "gres", "ghid", "gbr", "gproj", "xl", "xr"),
            local,
        )
    )
    names = list(mats)
    stage = lax.axis_index("pipe")
    place = lax.axis_index("dp")
    is_extra = (stage == 0) | (stage == stages - 1)
    width = mats["normed"].shape[1]
    where = [lax.rem(place // stride, size) for size, stride in dims]

    barrier = pltpu.get_barrier_semaphore()

    def greet(offset, carry):
        peer = lax.rem(place + offset, devices)
        pl.semaphore_signal(barrier, inc=1, device_id={"dp": peer}, device_id_type=MESH)
        return carry

    def greet_stage(offset, carry):
        peer = lax.rem(stage + offset, stages)
        pl.semaphore_signal(barrier, inc=1, device_id={"pipe": peer}, device_id_type=MESH)
        return carry

    lax.fori_loop(1, devices, greet, 0)
    lax.fori_loop(1, stages, greet_stage, 0)

    def load(name):
        i = names.index(name)
        return pltpu.make_async_copy(inputs[i], mats[name], in_sem.at[i])

    groups = [("mixed", "gbr"), ("gres", "active"), ("xr", "xl"), ("normed2", "ghid"), ("normed", "gproj")]

    def fetch(at):
        if at >= len(groups):
            return
        if groups[at] == ("xr", "xl"):
            @pl.when(is_extra)
            def _():
                load("xr").start()

            @pl.when(stage == stages - 1)
            def _():
                load("xl").start()

            at += 1
        for name in groups[at]:
            load(name).start()

    fetch(0)
    loaded = set()

    def need(*wanted):
        fresh = [name for name in wanted if name not in loaded]
        for name in fresh:
            loaded.add(name)
            load(name).wait()
        if fresh:
            at = [i for i, group in enumerate(groups) if group[0] == fresh[0]][0]
            fetch(at + 1)

    def identity(size):
        here = lax.broadcasted_iota(jnp.int32, (size, size), 0)
        there = lax.broadcasted_iota(jnp.int32, (size, size), 1)
        return jnp.where(here == there, 1.0, 0.0).astype(BF16)

    held = []

    def turn(name):
        if held[-1:] == [name]:
            return
        held.append(name)
        unit = identity(256)
        for q in range(width // 256):
            part = dot_nt(unit, mats[name][:, q * 256 : (q + 1) * 256])
            turned_left[q * 256 : (q + 1) * 256, :] = part.astype(BF16)

    bits = devices.bit_length() - 1
    vec_send, vec_recv = take(2)
    vec_sems = take(2)

    def vec_copy(k):
        peer = jnp.bitwise_xor(place, 1 << k)
        return pltpu.make_async_remote_copy(
            src_ref=vec_send.at[k],
            dst_ref=vec_recv.at[k],
            send_sem=vec_sems[0].at[k],
            recv_sem=vec_sems[1].at[k],
            device_id={"dp": peer},
            device_id_type=MESH,
        )

    def vec_step(k):
        def run():
            if k == 0:
                vec_send[0] = vec_in[...]
                ones = jnp.ones((16, mats["gres"].shape[0]), BF16)
                for name, start, row in (
                    ("gproj", 0, V_QUERY),
                    ("gproj", 2 * width, V_VALUE),
                    ("gbr", 0, V_BRANCH),
                    ("gres", 0, V_RESULT),
                ):
                    part = dot(ones, mats[name][:, start : start + width])
                    vec_send[0, row : row + 1, :] = part[0:1, :]
                for q in range(mats["ghid"].shape[1] // width):
                    part = dot(ones, mats["ghid"][:, q * width : (q + 1) * width])
                    vec_send[0, V_HIDDEN + q : V_HIDDEN + q + 1, :] = part[0:1, :]
            else:
                vec_copy(k - 1).wait_recv()
                vec_send[k] = vec_send[k - 1] + vec_recv[k - 1]
            if k < bits:
                vec_copy(k).start()

        return run

    final_send, final_recv = take(2)
    final_sems = take(2)

    def final_copy(offset):
        peer = lax.rem(stages - 1 + offset, stages)
        return pltpu.make_async_remote_copy(
            src_ref=final_send,
            dst_ref=final_recv,
            send_sem=final_sems[0].at[offset],
            recv_sem=final_sems[1].at[0],
            device_id={"pipe": peer},
            device_id_type=MESH,
        )

    def vec_last():
        vec_step(bits)()
        vec_out[...] = vec_send[bits]

        @pl.when(stage == stages - 1)
        def _():
            final_send[...] = vec_send[bits, 8:16, :]
            for offset in range(1, stages):
                final_copy(offset).start()

    def vec_finish():
        @pl.when(stage != stages - 1)
        def _():
            final_copy(1).wait_recv()
            vec_out[V_FINAL_GAIN : V_FINAL_BIAS + 1, :] = final_recv[
                V_FINAL_GAIN - 8 : V_FINAL_BIAS - 7, :
            ]

    def vec_drain():
        for k in range(bits):
            vec_copy(k).wait_send()

        @pl.when(stage == stages - 1)
        def _():
            for offset in range(1, stages):
                final_copy(offset).wait_send()

    extra_sum, extra_send_sem, extra_recv_sem = take(3)

    def extra_copy(source, offset, target):
        peer = lax.rem(source + offset, stages)
        return pltpu.make_async_remote_copy(
            src_ref=extra_sum.at[peer],
            dst_ref=target,
            send_sem=extra_send_sem.at[offset],
            recv_sem=extra_recv_sem.at[0 if source == 0 else 1],
            device_id={"pipe": peer},
            device_id_type=MESH,
        )

    down_full = {}

    def chunk_steps(kind, c, block, turned):
        order = list(range(len(dims)))
        if turned:
            order.reverse()
        full = take(1)[0]

        def compute():
            if kind == "down":
                need("gres", "active")
                turn("gres")
                if c % 2 == 1:
                    return
                half = width // 2
                lines = slice((c // 2) * half, (c // 2 + 1) * half)
                parts = dot(turned_left[lines, :], mats["active"][...]).astype(BF16)
                depth = block[0]
                unit = identity(depth)
                for d in range(devices):
                    back = dot_nt(unit, parts[:, d * depth : (d + 1) * depth]).astype(BF16)
                    down_full[c][split(d)] = back[:, 0 : half // 2]
                    down_full[c + 1][split(d)] = back[:, half // 2 : half]
            elif kind == "extra":
                vocab = turned_xl.shape[0]
                if c == 0:
                    load("xr").wait()

                @pl.when((stage == 0) & (c == 0))
                def _():
                    rows_n, seq = token_ids.shape
                    places = lax.broadcasted_iota(jnp.int32, (vocab, ROW), 0)
                    gap = jnp.full((1, ROW - seq), -1, jnp.int32)
                    for r in range(rows_n):
                        row = jnp.concatenate([token_ids[r : r + 1, :], gap], axis=1)
                        hot = jnp.where(places == row, 1.0, 0.0)
                        turned_xl[:, r * ROW : (r + 1) * ROW] = hot.astype(BF16)

                @pl.when((stage == stages - 1) & (c == 0))
                def _():
                    load("xl").wait()
                    unit = identity(256)
                    for q in range(vocab // 256):
                        part = dot_nt(unit, mats["xl"][:, q * 256 : (q + 1) * 256])
                        turned_xl[q * 256 : (q + 1) * 256, :] = part.astype(BF16)

                rows = vocab // stages
                for p in range(stages):
                    part = dot(
                        turned_xl[p * rows : (p + 1) * rows, :],
                        mats["xr"][:, c * (width // 2) : (c + 1) * (width // 2)],
                    )
                    part = part.astype(BF16).reshape((devices,) + block[1:])
                    for d in range(devices):
                        full[split(d) + (p,)] = part[d]
            else:
                left, right = {
                    "in": ("normed2", "ghid"),
                    "out": ("mixed", "gbr"),
                    "qkv": ("normed", "gproj"),
                }[kind]
                need(left, right)
                turn(left)
                cols = slice(c * width, (c + 1) * width)
                part = dot(turned_left[...], mats[right][:, cols]).astype(BF16)
                part = part.reshape((devices,) + block)
                for d in range(devices):
                    full[split(d)] = part[d]

        def split(d):
            return tuple((d // stride) % size for size, stride in reversed(dims))

        if kind == "down":
            down_full[c] = full
        steps = [[compute]]
        for at, phase in enumerate(order):
            size = dims[phase][0]
            buffers = take(3)
            done = order[:at]
            last = at == len(order) - 1
            steps[-1].append(functools.partial(line_step, phase, size, 1, full, buffers, done))
            for t in range(2, size):
                steps.append([functools.partial(line_step, phase, size, t, full, buffers, done)])
            drains.append((kind, functools.partial(line_drain, phase, size, full, buffers, done)))
            steps.append([functools.partial(line_final, kind, c, phase, size, full, buffers, done, last)])
        if kind == "extra":
            steps = [[gated([part]) for part in step] for step in steps]
        return steps

    def gated(step):
        def run():
            @pl.when(is_extra)
            def _():
                for part in step:
                    part()

        return run

    def block_of(full, phase, j, done):
        spot = [slice(None)] * len(dims)
        for other in done:
            spot[len(dims) - 1 - other] = where[other]
        spot[len(dims) - 1 - phase] = j
        return full.at[tuple(spot)]

    def line_copy(phase, size, t, side, full, buffers, done):
        recv, ssem, rsem = buffers
        i = where[phase]
        stride = dims[phase][1]
        if side == 0:
            j, peer = size - t + i, place + jnp.where(i < size - 1, stride, 0)
        else:
            j, peer = t - size + i, place - jnp.where(i > 0, stride, 0)
        return pltpu.make_async_remote_copy(
            src_ref=block_of(full, phase, jnp.clip(j, 0, size - 1), done),
            dst_ref=recv.at[0 if size == 2 else side, t - 1],
            send_sem=ssem.at[side, t - 1],
            recv_sem=rsem.at[side, t - 1],
            device_id={"dp": peer},
            device_id_type=MESH,
        )

    def sends(i, size, t, side):
        return (i <= t - 1) if side == 0 else (i >= size - t)

    def line_step(phase, size, t, full, buffers, done):
        i = where[phase]
        for side in range(2):
            at_end = (i == 0) if side == 0 else (i == size - 1)
            j = size - t + i if side == 0 else t - size + i
            j = jnp.clip(j, 0, size - 1)

            @pl.when(sends(i, size, t, side))
            def _():
                if t > 1:
                    @pl.when(jnp.logical_not(at_end))
                    def _():
                        line_copy(phase, size, t - 1, side, full, buffers, done).wait_recv()
                        own = block_of(full, phase, j, done)
                        got = buffers[0][0 if size == 2 else side, t - 2]
                        own[...] = (own[...].astype(F32) + got.astype(F32)).astype(BF16)

                line_copy(phase, size, t, side, full, buffers, done).start()

    def line_final(kind, c, phase, size, full, buffers, done, last):
        i = where[phase]
        own = block_of(full, phase, i, done)
        total = own
        if last:
            slots = {
                "qkv": lambda: qkv_out.at[:, c * width : (c + 1) * width],
                "in": lambda: in_out.at[:, c * width : (c + 1) * width],
                "out": lambda: out_out,
                "down": lambda: down_out.at[:, c * (width // 4) : (c + 1) * (width // 4)],
                "extra": lambda: extra_sum.at[:, :, c * (width // 2) : (c + 1) * (width // 2)],
            }
            total = slots[kind]()
        lower, upper = i > 0, i < size - 1

        def arrived(side):
            line_copy(phase, size, size - 1, side, full, buffers, done).wait_recv()
            return buffers[0][0 if size == 2 else side, size - 2].astype(F32)

        @pl.when(lower & upper)
        def _():
            total[...] = (own[...].astype(F32) + arrived(0) + arrived(1)).astype(total.dtype)

        @pl.when(lower & jnp.logical_not(upper))
        def _():
            total[...] = (own[...].astype(F32) + arrived(0)).astype(total.dtype)

        @pl.when(jnp.logical_not(lower))
        def _():
            total[...] = (own[...].astype(F32) + arrived(1)).astype(total.dtype)

        if last and kind == "extra" and c == 1:
            for source_stage, out in ((0, embed_out), (stages - 1, head_out)):
                @pl.when(stage == source_stage)
                def _():
                    for offset in range(1, stages):
                        extra_copy(source_stage, offset, extra_recv[0 if source_stage == 0 else 1]).start()
                    out[...] = extra_sum[source_stage]

    def line_drain(phase, size, full, buffers, done):
        i = where[phase]
        for side in range(2):
            for t in range(1, size):
                @pl.when(sends(i, size, t, side))
                def _():
                    line_copy(phase, size, t, side, full, buffers, done).wait_send()

    extra_recv = take(2)
    drains = []
    chains = [chunk_steps(*item) for item in plan]
    depth = len(chains[0])
    vec_chain = [vec_step(k) for k in range(bits)] + [vec_last]
    starts, first, extra_rounds = [], 0, iter((1, 3, 6, 8))
    for item in plan:
        if item[3]:
            starts.append(next(extra_rounds))
        else:
            starts.append(first)
            first += 1
    begun = False
    loaded_at = max(start for start, item in zip(starts, plan) if item[0] == "qkv" and item[1] == 0)
    for r in range(max(starts) + depth):
        for d in [0] + list(range(depth - 1, 0, -1)):
            for start, chain in zip(starts, chains):
                if r - start != d:
                    continue
                for part in chain[d]:
                    part()
                    if not begun:
                        begun = True
                        pl.semaphore_wait(barrier, devices - 1 + stages - 1)
        if 0 <= r - loaded_at < len(vec_chain):
            vec_chain[r - loaded_at]()
    vec_finish()
    for source_stage, out in ((0, embed_out), (stages - 1, head_out)):
        @pl.when(stage != source_stage)
        def _():
            got = extra_recv[0 if source_stage == 0 else 1]
            extra_copy(source_stage, 1, got).wait_recv()
            out[...] = got[...]

        @pl.when(stage == source_stage)
        def _():
            for offset in range(1, stages):
                extra_copy(source_stage, offset, extra_recv[0]).wait_send()

    vec_drain()
    for kind, drain in drains:
        if kind == "extra":
            gated([drain])()
        else:
            drain()


def run_gradients(stages, devices, saved, vec, token_ids):
    dims = line_dims(devices)
    rows, tokens, width = saved[0].shape
    hid, vocab = saved[3].shape[2], saved[8].shape[2]
    plan = chunk_plan(width, hid, vocab, stages, devices)
    saved = [member.reshape(rows * tokens, member.shape[2]) for member in saved]
    vmem = pl.BlockSpec(memory_space=pltpu.VMEM)
    hbm = pl.BlockSpec(memory_space=pl.ANY)
    bits = devices.bit_length() - 1
    share = vocab // (stages * devices)
    scratch = [pltpu.VMEM(member.shape, BF16) for member in saved]
    scratch += [pltpu.SemaphoreType.DMA((len(saved),))]
    scratch += [pltpu.VMEM((width, rows * tokens), BF16), pltpu.VMEM((vocab, rows * tokens), BF16)]
    scratch += [
        pltpu.VMEM((bits + 1,) + vec.shape, F32),
        pltpu.VMEM((bits,) + vec.shape, F32),
        pltpu.SemaphoreType.DMA((bits,)),
        pltpu.SemaphoreType.DMA((bits,)),
        pltpu.VMEM((8, width), F32),
        pltpu.VMEM((8, width), F32),
        pltpu.SemaphoreType.DMA((stages,)),
        pltpu.SemaphoreType.DMA((1,)),
        pltpu.VMEM((stages, share, width), F32),
        pltpu.SemaphoreType.DMA((stages,)),
        pltpu.SemaphoreType.DMA((2,)),
        pltpu.VMEM((share, width), F32),
        pltpu.VMEM((share, width), F32),
    ]
    sizes = [size for size, _ in reversed(dims)]
    for _, _, block, turned in plan:
        scratch.append(pltpu.VMEM(tuple(sizes) + block, BF16))
        remain = list(reversed(dims))
        for size, stride in dims[::-1] if turned else dims:
            remain.remove((size, stride))
            piece = tuple(other for other, _ in remain) + block
            scratch.append(pltpu.VMEM((1 if size == 2 else 2, size - 1) + piece, BF16))
            scratch += [pltpu.SemaphoreType.DMA((2, size - 1))] * 2
    return pl.pallas_call(
        functools.partial(gradient_kernel, stages, devices, plan),
        out_shape=[
            jax.ShapeDtypeStruct((width // devices, 3 * width), F32),
            jax.ShapeDtypeStruct((width // devices, width), F32),
            jax.ShapeDtypeStruct((width // devices, hid), F32),
            jax.ShapeDtypeStruct((hid // devices, width), F32),
            jax.ShapeDtypeStruct((share, width), F32),
            jax.ShapeDtypeStruct((share, width), F32),
            jax.ShapeDtypeStruct(vec.shape, F32),
        ],
        in_specs=[hbm] * len(saved) + [vmem] * 2,
        out_specs=[vmem] * 7,
        scratch_shapes=scratch,
        compiler_params=pltpu.CompilerParams(
            collective_id=1, has_side_effects=True, vmem_limit_bytes=62 * 1024 * 1024
        ),
        name="gradients",
    )(*saved, vec, token_ids)


def step_kernel(stages, micros, devices, plan, *refs):
    refs = list(refs)

    def take(amount):
        head, refs[:] = refs[:amount], refs[amount:]
        return head

    token_ids, segment_ids, target_ids = take(3)
    qv_b, out_b, in_b, gains, shifts, fin_gain, fin_bias = take(7)
    embed_h, head_h, qkv_h, out_h, in_h, down_h = take(6)
    qkv_out, out_out, in_out, down_out, embed_out, head_out, vec_out = take(7)
    side, qkv_w, out_w = take(3)
    in_w, down_w = take(4), take(4)
    instream, outb, gin, gs, proj, probs, mixed, middle, active, slope = take(10)
    lo, gmid, s_gbr, s_xl, vec, ids, frames = take(7)
    fsend, frecv, bsend, brecv, wsem = take(5)
    go = lo
    place = lax.axis_index("dp")
    stage = lax.axis_index("pipe")
    tokens, width = instream.shape[1], instream.shape[2]
    hidden_n = in_b.shape[1]
    vocab = side.shape[0]
    pairs = width // ROW
    chunk = 512
    is_first = stage == 0
    is_last = stage == stages - 1
    up = jnp.minimum(stage + 1, stages - 1)
    down = jnp.maximum(stage - 1, 0)

    def bring(index, source, target):
        return pltpu.make_async_copy(source, target, wsem.at[index])

    weights = [bring(1, qkv_h, qkv_w), bring(2, out_h, out_w)]
    for c in range(4):
        lanes = pl.ds(c * chunk, chunk)
        weights.append(bring(3 + c, in_h.at[:, :, :, lanes], in_w[c]))
        weights.append(bring(7 + c, down_h.at[c], down_w[c]))

    @pl.when(is_first)
    def _():
        bring(0, embed_h, side).start()

    for copy in weights:
        copy.start()

    @pl.when(is_last)
    def _():
        bring(0, head_h, side).start()

    barrier = pltpu.get_barrier_semaphore()

    def greet(offset, carry):
        peer = lax.rem(place + offset, devices)
        pl.semaphore_signal(barrier, inc=1, device_id={"dp": peer}, device_id_type=MESH)
        return carry

    def greet_stage(offset, carry):
        peer = lax.rem(stage + offset, stages)
        pl.semaphore_signal(barrier, inc=1, device_id={"pipe": peer}, device_id_type=MESH)
        return carry

    lax.fori_loop(1, devices, greet, 0)
    lax.fori_loop(1, stages, greet_stage, 0)

    def whole(part):
        return part[...].reshape(width, width)

    vec[...] = jnp.zeros_like(vec)
    rows_n, seq = token_ids.shape
    for index, member in enumerate((token_ids, segment_ids, target_ids)):
        ids[index] = jnp.full(ids.shape[1:], 4.0 if index == 1 else -1.0, F32)
        ids[index, 0:rows_n, 0:seq] = member[...].astype(F32)
    at_query = lax.broadcasted_iota(jnp.int32, (ROW, ROW), 1)
    at_key = lax.broadcasted_iota(jnp.int32, (ROW, ROW), 0)
    frames[...] = jnp.where(at_key < ((at_query * 43) // 256) * FRAME + FRAME, 1.0, 0.0)

    def column(index, row):
        values = jnp.broadcast_to(ids[index, pl.ds(row, 1), :], (8, ROW))
        return values.T[:, 0:1]

    def hot_rows(index, m):
        parts = [column(index, m * GROUP + r) for r in range(GROUP)]
        values = jnp.concatenate(parts, axis=0)
        places = lax.broadcasted_iota(jnp.int32, (tokens, vocab), 1).astype(F32)
        return values, jnp.where(values == places, 1.0, 0.0)

    def forward_copy(m):
        return pltpu.make_async_remote_copy(
            src_ref=outb.at[m],
            dst_ref=instream.at[m],
            send_sem=fsend.at[m],
            recv_sem=frecv.at[m],
            device_id={"pipe": up},
            device_id_type=MESH,
        )

    def backward_copy(m):
        return pltpu.make_async_remote_copy(
            src_ref=gs.at[m],
            dst_ref=gin.at[m],
            send_sem=bsend.at[m],
            recv_sem=brecv.at[m],
            device_id={"pipe": down},
            device_id_type=MESH,
        )

    @pl.when(is_first | is_last)
    def _():
        bring(0, embed_h, side).wait()

    for copy in weights:
        copy.wait()
    pl.semaphore_wait(barrier, devices - 1 + stages - 1)

    lane_low = lax.broadcasted_iota(jnp.int32, (ROW, ROW), 1) < ROW // 2

    def forward(m):
        @pl.when(is_first)
        def _():
            hot = hot_rows(0, m)[1].astype(BF16)
            instream[m] = dot(hot, side[...]).astype(BF16)

        @pl.when(jnp.logical_not(is_first))
        def _():
            forward_copy(m).wait_recv()

        normal, _ = normalise(instream[m].astype(F32))
        low = (normal * gains[0:1, :] + shifts[0:1, :]).astype(BF16)
        queries = dot(low, qkv_w[:, 0:width]) + qv_b[0:1, :]
        proj[m, :, 0:width] = (queries * (ROW // 2) ** -0.5).astype(BF16)
        proj[m, :, width : 2 * width] = dot(low, qkv_w[:, width : 2 * width]).astype(BF16)
        proj[m, :, 2 * width : 3 * width] = (
            dot(low, qkv_w[:, 2 * width : 3 * width]) + qv_b[1:2, :]
        ).astype(BF16)
        masks, scores = [], []
        for r in range(GROUP):
            rows = slice(r * ROW, (r + 1) * ROW)
            kinds = lax.broadcasted_iota(jnp.int32, (16, ROW), 0).astype(F32)
            member = jnp.where(ids[1, pl.ds(m * GROUP + r, 1), :] == kinds, 1.0, 0.0).astype(BF16)
            mask = jnp.where(dot_tn(member, member) * frames[...] > 0.5, 0.0, MASKED)
            masks.append(jnp.concatenate([mask, mask], axis=1))
            for p in range(pairs):
                q = stack_pair(proj[m, rows, p * ROW : (p + 1) * ROW], lane_low)
                k = proj[m, rows, width + p * ROW : width + (p + 1) * ROW]
                scores.append(dot_nt(k, q))

        def mix(unit):
            r, p = unit // pairs, unit % pairs
            rows = slice(r * ROW, (r + 1) * ROW)
            v = proj[m, rows, 2 * width + p * ROW : 2 * width + (p + 1) * ROW]
            both = dot_tn(probs[m, unit // 2, unit % 2], v)
            mixed[m, rows, p * ROW : (p + 1) * ROW] = join_pair(both, lane_low).astype(BF16)

        for unit in range(GROUP * pairs):
            masked = scores[unit] + masks[unit // pairs]
            expo = jnp.exp(masked - jnp.max(masked, axis=0, keepdims=True))
            total = jnp.sum(expo, axis=0, keepdims=True)
            probs[m, unit // 2, unit % 2] = (expo * (1.0 / total)).astype(BF16)
            if unit:
                mix(unit - 1)
        mix(GROUP * pairs - 1)
        mid = instream[m].astype(F32) + (dot(mixed[m], out_w[...]) + out_b[0:1, :])
        middle[m] = mid
        normal2, _ = normalise(mid)
        low2 = (normal2 * gains[1:2, :] + shifts[1:2, :]).astype(BF16)
        parts = hidden_n // chunk

        def spread(c):
            return dot(low2, whole(in_w[c]))

        total, ahead = None, spread(0)
        for c in range(parts):
            cols = slice(c * chunk, (c + 1) * chunk)
            hid = ahead + in_b[0:1, cols]
            if c + 1 < parts:
                ahead = spread(c + 1)
            square = hid * hid
            tan = jnp.tanh(hid * (GELU_A + (GELU_A * GELU_B) * square))
            half = 0.5 + 0.5 * tan
            act = (hid * half).astype(BF16)
            active[m, :, cols] = act
            rise = (1.0 - tan * tan) * (0.5 * GELU_A + (1.5 * GELU_A * GELU_B) * square)
            slope[m, :, cols] = (half + hid * rise).astype(BF16)
            term = dot(act, whole(down_w[c]))
            total = term if total is None else total + term
        lo[...] = middle[m] + (total + out_b[1:2, :])

        @pl.when(jnp.logical_not(is_last))
        def _():
            outb[m] = lo[...].astype(BF16)
            forward_copy(m).start()

    def head(m):
        normal, scale = normalise(lo[...])
        outb[m] = (normal * fin_gain[...] + fin_bias[...]).astype(BF16)
        logits = dot_nt(outb[m], side[...])
        top = jnp.max(logits, axis=-1, keepdims=True)
        expo = jnp.exp(logits - top)
        total = jnp.sum(expo, axis=-1, keepdims=True)
        target, hot = hot_rows(2, m)
        grad_logits = jnp.where(target >= 0.0, expo * (1.0 / total) - hot, 0.0).astype(BF16)
        s_xl[m] = grad_logits
        grad_final = dot(grad_logits, side[...])
        vec[V_FINAL_GAIN : V_FINAL_GAIN + 1, :] += column_sum(grad_final * normal)
        vec[V_FINAL_BIAS : V_FINAL_BIAS + 1, :] += column_sum(grad_final)
        go[...] = norm_backward(grad_final, normal, scale, fin_gain[...])

    def backward(m):
        @pl.when(jnp.logical_not(is_last))
        def _():
            backward_copy(m).wait_recv()
            go[...] = gin[m].astype(F32)

        gres = go[...].astype(BF16)
        gin[m] = gres
        parts = hidden_n // chunk

        def spread(c):
            return dot_nt(gres, whole(down_w[c]))

        total, ahead = None, spread(0)
        for c in range(parts):
            cols = slice(c * chunk, (c + 1) * chunk)
            gact = ahead
            if c + 1 < parts:
                ahead = spread(c + 1)
            ghid = (gact * slope[m, :, cols].astype(F32)).astype(BF16)
            slope[m, :, cols] = ghid
            term = dot_nt(ghid, whole(in_w[c]))
            total = term if total is None else total + term
        normal2, scale2 = normalise(middle[m])
        vec[V_GAIN2 : V_GAIN2 + 1, :] += column_sum(total * normal2)
        vec[V_SHIFT2 : V_SHIFT2 + 1, :] += column_sum(total)
        gmid[...] = go[...] + norm_backward(total, normal2, scale2, gains[1:2, :])
        gbr = gmid[...].astype(BF16)
        s_gbr[m] = gbr
        gmix = dot_nt(gbr, out_w[...]).astype(BF16)
        grads = []
        for r in range(GROUP):
            rows = slice(r * ROW, (r + 1) * ROW)
            for p in range(pairs):
                gm = stack_pair(gmix[rows, p * ROW : (p + 1) * ROW], lane_low)
                vlanes = slice(2 * width + p * ROW, 2 * width + (p + 1) * ROW)
                grads.append(dot_nt(proj[m, rows, vlanes], gm))
                unit = r * pairs + p
                proj[m, rows, vlanes] = dot(probs[m, unit // 2, unit % 2], gm).astype(BF16)

        def pull(unit, gsc):
            r, p = unit // pairs, unit % pairs
            rows = slice(r * ROW, (r + 1) * ROW)
            lanes = slice(p * ROW, (p + 1) * ROW)
            klanes = slice(width + p * ROW, width + (p + 1) * ROW)
            q = stack_pair(proj[m, rows, lanes], lane_low)
            gq = join_pair(dot_tn(gsc, proj[m, rows, klanes]), lane_low) * (ROW // 2) ** -0.5
            gk = dot(gsc, q)
            proj[m, rows, klanes] = gk.astype(BF16)
            proj[m, rows, lanes] = gq.astype(BF16)

        waiting = None
        for unit in range(GROUP * pairs):
            weights = probs[m, unit // 2, unit % 2].astype(F32)
            inner = jnp.sum(weights * grads[unit], axis=0, keepdims=True)
            gsc = (weights * (grads[unit] - inner)).astype(BF16)
            if waiting is not None:
                pull(unit - 1, waiting)
            waiting = gsc
        pull(GROUP * pairs - 1, waiting)
        gproj = proj[m]
        gnormed = dot_nt(gproj, qkv_w[...])
        normal, scale = normalise(instream[m].astype(F32))
        vec[V_GAIN1 : V_GAIN1 + 1, :] += column_sum(gnormed * normal)
        vec[V_SHIFT1 : V_SHIFT1 + 1, :] += column_sum(gnormed)
        gs[m] = (gmid[...] + norm_backward(gnormed, normal, scale, gains[0:1, :])).astype(BF16)

        @pl.when(jnp.logical_not(is_first))
        def _():
            backward_copy(m).start()

    def tick(t, carry):
        m_forward = t - stage
        m_backward = t - (2 * (stages - 1) - stage)

        @pl.when((m_forward >= 0) & (m_forward < micros))
        def _():
            forward(m_forward)

        @pl.when((m_backward >= 0) & (m_backward < micros))
        def _():
            @pl.when(is_last)
            def _():
                head(m_backward)

            backward(m_backward)

        return carry

    lax.fori_loop(0, micros + 2 * (stages - 1), tick, 0)

    embed_stage = stages - 2
    is_extra = (stage == embed_stage) | is_last
    dims = line_dims(devices)
    turned_left = qkv_w
    mats = {
        "mixed": mixed,
        "active": active,
        "gres": gin,
        "ghid": slope,
        "gbr": s_gbr,
        "gproj": proj,
    }

    def mat(name, lanes=slice(None)):
        value = mats[name][:, :, lanes]
        return value.reshape(micros * tokens, value.shape[2])

    where = [lax.rem(place // stride, size) for size, stride in dims]

    def identity(size):
        here = lax.broadcasted_iota(jnp.int32, (size, size), 0)
        there = lax.broadcasted_iota(jnp.int32, (size, size), 1)
        return jnp.where(here == there, 1.0, 0.0).astype(BF16)

    held = []

    def turn(name):
        if held[-1:] == [name]:
            return
        held.append(name)
        unit = identity(256)
        if name in ("normed", "normed2"):
            row = 0 if name == "normed" else 1
            source = instream if name == "normed" else middle
            for m in range(micros):
                normal, _ = normalise(source[m].astype(F32))
                again = (normal * gains[row : row + 1, :] + shifts[row : row + 1, :]).astype(BF16)
                for q in range(width // 256):
                    part = dot_nt(unit, again[:, q * 256 : (q + 1) * 256])
                    turned_left[q * 256 : (q + 1) * 256, m * tokens : (m + 1) * tokens] = part.astype(BF16)
            return
        for q in range(width // 256):
            part = dot_nt(unit, mat(name, slice(q * 256, (q + 1) * 256)))
            turned_left[q * 256 : (q + 1) * 256, :] = part.astype(BF16)

    bits = devices.bit_length() - 1
    vec_send, vec_recv = take(2)
    vec_sems = take(2)

    def vec_copy(k):
        peer = jnp.bitwise_xor(place, 1 << k)
        return pltpu.make_async_remote_copy(
            src_ref=vec_send.at[k],
            dst_ref=vec_recv.at[k],
            send_sem=vec_sems[0].at[k],
            recv_sem=vec_sems[1].at[k],
            device_id={"dp": peer},
            device_id_type=MESH,
        )

    def vec_step(k):
        def run():
            if k == 0:
                vec_send[0] = vec[...]
                ones = jnp.ones((16, micros * tokens), BF16)
                for name, start, row in (
                    ("gproj", 0, V_QUERY),
                    ("gproj", 2 * width, V_VALUE),
                    ("gbr", 0, V_BRANCH),
                    ("gres", 0, V_RESULT),
                ):
                    part = dot(ones, mat(name, slice(start, start + width)))
                    vec_send[0, row : row + 1, :] = part[0:1, :]
                for q in range(hidden_n // width):
                    part = dot(ones, mat("ghid", slice(q * width, (q + 1) * width)))
                    vec_send[0, V_HIDDEN + q : V_HIDDEN + q + 1, :] = part[0:1, :]
            else:
                vec_copy(k - 1).wait_recv()
                vec_send[k] = vec_send[k - 1] + vec_recv[k - 1]
            if k < bits:
                vec_copy(k).start()

        return run

    final_send, final_recv = take(2)
    final_sems = take(2)

    def final_copy(offset):
        peer = lax.rem(stages - 1 + offset, stages)
        return pltpu.make_async_remote_copy(
            src_ref=final_send,
            dst_ref=final_recv,
            send_sem=final_sems[0].at[offset],
            recv_sem=final_sems[1].at[0],
            device_id={"pipe": peer},
            device_id_type=MESH,
        )

    def vec_last():
        vec_step(bits)()
        vec_out[...] = vec_send[bits]

        @pl.when(stage == stages - 1)
        def _():
            final_send[...] = vec_send[bits, 8:16, :]
            for offset in range(1, stages):
                final_copy(offset).start()

    def vec_finish():
        @pl.when(stage != stages - 1)
        def _():
            final_copy(1).wait_recv()
            vec_out[V_FINAL_GAIN : V_FINAL_BIAS + 1, :] = final_recv[
                V_FINAL_GAIN - 8 : V_FINAL_BIAS - 7, :
            ]

    def vec_drain():
        for k in range(bits):
            vec_copy(k).wait_send()

        @pl.when(stage == stages - 1)
        def _():
            for offset in range(1, stages):
                final_copy(offset).wait_send()

    def ship():
        return pltpu.make_async_remote_copy(
            src_ref=s_xl.at[pl.ds(0, 2)],
            dst_ref=s_xl.at[pl.ds(0, 2)],
            send_sem=ship_sem.at[0],
            recv_sem=ship_sem.at[1],
            device_id={"pipe": embed_stage},
            device_id_type=MESH,
        )

    def ship_embed():
        rows, half = vocab // stages, width // 2

        @pl.when(is_first)
        def _():
            right = gs[...].reshape(micros * tokens, width)
            for p in range(stages):
                here = lax.broadcasted_iota(jnp.int32, (rows, ROW), 0).astype(F32) + p * rows
                hot = [
                    jnp.where(ids[0, r : r + 1, :] == here, 1.0, 0.0).astype(BF16) for r in range(rows_n)
                ]
                part = dot(jnp.concatenate(hot, axis=1), right).astype(BF16)
                for k in range(2):
                    s_xl[k, :, p * half : (p + 1) * half] = part[:, k * half : (k + 1) * half]
            ship().start()

    extra_sum, extra_send_sem, extra_recv_sem, last_sum, ship_sem = take(5)
    share = embed_out.shape[0]

    def extra_copy(source, offset, target):
        peer = lax.rem(source + offset, stages)
        return pltpu.make_async_remote_copy(
            src_ref=extra_sum.at[pl.ds(pl.multiple_of(peer * share, share), share)],
            dst_ref=target,
            send_sem=extra_send_sem.at[offset],
            recv_sem=extra_recv_sem.at[0 if source == embed_stage else 1],
            device_id={"pipe": peer},
            device_id_type=MESH,
        )

    def chunk_steps(kind, c, block, turned):
        order = list(range(len(dims)))
        if turned:
            order.reverse()
        if kind == "down":
            full = probs.at[c]
        elif kind == "extra":
            full = probs.at[4 + c]
        else:
            full = (down_w + in_w)[{"out": 0, "in": 1, "qkv": 5}[kind] + c]

        def compute():
            if kind == "down":
                if c % 2 == 1:
                    return
                turn("gres")
                half = width // 2
                lines = slice((c // 2) * half, (c // 2 + 1) * half)
                parts = dot(turned_left[lines, :], mat("active")).astype(BF16)
                depth = hidden_n // devices
                unit = identity(depth)
                for d in range(devices):
                    back = dot_nt(unit, parts[:, d * depth : (d + 1) * depth]).astype(BF16)
                    for k in range(2):
                        piece = back[:, k * ROW : (k + 1) * ROW]
                        piece = jnp.concatenate([piece[: depth // 2], piece[depth // 2 :]], axis=1)
                        probs[(c + k,) + split(d)] = piece
            elif kind == "extra":
                if c == 1:
                    return
                rows = vocab // stages
                share = rows // devices
                half = width // 2

                def fill(left, right):
                    for p in range(stages):
                        part = left(p, right).astype(BF16).reshape(devices, share, width)
                        for d in range(devices):
                            for k in range(2):
                                lines = slice(p * share, (p + 1) * share)
                                probs[(4 + k,) + split(d) + (lines,)] = part[
                                    d, :, k * half : (k + 1) * half
                                ]

                def flat(ref):
                    return ref[...].reshape(micros * tokens, ref.shape[2])

                @pl.when(stage == embed_stage)
                def _():
                    ship().wait_recv()
                    for d in range(devices):
                        for k in range(2):
                            for p in range(stages):
                                lines = slice(p * share, (p + 1) * share)
                                probs[(4 + k,) + split(d) + (lines,)] = s_xl[
                                    k, d * share : (d + 1) * share, p * half : (p + 1) * half
                                ]

                @pl.when(is_last)
                def _():
                    def soft_part(p, right):
                        left = s_xl[:, :, p * rows : (p + 1) * rows]
                        return dot_tn(left.reshape(micros * tokens, rows), right)

                    fill(soft_part, flat(outb))
            else:
                left, right = {
                    "in": ("normed2", "ghid"),
                    "out": ("mixed", "gbr"),
                    "qkv": ("normed", "gproj"),
                }[kind]
                turn(left)
                part = dot(turned_left[...], mat(right, slice(c * width, (c + 1) * width)))
                part = part.astype(BF16).reshape((devices,) + block)
                for d in range(devices):
                    full[split(d)] = part[d]

        def split(d):
            return tuple((d // stride) % size for size, stride in reversed(dims))

        steps = [[compute]]
        for at, phase in enumerate(order):
            size = dims[phase][0]
            buffers = take(3)
            done = order[:at]
            last = at == len(order) - 1
            steps[-1].append(functools.partial(line_step, phase, size, 1, full, buffers, done))
            for t in range(2, size):
                steps.append([functools.partial(line_step, phase, size, t, full, buffers, done)])
            drains.append((kind, functools.partial(line_drain, phase, size, full, buffers, done)))
            steps.append([functools.partial(line_final, kind, c, phase, size, full, buffers, done, last)])
        if kind == "extra":
            steps = [[gated([part]) for part in step] for step in steps]
        return steps

    def gated(step):
        def run():
            @pl.when(is_extra)
            def _():
                for part in step:
                    part()

        return run

    def block_of(full, phase, j, done):
        spot = [slice(None)] * len(dims)
        for other in done:
            spot[len(dims) - 1 - other] = where[other]
        spot[len(dims) - 1 - phase] = j
        return full.at[tuple(spot)]

    def line_copy(phase, size, t, side, full, buffers, done):
        recv, ssem, rsem = buffers
        i = where[phase]
        stride = dims[phase][1]
        if side == 0:
            j, peer = size - t + i, place + jnp.where(i < size - 1, stride, 0)
        else:
            j, peer = t - size + i, place - jnp.where(i > 0, stride, 0)
        return pltpu.make_async_remote_copy(
            src_ref=block_of(full, phase, jnp.clip(j, 0, size - 1), done),
            dst_ref=recv.at[0 if size == 2 else side, t - 1],
            send_sem=ssem.at[side, t - 1],
            recv_sem=rsem.at[side, t - 1],
            device_id={"dp": peer},
            device_id_type=MESH,
        )

    def sends(i, size, t, side):
        return (i <= t - 1) if side == 0 else (i >= size - t)

    def line_step(phase, size, t, full, buffers, done):
        i = where[phase]
        for side in range(2):
            at_end = (i == 0) if side == 0 else (i == size - 1)
            j = size - t + i if side == 0 else t - size + i
            j = jnp.clip(j, 0, size - 1)

            @pl.when(sends(i, size, t, side))
            def _():
                if t > 1:
                    @pl.when(jnp.logical_not(at_end))
                    def _():
                        line_copy(phase, size, t - 1, side, full, buffers, done).wait_recv()
                        own = block_of(full, phase, j, done)
                        got = buffers[0][0 if size == 2 else side, t - 2]
                        own[...] = (own[...].astype(F32) + got.astype(F32)).astype(BF16)

                line_copy(phase, size, t, side, full, buffers, done).start()

    def line_final(kind, c, phase, size, full, buffers, done, last):
        i = where[phase]
        own = block_of(full, phase, i, done)
        total = own
        if last:
            lanes = slice(c * width, (c + 1) * width)
            slots = {
                "qkv": lambda: qkv_out.at[:, lanes],
                "in": lambda: in_out.at[:, lanes],
                "out": lambda: out_out,
                "down": lambda: last_sum,
                "extra": lambda: extra_sum.at[:, c * (width // 2) : (c + 1) * (width // 2)],
            }
            total = slots[kind]()
        lower, upper = i > 0, i < size - 1

        def arrived(side):
            line_copy(phase, size, size - 1, side, full, buffers, done).wait_recv()
            return buffers[0][0 if size == 2 else side, size - 2].astype(F32)

        @pl.when(lower & upper)
        def _():
            total[...] = (own[...].astype(F32) + arrived(0) + arrived(1)).astype(total.dtype)

        @pl.when(lower & jnp.logical_not(upper))
        def _():
            total[...] = (own[...].astype(F32) + arrived(0)).astype(total.dtype)

        @pl.when(jnp.logical_not(lower))
        def _():
            total[...] = (own[...].astype(F32) + arrived(1)).astype(total.dtype)

        if last and kind == "down":
            deep = down_out.shape[0] // 2
            lanes = slice(c * ROW, (c + 1) * ROW)
            down_out[0:deep, lanes] = last_sum[:, 0:ROW]
            down_out[deep : 2 * deep, lanes] = last_sum[:, ROW : 2 * ROW]
        if last and kind == "extra" and c == 1:
            for source_stage, out in ((embed_stage, embed_out), (stages - 1, head_out)):
                @pl.when(stage == source_stage)
                def _():
                    for offset in range(1, stages):
                        extra_copy(source_stage, offset, extra_recv[0 if source_stage == embed_stage else 1]).start()
                    out[...] = extra_sum[source_stage * share : (source_stage + 1) * share, :]

    def line_drain(phase, size, full, buffers, done):
        i = where[phase]
        for side in range(2):
            for t in range(1, size):
                @pl.when(sends(i, size, t, side))
                def _():
                    line_copy(phase, size, t, side, full, buffers, done).wait_send()

    extra_recv = take(2)
    drains = []
    chains = [chunk_steps(*item) for item in plan]
    depth = len(chains[0])
    vec_chain = [vec_step(k) for k in range(bits)] + [vec_last]
    starts, first, extra_rounds = [], 0, iter((1, 2, 4, 6))
    for item in plan:
        if item[0] == "extra":
            starts.append(7 + item[1])
        elif item[3]:
            starts.append(next(extra_rounds))
        else:
            starts.append(first)
            first += 1
    loaded_at = max(start for start, item in zip(starts, plan) if item[0] == "qkv" and item[1] == 0)
    for r in range(max(starts) + depth):
        for d in [0] + list(range(depth - 1, 0, -1)):
            for start, chain in zip(starts, chains):
                if r - start != d:
                    continue
                for part in chain[d]:
                    part()
            if r == 1 and d == 0:
                ship_embed()
        if 0 <= r - loaded_at < len(vec_chain):
            vec_chain[r - loaded_at]()
    vec_finish()
    for source_stage, out in ((embed_stage, embed_out), (stages - 1, head_out)):
        @pl.when(stage != source_stage)
        def _():
            got = extra_recv[0 if source_stage == embed_stage else 1]
            extra_copy(source_stage, 1, got).wait_recv()
            out[...] = got[...]

        @pl.when(stage == source_stage)
        def _():
            for offset in range(1, stages):
                extra_copy(source_stage, offset, extra_recv[0]).wait_send()

    vec_drain()
    for kind, drain in drains:
        if kind == "extra":
            gated([drain])()
        else:
            drain()

    @pl.when(is_first)
    def _():
        ship().wait_send()

    for m in range(micros):
        @pl.when(jnp.logical_not(is_last))
        def _():
            forward_copy(m).wait_send()

        @pl.when(jnp.logical_not(is_first))
        def _():
            backward_copy(m).wait_send()


def step_plan(width, hid, vocab, stages, devices):
    plan = []
    for kind, c, _, turned in chunk_plan(width, hid, vocab, stages, devices):
        wide = kind in ("down", "extra")
        plan.append((kind, c, (ROW, 2 * ROW) if wide else (width // devices, width), turned))
    extra = [item for item in plan if item[0] == "extra"]
    rest = [item for item in plan if item[0] != "extra"]
    return rest + extra


def run_step(stages, devices, token_ids, segment_ids, target_ids, params):
    embed, qkv_w, qv_b, out_w, out_b, in_w, in_b, down_w, gains, shifts, fg, fb, head_w = params
    dims = line_dims(devices)
    width, hid, vocab = embed.shape[1], in_w.shape[1], head_w.shape[0]
    tokens = GROUP * ROW
    micros = token_ids.shape[0] // GROUP
    vmem = pl.BlockSpec(memory_space=pltpu.VMEM)
    hbm = pl.BlockSpec(memory_space=pl.ANY)
    sizes = tuple(size for size, _ in reversed(dims))
    slim = width // devices
    share = vocab // (stages * devices)
    plan = step_plan(width, hid, vocab, stages, devices)
    bits = devices.bit_length() - 1

    def scratch(lead, columns, kind=BF16):
        return pltpu.VMEM((lead, tokens, columns), kind)

    def sums(*shape):
        return pltpu.VMEM(shape, F32)

    dma = pltpu.SemaphoreType.DMA
    scratch_shapes = [
        pltpu.VMEM((vocab, width), BF16),
        pltpu.VMEM((width, 3 * width), BF16),
        pltpu.VMEM((width, width), BF16),
    ]
    scratch_shapes += [pltpu.VMEM(sizes + (slim, width), BF16)] * 8
    scratch_shapes += [
        scratch(micros, width),
        scratch(micros, width),
        scratch(micros, width),
        scratch(micros, width),
        scratch(micros, 3 * width),
        pltpu.VMEM((micros,) + sizes + (ROW, 2 * ROW), BF16),
        scratch(micros, width),
        scratch(micros, width, F32),
        scratch(micros, hid),
        scratch(micros, hid),
        sums(tokens, width),
        sums(tokens, width),
        scratch(micros, width),
        scratch(micros, vocab),
        sums(VEC_ROWS, width),
        sums(3, 16, ROW),
        sums(ROW, ROW),
        dma((micros,)),
        dma((micros,)),
        dma((micros,)),
        dma((micros,)),
        dma((11,)),
        sums(bits + 1, VEC_ROWS, width),
        sums(bits, VEC_ROWS, width),
        dma((bits,)),
        dma((bits,)),
        sums(8, width),
        sums(8, width),
        dma((stages,)),
        dma((1,)),
        sums(stages * share, width),
        dma((stages,)),
        dma((2,)),
        sums(ROW, 2 * ROW),
        dma((2,)),
        sums(share, width),
        sums(share, width),
    ]
    for _, _, block, turned in plan:
        remain = list(reversed(dims))
        for size, stride in dims[::-1] if turned else dims:
            remain.remove((size, stride))
            piece = tuple(other for other, _ in remain) + block
            scratch_shapes.append(pltpu.VMEM((1 if size == 2 else 2, size - 1) + piece, BF16))
            scratch_shapes += [dma((2, size - 1))] * 2

    def result(*shape):
        return jax.ShapeDtypeStruct(shape, F32)

    return pl.pallas_call(
        functools.partial(step_kernel, stages, micros, devices, plan),
        out_shape=[
            result(slim, 3 * width),
            result(slim, width),
            result(slim, hid),
            result(hid // devices, width),
            result(share, width),
            result(share, width),
            result(VEC_ROWS, width),
        ],
        in_specs=[vmem] * 10 + [hbm] * 6,
        out_specs=[vmem] * 7,
        scratch_shapes=scratch_shapes,
        compiler_params=pltpu.CompilerParams(
            collective_id=2, has_side_effects=True, vmem_limit_bytes=63 * 1024 * 1024
        ),
        name="step",
    )(
        token_ids,
        segment_ids,
        target_ids,
        qv_b,
        out_b,
        in_b,
        gains,
        shifts,
        fg,
        fb,
        embed,
        head_w,
        qkv_w,
        out_w,
        in_w.reshape(sizes + (slim, hid)),
        down_w.reshape((hid // width,) + sizes + (slim, width)),
    )


def finish_kernel(devices, embed_g, qkv_g, out_g, in_g, down_g, head_g, vec, *outs):
    place = lax.axis_index("dp")
    width = vec.shape[1]
    (embed_o, qkv_o, qv_o, out_o, outb_o, in_o, inb_o, down_o, gain_o, shift_o, fg_o, fb_o, head_o) = outs
    embed_o[...] = embed_g[...]
    head_o[...] = head_g[...]
    for source, target in ((qkv_g, qkv_o), (out_g, out_o), (in_g, in_o), (down_g, down_o)):
        target[0] = source[...]
    lanes = width // devices
    turned = pltpu.roll(vec[0:8, :], lax.rem(width - place * lanes, width), 1)
    for row, out in ((V_QUERY, qv_o), (V_BRANCH, outb_o), (V_GAIN1, gain_o), (V_SHIFT1, shift_o)):
        out[0] = turned[row : row + 2, 0:lanes]
    share = inb_o.shape[1]
    first = place * share
    row = vec[pl.ds(V_HIDDEN + first // width, 1), :]
    wide = jnp.broadcast_to(row, (8, width))
    inb_o[...] = pltpu.roll(wide, lax.rem(width - lax.rem(first, width), width), 1)[0:1, 0:share]
    fg_o[...] = vec[V_FINAL_GAIN : V_FINAL_GAIN + 1, :]
    fb_o[...] = vec[V_FINAL_BIAS : V_FINAL_BIAS + 1, :]


def run_finish(devices, embed_g, qkv_g, out_g, in_g, down_g, head_g, vec):
    vmem = pl.BlockSpec(memory_space=pltpu.VMEM)
    width = vec.shape[1]
    lanes = width // devices

    def shape(*sizes):
        return jax.ShapeDtypeStruct(sizes, F32)

    pair = shape(1, 2, lanes)
    return pl.pallas_call(
        functools.partial(finish_kernel, devices),
        out_shape=[
            shape(*embed_g.shape),
            shape(1, *qkv_g.shape),
            pair,
            shape(1, *out_g.shape),
            pair,
            shape(1, *in_g.shape),
            shape(1, in_g.shape[1] // devices),
            shape(1, *down_g.shape),
            pair,
            pair,
            shape(1, width),
            shape(1, width),
            shape(*head_g.shape),
        ],
        in_specs=[vmem] * 7,
        out_specs=[vmem] * 13,
        name="finish",
    )(embed_g, qkv_g, out_g, in_g, down_g, head_g, vec)


def on_device(
    token_ids,
    segment_ids,
    target_ids,
    embed_table,
    qkv_weight,
    qv_bias,
    out_weight,
    out_biases,
    ff_in,
    ff_in_bias,
    ff_out,
    norm_gains,
    norm_biases,
    final_gain,
    final_bias,
    head_weight,
):
    stages = lax.axis_size("pipe")
    devices = lax.axis_size("dp")
    params = (
        embed_table,
        qkv_weight[0],
        qv_bias[0],
        out_weight[0],
        out_biases[0],
        ff_in[0],
        ff_in_bias,
        ff_out[0],
        norm_gains[0],
        norm_biases[0],
        final_gain[None],
        final_bias[None],
        head_weight,
    )
    if devices == 8:
        grads = run_step(stages, devices, token_ids, segment_ids, target_ids, params)
    else:
        *saved, vec = run_pipeline(stages, token_ids, segment_ids, target_ids, params)
        grads = run_gradients(stages, devices, saved, vec, token_ids)
    qkv_g, out_g, in_g, down_g, embed_g, head_g, sums = grads
    done = list(run_finish(devices, embed_g, qkv_g, out_g, in_g, down_g, head_g, sums))
    done[10], done[11] = done[10][0], done[11][0]
    return tuple(done)


def solution(mesh):
    layer3 = P("pipe", None, None)
    return jax.shard_map(
        on_device,
        mesh=mesh,
        in_specs=(
            P("dp", None),
            P("dp", None),
            P("dp", None),
            P(),
            layer3,
            layer3,
            layer3,
            layer3,
            layer3,
            P("pipe", None),
            layer3,
            layer3,
            layer3,
            P(),
            P(),
            P(),
        ),
        out_specs=(
            P(("pipe", "dp"), None),
            P("pipe", "dp", None),
            P("pipe", None, "dp"),
            P("pipe", "dp", None),
            P("pipe", None, "dp"),
            P("pipe", "dp", None),
            P("pipe", "dp"),
            P("pipe", "dp", None),
            P("pipe", None, "dp"),
            P("pipe", None, "dp"),
            P(),
            P(),
            P(("pipe", "dp"), None),
        ),
        check_vma=False,
    )
```
